32 devices in a mesh: dev: 32 (over z, y, x, core).
Axes of the slice: x: 2, y: 2, z: 4, core: 2. Of those that a mesh axis runs over, the one named last changes fastest.
Arguments:
- patches: bfloat16 [64, 256, 588], P('dev'), may hold values from -6 to 6
- masked: int32 [64, 16], P('dev'), may hold values from 0 to 255, as said below
- slot_used: int32 [64], P('dev'), may hold values from 0 to 1, as said below
- stem: float32 [5831040], P('dev')
- stem_moment: float32 [5831040], P('dev'), may hold values from -8.940697e-08 to 8.940697e-08
- stem_second: float32 [5831040], P('dev'), may hold values from 3.4414446e-18 to 1.37657785e-17
- stem_teacher: float32 [5831040], P('dev')
- layers: float32 [2, 1771776], P(None, 'dev')
- layer_moment: float32 [2, 1771776], P(None, 'dev'), may hold values from -8.940697e-08 to 8.940697e-08
- layer_second: float32 [2, 1771776], P(None, 'dev'), may hold values from 3.4414446e-18 to 1.37657785e-17
- layer_teacher: float32 [2, 1771776], P(None, 'dev')
- protos: float32 [65536, 256], P('dev'), may hold values from -0.4375 to 0.4375
- proto_moment: float32 [65536, 256], P('dev'), may hold values from -8.940697e-08 to 8.940697e-08
- proto_second: float32 [65536, 256], P('dev'), may hold values from 3.4414446e-18 to 1.37657785e-17
- proto_teacher: float32 [65536, 256], P('dev'), may hold values from -0.4375 to 0.4375
- centre: float32 [65536], replicated, may hold values from -0.078125 to 0.078125
Outputs:
- loss_sum: float32 [], replicated
- image_count: float32 [], replicated
- clip_norm: float32 [], replicated
- new_centre: float32 [65536], replicated
- stem_moment_out: float32 [5831040], P('dev')
- stem_second_out: float32 [5831040], P('dev')
- stem_out: float32 [5831040], P('dev')
- stem_copy: bfloat16 [5831040], P('dev')
- stem_teacher_out: float32 [5831040], P('dev')
- layer_moment_out: float32 [2, 1771776], P(None, 'dev')
- layer_second_out: float32 [2, 1771776], P(None, 'dev')
- layers_out: float32 [2, 1771776], P(None, 'dev')
- layer_copy: bfloat16 [2, 1771776], P(None, 'dev')
- layer_teacher_out: float32 [2, 1771776], P(None, 'dev')
- proto_moment_out: float32 [65536, 256], P('dev')
- proto_second_out: float32 [65536, 256], P('dev')
- protos_out: float32 [65536, 256], P('dev')
- proto_copy: bfloat16 [65536, 256], P('dev')
- proto_teacher_out: float32 [65536, 256], P('dev')
The draws below stay inside these ranges and needn't reach their ends.
Inputs may be any that keep to these rules, and one draw needn't show every extreme that they name: `masked`: each row names 16 different patch positions. `slot_used`: the first of every device's 2 slots is 1.
All inputs are finite; a program needn't handle non-finite values.
Results may differ from the reference program's by a relative error of at most 0.0075.
The reference program's roundings to bfloat16 on the way count: a program that leaves them out, or rounds other values in their place, can miss the bound.
Values may be sent and summed in bfloat16 or wider, within the bound.
No kernel may reach another device: no remote copies, remote signals or barrier semaphores. Data moves between devices by JAX's collectives and lax.ppermute only.
A program may use at most 448 MiB of HBM per device.

```python
import math
import jax
import jax.numpy as jnp
from jax import lax

D = 384
HEADS = 6
HEAD_DIM = 64
FF = 1536
HID = 2048
BOT = 256
PROTOS = 65536
PIX = 588
PATCHES = 256
LAYERS = 2
MASKED = 16
STEP = 10
IMG_DEV = 2
SEQ = 257
IMAGES = 64
LAYER_FLAT = 1771776
STEM_FLAT = 5831040
NPARAM = 26151808


def flat_draw(key, specs, total_length):
    pieces = []
    used_length = 0
    for number in range(len(specs)):
        length, spread, centre_value = specs[number]
        pieces.append(centre_value + spread * jax.random.normal(jax.random.fold_in(key, number), (length,), jnp.float32))
        used_length = used_length + length
    pieces.append(0.02 * jax.random.normal(jax.random.fold_in(key, 97), (total_length - used_length,), jnp.float32))
    return jnp.concatenate(pieces)


def stem_specs():
    return ((PIX * D, PIX ** (-0.5), 0.0), (SEQ * D, 0.5, 0.0), (D, 1.0, 0.0), (D, 1.0, 0.0), (D, 0.2, 1.0), (D, 0.3, 0.0), (D * HID, D ** (-0.5), 0.0), (HID * HID, HID ** (-0.5), 0.0), (HID * BOT, HID ** (-0.5), 0.0))


def layer_specs():
    return ((3 * D * D, D ** (-0.5), 0.0), (D * D, 2.0 * D ** (-0.5), 0.0), (D * FF, D ** (-0.5), 0.0), (FF * D, FF ** (-0.5), 0.0), (D, 0.2, 1.0), (D, 0.3, 0.0), (D, 0.15, 0.6), (D, 0.2, 1.0), (D, 0.3, 0.0), (D, 0.15, 0.6))


def stack_layers(key):
    return jnp.stack([flat_draw(jax.random.fold_in(key, layer_index), layer_specs(), LAYER_FLAT) for layer_index in range(LAYERS)])


def draw_stem(key, part):
    key = jax.random.fold_in(key, 1)
    return flat_draw(key, stem_specs(), STEM_FLAT)


def draw_stem_teacher(key, part):
    key = jax.random.fold_in(key, 2)
    return flat_draw(key, stem_specs(), STEM_FLAT)


def draw_layers(key, part):
    key = jax.random.fold_in(key, 3)
    return stack_layers(key)


def draw_layer_teacher(key, part):
    key = jax.random.fold_in(key, 4)
    return stack_layers(key)


def draw_masked(key, part):
    key = jax.random.fold_in(key, 5)
    row_keys = jax.random.split(key, IMAGES)
    return jax.vmap(lambda row_key: jax.random.permutation(row_key, PATCHES)[:MASKED])(row_keys).astype(jnp.int32)


def draw_slot_used(key, part):
    key = jax.random.fold_in(key, 6)
    slot_index = jnp.arange(IMAGES, dtype=jnp.int32)
    device_index = slot_index // IMG_DEV
    device_count = IMAGES // IMG_DEV
    chances = jax.random.randint(key, (IMAGES,), 0, 3 * device_count, dtype=jnp.int32)
    chosen = (chances < device_count + 2 * device_index).astype(jnp.int32)
    return jnp.where(slot_index % IMG_DEV == 0, 1, chosen).astype(jnp.int32)


def block_levels(stream_key, shape, cuts, low, top_value):
    loudness = 1.0
    for axis_at, parts in cuts:
        heights = jax.random.uniform(jax.random.fold_in(jax.random.fold_in(stream_key, 6), axis_at), (parts,), jnp.float32, low / len(cuts), top_value / len(cuts))
        loudness = loudness * jnp.repeat(jnp.exp(heights), shape[axis_at] // parts).reshape((-1,) + (1,) * (len(shape) - 1 - axis_at))
    return loudness


def bell_draw(stream_key, extent, width, most, cuts=(), kind=jnp.bfloat16):
    array = width * jax.random.normal(stream_key, extent, jnp.float32)
    if cuts:
        array = array * block_levels(stream_key, extent, cuts, -0.22, 0.18)
    return jnp.clip(array, -most, most).astype(kind)


def setup_inputs(seed: int = 0) -> dict:
    keys = jax.random.split(jax.random.key(seed), 17)
    return {
        "patches": bell_draw(keys[0], (IMAGES, PATCHES, PIX), 1.0, 6.0, ((0, 32),)),
        "masked": draw_masked(jax.random.fold_in(keys[16], 71), 0),
        "slot_used": draw_slot_used(jax.random.fold_in(keys[16], 71), 0),
        "stem": draw_stem(jax.random.fold_in(keys[16], 71), 0),
        "stem_moment": bell_draw(keys[4], (STEM_FLAT,), (0.000033 * NPARAM ** -0.5), 8.940696716308594e-08, ((0, 32),), jnp.float32),
        "stem_second": jnp.clip(jnp.exp(math.log(1.3765778453888039e-17) - 1.3862944 * jax.random.uniform(keys[5], (STEM_FLAT,), jnp.float32) ** block_levels(keys[5], (STEM_FLAT,), ((0, 32),), -0.2, 0.2)), 3.4414446134720097e-18, 1.3765778453888039e-17),
        "stem_teacher": draw_stem_teacher(jax.random.fold_in(keys[16], 71), 0),
        "layers": draw_layers(jax.random.fold_in(keys[16], 71), 0),
        "layer_moment": bell_draw(keys[8], (LAYERS, LAYER_FLAT), (0.000033 * NPARAM ** -0.5), 8.940696716308594e-08, ((1, 32),), jnp.float32),
        "layer_second": jnp.clip(jnp.exp(math.log(1.3765778453888039e-17) - 1.3862944 * jax.random.uniform(keys[9], (LAYERS, LAYER_FLAT), jnp.float32) ** block_levels(keys[9], (LAYERS, LAYER_FLAT), ((1, 32),), -0.2, 0.2)), 3.4414446134720097e-18, 1.3765778453888039e-17),
        "layer_teacher": draw_layer_teacher(jax.random.fold_in(keys[16], 71), 0),
        "protos": bell_draw(keys[11], (PROTOS, BOT), 0.03, 0.4375, ((0, 32),), jnp.float32),
        "proto_moment": bell_draw(keys[12], (PROTOS, BOT), (0.000033 * NPARAM ** -0.5), 8.940696716308594e-08, ((0, 32),), jnp.float32),
        "proto_second": jnp.clip(jnp.exp(math.log(1.3765778453888039e-17) - 1.3862944 * jax.random.uniform(keys[13], (PROTOS, BOT), jnp.float32) ** block_levels(keys[13], (PROTOS, BOT), ((0, 32),), -0.2, 0.2)), 3.4414446134720097e-18, 1.3765778453888039e-17),
        "proto_teacher": bell_draw(keys[14], (PROTOS, BOT), 0.03, 0.4375, ((0, 32),), jnp.float32),
        "centre": bell_draw(keys[15], (PROTOS,), 0.005, 0.078125, (), jnp.float32),
    }


tau_student = 0.1
tau_teacher = 0.04
clip_limit = 0.003
learn_rate = 0.03
beta_one = 0.9
beta_two = 0.999
adam_eps = 1e-08
decay_rate = 0.04
teacher_keep = 0.8
centre_keep = 0.9
highest = lax.Precision.HIGHEST

@jax.custom_vjp
def low(v):
    return lax.optimization_barrier(v.astype(jnp.bfloat16)).astype(jnp.float32)

@jax.custom_vjp
def low_back(v):
    return v

def low_keep(v):
    return (low(v), None)

def low_pass(kept, grad):
    return (grad,)

def back_keep(v):
    return (v, None)

def back_low(kept, grad):
    return (low(grad),)
low.defvjp(low_keep, low_pass)
low_back.defvjp(back_keep, back_low)

def layer_shapes():
    return ((D, 3 * D), (D, D), (D, FF), (FF, D), (6, D))

def stem_shapes():
    return ((PIX, D), (SEQ, D), (4, D), (D, HID), (HID, HID), (HID, BOT))

def cut_flat(flat_row, shape_list):
    pieces = []
    offset = 0
    for shape_pair in shape_list:
        length = shape_pair[0] * shape_pair[1]
        pieces.append(flat_row[offset:offset + length].reshape(shape_pair))
        offset = offset + length
    return pieces

def product(left_arg, right_arg, form):
    return low_back(jnp.einsum(form, low(left_arg), low(right_arg), precision=highest))

def layer_norm(values, gain_row, bias_row):
    centred = values - lax.optimization_barrier(jnp.mean(values, axis=-1, keepdims=True))
    spread = lax.optimization_barrier(jnp.mean(centred * centred, axis=-1, keepdims=True))
    return centred * lax.rsqrt(spread + 1e-06) * gain_row + bias_row

def unit_rows(values):
    return values * lax.rsqrt(lax.optimization_barrier(jnp.sum(values * values, axis=-1, keepdims=True)) + 1e-06)

def block(stream, weights):
    w_qkv, w_proj, w_up, w_down, vectors = weights
    batch_size = stream.shape[0]
    normed = layer_norm(stream, vectors[0], vectors[1])
    packed = product(normed, w_qkv, 'bsd,de->bse').reshape(batch_size, SEQ, 3, HEADS, HEAD_DIM)
    raw_scores = product(packed[:, :, 0], packed[:, :, 1], 'bqhe,bkhe->bhqk')
    attn_probs = jax.nn.softmax(raw_scores * HEAD_DIM ** (-0.5), axis=-1)
    mixed = product(attn_probs, packed[:, :, 2], 'bhqk,bkhe->bqhe').reshape(batch_size, SEQ, D)
    stream = stream + vectors[2] * product(mixed, w_proj, 'bsd,de->bse')
    normed_two = layer_norm(stream, vectors[3], vectors[4])
    hidden = jax.nn.gelu(product(normed_two, w_up, 'bsd,df->bsf'))
    return stream + vectors[5] * product(hidden, w_down, 'bsf,fd->bsd')

def tower(param_set, image_rows, index_rows, student):
    stem_flat, layer_stack, proto_rows = param_set
    patch_w, position, extras, w_first, w_second, w_third = cut_flat(stem_flat, stem_shapes())
    embedded = product(image_rows, patch_w, 'gpc,cd->gpd')
    if student:
        masked_here = jnp.any(index_rows[:, :, None] == jnp.arange(PATCHES, dtype=jnp.int32)[None, None, :], axis=1)
        embedded = jnp.where(masked_here[:, :, None], extras[1], embedded)
    cls_rows = jnp.broadcast_to(extras[0], (image_rows.shape[0], 1, D))
    stream = jnp.concatenate([cls_rows, embedded], axis=1) + position
    for layer_index in range(LAYERS):
        stream = block(stream, cut_flat(layer_stack[layer_index], layer_shapes()))
    row_index = jnp.concatenate([jnp.zeros((image_rows.shape[0], 1), jnp.int32), index_rows.astype(jnp.int32) + 1], axis=1)
    chosen = layer_norm(jnp.take_along_axis(stream, row_index[:, :, None], axis=1), extras[2], extras[3])
    hidden_one = jax.nn.gelu(product(chosen, w_first, 'grd,dh->grh'))
    hidden_two = jax.nn.gelu(product(hidden_one, w_second, 'grh,hk->grk'))
    unit_z = unit_rows(product(hidden_two, w_third, 'grh,hb->grb'))
    return product(unit_z, unit_rows(proto_rows), 'grb,kb->grk')

def adam_update(weight, moment, second, grad, teacher):
    new_moment = beta_one * moment + (1.0 - beta_one) * grad
    new_second = beta_two * second + (1.0 - beta_two) * grad * grad
    direction = new_moment / (1.0 - beta_one ** STEP) / (jnp.sqrt(new_second / (1.0 - beta_two ** STEP)) + adam_eps)
    new_weight = weight - learn_rate * (direction + decay_rate * weight)
    return (new_moment, new_second, new_weight, new_weight.astype(jnp.bfloat16), teacher_keep * teacher + (1.0 - teacher_keep) * new_weight)

def reference(patches, masked, slot_used, stem, stem_moment, stem_second, stem_teacher, layers, layer_moment, layer_second, layer_teacher, protos, proto_moment, proto_second, proto_teacher, centre):
    group_count = IMAGES // IMG_DEV
    image_groups = patches.reshape(group_count, IMG_DEV, PATCHES, PIX)
    index_groups = masked.reshape(group_count, IMG_DEV, MASKED)
    keep_groups = slot_used.astype(jnp.float32).reshape(group_count, IMG_DEV)
    teacher_set = (low(stem_teacher), low(layer_teacher), low(proto_teacher))
    params = (stem, layers, protos)

    def group_step(running, group_data):
        image_rows, index_rows, kept_rows = group_data
        image_rows = image_rows.astype(jnp.float32)
        teacher_logits = tower(teacher_set, image_rows, index_rows, False)
        teacher_probs = jax.nn.softmax((teacher_logits - centre) / tau_teacher, axis=-1)

        def loss_fn(weights):
            lowered = (low(weights[0]), low(weights[1]), low(weights[2]))
            logits = tower(lowered, image_rows, index_rows, True)
            log_probs = jax.nn.log_softmax(logits / tau_student, axis=-1)
            cross = -lax.optimization_barrier(jnp.sum(teacher_probs * log_probs, axis=-1))
            return jnp.sum(kept_rows * (cross[:, 0] + lax.optimization_barrier(jnp.mean(cross[:, 1:], axis=1))))
        loss_value, puller = jax.vjp(loss_fn, params)
        grad_set = puller(jnp.float32(1.0))[0]
        grad_sum, loss_total, centre_total, count_total = running
        grad_sum = jax.tree.map(jnp.add, grad_sum, grad_set)
        centre_total = centre_total + lax.optimization_barrier(jnp.sum(kept_rows[:, None] * teacher_logits[:, 0], axis=0))
        return ((grad_sum, loss_total + loss_value, centre_total, count_total + jnp.sum(kept_rows)), None)
    start_state = (jax.tree.map(jnp.zeros_like, params), jnp.float32(0.0), jnp.zeros((PROTOS,), jnp.float32), jnp.float32(0.0))
    final_state = lax.scan(group_step, start_state, (image_groups, index_groups, keep_groups))[0]
    grad_sum, loss_total, centre_total, count_total = final_state
    square_total = jnp.sum(grad_sum[0] * grad_sum[0]) + jnp.sum(grad_sum[1] * grad_sum[1]) + jnp.sum(grad_sum[2] * grad_sum[2])
    grad_norm = jnp.sqrt(square_total) / count_total
    factor = jnp.minimum(1.0, clip_limit / (grad_norm + 1e-06)) / count_total
    new_centre = centre_keep * centre + (1.0 - centre_keep) * centre_total / count_total
    stem_set = adam_update(stem, stem_moment, stem_second, grad_sum[0] * factor, stem_teacher)
    layer_set = adam_update(layers, layer_moment, layer_second, grad_sum[1] * factor, layer_teacher)
    proto_set = adam_update(protos, proto_moment, proto_second, grad_sum[2] * factor, proto_teacher)
    return (loss_total, count_total, grad_norm, new_centre, stem_set[0], stem_set[1], stem_set[2], stem_set[3], stem_set[4], layer_set[0], layer_set[1], layer_set[2], layer_set[3], layer_set[4], proto_set[0], proto_set[1], proto_set[2], proto_set[3], proto_set[4])
```

```python
import jax
import jax.numpy as jnp
from jax import lax
from jax.sharding import PartitionSpec as P

D = 384
HEADS = 6
HEAD_DIM = 64
FF = 1536
HID = 2048
BOT = 256
PIX = 588
PATCHES = 256
LAYERS = 2
STEP = 10
SEQ = 257


tau_student = 0.1
tau_teacher = 0.04
clip_limit = 0.003
learn_rate = 0.03
beta_one = 0.9
beta_two = 0.999
adam_eps = 1e-08
decay_rate = 0.04
teacher_keep = 0.8
centre_keep = 0.9
narrow = jnp.bfloat16
single = jnp.float32


def layer_shapes():
    return ((D, 3 * D), (D, D), (D, FF), (FF, D), (6, D))


def stem_shapes():
    return ((PIX, D), (SEQ, D), (4, D), (D, HID), (HID, HID), (HID, BOT))


def cut_flat(flat_row, shape_list):
    pieces = []
    offset = 0
    for shape_pair in shape_list:
        length = shape_pair[0] * shape_pair[1]
        pieces.append(flat_row[offset : offset + length].reshape(shape_pair))
        offset = offset + length
    return pieces


def pack_flat(grad_list, total_length):
    joined = jnp.concatenate([grad_item.reshape(-1) for grad_item in grad_list])
    return jnp.concatenate([joined, jnp.zeros((total_length - joined.shape[0],), single)])


def contract(form, left_arg, right_arg):
    return jnp.einsum(form, left_arg, right_arg, preferred_element_type=single)


def layer_norm(values, gain_row, bias_row):
    centred = values - jnp.mean(values, axis=-1, keepdims=True)
    spread = jnp.mean(centred * centred, axis=-1, keepdims=True)
    return centred * lax.rsqrt(spread + 1e-06) * gain_row + bias_row


def unit_rows(values):
    return values * lax.rsqrt(jnp.sum(values * values, axis=-1, keepdims=True) + 1e-06)


def gelu_back(pre_act, grad_act):
    return jax.vjp(jax.nn.gelu, pre_act)[1](grad_act)[0]


def block_forward(stream, weights):
    w_qkv, w_proj, w_up, w_down, vectors = weights
    vectors = vectors.astype(single)
    batch_size = stream.shape[0]
    normed = layer_norm(stream, vectors[0], vectors[1]).astype(narrow)
    packed = (
        contract("bsd,de->bse", normed, w_qkv)
        .astype(narrow)
        .reshape(batch_size, SEQ, 3, HEADS, HEAD_DIM)
    )
    scores = contract("bqhe,bkhe->bhqk", packed[:, :, 0], packed[:, :, 1]) * HEAD_DIM ** (-0.5)
    top_score = jnp.max(scores, axis=-1, keepdims=True)
    exp_terms = jnp.exp(scores - top_score)
    totals = jnp.sum(exp_terms, axis=-1, keepdims=True)
    log_total = top_score + jnp.log(totals)
    mixed = contract("bhqk,bkhe->bqhe", (exp_terms / totals).astype(narrow), packed[:, :, 2])
    mixed = mixed.astype(narrow).reshape(batch_size, SEQ, D)
    attn_out = contract("bsd,de->bse", mixed, w_proj)
    middle = stream + vectors[2] * attn_out
    normed_two = layer_norm(middle, vectors[3], vectors[4]).astype(narrow)
    pre_act = contract("bsd,df->bsf", normed_two, w_up)
    hidden = jax.nn.gelu(pre_act).astype(narrow)
    mlp_out = contract("bsf,fd->bsd", hidden, w_down)
    saved = (
        stream,
        normed,
        packed,
        log_total,
        mixed,
        attn_out,
        middle,
        normed_two,
        pre_act,
        hidden,
        mlp_out,
    )
    return (middle + vectors[5] * mlp_out, saved)


def block_backward(grad_out, weights, saved):
    w_qkv, w_proj, w_up, w_down, vectors = weights
    vectors = vectors.astype(single)
    (
        stream,
        normed,
        packed,
        log_total,
        mixed,
        attn_out,
        middle,
        normed_two,
        pre_act,
        hidden,
        mlp_out,
    ) = saved
    batch_size = stream.shape[0]
    score_scale = HEAD_DIM ** (-0.5)
    grad_ls_two = jnp.sum(grad_out * mlp_out, axis=(0, 1))
    grad_mlp = (grad_out * vectors[5]).astype(narrow)
    grad_down = contract("bsf,bsd->fd", hidden, grad_mlp)
    grad_pre = gelu_back(pre_act, contract("bsd,fd->bsf", grad_mlp, w_down)).astype(narrow)
    grad_up = contract("bsd,bsf->df", normed_two, grad_pre)
    grad_normed_two = contract("bsf,df->bsd", grad_pre, w_up)
    grad_mid, grad_gain_two, grad_bias_two = jax.vjp(layer_norm, middle, vectors[3], vectors[4])[1](
        grad_normed_two
    )
    grad_mid = grad_mid + grad_out
    grad_ls_one = jnp.sum(grad_mid * attn_out, axis=(0, 1))
    grad_attn = (grad_mid * vectors[2]).astype(narrow)
    grad_proj = contract("bsd,bse->de", mixed, grad_attn)
    grad_mixed = (
        contract("bse,de->bsd", grad_attn, w_proj)
        .astype(narrow)
        .reshape(batch_size, SEQ, HEADS, HEAD_DIM)
    )
    query_rows = packed[:, :, 0]
    key_rows = packed[:, :, 1]
    value_rows = packed[:, :, 2]
    probs = jnp.exp(contract("bqhe,bkhe->bhqk", query_rows, key_rows) * score_scale - log_total)
    grad_probs = contract("bqhe,bkhe->bhqk", grad_mixed, value_rows)
    grad_values = contract("bhqk,bqhe->bkhe", probs.astype(narrow), grad_mixed)
    grad_scores = probs * (grad_probs - jnp.sum(probs * grad_probs, axis=-1, keepdims=True))
    grad_raw = (grad_scores * score_scale).astype(narrow)
    grad_queries = contract("bhqk,bkhe->bqhe", grad_raw, key_rows)
    grad_keys = contract("bhqk,bqhe->bkhe", grad_raw, query_rows)
    grad_packed = (
        jnp.stack([grad_queries, grad_keys, grad_values], axis=2)
        .astype(narrow)
        .reshape(batch_size, SEQ, 3 * D)
    )
    grad_qkv = contract("bsd,bse->de", normed, grad_packed)
    grad_normed = contract("bse,de->bsd", grad_packed, w_qkv)
    grad_in, grad_gain_one, grad_bias_one = jax.vjp(layer_norm, stream, vectors[0], vectors[1])[1](
        grad_normed
    )
    grad_vectors = jnp.stack(
        [grad_gain_one, grad_bias_one, grad_ls_one, grad_gain_two, grad_bias_two, grad_ls_two]
    )
    return (grad_in + grad_mid, (grad_qkv, grad_proj, grad_up, grad_down, grad_vectors))


def embed(stem_parts, image_rows, masked_here, student):
    patch_w, position, extras, w_first, w_second, w_third = stem_parts
    extras = extras.astype(single)
    embedded = contract("gpc,cd->gpd", image_rows, patch_w)
    if student:
        embedded = jnp.where(masked_here[:, :, None], extras[1], embedded)
    cls_rows = jnp.broadcast_to(extras[0], (image_rows.shape[0], 1, D))
    return jnp.concatenate([cls_rows, embedded], axis=1) + position.astype(single)


def embed_backward(grad_stream, image_rows, masked_here):
    grad_cls = jnp.sum(grad_stream[:, 0], axis=0)
    grad_position = jnp.sum(grad_stream, axis=0)
    grad_patch_rows = grad_stream[:, 1:]
    grad_mask_token = jnp.sum(jnp.where(masked_here[:, :, None], grad_patch_rows, 0.0), axis=(0, 1))
    grad_embedded = jnp.where(masked_here[:, :, None], 0.0, grad_patch_rows).astype(narrow)
    grad_patch_w = contract("gpc,gpd->cd", image_rows, grad_embedded)
    return (grad_patch_w, grad_position, grad_cls, grad_mask_token)


def head_forward(stem_parts, proto_rows, stream, row_index):
    patch_w, position, extras, w_first, w_second, w_third = stem_parts
    extras = extras.astype(single)
    chosen = jnp.take_along_axis(stream, row_index[:, :, None], axis=1)
    normed = layer_norm(chosen, extras[2], extras[3]).astype(narrow)
    pre_one = contract("grd,dh->grh", normed, w_first)
    hidden_one = jax.nn.gelu(pre_one).astype(narrow)
    pre_two = contract("grh,hk->grk", hidden_one, w_second)
    hidden_two = jax.nn.gelu(pre_two).astype(narrow)
    bottleneck = contract("grh,hb->grb", hidden_two, w_third)
    unit_z = unit_rows(bottleneck).astype(narrow)
    unit_protos = unit_rows(proto_rows.astype(single)).astype(narrow)
    logits = contract("grb,kb->grk", unit_z, unit_protos)
    return (
        logits,
        (chosen, normed, pre_one, hidden_one, pre_two, hidden_two, bottleneck, unit_z, unit_protos),
    )


def head_backward(grad_logits, stem_parts, saved, row_index, stream_shape):
    patch_w, position, extras, w_first, w_second, w_third = stem_parts
    extras = extras.astype(single)
    chosen, normed, pre_one, hidden_one, pre_two, hidden_two, bottleneck, unit_z, unit_protos = (
        saved
    )
    grad_rounded = grad_logits.astype(narrow)
    grad_unit_z = contract("grk,kb->grb", grad_rounded, unit_protos)
    grad_unit_protos = contract("grk,grb->kb", grad_rounded, unit_z)
    grad_bottle = jax.vjp(unit_rows, bottleneck)[1](grad_unit_z)[0].astype(narrow)
    grad_third = contract("grh,grb->hb", hidden_two, grad_bottle)
    grad_pre_two = gelu_back(pre_two, contract("grb,hb->grh", grad_bottle, w_third)).astype(narrow)
    grad_second = contract("grh,grk->hk", hidden_one, grad_pre_two)
    grad_pre_one = gelu_back(pre_one, contract("grk,hk->grh", grad_pre_two, w_second)).astype(
        narrow
    )
    grad_first = contract("grd,grh->dh", normed, grad_pre_one)
    grad_normed = contract("grh,dh->grd", grad_pre_one, w_first)
    grad_chosen, grad_gain, grad_bias = jax.vjp(layer_norm, chosen, extras[2], extras[3])[1](
        grad_normed
    )
    image_index = jnp.arange(row_index.shape[0], dtype=jnp.int32)[:, None]
    grad_stream = jnp.zeros(stream_shape, single).at[image_index, row_index].add(grad_chosen)
    return (
        grad_stream,
        (grad_first, grad_second, grad_third),
        grad_gain,
        grad_bias,
        grad_unit_protos,
    )


def adam_update(weight, moment, second, grad, teacher):
    new_moment = beta_one * moment + (1.0 - beta_one) * grad
    new_second = beta_two * second + (1.0 - beta_two) * grad * grad
    direction = (
        new_moment
        / (1.0 - beta_one**STEP)
        / (jnp.sqrt(new_second / (1.0 - beta_two**STEP)) + adam_eps)
    )
    new_weight = weight - learn_rate * (direction + decay_rate * weight)
    return (
        new_moment,
        new_second,
        new_weight,
        new_weight.astype(narrow),
        teacher_keep * teacher + (1.0 - teacher_keep) * new_weight,
    )


def spread_local(
    patches,
    masked,
    slot_used,
    stem,
    stem_moment,
    stem_second,
    stem_teacher,
    layers,
    layer_moment,
    layer_second,
    layer_teacher,
    protos,
    proto_moment,
    proto_second,
    proto_teacher,
    centre,
):
    images_here = patches.shape[0]
    row_index = jnp.concatenate([jnp.zeros((images_here, 1), jnp.int32), masked + 1], axis=1)
    masked_here = jnp.any(
        masked[:, :, None] == jnp.arange(PATCHES, dtype=jnp.int32)[None, None, :], axis=1
    )
    kept = slot_used.astype(single)
    teacher_flat, teacher_protos = (
        lax.all_gather(stem_teacher.astype(narrow), "dev", axis=0, tiled=True),
        lax.all_gather(proto_teacher.astype(narrow), "dev", axis=0, tiled=True),
    )
    teacher_parts = cut_flat(teacher_flat, stem_shapes())
    stream = embed(teacher_parts, patches, masked_here, False)
    for layer_index in range(LAYERS):
        teacher_layer = lax.all_gather(
            layer_teacher[layer_index].astype(narrow), "dev", axis=0, tiled=True
        )
        stream = block_forward(stream, cut_flat(teacher_layer, layer_shapes()))[0]
    teacher_logits = head_forward(teacher_parts, teacher_protos, stream, row_index)[0]
    teacher_probs = jax.nn.softmax((teacher_logits - centre) / tau_teacher, axis=-1)
    centre_terms = jnp.sum(kept[:, None] * teacher_logits[:, 0], axis=0)
    student_flat, student_protos = (
        lax.all_gather(stem.astype(narrow), "dev", axis=0, tiled=True),
        lax.all_gather(protos.astype(narrow), "dev", axis=0, tiled=True),
    )
    student_parts = cut_flat(student_flat, stem_shapes())
    stream = embed(student_parts, patches, masked_here, True)
    saved_layers = []
    gathered_layers = []
    for layer_index in range(LAYERS):
        layer_flat = lax.all_gather(layers[layer_index].astype(narrow), "dev", axis=0, tiled=True)
        gathered_layers.append(layer_flat)
        stream, saved = block_forward(stream, cut_flat(layer_flat, layer_shapes()))
        saved_layers.append(saved)
    logits, head_saved = head_forward(student_parts, student_protos, stream, row_index)

    def loss_piece(logit_rows):
        log_probs = jax.nn.log_softmax(logit_rows / tau_student, axis=-1)
        cross = -jnp.sum(teacher_probs * log_probs, axis=-1)
        return jnp.sum(kept * (cross[:, 0] + jnp.mean(cross[:, 1:], axis=1)))

    loss_local, loss_puller = jax.vjp(loss_piece, logits)
    grad_logits = loss_puller(jnp.float32(1.0))[0]
    count_local = jnp.sum(kept)
    loss_total, count_total, centre_total = lax.psum((loss_local, count_local, centre_terms), "dev")
    back_flat, back_protos = (
        lax.all_gather(stem.astype(narrow), "dev", axis=0, tiled=True),
        lax.all_gather(protos.astype(narrow), "dev", axis=0, tiled=True),
    )
    back_parts = cut_flat(back_flat, stem_shapes())
    grad_stream, head_grads, grad_gain, grad_bias, grad_unit_protos = head_backward(
        grad_logits, back_parts, head_saved, row_index, stream.shape
    )
    layer_grads = []
    for layer_index in reversed(range(LAYERS)):
        weight_flat = lax.all_gather(layers[layer_index].astype(narrow), "dev", axis=0, tiled=True)
        grad_stream, block_grads = block_backward(
            grad_stream, cut_flat(weight_flat, layer_shapes()), saved_layers[layer_index]
        )
        layer_grads.insert(
            0,
            lax.psum_scatter(
                pack_flat(block_grads, weight_flat.shape[0]), "dev", scatter_dimension=0, tiled=True
            ),
        )
    grad_patch_w, grad_position, grad_cls, grad_mask_token = embed_backward(
        grad_stream, patches, masked_here
    )
    grad_extras = jnp.stack([grad_cls, grad_mask_token, grad_gain, grad_bias])
    stem_flat_grad = pack_flat(
        (grad_patch_w, grad_position, grad_extras) + head_grads, back_flat.shape[0]
    )
    stem_grad, proto_row_grad = (
        lax.psum_scatter(stem_flat_grad, "dev", scatter_dimension=0, tiled=True),
        lax.psum_scatter(grad_unit_protos, "dev", scatter_dimension=0, tiled=True),
    )
    own_protos = lax.optimization_barrier(protos.astype(narrow)).astype(single)
    proto_grad = jax.vjp(unit_rows, own_protos)[1](proto_row_grad)[0]
    layer_grad = jnp.stack(layer_grads)
    square_local = (
        jnp.sum(stem_grad * stem_grad)
        + jnp.sum(layer_grad * layer_grad)
        + jnp.sum(proto_grad * proto_grad)
    )
    square_total = lax.psum(square_local, "dev")
    grad_norm = jnp.sqrt(square_total) / count_total
    factor = jnp.minimum(1.0, clip_limit / (grad_norm + 1e-06)) / count_total
    new_centre = centre_keep * centre + (1.0 - centre_keep) * centre_total / count_total
    stem_set = adam_update(stem, stem_moment, stem_second, stem_grad * factor, stem_teacher)
    layer_set = adam_update(layers, layer_moment, layer_second, layer_grad * factor, layer_teacher)
    proto_set = adam_update(protos, proto_moment, proto_second, proto_grad * factor, proto_teacher)
    return (
        loss_total,
        count_total,
        grad_norm,
        new_centre,
        stem_set[0],
        stem_set[1],
        stem_set[2],
        stem_set[3],
        stem_set[4],
        layer_set[0],
        layer_set[1],
        layer_set[2],
        layer_set[3],
        layer_set[4],
        proto_set[0],
        proto_set[1],
        proto_set[2],
        proto_set[3],
        proto_set[4],
    )


GROUP = 16
ROW = HID
MATRIX_ROWS = D * 3 + D + FF + FF
EMBED_ROWS = PIX + SEQ + 4
EMBED_FLAT = EMBED_ROWS * D
HEAD_ROWS = D + HID + BOT
BITS = ("b", "a", "y", "x", "c")
MASKS = {"c": 1, "x": 2, "y": 4, "a": 8, "b": 24}


def head_bounds(count, stem_piece):
    bounds = [-(-(stem_piece * device - EMBED_FLAT) // (ROW * GROUP)) * GROUP for device in range(count + 1)]
    bounds[0] = -(-EMBED_FLAT // (ROW * GROUP)) * -GROUP
    bounds[-1] = HEAD_ROWS
    return bounds


def fits(count, stem_piece, layer_piece):
    if count != 1 << len(BITS) or MATRIX_ROWS % (3 * count):
        return False
    bounds = head_bounds(count, stem_piece)
    sizes = [bounds[i + 1] - bounds[i] for i in range(count)]
    return (
        min(sizes) > GROUP
        and bounds[1] <= 0
        and stem_piece < EMBED_FLAT <= 2 * stem_piece
        and D in bounds
        and D + HID in bounds
        and stem_piece * count == EMBED_FLAT + HEAD_ROWS * ROW
    )


def pairs(count, mask):
    return [(i, i ^ mask) for i in range(count)]


def bit_flags(me):
    return {name: (me >> (len(BITS) - 1 - place)) & 1 for place, name in enumerate(BITS)}


def cube_gather(parts, orders):
    count = 1 << len(BITS)
    flags = bit_flags(lax.axis_index("dev"))
    held = [part[None] for part in parts]
    for turn in range(len(BITS)):
        got = [
            lax.ppermute(h, "dev", pairs(count, MASKS[order[turn]])) for h, order in zip(held, orders)
        ]
        held = [
            jnp.where(
                flags[order[turn]] == 1,
                jnp.concatenate([g, h], axis=0),
                jnp.concatenate([h, g], axis=0),
            )
            for h, g, order in zip(held, got, orders)
        ]
    return held


def cube_scatter(parts, orders, axes):
    count = 1 << len(BITS)
    flags = bit_flags(lax.axis_index("dev"))
    held = list(parts)
    names = [list(a) for a in axes]
    for turn in range(len(BITS)):
        sent, kept = [], []
        for h, order, name in zip(held, orders, names):
            place = name.index(order[turn])
            low = lax.index_in_dim(h, 0, place, keepdims=False)
            high = lax.index_in_dim(h, 1, place, keepdims=False)
            flag = flags[order[turn]] == 1
            sent.append(jnp.where(flag, low, high))
            kept.append(jnp.where(flag, high, low))
            name.pop(place)
        got = [
            lax.ppermute(s, "dev", pairs(count, MASKS[order[turn]])) for s, order in zip(sent, orders)
        ]
        held = [
            (k.astype(single) + g.astype(single)).astype(k.dtype) for k, g in zip(kept, got)
        ]
    return held


def cube_sum(values):
    for name in "cxyab":
        values = values + lax.ppermute(values, "dev", pairs(1 << len(BITS), MASKS[name]))
    return values


def split_bits(array):
    return array.reshape((2,) * len(BITS) + array.shape[1:])


def scatter_rows(array, cuts, axis):
    points = [0, cuts[0], cuts[0] + cuts[1], array.shape[axis]]
    parts = [
        split_bits(lax.slice_in_dim(array, points[i], points[i + 1], axis=axis)) for i in range(3)
    ]
    done = cube_scatter(parts, ("cxyba", "cyxba", "cbaxy"), (BITS,) * 3)
    return jnp.concatenate(done, axis=axis - 1)


def step_pairs(count, step):
    return [(i, i + step) for i in range(count) if 0 <= i + step < count]


def close_local(
    patches,
    masked,
    slot_used,
    stem,
    stem_moment,
    stem_second,
    stem_teacher,
    layers,
    layer_moment,
    layer_second,
    layer_teacher,
    protos,
    proto_moment,
    proto_second,
    proto_teacher,
    centre,
):
    count = 1 << len(BITS)
    me = lax.axis_index("dev")
    images_here = patches.shape[0]
    rows_here = images_here * 17
    stem_piece = stem.shape[0]
    layer_piece = layers.shape[1]
    block_rows = MATRIX_ROWS // count
    block = block_rows * D
    tail = layer_piece * count - MATRIX_ROWS * D
    drift = layer_piece - block
    bounds = head_bounds(count, stem_piece)
    sizes = [bounds[i + 1] - bounds[i] for i in range(count)]
    slot = max(sizes)
    starts = [b * ROW + EMBED_FLAT - stem_piece * i for i, b in enumerate(bounds[:-1])]
    first_w2 = bounds.index(D)
    first_w3 = bounds.index(D + HID)
    row_index = jnp.concatenate([jnp.zeros((images_here, 1), jnp.int32), masked + 1], axis=1)
    masked_here = jnp.any(
        masked[:, :, None] == jnp.arange(PATCHES, dtype=jnp.int32)[None, None, :], axis=1
    )
    kept = slot_used.astype(single)

    own_layers = jnp.stack([layer_teacher, layers]).astype(narrow).reshape(2 * LAYERS, layer_piece)
    own_tail = own_layers[:, layer_piece - tail :]
    before = lax.ppermute(own_tail, "dev", step_pairs(count, 1))
    joined = jnp.concatenate([before, own_layers], axis=1)
    layer_blocks = lax.dynamic_slice(joined, (0, tail - drift * me), (2 * LAYERS, block)).reshape(
        2 * LAYERS, block_rows, D
    )
    gathered = lax.all_gather(layer_blocks, "dev", axis=0)
    head_span = GROUP * ROW
    own_stems = jnp.stack([stem_teacher, stem]).astype(narrow)
    after = lax.ppermute(own_stems[:, :head_span], "dev", step_pairs(count, -1))
    start_here = jnp.array(starts, jnp.int32)[me]
    front = -min(starts) + (starts[0] % 128)
    joined = jnp.concatenate(
        [
            jnp.zeros((2, front), narrow),
            own_stems,
            after,
            jnp.zeros((2, slot * ROW), narrow),
        ],
        axis=1,
    )
    head_blocks = lax.dynamic_slice(joined, (0, front + start_here), (2, slot * ROW)).reshape(
        2, slot, ROW
    )
    gathered_head = lax.all_gather(head_blocks, "dev", axis=0)
    vectors_flat = lax.ppermute(own_tail, "dev", [(count - 1, 0)]).reshape(1, 2 * LAYERS * tail)
    seed = jnp.concatenate([own_stems.reshape(1, -1), vectors_flat], axis=1)
    spread = seed
    reached = [0, 1]
    for name in "baxy":
        moves = [(i, i ^ MASKS[name]) for i in reached]
        got = lax.ppermute(spread, "dev", moves)
        targets = [t for s, t in moves]
        is_target = jnp.array([i in targets for i in range(count)])[me]
        spread = jnp.where(is_target, got, spread)
        reached = reached + targets
    other = lax.ppermute(spread, "dev", pairs(count, 1))
    is_even = me % 2 == 0
    even = jnp.where(is_even, spread, other)[0]
    odd = jnp.where(is_even, other, spread)[0]
    rest = EMBED_FLAT - stem_piece
    embed_flat = [
        jnp.concatenate([even[m * stem_piece : (m + 1) * stem_piece], odd[m * stem_piece : m * stem_piece + rest]])
        for m in range(2)
    ]
    vectors_all = even[2 * stem_piece :].reshape(2, LAYERS, 6, D)

    def layer_weights(model, layer_index):
        flat = gathered[:, model * LAYERS + layer_index].reshape(MATRIX_ROWS, D)
        return (
            flat[: 3 * D].reshape(D, 3 * D),
            flat[3 * D : 4 * D],
            flat[4 * D : 4 * D + FF].reshape(D, FF),
            flat[4 * D + FF :],
            vectors_all[model, layer_index],
        )

    def head_weights(model):
        one = gathered_head[:, model]
        w_one = one[1:first_w2].reshape((first_w2 - 1) * slot, ROW)
        w_two = one[first_w2:first_w3].reshape((first_w3 - first_w2) * slot, ROW)
        w_three = jnp.concatenate([one[i, : sizes[i]] for i in range(first_w3, count)]).reshape(HID, BOT)
        return (w_one, w_two, w_three)

    def pad_columns(values, first, last, origin):
        pieces = []
        for i in range(first, last):
            low, high = bounds[i] - origin, bounds[i + 1] - origin
            if low < 0:
                pieces.append(jnp.zeros(values.shape[:-1] + (-low,), values.dtype))
            pieces.append(values[..., max(low, 0) : high])
            pieces.append(jnp.zeros(values.shape[:-1] + (slot - sizes[i],), values.dtype))
        return jnp.concatenate([p for p in pieces if p.shape[-1]], axis=-1)

    def cut_columns(values, first, last, origin):
        pieces = []
        for i in range(first, last):
            low, high = bounds[i] - origin, bounds[i + 1] - origin
            at = (i - first) * slot
            pieces.append(values[..., at + max(-low, 0) : at + sizes[i]])
        return jnp.concatenate(pieces, axis=-1)

    def embed_parts(model):
        patch_w = embed_flat[model][: PIX * D].reshape(PIX, D)
        position = embed_flat[model][PIX * D : (PIX + SEQ) * D].reshape(SEQ, D)
        extras = embed_flat[model][(PIX + SEQ) * D :].reshape(4, D)
        return (patch_w, position, extras, None, None, None)

    def head_up(stream, extras, weights):
        w_one, w_two, w_three = weights
        chosen = jnp.take_along_axis(stream, row_index[:, :, None], axis=1).reshape(rows_here, D)
        normed = layer_norm(chosen, extras[2].astype(single), extras[3].astype(single)).astype(narrow)
        normed_wide = pad_columns(normed, 1, first_w2, 0)
        pre_one = contract("rd,dh->rh", normed_wide, w_one)
        hidden_one = jax.nn.gelu(pre_one).astype(narrow)
        hidden_wide = pad_columns(hidden_one, first_w2, first_w3, D)
        pre_two = contract("rh,hk->rk", hidden_wide, w_two)
        hidden_two = jax.nn.gelu(pre_two).astype(narrow)
        bottleneck = contract("rh,hb->rb", hidden_two, w_three)
        unit_z = unit_rows(bottleneck).astype(narrow)
        return unit_z, (chosen, normed_wide, pre_one, hidden_wide, pre_two, hidden_two, bottleneck)

    student_parts = embed_parts(1)
    stream = embed(student_parts, patches, masked_here, True)
    saved_layers = []
    student_layers = []
    for layer_index in range(LAYERS):
        weights = layer_weights(1, layer_index)
        student_layers.append(weights)
        stream, saved = block_forward(stream, weights)
        saved_layers.append(saved)
    teacher_parts = embed_parts(0)
    teacher_stream = embed(teacher_parts, patches, masked_here, False)
    for layer_index in range(LAYERS):
        teacher_stream = block_forward(teacher_stream, layer_weights(0, layer_index))[0]
    student_head = head_weights(1)
    teacher_z, _ = head_up(teacher_stream, teacher_parts[2], head_weights(0))
    student_z, head_saved = head_up(stream, student_parts[2], student_head)

    all_rows = count * rows_here
    kept_row = jnp.broadcast_to(kept[:, None], (images_here, 17)).reshape(1, rows_here)
    all_kept = cube_gather([kept_row], ("xyabc",))[0].reshape(all_rows)
    z_all = cube_gather([jnp.stack([teacher_z, student_z])], ("xyabc",))[0]
    teacher_z_all = z_all[:, 0].reshape(all_rows, BOT)
    student_z_all = z_all[:, 1].reshape(all_rows, BOT)
    own_student = lax.optimization_barrier(protos.astype(narrow)).astype(single)
    own_teacher = lax.optimization_barrier(proto_teacher.astype(narrow)).astype(single)
    unit_student = unit_rows(own_student).astype(narrow)
    unit_teacher = unit_rows(own_teacher).astype(narrow)
    protos_here = protos.shape[0]
    own_centre = lax.dynamic_slice(centre, (me * protos_here,), (protos_here,))
    teacher_logits = contract("rb,kb->rk", teacher_z_all, unit_teacher)
    logits = contract("rb,kb->rk", student_z_all, unit_student)
    teacher_exp = jnp.exp((teacher_logits - own_centre) / tau_teacher)
    student_exp = jnp.exp(logits / tau_student)
    sums = jnp.stack(
        [
            jnp.sum(teacher_exp, axis=1),
            jnp.sum(student_exp, axis=1),
            jnp.sum(teacher_exp * logits, axis=1),
        ]
    )
    sums = cube_sum(sums)
    is_class = (jnp.arange(all_rows) % 17) == 0
    row_weight = all_kept * jnp.where(is_class, 1.0, 1.0 / 16.0)
    cross = jnp.log(sums[1]) - sums[2] / (sums[0] * tau_student)
    loss_total = jnp.sum(row_weight * cross)
    count_total = jnp.sum(jnp.where(is_class, all_kept, 0.0))
    centre_sum = jnp.sum(
        jnp.where(is_class, all_kept, 0.0)[:, None] * teacher_logits, axis=0
    )
    own_new_centre = centre_keep * own_centre + (1.0 - centre_keep) * centre_sum / count_total
    new_centre = cube_gather([own_new_centre.reshape(1, protos_here)], ("cxyab",))[0].reshape(-1)
    scale = row_weight / tau_student
    grad_logits = (
        student_exp * (scale / sums[1])[:, None] - teacher_exp * (scale / sums[0])[:, None]
    ).astype(narrow)
    z_partial = contract("rk,kb->rb", grad_logits, unit_student)
    proto_unit_grad = contract("rk,rb->kb", grad_logits, student_z_all)
    proto_grad = jax.vjp(unit_rows, own_student)[1](proto_unit_grad)[0]
    grad_unit_z = cube_scatter(
        [split_bits(z_partial.reshape(count, rows_here, BOT))], ("cbayx",), ("cbayx",)
    )[0]

    chosen, normed_wide, pre_one, hidden_wide, pre_two, hidden_two, bottleneck = head_saved
    w_one, w_two, w_three = student_head
    grad_bottle = jax.vjp(unit_rows, bottleneck)[1](grad_unit_z)[0].astype(narrow)
    grad_third = contract("rh,rb->hb", hidden_two, grad_bottle)
    grad_pre_two = gelu_back(pre_two, contract("rb,hb->rh", grad_bottle, w_three)).astype(narrow)
    grad_second = contract("rh,rk->hk", hidden_wide, grad_pre_two)
    grad_hidden = cut_columns(contract("rk,hk->rh", grad_pre_two, w_two), first_w2, first_w3, D)
    grad_pre_one = gelu_back(pre_one, grad_hidden).astype(narrow)
    grad_first = contract("rd,rh->dh", normed_wide, grad_pre_one)
    grad_normed = cut_columns(contract("rh,dh->rd", grad_pre_one, w_one), 1, first_w2, 0)
    extras = student_parts[2].astype(single)
    grad_chosen, grad_gain, grad_bias = jax.vjp(layer_norm, chosen, extras[2], extras[3])[1](
        grad_normed
    )
    third_rows = grad_third.reshape(BOT, ROW).astype(narrow)
    third_pieces = []
    for i in range(first_w3, count):
        at = bounds[i] - (D + HID)
        third_pieces.append(third_rows[at : at + sizes[i]])
        third_pieces.append(jnp.zeros((slot - sizes[i], ROW), narrow))
    head_grads = jnp.concatenate(
        [
            jnp.zeros((slot, ROW), narrow),
            grad_first.astype(narrow),
            grad_second.astype(narrow),
        ]
        + third_pieces
    ).reshape(count, slot, ROW)
    head_block_grad = scatter_rows(head_grads, (768, 768), 2).astype(single)
    image_index = jnp.arange(images_here, dtype=jnp.int32)[:, None]
    grad_stream = (
        jnp.zeros(stream.shape, single)
        .at[image_index, row_index]
        .add(grad_chosen.reshape(images_here, 17, D))
    )

    layer_block_grads = [None] * LAYERS
    vector_grads = [None] * LAYERS
    for layer_index in reversed(range(LAYERS)):
        grad_stream, grads = block_backward(
            grad_stream, student_layers[layer_index], saved_layers[layer_index]
        )
        grad_qkv, grad_proj, grad_up, grad_down, vector_grads[layer_index] = grads
        flat = jnp.concatenate(
            [
                grad_qkv.astype(narrow).reshape(3 * D, D),
                grad_proj.astype(narrow),
                grad_up.astype(narrow).reshape(FF, D),
                grad_down.astype(narrow),
            ]
        ).reshape(count, block_rows, D)
        layer_block_grads[layer_index] = scatter_rows(flat, (64, 48), 1).astype(single)
    grad_patch_w, grad_position, grad_cls, grad_mask_token = embed_backward(
        grad_stream, patches, masked_here
    )
    small = jnp.concatenate(
        [
            grad_patch_w,
            grad_position,
            jnp.stack([grad_cls, grad_mask_token, grad_gain, grad_bias]),
        ]
        + vector_grads
    )
    small_rows = -(-small.shape[0] // count)
    small = jnp.pad(small, ((0, small_rows * count - small.shape[0]), (0, 0)))
    small_block = cube_scatter(
        [split_bits(small.reshape(count, small_rows, D))], ("cxyba",), (BITS,)
    )[0]
    layer_block = jnp.stack(layer_block_grads)

    square_local = (
        jnp.sum(head_block_grad * head_block_grad)
        + jnp.sum(layer_block * layer_block)
        + jnp.sum(small_block * small_block)
        + jnp.sum(proto_grad * proto_grad)
    )
    square_total = cube_sum(square_local.reshape(1, 1))[0, 0]
    small_all = cube_gather([small_block], ("cxyab",))[0].reshape(small_rows * count, D)
    embed_grad = small_all[:EMBED_ROWS].reshape(-1)
    vector_grad = small_all[EMBED_ROWS : EMBED_ROWS + 6 * LAYERS].reshape(LAYERS, 6 * D)

    layer_block = layer_block.reshape(LAYERS, block)
    behind = lax.ppermute(layer_block[:, :tail], "dev", step_pairs(count, -1))
    behind = jnp.where(me == count - 1, vector_grad, behind)
    layer_grad = lax.dynamic_slice(
        jnp.concatenate([layer_block, behind], axis=1), (0, drift * me), (LAYERS, layer_piece)
    )
    last_rows = lax.dynamic_slice(
        head_block_grad, (jnp.array(sizes, jnp.int32)[me] - GROUP, 0), (GROUP, ROW)
    )
    previous = lax.ppermute(last_rows, "dev", step_pairs(count, 1))
    joined = jnp.concatenate(
        [previous.reshape(-1), head_block_grad.reshape(-1), jnp.zeros((head_span,), single)]
    )
    stem_grad = lax.dynamic_slice(joined, (head_span - start_here,), (stem_piece,))
    second_part = jnp.concatenate([embed_grad[stem_piece:], stem_grad[rest:]])
    stem_grad = jnp.where(
        me == 0, embed_grad[:stem_piece], jnp.where(me == 1, second_part, stem_grad)
    )

    grad_norm = jnp.sqrt(square_total) / count_total
    factor = jnp.minimum(1.0, clip_limit / (grad_norm + 1e-06)) / count_total
    stem_set = adam_update(stem, stem_moment, stem_second, stem_grad * factor, stem_teacher)
    layer_set = adam_update(layers, layer_moment, layer_second, layer_grad * factor, layer_teacher)
    proto_set = adam_update(protos, proto_moment, proto_second, proto_grad * factor, proto_teacher)
    return (loss_total, count_total, grad_norm, new_centre) + stem_set + layer_set + proto_set


def solution(mesh):
    count = mesh.shape["dev"]
    stem_length = -(-(EMBED_FLAT + HEAD_ROWS * ROW) // count) * count
    close = fits(count, stem_length // count, (MATRIX_ROWS + 6) * D // count)
    placed = (
        P("dev", None, None),
        P("dev", None),
        P("dev"),
        P("dev"),
        P("dev"),
        P("dev"),
        P("dev"),
        P(None, "dev"),
        P(None, "dev"),
        P(None, "dev"),
        P(None, "dev"),
        P("dev", None),
        P("dev", None),
        P("dev", None),
        P("dev", None),
        P(),
    )
    return jax.shard_map(
        close_local if close else spread_local,
        mesh=mesh,
        in_specs=placed,
        out_specs=(
            P(),
            P(),
            P(),
            P(),
            P("dev"),
            P("dev"),
            P("dev"),
            P("dev"),
            P("dev"),
            P(None, "dev"),
            P(None, "dev"),
            P(None, "dev"),
            P(None, "dev"),
            P(None, "dev"),
            P("dev", None),
            P("dev", None),
            P("dev", None),
            P("dev", None),
            P("dev", None),
        ),
        check_vma=False,
    )
```

```python
import jax
import jax.numpy as jnp
from jax import lax
from jax.experimental import pallas as pl
from jax.experimental.pallas import tpu as pltpu
from jax.sharding import PartitionSpec as P

D = 384
HEADS = 6
HEAD_DIM = 64
FF = 1536
HID = 2048
BOT = 256
PIX = 588
PATCHES = 256
LAYERS = 2
STEP = 10
SEQ = 257


tau_student = 0.1
tau_teacher = 0.04
clip_limit = 0.003
learn_rate = 0.03
beta_one = 0.9
beta_two = 0.999
adam_eps = 1e-08
decay_rate = 0.04
teacher_keep = 0.8
centre_keep = 0.9
narrow = jnp.bfloat16
single = jnp.float32


def layer_shapes():
    return ((D, 3 * D), (D, D), (D, FF), (FF, D), (6, D))


def stem_shapes():
    return ((PIX, D), (SEQ, D), (4, D), (D, HID), (HID, HID), (HID, BOT))


def cut_flat(flat_row, shape_list):
    pieces = []
    offset = 0
    for shape_pair in shape_list:
        length = shape_pair[0] * shape_pair[1]
        pieces.append(flat_row[offset : offset + length].reshape(shape_pair))
        offset = offset + length
    return pieces


def pack_flat(grad_list, total_length):
    joined = jnp.concatenate([grad_item.reshape(-1) for grad_item in grad_list])
    return jnp.concatenate([joined, jnp.zeros((total_length - joined.shape[0],), single)])


def contract(form, left_arg, right_arg):
    return jnp.einsum(form, left_arg, right_arg, preferred_element_type=single)


def layer_norm(values, gain_row, bias_row):
    centred = values - jnp.mean(values, axis=-1, keepdims=True)
    spread = jnp.mean(centred * centred, axis=-1, keepdims=True)
    return centred * lax.rsqrt(spread + 1e-06) * gain_row + bias_row


def unit_rows(values):
    return values * lax.rsqrt(jnp.sum(values * values, axis=-1, keepdims=True) + 1e-06)


def gelu_back(pre_act, grad_act):
    return jax.vjp(jax.nn.gelu, pre_act)[1](grad_act)[0]


def block_forward(stream, weights):
    w_qkv, w_proj, w_up, w_down, vectors = weights
    vectors = vectors.astype(single)
    batch_size = stream.shape[0]
    normed = layer_norm(stream, vectors[0], vectors[1]).astype(narrow)
    packed = (
        contract("bsd,de->bse", normed, w_qkv)
        .astype(narrow)
        .reshape(batch_size, SEQ, 3, HEADS, HEAD_DIM)
    )
    scores = contract("bqhe,bkhe->bhqk", packed[:, :, 0], packed[:, :, 1]) * HEAD_DIM ** (-0.5)
    top_score = jnp.max(scores, axis=-1, keepdims=True)
    exp_terms = jnp.exp(scores - top_score)
    totals = jnp.sum(exp_terms, axis=-1, keepdims=True)
    log_total = top_score + jnp.log(totals)
    mixed = contract("bhqk,bkhe->bqhe", (exp_terms / totals).astype(narrow), packed[:, :, 2])
    mixed = mixed.astype(narrow).reshape(batch_size, SEQ, D)
    attn_out = contract("bsd,de->bse", mixed, w_proj)
    middle = stream + vectors[2] * attn_out
    normed_two = layer_norm(middle, vectors[3], vectors[4]).astype(narrow)
    pre_act = contract("bsd,df->bsf", normed_two, w_up)
    hidden = jax.nn.gelu(pre_act).astype(narrow)
    mlp_out = contract("bsf,fd->bsd", hidden, w_down)
    saved = (
        stream,
        normed,
        packed,
        log_total,
        mixed,
        attn_out,
        middle,
        normed_two,
        pre_act,
        hidden,
        mlp_out,
    )
    return (middle + vectors[5] * mlp_out, saved)


def block_backward(grad_out, weights, saved):
    w_qkv, w_proj, w_up, w_down, vectors = weights
    vectors = vectors.astype(single)
    (
        stream,
        normed,
        packed,
        log_total,
        mixed,
        attn_out,
        middle,
        normed_two,
        pre_act,
        hidden,
        mlp_out,
    ) = saved
    batch_size = stream.shape[0]
    score_scale = HEAD_DIM ** (-0.5)
    grad_ls_two = jnp.sum(grad_out * mlp_out, axis=(0, 1))
    grad_mlp = (grad_out * vectors[5]).astype(narrow)
    grad_down = contract("bsf,bsd->fd", hidden, grad_mlp)
    grad_pre = gelu_back(pre_act, contract("bsd,fd->bsf", grad_mlp, w_down)).astype(narrow)
    grad_up = contract("bsd,bsf->df", normed_two, grad_pre)
    grad_normed_two = contract("bsf,df->bsd", grad_pre, w_up)
    grad_mid, grad_gain_two, grad_bias_two = jax.vjp(layer_norm, middle, vectors[3], vectors[4])[1](
        grad_normed_two
    )
    grad_mid = grad_mid + grad_out
    grad_ls_one = jnp.sum(grad_mid * attn_out, axis=(0, 1))
    grad_attn = (grad_mid * vectors[2]).astype(narrow)
    grad_proj = contract("bsd,bse->de", mixed, grad_attn)
    grad_mixed = (
        contract("bse,de->bsd", grad_attn, w_proj)
        .astype(narrow)
        .reshape(batch_size, SEQ, HEADS, HEAD_DIM)
    )
    query_rows = packed[:, :, 0]
    key_rows = packed[:, :, 1]
    value_rows = packed[:, :, 2]
    probs = jnp.exp(contract("bqhe,bkhe->bhqk", query_rows, key_rows) * score_scale - log_total)
    grad_probs = contract("bqhe,bkhe->bhqk", grad_mixed, value_rows)
    grad_values = contract("bhqk,bqhe->bkhe", probs.astype(narrow), grad_mixed)
    grad_scores = probs * (grad_probs - jnp.sum(probs * grad_probs, axis=-1, keepdims=True))
    grad_raw = (grad_scores * score_scale).astype(narrow)
    grad_queries = contract("bhqk,bkhe->bqhe", grad_raw, key_rows)
    grad_keys = contract("bhqk,bqhe->bkhe", grad_raw, query_rows)
    grad_packed = (
        jnp.stack([grad_queries, grad_keys, grad_values], axis=2)
        .astype(narrow)
        .reshape(batch_size, SEQ, 3 * D)
    )
    grad_qkv = contract("bsd,bse->de", normed, grad_packed)
    grad_normed = contract("bse,de->bsd", grad_packed, w_qkv)
    grad_in, grad_gain_one, grad_bias_one = jax.vjp(layer_norm, stream, vectors[0], vectors[1])[1](
        grad_normed
    )
    grad_vectors = jnp.stack(
        [grad_gain_one, grad_bias_one, grad_ls_one, grad_gain_two, grad_bias_two, grad_ls_two]
    )
    return (grad_in + grad_mid, (grad_qkv, grad_proj, grad_up, grad_down, grad_vectors))


def embed(stem_parts, image_rows, masked_here, student):
    patch_w, position, extras, w_first, w_second, w_third = stem_parts
    extras = extras.astype(single)
    embedded = contract("gpc,cd->gpd", image_rows, patch_w)
    if student:
        embedded = jnp.where(masked_here[:, :, None], extras[1], embedded)
    cls_rows = jnp.broadcast_to(extras[0], (image_rows.shape[0], 1, D))
    return jnp.concatenate([cls_rows, embedded], axis=1) + position.astype(single)


def embed_backward(grad_stream, image_rows, masked_here):
    grad_cls = jnp.sum(grad_stream[:, 0], axis=0)
    grad_position = jnp.sum(grad_stream, axis=0)
    grad_patch_rows = grad_stream[:, 1:]
    grad_mask_token = jnp.sum(jnp.where(masked_here[:, :, None], grad_patch_rows, 0.0), axis=(0, 1))
    grad_embedded = jnp.where(masked_here[:, :, None], 0.0, grad_patch_rows).astype(narrow)
    grad_patch_w = contract("gpc,gpd->cd", image_rows, grad_embedded)
    return (grad_patch_w, grad_position, grad_cls, grad_mask_token)


def head_forward(stem_parts, proto_rows, stream, row_index):
    patch_w, position, extras, w_first, w_second, w_third = stem_parts
    extras = extras.astype(single)
    chosen = jnp.take_along_axis(stream, row_index[:, :, None], axis=1)
    normed = layer_norm(chosen, extras[2], extras[3]).astype(narrow)
    pre_one = contract("grd,dh->grh", normed, w_first)
    hidden_one = jax.nn.gelu(pre_one).astype(narrow)
    pre_two = contract("grh,hk->grk", hidden_one, w_second)
    hidden_two = jax.nn.gelu(pre_two).astype(narrow)
    bottleneck = contract("grh,hb->grb", hidden_two, w_third)
    unit_z = unit_rows(bottleneck).astype(narrow)
    unit_protos = unit_rows(proto_rows.astype(single)).astype(narrow)
    logits = contract("grb,kb->grk", unit_z, unit_protos)
    return (
        logits,
        (chosen, normed, pre_one, hidden_one, pre_two, hidden_two, bottleneck, unit_z, unit_protos),
    )


def head_backward(grad_logits, stem_parts, saved, row_index, stream_shape):
    patch_w, position, extras, w_first, w_second, w_third = stem_parts
    extras = extras.astype(single)
    chosen, normed, pre_one, hidden_one, pre_two, hidden_two, bottleneck, unit_z, unit_protos = (
        saved
    )
    grad_rounded = grad_logits.astype(narrow)
    grad_unit_z = contract("grk,kb->grb", grad_rounded, unit_protos)
    grad_unit_protos = contract("grk,grb->kb", grad_rounded, unit_z)
    grad_bottle = jax.vjp(unit_rows, bottleneck)[1](grad_unit_z)[0].astype(narrow)
    grad_third = contract("grh,grb->hb", hidden_two, grad_bottle)
    grad_pre_two = gelu_back(pre_two, contract("grb,hb->grh", grad_bottle, w_third)).astype(narrow)
    grad_second = contract("grh,grk->hk", hidden_one, grad_pre_two)
    grad_pre_one = gelu_back(pre_one, contract("grk,hk->grh", grad_pre_two, w_second)).astype(
        narrow
    )
    grad_first = contract("grd,grh->dh", normed, grad_pre_one)
    grad_normed = contract("grh,dh->grd", grad_pre_one, w_first)
    grad_chosen, grad_gain, grad_bias = jax.vjp(layer_norm, chosen, extras[2], extras[3])[1](
        grad_normed
    )
    image_index = jnp.arange(row_index.shape[0], dtype=jnp.int32)[:, None]
    grad_stream = jnp.zeros(stream_shape, single).at[image_index, row_index].add(grad_chosen)
    return (
        grad_stream,
        (grad_first, grad_second, grad_third),
        grad_gain,
        grad_bias,
        grad_unit_protos,
    )


def adam_update(weight, moment, second, grad, teacher):
    new_moment = beta_one * moment + (1.0 - beta_one) * grad
    new_second = beta_two * second + (1.0 - beta_two) * grad * grad
    direction = (
        new_moment
        / (1.0 - beta_one**STEP)
        / (jnp.sqrt(new_second / (1.0 - beta_two**STEP)) + adam_eps)
    )
    new_weight = weight - learn_rate * (direction + decay_rate * weight)
    return (
        new_moment,
        new_second,
        new_weight,
        new_weight.astype(narrow),
        teacher_keep * teacher + (1.0 - teacher_keep) * new_weight,
    )


def spread_local(
    patches,
    masked,
    slot_used,
    stem,
    stem_moment,
    stem_second,
    stem_teacher,
    layers,
    layer_moment,
    layer_second,
    layer_teacher,
    protos,
    proto_moment,
    proto_second,
    proto_teacher,
    centre,
):
    images_here = patches.shape[0]
    row_index = jnp.concatenate([jnp.zeros((images_here, 1), jnp.int32), masked + 1], axis=1)
    masked_here = jnp.any(
        masked[:, :, None] == jnp.arange(PATCHES, dtype=jnp.int32)[None, None, :], axis=1
    )
    kept = slot_used.astype(single)
    teacher_flat, teacher_protos = (
        lax.all_gather(stem_teacher.astype(narrow), "dev", axis=0, tiled=True),
        lax.all_gather(proto_teacher.astype(narrow), "dev", axis=0, tiled=True),
    )
    teacher_parts = cut_flat(teacher_flat, stem_shapes())
    stream = embed(teacher_parts, patches, masked_here, False)
    for layer_index in range(LAYERS):
        teacher_layer = lax.all_gather(
            layer_teacher[layer_index].astype(narrow), "dev", axis=0, tiled=True
        )
        stream = block_forward(stream, cut_flat(teacher_layer, layer_shapes()))[0]
    teacher_logits = head_forward(teacher_parts, teacher_protos, stream, row_index)[0]
    teacher_probs = jax.nn.softmax((teacher_logits - centre) / tau_teacher, axis=-1)
    centre_terms = jnp.sum(kept[:, None] * teacher_logits[:, 0], axis=0)
    student_flat, student_protos = (
        lax.all_gather(stem.astype(narrow), "dev", axis=0, tiled=True),
        lax.all_gather(protos.astype(narrow), "dev", axis=0, tiled=True),
    )
    student_parts = cut_flat(student_flat, stem_shapes())
    stream = embed(student_parts, patches, masked_here, True)
    saved_layers = []
    gathered_layers = []
    for layer_index in range(LAYERS):
        layer_flat = lax.all_gather(layers[layer_index].astype(narrow), "dev", axis=0, tiled=True)
        gathered_layers.append(layer_flat)
        stream, saved = block_forward(stream, cut_flat(layer_flat, layer_shapes()))
        saved_layers.append(saved)
    logits, head_saved = head_forward(student_parts, student_protos, stream, row_index)

    def loss_piece(logit_rows):
        log_probs = jax.nn.log_softmax(logit_rows / tau_student, axis=-1)
        cross = -jnp.sum(teacher_probs * log_probs, axis=-1)
        return jnp.sum(kept * (cross[:, 0] + jnp.mean(cross[:, 1:], axis=1)))

    loss_local, loss_puller = jax.vjp(loss_piece, logits)
    grad_logits = loss_puller(jnp.float32(1.0))[0]
    count_local = jnp.sum(kept)
    loss_total, count_total, centre_total = lax.psum((loss_local, count_local, centre_terms), "dev")
    back_flat, back_protos = (
        lax.all_gather(stem.astype(narrow), "dev", axis=0, tiled=True),
        lax.all_gather(protos.astype(narrow), "dev", axis=0, tiled=True),
    )
    back_parts = cut_flat(back_flat, stem_shapes())
    grad_stream, head_grads, grad_gain, grad_bias, grad_unit_protos = head_backward(
        grad_logits, back_parts, head_saved, row_index, stream.shape
    )
    layer_grads = []
    for layer_index in reversed(range(LAYERS)):
        weight_flat = lax.all_gather(layers[layer_index].astype(narrow), "dev", axis=0, tiled=True)
        grad_stream, block_grads = block_backward(
            grad_stream, cut_flat(weight_flat, layer_shapes()), saved_layers[layer_index]
        )
        layer_grads.insert(
            0,
            lax.psum_scatter(
                pack_flat(block_grads, weight_flat.shape[0]), "dev", scatter_dimension=0, tiled=True
            ),
        )
    grad_patch_w, grad_position, grad_cls, grad_mask_token = embed_backward(
        grad_stream, patches, masked_here
    )
    grad_extras = jnp.stack([grad_cls, grad_mask_token, grad_gain, grad_bias])
    stem_flat_grad = pack_flat(
        (grad_patch_w, grad_position, grad_extras) + head_grads, back_flat.shape[0]
    )
    stem_grad, proto_row_grad = (
        lax.psum_scatter(stem_flat_grad, "dev", scatter_dimension=0, tiled=True),
        lax.psum_scatter(grad_unit_protos, "dev", scatter_dimension=0, tiled=True),
    )
    own_protos = lax.optimization_barrier(protos.astype(narrow)).astype(single)
    proto_grad = jax.vjp(unit_rows, own_protos)[1](proto_row_grad)[0]
    layer_grad = jnp.stack(layer_grads)
    square_local = (
        jnp.sum(stem_grad * stem_grad)
        + jnp.sum(layer_grad * layer_grad)
        + jnp.sum(proto_grad * proto_grad)
    )
    square_total = lax.psum(square_local, "dev")
    grad_norm = jnp.sqrt(square_total) / count_total
    factor = jnp.minimum(1.0, clip_limit / (grad_norm + 1e-06)) / count_total
    new_centre = centre_keep * centre + (1.0 - centre_keep) * centre_total / count_total
    stem_set = adam_update(stem, stem_moment, stem_second, stem_grad * factor, stem_teacher)
    layer_set = adam_update(layers, layer_moment, layer_second, layer_grad * factor, layer_teacher)
    proto_set = adam_update(protos, proto_moment, proto_second, proto_grad * factor, proto_teacher)
    return (
        loss_total,
        count_total,
        grad_norm,
        new_centre,
        stem_set[0],
        stem_set[1],
        stem_set[2],
        stem_set[3],
        stem_set[4],
        layer_set[0],
        layer_set[1],
        layer_set[2],
        layer_set[3],
        layer_set[4],
        proto_set[0],
        proto_set[1],
        proto_set[2],
        proto_set[3],
        proto_set[4],
    )


GROUP = 16
ROW = HID
MATRIX_ROWS = D * 3 + D + FF + FF
EMBED_ROWS = PIX + SEQ + 4
EMBED_FLAT = EMBED_ROWS * D
HEAD_ROWS = D + HID + BOT
BITS = ("b", "a", "y", "x", "c")
MASKS = {"c": 1, "x": 2, "y": 4, "a": 8, "b": 24, "g": 8}


def head_bounds(count, stem_piece):
    bounds = [-(-(stem_piece * device - EMBED_FLAT) // (ROW * GROUP)) * GROUP for device in range(count + 1)]
    bounds[0] = -(-EMBED_FLAT // (ROW * GROUP)) * -GROUP
    bounds[-1] = HEAD_ROWS
    return bounds


def fits(count, stem_piece, layer_piece):
    if count != 1 << len(BITS) or MATRIX_ROWS % (3 * count):
        return False
    bounds = head_bounds(count, stem_piece)
    sizes = [bounds[i + 1] - bounds[i] for i in range(count)]
    return (
        min(sizes) > GROUP
        and bounds[1] <= 0
        and stem_piece < EMBED_FLAT <= 2 * stem_piece
        and D in bounds
        and D + HID in bounds
        and stem_piece * count == EMBED_FLAT + HEAD_ROWS * ROW
    )


def pairs(count, mask):
    return [(i, i ^ mask) for i in range(count)]


def bit_flags(me):
    flags = {name: (me >> (len(BITS) - 1 - place)) & 1 for place, name in enumerate(BITS)}
    flags["g"] = flags["a"] ^ flags["b"]
    return flags


def cube_gather(part, order):
    count = 1 << len(BITS)
    flags = bit_flags(lax.axis_index("dev"))
    held = part[None]
    for name in order:
        got = lax.ppermute(held, "dev", pairs(count, MASKS[name]))
        held = jnp.where(
            flags[name] == 1,
            jnp.concatenate([got, held], axis=0),
            jnp.concatenate([held, got], axis=0),
        )
    return held


def cube_scatter(parts, orders, axes):
    count = 1 << len(BITS)
    flags = bit_flags(lax.axis_index("dev"))
    held = list(parts)
    names = [list(a) for a in axes]
    for turn in range(len(orders[0])):
        sent, kept = [], []
        for h, order, name in zip(held, orders, names):
            place = name.index(order[turn])
            low = lax.index_in_dim(h, 0, place, keepdims=False)
            high = lax.index_in_dim(h, 1, place, keepdims=False)
            flag = flags[order[turn]] == 1
            out = jnp.where(flag, low, high)
            sent.append(out if order[turn] == "c" else out.astype(narrow))
            kept.append(jnp.where(flag, high, low))
            name.pop(place)
        got = [
            lax.ppermute(s, "dev", pairs(count, MASKS[order[turn]])) for s, order in zip(sent, orders)
        ]
        held = [k + g.astype(single) for k, g in zip(kept, got)]
    return held


def cube_sum(values):
    for name in "cxyab":
        values = values + lax.ppermute(values, "dev", pairs(1 << len(BITS), MASKS[name]))
    return values


def split_bits(array):
    return array.reshape((2,) * len(BITS) + array.shape[1:])


def scatter_rows(array):
    half = array.shape[1] // 2
    done = cube_scatter(
        [split_bits(array[:, :half]), split_bits(array[:, half:])], ("cxyba", "cyxba"), (BITS, BITS)
    )
    return jnp.concatenate(done, axis=0)


def step_pairs(count, step):
    return [(i, i + step) for i in range(count) if 0 <= i + step < count]


def lane_rows(length):
    return -(-length // 1024) * 8


def as_lanes(flat):
    rows = lane_rows(flat.shape[-1])
    gap = rows * 128 - flat.shape[-1]
    padded = jnp.pad(flat, [(0, 0)] * (flat.ndim - 1) + [(0, gap)])
    return padded.reshape(flat.shape[:-1] + (rows, 128))


def shifted(line_ref, row, lane, first, rows, stride):
    spots = lax.broadcasted_iota(jnp.int32, (rows, 128), 1)
    turn = lax.rem(128 - lane, 128)
    here = pltpu.roll(line_ref[pl.ds(row + first, rows, stride=stride), :], turn, 1)
    there = pltpu.roll(line_ref[pl.ds(row + first + 1, rows, stride=stride), :], turn, 1)
    return jnp.where(spots < 128 - lane, here, there)


def blocks_kernel(
    shape,
    place_ref,
    stem_ref,
    after_ref,
    layer_ref,
    before_ref,
    head_ref,
    block_ref,
    embed_ref,
    vector_ref,
    line_ref,
    flat_ref,
):
    front, stem_piece, layer_piece, tail = shape
    stem_lines = stem_ref.shape[1]
    end_row, end_lane = stem_piece // 128, stem_piece % 128
    after_lines = after_ref.shape[1]
    slot = head_ref.shape[1]
    for model in range(2):
        line_ref[pl.ds(0, front), :] = jnp.zeros((front, 128), single)
        line_ref[pl.ds(front, end_row), :] = stem_ref[model, pl.ds(0, end_row), :]
        turned = pltpu.roll(after_ref[model], end_lane, 1)
        spots = lax.broadcasted_iota(jnp.int32, (after_lines, 128), 1)
        line_ref[pl.ds(front + end_row, after_lines), :] = turned
        line_ref[pl.ds(front + end_row + after_lines, 128), :] = jnp.zeros((128, 128), single)
        lower = pltpu.roll(turned, 1, 0)
        first_line = jnp.broadcast_to(stem_ref[model, pl.ds(end_row, 1), :], (after_lines, 128))
        number = lax.broadcasted_iota(jnp.int32, (after_lines, 128), 0)
        lower = jnp.where(number == 0, first_line, lower)
        line_ref[pl.ds(front + end_row, after_lines), :] = jnp.where(spots < end_lane, lower, turned)
        per_row = ROW // 128
        for chunk in range(per_row):
            head_ref[model, :, pl.ds(chunk * 128, 128)] = shifted(
                line_ref, place_ref[0], place_ref[1], chunk, slot, per_row
            ).astype(narrow)
        for chunk in range(D // 128):
            embed_ref[model, :, pl.ds(chunk * 128, 128)] = shifted(
                line_ref, place_ref[2], place_ref[3], chunk, embed_ref.shape[1], D // 128
            ).astype(narrow)
    tail_lines = tail // 128
    layer_lines = layer_ref.shape[1]
    vector_at = tail + layer_piece - tail
    for part in range(layer_ref.shape[0]):
        flat_ref[pl.ds(0, tail_lines), :] = before_ref[part]
        flat_ref[pl.ds(tail_lines, layer_lines), :] = layer_ref[part]
        for chunk in range(D // 128):
            block_ref[part, :, pl.ds(chunk * 128, 128)] = shifted(
                flat_ref, place_ref[4], place_ref[5], chunk, block_ref.shape[1], D // 128
            ).astype(narrow)
            vector_ref[part, :, pl.ds(chunk * 128, 128)] = shifted(
                flat_ref, vector_at // 128, vector_at % 128, chunk, 8, D // 128
            ).astype(narrow)


def own_blocks(place, stems, after, layer_rows, before, shape, slot, block_rows, embed_rows):
    front, stem_piece, layer_piece, tail = shape
    lines = front + stem_piece // 128 + after.shape[1] + slot * ROW // 128
    flats = tail // 128 + layer_rows.shape[1] + 48
    return pl.pallas_call(
        lambda *refs: blocks_kernel(shape, *refs),
        out_shape=[
            jax.ShapeDtypeStruct((2, slot, ROW), narrow),
            jax.ShapeDtypeStruct((2 * LAYERS, block_rows, D), narrow),
            jax.ShapeDtypeStruct((2, embed_rows, D), narrow),
            jax.ShapeDtypeStruct((2 * LAYERS, 8, D), narrow),
        ],
        in_specs=[pl.BlockSpec(memory_space=pltpu.SMEM)] + [pl.BlockSpec(memory_space=pltpu.VMEM)] * 4,
        out_specs=[pl.BlockSpec(memory_space=pltpu.VMEM)] * 4,
        scratch_shapes=[pltpu.VMEM((lines, 128), single), pltpu.VMEM((flats, 128), single)],
        compiler_params=pltpu.CompilerParams(vmem_limit_bytes=40 << 20),
    )(place, stems, after, layer_rows, before)


def shards_kernel(place_ref, head_ref, previous_ref, block_ref, behind_ref, stem_ref, layer_ref, line_ref, flat_ref):
    per_row = ROW // 128
    extra = previous_ref.shape[0]
    slot = head_ref.shape[0]
    for chunk in range(per_row):
        spot = pl.ds(chunk * 128, 128)
        line_ref[pl.ds(chunk, extra, stride=per_row), :] = previous_ref[:, spot]
        line_ref[pl.ds(extra * per_row + chunk, slot, stride=per_row), :] = head_ref[:, spot]
    stem_ref[...] = shifted(line_ref, place_ref[0], place_ref[1], 0, stem_ref.shape[0], 1)
    per_row = D // 128
    rows = block_ref.shape[1]
    for part in range(block_ref.shape[0]):
        for chunk in range(per_row):
            spot = pl.ds(chunk * 128, 128)
            flat_ref[pl.ds(chunk, rows, stride=per_row), :] = block_ref[part, :, spot]
            flat_ref[pl.ds(rows * per_row + chunk, 6, stride=per_row), :] = behind_ref[part, pl.ds(0, 6), spot]
        layer_ref[part] = shifted(flat_ref, place_ref[2], place_ref[3], 0, layer_ref.shape[1], 1)


def own_shards(place, head_grad, previous, block_grad, behind, stem_lines, layer_lines):
    per_row = ROW // 128
    lines = (head_grad.shape[0] + previous.shape[0]) * per_row + 256
    flats = max(block_grad.shape[1] * 3 + 18, layer_lines + 18) + 16
    return pl.pallas_call(
        shards_kernel,
        out_shape=[
            jax.ShapeDtypeStruct((stem_lines, 128), single),
            jax.ShapeDtypeStruct((block_grad.shape[0], layer_lines, 128), single),
        ],
        in_specs=[pl.BlockSpec(memory_space=pltpu.SMEM)] + [pl.BlockSpec(memory_space=pltpu.VMEM)] * 4,
        out_specs=[pl.BlockSpec(memory_space=pltpu.VMEM)] * 2,
        scratch_shapes=[pltpu.VMEM((lines, 128), single), pltpu.VMEM((flats, 128), single)],
        compiler_params=pltpu.CompilerParams(vmem_limit_bytes=40 << 20),
    )(place, head_grad, previous, block_grad, behind)


def close_local(
    patches,
    masked,
    slot_used,
    stem,
    stem_moment,
    stem_second,
    stem_teacher,
    layers,
    layer_moment,
    layer_second,
    layer_teacher,
    protos,
    proto_moment,
    proto_second,
    proto_teacher,
    centre,
):
    count = 1 << len(BITS)
    half = count // 2
    me = lax.axis_index("dev")
    across = MASKS["b"]
    student_side = me >= half
    groups = [list(range(half)), [i ^ across for i in range(half)]]
    images_here = patches.shape[0]
    rows_here = images_here * 17
    stem_piece = stem.shape[0]
    layer_piece = layers.shape[1]
    block_rows = MATRIX_ROWS // count
    block = block_rows * D
    tail = layer_piece * count - MATRIX_ROWS * D
    drift = layer_piece - block
    bounds = head_bounds(count, stem_piece)
    sizes = [bounds[i + 1] - bounds[i] for i in range(count)]
    slot = max(sizes)
    starts = [b * ROW + EMBED_FLAT - stem_piece * i for i, b in enumerate(bounds[:-1])]
    first_w2 = bounds.index(D)
    first_w3 = bounds.index(D + HID)
    row_index = jnp.concatenate([jnp.zeros((images_here, 1), jnp.int32), masked + 1], axis=1)
    masked_here = jnp.any(
        masked[:, :, None] == jnp.arange(PATCHES, dtype=jnp.int32)[None, None, :], axis=1
    )
    kept = slot_used.astype(single)

    front = 16
    early_rows = -(-stem_piece // D)
    late_start = early_rows * D - stem_piece
    embed_rows = -(-early_rows // 16) * 16
    own_layers = jnp.concatenate([layer_teacher, layers])
    own_tail = own_layers[:, layer_piece - tail :].reshape(2 * LAYERS, tail // 128, 128)
    before = lax.ppermute(own_tail, "dev", step_pairs(count, 1))
    head_span = GROUP * ROW
    stems = jnp.stack([as_lanes(stem_teacher), as_lanes(stem)])
    after = lax.ppermute(stems[:, : head_span // 128], "dev", step_pairs(count, -1))
    start_here = jnp.array(starts, jnp.int32)[me]
    head_at = start_here + front * 128
    embed_at = front * 128 + jnp.where(me == 0, 0, late_start)
    block_at = tail - drift * me
    place = jnp.stack(
        [head_at // 128, head_at % 128, embed_at // 128, embed_at % 128, block_at // 128, block_at % 128]
    ).astype(jnp.int32)
    head_blocks, layer_blocks, embed_blocks, vector_blocks = own_blocks(
        place,
        stems,
        after,
        as_lanes(own_layers),
        before,
        (front, stem_piece, layer_piece, tail),
        slot,
        block_rows,
        embed_rows,
    )

    other_layers = lax.ppermute(layer_blocks, "dev", pairs(count, across))
    both_layers = jnp.where(
        student_side,
        jnp.stack([other_layers, layer_blocks]),
        jnp.stack([layer_blocks, other_layers]),
    )
    gathered = lax.all_gather(both_layers, "dev", axis=0, axis_index_groups=groups)
    head_out = jnp.where(student_side, head_blocks[0], head_blocks[1])
    head_keep = jnp.where(student_side, head_blocks[1], head_blocks[0])
    head_got = lax.ppermute(head_out, "dev", pairs(count, across))
    both_head = jnp.where(
        student_side, jnp.stack([head_got, head_keep]), jnp.stack([head_keep, head_got])
    )
    gathered_head = lax.all_gather(both_head, "dev", axis=0, axis_index_groups=groups)

    vectors = lax.ppermute(vector_blocks, "dev", [(count - 1, 0)])
    seed = jnp.concatenate([embed_blocks.reshape(2 * embed_rows, D), vectors.reshape(8 * 2 * LAYERS, D)])
    third = -(-seed.shape[0] // 48) * 16
    spread_parts = []
    for number, order in enumerate(("xyba", "baxy", "ybax")):
        spread = seed[number * third : (number + 1) * third]
        reached = [0, 1]
        for name in order:
            moves = [(i, i ^ MASKS[name]) for i in reached]
            got = lax.ppermute(spread, "dev", moves)
            targets = [t for s, t in moves]
            is_target = jnp.array([i in targets for i in range(count)])[me]
            spread = jnp.where(is_target, got, spread)
            reached = reached + targets
        spread_parts.append(spread)
    spread = jnp.concatenate(spread_parts)
    other = lax.ppermute(spread, "dev", pairs(count, 1))
    is_even = me % 2 == 0
    even = jnp.where(is_even, spread, other)
    odd = jnp.where(is_even, other, spread)
    embed_all = [
        jnp.concatenate(
            [
                even[m * embed_rows : m * embed_rows + early_rows],
                odd[m * embed_rows : m * embed_rows + EMBED_ROWS - early_rows],
            ]
        )
        for m in range(2)
    ]
    vectors_all = even[2 * embed_rows :].reshape(2, LAYERS, 8, D)[:, :, :6]

    def layer_weights(model, layer_index):
        chosen = gathered[:, :, model * LAYERS + layer_index]
        flat = jnp.concatenate([chosen[:, 0], chosen[half // 2 :, 1], chosen[: half // 2, 1]]).reshape(MATRIX_ROWS, D)
        return (
            flat[: 3 * D].reshape(D, 3 * D),
            flat[3 * D : 4 * D],
            flat[4 * D : 4 * D + FF].reshape(D, FF),
            flat[4 * D + FF :],
            vectors_all[model, layer_index],
        )

    def head_slots(first, last):
        pieces = []
        i = first
        while i < last:
            side = i >= half
            at = i ^ across if side else i
            stop = i + 1
            while stop < last and (stop >= half) == side and (stop ^ across if side else stop) == at + stop - i:
                stop += 1
            pieces.append(gathered_head[at : at + stop - i, 1 if side else 0])
            i = stop
        return pieces

    def pad_columns(values, first, last, origin):
        pieces = []
        for i in range(first, last):
            low, high = bounds[i] - origin, bounds[i + 1] - origin
            if low < 0:
                pieces.append(jnp.zeros(values.shape[:-1] + (-low,), values.dtype))
            pieces.append(values[..., max(low, 0) : high])
            pieces.append(jnp.zeros(values.shape[:-1] + (slot - sizes[i],), values.dtype))
        return jnp.concatenate([p for p in pieces if p.shape[-1]], axis=-1)

    def cut_columns(values, first, last, origin):
        pieces = []
        for i in range(first, last):
            low = bounds[i] - origin
            at = (i - first) * slot
            pieces.append(values[..., at + max(-low, 0) : at + sizes[i]])
        return jnp.concatenate(pieces, axis=-1)

    def embed_parts(model):
        rows = embed_all[model]
        return (rows[:PIX], rows[PIX : PIX + SEQ], rows[PIX + SEQ :], None, None, None)

    def head_rows(stream, extras):
        chosen = jnp.take_along_axis(stream, row_index[:, :, None], axis=1).reshape(rows_here, D)
        normed = layer_norm(chosen, extras[2].astype(single), extras[3].astype(single)).astype(narrow)
        return chosen, normed

    student_parts = embed_parts(1)
    stream = embed(student_parts, patches, masked_here, True)
    saved_layers = []
    student_layers = []
    for layer_index in range(LAYERS):
        weights = layer_weights(1, layer_index)
        student_layers.append(weights)
        stream, saved = block_forward(stream, weights)
        saved_layers.append(saved)
    teacher_parts = embed_parts(0)
    teacher_stream = embed(teacher_parts, patches, masked_here, False)
    for layer_index in range(LAYERS):
        teacher_stream = block_forward(teacher_stream, layer_weights(0, layer_index))[0]
    chosen, student_normed = head_rows(stream, student_parts[2])
    teacher_normed = head_rows(teacher_stream, teacher_parts[2])[1]

    normed_got = lax.ppermute(
        jnp.where(student_side, teacher_normed, student_normed), "dev", pairs(count, across)
    )
    normed = jnp.where(
        student_side,
        jnp.concatenate([normed_got, student_normed]),
        jnp.concatenate([teacher_normed, normed_got]),
    )
    w_one = jnp.concatenate(head_slots(1, first_w2)).reshape(-1, ROW)
    w_two = jnp.concatenate(head_slots(first_w2, first_w3)).reshape(-1, ROW)
    w_three = jnp.concatenate(
        [head_slots(i, i + 1)[0][0, : sizes[i]] for i in range(first_w3, count)]
    ).reshape(HID, BOT)
    pre_one = contract("rd,dh->rh", pad_columns(normed, 1, first_w2, 0), w_one)
    hidden_one = jax.nn.gelu(pre_one).astype(narrow)
    pre_two = contract("rh,hk->rk", pad_columns(hidden_one, first_w2, first_w3, D), w_two)
    hidden_two = jax.nn.gelu(pre_two).astype(narrow)
    bottleneck = contract("rh,hb->rb", hidden_two, w_three)
    unit_z = unit_rows(bottleneck).astype(narrow)
    inputs_all = lax.all_gather(
        jnp.concatenate([normed, hidden_one, hidden_two], axis=1), "dev", axis=0, axis_index_groups=groups
    ).reshape(half * 2 * rows_here, D + 2 * HID)

    all_rows = count * rows_here
    kept_row = jnp.broadcast_to(kept[:, None], (images_here, 17)).reshape(1, rows_here)
    all_kept = cube_gather(kept_row, "bxygc").reshape(all_rows)
    z_pair = cube_gather(unit_z, "b")
    z_all = cube_gather(z_pair, "xygc")
    z_all = z_all.reshape(half, 2, 2 * rows_here, BOT)
    teacher_z_all = z_all[:, 0].reshape(all_rows, BOT)
    student_z_all = z_all[:, 1].reshape(all_rows, BOT)
    own_student = lax.optimization_barrier(protos.astype(narrow)).astype(single)
    own_teacher = lax.optimization_barrier(proto_teacher.astype(narrow)).astype(single)
    unit_student = unit_rows(own_student).astype(narrow)
    unit_teacher = unit_rows(own_teacher).astype(narrow)
    protos_here = protos.shape[0]
    own_centre = lax.dynamic_slice(centre, (me * protos_here,), (protos_here,))
    teacher_logits = contract("rb,kb->rk", teacher_z_all, unit_teacher)
    logits = contract("rb,kb->rk", student_z_all, unit_student)
    teacher_exp = jnp.exp((teacher_logits - own_centre) / tau_teacher)
    student_exp = jnp.exp(logits / tau_student)
    sums = jnp.stack(
        [
            jnp.sum(teacher_exp, axis=1),
            jnp.sum(student_exp, axis=1),
            jnp.sum(teacher_exp * logits, axis=1),
        ]
    )
    sums = cube_sum(sums)
    is_class = (jnp.arange(all_rows) % 17) == 0
    row_weight = all_kept * jnp.where(is_class, 1.0, 1.0 / 16.0)
    cross = jnp.log(sums[1]) - sums[2] / (sums[0] * tau_student)
    loss_total = jnp.sum(row_weight * cross)
    count_total = jnp.sum(jnp.where(is_class, all_kept, 0.0))
    centre_sum = jnp.sum(
        jnp.where(is_class, all_kept, 0.0)[:, None] * teacher_logits, axis=0
    )
    own_new_centre = centre_keep * own_centre + (1.0 - centre_keep) * centre_sum / count_total
    new_centre = cube_gather(own_new_centre.reshape(1, protos_here), "cxyab").reshape(-1)
    scale = row_weight / tau_student
    grad_logits = (
        student_exp * (scale / sums[1])[:, None] - teacher_exp * (scale / sums[0])[:, None]
    ).astype(narrow)
    z_partial = contract("rk,kb->rb", grad_logits, unit_student)
    proto_unit_grad = contract("rk,rb->kb", grad_logits, student_z_all)
    proto_grad = jax.vjp(unit_rows, own_student)[1](proto_unit_grad)[0]
    z_own = cube_scatter(
        [z_partial.reshape((2,) * 4 + (2 * rows_here, BOT))], ("cgyx",), ("cgyx",)
    )[0]
    grad_unit_z = z_own + lax.ppermute(z_own, "dev", [(i, i ^ across) for i in range(half)])

    grad_bottle = jax.vjp(unit_rows, bottleneck)[1](grad_unit_z)[0].astype(narrow)
    grad_pre_two = gelu_back(pre_two, contract("rb,hb->rh", grad_bottle, w_three)).astype(narrow)
    grad_hidden = cut_columns(contract("rk,hk->rh", grad_pre_two, w_two), first_w2, first_w3, D)
    grad_pre_one = gelu_back(pre_one, grad_hidden).astype(narrow)
    grad_normed = cut_columns(contract("rh,dh->rd", grad_pre_one, w_one), 1, first_w2, 0)
    grads_all = lax.all_gather(
        jnp.concatenate([grad_pre_one, grad_pre_two, grad_bottle], axis=1),
        "dev",
        axis=0,
        axis_index_groups=groups,
    ).reshape(half * 2 * rows_here, 2 * HID + BOT)
    normed_back = lax.ppermute(
        grad_normed[:rows_here], "dev", [(i, i ^ across) for i in range(half, count)]
    )
    own_grad_normed = jnp.where(student_side, grad_normed[rows_here:], normed_back)
    extras = student_parts[2].astype(single)
    grad_chosen, grad_gain, grad_bias = jax.vjp(layer_norm, chosen, extras[2], extras[3])[1](
        own_grad_normed
    )
    image_index = jnp.arange(images_here, dtype=jnp.int32)[:, None]
    grad_stream = (
        jnp.zeros(stream.shape, single)
        .at[image_index, row_index]
        .add(grad_chosen.reshape(images_here, 17, D))
    )

    layer_block_grads = [None] * LAYERS
    vector_grads = [None] * LAYERS
    for layer_index in reversed(range(LAYERS)):
        grad_stream, grads = block_backward(
            grad_stream, student_layers[layer_index], saved_layers[layer_index]
        )
        grad_qkv, grad_proj, grad_up, grad_down, vector_grads[layer_index] = grads
        flat = jnp.concatenate(
            [
                grad_qkv.reshape(3 * D, D),
                grad_proj,
                grad_up.reshape(FF, D),
                grad_down,
            ]
        ).reshape(count, block_rows, D)
        layer_block_grads[layer_index] = scatter_rows(flat)
    grad_patch_w, grad_position, grad_cls, grad_mask_token = embed_backward(
        grad_stream, patches, masked_here
    )
    small = jnp.concatenate(
        [
            grad_patch_w,
            grad_position,
            jnp.stack([grad_cls, grad_mask_token, grad_gain, grad_bias]),
        ]
        + vector_grads
    )
    small_rows = -(-small.shape[0] // count)
    small = jnp.pad(small, ((0, small_rows * count - small.shape[0]), (0, 0)))
    small_block = cube_scatter(
        [split_bits(small.reshape(count, small_rows, D))], ("cxyba",), (BITS,)
    )[0]
    layer_block = jnp.stack(layer_block_grads)

    padded = jnp.pad(inputs_all[:, : D + HID], ((0, 0), (-min(bounds[1], 0), slot)))

    def block_product(owner, grads):
        window = lax.dynamic_slice(
            padded, (0, jnp.array(bounds, jnp.int32)[owner] - bounds[1]), (all_rows, slot)
        )
        valid = jnp.arange(slot) < jnp.array(sizes, jnp.int32)[owner]
        return contract("rs,rh->sh", jnp.where(valid, window, 0), grads)

    partner = me ^ across
    grads_one, grads_two = grads_all[:, :HID], grads_all[:, HID : 2 * HID]
    third_from = [max(bounds[i] - (D + HID), 0) * (ROW // BOT) for i in range(count)]
    third_window = lax.dynamic_slice(
        jnp.pad(inputs_all[:, D + HID :], ((0, 0), (0, slot * ROW // BOT))),
        (0, jnp.array(third_from, jnp.int32)[me]),
        (all_rows, slot * ROW // BOT),
    )
    third_valid = jnp.arange(slot * ROW // BOT) < jnp.array(sizes, jnp.int32)[me] * (ROW // BOT)
    third_grad = contract(
        "rs,rb->sb", jnp.where(third_valid, third_window, 0), grads_all[:, 2 * HID :]
    ).reshape(slot, ROW)
    own_block_grad = jnp.where(me >= first_w3, third_grad, block_product(me, grads_two))
    partner_block_grad = block_product(partner, jnp.where(partner < first_w2, grads_one, grads_two))
    block_got = lax.ppermute(partner_block_grad, "dev", [(i, i ^ across) for i in range(half, count)])
    head_block_grad = jnp.where(student_side, own_block_grad, block_got)
    head_block_grad = jnp.where(me == 0, 0.0, head_block_grad)

    square_local = (
        jnp.sum(head_block_grad * head_block_grad)
        + jnp.sum(layer_block * layer_block)
        + jnp.sum(small_block * small_block)
        + jnp.sum(proto_grad * proto_grad)
    )
    square_total = cube_sum(square_local.reshape(1, 1))[0, 0]
    small_all = cube_gather(small_block, "cxyab").reshape(small_rows * count, D)
    embed_grad = small_all[:EMBED_ROWS].reshape(-1)
    vector_grad = small_all[EMBED_ROWS : EMBED_ROWS + 6 * LAYERS].reshape(LAYERS, 6, D)

    behind = lax.ppermute(layer_block[:, :6], "dev", step_pairs(count, -1))
    behind = jnp.where(me == count - 1, vector_grad, behind)
    last_rows = lax.dynamic_slice(
        head_block_grad, (jnp.array(sizes, jnp.int32)[me] - GROUP, 0), (GROUP, ROW)
    )
    previous = lax.ppermute(last_rows, "dev", step_pairs(count, 1))
    stem_at = head_span - start_here
    layer_at = drift * me
    place = jnp.stack([stem_at // 128, stem_at % 128, layer_at // 128, layer_at % 128]).astype(jnp.int32)
    stem_lines, layer_lines = own_shards(
        place, head_block_grad, previous, layer_block, behind, lane_rows(stem_piece), lane_rows(layer_piece)
    )
    layer_grad = layer_lines.reshape(LAYERS, -1)[:, :layer_piece]
    stem_grad = stem_lines.reshape(-1)[:stem_piece]
    rest = EMBED_FLAT - stem_piece
    second_part = jnp.concatenate([embed_grad[stem_piece:], stem_grad[rest:]])
    stem_grad = jnp.where(
        me == 0, embed_grad[:stem_piece], jnp.where(me == 1, second_part, stem_grad)
    )

    grad_norm = jnp.sqrt(square_total) / count_total
    factor = jnp.minimum(1.0, clip_limit / (grad_norm + 1e-06)) / count_total
    stem_set = adam_update(stem, stem_moment, stem_second, stem_grad * factor, stem_teacher)
    layer_set = adam_update(layers, layer_moment, layer_second, layer_grad * factor, layer_teacher)
    proto_set = adam_update(protos, proto_moment, proto_second, proto_grad * factor, proto_teacher)
    return (loss_total, count_total, grad_norm, new_centre) + stem_set + layer_set + proto_set


def solution(mesh):
    count = mesh.shape["dev"]
    stem_length = -(-(EMBED_FLAT + HEAD_ROWS * ROW) // count) * count
    close = fits(count, stem_length // count, (MATRIX_ROWS + 6) * D // count)
    placed = (
        P("dev", None, None),
        P("dev", None),
        P("dev"),
        P("dev"),
        P("dev"),
        P("dev"),
        P("dev"),
        P(None, "dev"),
        P(None, "dev"),
        P(None, "dev"),
        P(None, "dev"),
        P("dev", None),
        P("dev", None),
        P("dev", None),
        P("dev", None),
        P(),
    )
    return jax.shard_map(
        close_local if close else spread_local,
        mesh=mesh,
        in_specs=placed,
        out_specs=(
            P(),
            P(),
            P(),
            P(),
            P("dev"),
            P("dev"),
            P("dev"),
            P("dev"),
            P("dev"),
            P(None, "dev"),
            P(None, "dev"),
            P(None, "dev"),
            P(None, "dev"),
            P(None, "dev"),
            P("dev", None),
            P("dev", None),
            P("dev", None),
            P("dev", None),
            P("dev", None),
        ),
        check_vma=False,
    )
```

```python
import jax
import jax.numpy as jnp
from jax import lax
from jax.experimental import pallas as pl
from jax.experimental.pallas import tpu as pltpu
from jax.sharding import PartitionSpec as P

D = 384
HEADS = 6
HEAD_DIM = 64
FF = 1536
HID = 2048
BOT = 256
PIX = 588
PATCHES = 256
LAYERS = 2
STEP = 10
SEQ = 257


tau_student = 0.1
tau_teacher = 0.04
clip_limit = 0.003
learn_rate = 0.03
beta_one = 0.9
beta_two = 0.999
adam_eps = 1e-08
decay_rate = 0.04
teacher_keep = 0.8
centre_keep = 0.9
narrow = jnp.bfloat16
single = jnp.float32


def layer_shapes():
    return ((D, 3 * D), (D, D), (D, FF), (FF, D), (6, D))


def stem_shapes():
    return ((PIX, D), (SEQ, D), (4, D), (D, HID), (HID, HID), (HID, BOT))


def cut_flat(flat_row, shape_list):
    pieces = []
    offset = 0
    for shape_pair in shape_list:
        length = shape_pair[0] * shape_pair[1]
        pieces.append(flat_row[offset : offset + length].reshape(shape_pair))
        offset = offset + length
    return pieces


def pack_flat(grad_list, total_length):
    joined = jnp.concatenate([grad_item.reshape(-1) for grad_item in grad_list])
    return jnp.concatenate([joined, jnp.zeros((total_length - joined.shape[0],), single)])


def contract(form, left_arg, right_arg):
    return jnp.einsum(form, left_arg, right_arg, preferred_element_type=single)


def layer_norm(values, gain_row, bias_row):
    centred = values - jnp.mean(values, axis=-1, keepdims=True)
    spread = jnp.mean(centred * centred, axis=-1, keepdims=True)
    return centred * lax.rsqrt(spread + 1e-06) * gain_row + bias_row


def unit_rows(values):
    return values * lax.rsqrt(jnp.sum(values * values, axis=-1, keepdims=True) + 1e-06)


def gelu_back(pre_act, grad_act):
    return jax.vjp(jax.nn.gelu, pre_act)[1](grad_act)[0]


def block_forward(stream, weights):
    w_qkv, w_proj, w_up, w_down, vectors = weights
    vectors = vectors.astype(single)
    batch_size = stream.shape[0]
    normed = layer_norm(stream, vectors[0], vectors[1]).astype(narrow)
    packed = (
        contract("bsd,de->bse", normed, w_qkv)
        .astype(narrow)
        .reshape(batch_size, SEQ, 3, HEADS, HEAD_DIM)
    )
    scores = contract("bqhe,bkhe->bhqk", packed[:, :, 0], packed[:, :, 1]) * HEAD_DIM ** (-0.5)
    top_score = jnp.max(scores, axis=-1, keepdims=True)
    exp_terms = jnp.exp(scores - top_score)
    totals = jnp.sum(exp_terms, axis=-1, keepdims=True)
    log_total = top_score + jnp.log(totals)
    mixed = contract("bhqk,bkhe->bqhe", (exp_terms / totals).astype(narrow), packed[:, :, 2])
    mixed = mixed.astype(narrow).reshape(batch_size, SEQ, D)
    attn_out = contract("bsd,de->bse", mixed, w_proj)
    middle = stream + vectors[2] * attn_out
    normed_two = layer_norm(middle, vectors[3], vectors[4]).astype(narrow)
    pre_act = contract("bsd,df->bsf", normed_two, w_up)
    hidden = jax.nn.gelu(pre_act).astype(narrow)
    mlp_out = contract("bsf,fd->bsd", hidden, w_down)
    saved = (
        stream,
        normed,
        packed,
        log_total,
        mixed,
        attn_out,
        middle,
        normed_two,
        pre_act,
        hidden,
        mlp_out,
    )
    return (middle + vectors[5] * mlp_out, saved)


def block_backward(grad_out, weights, saved):
    w_qkv, w_proj, w_up, w_down, vectors = weights
    vectors = vectors.astype(single)
    (
        stream,
        normed,
        packed,
        log_total,
        mixed,
        attn_out,
        middle,
        normed_two,
        pre_act,
        hidden,
        mlp_out,
    ) = saved
    batch_size = stream.shape[0]
    score_scale = HEAD_DIM ** (-0.5)
    grad_ls_two = jnp.sum(grad_out * mlp_out, axis=(0, 1))
    grad_mlp = (grad_out * vectors[5]).astype(narrow)
    grad_down = contract("bsf,bsd->fd", hidden, grad_mlp)
    grad_pre = gelu_back(pre_act, contract("bsd,fd->bsf", grad_mlp, w_down)).astype(narrow)
    grad_up = contract("bsd,bsf->df", normed_two, grad_pre)
    grad_normed_two = contract("bsf,df->bsd", grad_pre, w_up)
    grad_mid, grad_gain_two, grad_bias_two = jax.vjp(layer_norm, middle, vectors[3], vectors[4])[1](
        grad_normed_two
    )
    grad_mid = grad_mid + grad_out
    grad_ls_one = jnp.sum(grad_mid * attn_out, axis=(0, 1))
    grad_attn = (grad_mid * vectors[2]).astype(narrow)
    grad_proj = contract("bsd,bse->de", mixed, grad_attn)
    grad_mixed = (
        contract("bse,de->bsd", grad_attn, w_proj)
        .astype(narrow)
        .reshape(batch_size, SEQ, HEADS, HEAD_DIM)
    )
    query_rows = packed[:, :, 0]
    key_rows = packed[:, :, 1]
    value_rows = packed[:, :, 2]
    probs = jnp.exp(contract("bqhe,bkhe->bhqk", query_rows, key_rows) * score_scale - log_total)
    grad_probs = contract("bqhe,bkhe->bhqk", grad_mixed, value_rows)
    grad_values = contract("bhqk,bqhe->bkhe", probs.astype(narrow), grad_mixed)
    grad_scores = probs * (grad_probs - jnp.sum(probs * grad_probs, axis=-1, keepdims=True))
    grad_raw = (grad_scores * score_scale).astype(narrow)
    grad_queries = contract("bhqk,bkhe->bqhe", grad_raw, key_rows)
    grad_keys = contract("bhqk,bqhe->bkhe", grad_raw, query_rows)
    grad_packed = (
        jnp.stack([grad_queries, grad_keys, grad_values], axis=2)
        .astype(narrow)
        .reshape(batch_size, SEQ, 3 * D)
    )
    grad_qkv = contract("bsd,bse->de", normed, grad_packed)
    grad_normed = contract("bse,de->bsd", grad_packed, w_qkv)
    grad_in, grad_gain_one, grad_bias_one = jax.vjp(layer_norm, stream, vectors[0], vectors[1])[1](
        grad_normed
    )
    grad_vectors = jnp.stack(
        [grad_gain_one, grad_bias_one, grad_ls_one, grad_gain_two, grad_bias_two, grad_ls_two]
    )
    return (grad_in + grad_mid, (grad_qkv, grad_proj, grad_up, grad_down, grad_vectors))


def embed(stem_parts, image_rows, masked_here, student):
    patch_w, position, extras, w_first, w_second, w_third = stem_parts
    extras = extras.astype(single)
    embedded = contract("gpc,cd->gpd", image_rows, patch_w)
    if student:
        embedded = jnp.where(masked_here[:, :, None], extras[1], embedded)
    cls_rows = jnp.broadcast_to(extras[0], (image_rows.shape[0], 1, D))
    return jnp.concatenate([cls_rows, embedded], axis=1) + position.astype(single)


def embed_backward(grad_stream, image_rows, masked_here):
    grad_cls = jnp.sum(grad_stream[:, 0], axis=0)
    grad_position = jnp.sum(grad_stream, axis=0)
    grad_patch_rows = grad_stream[:, 1:]
    grad_mask_token = jnp.sum(jnp.where(masked_here[:, :, None], grad_patch_rows, 0.0), axis=(0, 1))
    grad_embedded = jnp.where(masked_here[:, :, None], 0.0, grad_patch_rows).astype(narrow)
    grad_patch_w = contract("gpc,gpd->cd", image_rows, grad_embedded)
    return (grad_patch_w, grad_position, grad_cls, grad_mask_token)


def head_forward(stem_parts, proto_rows, stream, row_index):
    patch_w, position, extras, w_first, w_second, w_third = stem_parts
    extras = extras.astype(single)
    chosen = jnp.take_along_axis(stream, row_index[:, :, None], axis=1)
    normed = layer_norm(chosen, extras[2], extras[3]).astype(narrow)
    pre_one = contract("grd,dh->grh", normed, w_first)
    hidden_one = jax.nn.gelu(pre_one).astype(narrow)
    pre_two = contract("grh,hk->grk", hidden_one, w_second)
    hidden_two = jax.nn.gelu(pre_two).astype(narrow)
    bottleneck = contract("grh,hb->grb", hidden_two, w_third)
    unit_z = unit_rows(bottleneck).astype(narrow)
    unit_protos = unit_rows(proto_rows.astype(single)).astype(narrow)
    logits = contract("grb,kb->grk", unit_z, unit_protos)
    return (
        logits,
        (chosen, normed, pre_one, hidden_one, pre_two, hidden_two, bottleneck, unit_z, unit_protos),
    )


def head_backward(grad_logits, stem_parts, saved, row_index, stream_shape):
    patch_w, position, extras, w_first, w_second, w_third = stem_parts
    extras = extras.astype(single)
    chosen, normed, pre_one, hidden_one, pre_two, hidden_two, bottleneck, unit_z, unit_protos = (
        saved
    )
    grad_rounded = grad_logits.astype(narrow)
    grad_unit_z = contract("grk,kb->grb", grad_rounded, unit_protos)
    grad_unit_protos = contract("grk,grb->kb", grad_rounded, unit_z)
    grad_bottle = jax.vjp(unit_rows, bottleneck)[1](grad_unit_z)[0].astype(narrow)
    grad_third = contract("grh,grb->hb", hidden_two, grad_bottle)
    grad_pre_two = gelu_back(pre_two, contract("grb,hb->grh", grad_bottle, w_third)).astype(narrow)
    grad_second = contract("grh,grk->hk", hidden_one, grad_pre_two)
    grad_pre_one = gelu_back(pre_one, contract("grk,hk->grh", grad_pre_two, w_second)).astype(
        narrow
    )
    grad_first = contract("grd,grh->dh", normed, grad_pre_one)
    grad_normed = contract("grh,dh->grd", grad_pre_one, w_first)
    grad_chosen, grad_gain, grad_bias = jax.vjp(layer_norm, chosen, extras[2], extras[3])[1](
        grad_normed
    )
    image_index = jnp.arange(row_index.shape[0], dtype=jnp.int32)[:, None]
    grad_stream = jnp.zeros(stream_shape, single).at[image_index, row_index].add(grad_chosen)
    return (
        grad_stream,
        (grad_first, grad_second, grad_third),
        grad_gain,
        grad_bias,
        grad_unit_protos,
    )


def adam_update(weight, moment, second, grad, teacher):
    new_moment = beta_one * moment + (1.0 - beta_one) * grad
    new_second = beta_two * second + (1.0 - beta_two) * grad * grad
    direction = (
        new_moment
        / (1.0 - beta_one**STEP)
        / (jnp.sqrt(new_second / (1.0 - beta_two**STEP)) + adam_eps)
    )
    new_weight = weight - learn_rate * (direction + decay_rate * weight)
    return (
        new_moment,
        new_second,
        new_weight,
        new_weight.astype(narrow),
        teacher_keep * teacher + (1.0 - teacher_keep) * new_weight,
    )


def spread_local(
    patches,
    masked,
    slot_used,
    stem,
    stem_moment,
    stem_second,
    stem_teacher,
    layers,
    layer_moment,
    layer_second,
    layer_teacher,
    protos,
    proto_moment,
    proto_second,
    proto_teacher,
    centre,
):
    images_here = patches.shape[0]
    row_index = jnp.concatenate([jnp.zeros((images_here, 1), jnp.int32), masked + 1], axis=1)
    masked_here = jnp.any(
        masked[:, :, None] == jnp.arange(PATCHES, dtype=jnp.int32)[None, None, :], axis=1
    )
    kept = slot_used.astype(single)
    teacher_flat, teacher_protos = (
        lax.all_gather(stem_teacher.astype(narrow), "dev", axis=0, tiled=True),
        lax.all_gather(proto_teacher.astype(narrow), "dev", axis=0, tiled=True),
    )
    teacher_parts = cut_flat(teacher_flat, stem_shapes())
    stream = embed(teacher_parts, patches, masked_here, False)
    for layer_index in range(LAYERS):
        teacher_layer = lax.all_gather(
            layer_teacher[layer_index].astype(narrow), "dev", axis=0, tiled=True
        )
        stream = block_forward(stream, cut_flat(teacher_layer, layer_shapes()))[0]
    teacher_logits = head_forward(teacher_parts, teacher_protos, stream, row_index)[0]
    teacher_probs = jax.nn.softmax((teacher_logits - centre) / tau_teacher, axis=-1)
    centre_terms = jnp.sum(kept[:, None] * teacher_logits[:, 0], axis=0)
    student_flat, student_protos = (
        lax.all_gather(stem.astype(narrow), "dev", axis=0, tiled=True),
        lax.all_gather(protos.astype(narrow), "dev", axis=0, tiled=True),
    )
    student_parts = cut_flat(student_flat, stem_shapes())
    stream = embed(student_parts, patches, masked_here, True)
    saved_layers = []
    gathered_layers = []
    for layer_index in range(LAYERS):
        layer_flat = lax.all_gather(layers[layer_index].astype(narrow), "dev", axis=0, tiled=True)
        gathered_layers.append(layer_flat)
        stream, saved = block_forward(stream, cut_flat(layer_flat, layer_shapes()))
        saved_layers.append(saved)
    logits, head_saved = head_forward(student_parts, student_protos, stream, row_index)

    def loss_piece(logit_rows):
        log_probs = jax.nn.log_softmax(logit_rows / tau_student, axis=-1)
        cross = -jnp.sum(teacher_probs * log_probs, axis=-1)
        return jnp.sum(kept * (cross[:, 0] + jnp.mean(cross[:, 1:], axis=1)))

    loss_local, loss_puller = jax.vjp(loss_piece, logits)
    grad_logits = loss_puller(jnp.float32(1.0))[0]
    count_local = jnp.sum(kept)
    loss_total, count_total, centre_total = lax.psum((loss_local, count_local, centre_terms), "dev")
    back_flat, back_protos = (
        lax.all_gather(stem.astype(narrow), "dev", axis=0, tiled=True),
        lax.all_gather(protos.astype(narrow), "dev", axis=0, tiled=True),
    )
    back_parts = cut_flat(back_flat, stem_shapes())
    grad_stream, head_grads, grad_gain, grad_bias, grad_unit_protos = head_backward(
        grad_logits, back_parts, head_saved, row_index, stream.shape
    )
    layer_grads = []
    for layer_index in reversed(range(LAYERS)):
        weight_flat = lax.all_gather(layers[layer_index].astype(narrow), "dev", axis=0, tiled=True)
        grad_stream, block_grads = block_backward(
            grad_stream, cut_flat(weight_flat, layer_shapes()), saved_layers[layer_index]
        )
        layer_grads.insert(
            0,
            lax.psum_scatter(
                pack_flat(block_grads, weight_flat.shape[0]), "dev", scatter_dimension=0, tiled=True
            ),
        )
    grad_patch_w, grad_position, grad_cls, grad_mask_token = embed_backward(
        grad_stream, patches, masked_here
    )
    grad_extras = jnp.stack([grad_cls, grad_mask_token, grad_gain, grad_bias])
    stem_flat_grad = pack_flat(
        (grad_patch_w, grad_position, grad_extras) + head_grads, back_flat.shape[0]
    )
    stem_grad, proto_row_grad = (
        lax.psum_scatter(stem_flat_grad, "dev", scatter_dimension=0, tiled=True),
        lax.psum_scatter(grad_unit_protos, "dev", scatter_dimension=0, tiled=True),
    )
    own_protos = lax.optimization_barrier(protos.astype(narrow)).astype(single)
    proto_grad = jax.vjp(unit_rows, own_protos)[1](proto_row_grad)[0]
    layer_grad = jnp.stack(layer_grads)
    square_local = (
        jnp.sum(stem_grad * stem_grad)
        + jnp.sum(layer_grad * layer_grad)
        + jnp.sum(proto_grad * proto_grad)
    )
    square_total = lax.psum(square_local, "dev")
    grad_norm = jnp.sqrt(square_total) / count_total
    factor = jnp.minimum(1.0, clip_limit / (grad_norm + 1e-06)) / count_total
    new_centre = centre_keep * centre + (1.0 - centre_keep) * centre_total / count_total
    stem_set = adam_update(stem, stem_moment, stem_second, stem_grad * factor, stem_teacher)
    layer_set = adam_update(layers, layer_moment, layer_second, layer_grad * factor, layer_teacher)
    proto_set = adam_update(protos, proto_moment, proto_second, proto_grad * factor, proto_teacher)
    return (
        loss_total,
        count_total,
        grad_norm,
        new_centre,
        stem_set[0],
        stem_set[1],
        stem_set[2],
        stem_set[3],
        stem_set[4],
        layer_set[0],
        layer_set[1],
        layer_set[2],
        layer_set[3],
        layer_set[4],
        proto_set[0],
        proto_set[1],
        proto_set[2],
        proto_set[3],
        proto_set[4],
    )


GROUP = 16
ROW = HID
MATRIX_ROWS = D * 3 + D + FF + FF
EMBED_ROWS = PIX + SEQ + 4
EMBED_FLAT = EMBED_ROWS * D
HEAD_ROWS = D + HID + BOT
BITS = ("b", "a", "y", "x", "c")
MASKS = {"c": 1, "x": 2, "y": 4, "a": 8, "b": 24, "g": 8}


def head_bounds(count, stem_piece):
    bounds = [-(-(stem_piece * device - EMBED_FLAT) // (ROW * GROUP)) * GROUP for device in range(count + 1)]
    bounds[0] = -(-EMBED_FLAT // (ROW * GROUP)) * -GROUP
    bounds[-1] = HEAD_ROWS
    return bounds


def fits(count, stem_piece, layer_piece):
    if count != 1 << len(BITS) or MATRIX_ROWS % (3 * count):
        return False
    bounds = head_bounds(count, stem_piece)
    sizes = [bounds[i + 1] - bounds[i] for i in range(count)]
    return (
        min(sizes) > GROUP
        and bounds[1] <= 0
        and stem_piece < EMBED_FLAT <= 2 * stem_piece
        and D in bounds
        and D + HID in bounds
        and stem_piece * count == EMBED_FLAT + HEAD_ROWS * ROW
    )


def pairs(count, mask):
    return [(i, i ^ mask) for i in range(count)]


def bit_flags(me):
    flags = {name: (me >> (len(BITS) - 1 - place)) & 1 for place, name in enumerate(BITS)}
    flags["g"] = flags["a"] ^ flags["b"]
    return flags


def cube_gather(part, order):
    count = 1 << len(BITS)
    flags = bit_flags(lax.axis_index("dev"))
    held = part[None]
    for name in order:
        got = lax.ppermute(held, "dev", pairs(count, MASKS[name]))
        held = jnp.where(
            flags[name] == 1,
            jnp.concatenate([got, held], axis=0),
            jnp.concatenate([held, got], axis=0),
        )
    return held


def cube_scatter(parts, orders, axes, lead=0):
    count = 1 << len(BITS)
    flags = bit_flags(lax.axis_index("dev"))
    held = list(parts)
    names = [list(a) for a in axes]
    for turn in range(len(orders[0])):
        sent, kept = [], []
        for h, order, name in zip(held, orders, names):
            place = name.index(order[turn]) + lead
            low = lax.index_in_dim(h, 0, place, keepdims=False)
            high = lax.index_in_dim(h, 1, place, keepdims=False)
            flag = flags[order[turn]] == 1
            out = jnp.where(flag, low, high)
            sent.append(out if order[turn] == "c" else out.astype(narrow))
            kept.append(jnp.where(flag, high, low))
            name.pop(place - lead)
        got = [
            lax.ppermute(s, "dev", pairs(count, MASKS[order[turn]])) for s, order in zip(sent, orders)
        ]
        held = [k + g.astype(single) for k, g in zip(kept, got)]
    return held


def cube_sum(values):
    for name in "cxyab":
        values = values + lax.ppermute(values, "dev", pairs(1 << len(BITS), MASKS[name]))
    return values


def split_bits(array, lead=0):
    return array.reshape(array.shape[:lead] + (2,) * len(BITS) + array.shape[lead + 1 :])


def step_pairs(count, step):
    return [(i, i + step) for i in range(count) if 0 <= i + step < count]


def lane_rows(length):
    return -(-length // 1024) * 8


def as_lanes(flat):
    rows = lane_rows(flat.shape[-1])
    gap = rows * 128 - flat.shape[-1]
    padded = jnp.pad(flat, [(0, 0)] * (flat.ndim - 1) + [(0, gap)])
    return padded.reshape(flat.shape[:-1] + (rows, 128))


def shifted(line_ref, row, lane, first, rows, stride):
    spots = lax.broadcasted_iota(jnp.int32, (rows, 128), 1)
    turn = lax.rem(128 - lane, 128)
    here = pltpu.roll(line_ref[pl.ds(row + first, rows, stride=stride), :], turn, 1)
    there = pltpu.roll(line_ref[pl.ds(row + first + 1, rows, stride=stride), :], turn, 1)
    return jnp.where(spots < 128 - lane, here, there)


def blocks_kernel(
    shape,
    place_ref,
    stem_ref,
    after_ref,
    layer_ref,
    before_ref,
    head_ref,
    block_ref,
    embed_ref,
    vector_ref,
    line_ref,
    flat_ref,
):
    front, stem_piece, layer_piece, tail = shape
    stem_lines = stem_ref.shape[1]
    end_row, end_lane = stem_piece // 128, stem_piece % 128
    after_lines = after_ref.shape[1]
    slot = head_ref.shape[1]
    for model in range(2):
        line_ref[pl.ds(0, front), :] = jnp.zeros((front, 128), single)
        line_ref[pl.ds(front, end_row), :] = stem_ref[model, pl.ds(0, end_row), :]
        turned = pltpu.roll(after_ref[model], end_lane, 1)
        spots = lax.broadcasted_iota(jnp.int32, (after_lines, 128), 1)
        line_ref[pl.ds(front + end_row, after_lines), :] = turned
        line_ref[pl.ds(front + end_row + after_lines, 128), :] = jnp.zeros((128, 128), single)
        lower = pltpu.roll(turned, 1, 0)
        first_line = jnp.broadcast_to(stem_ref[model, pl.ds(end_row, 1), :], (after_lines, 128))
        number = lax.broadcasted_iota(jnp.int32, (after_lines, 128), 0)
        lower = jnp.where(number == 0, first_line, lower)
        line_ref[pl.ds(front + end_row, after_lines), :] = jnp.where(spots < end_lane, lower, turned)
        per_row = ROW // 128
        for chunk in range(per_row):
            head_ref[model, :, pl.ds(chunk * 128, 128)] = shifted(
                line_ref, place_ref[0], place_ref[1], chunk, slot, per_row
            ).astype(narrow)
        for chunk in range(D // 128):
            embed_ref[model, :, pl.ds(chunk * 128, 128)] = shifted(
                line_ref, place_ref[2], place_ref[3], chunk, embed_ref.shape[1], D // 128
            ).astype(narrow)
    tail_lines = tail // 128
    layer_lines = layer_ref.shape[1]
    vector_at = tail + layer_piece - tail
    for part in range(layer_ref.shape[0]):
        flat_ref[pl.ds(0, tail_lines), :] = before_ref[part]
        flat_ref[pl.ds(tail_lines, layer_lines), :] = layer_ref[part]
        for chunk in range(D // 128):
            block_ref[part, :, pl.ds(chunk * 128, 128)] = shifted(
                flat_ref, place_ref[4], place_ref[5], chunk, block_ref.shape[1], D // 128
            ).astype(narrow)
            vector_ref[part, :, pl.ds(chunk * 128, 128)] = shifted(
                flat_ref, vector_at // 128, vector_at % 128, chunk, 8, D // 128
            ).astype(narrow)


def own_blocks(place, stems, after, layer_rows, before, shape, slot, block_rows, embed_rows):
    front, stem_piece, layer_piece, tail = shape
    lines = front + stem_piece // 128 + after.shape[1] + slot * ROW // 128
    flats = tail // 128 + layer_rows.shape[1] + 48
    return pl.pallas_call(
        lambda *refs: blocks_kernel(shape, *refs),
        out_shape=[
            jax.ShapeDtypeStruct((2, slot, ROW), narrow),
            jax.ShapeDtypeStruct((2 * LAYERS, block_rows, D), narrow),
            jax.ShapeDtypeStruct((2, embed_rows, D), narrow),
            jax.ShapeDtypeStruct((2 * LAYERS, 8, D), narrow),
        ],
        in_specs=[pl.BlockSpec(memory_space=pltpu.SMEM)] + [pl.BlockSpec(memory_space=pltpu.VMEM)] * 4,
        out_specs=[pl.BlockSpec(memory_space=pltpu.VMEM)] * 4,
        scratch_shapes=[pltpu.VMEM((lines, 128), single), pltpu.VMEM((flats, 128), single)],
        compiler_params=pltpu.CompilerParams(vmem_limit_bytes=40 << 20),
    )(place, stems, after, layer_rows, before)


def shards_kernel(place_ref, head_ref, previous_ref, block_ref, behind_ref, stem_ref, layer_ref, line_ref, flat_ref):
    per_row = ROW // 128
    extra = previous_ref.shape[0]
    slot = head_ref.shape[0]
    for chunk in range(per_row):
        spot = pl.ds(chunk * 128, 128)
        line_ref[pl.ds(chunk, extra, stride=per_row), :] = previous_ref[:, spot]
        line_ref[pl.ds(extra * per_row + chunk, slot, stride=per_row), :] = head_ref[:, spot]
    stem_ref[...] = shifted(line_ref, place_ref[0], place_ref[1], 0, stem_ref.shape[0], 1)
    per_row = D // 128
    rows = block_ref.shape[2]
    for part in range(block_ref.shape[0]):
        for chunk in range(per_row):
            flat_ref[pl.ds(chunk, rows, stride=per_row), :] = block_ref[part, chunk]
            flat_ref[pl.ds(rows * per_row + chunk, 6, stride=per_row), :] = behind_ref[part, chunk]
        layer_ref[part] = shifted(flat_ref, place_ref[2], place_ref[3], 0, layer_ref.shape[1], 1)


def own_shards(place, head_grad, previous, block_grad, behind, stem_lines, layer_lines):
    per_row = ROW // 128
    lines = (head_grad.shape[0] + previous.shape[0]) * per_row + 256
    flats = max(block_grad.shape[2] * 3 + 18, layer_lines + 18) + 16
    return pl.pallas_call(
        shards_kernel,
        out_shape=[
            jax.ShapeDtypeStruct((stem_lines, 128), single),
            jax.ShapeDtypeStruct((block_grad.shape[0], layer_lines, 128), single),
        ],
        in_specs=[pl.BlockSpec(memory_space=pltpu.SMEM)] + [pl.BlockSpec(memory_space=pltpu.VMEM)] * 4,
        out_specs=[pl.BlockSpec(memory_space=pltpu.VMEM)] * 2,
        scratch_shapes=[pltpu.VMEM((lines, 128), single), pltpu.VMEM((flats, 128), single)],
        compiler_params=pltpu.CompilerParams(vmem_limit_bytes=40 << 20),
    )(place, head_grad, previous, block_grad, behind)


PAD_SEQ = 272
GELU_SCALE = 0.7978845608028654
GELU_CUBE = 0.044715


def product_plain(left, right):
    return lax.dot_general(left, right, (((1,), (0,)), ((), ())), preferred_element_type=single)


def product_right(left, right):
    return lax.dot_general(left, right, (((1,), (1,)), ((), ())), preferred_element_type=single)


def product_left(left, right):
    return lax.dot_general(left, right, (((0,), (0,)), ((), ())), preferred_element_type=single)


def norm_parts(values):
    centred = values - jnp.mean(values, axis=-1, keepdims=True)
    spread = lax.rsqrt(jnp.mean(centred * centred, axis=-1, keepdims=True) + 1e-06)
    return centred * spread, spread


def norm_back(grad, unit, spread, gain):
    grad_unit = grad * gain
    mean_one = jnp.mean(grad_unit, axis=-1, keepdims=True)
    mean_two = jnp.mean(grad_unit * unit, axis=-1, keepdims=True)
    return spread * (grad_unit - mean_one - unit * mean_two)


def gelu_tanh(values):
    return jnp.tanh(GELU_SCALE * (values + GELU_CUBE * values * values * values))


def fetch_rows(side_ref, part, gathered_ref, flat_ref, sems):
    quarter = flat_ref.shape[0] // 4
    side = side_ref[0]
    first, second = side * quarter, (1 - side) * quarter
    copies = [
        pltpu.make_async_copy(
            gathered_ref.at[pl.ds(at, quarter), owner, part],
            flat_ref.at[pl.ds(spot * quarter, quarter)],
            sems.at[spot],
        )
        for spot, (at, owner) in enumerate(((first, 0), (second, 0), (second, 1), (first, 1)))
    ]
    for copy in copies:
        copy.start()
    for copy in copies:
        copy.wait()


def matrix_rows(flat_ref, first_row, length):
    rows = flat_ref.shape[1]
    low, high = first_row // rows, -(-(first_row + length) // rows)
    lines = flat_ref[pl.ds(low, high - low)].reshape((high - low) * rows, D)
    at = first_row - low * rows
    return lines[at : at + length]


def spread_columns(flat_ref, first_row, width, wide_ref, out_ref):
    length = width * D
    lines = matrix_rows(flat_ref, first_row, length)
    for column in range(D // 128):
        lane = slice(column * 128, (column + 1) * 128)
        wide_ref[column, pl.ds(0, length), :] = lines[:, lane].astype(single)
    for group in range(width):
        for column in range(D // 128):
            out_ref[group, :, pl.ds(column * 128, 128)] = wide_ref[
                column, pl.ds(group, D, stride=width), :
            ].astype(narrow)


def head_lanes(values, odd):
    lanes = lax.broadcasted_iota(jnp.int32, values.shape, 1)
    return jnp.where((lanes >= HEAD_DIM) == odd, values, jnp.zeros_like(values))


def join_lanes(even, odd):
    lanes = lax.broadcasted_iota(jnp.int32, even.shape, 1)
    return jnp.where(lanes >= HEAD_DIM, odd, even)


def soft_rows(query, key):
    scores = product_right(query, key) * HEAD_DIM ** (-0.5)
    spots = lax.broadcasted_iota(jnp.int32, scores.shape, 1)
    scores = jnp.where(spots < SEQ, scores, -1e30)
    terms = jnp.exp(scores - jnp.max(scores, axis=-1, keepdims=True))
    return terms / jnp.sum(terms, axis=-1, keepdims=True)


def forward_kernel(part, keep, side_ref, stream_ref, vector_ref, gathered_ref, *refs):
    out_ref = refs[0]
    if keep:
        packed_ref, mixed_ref, attn_ref, pre_ref, mlp_ref = refs[1:6]
        flat_ref, wide_ref, qkv_ref, up_ref, hidden_ref, sems = refs[6:]
    else:
        flat_ref, wide_ref, qkv_ref, up_ref, hidden_ref, packed_ref, mixed_ref, sems = refs[1:]
    fetch_rows(side_ref, part, gathered_ref, flat_ref, sems)
    spread_columns(flat_ref, 0, 3, wide_ref, qkv_ref)
    spread_columns(flat_ref, 4 * D, FF // D, wide_ref, up_ref)
    w_proj = matrix_rows(flat_ref, 3 * D, D)
    w_down = matrix_rows(flat_ref, 4 * D + FF, FF)
    vectors = vector_ref[...].astype(single)
    stream = stream_ref[...]
    normed = (norm_parts(stream)[0] * vectors[0:1] + vectors[1:2]).astype(narrow)
    for group in range(3):
        packed_ref[:, pl.ds(group * D, D)] = product_plain(normed, qkv_ref[group]).astype(narrow)
    for image in range(stream.shape[0] // PAD_SEQ):
        rows = pl.ds(image * PAD_SEQ, PAD_SEQ)
        for pair in range(HEADS // 2):
            query, key, value = [
                packed_ref[rows, pl.ds(group * D + pair * 128, 128)] for group in range(3)
            ]
            done = [
                product_plain(soft_rows(head_lanes(query, odd), key).astype(narrow), value)
                for odd in (False, True)
            ]
            mixed_ref[rows, pl.ds(pair * 128, 128)] = join_lanes(*done).astype(narrow)
    attn = product_plain(mixed_ref[...], w_proj)
    middle = stream + vectors[2:3] * attn
    normed_two = (norm_parts(middle)[0] * vectors[3:4] + vectors[4:5]).astype(narrow)
    for group in range(FF // D):
        spot = pl.ds(group * D, D)
        pre = product_plain(normed_two, up_ref[group])
        if keep:
            pre_ref[:, spot] = pre
        hidden_ref[:, spot] = (0.5 * pre * (1.0 + gelu_tanh(pre))).astype(narrow)
    mlp = product_plain(hidden_ref[...], w_down)
    out_ref[...] = middle + vectors[5:6] * mlp
    if keep:
        attn_ref[...] = attn
        mlp_ref[...] = mlp


def layer_scratch(gathered):
    rows, blocks = gathered.shape[3], 2 * gathered.shape[0]
    return [
        pltpu.VMEM((blocks, rows, D), narrow),
        pltpu.VMEM((D // 128, FF, 128), single),
        pltpu.VMEM((3, D, D), narrow),
        pltpu.VMEM((FF // D, D, D), narrow),
    ]


def layer_specs_in(count):
    return (
        [pl.BlockSpec(memory_space=pltpu.SMEM)]
        + [pl.BlockSpec(memory_space=pltpu.VMEM)] * (count - 2)
        + [pl.BlockSpec(memory_space=pl.ANY)]
    )


def layer_forward(side, stream, vectors, gathered, part, keep):
    tokens = stream.shape[0]
    shapes = [jax.ShapeDtypeStruct((tokens, D), single)]
    extra = [
        jax.ShapeDtypeStruct((tokens, 3 * D), narrow),
        jax.ShapeDtypeStruct((tokens, D), narrow),
        jax.ShapeDtypeStruct((tokens, D), single),
        jax.ShapeDtypeStruct((tokens, FF), single),
        jax.ShapeDtypeStruct((tokens, D), single),
    ]
    scratch = layer_scratch(gathered) + [pltpu.VMEM((tokens, FF), narrow)]
    if keep:
        shapes = shapes + extra
    else:
        scratch = scratch + [pltpu.VMEM((tokens, 3 * D), narrow), pltpu.VMEM((tokens, D), narrow)]
    scratch.append(pltpu.SemaphoreType.DMA((4,)))
    return pl.pallas_call(
        lambda *refs: forward_kernel(part, keep, *refs),
        out_shape=shapes,
        in_specs=layer_specs_in(4),
        out_specs=[pl.BlockSpec(memory_space=pltpu.VMEM)] * len(shapes),
        scratch_shapes=scratch,
        compiler_params=pltpu.CompilerParams(vmem_limit_bytes=56 << 20),
        cost_estimate=pl.CostEstimate(flops=2 * 10**9, bytes_accessed=2 * 10**7, transcendentals=2 * 10**6),
    )(side, stream, vectors, gathered)


def mlp_back_kernel(
    part,
    side_ref,
    grad_ref,
    stream_ref,
    attn_ref,
    pre_ref,
    mlp_ref,
    vector_ref,
    gathered_ref,
    *refs,
):
    grad_mid_ref, all_grad_ref, vector_grad_ref = refs[-10:-7]
    flat_ref, wide_ref, up_ref, hidden_ref, grad_pre_ref, weight_grad_ref, sems = refs[-7:]
    fetch_rows(side_ref, part, gathered_ref, flat_ref, sems)
    spread_columns(flat_ref, 4 * D, FF // D, wide_ref, up_ref)
    w_down = matrix_rows(flat_ref, 4 * D + FF, FF)
    vectors = vector_ref[...].astype(single)
    grad_out = grad_ref[...]
    vector_grad_ref[...] = jnp.zeros_like(vector_grad_ref)
    attn = attn_ref[...]
    middle = stream_ref[...] + vectors[2:3] * attn
    unit_two, spread_two = norm_parts(middle)
    normed_two = (unit_two * vectors[3:4] + vectors[4:5]).astype(narrow)
    vector_grad_ref[pl.ds(5, 1), :] = jnp.sum(grad_out * mlp_ref[...], axis=0, keepdims=True)
    grad_mlp = (grad_out * vectors[5:6]).astype(narrow)
    grad_normed_two = jnp.zeros_like(grad_out)
    for group in range(FF // D):
        spot = pl.ds(group * D, D)
        pre = pre_ref[:, spot]
        bent = gelu_tanh(pre)
        hidden_ref[:, spot] = (0.5 * pre * (1.0 + bent)).astype(narrow)
        slope = 0.5 * (1.0 + bent) + 0.5 * pre * (1.0 - bent * bent) * GELU_SCALE * (
            1.0 + 3.0 * GELU_CUBE * pre * pre
        )
        grad_hidden = product_right(grad_mlp, w_down[group * D : (group + 1) * D])
        grad_pre = (grad_hidden * slope).astype(narrow)
        grad_pre_ref[:, spot] = grad_pre
        grad_normed_two = grad_normed_two + product_right(grad_pre, up_ref[group])
    for group in range(FF // D):
        spot = pl.ds(group * D, D)
        up_grad = product_left(normed_two, grad_pre_ref[:, spot])
        down_grad = product_left(hidden_ref[:, spot], grad_mlp)
        for column in range(D // 128):
            lane = slice(column * 128, (column + 1) * 128)
            weight_grad_ref[column, pl.ds(group, D, stride=FF // D), :] = up_grad[:, lane]
            weight_grad_ref[column, pl.ds(FF + group * D, D), :] = down_grad[:, lane]
    vector_grad_ref[pl.ds(3, 1), :] = jnp.sum(grad_normed_two * unit_two, axis=0, keepdims=True)
    vector_grad_ref[pl.ds(4, 1), :] = jnp.sum(grad_normed_two, axis=0, keepdims=True)
    grad_mid = grad_out + norm_back(grad_normed_two, unit_two, spread_two, vectors[3:4])
    vector_grad_ref[pl.ds(2, 1), :] = jnp.sum(grad_mid * attn, axis=0, keepdims=True)
    grad_mid_ref[...] = grad_mid
    store_rows(weight_grad_ref, all_grad_ref, 4 * D, sems.at[0])


def attention_back_kernel(
    part,
    side_ref,
    grad_ref,
    stream_ref,
    packed_ref,
    mixed_ref,
    vector_ref,
    gathered_ref,
    *refs,
):
    grad_in_ref, all_grad_ref, vector_grad_ref = refs[-10:-7]
    flat_ref, wide_ref, qkv_ref, grad_mixed_ref, grad_packed_ref, weight_grad_ref, sems = refs[-7:]
    fetch_rows(side_ref, part, gathered_ref, flat_ref, sems)
    spread_columns(flat_ref, 0, 3, wide_ref, qkv_ref)
    w_proj = matrix_rows(flat_ref, 3 * D, D)
    vectors = vector_ref[...].astype(single)
    vector_grad_ref[...] = jnp.zeros_like(vector_grad_ref)
    grad_mid = grad_ref[...]
    stream = stream_ref[...]
    grad_attn = (grad_mid * vectors[2:3]).astype(narrow)
    proj_grad = product_left(mixed_ref[...], grad_attn)
    for column in range(D // 128):
        weight_grad_ref[column, pl.ds(3 * D, D), :] = proj_grad[:, column * 128 : (column + 1) * 128]
    grad_mixed_ref[...] = product_right(grad_attn, w_proj).astype(narrow)
    for image in range(stream.shape[0] // PAD_SEQ):
        rows = pl.ds(image * PAD_SEQ, PAD_SEQ)
        for pair in range(HEADS // 2):
            query, key, value = [
                packed_ref[rows, pl.ds(group * D + pair * 128, 128)] for group in range(3)
            ]
            grad_mixed = grad_mixed_ref[rows, pl.ds(pair * 128, 128)]
            parts = []
            for odd in (False, True):
                probs = soft_rows(head_lanes(query, odd), key)
                grad_probs = product_right(head_lanes(grad_mixed, odd), value)
                grad_value = product_left(probs.astype(narrow), grad_mixed)
                grad_scores = probs * (grad_probs - jnp.sum(probs * grad_probs, axis=-1, keepdims=True))
                grad_raw = (grad_scores * HEAD_DIM ** (-0.5)).astype(narrow)
                parts.append((product_plain(grad_raw, key), product_left(grad_raw, query), grad_value))
            for group in range(3):
                grad_packed_ref[rows, pl.ds(group * D + pair * 128, 128)] = join_lanes(
                    parts[0][group], parts[1][group]
                ).astype(narrow)
    unit_one, spread_one = norm_parts(stream)
    normed = (unit_one * vectors[0:1] + vectors[1:2]).astype(narrow)
    grad_normed = jnp.zeros_like(grad_mid)
    for group in range(3):
        grad_part = grad_packed_ref[:, pl.ds(group * D, D)]
        grad_normed = grad_normed + product_right(grad_part, qkv_ref[group])
        qkv_grad = product_left(normed, grad_part)
        for column in range(D // 128):
            lane = slice(column * 128, (column + 1) * 128)
            weight_grad_ref[column, pl.ds(group, D, stride=3), :] = qkv_grad[:, lane]
    vector_grad_ref[pl.ds(0, 1), :] = jnp.sum(grad_normed * unit_one, axis=0, keepdims=True)
    vector_grad_ref[pl.ds(1, 1), :] = jnp.sum(grad_normed, axis=0, keepdims=True)
    grad_in_ref[...] = grad_mid + norm_back(grad_normed, unit_one, spread_one, vectors[0:1])
    store_rows(weight_grad_ref, all_grad_ref, 0, sems.at[0])


def store_rows(weight_grad_ref, all_grad_ref, first_row, sem):
    copy = pltpu.make_async_copy(
        weight_grad_ref, all_grad_ref.at[:, pl.ds(first_row, weight_grad_ref.shape[1])], sem
    )
    copy.start()
    copy.wait()


def layer_back(kernel, part, weight_rows, side, inputs, vectors, gathered, started, waits, columns, buffers):
    tokens = inputs[0].shape[0]
    rows, blocks = gathered.shape[3], 2 * gathered.shape[0]
    return pl.pallas_call(
        lambda *refs: kernel(part, *refs),
        out_shape=[
            jax.ShapeDtypeStruct((tokens, D), single),
            jax.ShapeDtypeStruct((D // 128, MATRIX_ROWS, 128), single),
            jax.ShapeDtypeStruct((8, D), single),
        ],
        in_specs=layer_specs_in(len(inputs) + 3)
        + [pl.BlockSpec(memory_space=pl.ANY)] * (len(started) + len(waits)),
        out_specs=[
            pl.BlockSpec(memory_space=pltpu.VMEM),
            pl.BlockSpec(memory_space=pl.ANY),
            pl.BlockSpec(memory_space=pltpu.VMEM),
        ],
        input_output_aliases={len(inputs) + 3: 1} if started else {},
        scratch_shapes=[
            pltpu.VMEM((blocks, rows, D), narrow),
            pltpu.VMEM((D // 128, columns * D, 128), single),
            pltpu.VMEM((columns, D, D), narrow),
        ]
        + [pltpu.VMEM((tokens, width), narrow) for width in buffers]
        + [pltpu.VMEM((D // 128, weight_rows, 128), single), pltpu.SemaphoreType.DMA((4,))],
        compiler_params=pltpu.CompilerParams(vmem_limit_bytes=56 << 20),
        cost_estimate=pl.CostEstimate(flops=5 * 10**9, bytes_accessed=4 * 10**7, transcendentals=2 * 10**6),
    )(side, *inputs, vectors, gathered, *started, *waits)


def mlp_back(side, grad_out, saved, vectors, gathered, part, waits):
    stream, packed, mixed, attn, pre, mlp = saved
    return layer_back(
        mlp_back_kernel, part, 2 * FF, side, (grad_out, stream, attn, pre, mlp), vectors, gathered, (), waits,
        FF // D, (FF, FF),
    )


def attention_back(side, grad_mid, saved, vectors, gathered, part, started, waits):
    stream, packed, mixed, attn, pre, mlp = saved
    return layer_back(
        attention_back_kernel, part, 4 * D, side, (grad_mid, stream, packed, mixed), vectors, gathered, (started,), waits,
        3, (D, 3 * D),
    )


def after_kernel(value_ref, token_ref, out_ref, sem):
    copy = pltpu.make_async_copy(value_ref, out_ref, sem)
    copy.start()
    copy.wait()


def after(value, token):
    return pl.pallas_call(
        after_kernel,
        out_shape=jax.ShapeDtypeStruct(value.shape, value.dtype),
        in_specs=[pl.BlockSpec(memory_space=pl.ANY)] * 2,
        out_specs=pl.BlockSpec(memory_space=pl.ANY),
        scratch_shapes=[pltpu.SemaphoreType.DMA(())],
    )(value, token)


def embed_back_kernel(grad_ref, patch_ref, shown_ref, gain_ref, vector_ref, out_ref):
    grad = grad_ref[...]
    images = grad.shape[0] // PAD_SEQ
    shown = shown_ref[...]
    position = jnp.zeros((PAD_SEQ, D), single)
    token = jnp.zeros((1, D), single)
    patch_grads = []
    for image in range(images):
        here = grad[image * PAD_SEQ : (image + 1) * PAD_SEQ]
        position = position + here
        rows = here[1:SEQ]
        seen = shown[image * PATCHES : (image + 1) * PATCHES]
        token = token + jnp.sum(rows * (1.0 - seen), axis=0, keepdims=True)
        patch_grads.append((rows * seen).astype(narrow))
    out_ref[...] = jnp.zeros_like(out_ref)
    out_ref[pl.ds(0, PIX), :] = product_left(patch_ref[...], jnp.concatenate(patch_grads))
    out_ref[pl.ds(PIX, SEQ), :] = position[:SEQ]
    out_ref[pl.ds(PIX + SEQ, 1), :] = position[0:1]
    out_ref[pl.ds(PIX + SEQ + 1, 1), :] = token
    out_ref[pl.ds(PIX + SEQ + 2, 2), :] = gain_ref[...]
    out_ref[pl.ds(EMBED_ROWS, vector_ref.shape[0]), :] = vector_ref[...]


def embed_back(grad, patch_rows, shown, gains, vector_grads, rows):
    return pl.pallas_call(
        embed_back_kernel,
        out_shape=jax.ShapeDtypeStruct((rows, D), single),
        in_specs=[pl.BlockSpec(memory_space=pltpu.VMEM)] * 5,
        out_specs=pl.BlockSpec(memory_space=pltpu.VMEM),
        compiler_params=pltpu.CompilerParams(vmem_limit_bytes=40 << 20),
    )(grad, patch_rows, shown, gains, vector_grads)


def close_local(
    patches,
    masked,
    slot_used,
    stem,
    stem_moment,
    stem_second,
    stem_teacher,
    layers,
    layer_moment,
    layer_second,
    layer_teacher,
    protos,
    proto_moment,
    proto_second,
    proto_teacher,
    centre,
):
    count = 1 << len(BITS)
    half = count // 2
    me = lax.axis_index("dev")
    across = MASKS["b"]
    student_side = me >= half
    groups = [list(range(half)), list(range(half, count))]
    quarter = half // 2
    swap = jnp.where(student_side, quarter, 0)
    side = student_side.astype(jnp.int32).reshape(1)
    images_here = patches.shape[0]
    rows_here = images_here * 17
    stem_piece = stem.shape[0]
    layer_piece = layers.shape[1]
    block_rows = MATRIX_ROWS // count
    block = block_rows * D
    tail = layer_piece * count - MATRIX_ROWS * D
    drift = layer_piece - block
    bounds = head_bounds(count, stem_piece)
    sizes = [bounds[i + 1] - bounds[i] for i in range(count)]
    slot = max(sizes)
    starts = [b * ROW + EMBED_FLAT - stem_piece * i for i, b in enumerate(bounds[:-1])]
    first_w2 = bounds.index(D)
    first_w3 = bounds.index(D + HID)
    row_index = jnp.concatenate([jnp.zeros((images_here, 1), jnp.int32), masked + 1], axis=1)
    masked_here = jnp.any(
        masked[:, :, None] == jnp.arange(PATCHES, dtype=jnp.int32)[None, None, :], axis=1
    )
    kept = slot_used.astype(single)

    front = 16
    early_rows = -(-stem_piece // D)
    late_start = early_rows * D - stem_piece
    embed_rows = -(-early_rows // 16) * 16
    own_layers = jnp.concatenate([layer_teacher, layers])
    own_tail = own_layers[:, layer_piece - tail :].reshape(2 * LAYERS, tail // 128, 128)
    before = lax.ppermute(own_tail, "dev", step_pairs(count, 1))
    head_span = GROUP * ROW
    stems = jnp.stack([as_lanes(stem_teacher), as_lanes(stem)])
    stems_next = lax.ppermute(stems[:, : head_span // 128], "dev", step_pairs(count, -1))
    start_here = jnp.array(starts, jnp.int32)[me]
    head_at = start_here + front * 128
    embed_at = front * 128 + jnp.where(me == 0, 0, late_start)
    block_at = tail - drift * me
    place = jnp.stack(
        [head_at // 128, head_at % 128, embed_at // 128, embed_at % 128, block_at // 128, block_at % 128]
    ).astype(jnp.int32)
    head_blocks, layer_blocks, embed_blocks, vector_blocks = own_blocks(
        place,
        stems,
        stems_next,
        as_lanes(own_layers),
        before,
        (front, stem_piece, layer_piece, tail),
        slot,
        block_rows,
        embed_rows,
    )

    other_layers = lax.ppermute(layer_blocks, "dev", pairs(count, across))
    both_layers = jnp.where(
        student_side,
        jnp.stack([other_layers, layer_blocks]),
        jnp.stack([layer_blocks, other_layers]),
    )
    gathered = lax.all_gather(both_layers, "dev", axis=0, axis_index_groups=groups)
    head_out = jnp.where(student_side, head_blocks[0], head_blocks[1])
    head_keep = jnp.where(student_side, head_blocks[1], head_blocks[0])
    head_got = lax.ppermute(head_out, "dev", pairs(count, across))
    both_head = jnp.where(
        student_side, jnp.stack([head_got, head_keep]), jnp.stack([head_keep, head_got])
    )
    gathered_head = lax.all_gather(after(both_head, gathered), "dev", axis=0, axis_index_groups=groups)

    vectors = lax.ppermute(vector_blocks, "dev", [(count - 1, 0)])
    seed = jnp.concatenate([embed_blocks.reshape(2 * embed_rows, D), vectors.reshape(8 * 2 * LAYERS, D)])
    third = -(-seed.shape[0] // 48) * 16
    spread_parts = []
    for number, order in enumerate(("xyba", "baxy", "ybax")):
        spread = seed[number * third : (number + 1) * third]
        reached = [0, 1]
        for name in order:
            moves = [(i, i ^ MASKS[name]) for i in reached]
            got = lax.ppermute(spread, "dev", moves)
            targets = [t for s, t in moves]
            is_target = jnp.array([i in targets for i in range(count)])[me]
            spread = jnp.where(is_target, got, spread)
            reached = reached + targets
        spread_parts.append(spread)
    spread = jnp.concatenate(spread_parts)
    other = lax.ppermute(spread, "dev", pairs(count, 1))
    is_even = me % 2 == 0
    even = jnp.where(is_even, spread, other)
    odd = jnp.where(is_even, other, spread)
    embed_all = [
        jnp.concatenate(
            [
                even[m * embed_rows : m * embed_rows + early_rows],
                odd[m * embed_rows : m * embed_rows + EMBED_ROWS - early_rows],
            ]
        )
        for m in range(2)
    ]
    vectors_all = even[2 * embed_rows :].reshape(2, LAYERS, 8, D)

    def head_slots(first, last):
        pieces = []
        i = first
        while i < last:
            stop = min(last, (i // quarter + 1) * quarter)
            owner = 1 if i >= half else 0
            at = (i ^ across if owner else i) ^ swap
            pieces.append(
                lax.dynamic_slice(
                    gathered_head, (at, owner, 0, 0), (stop - i, 1, slot, ROW)
                ).reshape(stop - i, slot, ROW)
            )
            i = stop
        return pieces

    def pad_columns(values, first, last, origin):
        pieces = []
        for i in range(first, last):
            low, high = bounds[i] - origin, bounds[i + 1] - origin
            if low < 0:
                pieces.append(jnp.zeros(values.shape[:-1] + (-low,), values.dtype))
            pieces.append(values[..., max(low, 0) : high])
            pieces.append(jnp.zeros(values.shape[:-1] + (slot - sizes[i],), values.dtype))
        return jnp.concatenate([p for p in pieces if p.shape[-1]], axis=-1)

    def cut_columns(values, first, last, origin):
        pieces = []
        for i in range(first, last):
            low = bounds[i] - origin
            at = (i - first) * slot
            pieces.append(values[..., at + max(-low, 0) : at + sizes[i]])
        return jnp.concatenate(pieces, axis=-1)

    def embed_parts(model):
        rows = embed_all[model]
        return (rows[:PIX], rows[PIX : PIX + SEQ], rows[PIX + SEQ :], None, None, None)

    def head_rows(stream, extras):
        chosen = jnp.take_along_axis(stream, row_index[:, :, None], axis=1).reshape(rows_here, D)
        normed = layer_norm(chosen, extras[2].astype(single), extras[3].astype(single)).astype(narrow)
        return chosen, normed

    def start_rows(parts, student):
        stream = embed(parts, patches, masked_here, student)
        return jnp.pad(stream, ((0, 0), (0, PAD_SEQ - SEQ), (0, 0))).reshape(images_here * PAD_SEQ, D)

    student_parts = embed_parts(1)
    stream = start_rows(student_parts, True)
    saved_layers = []
    for layer_index in range(LAYERS):
        before_layer = stream
        stream, *saved = layer_forward(
            side, stream, vectors_all[1, layer_index], gathered, LAYERS + layer_index, True
        )
        saved_layers.append((before_layer, *saved))
    teacher_parts = embed_parts(0)
    teacher_stream = start_rows(teacher_parts, False)
    for layer_index in range(LAYERS):
        teacher_stream = layer_forward(
            side, teacher_stream, vectors_all[0, layer_index], gathered, layer_index, False
        )[0]
    stream = stream.reshape(images_here, PAD_SEQ, D)
    teacher_stream = teacher_stream.reshape(images_here, PAD_SEQ, D)
    chosen, student_normed = head_rows(stream, student_parts[2])
    teacher_normed = head_rows(teacher_stream, teacher_parts[2])[1]

    normed_got = lax.ppermute(
        jnp.where(student_side, teacher_normed, student_normed), "dev", pairs(count, across)
    )
    normed = jnp.where(
        student_side,
        jnp.concatenate([normed_got, student_normed]),
        jnp.concatenate([teacher_normed, normed_got]),
    )
    w_one = jnp.concatenate(head_slots(1, first_w2)).reshape(-1, ROW)
    w_two = jnp.concatenate(head_slots(first_w2, first_w3)).reshape(-1, ROW)
    w_three = jnp.concatenate(
        [head_slots(i, i + 1)[0][0, : sizes[i]] for i in range(first_w3, count)]
    ).reshape(HID, BOT)
    pre_one = contract("rd,dh->rh", pad_columns(normed, 1, first_w2, 0), w_one)
    hidden_one = jax.nn.gelu(pre_one).astype(narrow)
    pre_two = contract("rh,hk->rk", pad_columns(hidden_one, first_w2, first_w3, D), w_two)
    hidden_two = jax.nn.gelu(pre_two).astype(narrow)
    bottleneck = contract("rh,hb->rb", hidden_two, w_three)
    unit_z = unit_rows(bottleneck).astype(narrow)
    pair_rows = -(-2 * rows_here // 16) * 16
    more_rows = ((0, pair_rows - 2 * rows_here), (0, 0))
    inputs_all = lax.all_gather(
        jnp.pad(jnp.concatenate([normed, hidden_one, hidden_two], axis=1), more_rows),
        "dev",
        axis=0,
        axis_index_groups=groups,
    ).reshape(half * pair_rows, D + 2 * HID)

    all_rows = count * rows_here
    kept_row = jnp.broadcast_to(kept[:, None], (images_here, 17)).reshape(1, rows_here)
    all_kept = cube_gather(kept_row, "bxygc").reshape(all_rows)
    z_pair = cube_gather(unit_z, "b")
    z_all = cube_gather(z_pair, "xygc")
    z_all = z_all.reshape(half, 2, 2 * rows_here, BOT)
    teacher_z_all = z_all[:, 0].reshape(all_rows, BOT)
    student_z_all = z_all[:, 1].reshape(all_rows, BOT)
    own_student = lax.optimization_barrier(protos.astype(narrow)).astype(single)
    own_teacher = lax.optimization_barrier(proto_teacher.astype(narrow)).astype(single)
    unit_student = unit_rows(own_student).astype(narrow)
    unit_teacher = unit_rows(own_teacher).astype(narrow)
    protos_here = protos.shape[0]
    own_centre = lax.dynamic_slice(centre, (me * protos_here,), (protos_here,))
    teacher_logits = contract("rb,kb->rk", teacher_z_all, unit_teacher)
    logits = contract("rb,kb->rk", student_z_all, unit_student)
    teacher_exp = jnp.exp((teacher_logits - own_centre) / tau_teacher)
    student_exp = jnp.exp(logits / tau_student)
    sums = jnp.stack(
        [
            jnp.sum(teacher_exp, axis=1),
            jnp.sum(student_exp, axis=1),
            jnp.sum(teacher_exp * logits, axis=1),
        ]
    )
    sums = cube_sum(sums)
    is_class = (jnp.arange(all_rows) % 17) == 0
    row_weight = all_kept * jnp.where(is_class, 1.0, 1.0 / 16.0)
    cross = jnp.log(sums[1]) - sums[2] / (sums[0] * tau_student)
    loss_total = jnp.sum(row_weight * cross)
    count_total = jnp.sum(jnp.where(is_class, all_kept, 0.0))
    centre_sum = jnp.sum(
        jnp.where(is_class, all_kept, 0.0)[:, None] * teacher_logits, axis=0
    )
    own_new_centre = centre_keep * own_centre + (1.0 - centre_keep) * centre_sum / count_total
    new_centre = cube_gather(own_new_centre.reshape(1, protos_here), "cxyab").reshape(-1)
    scale = row_weight / tau_student
    grad_logits = (
        student_exp * (scale / sums[1])[:, None] - teacher_exp * (scale / sums[0])[:, None]
    ).astype(narrow)
    z_partial = contract("rk,kb->rb", grad_logits, unit_student)
    proto_unit_grad = contract("rk,rb->kb", grad_logits, student_z_all)
    proto_grad = jax.vjp(unit_rows, own_student)[1](proto_unit_grad)[0]
    z_own = cube_scatter(
        [z_partial.reshape((2,) * 4 + (2 * rows_here, BOT))], ("cgyx",), ("cgyx",)
    )[0]
    grad_unit_z = z_own + lax.ppermute(z_own, "dev", [(i, i ^ across) for i in range(half)])

    grad_bottle = jax.vjp(unit_rows, bottleneck)[1](grad_unit_z)[0].astype(narrow)
    grad_pre_two = gelu_back(pre_two, contract("rb,hb->rh", grad_bottle, w_three)).astype(narrow)
    grad_hidden = cut_columns(contract("rk,hk->rh", grad_pre_two, w_two), first_w2, first_w3, D)
    grad_pre_one = gelu_back(pre_one, grad_hidden).astype(narrow)
    grad_normed = cut_columns(contract("rh,dh->rd", grad_pre_one, w_one), 1, first_w2, 0)
    grads_all = lax.all_gather(
        jnp.pad(jnp.concatenate([grad_pre_one, grad_pre_two, grad_bottle], axis=1), more_rows),
        "dev",
        axis=0,
        axis_index_groups=groups,
    ).reshape(half * pair_rows, 2 * HID + BOT)
    normed_back = lax.ppermute(
        grad_normed[:rows_here], "dev", [(i, i ^ across) for i in range(half, count)]
    )
    own_grad_normed = jnp.where(student_side, grad_normed[rows_here:], normed_back)
    extras = student_parts[2].astype(single)
    grad_chosen, grad_gain, grad_bias = jax.vjp(layer_norm, chosen, extras[2], extras[3])[1](
        own_grad_normed
    )
    image_index = jnp.arange(images_here, dtype=jnp.int32)[:, None]
    grad_stream = (
        jnp.zeros(stream.shape, single)
        .at[image_index, row_index]
        .add(grad_chosen.reshape(images_here, 17, D))
    )

    grad_stream = grad_stream.reshape(images_here * PAD_SEQ, D)
    middle_row = block_rows // 2
    moving = []
    vector_grads = [None] * LAYERS
    for layer_index in reversed(range(LAYERS)):
        saved, vectors = saved_layers[layer_index], vectors_all[1, layer_index]
        part = LAYERS + layer_index
        grad_stream, weight_grad, late_vectors = mlp_back(
            side, grad_stream, saved, vectors, gathered, part, ()
        )
        grad_stream, weight_grad, early_vectors = attention_back(
            side, grad_stream, saved, vectors, gathered, part, weight_grad, moving
        )
        vector_grads[layer_index] = (late_vectors + early_vectors)[:6]
        owned = split_bits(weight_grad.reshape(D // 128, count, block_rows, 128), 1)
        first = cube_scatter([owned], ("c",), (BITS,), 1)[0]
        moving = (first,)
        layer_first = [first] if layer_index == LAYERS - 1 else [first] + layer_first
    layer_block = jnp.stack(
        [
            jnp.concatenate(
                cube_scatter(
                    [first[..., :middle_row, :], first[..., middle_row:, :]],
                    ("xyba", "yxba"),
                    (BITS[:-1], BITS[:-1]),
                    1,
                ),
                axis=1,
            )
            for first in layer_first
        ]
    )
    small_rows = -(-(EMBED_ROWS + 6 * LAYERS) // count)
    small = embed_back(
        grad_stream,
        patches.reshape(images_here * PATCHES, PIX),
        jnp.where(masked_here, 0.0, 1.0).reshape(images_here * PATCHES, 1),
        jnp.stack([grad_gain, grad_bias]),
        jnp.concatenate(vector_grads),
        small_rows * count,
    )
    small_block = cube_scatter(
        [split_bits(small.reshape(count, small_rows, D))], ("cxyba",), (BITS,)
    )[0]

    padded = jnp.pad(inputs_all[:, : D + HID], ((0, 0), (-min(bounds[1], 0), slot)))

    def block_product(owner, grads):
        window = lax.dynamic_slice(
            padded, (0, jnp.array(bounds, jnp.int32)[owner] - bounds[1]), (half * pair_rows, slot)
        )
        valid = jnp.arange(slot) < jnp.array(sizes, jnp.int32)[owner]
        return contract("rs,rh->sh", jnp.where(valid, window, 0), grads)

    partner = me ^ across
    grads_one, grads_two = grads_all[:, :HID], grads_all[:, HID : 2 * HID]
    third_from = [max(bounds[i] - (D + HID), 0) * (ROW // BOT) for i in range(count)]
    third_window = lax.dynamic_slice(
        jnp.pad(inputs_all[:, D + HID :], ((0, 0), (0, slot * ROW // BOT))),
        (0, jnp.array(third_from, jnp.int32)[me]),
        (half * pair_rows, slot * ROW // BOT),
    )
    third_valid = jnp.arange(slot * ROW // BOT) < jnp.array(sizes, jnp.int32)[me] * (ROW // BOT)
    third_grad = contract(
        "rs,rb->sb", jnp.where(third_valid, third_window, 0), grads_all[:, 2 * HID :]
    ).reshape(slot, ROW)
    own_block_grad = jnp.where(me >= first_w3, third_grad, block_product(me, grads_two))
    partner_block_grad = block_product(partner, jnp.where(partner < first_w2, grads_one, grads_two))
    block_got = lax.ppermute(partner_block_grad, "dev", [(i, i ^ across) for i in range(half, count)])
    head_block_grad = jnp.where(student_side, own_block_grad, block_got)
    head_block_grad = jnp.where(me == 0, 0.0, head_block_grad)

    square_local = (
        jnp.sum(head_block_grad * head_block_grad)
        + jnp.sum(layer_block * layer_block)
        + jnp.sum(small_block * small_block)
        + jnp.sum(proto_grad * proto_grad)
    )
    square_total = cube_sum(square_local.reshape(1, 1))[0, 0]
    small_all = cube_gather(small_block, "cxyab").reshape(small_rows * count, D)
    embed_grad = small_all[:EMBED_ROWS].reshape(-1)
    vector_grad = small_all[EMBED_ROWS : EMBED_ROWS + 6 * LAYERS].reshape(LAYERS, 6, D)

    behind = lax.ppermute(layer_block[:, :, :6], "dev", step_pairs(count, -1))
    vector_columns = jnp.swapaxes(vector_grad.reshape(LAYERS, 6, D // 128, 128), 1, 2)
    behind = jnp.where(me == count - 1, vector_columns, behind)
    last_rows = lax.dynamic_slice(
        head_block_grad, (jnp.array(sizes, jnp.int32)[me] - GROUP, 0), (GROUP, ROW)
    )
    previous = lax.ppermute(last_rows, "dev", step_pairs(count, 1))
    stem_at = head_span - start_here
    layer_at = drift * me
    place = jnp.stack([stem_at // 128, stem_at % 128, layer_at // 128, layer_at % 128]).astype(jnp.int32)
    stem_lines, layer_lines = own_shards(
        place, head_block_grad, previous, layer_block, behind, lane_rows(stem_piece), lane_rows(layer_piece)
    )
    layer_grad = layer_lines.reshape(LAYERS, -1)[:, :layer_piece]
    stem_grad = stem_lines.reshape(-1)[:stem_piece]
    rest = EMBED_FLAT - stem_piece
    second_part = jnp.concatenate([embed_grad[stem_piece:], stem_grad[rest:]])
    stem_grad = jnp.where(
        me == 0, embed_grad[:stem_piece], jnp.where(me == 1, second_part, stem_grad)
    )

    grad_norm = jnp.sqrt(square_total) / count_total
    factor = jnp.minimum(1.0, clip_limit / (grad_norm + 1e-06)) / count_total
    stem_set = adam_update(stem, stem_moment, stem_second, stem_grad * factor, stem_teacher)
    layer_set = adam_update(layers, layer_moment, layer_second, layer_grad * factor, layer_teacher)
    proto_set = adam_update(protos, proto_moment, proto_second, proto_grad * factor, proto_teacher)
    return (loss_total, count_total, grad_norm, new_centre) + stem_set + layer_set + proto_set


def solution(mesh):
    count = mesh.shape["dev"]
    stem_length = -(-(EMBED_FLAT + HEAD_ROWS * ROW) // count) * count
    close = fits(count, stem_length // count, (MATRIX_ROWS + 6) * D // count)
    placed = (
        P("dev", None, None),
        P("dev", None),
        P("dev"),
        P("dev"),
        P("dev"),
        P("dev"),
        P("dev"),
        P(None, "dev"),
        P(None, "dev"),
        P(None, "dev"),
        P(None, "dev"),
        P("dev", None),
        P("dev", None),
        P("dev", None),
        P("dev", None),
        P(),
    )
    return jax.shard_map(
        close_local if close else spread_local,
        mesh=mesh,
        in_specs=placed,
        out_specs=(
            P(),
            P(),
            P(),
            P(),
            P("dev"),
            P("dev"),
            P("dev"),
            P("dev"),
            P("dev"),
            P(None, "dev"),
            P(None, "dev"),
            P(None, "dev"),
            P(None, "dev"),
            P(None, "dev"),
            P("dev", None),
            P("dev", None),
            P("dev", None),
            P("dev", None),
            P("dev", None),
        ),
        check_vma=False,
    )
```

```python
import jax
import jax.numpy as jnp
from jax import lax
from jax.experimental import pallas as pl
from jax.experimental.pallas import tpu as pltpu
from jax.sharding import PartitionSpec as P

D = 384
HEADS = 6
HEAD_DIM = 64
FF = 1536
HID = 2048
BOT = 256
PIX = 588
PATCHES = 256
LAYERS = 2
STEP = 10
SEQ = 257


tau_student = 0.1
tau_teacher = 0.04
clip_limit = 0.003
learn_rate = 0.03
beta_one = 0.9
beta_two = 0.999
adam_eps = 1e-08
decay_rate = 0.04
teacher_keep = 0.8
centre_keep = 0.9
narrow = jnp.bfloat16
single = jnp.float32


def layer_shapes():
    return ((D, 3 * D), (D, D), (D, FF), (FF, D), (6, D))


def stem_shapes():
    return ((PIX, D), (SEQ, D), (4, D), (D, HID), (HID, HID), (HID, BOT))


def cut_flat(flat_row, shape_list):
    pieces = []
    offset = 0
    for shape_pair in shape_list:
        length = shape_pair[0] * shape_pair[1]
        pieces.append(flat_row[offset : offset + length].reshape(shape_pair))
        offset = offset + length
    return pieces


def pack_flat(grad_list, total_length):
    joined = jnp.concatenate([grad_item.reshape(-1) for grad_item in grad_list])
    return jnp.concatenate([joined, jnp.zeros((total_length - joined.shape[0],), single)])


def contract(form, left_arg, right_arg):
    return jnp.einsum(form, left_arg, right_arg, preferred_element_type=single)


def layer_norm(values, gain_row, bias_row):
    centred = values - jnp.mean(values, axis=-1, keepdims=True)
    spread = jnp.mean(centred * centred, axis=-1, keepdims=True)
    return centred * lax.rsqrt(spread + 1e-06) * gain_row + bias_row


def unit_rows(values):
    return values * lax.rsqrt(jnp.sum(values * values, axis=-1, keepdims=True) + 1e-06)


def gelu_back(pre_act, grad_act):
    return jax.vjp(jax.nn.gelu, pre_act)[1](grad_act)[0]


def block_forward(stream, weights):
    w_qkv, w_proj, w_up, w_down, vectors = weights
    vectors = vectors.astype(single)
    batch_size = stream.shape[0]
    normed = layer_norm(stream, vectors[0], vectors[1]).astype(narrow)
    packed = (
        contract("bsd,de->bse", normed, w_qkv)
        .astype(narrow)
        .reshape(batch_size, SEQ, 3, HEADS, HEAD_DIM)
    )
    scores = contract("bqhe,bkhe->bhqk", packed[:, :, 0], packed[:, :, 1]) * HEAD_DIM ** (-0.5)
    top_score = jnp.max(scores, axis=-1, keepdims=True)
    exp_terms = jnp.exp(scores - top_score)
    totals = jnp.sum(exp_terms, axis=-1, keepdims=True)
    log_total = top_score + jnp.log(totals)
    mixed = contract("bhqk,bkhe->bqhe", (exp_terms / totals).astype(narrow), packed[:, :, 2])
    mixed = mixed.astype(narrow).reshape(batch_size, SEQ, D)
    attn_out = contract("bsd,de->bse", mixed, w_proj)
    middle = stream + vectors[2] * attn_out
    normed_two = layer_norm(middle, vectors[3], vectors[4]).astype(narrow)
    pre_act = contract("bsd,df->bsf", normed_two, w_up)
    hidden = jax.nn.gelu(pre_act).astype(narrow)
    mlp_out = contract("bsf,fd->bsd", hidden, w_down)
    saved = (
        stream,
        normed,
        packed,
        log_total,
        mixed,
        attn_out,
        middle,
        normed_two,
        pre_act,
        hidden,
        mlp_out,
    )
    return (middle + vectors[5] * mlp_out, saved)


def block_backward(grad_out, weights, saved):
    w_qkv, w_proj, w_up, w_down, vectors = weights
    vectors = vectors.astype(single)
    (
        stream,
        normed,
        packed,
        log_total,
        mixed,
        attn_out,
        middle,
        normed_two,
        pre_act,
        hidden,
        mlp_out,
    ) = saved
    batch_size = stream.shape[0]
    score_scale = HEAD_DIM ** (-0.5)
    grad_ls_two = jnp.sum(grad_out * mlp_out, axis=(0, 1))
    grad_mlp = (grad_out * vectors[5]).astype(narrow)
    grad_down = contract("bsf,bsd->fd", hidden, grad_mlp)
    grad_pre = gelu_back(pre_act, contract("bsd,fd->bsf", grad_mlp, w_down)).astype(narrow)
    grad_up = contract("bsd,bsf->df", normed_two, grad_pre)
    grad_normed_two = contract("bsf,df->bsd", grad_pre, w_up)
    grad_mid, grad_gain_two, grad_bias_two = jax.vjp(layer_norm, middle, vectors[3], vectors[4])[1](
        grad_normed_two
    )
    grad_mid = grad_mid + grad_out
    grad_ls_one = jnp.sum(grad_mid * attn_out, axis=(0, 1))
    grad_attn = (grad_mid * vectors[2]).astype(narrow)
    grad_proj = contract("bsd,bse->de", mixed, grad_attn)
    grad_mixed = (
        contract("bse,de->bsd", grad_attn, w_proj)
        .astype(narrow)
        .reshape(batch_size, SEQ, HEADS, HEAD_DIM)
    )
    query_rows = packed[:, :, 0]
    key_rows = packed[:, :, 1]
    value_rows = packed[:, :, 2]
    probs = jnp.exp(contract("bqhe,bkhe->bhqk", query_rows, key_rows) * score_scale - log_total)
    grad_probs = contract("bqhe,bkhe->bhqk", grad_mixed, value_rows)
    grad_values = contract("bhqk,bqhe->bkhe", probs.astype(narrow), grad_mixed)
    grad_scores = probs * (grad_probs - jnp.sum(probs * grad_probs, axis=-1, keepdims=True))
    grad_raw = (grad_scores * score_scale).astype(narrow)
    grad_queries = contract("bhqk,bkhe->bqhe", grad_raw, key_rows)
    grad_keys = contract("bhqk,bqhe->bkhe", grad_raw, query_rows)
    grad_packed = (
        jnp.stack([grad_queries, grad_keys, grad_values], axis=2)
        .astype(narrow)
        .reshape(batch_size, SEQ, 3 * D)
    )
    grad_qkv = contract("bsd,bse->de", normed, grad_packed)
    grad_normed = contract("bse,de->bsd", grad_packed, w_qkv)
    grad_in, grad_gain_one, grad_bias_one = jax.vjp(layer_norm, stream, vectors[0], vectors[1])[1](
        grad_normed
    )
    grad_vectors = jnp.stack(
        [grad_gain_one, grad_bias_one, grad_ls_one, grad_gain_two, grad_bias_two, grad_ls_two]
    )
    return (grad_in + grad_mid, (grad_qkv, grad_proj, grad_up, grad_down, grad_vectors))


def embed(stem_parts, image_rows, masked_here, student):
    patch_w, position, extras, w_first, w_second, w_third = stem_parts
    extras = extras.astype(single)
    embedded = contract("gpc,cd->gpd", image_rows, patch_w)
    if student:
        embedded = jnp.where(masked_here[:, :, None], extras[1], embedded)
    cls_rows = jnp.broadcast_to(extras[0], (image_rows.shape[0], 1, D))
    return jnp.concatenate([cls_rows, embedded], axis=1) + position.astype(single)


def embed_backward(grad_stream, image_rows, masked_here):
    grad_cls = jnp.sum(grad_stream[:, 0], axis=0)
    grad_position = jnp.sum(grad_stream, axis=0)
    grad_patch_rows = grad_stream[:, 1:]
    grad_mask_token = jnp.sum(jnp.where(masked_here[:, :, None], grad_patch_rows, 0.0), axis=(0, 1))
    grad_embedded = jnp.where(masked_here[:, :, None], 0.0, grad_patch_rows).astype(narrow)
    grad_patch_w = contract("gpc,gpd->cd", image_rows, grad_embedded)
    return (grad_patch_w, grad_position, grad_cls, grad_mask_token)


def head_forward(stem_parts, proto_rows, stream, row_index):
    patch_w, position, extras, w_first, w_second, w_third = stem_parts
    extras = extras.astype(single)
    chosen = jnp.take_along_axis(stream, row_index[:, :, None], axis=1)
    normed = layer_norm(chosen, extras[2], extras[3]).astype(narrow)
    pre_one = contract("grd,dh->grh", normed, w_first)
    hidden_one = jax.nn.gelu(pre_one).astype(narrow)
    pre_two = contract("grh,hk->grk", hidden_one, w_second)
    hidden_two = jax.nn.gelu(pre_two).astype(narrow)
    bottleneck = contract("grh,hb->grb", hidden_two, w_third)
    unit_z = unit_rows(bottleneck).astype(narrow)
    unit_protos = unit_rows(proto_rows.astype(single)).astype(narrow)
    logits = contract("grb,kb->grk", unit_z, unit_protos)
    return (
        logits,
        (chosen, normed, pre_one, hidden_one, pre_two, hidden_two, bottleneck, unit_z, unit_protos),
    )


def head_backward(grad_logits, stem_parts, saved, row_index, stream_shape):
    patch_w, position, extras, w_first, w_second, w_third = stem_parts
    extras = extras.astype(single)
    chosen, normed, pre_one, hidden_one, pre_two, hidden_two, bottleneck, unit_z, unit_protos = (
        saved
    )
    grad_rounded = grad_logits.astype(narrow)
    grad_unit_z = contract("grk,kb->grb", grad_rounded, unit_protos)
    grad_unit_protos = contract("grk,grb->kb", grad_rounded, unit_z)
    grad_bottle = jax.vjp(unit_rows, bottleneck)[1](grad_unit_z)[0].astype(narrow)
    grad_third = contract("grh,grb->hb", hidden_two, grad_bottle)
    grad_pre_two = gelu_back(pre_two, contract("grb,hb->grh", grad_bottle, w_third)).astype(narrow)
    grad_second = contract("grh,grk->hk", hidden_one, grad_pre_two)
    grad_pre_one = gelu_back(pre_one, contract("grk,hk->grh", grad_pre_two, w_second)).astype(
        narrow
    )
    grad_first = contract("grd,grh->dh", normed, grad_pre_one)
    grad_normed = contract("grh,dh->grd", grad_pre_one, w_first)
    grad_chosen, grad_gain, grad_bias = jax.vjp(layer_norm, chosen, extras[2], extras[3])[1](
        grad_normed
    )
    image_index = jnp.arange(row_index.shape[0], dtype=jnp.int32)[:, None]
    grad_stream = jnp.zeros(stream_shape, single).at[image_index, row_index].add(grad_chosen)
    return (
        grad_stream,
        (grad_first, grad_second, grad_third),
        grad_gain,
        grad_bias,
        grad_unit_protos,
    )


def adam_update(weight, moment, second, grad, teacher):
    new_moment = beta_one * moment + (1.0 - beta_one) * grad
    new_second = beta_two * second + (1.0 - beta_two) * grad * grad
    direction = (
        new_moment
        / (1.0 - beta_one**STEP)
        / (jnp.sqrt(new_second / (1.0 - beta_two**STEP)) + adam_eps)
    )
    new_weight = weight - learn_rate * (direction + decay_rate * weight)
    return (
        new_moment,
        new_second,
        new_weight,
        new_weight.astype(narrow),
        teacher_keep * teacher + (1.0 - teacher_keep) * new_weight,
    )


def spread_local(
    patches,
    masked,
    slot_used,
    stem,
    stem_moment,
    stem_second,
    stem_teacher,
    layers,
    layer_moment,
    layer_second,
    layer_teacher,
    protos,
    proto_moment,
    proto_second,
    proto_teacher,
    centre,
):
    images_here = patches.shape[0]
    row_index = jnp.concatenate([jnp.zeros((images_here, 1), jnp.int32), masked + 1], axis=1)
    masked_here = jnp.any(
        masked[:, :, None] == jnp.arange(PATCHES, dtype=jnp.int32)[None, None, :], axis=1
    )
    kept = slot_used.astype(single)
    teacher_flat, teacher_protos = (
        lax.all_gather(stem_teacher.astype(narrow), "dev", axis=0, tiled=True),
        lax.all_gather(proto_teacher.astype(narrow), "dev", axis=0, tiled=True),
    )
    teacher_parts = cut_flat(teacher_flat, stem_shapes())
    stream = embed(teacher_parts, patches, masked_here, False)
    for layer_index in range(LAYERS):
        teacher_layer = lax.all_gather(
            layer_teacher[layer_index].astype(narrow), "dev", axis=0, tiled=True
        )
        stream = block_forward(stream, cut_flat(teacher_layer, layer_shapes()))[0]
    teacher_logits = head_forward(teacher_parts, teacher_protos, stream, row_index)[0]
    teacher_probs = jax.nn.softmax((teacher_logits - centre) / tau_teacher, axis=-1)
    centre_terms = jnp.sum(kept[:, None] * teacher_logits[:, 0], axis=0)
    student_flat, student_protos = (
        lax.all_gather(stem.astype(narrow), "dev", axis=0, tiled=True),
        lax.all_gather(protos.astype(narrow), "dev", axis=0, tiled=True),
    )
    student_parts = cut_flat(student_flat, stem_shapes())
    stream = embed(student_parts, patches, masked_here, True)
    saved_layers = []
    gathered_layers = []
    for layer_index in range(LAYERS):
        layer_flat = lax.all_gather(layers[layer_index].astype(narrow), "dev", axis=0, tiled=True)
        gathered_layers.append(layer_flat)
        stream, saved = block_forward(stream, cut_flat(layer_flat, layer_shapes()))
        saved_layers.append(saved)
    logits, head_saved = head_forward(student_parts, student_protos, stream, row_index)

    def loss_piece(logit_rows):
        log_probs = jax.nn.log_softmax(logit_rows / tau_student, axis=-1)
        cross = -jnp.sum(teacher_probs * log_probs, axis=-1)
        return jnp.sum(kept * (cross[:, 0] + jnp.mean(cross[:, 1:], axis=1)))

    loss_local, loss_puller = jax.vjp(loss_piece, logits)
    grad_logits = loss_puller(jnp.float32(1.0))[0]
    count_local = jnp.sum(kept)
    loss_total, count_total, centre_total = lax.psum((loss_local, count_local, centre_terms), "dev")
    back_flat, back_protos = (
        lax.all_gather(stem.astype(narrow), "dev", axis=0, tiled=True),
        lax.all_gather(protos.astype(narrow), "dev", axis=0, tiled=True),
    )
    back_parts = cut_flat(back_flat, stem_shapes())
    grad_stream, head_grads, grad_gain, grad_bias, grad_unit_protos = head_backward(
        grad_logits, back_parts, head_saved, row_index, stream.shape
    )
    layer_grads = []
    for layer_index in reversed(range(LAYERS)):
        weight_flat = lax.all_gather(layers[layer_index].astype(narrow), "dev", axis=0, tiled=True)
        grad_stream, block_grads = block_backward(
            grad_stream, cut_flat(weight_flat, layer_shapes()), saved_layers[layer_index]
        )
        layer_grads.insert(
            0,
            lax.psum_scatter(
                pack_flat(block_grads, weight_flat.shape[0]), "dev", scatter_dimension=0, tiled=True
            ),
        )
    grad_patch_w, grad_position, grad_cls, grad_mask_token = embed_backward(
        grad_stream, patches, masked_here
    )
    grad_extras = jnp.stack([grad_cls, grad_mask_token, grad_gain, grad_bias])
    stem_flat_grad = pack_flat(
        (grad_patch_w, grad_position, grad_extras) + head_grads, back_flat.shape[0]
    )
    stem_grad, proto_row_grad = (
        lax.psum_scatter(stem_flat_grad, "dev", scatter_dimension=0, tiled=True),
        lax.psum_scatter(grad_unit_protos, "dev", scatter_dimension=0, tiled=True),
    )
    own_protos = lax.optimization_barrier(protos.astype(narrow)).astype(single)
    proto_grad = jax.vjp(unit_rows, own_protos)[1](proto_row_grad)[0]
    layer_grad = jnp.stack(layer_grads)
    square_local = (
        jnp.sum(stem_grad * stem_grad)
        + jnp.sum(layer_grad * layer_grad)
        + jnp.sum(proto_grad * proto_grad)
    )
    square_total = lax.psum(square_local, "dev")
    grad_norm = jnp.sqrt(square_total) / count_total
    factor = jnp.minimum(1.0, clip_limit / (grad_norm + 1e-06)) / count_total
    new_centre = centre_keep * centre + (1.0 - centre_keep) * centre_total / count_total
    stem_set = adam_update(stem, stem_moment, stem_second, stem_grad * factor, stem_teacher)
    layer_set = adam_update(layers, layer_moment, layer_second, layer_grad * factor, layer_teacher)
    proto_set = adam_update(protos, proto_moment, proto_second, proto_grad * factor, proto_teacher)
    return (
        loss_total,
        count_total,
        grad_norm,
        new_centre,
        stem_set[0],
        stem_set[1],
        stem_set[2],
        stem_set[3],
        stem_set[4],
        layer_set[0],
        layer_set[1],
        layer_set[2],
        layer_set[3],
        layer_set[4],
        proto_set[0],
        proto_set[1],
        proto_set[2],
        proto_set[3],
        proto_set[4],
    )


GROUP = 16
ROW = HID
MATRIX_ROWS = D * 3 + D + FF + FF
EMBED_ROWS = PIX + SEQ + 4
EMBED_FLAT = EMBED_ROWS * D
HEAD_ROWS = D + HID + BOT
BITS = ("b", "a", "y", "x", "c")
MASKS = {"c": 1, "x": 2, "y": 4, "a": 8, "b": 24, "g": 8}


def head_bounds(count, stem_piece):
    bounds = [-(-(stem_piece * device - EMBED_FLAT) // (ROW * GROUP)) * GROUP for device in range(count + 1)]
    bounds[0] = -(-EMBED_FLAT // (ROW * GROUP)) * -GROUP
    bounds[-1] = HEAD_ROWS
    return bounds


def fits(count, stem_piece, layer_piece):
    if count != 1 << len(BITS) or MATRIX_ROWS % (3 * count):
        return False
    bounds = head_bounds(count, stem_piece)
    sizes = [bounds[i + 1] - bounds[i] for i in range(count)]
    return (
        min(sizes) > GROUP
        and bounds[1] <= 0
        and stem_piece < EMBED_FLAT <= 2 * stem_piece
        and D in bounds
        and D + HID in bounds
        and stem_piece * count == EMBED_FLAT + HEAD_ROWS * ROW
    )


def pairs(count, mask):
    return [(i, i ^ mask) for i in range(count)]


def bit_flags(me):
    flags = {name: (me >> (len(BITS) - 1 - place)) & 1 for place, name in enumerate(BITS)}
    flags["g"] = flags["a"] ^ flags["b"]
    return flags


def cube_gather(part, order):
    count = 1 << len(BITS)
    flags = bit_flags(lax.axis_index("dev"))
    held = part[None]
    for name in order:
        got = lax.ppermute(held, "dev", pairs(count, MASKS[name]))
        held = jnp.where(
            flags[name] == 1,
            jnp.concatenate([got, held], axis=0),
            jnp.concatenate([held, got], axis=0),
        )
    return held


def cube_scatter(parts, orders, axes, lead=0):
    count = 1 << len(BITS)
    flags = bit_flags(lax.axis_index("dev"))
    held = list(parts)
    names = [list(a) for a in axes]
    for turn in range(len(orders[0])):
        sent, kept = [], []
        for h, order, name in zip(held, orders, names):
            place = name.index(order[turn]) + lead
            low = lax.index_in_dim(h, 0, place, keepdims=False)
            high = lax.index_in_dim(h, 1, place, keepdims=False)
            flag = flags[order[turn]] == 1
            out = jnp.where(flag, low, high)
            sent.append(out if order[turn] == "c" else out.astype(narrow))
            kept.append(jnp.where(flag, high, low))
            name.pop(place - lead)
        got = [
            lax.ppermute(s, "dev", pairs(count, MASKS[order[turn]])) for s, order in zip(sent, orders)
        ]
        held = [k + g.astype(single) for k, g in zip(kept, got)]
    return held


def cube_sum(values):
    for name in "cxyab":
        values = values + lax.ppermute(values, "dev", pairs(1 << len(BITS), MASKS[name]))
    return values


def split_bits(array, lead=0):
    return array.reshape(array.shape[:lead] + (2,) * len(BITS) + array.shape[lead + 1 :])


def step_pairs(count, step):
    return [(i, i + step) for i in range(count) if 0 <= i + step < count]


def lane_rows(length):
    return -(-length // 1024) * 8


def as_lanes(flat):
    rows = lane_rows(flat.shape[-1])
    gap = rows * 128 - flat.shape[-1]
    padded = jnp.pad(flat, [(0, 0)] * (flat.ndim - 1) + [(0, gap)])
    return padded.reshape(flat.shape[:-1] + (rows, 128))


def shifted(line_ref, row, lane, first, rows, stride):
    spots = lax.broadcasted_iota(jnp.int32, (rows, 128), 1)
    turn = lax.rem(128 - lane, 128)
    here = pltpu.roll(line_ref[pl.ds(row + first, rows, stride=stride), :], turn, 1)
    there = pltpu.roll(line_ref[pl.ds(row + first + 1, rows, stride=stride), :], turn, 1)
    return jnp.where(spots < 128 - lane, here, there)


def blocks_kernel(
    shape,
    place_ref,
    stem_ref,
    after_ref,
    layer_ref,
    before_ref,
    head_ref,
    block_ref,
    embed_ref,
    vector_ref,
    line_ref,
    flat_ref,
):
    front, stem_piece, layer_piece, tail = shape
    stem_lines = stem_ref.shape[1]
    end_row, end_lane = stem_piece // 128, stem_piece % 128
    after_lines = after_ref.shape[1]
    slot = head_ref.shape[1]
    for model in range(2):
        line_ref[pl.ds(0, front), :] = jnp.zeros((front, 128), single)
        line_ref[pl.ds(front, end_row), :] = stem_ref[model, pl.ds(0, end_row), :]
        turned = pltpu.roll(after_ref[model], end_lane, 1)
        spots = lax.broadcasted_iota(jnp.int32, (after_lines, 128), 1)
        line_ref[pl.ds(front + end_row, after_lines), :] = turned
        line_ref[pl.ds(front + end_row + after_lines, 128), :] = jnp.zeros((128, 128), single)
        lower = pltpu.roll(turned, 1, 0)
        first_line = jnp.broadcast_to(stem_ref[model, pl.ds(end_row, 1), :], (after_lines, 128))
        number = lax.broadcasted_iota(jnp.int32, (after_lines, 128), 0)
        lower = jnp.where(number == 0, first_line, lower)
        line_ref[pl.ds(front + end_row, after_lines), :] = jnp.where(spots < end_lane, lower, turned)
        per_row = ROW // 128
        for chunk in range(per_row):
            head_ref[model, :, pl.ds(chunk * 128, 128)] = shifted(
                line_ref, place_ref[0], place_ref[1], chunk, slot, per_row
            ).astype(narrow)
        for chunk in range(D // 128):
            embed_ref[model, :, pl.ds(chunk * 128, 128)] = shifted(
                line_ref, place_ref[2], place_ref[3], chunk, embed_ref.shape[1], D // 128
            ).astype(narrow)
    tail_lines = tail // 128
    layer_lines = layer_ref.shape[1]
    vector_at = tail + layer_piece - tail
    for part in range(layer_ref.shape[0]):
        flat_ref[pl.ds(0, tail_lines), :] = before_ref[part]
        flat_ref[pl.ds(tail_lines, layer_lines), :] = layer_ref[part]
        for chunk in range(D // 128):
            block_ref[part, :, pl.ds(chunk * 128, 128)] = shifted(
                flat_ref, place_ref[4], place_ref[5], chunk, block_ref.shape[1], D // 128
            ).astype(narrow)
            vector_ref[part, :, pl.ds(chunk * 128, 128)] = shifted(
                flat_ref, vector_at // 128, vector_at % 128, chunk, 8, D // 128
            ).astype(narrow)


def own_blocks(place, stems, after, layer_rows, before, shape, slot, block_rows, embed_rows):
    front, stem_piece, layer_piece, tail = shape
    lines = front + stem_piece // 128 + after.shape[1] + slot * ROW // 128
    flats = tail // 128 + layer_rows.shape[1] + 48
    return pl.pallas_call(
        lambda *refs: blocks_kernel(shape, *refs),
        out_shape=[
            jax.ShapeDtypeStruct((2, slot, ROW), narrow),
            jax.ShapeDtypeStruct((2 * LAYERS, block_rows, D), narrow),
            jax.ShapeDtypeStruct((2, embed_rows, D), narrow),
            jax.ShapeDtypeStruct((2 * LAYERS, 8, D), narrow),
        ],
        in_specs=[pl.BlockSpec(memory_space=pltpu.SMEM)] + [pl.BlockSpec(memory_space=pltpu.VMEM)] * 4,
        out_specs=[pl.BlockSpec(memory_space=pltpu.VMEM)] * 4,
        scratch_shapes=[pltpu.VMEM((lines, 128), single), pltpu.VMEM((flats, 128), single)],
        compiler_params=pltpu.CompilerParams(vmem_limit_bytes=40 << 20),
    )(place, stems, after, layer_rows, before)


def shards_kernel(place_ref, head_ref, previous_ref, block_ref, behind_ref, stem_ref, layer_ref, line_ref, flat_ref):
    per_row = ROW // 128
    extra = previous_ref.shape[0]
    slot = head_ref.shape[0]
    for chunk in range(per_row):
        spot = pl.ds(chunk * 128, 128)
        line_ref[pl.ds(chunk, extra, stride=per_row), :] = previous_ref[:, spot]
        line_ref[pl.ds(extra * per_row + chunk, slot, stride=per_row), :] = head_ref[:, spot]
    stem_ref[...] = shifted(line_ref, place_ref[0], place_ref[1], 0, stem_ref.shape[0], 1)
    per_row = D // 128
    rows = block_ref.shape[2]
    for part in range(block_ref.shape[0]):
        for chunk in range(per_row):
            flat_ref[pl.ds(chunk, rows, stride=per_row), :] = block_ref[part, chunk]
            flat_ref[pl.ds(rows * per_row + chunk, 6, stride=per_row), :] = behind_ref[part, chunk]
        layer_ref[part] = shifted(flat_ref, place_ref[2], place_ref[3], 0, layer_ref.shape[1], 1)


def own_shards(place, head_grad, previous, block_grad, behind, stem_lines, layer_lines):
    per_row = ROW // 128
    lines = (head_grad.shape[0] + previous.shape[0]) * per_row + 256
    flats = max(block_grad.shape[2] * 3 + 18, layer_lines + 18) + 16
    return pl.pallas_call(
        shards_kernel,
        out_shape=[
            jax.ShapeDtypeStruct((stem_lines, 128), single),
            jax.ShapeDtypeStruct((block_grad.shape[0], layer_lines, 128), single),
        ],
        in_specs=[pl.BlockSpec(memory_space=pltpu.SMEM)] + [pl.BlockSpec(memory_space=pltpu.VMEM)] * 4,
        out_specs=[pl.BlockSpec(memory_space=pltpu.VMEM)] * 2,
        scratch_shapes=[pltpu.VMEM((lines, 128), single), pltpu.VMEM((flats, 128), single)],
        compiler_params=pltpu.CompilerParams(vmem_limit_bytes=40 << 20),
    )(place, head_grad, previous, block_grad, behind)


PAD_SEQ = 272
GELU_SCALE = 0.7978845608028654
GELU_CUBE = 0.044715


def product_plain(left, right):
    return lax.dot_general(left, right, (((1,), (0,)), ((), ())), preferred_element_type=single)


def product_right(left, right):
    return lax.dot_general(left, right, (((1,), (1,)), ((), ())), preferred_element_type=single)


def product_left(left, right):
    return lax.dot_general(left, right, (((0,), (0,)), ((), ())), preferred_element_type=single)


def norm_parts(values):
    centred = values - jnp.mean(values, axis=-1, keepdims=True)
    spread = lax.rsqrt(jnp.mean(centred * centred, axis=-1, keepdims=True) + 1e-06)
    return centred * spread, spread


def norm_back(grad, unit, spread, gain):
    grad_unit = grad * gain
    mean_one = jnp.mean(grad_unit, axis=-1, keepdims=True)
    mean_two = jnp.mean(grad_unit * unit, axis=-1, keepdims=True)
    return spread * (grad_unit - mean_one - unit * mean_two)


def gelu_tanh(values):
    return jnp.tanh(GELU_SCALE * (values + GELU_CUBE * values * values * values))


def fetch_rows(side_ref, part, gathered_ref, flat_ref, sems):
    quarter = flat_ref.shape[0] // 4
    side = side_ref[0]
    first, second = side * quarter, (1 - side) * quarter
    copies = [
        pltpu.make_async_copy(
            gathered_ref.at[pl.ds(at, quarter), owner, part],
            flat_ref.at[pl.ds(spot * quarter, quarter)],
            sems.at[spot],
        )
        for spot, (at, owner) in enumerate(((first, 0), (second, 0), (second, 1), (first, 1)))
    ]
    for copy in copies:
        copy.start()
    for copy in copies:
        copy.wait()


def matrix_rows(flat_ref, first_row, length):
    rows = flat_ref.shape[1]
    low, high = first_row // rows, -(-(first_row + length) // rows)
    lines = flat_ref[pl.ds(low, high - low)].reshape((high - low) * rows, D)
    at = first_row - low * rows
    return lines[at : at + length]


def spread_columns(flat_ref, first_row, width, wide_ref, out_ref):
    length = width * D
    lines = matrix_rows(flat_ref, first_row, length)
    for column in range(D // 128):
        lane = slice(column * 128, (column + 1) * 128)
        wide_ref[column, pl.ds(0, length), :] = lines[:, lane].astype(single)
    for group in range(width):
        for column in range(D // 128):
            out_ref[group, :, pl.ds(column * 128, 128)] = wide_ref[
                column, pl.ds(group, D, stride=width), :
            ].astype(narrow)


def head_lanes(values, odd):
    lanes = lax.broadcasted_iota(jnp.int32, values.shape, 1)
    return jnp.where((lanes >= HEAD_DIM) == odd, values, jnp.zeros_like(values))


def join_lanes(even, odd):
    lanes = lax.broadcasted_iota(jnp.int32, even.shape, 1)
    return jnp.where(lanes >= HEAD_DIM, odd, even)


def soft_rows(query, key):
    scores = product_right(query, key) * HEAD_DIM ** (-0.5)
    spots = lax.broadcasted_iota(jnp.int32, scores.shape, 1)
    scores = jnp.where(spots < SEQ, scores, -1e30)
    terms = jnp.exp(scores - jnp.max(scores, axis=-1, keepdims=True))
    return terms / jnp.sum(terms, axis=-1, keepdims=True)


def forward_kernel(part, keep, side_ref, stream_ref, vector_ref, gathered_ref, *refs):
    out_ref = refs[0]
    if keep:
        packed_ref, mixed_ref, attn_ref, pre_ref, mlp_ref = refs[1:6]
        flat_ref, wide_ref, qkv_ref, up_ref, hidden_ref, sems = refs[6:]
    else:
        flat_ref, wide_ref, qkv_ref, up_ref, hidden_ref, packed_ref, mixed_ref, sems = refs[1:]
    fetch_rows(side_ref, part, gathered_ref, flat_ref, sems)
    spread_columns(flat_ref, 0, 3, wide_ref, qkv_ref)
    spread_columns(flat_ref, 4 * D, FF // D, wide_ref, up_ref)
    w_proj = matrix_rows(flat_ref, 3 * D, D)
    w_down = matrix_rows(flat_ref, 4 * D + FF, FF)
    vectors = vector_ref[...].astype(single)
    stream = stream_ref[...]
    normed = (norm_parts(stream)[0] * vectors[0:1] + vectors[1:2]).astype(narrow)
    for group in range(3):
        packed_ref[:, pl.ds(group * D, D)] = product_plain(normed, qkv_ref[group]).astype(narrow)
    for image in range(stream.shape[0] // PAD_SEQ):
        rows = pl.ds(image * PAD_SEQ, PAD_SEQ)
        for pair in range(HEADS // 2):
            query, key, value = [
                packed_ref[rows, pl.ds(group * D + pair * 128, 128)] for group in range(3)
            ]
            done = [
                product_plain(soft_rows(head_lanes(query, odd), key).astype(narrow), value)
                for odd in (False, True)
            ]
            mixed_ref[rows, pl.ds(pair * 128, 128)] = join_lanes(*done).astype(narrow)
    attn = product_plain(mixed_ref[...], w_proj)
    middle = stream + vectors[2:3] * attn
    normed_two = (norm_parts(middle)[0] * vectors[3:4] + vectors[4:5]).astype(narrow)
    for group in range(FF // D):
        spot = pl.ds(group * D, D)
        pre = product_plain(normed_two, up_ref[group])
        if keep:
            pre_ref[:, spot] = pre
        hidden_ref[:, spot] = (0.5 * pre * (1.0 + gelu_tanh(pre))).astype(narrow)
    mlp = product_plain(hidden_ref[...], w_down)
    out_ref[...] = middle + vectors[5:6] * mlp
    if keep:
        attn_ref[...] = attn
        mlp_ref[...] = mlp


def layer_scratch(gathered):
    rows, blocks = gathered.shape[3], 2 * gathered.shape[0]
    return [
        pltpu.VMEM((blocks, rows, D), narrow),
        pltpu.VMEM((D // 128, FF, 128), single),
        pltpu.VMEM((3, D, D), narrow),
        pltpu.VMEM((FF // D, D, D), narrow),
    ]


def layer_specs_in(count):
    return (
        [pl.BlockSpec(memory_space=pltpu.SMEM)]
        + [pl.BlockSpec(memory_space=pltpu.VMEM)] * (count - 2)
        + [pl.BlockSpec(memory_space=pl.ANY)]
    )


def layer_forward(side, stream, vectors, gathered, part, keep):
    tokens = stream.shape[0]
    shapes = [jax.ShapeDtypeStruct((tokens, D), single)]
    extra = [
        jax.ShapeDtypeStruct((tokens, 3 * D), narrow),
        jax.ShapeDtypeStruct((tokens, D), narrow),
        jax.ShapeDtypeStruct((tokens, D), single),
        jax.ShapeDtypeStruct((tokens, FF), single),
        jax.ShapeDtypeStruct((tokens, D), single),
    ]
    scratch = layer_scratch(gathered) + [pltpu.VMEM((tokens, FF), narrow)]
    if keep:
        shapes = shapes + extra
    else:
        scratch = scratch + [pltpu.VMEM((tokens, 3 * D), narrow), pltpu.VMEM((tokens, D), narrow)]
    scratch.append(pltpu.SemaphoreType.DMA((4,)))
    return pl.pallas_call(
        lambda *refs: forward_kernel(part, keep, *refs),
        out_shape=shapes,
        in_specs=layer_specs_in(4),
        out_specs=[pl.BlockSpec(memory_space=pltpu.VMEM)] * len(shapes),
        scratch_shapes=scratch,
        compiler_params=pltpu.CompilerParams(vmem_limit_bytes=56 << 20),
        cost_estimate=pl.CostEstimate(flops=2 * 10**9, bytes_accessed=2 * 10**7, transcendentals=2 * 10**6),
    )(side, stream, vectors, gathered)


def mlp_back_kernel(
    part,
    side_ref,
    grad_ref,
    stream_ref,
    attn_ref,
    pre_ref,
    mlp_ref,
    vector_ref,
    gathered_ref,
    *refs,
):
    grad_mid_ref, all_grad_ref, vector_grad_ref = refs[-10:-7]
    flat_ref, wide_ref, up_ref, hidden_ref, grad_pre_ref, weight_grad_ref, sems = refs[-7:]
    fetch_rows(side_ref, part, gathered_ref, flat_ref, sems)
    spread_columns(flat_ref, 4 * D, FF // D, wide_ref, up_ref)
    w_down = matrix_rows(flat_ref, 4 * D + FF, FF)
    vectors = vector_ref[...].astype(single)
    grad_out = grad_ref[...]
    vector_grad_ref[...] = jnp.zeros_like(vector_grad_ref)
    attn = attn_ref[...]
    middle = stream_ref[...] + vectors[2:3] * attn
    unit_two, spread_two = norm_parts(middle)
    normed_two = (unit_two * vectors[3:4] + vectors[4:5]).astype(narrow)
    vector_grad_ref[pl.ds(5, 1), :] = jnp.sum(grad_out * mlp_ref[...], axis=0, keepdims=True)
    grad_mlp = (grad_out * vectors[5:6]).astype(narrow)
    grad_normed_two = jnp.zeros_like(grad_out)
    for group in range(FF // D):
        spot = pl.ds(group * D, D)
        pre = pre_ref[:, spot]
        bent = gelu_tanh(pre)
        hidden_ref[:, spot] = (0.5 * pre * (1.0 + bent)).astype(narrow)
        slope = 0.5 * (1.0 + bent) + 0.5 * pre * (1.0 - bent * bent) * GELU_SCALE * (
            1.0 + 3.0 * GELU_CUBE * pre * pre
        )
        grad_hidden = product_right(grad_mlp, w_down[group * D : (group + 1) * D])
        grad_pre = (grad_hidden * slope).astype(narrow)
        grad_pre_ref[:, spot] = grad_pre
        grad_normed_two = grad_normed_two + product_right(grad_pre, up_ref[group])
    for group in range(FF // D):
        spot = pl.ds(group * D, D)
        up_grad = product_left(normed_two, grad_pre_ref[:, spot])
        down_grad = product_left(hidden_ref[:, spot], grad_mlp)
        for column in range(D // 128):
            lane = slice(column * 128, (column + 1) * 128)
            weight_grad_ref[column, pl.ds(group, D, stride=FF // D), :] = up_grad[:, lane]
            weight_grad_ref[column, pl.ds(FF + group * D, D), :] = down_grad[:, lane]
    vector_grad_ref[pl.ds(3, 1), :] = jnp.sum(grad_normed_two * unit_two, axis=0, keepdims=True)
    vector_grad_ref[pl.ds(4, 1), :] = jnp.sum(grad_normed_two, axis=0, keepdims=True)
    grad_mid = grad_out + norm_back(grad_normed_two, unit_two, spread_two, vectors[3:4])
    vector_grad_ref[pl.ds(2, 1), :] = jnp.sum(grad_mid * attn, axis=0, keepdims=True)
    grad_mid_ref[...] = grad_mid
    store_rows(weight_grad_ref, all_grad_ref, 4 * D, sems.at[0])


def attention_back_kernel(
    part,
    side_ref,
    grad_ref,
    stream_ref,
    packed_ref,
    mixed_ref,
    vector_ref,
    gathered_ref,
    *refs,
):
    grad_in_ref, all_grad_ref, vector_grad_ref = refs[-10:-7]
    flat_ref, wide_ref, qkv_ref, grad_mixed_ref, grad_packed_ref, weight_grad_ref, sems = refs[-7:]
    fetch_rows(side_ref, part, gathered_ref, flat_ref, sems)
    spread_columns(flat_ref, 0, 3, wide_ref, qkv_ref)
    w_proj = matrix_rows(flat_ref, 3 * D, D)
    vectors = vector_ref[...].astype(single)
    vector_grad_ref[...] = jnp.zeros_like(vector_grad_ref)
    grad_mid = grad_ref[...]
    stream = stream_ref[...]
    grad_attn = (grad_mid * vectors[2:3]).astype(narrow)
    proj_grad = product_left(mixed_ref[...], grad_attn)
    for column in range(D // 128):
        weight_grad_ref[column, pl.ds(3 * D, D), :] = proj_grad[:, column * 128 : (column + 1) * 128]
    grad_mixed_ref[...] = product_right(grad_attn, w_proj).astype(narrow)
    for image in range(stream.shape[0] // PAD_SEQ):
        rows = pl.ds(image * PAD_SEQ, PAD_SEQ)
        for pair in range(HEADS // 2):
            query, key, value = [
                packed_ref[rows, pl.ds(group * D + pair * 128, 128)] for group in range(3)
            ]
            grad_mixed = grad_mixed_ref[rows, pl.ds(pair * 128, 128)]
            parts = []
            for odd in (False, True):
                probs = soft_rows(head_lanes(query, odd), key)
                grad_probs = product_right(head_lanes(grad_mixed, odd), value)
                grad_value = product_left(probs.astype(narrow), grad_mixed)
                grad_scores = probs * (grad_probs - jnp.sum(probs * grad_probs, axis=-1, keepdims=True))
                grad_raw = (grad_scores * HEAD_DIM ** (-0.5)).astype(narrow)
                parts.append((product_plain(grad_raw, key), product_left(grad_raw, query), grad_value))
            for group in range(3):
                grad_packed_ref[rows, pl.ds(group * D + pair * 128, 128)] = join_lanes(
                    parts[0][group], parts[1][group]
                ).astype(narrow)
    unit_one, spread_one = norm_parts(stream)
    normed = (unit_one * vectors[0:1] + vectors[1:2]).astype(narrow)
    grad_normed = jnp.zeros_like(grad_mid)
    for group in range(3):
        grad_part = grad_packed_ref[:, pl.ds(group * D, D)]
        grad_normed = grad_normed + product_right(grad_part, qkv_ref[group])
        qkv_grad = product_left(normed, grad_part)
        for column in range(D // 128):
            lane = slice(column * 128, (column + 1) * 128)
            weight_grad_ref[column, pl.ds(group, D, stride=3), :] = qkv_grad[:, lane]
    vector_grad_ref[pl.ds(0, 1), :] = jnp.sum(grad_normed * unit_one, axis=0, keepdims=True)
    vector_grad_ref[pl.ds(1, 1), :] = jnp.sum(grad_normed, axis=0, keepdims=True)
    grad_in_ref[...] = grad_mid + norm_back(grad_normed, unit_one, spread_one, vectors[0:1])
    store_rows(weight_grad_ref, all_grad_ref, 0, sems.at[0])


def store_rows(weight_grad_ref, all_grad_ref, first_row, sem):
    copy = pltpu.make_async_copy(
        weight_grad_ref, all_grad_ref.at[:, pl.ds(first_row, weight_grad_ref.shape[1])], sem
    )
    copy.start()
    copy.wait()


def layer_back(kernel, part, weight_rows, side, inputs, vectors, gathered, started, waits, columns, buffers):
    tokens = inputs[0].shape[0]
    rows, blocks = gathered.shape[3], 2 * gathered.shape[0]
    return pl.pallas_call(
        lambda *refs: kernel(part, *refs),
        out_shape=[
            jax.ShapeDtypeStruct((tokens, D), single),
            jax.ShapeDtypeStruct((D // 128, MATRIX_ROWS, 128), single),
            jax.ShapeDtypeStruct((8, D), single),
        ],
        in_specs=layer_specs_in(len(inputs) + 3)
        + [pl.BlockSpec(memory_space=pl.ANY)] * (len(started) + len(waits)),
        out_specs=[
            pl.BlockSpec(memory_space=pltpu.VMEM),
            pl.BlockSpec(memory_space=pl.ANY),
            pl.BlockSpec(memory_space=pltpu.VMEM),
        ],
        input_output_aliases={len(inputs) + 3: 1} if started else {},
        scratch_shapes=[
            pltpu.VMEM((blocks, rows, D), narrow),
            pltpu.VMEM((D // 128, columns * D, 128), single),
            pltpu.VMEM((columns, D, D), narrow),
        ]
        + [pltpu.VMEM((tokens, width), narrow) for width in buffers]
        + [pltpu.VMEM((D // 128, weight_rows, 128), single), pltpu.SemaphoreType.DMA((4,))],
        compiler_params=pltpu.CompilerParams(vmem_limit_bytes=56 << 20),
        cost_estimate=pl.CostEstimate(flops=5 * 10**9, bytes_accessed=4 * 10**7, transcendentals=2 * 10**6),
    )(side, *inputs, vectors, gathered, *started, *waits)


def mlp_back(side, grad_out, saved, vectors, gathered, part, waits):
    stream, packed, mixed, attn, pre, mlp = saved
    return layer_back(
        mlp_back_kernel, part, 2 * FF, side, (grad_out, stream, attn, pre, mlp), vectors, gathered, (), waits,
        FF // D, (FF, FF),
    )


def attention_back(side, grad_mid, saved, vectors, gathered, part, started, waits):
    stream, packed, mixed, attn, pre, mlp = saved
    return layer_back(
        attention_back_kernel, part, 4 * D, side, (grad_mid, stream, packed, mixed), vectors, gathered, (started,), waits,
        3, (D, 3 * D),
    )


def after(value, *tokens):
    def kernel(*refs):
        refs[-1][...] = refs[0][...]

    return pl.pallas_call(
        kernel,
        out_shape=jax.ShapeDtypeStruct(value.shape, value.dtype),
        in_specs=[pl.BlockSpec(memory_space=pltpu.VMEM)] + [pl.BlockSpec(memory_space=pl.ANY)] * len(tokens),
        out_specs=pl.BlockSpec(memory_space=pltpu.VMEM),
    )(value, *tokens)


def embed_back_kernel(grad_ref, patch_ref, shown_ref, gain_ref, vector_ref, *refs):
    out_ref = refs[-1]
    grad = grad_ref[...]
    images = grad.shape[0] // PAD_SEQ
    shown = shown_ref[...]
    position = jnp.zeros((PAD_SEQ, D), single)
    token = jnp.zeros((1, D), single)
    patch_grads = []
    for image in range(images):
        here = grad[image * PAD_SEQ : (image + 1) * PAD_SEQ]
        position = position + here
        rows = here[1:SEQ]
        seen = shown[image * PATCHES : (image + 1) * PATCHES]
        token = token + jnp.sum(rows * (1.0 - seen), axis=0, keepdims=True)
        patch_grads.append((rows * seen).astype(narrow))
    patch_grad = product_left(patch_ref[...], jnp.concatenate(patch_grads))
    out_ref[...] = jnp.zeros_like(out_ref)
    for column in range(D // 128):
        lane = slice(column * 128, (column + 1) * 128)
        out_ref[column, pl.ds(0, PIX), :] = patch_grad[:, lane]
        out_ref[column, pl.ds(PIX, SEQ), :] = position[:SEQ, lane]
        out_ref[column, pl.ds(PIX + SEQ, 1), :] = position[0:1, lane]
        out_ref[column, pl.ds(PIX + SEQ + 1, 1), :] = token[:, lane]
        out_ref[column, pl.ds(PIX + SEQ + 2, 2), :] = gain_ref[:, lane]
        out_ref[column, pl.ds(EMBED_ROWS, vector_ref.shape[0]), :] = vector_ref[:, lane]


def embed_back(grad, patch_rows, shown, gains, vector_grads, rows, waits):
    return pl.pallas_call(
        embed_back_kernel,
        out_shape=jax.ShapeDtypeStruct((D // 128, rows, 128), single),
        in_specs=[pl.BlockSpec(memory_space=pltpu.VMEM)] * 5 + [pl.BlockSpec(memory_space=pl.ANY)] * len(waits),
        out_specs=pl.BlockSpec(memory_space=pltpu.VMEM),
        compiler_params=pltpu.CompilerParams(vmem_limit_bytes=40 << 20),
        cost_estimate=pl.CostEstimate(flops=10**9, bytes_accessed=2 * 10**7, transcendentals=0),
    )(grad, patch_rows, shown, gains, vector_grads, *waits)


def proto_units(values):
    rounded = values.astype(narrow).astype(single)
    scale = lax.rsqrt(jnp.sum(rounded * rounded, axis=-1, keepdims=True) + 1e-06)
    return rounded, scale, (rounded * scale).astype(narrow)


def proto_terms(teacher_z, student_z, teacher_unit, student_unit, centre_column):
    teacher_logits = product_right(teacher_unit, teacher_z)
    logits = product_right(student_unit, student_z)
    teacher_exp = jnp.exp((teacher_logits - centre_column) * (1.0 / tau_teacher))
    student_exp = jnp.exp(logits * (1.0 / tau_student))
    return teacher_logits, logits, teacher_exp, student_exp


def logits_kernel(
    teacher_z_ref,
    student_z_ref,
    teacher_ref,
    student_ref,
    centre_ref,
    class_ref,
    mixed_ref,
    sums_ref,
    centre_sum_ref,
    student_mix_ref,
    teacher_mix_ref,
    totals_ref,
):
    step = pl.program_id(0)

    @pl.when(step == 0)
    def _():
        student_mix_ref[...] = jnp.zeros_like(student_mix_ref)
        teacher_mix_ref[...] = jnp.zeros_like(teacher_mix_ref)
        totals_ref[...] = jnp.zeros_like(totals_ref)

    teacher_unit = proto_units(teacher_ref[...])[2]
    student_unit = proto_units(student_ref[...])[2]
    teacher_logits, logits, teacher_exp, student_exp = proto_terms(
        teacher_z_ref[...], student_z_ref[...], teacher_unit, student_unit, centre_ref[...]
    )
    totals_ref[pl.ds(0, 1), :] += jnp.sum(teacher_exp, axis=0, keepdims=True)
    totals_ref[pl.ds(1, 1), :] += jnp.sum(student_exp, axis=0, keepdims=True)
    totals_ref[pl.ds(2, 1), :] += jnp.sum(teacher_exp * logits, axis=0, keepdims=True)
    centre_sum_ref[...] = jnp.sum(teacher_logits * class_ref[0:1], axis=1, keepdims=True)
    student_mix_ref[...] += product_left(student_unit, student_exp.astype(narrow))
    teacher_mix_ref[...] += product_left(student_unit, teacher_exp.astype(narrow))

    @pl.when(step == pl.num_programs(0) - 1)
    def _():
        mixed_ref[:, pl.ds(0, BOT)] = student_mix_ref[...].T
        mixed_ref[:, pl.ds(BOT, BOT)] = teacher_mix_ref[...].T
        sums_ref[...] = totals_ref[...]


def proto_specs(rows, block):
    whole = pl.BlockSpec((rows, BOT), lambda i: (0, 0))
    table = pl.BlockSpec((block, BOT), lambda i: (i, 0))
    column = pl.BlockSpec((block, 1), lambda i: (i, 0))
    lines = pl.BlockSpec((8, rows), lambda i: (0, 0))
    return whole, table, column, lines


def logits_pass(teacher_z, student_z, teacher, student, centre_column, class_lines):
    rows, protos_here = teacher_z.shape[0], student.shape[0]
    block = protos_here // 4
    whole, table, column, lines = proto_specs(rows, block)
    return pl.pallas_call(
        logits_kernel,
        grid=(4,),
        out_shape=[
            jax.ShapeDtypeStruct((rows, 2 * BOT), single),
            jax.ShapeDtypeStruct((8, rows), single),
            jax.ShapeDtypeStruct((protos_here, 1), single),
        ],
        in_specs=[whole, whole, table, table, column, lines],
        out_specs=[pl.BlockSpec((rows, 2 * BOT), lambda i: (0, 0)), lines, column],
        scratch_shapes=[
            pltpu.VMEM((BOT, rows), single),
            pltpu.VMEM((BOT, rows), single),
            pltpu.VMEM((8, rows), single),
        ],
        compiler_params=pltpu.CompilerParams(vmem_limit_bytes=56 << 20),
        cost_estimate=pl.CostEstimate(flops=5 * 10**9, bytes_accessed=10**7, transcendentals=5 * 10**6),
    )(teacher_z, student_z, teacher, student, centre_column, class_lines)


def proto_grad_kernel(
    teacher_z_ref, student_z_ref, teacher_ref, student_ref, centre_ref, scale_ref, grad_ref, square_ref
):
    step = pl.program_id(0)

    @pl.when(step == 0)
    def _():
        square_ref[...] = jnp.zeros_like(square_ref)

    teacher_unit = proto_units(teacher_ref[...])[2]
    rounded, scale, student_unit = proto_units(student_ref[...])
    student_z = student_z_ref[...]
    _, _, teacher_exp, student_exp = proto_terms(
        teacher_z_ref[...], student_z, teacher_unit, student_unit, centre_ref[...]
    )
    grad_logits = (student_exp * scale_ref[0:1] - teacher_exp * scale_ref[1:2]).astype(narrow)
    unit_grad = product_plain(grad_logits, student_z)
    along = jnp.sum(unit_grad * rounded, axis=-1, keepdims=True)
    grad = scale * (unit_grad - rounded * (along * scale * scale))
    grad_ref[...] = grad
    square_ref[...] += jnp.broadcast_to(jnp.sum(grad * grad), square_ref.shape)


def proto_grad_pass(teacher_z, student_z, teacher, student, centre_column, scale_lines):
    rows, protos_here = teacher_z.shape[0], student.shape[0]
    block = protos_here // 4
    whole, table, column, lines = proto_specs(rows, block)
    return pl.pallas_call(
        proto_grad_kernel,
        grid=(4,),
        out_shape=[
            jax.ShapeDtypeStruct((protos_here, BOT), single),
            jax.ShapeDtypeStruct((8, 128), single),
        ],
        in_specs=[whole, whole, table, table, column, lines],
        out_specs=[table, pl.BlockSpec((8, 128), lambda i: (0, 0))],
        compiler_params=pltpu.CompilerParams(vmem_limit_bytes=56 << 20),
        cost_estimate=pl.CostEstimate(flops=4 * 10**9, bytes_accessed=10**7, transcendentals=5 * 10**6),
    )(teacher_z, student_z, teacher, student, centre_column, scale_lines)


def proto_update(factor, student, moment, second, teacher, grad):
    def kernel(factor_ref, *refs):
        weight, moment, second, teacher, grad = [ref[...] for ref in refs[:5]]
        done = adam_update(weight, moment, second, grad * factor_ref[0], teacher)
        for ref, value in zip(refs[5:], done):
            ref[...] = value

    block = student.shape[0] // 4
    table = pl.BlockSpec((block, BOT), lambda i: (i, 0))
    return pl.pallas_call(
        kernel,
        grid=(4,),
        out_shape=[
            jax.ShapeDtypeStruct(student.shape, narrow if number == 3 else single) for number in range(5)
        ],
        in_specs=[pl.BlockSpec(memory_space=pltpu.SMEM)] + [table] * 5,
        out_specs=[table] * 5,
        compiler_params=pltpu.CompilerParams(vmem_limit_bytes=40 << 20),
        cost_estimate=pl.CostEstimate(flops=10**7, bytes_accessed=2 * 10**7, transcendentals=0),
    )(factor.reshape(1), student, moment, second, teacher, grad)


def head_grads_kernel(
    place_ref, inputs_ref, grads_ref, own_ref, partner_ref, window_ref, rows_ref, product_ref,
    third_ref, bottle_ref, line_ref, sems,
):
    slot = own_ref.shape[0]
    lead = product_ref.shape[0] - window_ref.shape[1]
    number = lax.broadcasted_iota(jnp.int32, (slot, 1), 0)
    product_ref[pl.ds(0, lead), :] = jnp.zeros((lead, ROW), single)

    def block(at, out_ref):
        column = pl.multiple_of(place_ref[at], 128)
        grad_column = pl.multiple_of(place_ref[at + 3], 128)
        copies = [
            pltpu.make_async_copy(
                inputs_ref.at[:, pl.ds(column, window_ref.shape[1])], window_ref, sems.at[0]
            ),
            pltpu.make_async_copy(grads_ref.at[:, pl.ds(grad_column, ROW)], rows_ref, sems.at[1]),
        ]
        for copy in copies:
            copy.start()
        for copy in copies:
            copy.wait()
        window = window_ref[...]
        for piece in range(4):
            spot = pl.ds(piece * (ROW // 4), ROW // 4)
            product_ref[pl.ds(lead, window.shape[1]), spot] = product_left(window, rows_ref[:, spot])
        from_row = pl.multiple_of(lead + place_ref[at + 1], 8)
        out_ref[...] = jnp.where(number < place_ref[at + 2], product_ref[pl.ds(from_row, slot), :], 0.0)

    @pl.when(place_ref[8] == 0)
    def _():
        block(0, own_ref)

    @pl.when(place_ref[8] == 1)
    def _():
        column = pl.multiple_of(place_ref[9], 128)
        copies = [
            pltpu.make_async_copy(
                inputs_ref.at[:, pl.ds(column, third_ref.shape[1])], third_ref, sems.at[0]
            ),
            pltpu.make_async_copy(grads_ref.at[:, pl.ds(2 * HID, BOT)], bottle_ref, sems.at[1]),
        ]
        for copy in copies:
            copy.start()
        for copy in copies:
            copy.wait()
        third = product_left(third_ref[...], bottle_ref[...])
        for lane in range(BOT // 128):
            line_ref[lane] = third[:, lane * 128 : (lane + 1) * 128]
        for group in range(ROW // BOT):
            for lane in range(BOT // 128):
                value = line_ref[lane, pl.ds(group, slot, stride=ROW // BOT), :]
                own_ref[:, pl.ds(group * BOT + lane * 128, 128)] = jnp.where(
                    number < place_ref[2], value, 0.0
                )

    block(4, partner_ref)


def head_grads(place, inputs_all, grads_all, slot, lead):
    rows = inputs_all.shape[0]
    wide = slot * ROW // BOT
    return pl.pallas_call(
        head_grads_kernel,
        out_shape=[jax.ShapeDtypeStruct((slot, ROW), single)] * 2,
        in_specs=[pl.BlockSpec(memory_space=pltpu.SMEM)] + [pl.BlockSpec(memory_space=pl.ANY)] * 2,
        out_specs=[pl.BlockSpec(memory_space=pltpu.VMEM)] * 2,
        scratch_shapes=[
            pltpu.VMEM((rows, 256), narrow),
            pltpu.VMEM((rows, ROW), narrow),
            pltpu.VMEM((lead + 256, ROW), single),
            pltpu.VMEM((rows, wide), narrow),
            pltpu.VMEM((rows, BOT), narrow),
            pltpu.VMEM((BOT // 128, wide, 128), single),
            pltpu.SemaphoreType.DMA((2,)),
        ],
        compiler_params=pltpu.CompilerParams(vmem_limit_bytes=56 << 20),
        cost_estimate=pl.CostEstimate(flops=4 * 10**9, bytes_accessed=2 * 10**7, transcendentals=0),
    )(place, inputs_all, grads_all)


def close_local(
    patches,
    masked,
    slot_used,
    stem,
    stem_moment,
    stem_second,
    stem_teacher,
    layers,
    layer_moment,
    layer_second,
    layer_teacher,
    protos,
    proto_moment,
    proto_second,
    proto_teacher,
    centre,
):
    count = 1 << len(BITS)
    half = count // 2
    me = lax.axis_index("dev")
    across = MASKS["b"]
    student_side = me >= half
    groups = [list(range(half)), list(range(half, count))]
    quarter = half // 2
    swap = jnp.where(student_side, quarter, 0)
    side = student_side.astype(jnp.int32).reshape(1)
    images_here = patches.shape[0]
    rows_here = images_here * 17
    stem_piece = stem.shape[0]
    layer_piece = layers.shape[1]
    block_rows = MATRIX_ROWS // count
    block = block_rows * D
    tail = layer_piece * count - MATRIX_ROWS * D
    drift = layer_piece - block
    bounds = head_bounds(count, stem_piece)
    sizes = [bounds[i + 1] - bounds[i] for i in range(count)]
    slot = max(sizes)
    starts = [b * ROW + EMBED_FLAT - stem_piece * i for i, b in enumerate(bounds[:-1])]
    first_w2 = bounds.index(D)
    first_w3 = bounds.index(D + HID)
    row_index = jnp.concatenate([jnp.zeros((images_here, 1), jnp.int32), masked + 1], axis=1)
    masked_here = jnp.any(
        masked[:, :, None] == jnp.arange(PATCHES, dtype=jnp.int32)[None, None, :], axis=1
    )
    kept = slot_used.astype(single)

    front = 16
    early_rows = -(-stem_piece // D)
    late_start = early_rows * D - stem_piece
    embed_rows = -(-early_rows // 16) * 16
    own_layers = jnp.concatenate([layer_teacher, layers])
    own_tail = own_layers[:, layer_piece - tail :].reshape(2 * LAYERS, tail // 128, 128)
    before = lax.ppermute(own_tail, "dev", step_pairs(count, 1))
    head_span = GROUP * ROW
    stems = jnp.stack([as_lanes(stem_teacher), as_lanes(stem)])
    stems_next = lax.ppermute(stems[:, : head_span // 128], "dev", step_pairs(count, -1))
    start_here = jnp.array(starts, jnp.int32)[me]
    head_at = start_here + front * 128
    embed_at = front * 128 + jnp.where(me == 0, 0, late_start)
    block_at = tail - drift * me
    place = jnp.stack(
        [head_at // 128, head_at % 128, embed_at // 128, embed_at % 128, block_at // 128, block_at % 128]
    ).astype(jnp.int32)
    head_blocks, layer_blocks, embed_blocks, vector_blocks = own_blocks(
        place,
        stems,
        stems_next,
        as_lanes(own_layers),
        before,
        (front, stem_piece, layer_piece, tail),
        slot,
        block_rows,
        embed_rows,
    )

    other_layers = lax.ppermute(layer_blocks, "dev", pairs(count, across))
    both_layers = jnp.where(
        student_side,
        jnp.stack([other_layers, layer_blocks]),
        jnp.stack([layer_blocks, other_layers]),
    )
    gathered = lax.all_gather(both_layers, "dev", axis=0, axis_index_groups=groups)
    head_out = jnp.where(student_side, head_blocks[0], head_blocks[1])
    head_keep = jnp.where(student_side, head_blocks[1], head_blocks[0])
    head_got = lax.ppermute(head_out, "dev", pairs(count, across))
    both_head = jnp.where(
        student_side, jnp.stack([head_got, head_keep]), jnp.stack([head_keep, head_got])
    )

    vectors = lax.ppermute(vector_blocks, "dev", [(count - 1, 0)])
    seed = jnp.concatenate([embed_blocks.reshape(2 * embed_rows, D), vectors.reshape(8 * 2 * LAYERS, D)])
    third = -(-seed.shape[0] // 48) * 16
    spread_parts = []
    for number, order in enumerate(("xyba", "baxy", "ybax")):
        spread = seed[number * third : (number + 1) * third]
        reached = [0, 1]
        for name in order:
            moves = [(i, i ^ MASKS[name]) for i in reached]
            got = lax.ppermute(spread, "dev", moves)
            targets = [t for s, t in moves]
            is_target = jnp.array([i in targets for i in range(count)])[me]
            spread = jnp.where(is_target, got, spread)
            reached = reached + targets
        spread_parts.append(spread)
    spread = jnp.concatenate(spread_parts)
    other = lax.ppermute(spread, "dev", pairs(count, 1))
    is_even = me % 2 == 0
    even = jnp.where(is_even, spread, other)
    odd = jnp.where(is_even, other, spread)
    embed_all = [
        jnp.concatenate(
            [
                even[m * embed_rows : m * embed_rows + early_rows],
                odd[m * embed_rows : m * embed_rows + EMBED_ROWS - early_rows],
            ]
        )
        for m in range(2)
    ]
    gathered_head = lax.all_gather(after(both_head, gathered, even, odd), "dev", axis=0, axis_index_groups=groups)
    vectors_all = even[2 * embed_rows :].reshape(2, LAYERS, 8, D)

    def head_slots(first, last):
        pieces = []
        i = first
        while i < last:
            stop = min(last, (i // quarter + 1) * quarter)
            owner = 1 if i >= half else 0
            at = (i ^ across if owner else i) ^ swap
            pieces.append(
                lax.dynamic_slice(
                    gathered_head, (at, owner, 0, 0), (stop - i, 1, slot, ROW)
                ).reshape(stop - i, slot, ROW)
            )
            i = stop
        return pieces

    def pad_columns(values, first, last, origin):
        pieces = []
        for i in range(first, last):
            low, high = bounds[i] - origin, bounds[i + 1] - origin
            if low < 0:
                pieces.append(jnp.zeros(values.shape[:-1] + (-low,), values.dtype))
            pieces.append(values[..., max(low, 0) : high])
            pieces.append(jnp.zeros(values.shape[:-1] + (slot - sizes[i],), values.dtype))
        return jnp.concatenate([p for p in pieces if p.shape[-1]], axis=-1)

    def cut_columns(values, first, last, origin):
        pieces = []
        for i in range(first, last):
            low = bounds[i] - origin
            at = (i - first) * slot
            pieces.append(values[..., at + max(-low, 0) : at + sizes[i]])
        return jnp.concatenate(pieces, axis=-1)

    def embed_parts(model):
        rows = embed_all[model]
        return (rows[:PIX], rows[PIX : PIX + SEQ], rows[PIX + SEQ :], None, None, None)

    def head_rows(stream, extras):
        chosen = jnp.take_along_axis(stream, row_index[:, :, None], axis=1).reshape(rows_here, D)
        normed = layer_norm(chosen, extras[2].astype(single), extras[3].astype(single)).astype(narrow)
        return chosen, normed

    def start_rows(parts, student):
        stream = embed(parts, patches, masked_here, student)
        return jnp.pad(stream, ((0, 0), (0, PAD_SEQ - SEQ), (0, 0))).reshape(images_here * PAD_SEQ, D)

    student_parts = embed_parts(1)
    stream = start_rows(student_parts, True)
    saved_layers = []
    for layer_index in range(LAYERS):
        before_layer = stream
        stream, *saved = layer_forward(
            side, stream, vectors_all[1, layer_index], gathered, LAYERS + layer_index, True
        )
        saved_layers.append((before_layer, *saved))
    teacher_parts = embed_parts(0)
    teacher_stream = start_rows(teacher_parts, False)
    for layer_index in range(LAYERS):
        teacher_stream = layer_forward(
            side, teacher_stream, vectors_all[0, layer_index], gathered, layer_index, False
        )[0]
    stream = stream.reshape(images_here, PAD_SEQ, D)
    teacher_stream = teacher_stream.reshape(images_here, PAD_SEQ, D)
    chosen, student_normed = head_rows(stream, student_parts[2])
    teacher_normed = head_rows(teacher_stream, teacher_parts[2])[1]

    normed_got = lax.ppermute(
        jnp.where(student_side, teacher_normed, student_normed), "dev", pairs(count, across)
    )
    normed = jnp.where(
        student_side,
        jnp.concatenate([normed_got, student_normed]),
        jnp.concatenate([teacher_normed, normed_got]),
    )
    w_one = jnp.concatenate(head_slots(1, first_w2)).reshape(-1, ROW)
    w_two = jnp.concatenate(head_slots(first_w2, first_w3)).reshape(-1, ROW)
    w_three = jnp.concatenate(
        [head_slots(i, i + 1)[0][0, : sizes[i]] for i in range(first_w3, count)]
    ).reshape(HID, BOT)
    pre_one = contract("rd,dh->rh", pad_columns(normed, 1, first_w2, 0), w_one)
    hidden_one = jax.nn.gelu(pre_one).astype(narrow)
    pre_two = contract("rh,hk->rk", pad_columns(hidden_one, first_w2, first_w3, D), w_two)
    hidden_two = jax.nn.gelu(pre_two).astype(narrow)
    bottleneck = contract("rh,hb->rb", hidden_two, w_three)
    unit_z = unit_rows(bottleneck).astype(narrow)
    pair_rows = -(-2 * rows_here // 16) * 16
    more_rows = ((0, pair_rows - 2 * rows_here), (0, 0))
    third_end = (bounds[-2] - D - HID + slot) * (ROW // BOT)
    more_inputs = (more_rows[0], (0, max(third_end - HID, 0)))
    inputs_all = lax.all_gather(
        jnp.pad(jnp.concatenate([normed, hidden_one, hidden_two], axis=1), more_inputs),
        "dev",
        axis=0,
        axis_index_groups=groups,
    ).reshape(half * pair_rows, -1)

    all_rows = count * rows_here
    kept_row = jnp.broadcast_to(kept[:, None], (images_here, 17)).reshape(1, rows_here)
    all_kept = cube_gather(kept_row, "bxygc").reshape(all_rows)
    z_pair = cube_gather(unit_z, "b")
    z_all = cube_gather(z_pair, "xygc")
    z_all = z_all.reshape(half, 2, 2 * rows_here, BOT)
    wide_rows = -(-all_rows // 128) * 128
    teacher_z_all, student_z_all = [
        jnp.pad(z_all[:, model].reshape(all_rows, BOT), ((0, wide_rows - all_rows), (0, 0))) for model in range(2)
    ]
    protos_here = protos.shape[0]
    own_centre = lax.dynamic_slice(centre, (me * protos_here,), (protos_here,))
    centre_column = own_centre.reshape(protos_here, 1)
    is_class = (jnp.arange(all_rows) % 17) == 0
    class_kept = jnp.where(is_class, all_kept, 0.0)
    row_weight = jnp.where(is_class, all_kept, all_kept * (1.0 / 16.0))
    count_total = jnp.sum(class_kept)

    def lines(*values):
        held = jnp.pad(jnp.stack(values), ((0, 8 - len(values)), (0, wide_rows - all_rows)))
        return held

    mixed_rows, sums, centre_sum = logits_pass(
        teacher_z_all, student_z_all, proto_teacher, protos, centre_column, lines(class_kept)
    )
    mixed_own = cube_scatter(
        [mixed_rows[:all_rows].reshape((2,) * 4 + (2 * rows_here, 2 * BOT))], ("cgyx",), ("cgyx",)
    )[0]
    mixed_own = mixed_own + lax.ppermute(
        mixed_own.astype(narrow), "dev", [(i, i ^ across) for i in range(half)]
    ).astype(single)
    sums = cube_sum(sums[:3, :all_rows])
    cross = jnp.log(sums[1]) - sums[2] / (sums[0] * tau_student)
    loss_total = jnp.sum(row_weight * cross)
    scale = row_weight / tau_student
    student_scale, teacher_scale = scale / sums[1], scale / sums[0]
    flags = bit_flags(me)
    pair_at = flags["c"] * 8 + flags["g"] * 4 + flags["y"] * 2 + flags["x"]
    own_scales = lax.dynamic_slice(
        jnp.stack([student_scale, teacher_scale]), (0, pair_at * 2 * rows_here), (2, 2 * rows_here)
    )
    grad_unit_z = (
        mixed_own[:, :BOT] * own_scales[0][:, None] - mixed_own[:, BOT:] * own_scales[1][:, None]
    )
    own_new_centre = (
        centre_keep * own_centre + (1.0 - centre_keep) * centre_sum.reshape(protos_here) / count_total
    )
    new_centre = cube_gather(own_new_centre.reshape(1, protos_here), "cxyab").reshape(-1)
    proto_grad, proto_square = proto_grad_pass(
        teacher_z_all, student_z_all, proto_teacher, protos, centre_column, lines(student_scale, teacher_scale)
    )

    grad_bottle = jax.vjp(unit_rows, bottleneck)[1](grad_unit_z)[0].astype(narrow)
    grad_pre_two = gelu_back(pre_two, contract("rb,hb->rh", grad_bottle, w_three)).astype(narrow)
    grad_hidden = cut_columns(contract("rk,hk->rh", grad_pre_two, w_two), first_w2, first_w3, D)
    grad_pre_one = gelu_back(pre_one, grad_hidden).astype(narrow)
    grad_normed = cut_columns(contract("rh,dh->rd", grad_pre_one, w_one), 1, first_w2, 0)
    grads_all = lax.all_gather(
        jnp.pad(jnp.concatenate([grad_pre_one, grad_pre_two, grad_bottle], axis=1), more_rows),
        "dev",
        axis=0,
        axis_index_groups=groups,
    ).reshape(half * pair_rows, 2 * HID + BOT)
    normed_back = lax.ppermute(
        grad_normed[:rows_here], "dev", [(i, i ^ across) for i in range(half, count)]
    )
    own_grad_normed = jnp.where(student_side, grad_normed[rows_here:], normed_back)
    extras = student_parts[2].astype(single)
    grad_chosen, grad_gain, grad_bias = jax.vjp(layer_norm, chosen, extras[2], extras[3])[1](
        own_grad_normed
    )
    image_index = jnp.arange(images_here, dtype=jnp.int32)[:, None]
    grad_stream = (
        jnp.zeros(stream.shape, single)
        .at[image_index, row_index]
        .add(grad_chosen.reshape(images_here, 17, D))
    )

    grad_stream = grad_stream.reshape(images_here * PAD_SEQ, D)
    middle_row = block_rows // 2
    small_rows = -(-(EMBED_ROWS + 6 * LAYERS) // (16 * count)) * 16
    vector_grads = [None] * LAYERS
    firsts = [None] * LAYERS
    seconds = [None] * LAYERS
    waits = ()
    for layer_index in reversed(range(LAYERS)):
        saved, vectors = saved_layers[layer_index], vectors_all[1, layer_index]
        part = LAYERS + layer_index
        grad_stream, weight_grad, late_vectors = mlp_back(
            side, grad_stream, saved, vectors, gathered, part, ()
        )
        grad_stream, weight_grad, early_vectors = attention_back(
            side, grad_stream, saved, vectors, gathered, part, weight_grad, waits
        )
        vector_grads[layer_index] = (late_vectors + early_vectors)[:6]
        owned = split_bits(weight_grad.reshape(D // 128, count, block_rows, 128), 1)
        firsts[layer_index] = cube_scatter([owned], ("c",), (BITS,), 1)[0]
        waits = (firsts[layer_index],)

    def second_round(parts):
        return cube_scatter(parts, ("x", "y"), ("bayx", "bayx"), 1)

    def halves(array):
        return [array[..., : array.shape[-2] // 2, :], array[..., array.shape[-2] // 2 :, :]]

    def table(values):
        return jnp.array(values, jnp.int32)

    columns = [max(bound, 0) // 128 * 128 for bound in bounds[:-1]]
    offsets = [bound - column for bound, column in zip(bounds, columns)]
    offsets[0] = 0
    valid = [0] + sizes[1:]
    thirds = [D + HID + max(bound - D - HID, 0) * (ROW // BOT) for bound in bounds[:-1]]
    partner = me ^ across
    is_third = (me >= first_w3).astype(jnp.int32)
    place = jnp.stack(
        [
            jnp.where(is_third == 1, 0, table(columns)[me]),
            jnp.where(is_third == 1, 0, table(offsets)[me]),
            table(valid)[me],
            jnp.int32(HID),
            table(columns)[partner],
            table(offsets)[partner],
            table(valid)[partner],
            jnp.where(partner < first_w2, 0, HID),
            is_third,
            table(thirds)[me],
        ]
    ).astype(jnp.int32)
    own_block_grad, partner_block_grad = head_grads(place, inputs_all, grads_all, slot, -min(bounds[1], 0))
    block_got = lax.ppermute(partner_block_grad, "dev", [(i, i ^ across) for i in range(half, count)])
    head_block_grad = jnp.where(student_side, own_block_grad, block_got)

    later = [second_round(halves(firsts[i])) for i in range(1, LAYERS)]
    small = embed_back(
        grad_stream,
        patches.reshape(images_here * PATCHES, PIX),
        jnp.where(masked_here, 0.0, 1.0).reshape(images_here * PATCHES, 1),
        jnp.stack([grad_gain, grad_bias]),
        jnp.concatenate(vector_grads),
        small_rows * count,
        [array for pair in later for array in pair] + [own_block_grad],
    )
    small_first = cube_scatter(
        [split_bits(small.reshape(D // 128, count, small_rows, 128), 1)], ("c",), (BITS,), 1
    )[0]
    last = second_round(
        [jnp.concatenate(pair, axis=-2) for pair in zip(halves(firsts[0]), halves(small_first))]
    )
    joined = [jnp.concatenate(parts, axis=-2) for parts in zip(last, *later)]
    done = cube_scatter(joined, ("yba", "xba"), ("bay", "bax"), 1)
    middle_row, small_middle = block_rows // 2, small_rows // 2
    small_block = jnp.concatenate([part[:, middle_row : middle_row + small_middle] for part in done], axis=1)
    blocks = [jnp.concatenate([part[:, :middle_row] for part in done], axis=1)]
    for number in range(LAYERS - 1):
        at = middle_row + small_middle + number * middle_row
        blocks.append(jnp.concatenate([part[:, at : at + middle_row] for part in done], axis=1))
    layer_block = jnp.stack(blocks)

    square_local = (
        jnp.sum(head_block_grad * head_block_grad)
        + jnp.sum(layer_block * layer_block)
        + jnp.sum(small_block * small_block)
        + proto_square[0, 0]
    )
    square_total = cube_sum(square_local.reshape(1, 1))[0, 0]
    small_all = cube_gather(small_block, "cxyab").reshape((count,) + small_block.shape)
    small_all = jnp.transpose(small_all, (0, 2, 1, 3)).reshape(small_rows * count, D)
    embed_grad = small_all[:EMBED_ROWS].reshape(-1)
    vector_grad = small_all[EMBED_ROWS : EMBED_ROWS + 6 * LAYERS].reshape(LAYERS, 6, D)

    behind = lax.ppermute(layer_block[:, :, :6], "dev", step_pairs(count, -1))
    vector_columns = jnp.swapaxes(vector_grad.reshape(LAYERS, 6, D // 128, 128), 1, 2)
    behind = jnp.where(me == count - 1, vector_columns, behind)
    last_rows = lax.dynamic_slice(
        head_block_grad, (jnp.array(sizes, jnp.int32)[me] - GROUP, 0), (GROUP, ROW)
    )
    previous = lax.ppermute(last_rows, "dev", step_pairs(count, 1))
    stem_at = head_span - start_here
    layer_at = drift * me
    place = jnp.stack([stem_at // 128, stem_at % 128, layer_at // 128, layer_at % 128]).astype(jnp.int32)
    stem_lines, layer_lines = own_shards(
        place, head_block_grad, previous, layer_block, behind, lane_rows(stem_piece), lane_rows(layer_piece)
    )
    layer_grad = layer_lines.reshape(LAYERS, -1)[:, :layer_piece]
    stem_grad = stem_lines.reshape(-1)[:stem_piece]
    rest = EMBED_FLAT - stem_piece
    second_part = jnp.concatenate([embed_grad[stem_piece:], stem_grad[rest:]])
    stem_grad = jnp.where(
        me == 0, embed_grad[:stem_piece], jnp.where(me == 1, second_part, stem_grad)
    )

    grad_norm = jnp.sqrt(square_total) / count_total
    factor = jnp.minimum(1.0, clip_limit / (grad_norm + 1e-06)) / count_total
    stem_set = adam_update(stem, stem_moment, stem_second, stem_grad * factor, stem_teacher)
    layer_set = adam_update(layers, layer_moment, layer_second, layer_grad * factor, layer_teacher)
    proto_set = proto_update(factor, protos, proto_moment, proto_second, proto_teacher, proto_grad)
    return (loss_total, count_total, grad_norm, new_centre) + stem_set + layer_set + tuple(proto_set)


def solution(mesh):
    count = mesh.shape["dev"]
    stem_length = -(-(EMBED_FLAT + HEAD_ROWS * ROW) // count) * count
    close = fits(count, stem_length // count, (MATRIX_ROWS + 6) * D // count)
    placed = (
        P("dev", None, None),
        P("dev", None),
        P("dev"),
        P("dev"),
        P("dev"),
        P("dev"),
        P("dev"),
        P(None, "dev"),
        P(None, "dev"),
        P(None, "dev"),
        P(None, "dev"),
        P("dev", None),
        P("dev", None),
        P("dev", None),
        P("dev", None),
        P(),
    )
    return jax.shard_map(
        close_local if close else spread_local,
        mesh=mesh,
        in_specs=placed,
        out_specs=(
            P(),
            P(),
            P(),
            P(),
            P("dev"),
            P("dev"),
            P("dev"),
            P("dev"),
            P("dev"),
            P(None, "dev"),
            P(None, "dev"),
            P(None, "dev"),
            P(None, "dev"),
            P(None, "dev"),
            P("dev", None),
            P("dev", None),
            P("dev", None),
            P("dev", None),
            P("dev", None),
        ),
        check_vma=False,
    )
```

```python
import jax
import jax.numpy as jnp
from jax import lax
from jax.experimental import pallas as pl
from jax.experimental.pallas import tpu as pltpu
from jax.sharding import PartitionSpec as P

D = 384
HEADS = 6
HEAD_DIM = 64
FF = 1536
HID = 2048
BOT = 256
PIX = 588
PATCHES = 256
LAYERS = 2
STEP = 10
SEQ = 257


tau_student = 0.1
tau_teacher = 0.04
clip_limit = 0.003
learn_rate = 0.03
beta_one = 0.9
beta_two = 0.999
adam_eps = 1e-08
decay_rate = 0.04
teacher_keep = 0.8
centre_keep = 0.9
narrow = jnp.bfloat16
single = jnp.float32


def layer_shapes():
    return ((D, 3 * D), (D, D), (D, FF), (FF, D), (6, D))


def stem_shapes():
    return ((PIX, D), (SEQ, D), (4, D), (D, HID), (HID, HID), (HID, BOT))


def cut_flat(flat_row, shape_list):
    pieces = []
    offset = 0
    for shape_pair in shape_list:
        length = shape_pair[0] * shape_pair[1]
        pieces.append(flat_row[offset : offset + length].reshape(shape_pair))
        offset = offset + length
    return pieces


def pack_flat(grad_list, total_length):
    joined = jnp.concatenate([grad_item.reshape(-1) for grad_item in grad_list])
    return jnp.concatenate([joined, jnp.zeros((total_length - joined.shape[0],), single)])


def contract(form, left_arg, right_arg):
    return jnp.einsum(form, left_arg, right_arg, preferred_element_type=single)


def layer_norm(values, gain_row, bias_row):
    centred = values - jnp.mean(values, axis=-1, keepdims=True)
    spread = jnp.mean(centred * centred, axis=-1, keepdims=True)
    return centred * lax.rsqrt(spread + 1e-06) * gain_row + bias_row


def unit_rows(values):
    return values * lax.rsqrt(jnp.sum(values * values, axis=-1, keepdims=True) + 1e-06)


def gelu_back(pre_act, grad_act):
    return jax.vjp(jax.nn.gelu, pre_act)[1](grad_act)[0]


def block_forward(stream, weights):
    w_qkv, w_proj, w_up, w_down, vectors = weights
    vectors = vectors.astype(single)
    batch_size = stream.shape[0]
    normed = layer_norm(stream, vectors[0], vectors[1]).astype(narrow)
    packed = (
        contract("bsd,de->bse", normed, w_qkv)
        .astype(narrow)
        .reshape(batch_size, SEQ, 3, HEADS, HEAD_DIM)
    )
    scores = contract("bqhe,bkhe->bhqk", packed[:, :, 0], packed[:, :, 1]) * HEAD_DIM ** (-0.5)
    top_score = jnp.max(scores, axis=-1, keepdims=True)
    exp_terms = jnp.exp(scores - top_score)
    totals = jnp.sum(exp_terms, axis=-1, keepdims=True)
    log_total = top_score + jnp.log(totals)
    mixed = contract("bhqk,bkhe->bqhe", (exp_terms / totals).astype(narrow), packed[:, :, 2])
    mixed = mixed.astype(narrow).reshape(batch_size, SEQ, D)
    attn_out = contract("bsd,de->bse", mixed, w_proj)
    middle = stream + vectors[2] * attn_out
    normed_two = layer_norm(middle, vectors[3], vectors[4]).astype(narrow)
    pre_act = contract("bsd,df->bsf", normed_two, w_up)
    hidden = jax.nn.gelu(pre_act).astype(narrow)
    mlp_out = contract("bsf,fd->bsd", hidden, w_down)
    saved = (
        stream,
        normed,
        packed,
        log_total,
        mixed,
        attn_out,
        middle,
        normed_two,
        pre_act,
        hidden,
        mlp_out,
    )
    return (middle + vectors[5] * mlp_out, saved)


def block_backward(grad_out, weights, saved):
    w_qkv, w_proj, w_up, w_down, vectors = weights
    vectors = vectors.astype(single)
    (
        stream,
        normed,
        packed,
        log_total,
        mixed,
        attn_out,
        middle,
        normed_two,
        pre_act,
        hidden,
        mlp_out,
    ) = saved
    batch_size = stream.shape[0]
    score_scale = HEAD_DIM ** (-0.5)
    grad_ls_two = jnp.sum(grad_out * mlp_out, axis=(0, 1))
    grad_mlp = (grad_out * vectors[5]).astype(narrow)
    grad_down = contract("bsf,bsd->fd", hidden, grad_mlp)
    grad_pre = gelu_back(pre_act, contract("bsd,fd->bsf", grad_mlp, w_down)).astype(narrow)
    grad_up = contract("bsd,bsf->df", normed_two, grad_pre)
    grad_normed_two = contract("bsf,df->bsd", grad_pre, w_up)
    grad_mid, grad_gain_two, grad_bias_two = jax.vjp(layer_norm, middle, vectors[3], vectors[4])[1](
        grad_normed_two
    )
    grad_mid = grad_mid + grad_out
    grad_ls_one = jnp.sum(grad_mid * attn_out, axis=(0, 1))
    grad_attn = (grad_mid * vectors[2]).astype(narrow)
    grad_proj = contract("bsd,bse->de", mixed, grad_attn)
    grad_mixed = (
        contract("bse,de->bsd", grad_attn, w_proj)
        .astype(narrow)
        .reshape(batch_size, SEQ, HEADS, HEAD_DIM)
    )
    query_rows = packed[:, :, 0]
    key_rows = packed[:, :, 1]
    value_rows = packed[:, :, 2]
    probs = jnp.exp(contract("bqhe,bkhe->bhqk", query_rows, key_rows) * score_scale - log_total)
    grad_probs = contract("bqhe,bkhe->bhqk", grad_mixed, value_rows)
    grad_values = contract("bhqk,bqhe->bkhe", probs.astype(narrow), grad_mixed)
    grad_scores = probs * (grad_probs - jnp.sum(probs * grad_probs, axis=-1, keepdims=True))
    grad_raw = (grad_scores * score_scale).astype(narrow)
    grad_queries = contract("bhqk,bkhe->bqhe", grad_raw, key_rows)
    grad_keys = contract("bhqk,bqhe->bkhe", grad_raw, query_rows)
    grad_packed = (
        jnp.stack([grad_queries, grad_keys, grad_values], axis=2)
        .astype(narrow)
        .reshape(batch_size, SEQ, 3 * D)
    )
    grad_qkv = contract("bsd,bse->de", normed, grad_packed)
    grad_normed = contract("bse,de->bsd", grad_packed, w_qkv)
    grad_in, grad_gain_one, grad_bias_one = jax.vjp(layer_norm, stream, vectors[0], vectors[1])[1](
        grad_normed
    )
    grad_vectors = jnp.stack(
        [grad_gain_one, grad_bias_one, grad_ls_one, grad_gain_two, grad_bias_two, grad_ls_two]
    )
    return (grad_in + grad_mid, (grad_qkv, grad_proj, grad_up, grad_down, grad_vectors))


def embed(stem_parts, image_rows, masked_here, student):
    patch_w, position, extras, w_first, w_second, w_third = stem_parts
    extras = extras.astype(single)
    embedded = contract("gpc,cd->gpd", image_rows, patch_w)
    if student:
        embedded = jnp.where(masked_here[:, :, None], extras[1], embedded)
    cls_rows = jnp.broadcast_to(extras[0], (image_rows.shape[0], 1, D))
    return jnp.concatenate([cls_rows, embedded], axis=1) + position.astype(single)


def embed_backward(grad_stream, image_rows, masked_here):
    grad_cls = jnp.sum(grad_stream[:, 0], axis=0)
    grad_position = jnp.sum(grad_stream, axis=0)
    grad_patch_rows = grad_stream[:, 1:]
    grad_mask_token = jnp.sum(jnp.where(masked_here[:, :, None], grad_patch_rows, 0.0), axis=(0, 1))
    grad_embedded = jnp.where(masked_here[:, :, None], 0.0, grad_patch_rows).astype(narrow)
    grad_patch_w = contract("gpc,gpd->cd", image_rows, grad_embedded)
    return (grad_patch_w, grad_position, grad_cls, grad_mask_token)


def head_forward(stem_parts, proto_rows, stream, row_index):
    patch_w, position, extras, w_first, w_second, w_third = stem_parts
    extras = extras.astype(single)
    chosen = jnp.take_along_axis(stream, row_index[:, :, None], axis=1)
    normed = layer_norm(chosen, extras[2], extras[3]).astype(narrow)
    pre_one = contract("grd,dh->grh", normed, w_first)
    hidden_one = jax.nn.gelu(pre_one).astype(narrow)
    pre_two = contract("grh,hk->grk", hidden_one, w_second)
    hidden_two = jax.nn.gelu(pre_two).astype(narrow)
    bottleneck = contract("grh,hb->grb", hidden_two, w_third)
    unit_z = unit_rows(bottleneck).astype(narrow)
    unit_protos = unit_rows(proto_rows.astype(single)).astype(narrow)
    logits = contract("grb,kb->grk", unit_z, unit_protos)
    return (
        logits,
        (chosen, normed, pre_one, hidden_one, pre_two, hidden_two, bottleneck, unit_z, unit_protos),
    )


def head_backward(grad_logits, stem_parts, saved, row_index, stream_shape):
    patch_w, position, extras, w_first, w_second, w_third = stem_parts
    extras = extras.astype(single)
    chosen, normed, pre_one, hidden_one, pre_two, hidden_two, bottleneck, unit_z, unit_protos = (
        saved
    )
    grad_rounded = grad_logits.astype(narrow)
    grad_unit_z = contract("grk,kb->grb", grad_rounded, unit_protos)
    grad_unit_protos = contract("grk,grb->kb", grad_rounded, unit_z)
    grad_bottle = jax.vjp(unit_rows, bottleneck)[1](grad_unit_z)[0].astype(narrow)
    grad_third = contract("grh,grb->hb", hidden_two, grad_bottle)
    grad_pre_two = gelu_back(pre_two, contract("grb,hb->grh", grad_bottle, w_third)).astype(narrow)
    grad_second = contract("grh,grk->hk", hidden_one, grad_pre_two)
    grad_pre_one = gelu_back(pre_one, contract("grk,hk->grh", grad_pre_two, w_second)).astype(
        narrow
    )
    grad_first = contract("grd,grh->dh", normed, grad_pre_one)
    grad_normed = contract("grh,dh->grd", grad_pre_one, w_first)
    grad_chosen, grad_gain, grad_bias = jax.vjp(layer_norm, chosen, extras[2], extras[3])[1](
        grad_normed
    )
    image_index = jnp.arange(row_index.shape[0], dtype=jnp.int32)[:, None]
    grad_stream = jnp.zeros(stream_shape, single).at[image_index, row_index].add(grad_chosen)
    return (
        grad_stream,
        (grad_first, grad_second, grad_third),
        grad_gain,
        grad_bias,
        grad_unit_protos,
    )


def adam_update(weight, moment, second, grad, teacher):
    new_moment = beta_one * moment + (1.0 - beta_one) * grad
    new_second = beta_two * second + (1.0 - beta_two) * grad * grad
    direction = (
        new_moment
        / (1.0 - beta_one**STEP)
        / (jnp.sqrt(new_second / (1.0 - beta_two**STEP)) + adam_eps)
    )
    new_weight = weight - learn_rate * (direction + decay_rate * weight)
    return (
        new_moment,
        new_second,
        new_weight,
        new_weight.astype(narrow),
        teacher_keep * teacher + (1.0 - teacher_keep) * new_weight,
    )


def spread_local(
    patches,
    masked,
    slot_used,
    stem,
    stem_moment,
    stem_second,
    stem_teacher,
    layers,
    layer_moment,
    layer_second,
    layer_teacher,
    protos,
    proto_moment,
    proto_second,
    proto_teacher,
    centre,
):
    images_here = patches.shape[0]
    row_index = jnp.concatenate([jnp.zeros((images_here, 1), jnp.int32), masked + 1], axis=1)
    masked_here = jnp.any(
        masked[:, :, None] == jnp.arange(PATCHES, dtype=jnp.int32)[None, None, :], axis=1
    )
    kept = slot_used.astype(single)
    teacher_flat, teacher_protos = (
        lax.all_gather(stem_teacher.astype(narrow), "dev", axis=0, tiled=True),
        lax.all_gather(proto_teacher.astype(narrow), "dev", axis=0, tiled=True),
    )
    teacher_parts = cut_flat(teacher_flat, stem_shapes())
    stream = embed(teacher_parts, patches, masked_here, False)
    for layer_index in range(LAYERS):
        teacher_layer = lax.all_gather(
            layer_teacher[layer_index].astype(narrow), "dev", axis=0, tiled=True
        )
        stream = block_forward(stream, cut_flat(teacher_layer, layer_shapes()))[0]
    teacher_logits = head_forward(teacher_parts, teacher_protos, stream, row_index)[0]
    teacher_probs = jax.nn.softmax((teacher_logits - centre) / tau_teacher, axis=-1)
    centre_terms = jnp.sum(kept[:, None] * teacher_logits[:, 0], axis=0)
    student_flat, student_protos = (
        lax.all_gather(stem.astype(narrow), "dev", axis=0, tiled=True),
        lax.all_gather(protos.astype(narrow), "dev", axis=0, tiled=True),
    )
    student_parts = cut_flat(student_flat, stem_shapes())
    stream = embed(student_parts, patches, masked_here, True)
    saved_layers = []
    gathered_layers = []
    for layer_index in range(LAYERS):
        layer_flat = lax.all_gather(layers[layer_index].astype(narrow), "dev", axis=0, tiled=True)
        gathered_layers.append(layer_flat)
        stream, saved = block_forward(stream, cut_flat(layer_flat, layer_shapes()))
        saved_layers.append(saved)
    logits, head_saved = head_forward(student_parts, student_protos, stream, row_index)

    def loss_piece(logit_rows):
        log_probs = jax.nn.log_softmax(logit_rows / tau_student, axis=-1)
        cross = -jnp.sum(teacher_probs * log_probs, axis=-1)
        return jnp.sum(kept * (cross[:, 0] + jnp.mean(cross[:, 1:], axis=1)))

    loss_local, loss_puller = jax.vjp(loss_piece, logits)
    grad_logits = loss_puller(jnp.float32(1.0))[0]
    count_local = jnp.sum(kept)
    loss_total, count_total, centre_total = lax.psum((loss_local, count_local, centre_terms), "dev")
    back_flat, back_protos = (
        lax.all_gather(stem.astype(narrow), "dev", axis=0, tiled=True),
        lax.all_gather(protos.astype(narrow), "dev", axis=0, tiled=True),
    )
    back_parts = cut_flat(back_flat, stem_shapes())
    grad_stream, head_grads, grad_gain, grad_bias, grad_unit_protos = head_backward(
        grad_logits, back_parts, head_saved, row_index, stream.shape
    )
    layer_grads = []
    for layer_index in reversed(range(LAYERS)):
        weight_flat = lax.all_gather(layers[layer_index].astype(narrow), "dev", axis=0, tiled=True)
        grad_stream, block_grads = block_backward(
            grad_stream, cut_flat(weight_flat, layer_shapes()), saved_layers[layer_index]
        )
        layer_grads.insert(
            0,
            lax.psum_scatter(
                pack_flat(block_grads, weight_flat.shape[0]), "dev", scatter_dimension=0, tiled=True
            ),
        )
    grad_patch_w, grad_position, grad_cls, grad_mask_token = embed_backward(
        grad_stream, patches, masked_here
    )
    grad_extras = jnp.stack([grad_cls, grad_mask_token, grad_gain, grad_bias])
    stem_flat_grad = pack_flat(
        (grad_patch_w, grad_position, grad_extras) + head_grads, back_flat.shape[0]
    )
    stem_grad, proto_row_grad = (
        lax.psum_scatter(stem_flat_grad, "dev", scatter_dimension=0, tiled=True),
        lax.psum_scatter(grad_unit_protos, "dev", scatter_dimension=0, tiled=True),
    )
    own_protos = lax.optimization_barrier(protos.astype(narrow)).astype(single)
    proto_grad = jax.vjp(unit_rows, own_protos)[1](proto_row_grad)[0]
    layer_grad = jnp.stack(layer_grads)
    square_local = (
        jnp.sum(stem_grad * stem_grad)
        + jnp.sum(layer_grad * layer_grad)
        + jnp.sum(proto_grad * proto_grad)
    )
    square_total = lax.psum(square_local, "dev")
    grad_norm = jnp.sqrt(square_total) / count_total
    factor = jnp.minimum(1.0, clip_limit / (grad_norm + 1e-06)) / count_total
    new_centre = centre_keep * centre + (1.0 - centre_keep) * centre_total / count_total
    stem_set = adam_update(stem, stem_moment, stem_second, stem_grad * factor, stem_teacher)
    layer_set = adam_update(layers, layer_moment, layer_second, layer_grad * factor, layer_teacher)
    proto_set = adam_update(protos, proto_moment, proto_second, proto_grad * factor, proto_teacher)
    return (
        loss_total,
        count_total,
        grad_norm,
        new_centre,
        stem_set[0],
        stem_set[1],
        stem_set[2],
        stem_set[3],
        stem_set[4],
        layer_set[0],
        layer_set[1],
        layer_set[2],
        layer_set[3],
        layer_set[4],
        proto_set[0],
        proto_set[1],
        proto_set[2],
        proto_set[3],
        proto_set[4],
    )


GROUP = 16
ROW = HID
MATRIX_ROWS = D * 3 + D + FF + FF
EMBED_ROWS = PIX + SEQ + 4
EMBED_FLAT = EMBED_ROWS * D
HEAD_ROWS = D + HID + BOT
BITS = ("b", "a", "y", "x", "c")
MASKS = {"c": 1, "x": 2, "y": 4, "a": 8, "b": 24, "g": 8}


def head_bounds(count, stem_piece):
    bounds = [-(-(stem_piece * device - EMBED_FLAT) // (ROW * GROUP)) * GROUP for device in range(count + 1)]
    bounds[0] = -(-EMBED_FLAT // (ROW * GROUP)) * -GROUP
    bounds[-1] = HEAD_ROWS
    return bounds


def fits(count, stem_piece, layer_piece):
    if count != 1 << len(BITS) or MATRIX_ROWS % (3 * count):
        return False
    bounds = head_bounds(count, stem_piece)
    sizes = [bounds[i + 1] - bounds[i] for i in range(count)]
    return (
        min(sizes) > GROUP
        and bounds[1] <= 0
        and stem_piece < EMBED_FLAT <= 2 * stem_piece
        and D in bounds
        and D + HID in bounds
        and stem_piece * count == EMBED_FLAT + HEAD_ROWS * ROW
    )


def pairs(count, mask):
    return [(i, i ^ mask) for i in range(count)]


def bit_flags(me):
    flags = {name: (me >> (len(BITS) - 1 - place)) & 1 for place, name in enumerate(BITS)}
    flags["g"] = flags["a"] ^ flags["b"]
    return flags


def cube_gather(part, order):
    count = 1 << len(BITS)
    flags = bit_flags(lax.axis_index("dev"))
    held = part[None]
    for name in order:
        got = lax.ppermute(held, "dev", pairs(count, MASKS[name]))
        held = jnp.where(
            flags[name] == 1,
            jnp.concatenate([got, held], axis=0),
            jnp.concatenate([held, got], axis=0),
        )
    return held


def cut(array, names, name, lead):
    flag = bit_flags(lax.axis_index("dev"))[name] == 1
    place = names.index(name) + lead
    low = lax.index_in_dim(array, 0, place, keepdims=False)
    high = lax.index_in_dim(array, 1, place, keepdims=False)
    sent = jnp.where(flag, low, high)
    return (sent if name == "c" else sent.astype(narrow)), jnp.where(flag, high, low), names.replace(name, "")


def move(sent, kept, name):
    return kept + lax.ppermute(sent, "dev", pairs(1 << len(BITS), MASKS[name])).astype(single)


def cube_scatter(array, names, order, lead=0):
    for name in order:
        sent, kept, names = cut(array, names, name, lead)
        array = move(sent, kept, name)
    return array


def cube_sum(values):
    for name in "cxyab":
        values = values + lax.ppermute(values, "dev", pairs(1 << len(BITS), MASKS[name]))
    return values


def split_bits(array, lead=0):
    return array.reshape(array.shape[:lead] + (2,) * len(BITS) + array.shape[lead + 1 :])


def step_pairs(count, step):
    return [(i, i + step) for i in range(count) if 0 <= i + step < count]


def lane_rows(length):
    return -(-length // 1024) * 8


def as_lanes(flat):
    rows = lane_rows(flat.shape[-1])
    gap = rows * 128 - flat.shape[-1]
    padded = jnp.pad(flat, [(0, 0)] * (flat.ndim - 1) + [(0, gap)])
    return padded.reshape(flat.shape[:-1] + (rows, 128))


def shifted(line_ref, row, lane, first, rows, stride):
    spots = lax.broadcasted_iota(jnp.int32, (rows, 128), 1)
    turn = lax.rem(128 - lane, 128)
    here = pltpu.roll(line_ref[pl.ds(row + first, rows, stride=stride), :], turn, 1)
    there = pltpu.roll(line_ref[pl.ds(row + first + 1, rows, stride=stride), :], turn, 1)
    return jnp.where(spots < 128 - lane, here, there)


def blocks_kernel(
    shape,
    place_ref,
    stem_ref,
    after_ref,
    layer_ref,
    before_ref,
    head_ref,
    block_ref,
    embed_ref,
    vector_ref,
    line_ref,
    flat_ref,
):
    front, stem_piece, layer_piece, tail = shape
    stem_lines = stem_ref.shape[1]
    end_row, end_lane = stem_piece // 128, stem_piece % 128
    after_lines = after_ref.shape[1]
    slot = head_ref.shape[1]
    for model in range(2):
        line_ref[pl.ds(0, front), :] = jnp.zeros((front, 128), single)
        line_ref[pl.ds(front, end_row), :] = stem_ref[model, pl.ds(0, end_row), :]
        turned = pltpu.roll(after_ref[model], end_lane, 1)
        spots = lax.broadcasted_iota(jnp.int32, (after_lines, 128), 1)
        line_ref[pl.ds(front + end_row, after_lines), :] = turned
        line_ref[pl.ds(front + end_row + after_lines, 128), :] = jnp.zeros((128, 128), single)
        lower = pltpu.roll(turned, 1, 0)
        first_line = jnp.broadcast_to(stem_ref[model, pl.ds(end_row, 1), :], (after_lines, 128))
        number = lax.broadcasted_iota(jnp.int32, (after_lines, 128), 0)
        lower = jnp.where(number == 0, first_line, lower)
        line_ref[pl.ds(front + end_row, after_lines), :] = jnp.where(spots < end_lane, lower, turned)
        per_row = ROW // 128
        for chunk in range(per_row):
            head_ref[model, :, pl.ds(chunk * 128, 128)] = shifted(
                line_ref, place_ref[0], place_ref[1], chunk, slot, per_row
            ).astype(narrow)
        for chunk in range(D // 128):
            embed_ref[model, :, pl.ds(chunk * 128, 128)] = shifted(
                line_ref, place_ref[2], place_ref[3], chunk, embed_ref.shape[1], D // 128
            ).astype(narrow)
    tail_lines = tail // 128
    layer_lines = layer_ref.shape[1]
    vector_at = tail + layer_piece - tail
    for part in range(layer_ref.shape[0]):
        flat_ref[pl.ds(0, tail_lines), :] = before_ref[part]
        flat_ref[pl.ds(tail_lines, layer_lines), :] = layer_ref[part]
        for chunk in range(D // 128):
            block_ref[part, :, pl.ds(chunk * 128, 128)] = shifted(
                flat_ref, place_ref[4], place_ref[5], chunk, block_ref.shape[1], D // 128
            ).astype(narrow)
            vector_ref[part, :, pl.ds(chunk * 128, 128)] = shifted(
                flat_ref, vector_at // 128, vector_at % 128, chunk, 8, D // 128
            ).astype(narrow)


def own_blocks(place, stems, after, layer_rows, before, shape, slot, block_rows, embed_rows):
    front, stem_piece, layer_piece, tail = shape
    lines = front + stem_piece // 128 + after.shape[1] + slot * ROW // 128
    flats = tail // 128 + layer_rows.shape[1] + 48
    return pl.pallas_call(
        lambda *refs: blocks_kernel(shape, *refs),
        out_shape=[
            jax.ShapeDtypeStruct((2, slot, ROW), narrow),
            jax.ShapeDtypeStruct((2 * LAYERS, block_rows, D), narrow),
            jax.ShapeDtypeStruct((2, embed_rows, D), narrow),
            jax.ShapeDtypeStruct((2 * LAYERS, 8, D), narrow),
        ],
        in_specs=[pl.BlockSpec(memory_space=pltpu.SMEM)] + [pl.BlockSpec(memory_space=pltpu.VMEM)] * 4,
        out_specs=[pl.BlockSpec(memory_space=pltpu.VMEM)] * 4,
        scratch_shapes=[pltpu.VMEM((lines, 128), single), pltpu.VMEM((flats, 128), single)],
        compiler_params=pltpu.CompilerParams(vmem_limit_bytes=40 << 20),
    )(place, stems, after, layer_rows, before)


def shards_kernel(place_ref, head_ref, previous_ref, block_ref, behind_ref, stem_ref, layer_ref, line_ref, flat_ref):
    per_row = ROW // 128
    extra = previous_ref.shape[0]
    slot = head_ref.shape[0]
    for chunk in range(per_row):
        spot = pl.ds(chunk * 128, 128)
        line_ref[pl.ds(chunk, extra, stride=per_row), :] = previous_ref[:, spot]
        line_ref[pl.ds(extra * per_row + chunk, slot, stride=per_row), :] = head_ref[:, spot]
    stem_ref[...] = shifted(line_ref, place_ref[0], place_ref[1], 0, stem_ref.shape[0], 1)
    per_row = D // 128
    rows = block_ref.shape[2]
    for part in range(block_ref.shape[0]):
        for chunk in range(per_row):
            flat_ref[pl.ds(chunk, rows, stride=per_row), :] = block_ref[part, chunk]
            flat_ref[pl.ds(rows * per_row + chunk, 6, stride=per_row), :] = behind_ref[part, chunk]
        layer_ref[part] = shifted(flat_ref, place_ref[2], place_ref[3], 0, layer_ref.shape[1], 1)


def own_shards(place, head_grad, previous, block_grad, behind, stem_lines, layer_lines):
    per_row = ROW // 128
    lines = (head_grad.shape[0] + previous.shape[0]) * per_row + 256
    flats = max(block_grad.shape[2] * 3 + 18, layer_lines + 18) + 16
    return pl.pallas_call(
        shards_kernel,
        out_shape=[
            jax.ShapeDtypeStruct((stem_lines, 128), single),
            jax.ShapeDtypeStruct((block_grad.shape[0], layer_lines, 128), single),
        ],
        in_specs=[pl.BlockSpec(memory_space=pltpu.SMEM)] + [pl.BlockSpec(memory_space=pltpu.VMEM)] * 4,
        out_specs=[pl.BlockSpec(memory_space=pltpu.VMEM)] * 2,
        scratch_shapes=[pltpu.VMEM((lines, 128), single), pltpu.VMEM((flats, 128), single)],
        compiler_params=pltpu.CompilerParams(vmem_limit_bytes=40 << 20),
    )(place, head_grad, previous, block_grad, behind)


PAD_SEQ = 272
GELU_SCALE = 0.7978845608028654
GELU_CUBE = 0.044715


def product_plain(left, right):
    return lax.dot_general(left, right, (((1,), (0,)), ((), ())), preferred_element_type=single)


def product_right(left, right):
    return lax.dot_general(left, right, (((1,), (1,)), ((), ())), preferred_element_type=single)


def product_left(left, right):
    return lax.dot_general(left, right, (((0,), (0,)), ((), ())), preferred_element_type=single)


def norm_parts(values):
    centred = values - jnp.mean(values, axis=-1, keepdims=True)
    spread = lax.rsqrt(jnp.mean(centred * centred, axis=-1, keepdims=True) + 1e-06)
    return centred * spread, spread


def norm_back(grad, unit, spread, gain):
    grad_unit = grad * gain
    mean_one = jnp.mean(grad_unit, axis=-1, keepdims=True)
    mean_two = jnp.mean(grad_unit * unit, axis=-1, keepdims=True)
    return spread * (grad_unit - mean_one - unit * mean_two)


def gelu_tanh(values):
    return jnp.tanh(GELU_SCALE * (values + GELU_CUBE * values * values * values))


def fetch_rows(side_ref, part, gathered_ref, flat_ref, sems):
    quarter = flat_ref.shape[0] // 4
    side = side_ref[0]
    first, second = side * quarter, (1 - side) * quarter
    copies = [
        pltpu.make_async_copy(
            gathered_ref.at[pl.ds(at, quarter), owner, part],
            flat_ref.at[pl.ds(spot * quarter, quarter)],
            sems.at[spot],
        )
        for spot, (at, owner) in enumerate(((first, 0), (second, 0), (second, 1), (first, 1)))
    ]
    for copy in copies:
        copy.start()
    for copy in copies:
        copy.wait()


def matrix_rows(flat_ref, first_row, length):
    rows = flat_ref.shape[1]
    low, high = first_row // rows, -(-(first_row + length) // rows)
    lines = flat_ref[pl.ds(low, high - low)].reshape((high - low) * rows, D)
    at = first_row - low * rows
    return lines[at : at + length]


def spread_columns(flat_ref, first_row, width, wide_ref, out_ref):
    length = width * D
    lines = matrix_rows(flat_ref, first_row, length)
    for column in range(D // 128):
        lane = slice(column * 128, (column + 1) * 128)
        wide_ref[column, pl.ds(0, length), :] = lines[:, lane].astype(single)
    for group in range(width):
        for column in range(D // 128):
            out_ref[group, :, pl.ds(column * 128, 128)] = wide_ref[
                column, pl.ds(group, D, stride=width), :
            ].astype(narrow)


def head_lanes(values, odd):
    lanes = lax.broadcasted_iota(jnp.int32, values.shape, 1)
    return jnp.where((lanes >= HEAD_DIM) == odd, values, jnp.zeros_like(values))


def join_lanes(even, odd):
    lanes = lax.broadcasted_iota(jnp.int32, even.shape, 1)
    return jnp.where(lanes >= HEAD_DIM, odd, even)


def soft_rows(query, key):
    scores = product_right(query, key) * HEAD_DIM ** (-0.5)
    spots = lax.broadcasted_iota(jnp.int32, scores.shape, 1)
    scores = jnp.where(spots < SEQ, scores, -1e30)
    terms = jnp.exp(scores - jnp.max(scores, axis=-1, keepdims=True))
    return terms / jnp.sum(terms, axis=-1, keepdims=True)


def forward_kernel(part, keep, side_ref, stream_ref, vector_ref, gathered_ref, *refs):
    out_ref = refs[0]
    if keep:
        packed_ref, mixed_ref, attn_ref, pre_ref, mlp_ref = refs[1:6]
        flat_ref, wide_ref, qkv_ref, up_ref, hidden_ref, sems = refs[6:]
    else:
        flat_ref, wide_ref, qkv_ref, up_ref, hidden_ref, packed_ref, mixed_ref, sems = refs[1:]
    fetch_rows(side_ref, part, gathered_ref, flat_ref, sems)
    spread_columns(flat_ref, 0, 3, wide_ref, qkv_ref)
    spread_columns(flat_ref, 4 * D, FF // D, wide_ref, up_ref)
    w_proj = matrix_rows(flat_ref, 3 * D, D)
    w_down = matrix_rows(flat_ref, 4 * D + FF, FF)
    vectors = vector_ref[...].astype(single)
    stream = stream_ref[...]
    normed = (norm_parts(stream)[0] * vectors[0:1] + vectors[1:2]).astype(narrow)
    for group in range(3):
        packed_ref[:, pl.ds(group * D, D)] = product_plain(normed, qkv_ref[group]).astype(narrow)
    for image in range(stream.shape[0] // PAD_SEQ):
        rows = pl.ds(image * PAD_SEQ, PAD_SEQ)
        for pair in range(HEADS // 2):
            query, key, value = [
                packed_ref[rows, pl.ds(group * D + pair * 128, 128)] for group in range(3)
            ]
            done = [
                product_plain(soft_rows(head_lanes(query, odd), key).astype(narrow), value)
                for odd in (False, True)
            ]
            mixed_ref[rows, pl.ds(pair * 128, 128)] = join_lanes(*done).astype(narrow)
    attn = product_plain(mixed_ref[...], w_proj)
    middle = stream + vectors[2:3] * attn
    normed_two = (norm_parts(middle)[0] * vectors[3:4] + vectors[4:5]).astype(narrow)
    for group in range(FF // D):
        spot = pl.ds(group * D, D)
        pre = product_plain(normed_two, up_ref[group])
        if keep:
            pre_ref[:, spot] = pre
        hidden_ref[:, spot] = (0.5 * pre * (1.0 + gelu_tanh(pre))).astype(narrow)
    mlp = product_plain(hidden_ref[...], w_down)
    out_ref[...] = middle + vectors[5:6] * mlp
    if keep:
        attn_ref[...] = attn
        mlp_ref[...] = mlp


def layer_scratch(gathered):
    rows, blocks = gathered.shape[3], 2 * gathered.shape[0]
    return [
        pltpu.VMEM((blocks, rows, D), narrow),
        pltpu.VMEM((D // 128, FF, 128), single),
        pltpu.VMEM((3, D, D), narrow),
        pltpu.VMEM((FF // D, D, D), narrow),
    ]


def layer_specs_in(count):
    return (
        [pl.BlockSpec(memory_space=pltpu.SMEM)]
        + [pl.BlockSpec(memory_space=pltpu.VMEM)] * (count - 2)
        + [pl.BlockSpec(memory_space=pl.ANY)]
    )


def layer_forward(side, stream, vectors, gathered, part, keep):
    tokens = stream.shape[0]
    shapes = [jax.ShapeDtypeStruct((tokens, D), single)]
    extra = [
        jax.ShapeDtypeStruct((tokens, 3 * D), narrow),
        jax.ShapeDtypeStruct((tokens, D), narrow),
        jax.ShapeDtypeStruct((tokens, D), single),
        jax.ShapeDtypeStruct((tokens, FF), single),
        jax.ShapeDtypeStruct((tokens, D), single),
    ]
    scratch = layer_scratch(gathered) + [pltpu.VMEM((tokens, FF), narrow)]
    if keep:
        shapes = shapes + extra
    else:
        scratch = scratch + [pltpu.VMEM((tokens, 3 * D), narrow), pltpu.VMEM((tokens, D), narrow)]
    scratch.append(pltpu.SemaphoreType.DMA((4,)))
    return pl.pallas_call(
        lambda *refs: forward_kernel(part, keep, *refs),
        out_shape=shapes,
        in_specs=layer_specs_in(4),
        out_specs=[pl.BlockSpec(memory_space=pltpu.VMEM)] * len(shapes),
        scratch_shapes=scratch,
        compiler_params=pltpu.CompilerParams(vmem_limit_bytes=56 << 20),
        cost_estimate=pl.CostEstimate(flops=2 * 10**9, bytes_accessed=2 * 10**7, transcendentals=2 * 10**6),
    )(side, stream, vectors, gathered)


def mlp_back_kernel(
    part,
    side_ref,
    grad_ref,
    stream_ref,
    attn_ref,
    pre_ref,
    mlp_ref,
    vector_ref,
    gathered_ref,
    *refs,
):
    grad_mid_ref, all_grad_ref, vector_grad_ref = refs[-10:-7]
    flat_ref, wide_ref, up_ref, hidden_ref, grad_pre_ref, weight_grad_ref, sems = refs[-7:]
    fetch_rows(side_ref, part, gathered_ref, flat_ref, sems)
    spread_columns(flat_ref, 4 * D, FF // D, wide_ref, up_ref)
    w_down = matrix_rows(flat_ref, 4 * D + FF, FF)
    vectors = vector_ref[...].astype(single)
    grad_out = grad_ref[...]
    vector_grad_ref[...] = jnp.zeros_like(vector_grad_ref)
    attn = attn_ref[...]
    middle = stream_ref[...] + vectors[2:3] * attn
    unit_two, spread_two = norm_parts(middle)
    normed_two = (unit_two * vectors[3:4] + vectors[4:5]).astype(narrow)
    vector_grad_ref[pl.ds(5, 1), :] = jnp.sum(grad_out * mlp_ref[...], axis=0, keepdims=True)
    grad_mlp = (grad_out * vectors[5:6]).astype(narrow)
    grad_normed_two = jnp.zeros_like(grad_out)
    for group in range(FF // D):
        spot = pl.ds(group * D, D)
        pre = pre_ref[:, spot]
        bent = gelu_tanh(pre)
        hidden_ref[:, spot] = (0.5 * pre * (1.0 + bent)).astype(narrow)
        slope = 0.5 * (1.0 + bent) + 0.5 * pre * (1.0 - bent * bent) * GELU_SCALE * (
            1.0 + 3.0 * GELU_CUBE * pre * pre
        )
        grad_hidden = product_right(grad_mlp, w_down[group * D : (group + 1) * D])
        grad_pre = (grad_hidden * slope).astype(narrow)
        grad_pre_ref[:, spot] = grad_pre
        grad_normed_two = grad_normed_two + product_right(grad_pre, up_ref[group])
    for group in range(FF // D):
        spot = pl.ds(group * D, D)
        up_grad = product_left(normed_two, grad_pre_ref[:, spot])
        down_grad = product_left(hidden_ref[:, spot], grad_mlp)
        for column in range(D // 128):
            lane = slice(column * 128, (column + 1) * 128)
            weight_grad_ref[column, pl.ds(group, D, stride=FF // D), :] = up_grad[:, lane]
            weight_grad_ref[column, pl.ds(FF + group * D, D), :] = down_grad[:, lane]
    vector_grad_ref[pl.ds(3, 1), :] = jnp.sum(grad_normed_two * unit_two, axis=0, keepdims=True)
    vector_grad_ref[pl.ds(4, 1), :] = jnp.sum(grad_normed_two, axis=0, keepdims=True)
    grad_mid = grad_out + norm_back(grad_normed_two, unit_two, spread_two, vectors[3:4])
    vector_grad_ref[pl.ds(2, 1), :] = jnp.sum(grad_mid * attn, axis=0, keepdims=True)
    grad_mid_ref[...] = grad_mid
    store_rows(weight_grad_ref, all_grad_ref, 4 * D, sems.at[0])


def attention_back_kernel(
    part,
    side_ref,
    grad_ref,
    stream_ref,
    packed_ref,
    mixed_ref,
    vector_ref,
    gathered_ref,
    *refs,
):
    grad_in_ref, all_grad_ref, vector_grad_ref = refs[-10:-7]
    flat_ref, wide_ref, qkv_ref, grad_mixed_ref, grad_packed_ref, weight_grad_ref, sems = refs[-7:]
    fetch_rows(side_ref, part, gathered_ref, flat_ref, sems)
    spread_columns(flat_ref, 0, 3, wide_ref, qkv_ref)
    w_proj = matrix_rows(flat_ref, 3 * D, D)
    vectors = vector_ref[...].astype(single)
    vector_grad_ref[...] = jnp.zeros_like(vector_grad_ref)
    grad_mid = grad_ref[...]
    stream = stream_ref[...]
    grad_attn = (grad_mid * vectors[2:3]).astype(narrow)
    proj_grad = product_left(mixed_ref[...], grad_attn)
    for column in range(D // 128):
        weight_grad_ref[column, pl.ds(3 * D, D), :] = proj_grad[:, column * 128 : (column + 1) * 128]
    grad_mixed_ref[...] = product_right(grad_attn, w_proj).astype(narrow)
    for image in range(stream.shape[0] // PAD_SEQ):
        rows = pl.ds(image * PAD_SEQ, PAD_SEQ)
        for pair in range(HEADS // 2):
            query, key, value = [
                packed_ref[rows, pl.ds(group * D + pair * 128, 128)] for group in range(3)
            ]
            grad_mixed = grad_mixed_ref[rows, pl.ds(pair * 128, 128)]
            parts = []
            for odd in (False, True):
                probs = soft_rows(head_lanes(query, odd), key)
                grad_probs = product_right(head_lanes(grad_mixed, odd), value)
                grad_value = product_left(probs.astype(narrow), grad_mixed)
                grad_scores = probs * (grad_probs - jnp.sum(probs * grad_probs, axis=-1, keepdims=True))
                grad_raw = (grad_scores * HEAD_DIM ** (-0.5)).astype(narrow)
                parts.append((product_plain(grad_raw, key), product_left(grad_raw, query), grad_value))
            for group in range(3):
                grad_packed_ref[rows, pl.ds(group * D + pair * 128, 128)] = join_lanes(
                    parts[0][group], parts[1][group]
                ).astype(narrow)
    unit_one, spread_one = norm_parts(stream)
    normed = (unit_one * vectors[0:1] + vectors[1:2]).astype(narrow)
    grad_normed = jnp.zeros_like(grad_mid)
    for group in range(3):
        grad_part = grad_packed_ref[:, pl.ds(group * D, D)]
        grad_normed = grad_normed + product_right(grad_part, qkv_ref[group])
        qkv_grad = product_left(normed, grad_part)
        for column in range(D // 128):
            lane = slice(column * 128, (column + 1) * 128)
            weight_grad_ref[column, pl.ds(group, D, stride=3), :] = qkv_grad[:, lane]
    vector_grad_ref[pl.ds(0, 1), :] = jnp.sum(grad_normed * unit_one, axis=0, keepdims=True)
    vector_grad_ref[pl.ds(1, 1), :] = jnp.sum(grad_normed, axis=0, keepdims=True)
    grad_in_ref[...] = grad_mid + norm_back(grad_normed, unit_one, spread_one, vectors[0:1])
    store_rows(weight_grad_ref, all_grad_ref, 0, sems.at[0])


def store_rows(weight_grad_ref, all_grad_ref, first_row, sem):
    copy = pltpu.make_async_copy(
        weight_grad_ref, all_grad_ref.at[:, pl.ds(first_row, weight_grad_ref.shape[1])], sem
    )
    copy.start()
    copy.wait()


def layer_back(kernel, part, weight_rows, side, inputs, vectors, gathered, started, waits, columns, buffers):
    tokens = inputs[0].shape[0]
    rows, blocks = gathered.shape[3], 2 * gathered.shape[0]
    return pl.pallas_call(
        lambda *refs: kernel(part, *refs),
        out_shape=[
            jax.ShapeDtypeStruct((tokens, D), single),
            jax.ShapeDtypeStruct((D // 128, MATRIX_ROWS, 128), single),
            jax.ShapeDtypeStruct((8, D), single),
        ],
        in_specs=layer_specs_in(len(inputs) + 3)
        + [pl.BlockSpec(memory_space=pl.ANY)] * (len(started) + len(waits)),
        out_specs=[
            pl.BlockSpec(memory_space=pltpu.VMEM),
            pl.BlockSpec(memory_space=pl.ANY),
            pl.BlockSpec(memory_space=pltpu.VMEM),
        ],
        input_output_aliases={len(inputs) + 3: 1} if started else {},
        scratch_shapes=[
            pltpu.VMEM((blocks, rows, D), narrow),
            pltpu.VMEM((D // 128, columns * D, 128), single),
            pltpu.VMEM((columns, D, D), narrow),
        ]
        + [pltpu.VMEM((tokens, width), narrow) for width in buffers]
        + [pltpu.VMEM((D // 128, weight_rows, 128), single), pltpu.SemaphoreType.DMA((4,))],
        compiler_params=pltpu.CompilerParams(vmem_limit_bytes=56 << 20),
        cost_estimate=pl.CostEstimate(flops=5 * 10**9, bytes_accessed=4 * 10**7, transcendentals=2 * 10**6),
    )(side, *inputs, vectors, gathered, *started, *waits)


def mlp_back(side, grad_out, saved, vectors, gathered, part, waits):
    stream, packed, mixed, attn, pre, mlp = saved
    return layer_back(
        mlp_back_kernel, part, 2 * FF, side, (grad_out, stream, attn, pre, mlp), vectors, gathered, (), waits,
        FF // D, (FF, FF),
    )


def attention_back(side, grad_mid, saved, vectors, gathered, part, started, waits):
    stream, packed, mixed, attn, pre, mlp = saved
    return layer_back(
        attention_back_kernel, part, 4 * D, side, (grad_mid, stream, packed, mixed), vectors, gathered, (started,), waits,
        3, (D, 3 * D),
    )


def after(value, *tokens):
    def kernel(*refs):
        refs[-1][...] = refs[0][...]

    return pl.pallas_call(
        kernel,
        out_shape=jax.ShapeDtypeStruct(value.shape, value.dtype),
        in_specs=[pl.BlockSpec(memory_space=pltpu.VMEM)] + [pl.BlockSpec(memory_space=pl.ANY)] * len(tokens),
        out_specs=pl.BlockSpec(memory_space=pltpu.VMEM),
    )(value, *tokens)


def embed_back_kernel(grad_ref, patch_ref, shown_ref, gain_ref, vector_ref, *refs):
    out_ref = refs[-1]
    grad = grad_ref[...]
    images = grad.shape[0] // PAD_SEQ
    shown = shown_ref[...]
    position = jnp.zeros((PAD_SEQ, D), single)
    token = jnp.zeros((1, D), single)
    patch_grads = []
    for image in range(images):
        here = grad[image * PAD_SEQ : (image + 1) * PAD_SEQ]
        position = position + here
        rows = here[1:SEQ]
        seen = shown[image * PATCHES : (image + 1) * PATCHES]
        token = token + jnp.sum(rows * (1.0 - seen), axis=0, keepdims=True)
        patch_grads.append((rows * seen).astype(narrow))
    patch_grad = product_left(patch_ref[...], jnp.concatenate(patch_grads))
    out_ref[...] = jnp.zeros_like(out_ref)
    for column in range(D // 128):
        lane = slice(column * 128, (column + 1) * 128)
        out_ref[column, pl.ds(0, PIX), :] = patch_grad[:, lane]
        out_ref[column, pl.ds(PIX, SEQ), :] = position[:SEQ, lane]
        out_ref[column, pl.ds(PIX + SEQ, 1), :] = position[0:1, lane]
        out_ref[column, pl.ds(PIX + SEQ + 1, 1), :] = token[:, lane]
        out_ref[column, pl.ds(PIX + SEQ + 2, 2), :] = gain_ref[:, lane]
        out_ref[column, pl.ds(EMBED_ROWS, vector_ref.shape[0]), :] = vector_ref[:, lane]


def embed_back(grad, patch_rows, shown, gains, vector_grads, rows, waits):
    return pl.pallas_call(
        embed_back_kernel,
        out_shape=jax.ShapeDtypeStruct((D // 128, rows, 128), single),
        in_specs=[pl.BlockSpec(memory_space=pltpu.VMEM)] * 5 + [pl.BlockSpec(memory_space=pl.ANY)] * len(waits),
        out_specs=pl.BlockSpec(memory_space=pltpu.VMEM),
        compiler_params=pltpu.CompilerParams(vmem_limit_bytes=40 << 20),
        cost_estimate=pl.CostEstimate(flops=10**9, bytes_accessed=2 * 10**7, transcendentals=0),
    )(grad, patch_rows, shown, gains, vector_grads, *waits)


def proto_units(values):
    rounded = values.astype(narrow).astype(single)
    scale = lax.rsqrt(jnp.sum(rounded * rounded, axis=-1, keepdims=True) + 1e-06)
    return rounded, scale, (rounded * scale).astype(narrow)


def proto_terms(teacher_z, student_z, teacher_unit, student_unit, centre_column):
    teacher_logits = product_right(teacher_unit, teacher_z)
    logits = product_right(student_unit, student_z)
    teacher_exp = jnp.exp((teacher_logits - centre_column) * (1.0 / tau_teacher))
    student_exp = jnp.exp(logits * (1.0 / tau_student))
    return teacher_logits, logits, teacher_exp, student_exp


def logits_kernel(
    teacher_z_ref,
    student_z_ref,
    teacher_ref,
    student_ref,
    centre_ref,
    class_ref,
    mixed_ref,
    sums_ref,
    centre_sum_ref,
    student_mix_ref,
    teacher_mix_ref,
    totals_ref,
):
    step = pl.program_id(0)

    @pl.when(step == 0)
    def _():
        student_mix_ref[...] = jnp.zeros_like(student_mix_ref)
        teacher_mix_ref[...] = jnp.zeros_like(teacher_mix_ref)
        totals_ref[...] = jnp.zeros_like(totals_ref)

    teacher_unit = proto_units(teacher_ref[...])[2]
    student_unit = proto_units(student_ref[...])[2]
    teacher_logits, logits, teacher_exp, student_exp = proto_terms(
        teacher_z_ref[...], student_z_ref[...], teacher_unit, student_unit, centre_ref[...]
    )
    totals_ref[pl.ds(0, 1), :] += jnp.sum(teacher_exp, axis=0, keepdims=True)
    totals_ref[pl.ds(1, 1), :] += jnp.sum(student_exp, axis=0, keepdims=True)
    totals_ref[pl.ds(2, 1), :] += jnp.sum(teacher_exp * logits, axis=0, keepdims=True)
    centre_sum_ref[...] = jnp.sum(teacher_logits * class_ref[0:1], axis=1, keepdims=True)
    student_mix_ref[...] += product_left(student_unit, student_exp.astype(narrow))
    teacher_mix_ref[...] += product_left(student_unit, teacher_exp.astype(narrow))

    @pl.when(step == pl.num_programs(0) - 1)
    def _():
        mixed_ref[:, pl.ds(0, BOT)] = student_mix_ref[...].T
        mixed_ref[:, pl.ds(BOT, BOT)] = teacher_mix_ref[...].T
        sums_ref[...] = totals_ref[...]


def proto_specs(rows, block):
    whole = pl.BlockSpec((rows, BOT), lambda i: (0, 0))
    table = pl.BlockSpec((block, BOT), lambda i: (i, 0))
    column = pl.BlockSpec((block, 1), lambda i: (i, 0))
    lines = pl.BlockSpec((8, rows), lambda i: (0, 0))
    return whole, table, column, lines


def logits_pass(teacher_z, student_z, teacher, student, centre_column, class_lines):
    rows, protos_here = teacher_z.shape[0], student.shape[0]
    block = protos_here // 4
    whole, table, column, lines = proto_specs(rows, block)
    return pl.pallas_call(
        logits_kernel,
        grid=(4,),
        out_shape=[
            jax.ShapeDtypeStruct((rows, 2 * BOT), single),
            jax.ShapeDtypeStruct((8, rows), single),
            jax.ShapeDtypeStruct((protos_here, 1), single),
        ],
        in_specs=[whole, whole, table, table, column, lines],
        out_specs=[pl.BlockSpec((rows, 2 * BOT), lambda i: (0, 0)), lines, column],
        scratch_shapes=[
            pltpu.VMEM((BOT, rows), single),
            pltpu.VMEM((BOT, rows), single),
            pltpu.VMEM((8, rows), single),
        ],
        compiler_params=pltpu.CompilerParams(vmem_limit_bytes=56 << 20),
        cost_estimate=pl.CostEstimate(flops=5 * 10**9, bytes_accessed=10**7, transcendentals=5 * 10**6),
    )(teacher_z, student_z, teacher, student, centre_column, class_lines)


def proto_grad_kernel(
    teacher_z_ref, student_z_ref, teacher_ref, student_ref, centre_ref, scale_ref, *refs
):
    grad_ref, square_ref = refs[-2:]
    step = pl.program_id(0)

    @pl.when(step == 0)
    def _():
        square_ref[...] = jnp.zeros_like(square_ref)

    teacher_unit = proto_units(teacher_ref[...])[2]
    rounded, scale, student_unit = proto_units(student_ref[...])
    student_z = student_z_ref[...]
    _, _, teacher_exp, student_exp = proto_terms(
        teacher_z_ref[...], student_z, teacher_unit, student_unit, centre_ref[...]
    )
    grad_logits = (student_exp * scale_ref[0:1] - teacher_exp * scale_ref[1:2]).astype(narrow)
    unit_grad = product_plain(grad_logits, student_z)
    along = jnp.sum(unit_grad * rounded, axis=-1, keepdims=True)
    grad = scale * (unit_grad - rounded * (along * scale * scale))
    grad_ref[...] = grad
    square_ref[...] += jnp.broadcast_to(jnp.sum(grad * grad), square_ref.shape)


def proto_grad_pass(teacher_z, student_z, teacher, student, centre_column, scale_lines, waits):
    rows, protos_here = teacher_z.shape[0], student.shape[0]
    block = protos_here // 4
    whole, table, column, lines = proto_specs(rows, block)
    return pl.pallas_call(
        proto_grad_kernel,
        grid=(4,),
        out_shape=[
            jax.ShapeDtypeStruct((protos_here, BOT), single),
            jax.ShapeDtypeStruct((8, 128), single),
        ],
        in_specs=[whole, whole, table, table, column, lines]
        + [pl.BlockSpec(memory_space=pl.ANY)] * len(waits),
        out_specs=[table, pl.BlockSpec((8, 128), lambda i: (0, 0))],
        compiler_params=pltpu.CompilerParams(vmem_limit_bytes=56 << 20),
        cost_estimate=pl.CostEstimate(flops=4 * 10**9, bytes_accessed=10**7, transcendentals=5 * 10**6),
    )(teacher_z, student_z, teacher, student, centre_column, scale_lines, *waits)


def proto_update(factor, student, moment, second, teacher, grad):
    def kernel(factor_ref, *refs):
        weight, moment, second, teacher, grad = [ref[...] for ref in refs[:5]]
        done = adam_update(weight, moment, second, grad * factor_ref[0], teacher)
        for ref, value in zip(refs[5:], done):
            ref[...] = value

    block = student.shape[0] // 4
    table = pl.BlockSpec((block, BOT), lambda i: (i, 0))
    return pl.pallas_call(
        kernel,
        grid=(4,),
        out_shape=[
            jax.ShapeDtypeStruct(student.shape, narrow if number == 3 else single) for number in range(5)
        ],
        in_specs=[pl.BlockSpec(memory_space=pltpu.SMEM)] + [table] * 5,
        out_specs=[table] * 5,
        compiler_params=pltpu.CompilerParams(vmem_limit_bytes=40 << 20),
        cost_estimate=pl.CostEstimate(flops=10**7, bytes_accessed=2 * 10**7, transcendentals=0),
    )(factor.reshape(1), student, moment, second, teacher, grad)


def head_grads_kernel(
    place_ref, inputs_ref, grads_ref, *refs,
):
    own_ref, partner_ref, window_ref, rows_ref, product_ref, third_ref, bottle_ref, line_ref, sems = refs[-9:]
    slot = own_ref.shape[0]
    lead = product_ref.shape[0] - window_ref.shape[1]
    number = lax.broadcasted_iota(jnp.int32, (slot, 1), 0)
    product_ref[pl.ds(0, lead), :] = jnp.zeros((lead, ROW), single)

    def block(at, out_ref):
        column = pl.multiple_of(place_ref[at], 128)
        grad_column = pl.multiple_of(place_ref[at + 3], 128)
        copies = [
            pltpu.make_async_copy(
                inputs_ref.at[:, pl.ds(column, window_ref.shape[1])], window_ref, sems.at[0]
            ),
            pltpu.make_async_copy(grads_ref.at[:, pl.ds(grad_column, ROW)], rows_ref, sems.at[1]),
        ]
        for copy in copies:
            copy.start()
        for copy in copies:
            copy.wait()
        window = window_ref[...]
        for piece in range(4):
            spot = pl.ds(piece * (ROW // 4), ROW // 4)
            product_ref[pl.ds(lead, window.shape[1]), spot] = product_left(window, rows_ref[:, spot])
        from_row = pl.multiple_of(lead + place_ref[at + 1], 8)
        kept = jnp.where(number < place_ref[at + 2], product_ref[pl.ds(from_row, slot), :], 0.0)
        out_ref[...] = kept.astype(out_ref.dtype)

    @pl.when(place_ref[8] == 0)
    def _():
        block(0, own_ref)

    @pl.when(place_ref[8] == 1)
    def _():
        column = pl.multiple_of(place_ref[9], 128)
        copies = [
            pltpu.make_async_copy(
                inputs_ref.at[:, pl.ds(column, third_ref.shape[1])], third_ref, sems.at[0]
            ),
            pltpu.make_async_copy(grads_ref.at[:, pl.ds(2 * HID, BOT)], bottle_ref, sems.at[1]),
        ]
        for copy in copies:
            copy.start()
        for copy in copies:
            copy.wait()
        third = product_left(third_ref[...], bottle_ref[...])
        for lane in range(BOT // 128):
            line_ref[lane] = third[:, lane * 128 : (lane + 1) * 128]
        for group in range(ROW // BOT):
            for lane in range(BOT // 128):
                value = line_ref[lane, pl.ds(group, slot, stride=ROW // BOT), :]
                own_ref[:, pl.ds(group * BOT + lane * 128, 128)] = jnp.where(
                    number < place_ref[2], value, 0.0
                )

    block(4, partner_ref)


def head_grads(place, inputs_all, grads_all, slot, lead, waits):
    rows = inputs_all.shape[0]
    wide = slot * ROW // BOT
    return pl.pallas_call(
        head_grads_kernel,
        out_shape=[jax.ShapeDtypeStruct((slot, ROW), kind) for kind in (single, narrow)],
        in_specs=[pl.BlockSpec(memory_space=pltpu.SMEM)]
        + [pl.BlockSpec(memory_space=pl.ANY)] * (2 + len(waits)),
        out_specs=[pl.BlockSpec(memory_space=pltpu.VMEM)] * 2,
        scratch_shapes=[
            pltpu.VMEM((rows, 256), narrow),
            pltpu.VMEM((rows, ROW), narrow),
            pltpu.VMEM((lead + 256, ROW), single),
            pltpu.VMEM((rows, wide), narrow),
            pltpu.VMEM((rows, BOT), narrow),
            pltpu.VMEM((BOT // 128, wide, 128), single),
            pltpu.SemaphoreType.DMA((2,)),
        ],
        compiler_params=pltpu.CompilerParams(vmem_limit_bytes=56 << 20),
        cost_estimate=pl.CostEstimate(flops=4 * 10**9, bytes_accessed=2 * 10**7, transcendentals=0),
    )(place, inputs_all, grads_all, *waits)


def close_local(
    patches,
    masked,
    slot_used,
    stem,
    stem_moment,
    stem_second,
    stem_teacher,
    layers,
    layer_moment,
    layer_second,
    layer_teacher,
    protos,
    proto_moment,
    proto_second,
    proto_teacher,
    centre,
):
    count = 1 << len(BITS)
    half = count // 2
    me = lax.axis_index("dev")
    across = MASKS["b"]
    student_side = me >= half
    groups = [list(range(half)), list(range(half, count))]
    quarter = half // 2
    swap = jnp.where(student_side, quarter, 0)
    side = student_side.astype(jnp.int32).reshape(1)
    images_here = patches.shape[0]
    rows_here = images_here * 17
    pair_rows = -(-2 * rows_here // 16) * 16
    more_rows = pair_rows - 2 * rows_here
    stem_piece = stem.shape[0]
    layer_piece = layers.shape[1]
    block_rows = MATRIX_ROWS // count
    block = block_rows * D
    tail = layer_piece * count - MATRIX_ROWS * D
    drift = layer_piece - block
    bounds = head_bounds(count, stem_piece)
    sizes = [bounds[i + 1] - bounds[i] for i in range(count)]
    slot = max(sizes)
    starts = [b * ROW + EMBED_FLAT - stem_piece * i for i, b in enumerate(bounds[:-1])]
    first_w2 = bounds.index(D)
    first_w3 = bounds.index(D + HID)
    row_index = jnp.concatenate([jnp.zeros((images_here, 1), jnp.int32), masked + 1], axis=1)
    masked_here = jnp.any(
        masked[:, :, None] == jnp.arange(PATCHES, dtype=jnp.int32)[None, None, :], axis=1
    )
    kept = slot_used.astype(single)

    front = 16
    early_rows = -(-stem_piece // D)
    late_start = early_rows * D - stem_piece
    embed_rows = -(-early_rows // 16) * 16
    own_layers = jnp.concatenate([layer_teacher, layers])
    own_tail = own_layers[:, layer_piece - tail :].reshape(2 * LAYERS, tail // 128, 128)
    before = lax.ppermute(own_tail, "dev", step_pairs(count, 1))
    head_span = GROUP * ROW
    stems = jnp.stack([as_lanes(stem_teacher), as_lanes(stem)])
    stems_next = lax.ppermute(stems[:, : head_span // 128], "dev", step_pairs(count, -1))
    start_here = jnp.array(starts, jnp.int32)[me]
    head_at = start_here + front * 128
    embed_at = front * 128 + jnp.where(me == 0, 0, late_start)
    block_at = tail - drift * me
    place = jnp.stack(
        [head_at // 128, head_at % 128, embed_at // 128, embed_at % 128, block_at // 128, block_at % 128]
    ).astype(jnp.int32)
    head_blocks, layer_blocks, embed_blocks, vector_blocks = own_blocks(
        place,
        stems,
        stems_next,
        as_lanes(own_layers),
        before,
        (front, stem_piece, layer_piece, tail),
        slot,
        block_rows,
        embed_rows,
    )

    other_layers = lax.ppermute(layer_blocks, "dev", pairs(count, across))
    both_layers = jnp.where(
        student_side,
        jnp.stack([other_layers, layer_blocks]),
        jnp.stack([layer_blocks, other_layers]),
    )
    gathered = lax.all_gather(both_layers, "dev", axis=0, axis_index_groups=groups)
    head_out = jnp.where(student_side, head_blocks[0], head_blocks[1])
    head_keep = jnp.where(student_side, head_blocks[1], head_blocks[0])
    head_got = lax.ppermute(head_out, "dev", pairs(count, across))
    both_head = jnp.where(
        student_side, jnp.stack([head_got, head_keep]), jnp.stack([head_keep, head_got])
    )

    vectors = lax.ppermute(vector_blocks, "dev", [(count - 1, 0)])
    seed = jnp.concatenate([embed_blocks.reshape(2 * embed_rows, D), vectors.reshape(8 * 2 * LAYERS, D)])
    third = -(-seed.shape[0] // 48) * 16
    spread_parts = []
    for number, order in enumerate(("xyba", "baxy", "ybax")):
        spread = seed[number * third : (number + 1) * third]
        reached = [0, 1]
        for name in order:
            moves = [(i, i ^ MASKS[name]) for i in reached]
            got = lax.ppermute(spread, "dev", moves)
            targets = [t for s, t in moves]
            is_target = jnp.array([i in targets for i in range(count)])[me]
            spread = jnp.where(is_target, got, spread)
            reached = reached + targets
        spread_parts.append(spread)
    spread = jnp.concatenate(spread_parts)
    other = lax.ppermute(spread, "dev", pairs(count, 1))
    is_even = me % 2 == 0
    even = jnp.where(is_even, spread, other)
    odd = jnp.where(is_even, other, spread)
    embed_all = [
        jnp.concatenate(
            [
                even[m * embed_rows : m * embed_rows + early_rows],
                odd[m * embed_rows : m * embed_rows + EMBED_ROWS - early_rows],
            ]
        )
        for m in range(2)
    ]
    gathered_head = lax.all_gather(after(both_head, gathered, even, odd), "dev", axis=0, axis_index_groups=groups)
    vectors_all = even[2 * embed_rows :].reshape(2, LAYERS, 8, D)

    def head_slots(first, last):
        pieces = []
        i = first
        while i < last:
            stop = min(last, (i // quarter + 1) * quarter)
            owner = 1 if i >= half else 0
            at = (i ^ across if owner else i) ^ swap
            pieces.append(
                lax.dynamic_slice(
                    gathered_head, (at, owner, 0, 0), (stop - i, 1, slot, ROW)
                ).reshape(stop - i, slot, ROW)
            )
            i = stop
        return pieces

    def pad_columns(values, first, last, origin):
        pieces = []
        for i in range(first, last):
            low, high = bounds[i] - origin, bounds[i + 1] - origin
            if low < 0:
                pieces.append(jnp.zeros(values.shape[:-1] + (-low,), values.dtype))
            pieces.append(values[..., max(low, 0) : high])
            pieces.append(jnp.zeros(values.shape[:-1] + (slot - sizes[i],), values.dtype))
        return jnp.concatenate([p for p in pieces if p.shape[-1]], axis=-1)

    def cut_columns(values, first, last, origin):
        pieces = []
        for i in range(first, last):
            low = bounds[i] - origin
            at = (i - first) * slot
            pieces.append(values[..., at + max(-low, 0) : at + sizes[i]])
        return jnp.concatenate(pieces, axis=-1)

    def embed_parts(model):
        rows = embed_all[model]
        return (rows[:PIX], rows[PIX : PIX + SEQ], rows[PIX + SEQ :], None, None, None)

    def head_rows(stream, extras):
        chosen = jnp.take_along_axis(stream, row_index[:, :, None], axis=1).reshape(rows_here, D)
        normed = layer_norm(chosen, extras[2].astype(single), extras[3].astype(single)).astype(narrow)
        return chosen, normed

    def start_rows(parts, student):
        stream = embed(parts, patches, masked_here, student)
        return jnp.pad(stream, ((0, 0), (0, PAD_SEQ - SEQ), (0, 0))).reshape(images_here * PAD_SEQ, D)

    student_parts = embed_parts(1)
    stream = start_rows(student_parts, True)
    saved_layers = []
    for layer_index in range(LAYERS):
        before_layer = stream
        stream, *saved = layer_forward(
            side, stream, vectors_all[1, layer_index], gathered, LAYERS + layer_index, True
        )
        saved_layers.append((before_layer, *saved))
    teacher_parts = embed_parts(0)
    teacher_stream = start_rows(teacher_parts, False)
    for layer_index in range(LAYERS):
        teacher_stream = layer_forward(
            side, teacher_stream, vectors_all[0, layer_index], gathered, layer_index, False
        )[0]
    stream = stream.reshape(images_here, PAD_SEQ, D)
    teacher_stream = teacher_stream.reshape(images_here, PAD_SEQ, D)
    chosen, student_normed = head_rows(stream, student_parts[2])
    teacher_normed = head_rows(teacher_stream, teacher_parts[2])[1]

    normed_got = lax.ppermute(
        jnp.where(student_side, teacher_normed, student_normed), "dev", pairs(count, across)
    )
    normed = jnp.where(
        student_side,
        jnp.concatenate([normed_got, student_normed]),
        jnp.concatenate([teacher_normed, normed_got]),
    )
    normed = jnp.pad(normed, ((0, more_rows), (0, 0)))
    w_one = jnp.concatenate(head_slots(1, first_w2)).reshape(-1, ROW)
    w_two = jnp.concatenate(head_slots(first_w2, first_w3)).reshape(-1, ROW)
    w_three = jnp.concatenate(
        [head_slots(i, i + 1)[0][0, : sizes[i]] for i in range(first_w3, count)]
    ).reshape(HID, BOT)
    pre_one = contract("rd,dh->rh", pad_columns(normed, 1, first_w2, 0), w_one)
    hidden_one = jax.nn.gelu(pre_one).astype(narrow)
    pre_two = contract("rh,hk->rk", pad_columns(hidden_one, first_w2, first_w3, D), w_two)
    hidden_two = jax.nn.gelu(pre_two).astype(narrow)
    bottleneck = contract("rh,hb->rb", hidden_two, w_three)
    unit_z = unit_rows(bottleneck).astype(narrow)
    third_end = (bounds[-2] - D - HID + slot) * (ROW // BOT)
    more_inputs = ((0, 0), (0, max(third_end - HID, 0)))
    inputs_all = lax.all_gather(
        jnp.pad(jnp.concatenate([normed, hidden_one, hidden_two], axis=1), more_inputs),
        "dev",
        axis=0,
        axis_index_groups=groups,
    ).reshape(half * pair_rows, -1)

    all_rows = half * pair_rows
    kept_row = jnp.broadcast_to(kept[:, None], (images_here, 17)).reshape(1, rows_here)
    kept_pair = cube_gather(kept_row, "b").reshape(1, 2 * rows_here)
    kept_pair = jnp.pad(kept_pair, ((0, 0), (0, more_rows)))
    all_kept = cube_gather(kept_pair, "xygc").reshape(all_rows)
    z_pair = cube_gather(unit_z, "b")
    teacher_z_all = cube_gather(z_pair[0], "xygc").reshape(all_rows, BOT)
    student_z_all = cube_gather(z_pair[1], "gxyc").reshape((2,) * 4 + (pair_rows, BOT))
    student_z_all = jnp.transpose(student_z_all, (0, 3, 1, 2, 4, 5)).reshape(all_rows, BOT)
    protos_here = protos.shape[0]
    own_centre = lax.dynamic_slice(centre, (me * protos_here,), (protos_here,))
    centre_column = own_centre.reshape(protos_here, 1)
    spot_in_pair = jnp.arange(all_rows) % pair_rows
    is_class = (spot_in_pair % 17) == 0
    class_kept = jnp.where(is_class, all_kept, 0.0)
    row_weight = jnp.where(is_class, all_kept, all_kept * (1.0 / 16.0))
    count_total = jnp.sum(class_kept)

    def lines(*values):
        return jnp.pad(jnp.stack(values), ((0, 8 - len(values)), (0, 0)))

    mixed_rows, sums, centre_sum = logits_pass(
        teacher_z_all, student_z_all, proto_teacher, protos, centre_column, lines(class_kept)
    )
    mixed_own = cube_scatter(mixed_rows.reshape((2,) * 4 + (pair_rows, 2 * BOT)), "cgyx", "cgyx")
    mixed_own = mixed_own + lax.ppermute(
        mixed_own.astype(narrow), "dev", [(i, i ^ across) for i in range(half)]
    ).astype(single)
    sums = cube_sum(sums[:3])
    cross = jnp.log(sums[1]) - sums[2] / (sums[0] * tau_student)
    loss_total = jnp.sum(row_weight * cross)
    scale = row_weight / tau_student
    student_scale, teacher_scale = scale / sums[1], scale / sums[0]
    flags = bit_flags(me)
    pair_at = flags["c"] * 8 + flags["g"] * 4 + flags["y"] * 2 + flags["x"]
    own_scales = lax.dynamic_slice(
        jnp.stack([student_scale, teacher_scale]), (0, pair_at * pair_rows), (2, pair_rows)
    )
    grad_unit_z = (
        mixed_own[:, :BOT] * own_scales[0][:, None] - mixed_own[:, BOT:] * own_scales[1][:, None]
    )
    own_new_centre = (
        centre_keep * own_centre + (1.0 - centre_keep) * centre_sum.reshape(protos_here) / count_total
    )
    new_centre = cube_gather(own_new_centre.reshape(1, protos_here), "cxyab").reshape(-1)

    grad_bottle = jax.vjp(unit_rows, bottleneck)[1](grad_unit_z)[0].astype(narrow)
    grad_pre_two = gelu_back(pre_two, contract("rb,hb->rh", grad_bottle, w_three)).astype(narrow)
    grad_hidden = cut_columns(contract("rk,hk->rh", grad_pre_two, w_two), first_w2, first_w3, D)
    grad_pre_one = gelu_back(pre_one, grad_hidden).astype(narrow)
    grad_normed = cut_columns(contract("rh,dh->rd", grad_pre_one, w_one), 1, first_w2, 0)
    grads_all = lax.all_gather(
        jnp.concatenate([grad_pre_one, grad_pre_two, grad_bottle], axis=1),
        "dev",
        axis=0,
        axis_index_groups=groups,
    ).reshape(half * pair_rows, 2 * HID + BOT)
    normed_back = lax.ppermute(
        grad_normed[:rows_here], "dev", [(i, i ^ across) for i in range(half, count)]
    )
    own_grad_normed = jnp.where(student_side, grad_normed[rows_here : 2 * rows_here], normed_back)
    extras = student_parts[2].astype(single)
    grad_chosen, grad_gain, grad_bias = jax.vjp(layer_norm, chosen, extras[2], extras[3])[1](
        own_grad_normed
    )
    image_index = jnp.arange(images_here, dtype=jnp.int32)[:, None]
    grad_stream = (
        jnp.zeros(stream.shape, single)
        .at[image_index, row_index]
        .add(grad_chosen.reshape(images_here, 17, D))
    )

    grad_stream = grad_stream.reshape(images_here * PAD_SEQ, D)
    middle_row = block_rows // 2
    small_rows = -(-(EMBED_ROWS + 6 * LAYERS) // (16 * count)) * 16
    vector_grads = [None] * LAYERS

    def halves(array):
        middle = array.shape[-2] // 2
        return [array[..., :middle, :], array[..., middle:, :]]

    def cuts(parts, names, order):
        return [cut(part, name, axis, 1) for part, name, axis in zip(parts, names, order)]

    def moves(pieces, order):
        return [move(sent, kept, axis) for (sent, kept, left), axis in zip(pieces, order)]

    def blocks_of(weight_grad, rows):
        return split_bits(weight_grad.reshape(D // 128, count, rows, 128), 1)

    rounds = (("c",), ("x", "y"), ("y", "x"), ("b", "b"), ("a", "a"))

    def advance(state):
        pieces, stage = state
        parts = moves(pieces, rounds[stage])
        names = [left for sent, kept, left in pieces]
        if stage == 0:
            parts, names = halves(parts[0]), names * 2
        return cuts(parts, names, rounds[stage + 1]), stage + 1

    def finish(state):
        while state[1] < len(rounds) - 1:
            state = advance(state)
        return moves(state[0], rounds[-1])

    def sends(states):
        return tuple(sent for pieces, stage in states for sent, kept, left in pieces)

    started = []
    waits = ()
    for layer_index in reversed(range(LAYERS)):
        saved, vectors = saved_layers[layer_index], vectors_all[1, layer_index]
        part = LAYERS + layer_index
        started = [advance(state) for state in started]
        grad_stream, weight_grad, late_vectors = mlp_back(
            side, grad_stream, saved, vectors, gathered, part, waits + sends(started)
        )
        started = [advance(state) for state in started]
        grad_stream, weight_grad, early_vectors = attention_back(
            side, grad_stream, saved, vectors, gathered, part, weight_grad, sends(started)
        )
        vector_grads[layer_index] = (late_vectors + early_vectors)[:6]
        first = (cuts([blocks_of(weight_grad, block_rows)], ["bayxc"], rounds[0]), 0)
        if layer_index == LAYERS - 1:
            proto_grad, proto_square = proto_grad_pass(
                teacher_z_all,
                student_z_all,
                proto_teacher,
                protos,
                centre_column,
                lines(student_scale, teacher_scale),
                sends([first]),
            )
            waits = (proto_square,)
        if layer_index > 0:
            started.append(first)
    started = [advance(state) for state in started]
    small = embed_back(
        grad_stream,
        patches.reshape(images_here * PATCHES, PIX),
        jnp.where(masked_here, 0.0, 1.0).reshape(images_here * PATCHES, 1),
        jnp.stack([grad_gain, grad_bias]),
        jnp.concatenate(vector_grads),
        small_rows * count,
        sends([first] + started),
    )
    small_first = cuts([blocks_of(small, small_rows)], ["bayxc"], rounds[0])
    joined = [
        jnp.concatenate(pair, axis=-2)
        for pair in zip(halves(moves(first[0], "c")[0]), halves(moves(small_first, "c")[0]))
    ]
    last = (cuts(joined, ["bayx"] * 2, rounds[1]), 1)
    later_blocks = [jnp.concatenate(finish(state), axis=1) for state in started]

    def table(values):
        return jnp.array(values, jnp.int32)

    columns = [max(bound, 0) // 128 * 128 for bound in bounds[:-1]]
    offsets = [bound - column for bound, column in zip(bounds, columns)]
    offsets[0] = 0
    valid = [0] + sizes[1:]
    thirds = [D + HID + max(bound - D - HID, 0) * (ROW // BOT) for bound in bounds[:-1]]
    partner = me ^ across
    is_third = (me >= first_w3).astype(jnp.int32)
    place = jnp.stack(
        [
            jnp.where(is_third == 1, 0, table(columns)[me]),
            jnp.where(is_third == 1, 0, table(offsets)[me]),
            table(valid)[me],
            jnp.int32(HID),
            table(columns)[partner],
            table(offsets)[partner],
            table(valid)[partner],
            jnp.where(partner < first_w2, 0, HID),
            is_third,
            table(thirds)[me],
        ]
    ).astype(jnp.int32)
    own_block_grad, partner_block_grad = head_grads(
        place, inputs_all, grads_all, slot, -min(bounds[1], 0), sends([last])
    )
    block_got = lax.ppermute(partner_block_grad, "dev", [(i, i ^ across) for i in range(half, count)])
    head_block_grad = jnp.where(student_side, own_block_grad, block_got.astype(single))
    pieces, stage = advance(last)
    parts = finish(([(after(sent, own_block_grad), stay, left) for sent, stay, left in pieces], stage))
    middle_row = block_rows // 2
    small_block = jnp.concatenate([part[:, middle_row:] for part in parts], axis=1)
    layer_block = jnp.stack(
        [jnp.concatenate([part[:, :middle_row] for part in parts], axis=1)] + later_blocks[::-1]
    )

    square_local = (
        jnp.sum(head_block_grad * head_block_grad)
        + jnp.sum(layer_block * layer_block)
        + jnp.sum(small_block * small_block)
        + proto_square[0, 0]
    )
    high = square_local.astype(narrow)
    middle = (square_local - high.astype(single)).astype(narrow)
    low = (square_local - high.astype(single) - middle.astype(single)).astype(narrow)
    tile = jnp.pad(jnp.stack([high, middle, low]).reshape(3, 1, 1), ((0, 0), (0, 15), (0, 127)))
    shared = cube_gather(jnp.concatenate([small_block.astype(narrow), tile], axis=1), "xyabc")
    shared = jnp.moveaxis(shared.reshape((2,) + (half,) + shared.shape[1:]), 0, 1)
    shared = shared.reshape((count,) + shared.shape[2:]).astype(single)
    square_total = jnp.sum(shared[:, :, small_rows, 0])
    small_all = jnp.transpose(shared[:, :, :small_rows], (0, 2, 1, 3)).reshape(small_rows * count, D)
    embed_grad = small_all[:EMBED_ROWS].reshape(-1)
    vector_grad = small_all[EMBED_ROWS : EMBED_ROWS + 6 * LAYERS].reshape(LAYERS, 6, D)

    behind = lax.ppermute(layer_block[:, :, :6], "dev", step_pairs(count, -1))
    vector_columns = jnp.swapaxes(vector_grad.reshape(LAYERS, 6, D // 128, 128), 1, 2)
    behind = jnp.where(me == count - 1, vector_columns, behind)
    last_rows = lax.dynamic_slice(
        head_block_grad, (jnp.array(sizes, jnp.int32)[me] - GROUP, 0), (GROUP, ROW)
    )
    previous = lax.ppermute(last_rows, "dev", step_pairs(count, 1))
    stem_at = head_span - start_here
    layer_at = drift * me
    place = jnp.stack([stem_at // 128, stem_at % 128, layer_at // 128, layer_at % 128]).astype(jnp.int32)
    stem_lines, layer_lines = own_shards(
        place, head_block_grad, previous, layer_block, behind, lane_rows(stem_piece), lane_rows(layer_piece)
    )
    layer_grad = layer_lines.reshape(LAYERS, -1)[:, :layer_piece]
    stem_grad = stem_lines.reshape(-1)[:stem_piece]
    rest = EMBED_FLAT - stem_piece
    second_part = jnp.concatenate([embed_grad[stem_piece:], stem_grad[rest:]])
    stem_grad = jnp.where(
        me == 0, embed_grad[:stem_piece], jnp.where(me == 1, second_part, stem_grad)
    )

    grad_norm = jnp.sqrt(square_total) / count_total
    factor = jnp.minimum(1.0, clip_limit / (grad_norm + 1e-06)) / count_total
    stem_set = adam_update(stem, stem_moment, stem_second, stem_grad * factor, stem_teacher)
    layer_set = adam_update(layers, layer_moment, layer_second, layer_grad * factor, layer_teacher)
    proto_set = proto_update(factor, protos, proto_moment, proto_second, proto_teacher, proto_grad)
    return (loss_total, count_total, grad_norm, new_centre) + stem_set + layer_set + tuple(proto_set)


def solution(mesh):
    count = mesh.shape["dev"]
    stem_length = -(-(EMBED_FLAT + HEAD_ROWS * ROW) // count) * count
    close = fits(count, stem_length // count, (MATRIX_ROWS + 6) * D // count)
    placed = (
        P("dev", None, None),
        P("dev", None),
        P("dev"),
        P("dev"),
        P("dev"),
        P("dev"),
        P("dev"),
        P(None, "dev"),
        P(None, "dev"),
        P(None, "dev"),
        P(None, "dev"),
        P("dev", None),
        P("dev", None),
        P("dev", None),
        P("dev", None),
        P(),
    )
    return jax.shard_map(
        close_local if close else spread_local,
        mesh=mesh,
        in_specs=placed,
        out_specs=(
            P(),
            P(),
            P(),
            P(),
            P("dev"),
            P("dev"),
            P("dev"),
            P("dev"),
            P("dev"),
            P(None, "dev"),
            P(None, "dev"),
            P(None, "dev"),
            P(None, "dev"),
            P(None, "dev"),
            P("dev", None),
            P("dev", None),
            P("dev", None),
            P("dev", None),
            P("dev", None),
        ),
        check_vma=False,
    )
```

```python
import jax
import jax.numpy as jnp
from jax import lax
from jax.experimental import pallas as pl
from jax.experimental.pallas import tpu as pltpu
from jax.sharding import PartitionSpec as P

D = 384
HEADS = 6
HEAD_DIM = 64
FF = 1536
HID = 2048
BOT = 256
PIX = 588
PATCHES = 256
LAYERS = 2
STEP = 10
SEQ = 257


tau_student = 0.1
tau_teacher = 0.04
clip_limit = 0.003
learn_rate = 0.03
beta_one = 0.9
beta_two = 0.999
adam_eps = 1e-08
decay_rate = 0.04
teacher_keep = 0.8
centre_keep = 0.9
narrow = jnp.bfloat16
single = jnp.float32


def layer_shapes():
    return ((D, 3 * D), (D, D), (D, FF), (FF, D), (6, D))


def stem_shapes():
    return ((PIX, D), (SEQ, D), (4, D), (D, HID), (HID, HID), (HID, BOT))


def cut_flat(flat_row, shape_list):
    pieces = []
    offset = 0
    for shape_pair in shape_list:
        length = shape_pair[0] * shape_pair[1]
        pieces.append(flat_row[offset : offset + length].reshape(shape_pair))
        offset = offset + length
    return pieces


def pack_flat(grad_list, total_length):
    joined = jnp.concatenate([grad_item.reshape(-1) for grad_item in grad_list])
    return jnp.concatenate([joined, jnp.zeros((total_length - joined.shape[0],), single)])


def contract(form, left_arg, right_arg):
    return jnp.einsum(form, left_arg, right_arg, preferred_element_type=single)


def layer_norm(values, gain_row, bias_row):
    centred = values - jnp.mean(values, axis=-1, keepdims=True)
    spread = jnp.mean(centred * centred, axis=-1, keepdims=True)
    return centred * lax.rsqrt(spread + 1e-06) * gain_row + bias_row


def unit_rows(values):
    return values * lax.rsqrt(jnp.sum(values * values, axis=-1, keepdims=True) + 1e-06)


def gelu_back(pre_act, grad_act):
    return jax.vjp(jax.nn.gelu, pre_act)[1](grad_act)[0]


def block_forward(stream, weights):
    w_qkv, w_proj, w_up, w_down, vectors = weights
    vectors = vectors.astype(single)
    batch_size = stream.shape[0]
    normed = layer_norm(stream, vectors[0], vectors[1]).astype(narrow)
    packed = (
        contract("bsd,de->bse", normed, w_qkv)
        .astype(narrow)
        .reshape(batch_size, SEQ, 3, HEADS, HEAD_DIM)
    )
    scores = contract("bqhe,bkhe->bhqk", packed[:, :, 0], packed[:, :, 1]) * HEAD_DIM ** (-0.5)
    top_score = jnp.max(scores, axis=-1, keepdims=True)
    exp_terms = jnp.exp(scores - top_score)
    totals = jnp.sum(exp_terms, axis=-1, keepdims=True)
    log_total = top_score + jnp.log(totals)
    mixed = contract("bhqk,bkhe->bqhe", (exp_terms / totals).astype(narrow), packed[:, :, 2])
    mixed = mixed.astype(narrow).reshape(batch_size, SEQ, D)
    attn_out = contract("bsd,de->bse", mixed, w_proj)
    middle = stream + vectors[2] * attn_out
    normed_two = layer_norm(middle, vectors[3], vectors[4]).astype(narrow)
    pre_act = contract("bsd,df->bsf", normed_two, w_up)
    hidden = jax.nn.gelu(pre_act).astype(narrow)
    mlp_out = contract("bsf,fd->bsd", hidden, w_down)
    saved = (
        stream,
        normed,
        packed,
        log_total,
        mixed,
        attn_out,
        middle,
        normed_two,
        pre_act,
        hidden,
        mlp_out,
    )
    return (middle + vectors[5] * mlp_out, saved)


def block_backward(grad_out, weights, saved):
    w_qkv, w_proj, w_up, w_down, vectors = weights
    vectors = vectors.astype(single)
    (
        stream,
        normed,
        packed,
        log_total,
        mixed,
        attn_out,
        middle,
        normed_two,
        pre_act,
        hidden,
        mlp_out,
    ) = saved
    batch_size = stream.shape[0]
    score_scale = HEAD_DIM ** (-0.5)
    grad_ls_two = jnp.sum(grad_out * mlp_out, axis=(0, 1))
    grad_mlp = (grad_out * vectors[5]).astype(narrow)
    grad_down = contract("bsf,bsd->fd", hidden, grad_mlp)
    grad_pre = gelu_back(pre_act, contract("bsd,fd->bsf", grad_mlp, w_down)).astype(narrow)
    grad_up = contract("bsd,bsf->df", normed_two, grad_pre)
    grad_normed_two = contract("bsf,df->bsd", grad_pre, w_up)
    grad_mid, grad_gain_two, grad_bias_two = jax.vjp(layer_norm, middle, vectors[3], vectors[4])[1](
        grad_normed_two
    )
    grad_mid = grad_mid + grad_out
    grad_ls_one = jnp.sum(grad_mid * attn_out, axis=(0, 1))
    grad_attn = (grad_mid * vectors[2]).astype(narrow)
    grad_proj = contract("bsd,bse->de", mixed, grad_attn)
    grad_mixed = (
        contract("bse,de->bsd", grad_attn, w_proj)
        .astype(narrow)
        .reshape(batch_size, SEQ, HEADS, HEAD_DIM)
    )
    query_rows = packed[:, :, 0]
    key_rows = packed[:, :, 1]
    value_rows = packed[:, :, 2]
    probs = jnp.exp(contract("bqhe,bkhe->bhqk", query_rows, key_rows) * score_scale - log_total)
    grad_probs = contract("bqhe,bkhe->bhqk", grad_mixed, value_rows)
    grad_values = contract("bhqk,bqhe->bkhe", probs.astype(narrow), grad_mixed)
    grad_scores = probs * (grad_probs - jnp.sum(probs * grad_probs, axis=-1, keepdims=True))
    grad_raw = (grad_scores * score_scale).astype(narrow)
    grad_queries = contract("bhqk,bkhe->bqhe", grad_raw, key_rows)
    grad_keys = contract("bhqk,bqhe->bkhe", grad_raw, query_rows)
    grad_packed = (
        jnp.stack([grad_queries, grad_keys, grad_values], axis=2)
        .astype(narrow)
        .reshape(batch_size, SEQ, 3 * D)
    )
    grad_qkv = contract("bsd,bse->de", normed, grad_packed)
    grad_normed = contract("bse,de->bsd", grad_packed, w_qkv)
    grad_in, grad_gain_one, grad_bias_one = jax.vjp(layer_norm, stream, vectors[0], vectors[1])[1](
        grad_normed
    )
    grad_vectors = jnp.stack(
        [grad_gain_one, grad_bias_one, grad_ls_one, grad_gain_two, grad_bias_two, grad_ls_two]
    )
    return (grad_in + grad_mid, (grad_qkv, grad_proj, grad_up, grad_down, grad_vectors))


def embed(stem_parts, image_rows, masked_here, student):
    patch_w, position, extras, w_first, w_second, w_third = stem_parts
    extras = extras.astype(single)
    embedded = contract("gpc,cd->gpd", image_rows, patch_w)
    if student:
        embedded = jnp.where(masked_here[:, :, None], extras[1], embedded)
    cls_rows = jnp.broadcast_to(extras[0], (image_rows.shape[0], 1, D))
    return jnp.concatenate([cls_rows, embedded], axis=1) + position.astype(single)


def embed_backward(grad_stream, image_rows, masked_here):
    grad_cls = jnp.sum(grad_stream[:, 0], axis=0)
    grad_position = jnp.sum(grad_stream, axis=0)
    grad_patch_rows = grad_stream[:, 1:]
    grad_mask_token = jnp.sum(jnp.where(masked_here[:, :, None], grad_patch_rows, 0.0), axis=(0, 1))
    grad_embedded = jnp.where(masked_here[:, :, None], 0.0, grad_patch_rows).astype(narrow)
    grad_patch_w = contract("gpc,gpd->cd", image_rows, grad_embedded)
    return (grad_patch_w, grad_position, grad_cls, grad_mask_token)


def head_forward(stem_parts, proto_rows, stream, row_index):
    patch_w, position, extras, w_first, w_second, w_third = stem_parts
    extras = extras.astype(single)
    chosen = jnp.take_along_axis(stream, row_index[:, :, None], axis=1)
    normed = layer_norm(chosen, extras[2], extras[3]).astype(narrow)
    pre_one = contract("grd,dh->grh", normed, w_first)
    hidden_one = jax.nn.gelu(pre_one).astype(narrow)
    pre_two = contract("grh,hk->grk", hidden_one, w_second)
    hidden_two = jax.nn.gelu(pre_two).astype(narrow)
    bottleneck = contract("grh,hb->grb", hidden_two, w_third)
    unit_z = unit_rows(bottleneck).astype(narrow)
    unit_protos = unit_rows(proto_rows.astype(single)).astype(narrow)
    logits = contract("grb,kb->grk", unit_z, unit_protos)
    return (
        logits,
        (chosen, normed, pre_one, hidden_one, pre_two, hidden_two, bottleneck, unit_z, unit_protos),
    )


def head_backward(grad_logits, stem_parts, saved, row_index, stream_shape):
    patch_w, position, extras, w_first, w_second, w_third = stem_parts
    extras = extras.astype(single)
    chosen, normed, pre_one, hidden_one, pre_two, hidden_two, bottleneck, unit_z, unit_protos = (
        saved
    )
    grad_rounded = grad_logits.astype(narrow)
    grad_unit_z = contract("grk,kb->grb", grad_rounded, unit_protos)
    grad_unit_protos = contract("grk,grb->kb", grad_rounded, unit_z)
    grad_bottle = jax.vjp(unit_rows, bottleneck)[1](grad_unit_z)[0].astype(narrow)
    grad_third = contract("grh,grb->hb", hidden_two, grad_bottle)
    grad_pre_two = gelu_back(pre_two, contract("grb,hb->grh", grad_bottle, w_third)).astype(narrow)
    grad_second = contract("grh,grk->hk", hidden_one, grad_pre_two)
    grad_pre_one = gelu_back(pre_one, contract("grk,hk->grh", grad_pre_two, w_second)).astype(
        narrow
    )
    grad_first = contract("grd,grh->dh", normed, grad_pre_one)
    grad_normed = contract("grh,dh->grd", grad_pre_one, w_first)
    grad_chosen, grad_gain, grad_bias = jax.vjp(layer_norm, chosen, extras[2], extras[3])[1](
        grad_normed
    )
    image_index = jnp.arange(row_index.shape[0], dtype=jnp.int32)[:, None]
    grad_stream = jnp.zeros(stream_shape, single).at[image_index, row_index].add(grad_chosen)
    return (
        grad_stream,
        (grad_first, grad_second, grad_third),
        grad_gain,
        grad_bias,
        grad_unit_protos,
    )


def adam_update(weight, moment, second, grad, teacher):
    new_moment = beta_one * moment + (1.0 - beta_one) * grad
    new_second = beta_two * second + (1.0 - beta_two) * grad * grad
    direction = (
        new_moment
        / (1.0 - beta_one**STEP)
        / (jnp.sqrt(new_second / (1.0 - beta_two**STEP)) + adam_eps)
    )
    new_weight = weight - learn_rate * (direction + decay_rate * weight)
    return (
        new_moment,
        new_second,
        new_weight,
        new_weight.astype(narrow),
        teacher_keep * teacher + (1.0 - teacher_keep) * new_weight,
    )


def spread_local(
    patches,
    masked,
    slot_used,
    stem,
    stem_moment,
    stem_second,
    stem_teacher,
    layers,
    layer_moment,
    layer_second,
    layer_teacher,
    protos,
    proto_moment,
    proto_second,
    proto_teacher,
    centre,
):
    images_here = patches.shape[0]
    row_index = jnp.concatenate([jnp.zeros((images_here, 1), jnp.int32), masked + 1], axis=1)
    masked_here = jnp.any(
        masked[:, :, None] == jnp.arange(PATCHES, dtype=jnp.int32)[None, None, :], axis=1
    )
    kept = slot_used.astype(single)
    teacher_flat, teacher_protos = (
        lax.all_gather(stem_teacher.astype(narrow), "dev", axis=0, tiled=True),
        lax.all_gather(proto_teacher.astype(narrow), "dev", axis=0, tiled=True),
    )
    teacher_parts = cut_flat(teacher_flat, stem_shapes())
    stream = embed(teacher_parts, patches, masked_here, False)
    for layer_index in range(LAYERS):
        teacher_layer = lax.all_gather(
            layer_teacher[layer_index].astype(narrow), "dev", axis=0, tiled=True
        )
        stream = block_forward(stream, cut_flat(teacher_layer, layer_shapes()))[0]
    teacher_logits = head_forward(teacher_parts, teacher_protos, stream, row_index)[0]
    teacher_probs = jax.nn.softmax((teacher_logits - centre) / tau_teacher, axis=-1)
    centre_terms = jnp.sum(kept[:, None] * teacher_logits[:, 0], axis=0)
    student_flat, student_protos = (
        lax.all_gather(stem.astype(narrow), "dev", axis=0, tiled=True),
        lax.all_gather(protos.astype(narrow), "dev", axis=0, tiled=True),
    )
    student_parts = cut_flat(student_flat, stem_shapes())
    stream = embed(student_parts, patches, masked_here, True)
    saved_layers = []
    gathered_layers = []
    for layer_index in range(LAYERS):
        layer_flat = lax.all_gather(layers[layer_index].astype(narrow), "dev", axis=0, tiled=True)
        gathered_layers.append(layer_flat)
        stream, saved = block_forward(stream, cut_flat(layer_flat, layer_shapes()))
        saved_layers.append(saved)
    logits, head_saved = head_forward(student_parts, student_protos, stream, row_index)

    def loss_piece(logit_rows):
        log_probs = jax.nn.log_softmax(logit_rows / tau_student, axis=-1)
        cross = -jnp.sum(teacher_probs * log_probs, axis=-1)
        return jnp.sum(kept * (cross[:, 0] + jnp.mean(cross[:, 1:], axis=1)))

    loss_local, loss_puller = jax.vjp(loss_piece, logits)
    grad_logits = loss_puller(jnp.float32(1.0))[0]
    count_local = jnp.sum(kept)
    loss_total, count_total, centre_total = lax.psum((loss_local, count_local, centre_terms), "dev")
    back_flat, back_protos = (
        lax.all_gather(stem.astype(narrow), "dev", axis=0, tiled=True),
        lax.all_gather(protos.astype(narrow), "dev", axis=0, tiled=True),
    )
    back_parts = cut_flat(back_flat, stem_shapes())
    grad_stream, head_grads, grad_gain, grad_bias, grad_unit_protos = head_backward(
        grad_logits, back_parts, head_saved, row_index, stream.shape
    )
    layer_grads = []
    for layer_index in reversed(range(LAYERS)):
        weight_flat = lax.all_gather(layers[layer_index].astype(narrow), "dev", axis=0, tiled=True)
        grad_stream, block_grads = block_backward(
            grad_stream, cut_flat(weight_flat, layer_shapes()), saved_layers[layer_index]
        )
        layer_grads.insert(
            0,
            lax.psum_scatter(
                pack_flat(block_grads, weight_flat.shape[0]), "dev", scatter_dimension=0, tiled=True
            ),
        )
    grad_patch_w, grad_position, grad_cls, grad_mask_token = embed_backward(
        grad_stream, patches, masked_here
    )
    grad_extras = jnp.stack([grad_cls, grad_mask_token, grad_gain, grad_bias])
    stem_flat_grad = pack_flat(
        (grad_patch_w, grad_position, grad_extras) + head_grads, back_flat.shape[0]
    )
    stem_grad, proto_row_grad = (
        lax.psum_scatter(stem_flat_grad, "dev", scatter_dimension=0, tiled=True),
        lax.psum_scatter(grad_unit_protos, "dev", scatter_dimension=0, tiled=True),
    )
    own_protos = lax.optimization_barrier(protos.astype(narrow)).astype(single)
    proto_grad = jax.vjp(unit_rows, own_protos)[1](proto_row_grad)[0]
    layer_grad = jnp.stack(layer_grads)
    square_local = (
        jnp.sum(stem_grad * stem_grad)
        + jnp.sum(layer_grad * layer_grad)
        + jnp.sum(proto_grad * proto_grad)
    )
    square_total = lax.psum(square_local, "dev")
    grad_norm = jnp.sqrt(square_total) / count_total
    factor = jnp.minimum(1.0, clip_limit / (grad_norm + 1e-06)) / count_total
    new_centre = centre_keep * centre + (1.0 - centre_keep) * centre_total / count_total
    stem_set = adam_update(stem, stem_moment, stem_second, stem_grad * factor, stem_teacher)
    layer_set = adam_update(layers, layer_moment, layer_second, layer_grad * factor, layer_teacher)
    proto_set = adam_update(protos, proto_moment, proto_second, proto_grad * factor, proto_teacher)
    return (
        loss_total,
        count_total,
        grad_norm,
        new_centre,
        stem_set[0],
        stem_set[1],
        stem_set[2],
        stem_set[3],
        stem_set[4],
        layer_set[0],
        layer_set[1],
        layer_set[2],
        layer_set[3],
        layer_set[4],
        proto_set[0],
        proto_set[1],
        proto_set[2],
        proto_set[3],
        proto_set[4],
    )


GROUP = 16
ROW = HID
MATRIX_ROWS = D * 3 + D + FF + FF
EMBED_ROWS = PIX + SEQ + 4
EMBED_FLAT = EMBED_ROWS * D
HEAD_ROWS = D + HID + BOT
BITS = ("b", "a", "y", "x", "c")
MASKS = {"c": 1, "x": 2, "y": 4, "a": 8, "b": 24, "g": 8}


def head_bounds(count, stem_piece):
    bounds = [-(-(stem_piece * device - EMBED_FLAT) // (ROW * GROUP)) * GROUP for device in range(count + 1)]
    bounds[0] = -(-EMBED_FLAT // (ROW * GROUP)) * -GROUP
    bounds[-1] = HEAD_ROWS
    return bounds


def fits(count, stem_piece, layer_piece):
    if count != 1 << len(BITS) or MATRIX_ROWS % (3 * count):
        return False
    bounds = head_bounds(count, stem_piece)
    sizes = [bounds[i + 1] - bounds[i] for i in range(count)]
    return (
        min(sizes) > GROUP
        and bounds[1] <= 0
        and stem_piece < EMBED_FLAT <= 2 * stem_piece
        and D in bounds
        and D + HID in bounds
        and stem_piece * count == EMBED_FLAT + HEAD_ROWS * ROW
    )


def pairs(count, mask):
    return [(i, i ^ mask) for i in range(count)]


def bit_flags(me):
    flags = {name: (me >> (len(BITS) - 1 - place)) & 1 for place, name in enumerate(BITS)}
    flags["g"] = flags["a"] ^ flags["b"]
    return flags


def cube_gather(part, order):
    count = 1 << len(BITS)
    flags = bit_flags(lax.axis_index("dev"))
    held = part[None]
    for name in order:
        got = lax.ppermute(held, "dev", pairs(count, MASKS[name]))
        held = jnp.where(
            flags[name] == 1,
            jnp.concatenate([got, held], axis=0),
            jnp.concatenate([held, got], axis=0),
        )
    return held


def cut(array, names, name, lead):
    flag = bit_flags(lax.axis_index("dev"))[name] == 1
    place = names.index(name) + lead
    low = lax.index_in_dim(array, 0, place, keepdims=False)
    high = lax.index_in_dim(array, 1, place, keepdims=False)
    sent = jnp.where(flag, low, high)
    return (sent if name == "c" else sent.astype(narrow)), jnp.where(flag, high, low), names.replace(name, "")


def move(sent, kept, name):
    return kept + lax.ppermute(sent, "dev", pairs(1 << len(BITS), MASKS[name])).astype(single)


def cube_scatter(array, names, order, lead=0):
    for name in order:
        sent, kept, names = cut(array, names, name, lead)
        array = move(sent, kept, name)
    return array


def cube_sum(values):
    for name in "cxyab":
        values = values + lax.ppermute(values, "dev", pairs(1 << len(BITS), MASKS[name]))
    return values


def split_bits(array, lead=0):
    return array.reshape(array.shape[:lead] + (2,) * len(BITS) + array.shape[lead + 1 :])


def step_pairs(count, step):
    return [(i, i + step) for i in range(count) if 0 <= i + step < count]


def lane_rows(length):
    return -(-length // 1024) * 8


def as_lanes(flat):
    rows = lane_rows(flat.shape[-1])
    gap = rows * 128 - flat.shape[-1]
    padded = jnp.pad(flat, [(0, 0)] * (flat.ndim - 1) + [(0, gap)])
    return padded.reshape(flat.shape[:-1] + (rows, 128))


def shifted(line_ref, row, lane, first, rows, stride):
    spots = lax.broadcasted_iota(jnp.int32, (rows, 128), 1)
    turn = lax.rem(128 - lane, 128)
    here = pltpu.roll(line_ref[pl.ds(row + first, rows, stride=stride), :], turn, 1)
    there = pltpu.roll(line_ref[pl.ds(row + first + 1, rows, stride=stride), :], turn, 1)
    return jnp.where(spots < 128 - lane, here, there)


def blocks_kernel(
    shape,
    place_ref,
    stem_ref,
    after_ref,
    layer_ref,
    before_ref,
    head_ref,
    block_ref,
    embed_ref,
    vector_ref,
    line_ref,
    flat_ref,
):
    front, stem_piece, layer_piece, tail = shape
    stem_lines = stem_ref.shape[1]
    end_row, end_lane = stem_piece // 128, stem_piece % 128
    after_lines = after_ref.shape[1]
    slot = head_ref.shape[1]
    for model in range(2):
        line_ref[pl.ds(0, front), :] = jnp.zeros((front, 128), single)
        line_ref[pl.ds(front, end_row), :] = stem_ref[model, pl.ds(0, end_row), :]
        turned = pltpu.roll(after_ref[model], end_lane, 1)
        spots = lax.broadcasted_iota(jnp.int32, (after_lines, 128), 1)
        line_ref[pl.ds(front + end_row, after_lines), :] = turned
        line_ref[pl.ds(front + end_row + after_lines, 128), :] = jnp.zeros((128, 128), single)
        lower = pltpu.roll(turned, 1, 0)
        first_line = jnp.broadcast_to(stem_ref[model, pl.ds(end_row, 1), :], (after_lines, 128))
        number = lax.broadcasted_iota(jnp.int32, (after_lines, 128), 0)
        lower = jnp.where(number == 0, first_line, lower)
        line_ref[pl.ds(front + end_row, after_lines), :] = jnp.where(spots < end_lane, lower, turned)
        per_row = ROW // 128
        for chunk in range(per_row):
            head_ref[model, :, pl.ds(chunk * 128, 128)] = shifted(
                line_ref, place_ref[0], place_ref[1], chunk, slot, per_row
            ).astype(narrow)
        for chunk in range(D // 128):
            embed_ref[model, :, pl.ds(chunk * 128, 128)] = shifted(
                line_ref, place_ref[2], place_ref[3], chunk, embed_ref.shape[1], D // 128
            ).astype(narrow)
    tail_lines = tail // 128
    layer_lines = layer_ref.shape[1]
    vector_at = tail + layer_piece - tail
    for part in range(layer_ref.shape[0]):
        flat_ref[pl.ds(0, tail_lines), :] = before_ref[part]
        flat_ref[pl.ds(tail_lines, layer_lines), :] = layer_ref[part]
        for chunk in range(D // 128):
            block_ref[part, :, pl.ds(chunk * 128, 128)] = shifted(
                flat_ref, place_ref[4], place_ref[5], chunk, block_ref.shape[1], D // 128
            ).astype(narrow)
            vector_ref[part, :, pl.ds(chunk * 128, 128)] = shifted(
                flat_ref, vector_at // 128, vector_at % 128, chunk, 8, D // 128
            ).astype(narrow)


def own_blocks(place, stems, after, layer_rows, before, shape, slot, block_rows, embed_rows):
    front, stem_piece, layer_piece, tail = shape
    lines = front + stem_piece // 128 + after.shape[1] + slot * ROW // 128
    flats = tail // 128 + layer_rows.shape[1] + 48
    return pl.pallas_call(
        lambda *refs: blocks_kernel(shape, *refs),
        out_shape=[
            jax.ShapeDtypeStruct((2, slot, ROW), narrow),
            jax.ShapeDtypeStruct((2 * LAYERS, block_rows, D), narrow),
            jax.ShapeDtypeStruct((2, embed_rows, D), narrow),
            jax.ShapeDtypeStruct((2 * LAYERS, 8, D), narrow),
        ],
        in_specs=[pl.BlockSpec(memory_space=pltpu.SMEM)] + [pl.BlockSpec(memory_space=pltpu.VMEM)] * 4,
        out_specs=[pl.BlockSpec(memory_space=pltpu.VMEM)] * 4,
        scratch_shapes=[pltpu.VMEM((lines, 128), single), pltpu.VMEM((flats, 128), single)],
        compiler_params=pltpu.CompilerParams(vmem_limit_bytes=40 << 20),
    )(place, stems, after, layer_rows, before)


def shards_kernel(place_ref, head_ref, previous_ref, block_ref, behind_ref, stem_ref, layer_ref, line_ref, flat_ref):
    per_row = ROW // 128
    extra = previous_ref.shape[0]
    slot = head_ref.shape[0]
    for chunk in range(per_row):
        spot = pl.ds(chunk * 128, 128)
        line_ref[pl.ds(chunk, extra, stride=per_row), :] = previous_ref[:, spot]
        line_ref[pl.ds(extra * per_row + chunk, slot, stride=per_row), :] = head_ref[:, spot]
    stem_ref[...] = shifted(line_ref, place_ref[0], place_ref[1], 0, stem_ref.shape[0], 1)
    per_row = D // 128
    rows = block_ref.shape[2]
    for part in range(block_ref.shape[0]):
        for chunk in range(per_row):
            flat_ref[pl.ds(chunk, rows, stride=per_row), :] = block_ref[part, chunk]
            flat_ref[pl.ds(rows * per_row + chunk, 6, stride=per_row), :] = behind_ref[part, chunk]
        layer_ref[part] = shifted(flat_ref, place_ref[2], place_ref[3], 0, layer_ref.shape[1], 1)


def own_shards(place, head_grad, previous, block_grad, behind, stem_lines, layer_lines):
    per_row = ROW // 128
    lines = (head_grad.shape[0] + previous.shape[0]) * per_row + 256
    flats = max(block_grad.shape[2] * 3 + 18, layer_lines + 18) + 16
    return pl.pallas_call(
        shards_kernel,
        out_shape=[
            jax.ShapeDtypeStruct((stem_lines, 128), single),
            jax.ShapeDtypeStruct((block_grad.shape[0], layer_lines, 128), single),
        ],
        in_specs=[pl.BlockSpec(memory_space=pltpu.SMEM)] + [pl.BlockSpec(memory_space=pltpu.VMEM)] * 4,
        out_specs=[pl.BlockSpec(memory_space=pltpu.VMEM)] * 2,
        scratch_shapes=[pltpu.VMEM((lines, 128), single), pltpu.VMEM((flats, 128), single)],
        compiler_params=pltpu.CompilerParams(vmem_limit_bytes=40 << 20),
    )(place, head_grad, previous, block_grad, behind)


PAD_SEQ = 272
GELU_SCALE = 0.7978845608028654
GELU_CUBE = 0.044715


def product_plain(left, right):
    return lax.dot_general(left, right, (((1,), (0,)), ((), ())), preferred_element_type=single)


def product_right(left, right):
    return lax.dot_general(left, right, (((1,), (1,)), ((), ())), preferred_element_type=single)


def product_left(left, right):
    return lax.dot_general(left, right, (((0,), (0,)), ((), ())), preferred_element_type=single)


def norm_parts(values):
    centred = values - jnp.mean(values, axis=-1, keepdims=True)
    spread = lax.rsqrt(jnp.mean(centred * centred, axis=-1, keepdims=True) + 1e-06)
    return centred * spread, spread


def norm_back(grad, unit, spread, gain):
    grad_unit = grad * gain
    mean_one = jnp.mean(grad_unit, axis=-1, keepdims=True)
    mean_two = jnp.mean(grad_unit * unit, axis=-1, keepdims=True)
    return spread * (grad_unit - mean_one - unit * mean_two)


def gelu_tanh(values):
    return jnp.tanh(GELU_SCALE * (values + GELU_CUBE * values * values * values))


def gelu_value(values):
    return 0.5 * values * (1.0 + gelu_tanh(values))


def gelu_slope(values):
    bent = gelu_tanh(values)
    return 0.5 * (1.0 + bent) + 0.5 * values * (1.0 - bent * bent) * GELU_SCALE * (
        1.0 + 3.0 * GELU_CUBE * values * values
    )


def head_copies(plan, side_ref, gathered_ref, one_ref, two_ref, lines_ref, sems):
    quarter = gathered_ref.shape[0] // 2
    shift = side_ref[0] * quarter
    targets = (one_ref, two_ref, lines_ref)
    copies = []
    for number, (at, owner, first, rows, target, row) in enumerate(plan):
        spot = at + shift if at < quarter else at - shift
        copies.append(
            pltpu.make_async_copy(
                gathered_ref.at[spot, owner, pl.ds(first, rows)],
                targets[target].at[pl.ds(row, rows)],
                sems.at[number],
            )
        )
    for copy in copies:
        copy.start()
    return [[copy for copy, item in zip(copies, plan) if item[4] == target] for target in range(3)]


def wait_all(copies):
    for copy in copies:
        copy.wait()


def spread_third(lines_ref, wide_ref, third_ref):
    groups = ROW // BOT
    for lane in range(BOT // 128):
        for group in range(groups):
            at = group * BOT + lane * 128
            wide_ref[lane, pl.ds(group, lines_ref.shape[0], stride=groups), :] = lines_ref[
                :, at : at + 128
            ].astype(single)
        third_ref[:, pl.ds(lane * 128, 128)] = wide_ref[lane].astype(narrow)


def head_up_kernel(
    plan, side_ref, normed_ref, gathered_ref, unit_ref, acts_ref, bottle_ref, pre_one_ref, pre_two_ref,
    one_ref, two_ref, lines_ref, wide_ref, third_ref, sems,
):
    copies = head_copies(plan, side_ref, gathered_ref, one_ref, two_ref, lines_ref, sems)
    acts_ref[...] = jnp.zeros_like(acts_ref)
    normed = normed_ref[...]
    acts_ref[:, pl.ds(0, D)] = normed
    piece = HID // 4
    wait_all(copies[0])
    for number in range(4):
        spot = pl.ds(number * piece, piece)
        pre = product_plain(normed, one_ref[:, spot])
        pre_one_ref[:, spot] = pre
        acts_ref[:, pl.ds(D + number * piece, piece)] = gelu_value(pre).astype(narrow)
    wait_all(copies[2])
    spread_third(lines_ref, wide_ref, third_ref)
    wait_all(copies[1])
    hidden = acts_ref[:, pl.ds(D, HID)]
    for number in range(4):
        spot = pl.ds(number * piece, piece)
        pre = product_plain(hidden, two_ref[:, spot])
        pre_two_ref[:, spot] = pre
        acts_ref[:, pl.ds(D + HID + number * piece, piece)] = gelu_value(pre).astype(narrow)
    bottle = product_plain(acts_ref[:, pl.ds(D + HID, HID)], third_ref[...])
    bottle_ref[...] = bottle
    unit_ref[...] = (
        bottle * lax.rsqrt(jnp.sum(bottle * bottle, axis=-1, keepdims=True) + 1e-06)
    ).astype(narrow)


def head_down_kernel(
    plan, side_ref, grad_ref, bottle_ref, pre_one_ref, pre_two_ref, gathered_ref, grads_ref, normed_grad_ref,
    one_ref, two_ref, lines_ref, wide_ref, third_ref, sems,
):
    copies = head_copies(plan, side_ref, gathered_ref, one_ref, two_ref, lines_ref, sems)
    grad, bottle = grad_ref[...], bottle_ref[...]
    scale = lax.rsqrt(jnp.sum(bottle * bottle, axis=-1, keepdims=True) + 1e-06)
    along = jnp.sum(grad * bottle, axis=-1, keepdims=True)
    grad_bottle = (scale * (grad - bottle * (along * scale * scale))).astype(narrow)
    grads_ref[:, pl.ds(2 * HID, BOT)] = grad_bottle
    wait_all(copies[2])
    spread_third(lines_ref, wide_ref, third_ref)
    piece = HID // 4
    for number in range(4):
        spot = pl.ds(number * piece, piece)
        back = product_right(grad_bottle, third_ref[spot, :])
        grads_ref[:, pl.ds(HID + number * piece, piece)] = (back * gelu_slope(pre_two_ref[:, spot])).astype(narrow)
    wait_all(copies[1])
    grad_two = grads_ref[:, pl.ds(HID, HID)]
    for number in range(4):
        spot = pl.ds(number * piece, piece)
        back = product_right(grad_two, two_ref[spot, :])
        grads_ref[:, spot] = (back * gelu_slope(pre_one_ref[:, spot])).astype(narrow)
    wait_all(copies[0])
    normed_grad_ref[...] = product_right(grads_ref[:, pl.ds(0, HID)], one_ref[...])


def head_pass(kernel, plan, side, inputs, gathered, shapes, waits=()):
    read = len(inputs) + 2
    return pl.pallas_call(
        lambda *refs: kernel(plan, *refs[:read], *refs[read + len(waits) :]),
        out_shape=shapes,
        in_specs=[pl.BlockSpec(memory_space=pltpu.SMEM)]
        + [pl.BlockSpec(memory_space=pltpu.VMEM)] * len(inputs)
        + [pl.BlockSpec(memory_space=pl.ANY)] * (1 + len(waits)),
        out_specs=[pl.BlockSpec(memory_space=pltpu.VMEM)] * len(shapes),
        scratch_shapes=[
            pltpu.VMEM((D, HID), narrow),
            pltpu.VMEM((HID, HID), narrow),
            pltpu.VMEM((BOT, ROW), narrow),
            pltpu.VMEM((BOT // 128, HID, 128), single),
            pltpu.VMEM((HID, BOT), narrow),
            pltpu.SemaphoreType.DMA((len(plan),)),
        ],
        compiler_params=pltpu.CompilerParams(vmem_limit_bytes=56 << 20),
        cost_estimate=pl.CostEstimate(flops=10**9, bytes_accessed=2 * 10**7, transcendentals=10**6),
    )(side, *inputs, gathered, *waits)


def fetch_rows(side_ref, part, gathered_ref, flat_ref, sems):
    quarter = flat_ref.shape[0] // 4
    side = side_ref[0]
    first, second = side * quarter, (1 - side) * quarter
    copies = [
        pltpu.make_async_copy(
            gathered_ref.at[pl.ds(at, quarter), owner, part],
            flat_ref.at[pl.ds(spot * quarter, quarter)],
            sems.at[spot],
        )
        for spot, (at, owner) in enumerate(((first, 0), (second, 0), (second, 1), (first, 1)))
    ]
    for copy in copies:
        copy.start()
    for copy in copies:
        copy.wait()


def matrix_rows(flat_ref, first_row, length):
    rows = flat_ref.shape[1]
    low, high = first_row // rows, -(-(first_row + length) // rows)
    lines = flat_ref[pl.ds(low, high - low)].reshape((high - low) * rows, D)
    at = first_row - low * rows
    return lines[at : at + length]


def spread_columns(flat_ref, first_row, width, wide_ref, out_ref):
    length = width * D
    lines = matrix_rows(flat_ref, first_row, length)
    for column in range(D // 128):
        lane = slice(column * 128, (column + 1) * 128)
        wide_ref[column, pl.ds(0, length), :] = lines[:, lane].astype(single)
    for group in range(width):
        for column in range(D // 128):
            out_ref[group, :, pl.ds(column * 128, 128)] = wide_ref[
                column, pl.ds(group, D, stride=width), :
            ].astype(narrow)


def head_lanes(values, odd):
    lanes = lax.broadcasted_iota(jnp.int32, values.shape, 1)
    return jnp.where((lanes >= HEAD_DIM) == odd, values, jnp.zeros_like(values))


def join_lanes(even, odd):
    lanes = lax.broadcasted_iota(jnp.int32, even.shape, 1)
    return jnp.where(lanes >= HEAD_DIM, odd, even)


def soft_rows(query, key):
    scores = product_right(query, key) * HEAD_DIM ** (-0.5)
    spots = lax.broadcasted_iota(jnp.int32, scores.shape, 1)
    scores = jnp.where(spots < SEQ, scores, -1e30)
    terms = jnp.exp(scores - jnp.max(scores, axis=-1, keepdims=True))
    return terms / jnp.sum(terms, axis=-1, keepdims=True)


def forward_kernel(part, keep, side_ref, stream_ref, vector_ref, gathered_ref, *refs):
    out_ref = refs[0]
    if keep:
        packed_ref, mixed_ref, attn_ref, pre_ref, mlp_ref = refs[1:6]
        flat_ref, wide_ref, qkv_ref, up_ref, hidden_ref, sems = refs[6:]
    else:
        flat_ref, wide_ref, qkv_ref, up_ref, hidden_ref, packed_ref, mixed_ref, sems = refs[1:]
    fetch_rows(side_ref, part, gathered_ref, flat_ref, sems)
    spread_columns(flat_ref, 0, 3, wide_ref, qkv_ref)
    spread_columns(flat_ref, 4 * D, FF // D, wide_ref, up_ref)
    w_proj = matrix_rows(flat_ref, 3 * D, D)
    w_down = matrix_rows(flat_ref, 4 * D + FF, FF)
    vectors = vector_ref[...].astype(single)
    stream = stream_ref[...]
    normed = (norm_parts(stream)[0] * vectors[0:1] + vectors[1:2]).astype(narrow)
    for group in range(3):
        packed_ref[:, pl.ds(group * D, D)] = product_plain(normed, qkv_ref[group]).astype(narrow)
    for image in range(stream.shape[0] // PAD_SEQ):
        rows = pl.ds(image * PAD_SEQ, PAD_SEQ)
        for pair in range(HEADS // 2):
            query, key, value = [
                packed_ref[rows, pl.ds(group * D + pair * 128, 128)] for group in range(3)
            ]
            done = [
                product_plain(soft_rows(head_lanes(query, odd), key).astype(narrow), value)
                for odd in (False, True)
            ]
            mixed_ref[rows, pl.ds(pair * 128, 128)] = join_lanes(*done).astype(narrow)
    attn = product_plain(mixed_ref[...], w_proj)
    middle = stream + vectors[2:3] * attn
    normed_two = (norm_parts(middle)[0] * vectors[3:4] + vectors[4:5]).astype(narrow)
    for group in range(FF // D):
        spot = pl.ds(group * D, D)
        pre = product_plain(normed_two, up_ref[group])
        if keep:
            pre_ref[:, spot] = pre
        hidden_ref[:, spot] = (0.5 * pre * (1.0 + gelu_tanh(pre))).astype(narrow)
    mlp = product_plain(hidden_ref[...], w_down)
    out_ref[...] = middle + vectors[5:6] * mlp
    if keep:
        attn_ref[...] = attn
        mlp_ref[...] = mlp


def layer_scratch(gathered):
    rows, blocks = gathered.shape[3], 2 * gathered.shape[0]
    return [
        pltpu.VMEM((blocks, rows, D), narrow),
        pltpu.VMEM((D // 128, FF, 128), single),
        pltpu.VMEM((3, D, D), narrow),
        pltpu.VMEM((FF // D, D, D), narrow),
    ]


def layer_specs_in(count):
    return (
        [pl.BlockSpec(memory_space=pltpu.SMEM)]
        + [pl.BlockSpec(memory_space=pltpu.VMEM)] * (count - 2)
        + [pl.BlockSpec(memory_space=pl.ANY)]
    )


def layer_forward(side, stream, vectors, gathered, part, keep):
    tokens = stream.shape[0]
    shapes = [jax.ShapeDtypeStruct((tokens, D), single)]
    extra = [
        jax.ShapeDtypeStruct((tokens, 3 * D), narrow),
        jax.ShapeDtypeStruct((tokens, D), narrow),
        jax.ShapeDtypeStruct((tokens, D), single),
        jax.ShapeDtypeStruct((tokens, FF), single),
        jax.ShapeDtypeStruct((tokens, D), single),
    ]
    scratch = layer_scratch(gathered) + [pltpu.VMEM((tokens, FF), narrow)]
    if keep:
        shapes = shapes + extra
    else:
        scratch = scratch + [pltpu.VMEM((tokens, 3 * D), narrow), pltpu.VMEM((tokens, D), narrow)]
    scratch.append(pltpu.SemaphoreType.DMA((4,)))
    return pl.pallas_call(
        lambda *refs: forward_kernel(part, keep, *refs),
        out_shape=shapes,
        in_specs=layer_specs_in(4),
        out_specs=[pl.BlockSpec(memory_space=pltpu.VMEM)] * len(shapes),
        scratch_shapes=scratch,
        compiler_params=pltpu.CompilerParams(vmem_limit_bytes=56 << 20),
        cost_estimate=pl.CostEstimate(flops=2 * 10**9, bytes_accessed=2 * 10**7, transcendentals=2 * 10**6),
    )(side, stream, vectors, gathered)


def mlp_back_kernel(
    part,
    side_ref,
    grad_ref,
    stream_ref,
    attn_ref,
    pre_ref,
    mlp_ref,
    vector_ref,
    gathered_ref,
    *refs,
):
    grad_mid_ref, all_grad_ref, vector_grad_ref = refs[-10:-7]
    flat_ref, wide_ref, up_ref, hidden_ref, grad_pre_ref, weight_grad_ref, sems = refs[-7:]
    fetch_rows(side_ref, part, gathered_ref, flat_ref, sems)
    spread_columns(flat_ref, 4 * D, FF // D, wide_ref, up_ref)
    w_down = matrix_rows(flat_ref, 4 * D + FF, FF)
    vectors = vector_ref[...].astype(single)
    grad_out = grad_ref[...]
    vector_grad_ref[...] = jnp.zeros_like(vector_grad_ref)
    attn = attn_ref[...]
    middle = stream_ref[...] + vectors[2:3] * attn
    unit_two, spread_two = norm_parts(middle)
    normed_two = (unit_two * vectors[3:4] + vectors[4:5]).astype(narrow)
    vector_grad_ref[pl.ds(5, 1), :] = jnp.sum(grad_out * mlp_ref[...], axis=0, keepdims=True)
    grad_mlp = (grad_out * vectors[5:6]).astype(narrow)
    grad_normed_two = jnp.zeros_like(grad_out)
    for group in range(FF // D):
        spot = pl.ds(group * D, D)
        pre = pre_ref[:, spot]
        bent = gelu_tanh(pre)
        hidden_ref[:, spot] = (0.5 * pre * (1.0 + bent)).astype(narrow)
        slope = 0.5 * (1.0 + bent) + 0.5 * pre * (1.0 - bent * bent) * GELU_SCALE * (
            1.0 + 3.0 * GELU_CUBE * pre * pre
        )
        grad_hidden = product_right(grad_mlp, w_down[group * D : (group + 1) * D])
        grad_pre = (grad_hidden * slope).astype(narrow)
        grad_pre_ref[:, spot] = grad_pre
        grad_normed_two = grad_normed_two + product_right(grad_pre, up_ref[group])
    for group in range(FF // D):
        spot = pl.ds(group * D, D)
        up_grad = product_left(normed_two, grad_pre_ref[:, spot])
        down_grad = product_left(hidden_ref[:, spot], grad_mlp)
        for column in range(D // 128):
            lane = slice(column * 128, (column + 1) * 128)
            weight_grad_ref[column, pl.ds(group, D, stride=FF // D), :] = up_grad[:, lane]
            weight_grad_ref[column, pl.ds(FF + group * D, D), :] = down_grad[:, lane]
    vector_grad_ref[pl.ds(3, 1), :] = jnp.sum(grad_normed_two * unit_two, axis=0, keepdims=True)
    vector_grad_ref[pl.ds(4, 1), :] = jnp.sum(grad_normed_two, axis=0, keepdims=True)
    grad_mid = grad_out + norm_back(grad_normed_two, unit_two, spread_two, vectors[3:4])
    vector_grad_ref[pl.ds(2, 1), :] = jnp.sum(grad_mid * attn, axis=0, keepdims=True)
    grad_mid_ref[...] = grad_mid
    store_rows(weight_grad_ref, all_grad_ref, 4 * D, sems.at[0])


def attention_back_kernel(
    part,
    side_ref,
    grad_ref,
    stream_ref,
    packed_ref,
    mixed_ref,
    vector_ref,
    gathered_ref,
    *refs,
):
    grad_in_ref, all_grad_ref, vector_grad_ref = refs[-10:-7]
    flat_ref, wide_ref, qkv_ref, grad_mixed_ref, grad_packed_ref, weight_grad_ref, sems = refs[-7:]
    fetch_rows(side_ref, part, gathered_ref, flat_ref, sems)
    spread_columns(flat_ref, 0, 3, wide_ref, qkv_ref)
    w_proj = matrix_rows(flat_ref, 3 * D, D)
    vectors = vector_ref[...].astype(single)
    vector_grad_ref[...] = jnp.zeros_like(vector_grad_ref)
    grad_mid = grad_ref[...]
    stream = stream_ref[...]
    grad_attn = (grad_mid * vectors[2:3]).astype(narrow)
    proj_grad = product_left(mixed_ref[...], grad_attn)
    for column in range(D // 128):
        weight_grad_ref[column, pl.ds(3 * D, D), :] = proj_grad[:, column * 128 : (column + 1) * 128]
    grad_mixed_ref[...] = product_right(grad_attn, w_proj).astype(narrow)
    for image in range(stream.shape[0] // PAD_SEQ):
        rows = pl.ds(image * PAD_SEQ, PAD_SEQ)
        for pair in range(HEADS // 2):
            query, key, value = [
                packed_ref[rows, pl.ds(group * D + pair * 128, 128)] for group in range(3)
            ]
            grad_mixed = grad_mixed_ref[rows, pl.ds(pair * 128, 128)]
            parts = []
            for odd in (False, True):
                probs = soft_rows(head_lanes(query, odd), key)
                grad_probs = product_right(head_lanes(grad_mixed, odd), value)
                grad_value = product_left(probs.astype(narrow), grad_mixed)
                grad_scores = probs * (grad_probs - jnp.sum(probs * grad_probs, axis=-1, keepdims=True))
                grad_raw = (grad_scores * HEAD_DIM ** (-0.5)).astype(narrow)
                parts.append((product_plain(grad_raw, key), product_left(grad_raw, query), grad_value))
            for group in range(3):
                grad_packed_ref[rows, pl.ds(group * D + pair * 128, 128)] = join_lanes(
                    parts[0][group], parts[1][group]
                ).astype(narrow)
    unit_one, spread_one = norm_parts(stream)
    normed = (unit_one * vectors[0:1] + vectors[1:2]).astype(narrow)
    grad_normed = jnp.zeros_like(grad_mid)
    for group in range(3):
        grad_part = grad_packed_ref[:, pl.ds(group * D, D)]
        grad_normed = grad_normed + product_right(grad_part, qkv_ref[group])
        qkv_grad = product_left(normed, grad_part)
        for column in range(D // 128):
            lane = slice(column * 128, (column + 1) * 128)
            weight_grad_ref[column, pl.ds(group, D, stride=3), :] = qkv_grad[:, lane]
    vector_grad_ref[pl.ds(0, 1), :] = jnp.sum(grad_normed * unit_one, axis=0, keepdims=True)
    vector_grad_ref[pl.ds(1, 1), :] = jnp.sum(grad_normed, axis=0, keepdims=True)
    grad_in_ref[...] = grad_mid + norm_back(grad_normed, unit_one, spread_one, vectors[0:1])
    store_rows(weight_grad_ref, all_grad_ref, 0, sems.at[0])


def store_rows(weight_grad_ref, all_grad_ref, first_row, sem):
    copy = pltpu.make_async_copy(
        weight_grad_ref, all_grad_ref.at[:, pl.ds(first_row, weight_grad_ref.shape[1])], sem
    )
    copy.start()
    copy.wait()


def layer_back(kernel, part, weight_rows, side, inputs, vectors, gathered, started, waits, columns, buffers):
    tokens = inputs[0].shape[0]
    rows, blocks = gathered.shape[3], 2 * gathered.shape[0]
    return pl.pallas_call(
        lambda *refs: kernel(part, *refs),
        out_shape=[
            jax.ShapeDtypeStruct((tokens, D), single),
            jax.ShapeDtypeStruct((D // 128, MATRIX_ROWS, 128), single),
            jax.ShapeDtypeStruct((8, D), single),
        ],
        in_specs=layer_specs_in(len(inputs) + 3)
        + [pl.BlockSpec(memory_space=pl.ANY)] * (len(started) + len(waits)),
        out_specs=[
            pl.BlockSpec(memory_space=pltpu.VMEM),
            pl.BlockSpec(memory_space=pl.ANY),
            pl.BlockSpec(memory_space=pltpu.VMEM),
        ],
        input_output_aliases={len(inputs) + 3: 1} if started else {},
        scratch_shapes=[
            pltpu.VMEM((blocks, rows, D), narrow),
            pltpu.VMEM((D // 128, columns * D, 128), single),
            pltpu.VMEM((columns, D, D), narrow),
        ]
        + [pltpu.VMEM((tokens, width), narrow) for width in buffers]
        + [pltpu.VMEM((D // 128, weight_rows, 128), single), pltpu.SemaphoreType.DMA((4,))],
        compiler_params=pltpu.CompilerParams(vmem_limit_bytes=56 << 20),
        cost_estimate=pl.CostEstimate(flops=5 * 10**9, bytes_accessed=4 * 10**7, transcendentals=2 * 10**6),
    )(side, *inputs, vectors, gathered, *started, *waits)


def mlp_back(side, grad_out, saved, vectors, gathered, part, waits):
    stream, packed, mixed, attn, pre, mlp = saved
    return layer_back(
        mlp_back_kernel, part, 2 * FF, side, (grad_out, stream, attn, pre, mlp), vectors, gathered, (), waits,
        FF // D, (FF, FF),
    )


def attention_back(side, grad_mid, saved, vectors, gathered, part, started, waits):
    stream, packed, mixed, attn, pre, mlp = saved
    return layer_back(
        attention_back_kernel, part, 4 * D, side, (grad_mid, stream, packed, mixed), vectors, gathered, (started,), waits,
        3, (D, 3 * D),
    )


def after(value, *tokens):
    def kernel(*refs):
        refs[-1][...] = refs[0][...]

    return pl.pallas_call(
        kernel,
        out_shape=jax.ShapeDtypeStruct(value.shape, value.dtype),
        in_specs=[pl.BlockSpec(memory_space=pltpu.VMEM)] + [pl.BlockSpec(memory_space=pl.ANY)] * len(tokens),
        out_specs=pl.BlockSpec(memory_space=pltpu.VMEM),
    )(value, *tokens)


def embed_back_kernel(grad_ref, patch_ref, shown_ref, gain_ref, vector_ref, *refs):
    out_ref = refs[-1]
    grad = grad_ref[...]
    images = grad.shape[0] // PAD_SEQ
    shown = shown_ref[...]
    position = jnp.zeros((PAD_SEQ, D), single)
    token = jnp.zeros((1, D), single)
    patch_grads = []
    for image in range(images):
        here = grad[image * PAD_SEQ : (image + 1) * PAD_SEQ]
        position = position + here
        rows = here[1:SEQ]
        seen = shown[image * PATCHES : (image + 1) * PATCHES]
        token = token + jnp.sum(rows * (1.0 - seen), axis=0, keepdims=True)
        patch_grads.append((rows * seen).astype(narrow))
    patch_grad = product_left(patch_ref[...], jnp.concatenate(patch_grads))
    out_ref[...] = jnp.zeros_like(out_ref)
    for column in range(D // 128):
        lane = slice(column * 128, (column + 1) * 128)
        out_ref[column, pl.ds(0, PIX), :] = patch_grad[:, lane]
        out_ref[column, pl.ds(PIX, SEQ), :] = position[:SEQ, lane]
        out_ref[column, pl.ds(PIX + SEQ, 1), :] = position[0:1, lane]
        out_ref[column, pl.ds(PIX + SEQ + 1, 1), :] = token[:, lane]
        out_ref[column, pl.ds(PIX + SEQ + 2, 2), :] = gain_ref[:, lane]
        out_ref[column, pl.ds(EMBED_ROWS, vector_ref.shape[0]), :] = vector_ref[:, lane]


def embed_back(grad, patch_rows, shown, gains, vector_grads, rows, waits):
    return pl.pallas_call(
        embed_back_kernel,
        out_shape=jax.ShapeDtypeStruct((D // 128, rows, 128), single),
        in_specs=[pl.BlockSpec(memory_space=pltpu.VMEM)] * 5 + [pl.BlockSpec(memory_space=pl.ANY)] * len(waits),
        out_specs=pl.BlockSpec(memory_space=pltpu.VMEM),
        compiler_params=pltpu.CompilerParams(vmem_limit_bytes=40 << 20),
        cost_estimate=pl.CostEstimate(flops=10**9, bytes_accessed=2 * 10**7, transcendentals=0),
    )(grad, patch_rows, shown, gains, vector_grads, *waits)


def proto_units(values):
    rounded = values.astype(narrow).astype(single)
    scale = lax.rsqrt(jnp.sum(rounded * rounded, axis=-1, keepdims=True) + 1e-06)
    return rounded, scale, (rounded * scale).astype(narrow)


def proto_terms(teacher_z, student_z, teacher_unit, student_unit, centre_column):
    teacher_logits = product_right(teacher_unit, teacher_z)
    logits = product_right(student_unit, student_z)
    teacher_exp = jnp.exp((teacher_logits - centre_column) * (1.0 / tau_teacher))
    student_exp = jnp.exp(logits * (1.0 / tau_student))
    return teacher_logits, logits, teacher_exp, student_exp


def logits_kernel(
    teacher_z_ref,
    student_z_ref,
    teacher_ref,
    student_ref,
    centre_ref,
    class_ref,
    mixed_ref,
    sums_ref,
    centre_sum_ref,
    student_mix_ref,
    teacher_mix_ref,
    totals_ref,
):
    step = pl.program_id(0)

    @pl.when(step == 0)
    def _():
        student_mix_ref[...] = jnp.zeros_like(student_mix_ref)
        teacher_mix_ref[...] = jnp.zeros_like(teacher_mix_ref)
        totals_ref[...] = jnp.zeros_like(totals_ref)

    teacher_unit = proto_units(teacher_ref[...])[2]
    student_unit = proto_units(student_ref[...])[2]
    teacher_logits, logits, teacher_exp, student_exp = proto_terms(
        teacher_z_ref[...], student_z_ref[...], teacher_unit, student_unit, centre_ref[...]
    )
    totals_ref[pl.ds(0, 1), :] += jnp.sum(teacher_exp, axis=0, keepdims=True)
    totals_ref[pl.ds(1, 1), :] += jnp.sum(student_exp, axis=0, keepdims=True)
    totals_ref[pl.ds(2, 1), :] += jnp.sum(teacher_exp * logits, axis=0, keepdims=True)
    centre_sum_ref[...] = jnp.sum(teacher_logits * class_ref[0:1], axis=1, keepdims=True)
    student_mix_ref[...] += product_left(student_unit, student_exp.astype(narrow))
    teacher_mix_ref[...] += product_left(student_unit, teacher_exp.astype(narrow))

    @pl.when(step == pl.num_programs(0) - 1)
    def _():
        mixed_ref[:, pl.ds(0, BOT)] = student_mix_ref[...].T
        mixed_ref[:, pl.ds(BOT, BOT)] = teacher_mix_ref[...].T
        lower = jnp.zeros((128 - totals_ref.shape[0], totals_ref.shape[1]), single)
        mixed_ref[:, pl.ds(2 * BOT, 128)] = jnp.concatenate([totals_ref[...], lower]).T
        sums_ref[...] = totals_ref[...]


def proto_specs(rows, block):
    whole = pl.BlockSpec((rows, BOT), lambda i: (0, 0))
    table = pl.BlockSpec((block, BOT), lambda i: (i, 0))
    column = pl.BlockSpec((block, 1), lambda i: (i, 0))
    lines = pl.BlockSpec((8, rows), lambda i: (0, 0))
    return whole, table, column, lines


def logits_pass(teacher_z, student_z, teacher, student, centre_column, class_lines):
    rows, protos_here = teacher_z.shape[0], student.shape[0]
    block = protos_here // 4
    whole, table, column, lines = proto_specs(rows, block)
    return pl.pallas_call(
        logits_kernel,
        grid=(4,),
        out_shape=[
            jax.ShapeDtypeStruct((rows, 2 * BOT + 128), single),
            jax.ShapeDtypeStruct((8, rows), single),
            jax.ShapeDtypeStruct((protos_here, 1), single),
        ],
        in_specs=[whole, whole, table, table, column, lines],
        out_specs=[pl.BlockSpec((rows, 2 * BOT + 128), lambda i: (0, 0)), lines, column],
        scratch_shapes=[
            pltpu.VMEM((BOT, rows), single),
            pltpu.VMEM((BOT, rows), single),
            pltpu.VMEM((8, rows), single),
        ],
        compiler_params=pltpu.CompilerParams(vmem_limit_bytes=56 << 20),
        cost_estimate=pl.CostEstimate(flops=5 * 10**9, bytes_accessed=10**7, transcendentals=5 * 10**6),
    )(teacher_z, student_z, teacher, student, centre_column, class_lines)


def proto_grad_kernel(
    teacher_z_ref, student_z_ref, teacher_ref, student_ref, centre_ref, scale_ref, *refs
):
    grad_ref, square_ref = refs[-2:]
    step = pl.program_id(0)

    @pl.when(step == 0)
    def _():
        square_ref[...] = jnp.zeros_like(square_ref)

    teacher_unit = proto_units(teacher_ref[...])[2]
    rounded, scale, student_unit = proto_units(student_ref[...])
    student_z = student_z_ref[...]
    _, _, teacher_exp, student_exp = proto_terms(
        teacher_z_ref[...], student_z, teacher_unit, student_unit, centre_ref[...]
    )
    grad_logits = (student_exp * scale_ref[0:1] - teacher_exp * scale_ref[1:2]).astype(narrow)
    unit_grad = product_plain(grad_logits, student_z)
    along = jnp.sum(unit_grad * rounded, axis=-1, keepdims=True)
    grad = scale * (unit_grad - rounded * (along * scale * scale))
    grad_ref[...] = grad
    square_ref[...] += jnp.broadcast_to(jnp.sum(grad * grad), square_ref.shape)


def proto_grad_pass(teacher_z, student_z, teacher, student, centre_column, scale_lines, waits):
    rows, protos_here = teacher_z.shape[0], student.shape[0]
    block = protos_here // 4
    whole, table, column, lines = proto_specs(rows, block)
    return pl.pallas_call(
        proto_grad_kernel,
        grid=(4,),
        out_shape=[
            jax.ShapeDtypeStruct((protos_here, BOT), single),
            jax.ShapeDtypeStruct((8, 128), single),
        ],
        in_specs=[whole, whole, table, table, column, lines]
        + [pl.BlockSpec(memory_space=pl.ANY)] * len(waits),
        out_specs=[table, pl.BlockSpec((8, 128), lambda i: (0, 0))],
        compiler_params=pltpu.CompilerParams(vmem_limit_bytes=56 << 20),
        cost_estimate=pl.CostEstimate(flops=4 * 10**9, bytes_accessed=10**7, transcendentals=5 * 10**6),
    )(teacher_z, student_z, teacher, student, centre_column, scale_lines, *waits)


def proto_update(factor, student, moment, second, teacher, grad):
    def kernel(factor_ref, *refs):
        weight, moment, second, teacher, grad = [ref[...] for ref in refs[:5]]
        done = adam_update(weight, moment, second, grad * factor_ref[0], teacher)
        for ref, value in zip(refs[5:], done):
            ref[...] = value

    block = student.shape[0] // 4
    table = pl.BlockSpec((block, BOT), lambda i: (i, 0))
    return pl.pallas_call(
        kernel,
        grid=(4,),
        out_shape=[
            jax.ShapeDtypeStruct(student.shape, narrow if number == 3 else single) for number in range(5)
        ],
        in_specs=[pl.BlockSpec(memory_space=pltpu.SMEM)] + [table] * 5,
        out_specs=[table] * 5,
        compiler_params=pltpu.CompilerParams(vmem_limit_bytes=40 << 20),
        cost_estimate=pl.CostEstimate(flops=10**7, bytes_accessed=2 * 10**7, transcendentals=0),
    )(factor.reshape(1), student, moment, second, teacher, grad)


def head_grads_kernel(
    place_ref, inputs_ref, grads_ref, *refs,
):
    own_ref, partner_ref, window_ref, rows_ref, product_ref, third_ref, bottle_ref, line_ref, sems = refs[-9:]
    slot = own_ref.shape[0]
    lead = product_ref.shape[0] - window_ref.shape[1]
    number = lax.broadcasted_iota(jnp.int32, (slot, 1), 0)
    product_ref[pl.ds(0, lead), :] = jnp.zeros((lead, ROW), single)

    def block(at, out_ref):
        column = pl.multiple_of(place_ref[at], 128)
        grad_column = pl.multiple_of(place_ref[at + 3], 128)
        copies = [
            pltpu.make_async_copy(
                inputs_ref.at[:, pl.ds(column, window_ref.shape[1])], window_ref, sems.at[0]
            ),
            pltpu.make_async_copy(grads_ref.at[:, pl.ds(grad_column, ROW)], rows_ref, sems.at[1]),
        ]
        for copy in copies:
            copy.start()
        for copy in copies:
            copy.wait()
        window = window_ref[...]
        for piece in range(4):
            spot = pl.ds(piece * (ROW // 4), ROW // 4)
            product_ref[pl.ds(lead, window.shape[1]), spot] = product_left(window, rows_ref[:, spot])
        from_row = pl.multiple_of(lead + place_ref[at + 1], 8)
        kept = jnp.where(number < place_ref[at + 2], product_ref[pl.ds(from_row, slot), :], 0.0)
        out_ref[...] = kept.astype(out_ref.dtype)

    @pl.when(place_ref[8] == 0)
    def _():
        block(0, own_ref)

    @pl.when(place_ref[8] == 1)
    def _():
        column = pl.multiple_of(place_ref[9], 128)
        copies = [
            pltpu.make_async_copy(
                inputs_ref.at[:, pl.ds(column, third_ref.shape[1])], third_ref, sems.at[0]
            ),
            pltpu.make_async_copy(grads_ref.at[:, pl.ds(2 * HID, BOT)], bottle_ref, sems.at[1]),
        ]
        for copy in copies:
            copy.start()
        for copy in copies:
            copy.wait()
        third = product_left(third_ref[...], bottle_ref[...])
        for lane in range(BOT // 128):
            line_ref[lane] = third[:, lane * 128 : (lane + 1) * 128]
        for group in range(ROW // BOT):
            for lane in range(BOT // 128):
                value = line_ref[lane, pl.ds(group, slot, stride=ROW // BOT), :]
                own_ref[:, pl.ds(group * BOT + lane * 128, 128)] = jnp.where(
                    number < place_ref[2], value, 0.0
                )

    block(4, partner_ref)


def head_grads(place, inputs_all, grads_all, slot, lead, waits):
    rows = inputs_all.shape[0]
    wide = slot * ROW // BOT
    return pl.pallas_call(
        head_grads_kernel,
        out_shape=[jax.ShapeDtypeStruct((slot, ROW), kind) for kind in (single, narrow)],
        in_specs=[pl.BlockSpec(memory_space=pltpu.SMEM)]
        + [pl.BlockSpec(memory_space=pl.ANY)] * (2 + len(waits)),
        out_specs=[pl.BlockSpec(memory_space=pltpu.VMEM)] * 2,
        scratch_shapes=[
            pltpu.VMEM((rows, 256), narrow),
            pltpu.VMEM((rows, ROW), narrow),
            pltpu.VMEM((lead + 256, ROW), single),
            pltpu.VMEM((rows, wide), narrow),
            pltpu.VMEM((rows, BOT), narrow),
            pltpu.VMEM((BOT // 128, wide, 128), single),
            pltpu.SemaphoreType.DMA((2,)),
        ],
        compiler_params=pltpu.CompilerParams(vmem_limit_bytes=56 << 20),
        cost_estimate=pl.CostEstimate(flops=4 * 10**9, bytes_accessed=2 * 10**7, transcendentals=0),
    )(place, inputs_all, grads_all, *waits)


def close_local(
    patches,
    masked,
    slot_used,
    stem,
    stem_moment,
    stem_second,
    stem_teacher,
    layers,
    layer_moment,
    layer_second,
    layer_teacher,
    protos,
    proto_moment,
    proto_second,
    proto_teacher,
    centre,
):
    count = 1 << len(BITS)
    half = count // 2
    me = lax.axis_index("dev")
    across = MASKS["b"]
    student_side = me >= half
    groups = [list(range(half)), list(range(half, count))]
    quarter = half // 2
    swap = jnp.where(student_side, quarter, 0)
    side = student_side.astype(jnp.int32).reshape(1)
    images_here = patches.shape[0]
    rows_here = images_here * 17
    pair_rows = -(-2 * rows_here // 16) * 16
    more_rows = pair_rows - 2 * rows_here
    stem_piece = stem.shape[0]
    layer_piece = layers.shape[1]
    block_rows = MATRIX_ROWS // count
    block = block_rows * D
    tail = layer_piece * count - MATRIX_ROWS * D
    drift = layer_piece - block
    bounds = head_bounds(count, stem_piece)
    sizes = [bounds[i + 1] - bounds[i] for i in range(count)]
    slot = max(sizes)
    starts = [b * ROW + EMBED_FLAT - stem_piece * i for i, b in enumerate(bounds[:-1])]
    first_w2 = bounds.index(D)
    first_w3 = bounds.index(D + HID)
    row_index = jnp.concatenate([jnp.zeros((images_here, 1), jnp.int32), masked + 1], axis=1)
    masked_here = jnp.any(
        masked[:, :, None] == jnp.arange(PATCHES, dtype=jnp.int32)[None, None, :], axis=1
    )
    kept = slot_used.astype(single)

    front = 16
    early_rows = -(-stem_piece // D)
    late_start = early_rows * D - stem_piece
    embed_rows = -(-early_rows // 16) * 16
    own_layers = jnp.concatenate([layer_teacher, layers])
    own_tail = own_layers[:, layer_piece - tail :].reshape(2 * LAYERS, tail // 128, 128)
    before = lax.ppermute(own_tail, "dev", step_pairs(count, 1))
    head_span = GROUP * ROW
    stems = jnp.stack([as_lanes(stem_teacher), as_lanes(stem)])
    stems_next = lax.ppermute(stems[:, : head_span // 128], "dev", step_pairs(count, -1))
    def per_device(rows):
        return lax.dynamic_slice(jnp.array(rows, jnp.int32), (me, 0), (1, len(rows[0]))).reshape(-1)

    def spots(*values):
        return [part for value in values for part in (value // 128, value % 128)]

    place = per_device(
        [
            spots(starts[i] + front * 128, front * 128 + (0 if i == 0 else late_start), tail - drift * i)
            for i in range(count)
        ]
    )
    head_blocks, layer_blocks, embed_blocks, vector_blocks = own_blocks(
        place,
        stems,
        stems_next,
        as_lanes(own_layers),
        before,
        (front, stem_piece, layer_piece, tail),
        slot,
        block_rows,
        embed_rows,
    )

    other_layers = lax.ppermute(layer_blocks, "dev", pairs(count, across))
    both_layers = jnp.where(
        student_side,
        jnp.stack([other_layers, layer_blocks]),
        jnp.stack([layer_blocks, other_layers]),
    )
    gathered = lax.all_gather(both_layers, "dev", axis=0, axis_index_groups=groups)
    head_out = jnp.where(student_side, head_blocks[0], head_blocks[1])
    head_keep = jnp.where(student_side, head_blocks[1], head_blocks[0])
    head_got = lax.ppermute(head_out, "dev", pairs(count, across))
    both_head = jnp.where(
        student_side, jnp.stack([head_got, head_keep]), jnp.stack([head_keep, head_got])
    )

    vectors = lax.ppermute(vector_blocks, "dev", [(count - 1, 0)])
    seed = jnp.concatenate([embed_blocks.reshape(2 * embed_rows, D), vectors.reshape(8 * 2 * LAYERS, D)])
    third = -(-seed.shape[0] // 48) * 16
    spread_parts = []
    for number, order in enumerate(("xyba", "baxy", "ybax")):
        spread = seed[number * third : (number + 1) * third]
        reached = [0, 1]
        for name in order:
            moves = [(i, i ^ MASKS[name]) for i in reached]
            got = lax.ppermute(spread, "dev", moves)
            targets = [t for s, t in moves]
            is_target = jnp.array([i in targets for i in range(count)])[me]
            spread = jnp.where(is_target, got, spread)
            reached = reached + targets
        spread_parts.append(spread)
    spread = jnp.concatenate(spread_parts)
    other = lax.ppermute(spread, "dev", pairs(count, 1))
    is_even = me % 2 == 0
    even = jnp.where(is_even, spread, other)
    odd = jnp.where(is_even, other, spread)
    embed_all = [
        jnp.concatenate(
            [
                even[m * embed_rows : m * embed_rows + early_rows],
                odd[m * embed_rows : m * embed_rows + EMBED_ROWS - early_rows],
            ]
        )
        for m in range(2)
    ]
    gathered_head = lax.all_gather(after(both_head, gathered, even, odd), "dev", axis=0, axis_index_groups=groups)
    vectors_all = even[2 * embed_rows :].reshape(2, LAYERS, 8, D)

    plan = []
    for i in range(1, count):
        target = 0 if i < first_w2 else 1 if i < first_w3 else 2
        row = bounds[i] - (0, D, D + HID)[target]
        skip = max(-row, 0)
        owner = 1 if i >= half else 0
        plan.append((i ^ across if owner else i, owner, skip, sizes[i] - skip, target, row + skip))

    def embed_parts(model):
        rows = embed_all[model]
        return (rows[:PIX], rows[PIX : PIX + SEQ], rows[PIX + SEQ :], None, None, None)

    def head_rows(stream, extras):
        chosen = jnp.take_along_axis(stream, row_index[:, :, None], axis=1).reshape(rows_here, D)
        normed = layer_norm(chosen, extras[2].astype(single), extras[3].astype(single)).astype(narrow)
        return chosen, normed

    def start_rows(parts, student):
        stream = embed(parts, patches, masked_here, student)
        return jnp.pad(stream, ((0, 0), (0, PAD_SEQ - SEQ), (0, 0))).reshape(images_here * PAD_SEQ, D)

    student_parts = embed_parts(1)
    stream = start_rows(student_parts, True)
    saved_layers = []
    for layer_index in range(LAYERS):
        before_layer = stream
        stream, *saved = layer_forward(
            side, stream, vectors_all[1, layer_index], gathered, LAYERS + layer_index, True
        )
        saved_layers.append((before_layer, *saved))
    teacher_parts = embed_parts(0)
    teacher_stream = start_rows(teacher_parts, False)
    for layer_index in range(LAYERS):
        teacher_stream = layer_forward(
            side, teacher_stream, vectors_all[0, layer_index], gathered, layer_index, False
        )[0]
    stream = stream.reshape(images_here, PAD_SEQ, D)
    teacher_stream = teacher_stream.reshape(images_here, PAD_SEQ, D)
    chosen, student_normed = head_rows(stream, student_parts[2])
    teacher_normed = head_rows(teacher_stream, teacher_parts[2])[1]

    normed_got = lax.ppermute(
        jnp.where(student_side, teacher_normed, student_normed), "dev", pairs(count, across)
    )
    normed = jnp.where(
        student_side,
        jnp.concatenate([normed_got, student_normed]),
        jnp.concatenate([teacher_normed, normed_got]),
    )
    normed = jnp.pad(normed, ((0, more_rows), (0, 0)))
    third_end = (bounds[-2] - D - HID + slot) * (ROW // BOT)
    acts_width = D + HID + max(third_end, HID)
    unit_z, acts, bottleneck, pre_one, pre_two = head_pass(
        head_up_kernel,
        plan,
        side,
        (normed,),
        gathered_head,
        [
            jax.ShapeDtypeStruct((pair_rows, BOT), narrow),
            jax.ShapeDtypeStruct((pair_rows, acts_width), narrow),
            jax.ShapeDtypeStruct((pair_rows, BOT), single),
            jax.ShapeDtypeStruct((pair_rows, HID), single),
            jax.ShapeDtypeStruct((pair_rows, HID), single),
        ],
    )
    inputs_all = lax.all_gather(acts, "dev", axis=0, axis_index_groups=groups).reshape(half * pair_rows, -1)

    all_rows = half * pair_rows
    kept_row = jnp.broadcast_to(kept[:, None], (images_here, 17)).reshape(1, rows_here)
    kept_pair = cube_gather(kept_row, "b").reshape(1, 2 * rows_here)
    kept_pair = jnp.pad(kept_pair, ((0, 0), (0, more_rows)))
    all_kept = cube_gather(kept_pair, "xygc").reshape(all_rows)
    z_pair = cube_gather(unit_z, "b")
    teacher_z_all = cube_gather(z_pair[0], "xygc").reshape(all_rows, BOT)
    student_z_all = cube_gather(z_pair[1], "gxyc").reshape((2,) * 4 + (pair_rows, BOT))
    student_z_all = jnp.transpose(student_z_all, (0, 3, 1, 2, 4, 5)).reshape(all_rows, BOT)
    protos_here = protos.shape[0]
    own_centre = lax.dynamic_slice(centre, (me * protos_here,), (protos_here,))
    centre_column = own_centre.reshape(protos_here, 1)
    spot_in_pair = jnp.arange(all_rows) % pair_rows
    is_class = (spot_in_pair % 17) == 0
    class_kept = jnp.where(is_class, all_kept, 0.0)
    row_weight = jnp.where(is_class, all_kept, all_kept * (1.0 / 16.0))
    count_total = jnp.sum(class_kept)

    def lines(*values):
        return jnp.pad(jnp.stack(values), ((0, 8 - len(values)), (0, 0)))

    mixed_rows, sums, centre_sum = logits_pass(
        teacher_z_all, student_z_all, proto_teacher, protos, centre_column, lines(class_kept)
    )
    mixed_own = cube_scatter(mixed_rows.reshape((2,) * 4 + (pair_rows, 2 * BOT + 128)), "cgyx", "cgyx")
    mixed_own = mixed_own + lax.ppermute(
        mixed_own.astype(narrow), "dev", [(i, i ^ across) for i in range(half)]
    ).astype(single)
    stages = [sums[:3]]
    for name in "cxyab":
        stages.append(stages[-1] + lax.ppermute(stages[-1], "dev", pairs(count, MASKS[name])))
    sums = stages[-1]
    cross = jnp.log(sums[1]) - sums[2] / (sums[0] * tau_student)
    loss_total = jnp.sum(row_weight * cross)
    scale = row_weight / tau_student
    student_scale, teacher_scale = scale / sums[1], scale / sums[0]
    flags = bit_flags(me)
    pair_at = flags["c"] * 8 + flags["g"] * 4 + flags["y"] * 2 + flags["x"]
    own_scale = lax.dynamic_slice(scale, (pair_at * pair_rows,), (pair_rows,))[:, None]
    grad_unit_z = own_scale * (
        mixed_own[:, :BOT] / mixed_own[:, 2 * BOT + 1 : 2 * BOT + 2]
        - mixed_own[:, BOT : 2 * BOT] / mixed_own[:, 2 * BOT : 2 * BOT + 1]
    )
    own_new_centre = (
        centre_keep * own_centre + (1.0 - centre_keep) * centre_sum.reshape(protos_here) / count_total
    )
    new_centre = cube_gather(own_new_centre.reshape(1, protos_here), "cxyab").reshape(-1)

    grads, grad_normed = head_pass(
        head_down_kernel,
        plan,
        side,
        (grad_unit_z, bottleneck, pre_one, pre_two),
        gathered_head,
        [
            jax.ShapeDtypeStruct((pair_rows, 2 * HID + BOT), narrow),
            jax.ShapeDtypeStruct((pair_rows, D), single),
        ],
        (stages[2],),
    )
    grads_all = lax.all_gather(grads, "dev", axis=0, axis_index_groups=groups).reshape(half * pair_rows, -1)
    normed_back = lax.ppermute(
        grad_normed[:rows_here], "dev", [(i, i ^ across) for i in range(half, count)]
    )
    own_grad_normed = jnp.where(student_side, grad_normed[rows_here : 2 * rows_here], normed_back)
    extras = student_parts[2].astype(single)
    grad_chosen, grad_gain, grad_bias = jax.vjp(layer_norm, chosen, extras[2], extras[3])[1](
        own_grad_normed
    )
    image_index = jnp.arange(images_here, dtype=jnp.int32)[:, None]
    grad_stream = (
        jnp.zeros(stream.shape, single)
        .at[image_index, row_index]
        .add(grad_chosen.reshape(images_here, 17, D))
    )

    grad_stream = grad_stream.reshape(images_here * PAD_SEQ, D)
    middle_row = block_rows // 2
    small_rows = -(-(EMBED_ROWS + 6 * LAYERS) // (16 * count)) * 16
    vector_grads = [None] * LAYERS

    def halves(array):
        middle = array.shape[-2] // 2
        return [array[..., :middle, :], array[..., middle:, :]]

    def cuts(parts, names, order):
        return [cut(part, name, axis, 1) for part, name, axis in zip(parts, names, order)]

    def moves(pieces, order):
        return [move(sent, kept, axis) for (sent, kept, left), axis in zip(pieces, order)]

    def blocks_of(weight_grad, rows):
        return split_bits(weight_grad.reshape(D // 128, count, rows, 128), 1)

    rounds = (("c",), ("x", "b"), ("y", "a"), ("b", "x"), ("a", "y"))

    def advance(state):
        pieces, stage = state
        parts = moves(pieces, rounds[stage])
        names = [left for sent, kept, left in pieces]
        if stage == 0:
            parts, names = halves(parts[0]), names * 2
        return cuts(parts, names, rounds[stage + 1]), stage + 1

    def finish(state):
        while state[1] < len(rounds) - 1:
            state = advance(state)
        return moves(state[0], rounds[-1])

    def sends(states):
        return tuple(sent for pieces, stage in states for sent, kept, left in pieces)

    started = []
    waits, later_waits = (stages[3],), (stages[4],)
    for layer_index in reversed(range(LAYERS)):
        saved, vectors = saved_layers[layer_index], vectors_all[1, layer_index]
        part = LAYERS + layer_index
        started = [advance(state) for state in started]
        grad_stream, weight_grad, late_vectors = mlp_back(
            side, grad_stream, saved, vectors, gathered, part, waits + sends(started)
        )
        started = [advance(state) for state in started]
        grad_stream, weight_grad, early_vectors = attention_back(
            side, grad_stream, saved, vectors, gathered, part, weight_grad, later_waits + sends(started)
        )
        waits, later_waits = (), ()
        vector_grads[layer_index] = (late_vectors + early_vectors)[:6]
        first = (cuts([blocks_of(weight_grad, block_rows)], ["bayxc"], rounds[0]), 0)
        if layer_index == LAYERS - 1:
            proto_grad, proto_square = proto_grad_pass(
                teacher_z_all,
                student_z_all,
                proto_teacher,
                protos,
                centre_column,
                lines(student_scale, teacher_scale),
                sends([first]),
            )
            waits = (proto_square,)
        if layer_index > 0:
            started.append(first)
    started = [advance(state) for state in started]
    small = embed_back(
        grad_stream,
        patches.reshape(images_here * PATCHES, PIX),
        jnp.where(masked_here, 0.0, 1.0).reshape(images_here * PATCHES, 1),
        jnp.stack([grad_gain, grad_bias]),
        jnp.concatenate(vector_grads),
        small_rows * count,
        sends([first] + started),
    )
    small_first = cuts([blocks_of(small, small_rows)], ["bayxc"], rounds[0])
    joined = [
        jnp.concatenate(pair, axis=-2)
        for pair in zip(halves(moves(first[0], "c")[0]), halves(moves(small_first, "c")[0]))
    ]
    last = (cuts(joined, ["bayx"] * 2, rounds[1]), 1)
    later_blocks = [jnp.concatenate(finish(state), axis=1) for state in started]

    def block_place(i):
        column = max(bounds[i], 0) // 128 * 128
        grad_column = 0 if i < first_w2 else HID
        return [column, bounds[i] - column if i else 0, sizes[i] if i else 0, grad_column]

    def third_place(i):
        return [0, 0, sizes[i], 0]

    place = per_device(
        [
            (third_place(i) if i >= first_w3 else block_place(i))
            + block_place(i ^ across)
            + [int(i >= first_w3), D + HID + max(bounds[i] - D - HID, 0) * (ROW // BOT)]
            for i in range(count)
        ]
    )
    own_block_grad, partner_block_grad = head_grads(
        place, inputs_all, grads_all, slot, -min(bounds[1], 0), sends([last])
    )
    block_got = lax.ppermute(partner_block_grad, "dev", [(i, i ^ across) for i in range(half, count)])
    head_block_grad = jnp.where(student_side, own_block_grad, block_got.astype(single))
    pieces, stage = advance(last)
    parts = finish(([(after(sent, own_block_grad), stay, left) for sent, stay, left in pieces], stage))
    middle_row = block_rows // 2
    small_block = jnp.concatenate([part[:, middle_row:] for part in parts], axis=1)
    layer_block = jnp.stack(
        [jnp.concatenate([part[:, :middle_row] for part in parts], axis=1)] + later_blocks[::-1]
    )

    square_local = (
        jnp.sum(head_block_grad * head_block_grad)
        + jnp.sum(layer_block * layer_block)
        + jnp.sum(small_block * small_block)
        + proto_square[0, 0]
    )
    high = square_local.astype(narrow)
    middle = (square_local - high.astype(single)).astype(narrow)
    low = (square_local - high.astype(single) - middle.astype(single)).astype(narrow)
    tile = jnp.pad(jnp.stack([high, middle, low]).reshape(3, 1, 1), ((0, 0), (0, 15), (0, 127)))
    behind = lax.ppermute(layer_block[:, :, :6], "dev", step_pairs(count, -1))
    last_rows = lax.dynamic_slice(
        head_block_grad, (jnp.array(sizes, jnp.int32)[me] - GROUP, 0), (GROUP, ROW)
    )
    previous = lax.ppermute(last_rows, "dev", step_pairs(count, 1))
    place = per_device([spots(head_span - starts[i], drift * i) for i in range(count)])
    stem_lines, layer_lines = own_shards(
        place, head_block_grad, previous, layer_block, behind, lane_rows(stem_piece), lane_rows(layer_piece)
    )
    shared = cube_gather(jnp.concatenate([small_block.astype(narrow), tile], axis=1), "xya")
    shared = cube_gather(after(shared, stem_lines), "bc")
    shared = jnp.moveaxis(shared.reshape((2, 2) + shared.shape[1:]), 0, 2)
    shared = shared.reshape((count,) + shared.shape[3:]).astype(single)
    square_total = jnp.sum(shared[:, :, small_rows, 0])
    small_all = jnp.transpose(shared[:, :, :small_rows], (0, 2, 1, 3)).reshape(small_rows * count, D)
    embed_grad = small_all[:EMBED_ROWS].reshape(-1)
    vector_grad = small_all[EMBED_ROWS : EMBED_ROWS + 6 * LAYERS].reshape(LAYERS, 6 * D)
    layer_grad = layer_lines.reshape(LAYERS, -1)[:, :layer_piece]
    layer_grad = jnp.concatenate(
        [
            layer_grad[:, : layer_piece - tail],
            jnp.where(me == count - 1, vector_grad, layer_grad[:, layer_piece - tail :]),
        ],
        axis=1,
    )
    stem_grad = stem_lines.reshape(-1)[:stem_piece]
    rest = EMBED_FLAT - stem_piece
    second_part = jnp.concatenate([embed_grad[stem_piece:], stem_grad[rest:]])
    stem_grad = jnp.where(
        me == 0, embed_grad[:stem_piece], jnp.where(me == 1, second_part, stem_grad)
    )

    grad_norm = jnp.sqrt(square_total) / count_total
    factor = jnp.minimum(1.0, clip_limit / (grad_norm + 1e-06)) / count_total
    stem_set = adam_update(stem, stem_moment, stem_second, stem_grad * factor, stem_teacher)
    layer_set = adam_update(layers, layer_moment, layer_second, layer_grad * factor, layer_teacher)
    proto_set = proto_update(factor, protos, proto_moment, proto_second, proto_teacher, proto_grad)
    return (loss_total, count_total, grad_norm, new_centre) + stem_set + layer_set + tuple(proto_set)


def solution(mesh):
    count = mesh.shape["dev"]
    stem_length = -(-(EMBED_FLAT + HEAD_ROWS * ROW) // count) * count
    close = fits(count, stem_length // count, (MATRIX_ROWS + 6) * D // count)
    placed = (
        P("dev", None, None),
        P("dev", None),
        P("dev"),
        P("dev"),
        P("dev"),
        P("dev"),
        P("dev"),
        P(None, "dev"),
        P(None, "dev"),
        P(None, "dev"),
        P(None, "dev"),
        P("dev", None),
        P("dev", None),
        P("dev", None),
        P("dev", None),
        P(),
    )
    return jax.shard_map(
        close_local if close else spread_local,
        mesh=mesh,
        in_specs=placed,
        out_specs=(
            P(),
            P(),
            P(),
            P(),
            P("dev"),
            P("dev"),
            P("dev"),
            P("dev"),
            P("dev"),
            P(None, "dev"),
            P(None, "dev"),
            P(None, "dev"),
            P(None, "dev"),
            P(None, "dev"),
            P("dev", None),
            P("dev", None),
            P("dev", None),
            P("dev", None),
            P("dev", None),
        ),
        check_vma=False,
    )
```

```python
import jax
import jax.numpy as jnp
from jax import lax
from jax.experimental import pallas as pl
from jax.experimental.pallas import tpu as pltpu
from jax.sharding import PartitionSpec as P

D = 384
HEADS = 6
HEAD_DIM = 64
FF = 1536
HID = 2048
BOT = 256
PIX = 588
PATCHES = 256
LAYERS = 2
STEP = 10
SEQ = 257


tau_student = 0.1
tau_teacher = 0.04
clip_limit = 0.003
learn_rate = 0.03
beta_one = 0.9
beta_two = 0.999
adam_eps = 1e-08
decay_rate = 0.04
teacher_keep = 0.8
centre_keep = 0.9
narrow = jnp.bfloat16
single = jnp.float32


def layer_shapes():
    return ((D, 3 * D), (D, D), (D, FF), (FF, D), (6, D))


def stem_shapes():
    return ((PIX, D), (SEQ, D), (4, D), (D, HID), (HID, HID), (HID, BOT))


def cut_flat(flat_row, shape_list):
    pieces = []
    offset = 0
    for shape_pair in shape_list:
        length = shape_pair[0] * shape_pair[1]
        pieces.append(flat_row[offset : offset + length].reshape(shape_pair))
        offset = offset + length
    return pieces


def pack_flat(grad_list, total_length):
    joined = jnp.concatenate([grad_item.reshape(-1) for grad_item in grad_list])
    return jnp.concatenate([joined, jnp.zeros((total_length - joined.shape[0],), single)])


def contract(form, left_arg, right_arg):
    return jnp.einsum(form, left_arg, right_arg, preferred_element_type=single)


def layer_norm(values, gain_row, bias_row):
    centred = values - jnp.mean(values, axis=-1, keepdims=True)
    spread = jnp.mean(centred * centred, axis=-1, keepdims=True)
    return centred * lax.rsqrt(spread + 1e-06) * gain_row + bias_row


def unit_rows(values):
    return values * lax.rsqrt(jnp.sum(values * values, axis=-1, keepdims=True) + 1e-06)


def gelu_back(pre_act, grad_act):
    return jax.vjp(jax.nn.gelu, pre_act)[1](grad_act)[0]


def block_forward(stream, weights):
    w_qkv, w_proj, w_up, w_down, vectors = weights
    vectors = vectors.astype(single)
    batch_size = stream.shape[0]
    normed = layer_norm(stream, vectors[0], vectors[1]).astype(narrow)
    packed = (
        contract("bsd,de->bse", normed, w_qkv)
        .astype(narrow)
        .reshape(batch_size, SEQ, 3, HEADS, HEAD_DIM)
    )
    scores = contract("bqhe,bkhe->bhqk", packed[:, :, 0], packed[:, :, 1]) * HEAD_DIM ** (-0.5)
    top_score = jnp.max(scores, axis=-1, keepdims=True)
    exp_terms = jnp.exp(scores - top_score)
    totals = jnp.sum(exp_terms, axis=-1, keepdims=True)
    log_total = top_score + jnp.log(totals)
    mixed = contract("bhqk,bkhe->bqhe", (exp_terms / totals).astype(narrow), packed[:, :, 2])
    mixed = mixed.astype(narrow).reshape(batch_size, SEQ, D)
    attn_out = contract("bsd,de->bse", mixed, w_proj)
    middle = stream + vectors[2] * attn_out
    normed_two = layer_norm(middle, vectors[3], vectors[4]).astype(narrow)
    pre_act = contract("bsd,df->bsf", normed_two, w_up)
    hidden = jax.nn.gelu(pre_act).astype(narrow)
    mlp_out = contract("bsf,fd->bsd", hidden, w_down)
    saved = (
        stream,
        normed,
        packed,
        log_total,
        mixed,
        attn_out,
        middle,
        normed_two,
        pre_act,
        hidden,
        mlp_out,
    )
    return (middle + vectors[5] * mlp_out, saved)


def block_backward(grad_out, weights, saved):
    w_qkv, w_proj, w_up, w_down, vectors = weights
    vectors = vectors.astype(single)
    (
        stream,
        normed,
        packed,
        log_total,
        mixed,
        attn_out,
        middle,
        normed_two,
        pre_act,
        hidden,
        mlp_out,
    ) = saved
    batch_size = stream.shape[0]
    score_scale = HEAD_DIM ** (-0.5)
    grad_ls_two = jnp.sum(grad_out * mlp_out, axis=(0, 1))
    grad_mlp = (grad_out * vectors[5]).astype(narrow)
    grad_down = contract("bsf,bsd->fd", hidden, grad_mlp)
    grad_pre = gelu_back(pre_act, contract("bsd,fd->bsf", grad_mlp, w_down)).astype(narrow)
    grad_up = contract("bsd,bsf->df", normed_two, grad_pre)
    grad_normed_two = contract("bsf,df->bsd", grad_pre, w_up)
    grad_mid, grad_gain_two, grad_bias_two = jax.vjp(layer_norm, middle, vectors[3], vectors[4])[1](
        grad_normed_two
    )
    grad_mid = grad_mid + grad_out
    grad_ls_one = jnp.sum(grad_mid * attn_out, axis=(0, 1))
    grad_attn = (grad_mid * vectors[2]).astype(narrow)
    grad_proj = contract("bsd,bse->de", mixed, grad_attn)
    grad_mixed = (
        contract("bse,de->bsd", grad_attn, w_proj)
        .astype(narrow)
        .reshape(batch_size, SEQ, HEADS, HEAD_DIM)
    )
    query_rows = packed[:, :, 0]
    key_rows = packed[:, :, 1]
    value_rows = packed[:, :, 2]
    probs = jnp.exp(contract("bqhe,bkhe->bhqk", query_rows, key_rows) * score_scale - log_total)
    grad_probs = contract("bqhe,bkhe->bhqk", grad_mixed, value_rows)
    grad_values = contract("bhqk,bqhe->bkhe", probs.astype(narrow), grad_mixed)
    grad_scores = probs * (grad_probs - jnp.sum(probs * grad_probs, axis=-1, keepdims=True))
    grad_raw = (grad_scores * score_scale).astype(narrow)
    grad_queries = contract("bhqk,bkhe->bqhe", grad_raw, key_rows)
    grad_keys = contract("bhqk,bqhe->bkhe", grad_raw, query_rows)
    grad_packed = (
        jnp.stack([grad_queries, grad_keys, grad_values], axis=2)
        .astype(narrow)
        .reshape(batch_size, SEQ, 3 * D)
    )
    grad_qkv = contract("bsd,bse->de", normed, grad_packed)
    grad_normed = contract("bse,de->bsd", grad_packed, w_qkv)
    grad_in, grad_gain_one, grad_bias_one = jax.vjp(layer_norm, stream, vectors[0], vectors[1])[1](
        grad_normed
    )
    grad_vectors = jnp.stack(
        [grad_gain_one, grad_bias_one, grad_ls_one, grad_gain_two, grad_bias_two, grad_ls_two]
    )
    return (grad_in + grad_mid, (grad_qkv, grad_proj, grad_up, grad_down, grad_vectors))


def embed(stem_parts, image_rows, masked_here, student):
    patch_w, position, extras, w_first, w_second, w_third = stem_parts
    extras = extras.astype(single)
    embedded = contract("gpc,cd->gpd", image_rows, patch_w)
    if student:
        embedded = jnp.where(masked_here[:, :, None], extras[1], embedded)
    cls_rows = jnp.broadcast_to(extras[0], (image_rows.shape[0], 1, D))
    return jnp.concatenate([cls_rows, embedded], axis=1) + position.astype(single)


def embed_backward(grad_stream, image_rows, masked_here):
    grad_cls = jnp.sum(grad_stream[:, 0], axis=0)
    grad_position = jnp.sum(grad_stream, axis=0)
    grad_patch_rows = grad_stream[:, 1:]
    grad_mask_token = jnp.sum(jnp.where(masked_here[:, :, None], grad_patch_rows, 0.0), axis=(0, 1))
    grad_embedded = jnp.where(masked_here[:, :, None], 0.0, grad_patch_rows).astype(narrow)
    grad_patch_w = contract("gpc,gpd->cd", image_rows, grad_embedded)
    return (grad_patch_w, grad_position, grad_cls, grad_mask_token)


def head_forward(stem_parts, proto_rows, stream, row_index):
    patch_w, position, extras, w_first, w_second, w_third = stem_parts
    extras = extras.astype(single)
    chosen = jnp.take_along_axis(stream, row_index[:, :, None], axis=1)
    normed = layer_norm(chosen, extras[2], extras[3]).astype(narrow)
    pre_one = contract("grd,dh->grh", normed, w_first)
    hidden_one = jax.nn.gelu(pre_one).astype(narrow)
    pre_two = contract("grh,hk->grk", hidden_one, w_second)
    hidden_two = jax.nn.gelu(pre_two).astype(narrow)
    bottleneck = contract("grh,hb->grb", hidden_two, w_third)
    unit_z = unit_rows(bottleneck).astype(narrow)
    unit_protos = unit_rows(proto_rows.astype(single)).astype(narrow)
    logits = contract("grb,kb->grk", unit_z, unit_protos)
    return (
        logits,
        (chosen, normed, pre_one, hidden_one, pre_two, hidden_two, bottleneck, unit_z, unit_protos),
    )


def head_backward(grad_logits, stem_parts, saved, row_index, stream_shape):
    patch_w, position, extras, w_first, w_second, w_third = stem_parts
    extras = extras.astype(single)
    chosen, normed, pre_one, hidden_one, pre_two, hidden_two, bottleneck, unit_z, unit_protos = (
        saved
    )
    grad_rounded = grad_logits.astype(narrow)
    grad_unit_z = contract("grk,kb->grb", grad_rounded, unit_protos)
    grad_unit_protos = contract("grk,grb->kb", grad_rounded, unit_z)
    grad_bottle = jax.vjp(unit_rows, bottleneck)[1](grad_unit_z)[0].astype(narrow)
    grad_third = contract("grh,grb->hb", hidden_two, grad_bottle)
    grad_pre_two = gelu_back(pre_two, contract("grb,hb->grh", grad_bottle, w_third)).astype(narrow)
    grad_second = contract("grh,grk->hk", hidden_one, grad_pre_two)
    grad_pre_one = gelu_back(pre_one, contract("grk,hk->grh", grad_pre_two, w_second)).astype(
        narrow
    )
    grad_first = contract("grd,grh->dh", normed, grad_pre_one)
    grad_normed = contract("grh,dh->grd", grad_pre_one, w_first)
    grad_chosen, grad_gain, grad_bias = jax.vjp(layer_norm, chosen, extras[2], extras[3])[1](
        grad_normed
    )
    image_index = jnp.arange(row_index.shape[0], dtype=jnp.int32)[:, None]
    grad_stream = jnp.zeros(stream_shape, single).at[image_index, row_index].add(grad_chosen)
    return (
        grad_stream,
        (grad_first, grad_second, grad_third),
        grad_gain,
        grad_bias,
        grad_unit_protos,
    )


def adam_update(weight, moment, second, grad, teacher):
    new_moment = beta_one * moment + (1.0 - beta_one) * grad
    new_second = beta_two * second + (1.0 - beta_two) * grad * grad
    direction = (
        new_moment
        / (1.0 - beta_one**STEP)
        / (jnp.sqrt(new_second / (1.0 - beta_two**STEP)) + adam_eps)
    )
    new_weight = weight - learn_rate * (direction + decay_rate * weight)
    return (
        new_moment,
        new_second,
        new_weight,
        new_weight.astype(narrow),
        teacher_keep * teacher + (1.0 - teacher_keep) * new_weight,
    )


def spread_local(
    patches,
    masked,
    slot_used,
    stem,
    stem_moment,
    stem_second,
    stem_teacher,
    layers,
    layer_moment,
    layer_second,
    layer_teacher,
    protos,
    proto_moment,
    proto_second,
    proto_teacher,
    centre,
):
    images_here = patches.shape[0]
    row_index = jnp.concatenate([jnp.zeros((images_here, 1), jnp.int32), masked + 1], axis=1)
    masked_here = jnp.any(
        masked[:, :, None] == jnp.arange(PATCHES, dtype=jnp.int32)[None, None, :], axis=1
    )
    kept = slot_used.astype(single)
    teacher_flat, teacher_protos = (
        lax.all_gather(stem_teacher.astype(narrow), "dev", axis=0, tiled=True),
        lax.all_gather(proto_teacher.astype(narrow), "dev", axis=0, tiled=True),
    )
    teacher_parts = cut_flat(teacher_flat, stem_shapes())
    stream = embed(teacher_parts, patches, masked_here, False)
    for layer_index in range(LAYERS):
        teacher_layer = lax.all_gather(
            layer_teacher[layer_index].astype(narrow), "dev", axis=0, tiled=True
        )
        stream = block_forward(stream, cut_flat(teacher_layer, layer_shapes()))[0]
    teacher_logits = head_forward(teacher_parts, teacher_protos, stream, row_index)[0]
    teacher_probs = jax.nn.softmax((teacher_logits - centre) / tau_teacher, axis=-1)
    centre_terms = jnp.sum(kept[:, None] * teacher_logits[:, 0], axis=0)
    student_flat, student_protos = (
        lax.all_gather(stem.astype(narrow), "dev", axis=0, tiled=True),
        lax.all_gather(protos.astype(narrow), "dev", axis=0, tiled=True),
    )
    student_parts = cut_flat(student_flat, stem_shapes())
    stream = embed(student_parts, patches, masked_here, True)
    saved_layers = []
    gathered_layers = []
    for layer_index in range(LAYERS):
        layer_flat = lax.all_gather(layers[layer_index].astype(narrow), "dev", axis=0, tiled=True)
        gathered_layers.append(layer_flat)
        stream, saved = block_forward(stream, cut_flat(layer_flat, layer_shapes()))
        saved_layers.append(saved)
    logits, head_saved = head_forward(student_parts, student_protos, stream, row_index)

    def loss_piece(logit_rows):
        log_probs = jax.nn.log_softmax(logit_rows / tau_student, axis=-1)
        cross = -jnp.sum(teacher_probs * log_probs, axis=-1)
        return jnp.sum(kept * (cross[:, 0] + jnp.mean(cross[:, 1:], axis=1)))

    loss_local, loss_puller = jax.vjp(loss_piece, logits)
    grad_logits = loss_puller(jnp.float32(1.0))[0]
    count_local = jnp.sum(kept)
    loss_total, count_total, centre_total = lax.psum((loss_local, count_local, centre_terms), "dev")
    back_flat, back_protos = (
        lax.all_gather(stem.astype(narrow), "dev", axis=0, tiled=True),
        lax.all_gather(protos.astype(narrow), "dev", axis=0, tiled=True),
    )
    back_parts = cut_flat(back_flat, stem_shapes())
    grad_stream, head_grads, grad_gain, grad_bias, grad_unit_protos = head_backward(
        grad_logits, back_parts, head_saved, row_index, stream.shape
    )
    layer_grads = []
    for layer_index in reversed(range(LAYERS)):
        weight_flat = lax.all_gather(layers[layer_index].astype(narrow), "dev", axis=0, tiled=True)
        grad_stream, block_grads = block_backward(
            grad_stream, cut_flat(weight_flat, layer_shapes()), saved_layers[layer_index]
        )
        layer_grads.insert(
            0,
            lax.psum_scatter(
                pack_flat(block_grads, weight_flat.shape[0]), "dev", scatter_dimension=0, tiled=True
            ),
        )
    grad_patch_w, grad_position, grad_cls, grad_mask_token = embed_backward(
        grad_stream, patches, masked_here
    )
    grad_extras = jnp.stack([grad_cls, grad_mask_token, grad_gain, grad_bias])
    stem_flat_grad = pack_flat(
        (grad_patch_w, grad_position, grad_extras) + head_grads, back_flat.shape[0]
    )
    stem_grad, proto_row_grad = (
        lax.psum_scatter(stem_flat_grad, "dev", scatter_dimension=0, tiled=True),
        lax.psum_scatter(grad_unit_protos, "dev", scatter_dimension=0, tiled=True),
    )
    own_protos = lax.optimization_barrier(protos.astype(narrow)).astype(single)
    proto_grad = jax.vjp(unit_rows, own_protos)[1](proto_row_grad)[0]
    layer_grad = jnp.stack(layer_grads)
    square_local = (
        jnp.sum(stem_grad * stem_grad)
        + jnp.sum(layer_grad * layer_grad)
        + jnp.sum(proto_grad * proto_grad)
    )
    square_total = lax.psum(square_local, "dev")
    grad_norm = jnp.sqrt(square_total) / count_total
    factor = jnp.minimum(1.0, clip_limit / (grad_norm + 1e-06)) / count_total
    new_centre = centre_keep * centre + (1.0 - centre_keep) * centre_total / count_total
    stem_set = adam_update(stem, stem_moment, stem_second, stem_grad * factor, stem_teacher)
    layer_set = adam_update(layers, layer_moment, layer_second, layer_grad * factor, layer_teacher)
    proto_set = adam_update(protos, proto_moment, proto_second, proto_grad * factor, proto_teacher)
    return (
        loss_total,
        count_total,
        grad_norm,
        new_centre,
        stem_set[0],
        stem_set[1],
        stem_set[2],
        stem_set[3],
        stem_set[4],
        layer_set[0],
        layer_set[1],
        layer_set[2],
        layer_set[3],
        layer_set[4],
        proto_set[0],
        proto_set[1],
        proto_set[2],
        proto_set[3],
        proto_set[4],
    )


GROUP = 16
ROW = HID
MATRIX_ROWS = D * 3 + D + FF + FF
EMBED_ROWS = PIX + SEQ + 4
EMBED_FLAT = EMBED_ROWS * D
HEAD_ROWS = D + HID + BOT
BITS = ("b", "a", "y", "x", "c")
MASKS = {"c": 1, "x": 2, "y": 4, "a": 8, "b": 24, "g": 8}


def head_bounds(count, stem_piece):
    bounds = [-(-(stem_piece * device - EMBED_FLAT) // (ROW * GROUP)) * GROUP for device in range(count + 1)]
    bounds[0] = -(-EMBED_FLAT // (ROW * GROUP)) * -GROUP
    bounds[-1] = HEAD_ROWS
    return bounds


def fits(count, stem_piece, layer_piece):
    if count != 1 << len(BITS) or MATRIX_ROWS % (3 * count):
        return False
    bounds = head_bounds(count, stem_piece)
    sizes = [bounds[i + 1] - bounds[i] for i in range(count)]
    return (
        min(sizes) > GROUP
        and bounds[1] <= 0
        and stem_piece < EMBED_FLAT <= 2 * stem_piece
        and D in bounds
        and D + HID in bounds
        and stem_piece * count == EMBED_FLAT + HEAD_ROWS * ROW
    )


def pairs(count, mask):
    return [(i, i ^ mask) for i in range(count)]


def bit_flags(me):
    flags = {name: (me >> (len(BITS) - 1 - place)) & 1 for place, name in enumerate(BITS)}
    flags["g"] = flags["a"] ^ flags["b"]
    return flags


def cube_gather(part, order):
    count = 1 << len(BITS)
    flags = bit_flags(lax.axis_index("dev"))
    held = part[None]
    for name in order:
        got = lax.ppermute(held, "dev", pairs(count, MASKS[name]))
        held = jnp.where(
            flags[name] == 1,
            jnp.concatenate([got, held], axis=0),
            jnp.concatenate([held, got], axis=0),
        )
    return held


def cut(array, names, name, lead):
    flag = bit_flags(lax.axis_index("dev"))[name] == 1
    place = names.index(name) + lead
    low = lax.index_in_dim(array, 0, place, keepdims=False)
    high = lax.index_in_dim(array, 1, place, keepdims=False)
    sent = jnp.where(flag, low, high)
    return (sent if name == "c" else sent.astype(narrow)), jnp.where(flag, high, low), names.replace(name, "")


def move(sent, kept, name):
    return kept + lax.ppermute(sent, "dev", pairs(1 << len(BITS), MASKS[name])).astype(single)


def cube_scatter(array, names, order, lead=0):
    for name in order:
        sent, kept, names = cut(array, names, name, lead)
        array = move(sent, kept, name)
    return array


def cube_sum(values):
    for name in "cxyab":
        values = values + lax.ppermute(values, "dev", pairs(1 << len(BITS), MASKS[name]))
    return values


def split_bits(array, lead=0):
    return array.reshape(array.shape[:lead] + (2,) * len(BITS) + array.shape[lead + 1 :])


def step_pairs(count, step):
    return [(i, i + step) for i in range(count) if 0 <= i + step < count]


def lane_rows(length):
    return -(-length // 1024) * 8


def as_lanes(flat):
    rows = lane_rows(flat.shape[-1])
    gap = rows * 128 - flat.shape[-1]
    padded = jnp.pad(flat, [(0, 0)] * (flat.ndim - 1) + [(0, gap)])
    return padded.reshape(flat.shape[:-1] + (rows, 128))


def shifted(line_ref, row, lane, first, rows, stride):
    spots = lax.broadcasted_iota(jnp.int32, (rows, 128), 1)
    turn = lax.rem(128 - lane, 128)
    here = pltpu.roll(line_ref[pl.ds(row + first, rows, stride=stride), :], turn, 1)
    there = pltpu.roll(line_ref[pl.ds(row + first + 1, rows, stride=stride), :], turn, 1)
    return jnp.where(spots < 128 - lane, here, there)


def blocks_kernel(
    shape,
    place_ref,
    stem_ref,
    after_ref,
    layer_ref,
    before_ref,
    head_ref,
    block_ref,
    embed_ref,
    vector_ref,
    line_ref,
    flat_ref,
):
    front, stem_piece, layer_piece, tail = shape
    stem_lines = stem_ref.shape[1]
    end_row, end_lane = stem_piece // 128, stem_piece % 128
    after_lines = after_ref.shape[1]
    slot = head_ref.shape[1]
    for model in range(2):
        line_ref[pl.ds(0, front), :] = jnp.zeros((front, 128), single)
        line_ref[pl.ds(front, end_row), :] = stem_ref[model, pl.ds(0, end_row), :]
        turned = pltpu.roll(after_ref[model], end_lane, 1)
        spots = lax.broadcasted_iota(jnp.int32, (after_lines, 128), 1)
        line_ref[pl.ds(front + end_row, after_lines), :] = turned
        line_ref[pl.ds(front + end_row + after_lines, 128), :] = jnp.zeros((128, 128), single)
        lower = pltpu.roll(turned, 1, 0)
        first_line = jnp.broadcast_to(stem_ref[model, pl.ds(end_row, 1), :], (after_lines, 128))
        number = lax.broadcasted_iota(jnp.int32, (after_lines, 128), 0)
        lower = jnp.where(number == 0, first_line, lower)
        line_ref[pl.ds(front + end_row, after_lines), :] = jnp.where(spots < end_lane, lower, turned)
        per_row = ROW // 128
        for chunk in range(per_row):
            head_ref[model, :, pl.ds(chunk * 128, 128)] = shifted(
                line_ref, place_ref[0], place_ref[1], chunk, slot, per_row
            ).astype(narrow)
        for chunk in range(D // 128):
            embed_ref[model, :, pl.ds(chunk * 128, 128)] = shifted(
                line_ref, place_ref[2], place_ref[3], chunk, embed_ref.shape[1], D // 128
            ).astype(narrow)
    tail_lines = tail // 128
    layer_lines = layer_ref.shape[1]
    vector_at = tail + layer_piece - tail
    for part in range(layer_ref.shape[0]):
        flat_ref[pl.ds(0, tail_lines), :] = before_ref[part]
        flat_ref[pl.ds(tail_lines, layer_lines), :] = layer_ref[part]
        for chunk in range(D // 128):
            block_ref[part, :, pl.ds(chunk * 128, 128)] = shifted(
                flat_ref, place_ref[4], place_ref[5], chunk, block_ref.shape[1], D // 128
            ).astype(narrow)
            vector_ref[part, :, pl.ds(chunk * 128, 128)] = shifted(
                flat_ref, vector_at // 128, vector_at % 128, chunk, 8, D // 128
            ).astype(narrow)


def own_blocks(place, stems, after, layer_rows, before, shape, slot, block_rows, embed_rows):
    front, stem_piece, layer_piece, tail = shape
    lines = front + stem_piece // 128 + after.shape[1] + slot * ROW // 128
    flats = tail // 128 + layer_rows.shape[1] + 48
    return pl.pallas_call(
        lambda *refs: blocks_kernel(shape, *refs),
        out_shape=[
            jax.ShapeDtypeStruct((2, slot, ROW), narrow),
            jax.ShapeDtypeStruct((2 * LAYERS, block_rows, D), narrow),
            jax.ShapeDtypeStruct((2, embed_rows, D), narrow),
            jax.ShapeDtypeStruct((2 * LAYERS, 8, D), narrow),
        ],
        in_specs=[pl.BlockSpec(memory_space=pltpu.SMEM)] + [pl.BlockSpec(memory_space=pltpu.VMEM)] * 4,
        out_specs=[pl.BlockSpec(memory_space=pltpu.VMEM)] * 4,
        scratch_shapes=[pltpu.VMEM((lines, 128), single), pltpu.VMEM((flats, 128), single)],
        compiler_params=pltpu.CompilerParams(vmem_limit_bytes=40 << 20),
    )(place, stems, after, layer_rows, before)


def shards_kernel(place_ref, head_ref, previous_ref, block_ref, behind_ref, stem_ref, layer_ref, line_ref, flat_ref):
    per_row = ROW // 128
    extra = previous_ref.shape[0]
    slot = head_ref.shape[0]
    for chunk in range(per_row):
        spot = pl.ds(chunk * 128, 128)
        line_ref[pl.ds(chunk, extra, stride=per_row), :] = previous_ref[:, spot]
        line_ref[pl.ds(extra * per_row + chunk, slot, stride=per_row), :] = head_ref[:, spot]
    stem_ref[...] = shifted(line_ref, place_ref[0], place_ref[1], 0, stem_ref.shape[0], 1)
    per_row = D // 128
    rows = block_ref.shape[2]
    for part in range(block_ref.shape[0]):
        for chunk in range(per_row):
            flat_ref[pl.ds(chunk, rows, stride=per_row), :] = block_ref[part, chunk]
            flat_ref[pl.ds(rows * per_row + chunk, 6, stride=per_row), :] = behind_ref[part, chunk]
        layer_ref[part] = shifted(flat_ref, place_ref[2], place_ref[3], 0, layer_ref.shape[1], 1)


def own_shards(place, head_grad, previous, block_grad, behind, stem_lines, layer_lines):
    per_row = ROW // 128
    lines = (head_grad.shape[0] + previous.shape[0]) * per_row + 256
    flats = max(block_grad.shape[2] * 3 + 18, layer_lines + 18) + 16
    return pl.pallas_call(
        shards_kernel,
        out_shape=[
            jax.ShapeDtypeStruct((stem_lines, 128), single),
            jax.ShapeDtypeStruct((block_grad.shape[0], layer_lines, 128), single),
        ],
        in_specs=[pl.BlockSpec(memory_space=pltpu.SMEM)] + [pl.BlockSpec(memory_space=pltpu.VMEM)] * 4,
        out_specs=[pl.BlockSpec(memory_space=pltpu.VMEM)] * 2,
        scratch_shapes=[pltpu.VMEM((lines, 128), single), pltpu.VMEM((flats, 128), single)],
        compiler_params=pltpu.CompilerParams(vmem_limit_bytes=40 << 20),
    )(place, head_grad, previous, block_grad, behind)


PAD_SEQ = 272
GELU_SCALE = 0.7978845608028654
GELU_CUBE = 0.044715


def product_plain(left, right):
    return lax.dot_general(left, right, (((1,), (0,)), ((), ())), preferred_element_type=single)


def product_right(left, right):
    return lax.dot_general(left, right, (((1,), (1,)), ((), ())), preferred_element_type=single)


def product_left(left, right):
    return lax.dot_general(left, right, (((0,), (0,)), ((), ())), preferred_element_type=single)


def norm_parts(values):
    centred = values - jnp.mean(values, axis=-1, keepdims=True)
    spread = lax.rsqrt(jnp.mean(centred * centred, axis=-1, keepdims=True) + 1e-06)
    return centred * spread, spread


def norm_back(grad, unit, spread, gain):
    grad_unit = grad * gain
    mean_one = jnp.mean(grad_unit, axis=-1, keepdims=True)
    mean_two = jnp.mean(grad_unit * unit, axis=-1, keepdims=True)
    return spread * (grad_unit - mean_one - unit * mean_two)


def gelu_tanh(values):
    return jnp.tanh(GELU_SCALE * (values + GELU_CUBE * values * values * values))


def gelu_value(values):
    return 0.5 * values * (1.0 + gelu_tanh(values))


def gelu_slope(values):
    bent = gelu_tanh(values)
    return 0.5 * (1.0 + bent) + 0.5 * values * (1.0 - bent * bent) * GELU_SCALE * (
        1.0 + 3.0 * GELU_CUBE * values * values
    )


def head_copies(plan, side_ref, gathered_ref, one_ref, two_ref, lines_ref, sems):
    quarter = gathered_ref.shape[0] // 2
    shift = side_ref[0] * quarter
    targets = (one_ref, two_ref, lines_ref)
    copies = []
    for number, (at, owner, first, rows, target, row) in enumerate(plan):
        spot = at + shift if at < quarter else at - shift
        copies.append(
            pltpu.make_async_copy(
                gathered_ref.at[spot, owner, pl.ds(first, rows)],
                targets[target].at[pl.ds(row, rows)],
                sems.at[number],
            )
        )
    for copy in copies:
        copy.start()
    return [[copy for copy, item in zip(copies, plan) if item[4] == target] for target in range(3)]


def wait_all(copies):
    for copy in copies:
        copy.wait()


def spread_third(lines_ref, wide_ref, third_ref):
    groups = ROW // BOT
    for lane in range(BOT // 128):
        for group in range(groups):
            at = group * BOT + lane * 128
            wide_ref[lane, pl.ds(group, lines_ref.shape[0], stride=groups), :] = lines_ref[
                :, at : at + 128
            ].astype(single)
        third_ref[:, pl.ds(lane * 128, 128)] = wide_ref[lane].astype(narrow)


def head_up_kernel(
    plan, side_ref, normed_ref, gathered_ref, unit_ref, acts_ref, bottle_ref, pre_one_ref, pre_two_ref,
    one_ref, two_ref, lines_ref, wide_ref, third_ref, sems,
):
    copies = head_copies(plan, side_ref, gathered_ref, one_ref, two_ref, lines_ref, sems)
    acts_ref[...] = jnp.zeros_like(acts_ref)
    normed = normed_ref[...]
    acts_ref[:, pl.ds(0, D)] = normed
    piece = HID // 4
    wait_all(copies[0])
    for number in range(4):
        spot = pl.ds(number * piece, piece)
        pre = product_plain(normed, one_ref[:, spot])
        pre_one_ref[:, spot] = pre
        acts_ref[:, pl.ds(D + number * piece, piece)] = gelu_value(pre).astype(narrow)
    wait_all(copies[2])
    spread_third(lines_ref, wide_ref, third_ref)
    wait_all(copies[1])
    hidden = acts_ref[:, pl.ds(D, HID)]
    for number in range(4):
        spot = pl.ds(number * piece, piece)
        pre = product_plain(hidden, two_ref[:, spot])
        pre_two_ref[:, spot] = pre
        acts_ref[:, pl.ds(D + HID + number * piece, piece)] = gelu_value(pre).astype(narrow)
    bottle = product_plain(acts_ref[:, pl.ds(D + HID, HID)], third_ref[...])
    bottle_ref[...] = bottle
    unit_ref[...] = (
        bottle * lax.rsqrt(jnp.sum(bottle * bottle, axis=-1, keepdims=True) + 1e-06)
    ).astype(narrow)


def head_down_kernel(
    plan, side_ref, grad_ref, bottle_ref, pre_one_ref, pre_two_ref, gathered_ref, grads_ref, normed_grad_ref,
    one_ref, two_ref, lines_ref, wide_ref, third_ref, sems,
):
    copies = head_copies(plan, side_ref, gathered_ref, one_ref, two_ref, lines_ref, sems)
    grad, bottle = grad_ref[...], bottle_ref[...]
    scale = lax.rsqrt(jnp.sum(bottle * bottle, axis=-1, keepdims=True) + 1e-06)
    along = jnp.sum(grad * bottle, axis=-1, keepdims=True)
    grad_bottle = (scale * (grad - bottle * (along * scale * scale))).astype(narrow)
    grads_ref[:, pl.ds(2 * HID, BOT)] = grad_bottle
    wait_all(copies[2])
    spread_third(lines_ref, wide_ref, third_ref)
    piece = HID // 4
    for number in range(4):
        spot = pl.ds(number * piece, piece)
        back = product_right(grad_bottle, third_ref[spot, :])
        grads_ref[:, pl.ds(HID + number * piece, piece)] = (back * gelu_slope(pre_two_ref[:, spot])).astype(narrow)
    wait_all(copies[1])
    grad_two = grads_ref[:, pl.ds(HID, HID)]
    for number in range(4):
        spot = pl.ds(number * piece, piece)
        back = product_right(grad_two, two_ref[spot, :])
        grads_ref[:, spot] = (back * gelu_slope(pre_one_ref[:, spot])).astype(narrow)
    wait_all(copies[0])
    normed_grad_ref[...] = product_right(grads_ref[:, pl.ds(0, HID)], one_ref[...])


def head_pass(kernel, plan, side, inputs, gathered, shapes, waits=()):
    read = len(inputs) + 2
    return pl.pallas_call(
        lambda *refs: kernel(plan, *refs[:read], *refs[read + len(waits) :]),
        out_shape=shapes,
        in_specs=[pl.BlockSpec(memory_space=pltpu.SMEM)]
        + [pl.BlockSpec(memory_space=pltpu.VMEM)] * len(inputs)
        + [pl.BlockSpec(memory_space=pl.ANY)] * (1 + len(waits)),
        out_specs=[pl.BlockSpec(memory_space=pltpu.VMEM)] * len(shapes),
        scratch_shapes=[
            pltpu.VMEM((D, HID), narrow),
            pltpu.VMEM((HID, HID), narrow),
            pltpu.VMEM((BOT, ROW), narrow),
            pltpu.VMEM((BOT // 128, HID, 128), single),
            pltpu.VMEM((HID, BOT), narrow),
            pltpu.SemaphoreType.DMA((len(plan),)),
        ],
        compiler_params=pltpu.CompilerParams(vmem_limit_bytes=56 << 20),
        cost_estimate=pl.CostEstimate(flops=100 * 10**6, bytes_accessed=370 * 10**5, transcendentals=0),
    )(side, *inputs, gathered, *waits)


def fetch_rows(side_ref, part, gathered_ref, flat_ref, sems):
    quarter = flat_ref.shape[0] // 4
    side = side_ref[0]
    first, second = side * quarter, (1 - side) * quarter
    copies = [
        pltpu.make_async_copy(
            gathered_ref.at[pl.ds(at, quarter), owner, part],
            flat_ref.at[pl.ds(spot * quarter, quarter)],
            sems.at[spot],
        )
        for spot, (at, owner) in enumerate(((first, 0), (second, 0), (second, 1), (first, 1)))
    ]
    for copy in copies:
        copy.start()
    for copy in copies:
        copy.wait()


def matrix_rows(flat_ref, first_row, length):
    rows = flat_ref.shape[1]
    low, high = first_row // rows, -(-(first_row + length) // rows)
    lines = flat_ref[pl.ds(low, high - low)].reshape((high - low) * rows, D)
    at = first_row - low * rows
    return lines[at : at + length]


def spread_columns(flat_ref, first_row, width, wide_ref, out_ref):
    length = width * D
    lines = matrix_rows(flat_ref, first_row, length)
    for column in range(D // 128):
        lane = slice(column * 128, (column + 1) * 128)
        wide_ref[column, pl.ds(0, length), :] = lines[:, lane].astype(single)
    for group in range(width):
        for column in range(D // 128):
            out_ref[group, :, pl.ds(column * 128, 128)] = wide_ref[
                column, pl.ds(group, D, stride=width), :
            ].astype(narrow)


def head_lanes(values, odd):
    lanes = lax.broadcasted_iota(jnp.int32, values.shape, 1)
    return jnp.where((lanes >= HEAD_DIM) == odd, values, jnp.zeros_like(values))


def join_lanes(even, odd):
    lanes = lax.broadcasted_iota(jnp.int32, even.shape, 1)
    return jnp.where(lanes >= HEAD_DIM, odd, even)


def soft_rows(query, key):
    scores = product_right(query, key) * HEAD_DIM ** (-0.5)
    spots = lax.broadcasted_iota(jnp.int32, scores.shape, 1)
    scores = jnp.where(spots < SEQ, scores, -1e30)
    terms = jnp.exp(scores - jnp.max(scores, axis=-1, keepdims=True))
    return terms / jnp.sum(terms, axis=-1, keepdims=True)


def forward_kernel(part, keep, side_ref, stream_ref, vector_ref, gathered_ref, *refs):
    out_ref = refs[0]
    if keep:
        packed_ref, mixed_ref, attn_ref, pre_ref, mlp_ref = refs[1:6]
        flat_ref, wide_ref, qkv_ref, up_ref, hidden_ref, sems = refs[6:]
    else:
        flat_ref, wide_ref, qkv_ref, up_ref, hidden_ref, packed_ref, mixed_ref, sems = refs[1:]
    fetch_rows(side_ref, part, gathered_ref, flat_ref, sems)
    spread_columns(flat_ref, 0, 3, wide_ref, qkv_ref)
    spread_columns(flat_ref, 4 * D, FF // D, wide_ref, up_ref)
    w_proj = matrix_rows(flat_ref, 3 * D, D)
    w_down = matrix_rows(flat_ref, 4 * D + FF, FF)
    vectors = vector_ref[...].astype(single)
    stream = stream_ref[...]
    normed = (norm_parts(stream)[0] * vectors[0:1] + vectors[1:2]).astype(narrow)
    for group in range(3):
        packed_ref[:, pl.ds(group * D, D)] = product_plain(normed, qkv_ref[group]).astype(narrow)
    for image in range(stream.shape[0] // PAD_SEQ):
        rows = pl.ds(image * PAD_SEQ, PAD_SEQ)
        for pair in range(HEADS // 2):
            query, key, value = [
                packed_ref[rows, pl.ds(group * D + pair * 128, 128)] for group in range(3)
            ]
            done = [
                product_plain(soft_rows(head_lanes(query, odd), key).astype(narrow), value)
                for odd in (False, True)
            ]
            mixed_ref[rows, pl.ds(pair * 128, 128)] = join_lanes(*done).astype(narrow)
    attn = product_plain(mixed_ref[...], w_proj)
    middle = stream + vectors[2:3] * attn
    normed_two = (norm_parts(middle)[0] * vectors[3:4] + vectors[4:5]).astype(narrow)
    for group in range(FF // D):
        spot = pl.ds(group * D, D)
        pre = product_plain(normed_two, up_ref[group])
        if keep:
            pre_ref[:, spot] = pre
        hidden_ref[:, spot] = (0.5 * pre * (1.0 + gelu_tanh(pre))).astype(narrow)
    mlp = product_plain(hidden_ref[...], w_down)
    out_ref[...] = middle + vectors[5:6] * mlp
    if keep:
        attn_ref[...] = attn
        mlp_ref[...] = mlp


def layer_scratch(gathered):
    rows, blocks = gathered.shape[3], 2 * gathered.shape[0]
    return [
        pltpu.VMEM((blocks, rows, D), narrow),
        pltpu.VMEM((D // 128, FF, 128), single),
        pltpu.VMEM((3, D, D), narrow),
        pltpu.VMEM((FF // D, D, D), narrow),
    ]


def layer_specs_in(count):
    return (
        [pl.BlockSpec(memory_space=pltpu.SMEM)]
        + [pl.BlockSpec(memory_space=pltpu.VMEM)] * (count - 2)
        + [pl.BlockSpec(memory_space=pl.ANY)]
    )


def layer_forward(side, stream, vectors, gathered, part, keep):
    tokens = stream.shape[0]
    shapes = [jax.ShapeDtypeStruct((tokens, D), single)]
    extra = [
        jax.ShapeDtypeStruct((tokens, 3 * D), narrow),
        jax.ShapeDtypeStruct((tokens, D), narrow),
        jax.ShapeDtypeStruct((tokens, D), single),
        jax.ShapeDtypeStruct((tokens, FF), single),
        jax.ShapeDtypeStruct((tokens, D), single),
    ]
    scratch = layer_scratch(gathered) + [pltpu.VMEM((tokens, FF), narrow)]
    if keep:
        shapes = shapes + extra
    else:
        scratch = scratch + [pltpu.VMEM((tokens, 3 * D), narrow), pltpu.VMEM((tokens, D), narrow)]
    scratch.append(pltpu.SemaphoreType.DMA((4,)))
    return pl.pallas_call(
        lambda *refs: forward_kernel(part, keep, *refs),
        out_shape=shapes,
        in_specs=layer_specs_in(4),
        out_specs=[pl.BlockSpec(memory_space=pltpu.VMEM)] * len(shapes),
        scratch_shapes=scratch,
        compiler_params=pltpu.CompilerParams(vmem_limit_bytes=56 << 20),
        cost_estimate=pl.CostEstimate(flops=100 * 10**6, bytes_accessed=430 * 10**5, transcendentals=0),
    )(side, stream, vectors, gathered)


def mlp_back_kernel(
    part,
    side_ref,
    grad_ref,
    stream_ref,
    attn_ref,
    pre_ref,
    mlp_ref,
    vector_ref,
    gathered_ref,
    *refs,
):
    grad_mid_ref, weight_grad_ref, vector_grad_ref = refs[-9:-6]
    flat_ref, wide_ref, up_ref, hidden_ref, grad_pre_ref, sems = refs[-6:]
    lead = weight_grad_ref.shape[1] - 2 * FF
    weight_grad_ref[:, pl.ds(0, lead), :] = jnp.zeros((D // 128, lead, 128), single)
    fetch_rows(side_ref, part, gathered_ref, flat_ref, sems)
    spread_columns(flat_ref, 4 * D, FF // D, wide_ref, up_ref)
    w_down = matrix_rows(flat_ref, 4 * D + FF, FF)
    vectors = vector_ref[...].astype(single)
    grad_out = grad_ref[...]
    vector_grad_ref[...] = jnp.zeros_like(vector_grad_ref)
    attn = attn_ref[...]
    middle = stream_ref[...] + vectors[2:3] * attn
    unit_two, spread_two = norm_parts(middle)
    normed_two = (unit_two * vectors[3:4] + vectors[4:5]).astype(narrow)
    vector_grad_ref[pl.ds(5, 1), :] = jnp.sum(grad_out * mlp_ref[...], axis=0, keepdims=True)
    grad_mlp = (grad_out * vectors[5:6]).astype(narrow)
    grad_normed_two = jnp.zeros_like(grad_out)
    for group in range(FF // D):
        spot = pl.ds(group * D, D)
        pre = pre_ref[:, spot]
        bent = gelu_tanh(pre)
        hidden_ref[:, spot] = (0.5 * pre * (1.0 + bent)).astype(narrow)
        slope = 0.5 * (1.0 + bent) + 0.5 * pre * (1.0 - bent * bent) * GELU_SCALE * (
            1.0 + 3.0 * GELU_CUBE * pre * pre
        )
        grad_hidden = product_right(grad_mlp, w_down[group * D : (group + 1) * D])
        grad_pre = (grad_hidden * slope).astype(narrow)
        grad_pre_ref[:, spot] = grad_pre
        grad_normed_two = grad_normed_two + product_right(grad_pre, up_ref[group])
    for group in range(FF // D):
        spot = pl.ds(group * D, D)
        up_grad = product_left(normed_two, grad_pre_ref[:, spot])
        down_grad = product_left(hidden_ref[:, spot], grad_mlp)
        for column in range(D // 128):
            lane = slice(column * 128, (column + 1) * 128)
            weight_grad_ref[column, pl.ds(lead + group, D, stride=FF // D), :] = up_grad[:, lane]
            weight_grad_ref[column, pl.ds(lead + FF + group * D, D), :] = down_grad[:, lane]
    vector_grad_ref[pl.ds(3, 1), :] = jnp.sum(grad_normed_two * unit_two, axis=0, keepdims=True)
    vector_grad_ref[pl.ds(4, 1), :] = jnp.sum(grad_normed_two, axis=0, keepdims=True)
    grad_mid = grad_out + norm_back(grad_normed_two, unit_two, spread_two, vectors[3:4])
    vector_grad_ref[pl.ds(2, 1), :] = jnp.sum(grad_mid * attn, axis=0, keepdims=True)
    grad_mid_ref[...] = grad_mid


def attention_back_kernel(
    part,
    side_ref,
    grad_ref,
    stream_ref,
    packed_ref,
    mixed_ref,
    vector_ref,
    gathered_ref,
    *refs,
):
    grad_in_ref, weight_grad_ref, vector_grad_ref = refs[-9:-6]
    flat_ref, wide_ref, qkv_ref, grad_mixed_ref, grad_packed_ref, sems = refs[-6:]
    rest = weight_grad_ref.shape[1] - 4 * D
    weight_grad_ref[:, pl.ds(4 * D, rest), :] = jnp.zeros((D // 128, rest, 128), single)
    fetch_rows(side_ref, part, gathered_ref, flat_ref, sems)
    spread_columns(flat_ref, 0, 3, wide_ref, qkv_ref)
    w_proj = matrix_rows(flat_ref, 3 * D, D)
    vectors = vector_ref[...].astype(single)
    vector_grad_ref[...] = jnp.zeros_like(vector_grad_ref)
    grad_mid = grad_ref[...]
    stream = stream_ref[...]
    grad_attn = (grad_mid * vectors[2:3]).astype(narrow)
    proj_grad = product_left(mixed_ref[...], grad_attn)
    for column in range(D // 128):
        weight_grad_ref[column, pl.ds(3 * D, D), :] = proj_grad[:, column * 128 : (column + 1) * 128]
    grad_mixed_ref[...] = product_right(grad_attn, w_proj).astype(narrow)
    for image in range(stream.shape[0] // PAD_SEQ):
        rows = pl.ds(image * PAD_SEQ, PAD_SEQ)
        for pair in range(HEADS // 2):
            query, key, value = [
                packed_ref[rows, pl.ds(group * D + pair * 128, 128)] for group in range(3)
            ]
            grad_mixed = grad_mixed_ref[rows, pl.ds(pair * 128, 128)]
            parts = []
            for odd in (False, True):
                probs = soft_rows(head_lanes(query, odd), key)
                grad_probs = product_right(head_lanes(grad_mixed, odd), value)
                grad_value = product_left(probs.astype(narrow), grad_mixed)
                grad_scores = probs * (grad_probs - jnp.sum(probs * grad_probs, axis=-1, keepdims=True))
                grad_raw = (grad_scores * HEAD_DIM ** (-0.5)).astype(narrow)
                parts.append((product_plain(grad_raw, key), product_left(grad_raw, query), grad_value))
            for group in range(3):
                grad_packed_ref[rows, pl.ds(group * D + pair * 128, 128)] = join_lanes(
                    parts[0][group], parts[1][group]
                ).astype(narrow)
    unit_one, spread_one = norm_parts(stream)
    normed = (unit_one * vectors[0:1] + vectors[1:2]).astype(narrow)
    grad_normed = jnp.zeros_like(grad_mid)
    for group in range(3):
        grad_part = grad_packed_ref[:, pl.ds(group * D, D)]
        grad_normed = grad_normed + product_right(grad_part, qkv_ref[group])
        qkv_grad = product_left(normed, grad_part)
        for column in range(D // 128):
            lane = slice(column * 128, (column + 1) * 128)
            weight_grad_ref[column, pl.ds(group, D, stride=3), :] = qkv_grad[:, lane]
    vector_grad_ref[pl.ds(0, 1), :] = jnp.sum(grad_normed * unit_one, axis=0, keepdims=True)
    vector_grad_ref[pl.ds(1, 1), :] = jnp.sum(grad_normed, axis=0, keepdims=True)
    grad_in_ref[...] = grad_mid + norm_back(grad_normed, unit_one, spread_one, vectors[0:1])


def layer_back(kernel, part, weight_rows, side, inputs, vectors, gathered, waits, columns, buffers):
    tokens = inputs[0].shape[0]
    rows, blocks = gathered.shape[3], 2 * gathered.shape[0]
    return pl.pallas_call(
        lambda *refs: kernel(part, *refs),
        out_shape=[
            jax.ShapeDtypeStruct((tokens, D), single),
            jax.ShapeDtypeStruct((D // 128, weight_rows, 128), single),
            jax.ShapeDtypeStruct((8, D), single),
        ],
        in_specs=layer_specs_in(len(inputs) + 3) + [pl.BlockSpec(memory_space=pl.ANY)] * len(waits),
        out_specs=[pl.BlockSpec(memory_space=pltpu.VMEM)] * 3,
        scratch_shapes=[
            pltpu.VMEM((blocks, rows, D), narrow),
            pltpu.VMEM((D // 128, columns * D, 128), single),
            pltpu.VMEM((columns, D, D), narrow),
        ]
        + [pltpu.VMEM((tokens, width), narrow) for width in buffers]
        + [pltpu.SemaphoreType.DMA((4,))],
        compiler_params=pltpu.CompilerParams(vmem_limit_bytes=56 << 20),
        cost_estimate=pl.CostEstimate(flops=100 * 10**6, bytes_accessed=600 * 10**5, transcendentals=0),
    )(side, *inputs, vectors, gathered, *waits)


def pair_rows_of(block_rows):
    pair = 2 * block_rows
    return 4 * D // pair * pair, -(-4 * D // pair) * pair


def mlp_back(side, grad_out, saved, vectors, gathered, part, waits):
    stream, packed, mixed, attn, pre, mlp = saved
    return layer_back(
        mlp_back_kernel, part, MATRIX_ROWS - pair_rows_of(gathered.shape[3])[0], side,
        (grad_out, stream, attn, pre, mlp), vectors, gathered, waits,
        FF // D, (FF, FF),
    )


def attention_back(side, grad_mid, saved, vectors, gathered, part, waits):
    stream, packed, mixed, attn, pre, mlp = saved
    return layer_back(
        attention_back_kernel, part, pair_rows_of(gathered.shape[3])[1], side,
        (grad_mid, stream, packed, mixed), vectors, gathered, waits,
        3, (D, 3 * D),
    )


def after(value, *tokens):
    def kernel(*refs):
        refs[-1][...] = refs[0][...]

    return pl.pallas_call(
        kernel,
        out_shape=jax.ShapeDtypeStruct(value.shape, value.dtype),
        in_specs=[pl.BlockSpec(memory_space=pltpu.VMEM)] + [pl.BlockSpec(memory_space=pl.ANY)] * len(tokens),
        out_specs=pl.BlockSpec(memory_space=pltpu.VMEM),
    )(value, *tokens)


def embed_back_kernel(grad_ref, patch_ref, shown_ref, gain_ref, vector_ref, *refs):
    out_ref = refs[-1]
    grad = grad_ref[...]
    images = grad.shape[0] // PAD_SEQ
    shown = shown_ref[...]
    position = jnp.zeros((PAD_SEQ, D), single)
    token = jnp.zeros((1, D), single)
    patch_grads = []
    for image in range(images):
        here = grad[image * PAD_SEQ : (image + 1) * PAD_SEQ]
        position = position + here
        rows = here[1:SEQ]
        seen = shown[image * PATCHES : (image + 1) * PATCHES]
        token = token + jnp.sum(rows * (1.0 - seen), axis=0, keepdims=True)
        patch_grads.append((rows * seen).astype(narrow))
    patch_grad = product_left(patch_ref[...], jnp.concatenate(patch_grads))
    out_ref[...] = jnp.zeros_like(out_ref)
    for column in range(D // 128):
        lane = slice(column * 128, (column + 1) * 128)
        out_ref[column, pl.ds(0, PIX), :] = patch_grad[:, lane]
        out_ref[column, pl.ds(PIX, SEQ), :] = position[:SEQ, lane]
        out_ref[column, pl.ds(PIX + SEQ, 1), :] = position[0:1, lane]
        out_ref[column, pl.ds(PIX + SEQ + 1, 1), :] = token[:, lane]
        out_ref[column, pl.ds(PIX + SEQ + 2, 2), :] = gain_ref[:, lane]
        out_ref[column, pl.ds(EMBED_ROWS, vector_ref.shape[0]), :] = vector_ref[:, lane]


def embed_back(grad, patch_rows, shown, gains, vector_grads, rows, waits):
    return pl.pallas_call(
        embed_back_kernel,
        out_shape=jax.ShapeDtypeStruct((D // 128, rows, 128), single),
        in_specs=[pl.BlockSpec(memory_space=pltpu.VMEM)] * 5 + [pl.BlockSpec(memory_space=pl.ANY)] * len(waits),
        out_specs=pl.BlockSpec(memory_space=pltpu.VMEM),
        compiler_params=pltpu.CompilerParams(vmem_limit_bytes=40 << 20),
        cost_estimate=pl.CostEstimate(flops=100 * 10**6, bytes_accessed=37 * 10**5, transcendentals=0),
    )(grad, patch_rows, shown, gains, vector_grads, *waits)


def proto_units(values):
    rounded = values.astype(narrow).astype(single)
    scale = lax.rsqrt(jnp.sum(rounded * rounded, axis=-1, keepdims=True) + 1e-06)
    return rounded, scale, (rounded * scale).astype(narrow)


def proto_terms(teacher_z, student_z, teacher_unit, student_unit, centre_column):
    teacher_logits = product_right(teacher_unit, teacher_z)
    logits = product_right(student_unit, student_z)
    teacher_exp = jnp.exp((teacher_logits - centre_column) * (1.0 / tau_teacher))
    student_exp = jnp.exp(logits * (1.0 / tau_student))
    return teacher_logits, logits, teacher_exp, student_exp


def logits_kernel(
    teacher_z_ref,
    student_z_ref,
    teacher_ref,
    student_ref,
    centre_ref,
    class_ref,
    mixed_ref,
    sums_ref,
    centre_sum_ref,
    student_mix_ref,
    teacher_mix_ref,
    totals_ref,
):
    step = pl.program_id(0)

    @pl.when(step == 0)
    def _():
        student_mix_ref[...] = jnp.zeros_like(student_mix_ref)
        teacher_mix_ref[...] = jnp.zeros_like(teacher_mix_ref)
        totals_ref[...] = jnp.zeros_like(totals_ref)

    teacher_unit = proto_units(teacher_ref[...])[2]
    student_unit = proto_units(student_ref[...])[2]
    teacher_logits, logits, teacher_exp, student_exp = proto_terms(
        teacher_z_ref[...], student_z_ref[...], teacher_unit, student_unit, centre_ref[...]
    )
    totals_ref[pl.ds(0, 1), :] += jnp.sum(teacher_exp, axis=0, keepdims=True)
    totals_ref[pl.ds(1, 1), :] += jnp.sum(student_exp, axis=0, keepdims=True)
    totals_ref[pl.ds(2, 1), :] += jnp.sum(teacher_exp * logits, axis=0, keepdims=True)
    centre_sum_ref[...] = jnp.sum(teacher_logits * class_ref[0:1], axis=1, keepdims=True)
    student_mix_ref[...] += product_left(student_unit, student_exp.astype(narrow))
    teacher_mix_ref[...] += product_left(student_unit, teacher_exp.astype(narrow))

    @pl.when(step == pl.num_programs(0) - 1)
    def _():
        mixed_ref[:, pl.ds(0, BOT)] = student_mix_ref[...].T
        mixed_ref[:, pl.ds(BOT, BOT)] = teacher_mix_ref[...].T
        lower = jnp.zeros((128 - totals_ref.shape[0], totals_ref.shape[1]), single)
        mixed_ref[:, pl.ds(2 * BOT, 128)] = jnp.concatenate([totals_ref[...], lower]).T
        sums_ref[...] = totals_ref[...]


def proto_specs(rows, block):
    whole = pl.BlockSpec((rows, BOT), lambda i: (0, 0))
    table = pl.BlockSpec((block, BOT), lambda i: (i, 0))
    column = pl.BlockSpec((block, 1), lambda i: (i, 0))
    lines = pl.BlockSpec((8, rows), lambda i: (0, 0))
    return whole, table, column, lines


def logits_pass(teacher_z, student_z, teacher, student, centre_column, class_lines):
    rows, protos_here = teacher_z.shape[0], student.shape[0]
    block = protos_here // 4
    whole, table, column, lines = proto_specs(rows, block)
    return pl.pallas_call(
        logits_kernel,
        grid=(4,),
        out_shape=[
            jax.ShapeDtypeStruct((rows, 2 * BOT + 128), single),
            jax.ShapeDtypeStruct((8, rows), single),
            jax.ShapeDtypeStruct((protos_here, 1), single),
        ],
        in_specs=[whole, whole, table, table, column, lines],
        out_specs=[pl.BlockSpec((rows, 2 * BOT + 128), lambda i: (0, 0)), lines, column],
        scratch_shapes=[
            pltpu.VMEM((BOT, rows), single),
            pltpu.VMEM((BOT, rows), single),
            pltpu.VMEM((8, rows), single),
        ],
        compiler_params=pltpu.CompilerParams(vmem_limit_bytes=56 << 20),
        cost_estimate=pl.CostEstimate(flops=100 * 10**6, bytes_accessed=520 * 10**5, transcendentals=0),
    )(teacher_z, student_z, teacher, student, centre_column, class_lines)


def proto_grad_kernel(
    teacher_z_ref, student_z_ref, teacher_ref, student_ref, centre_ref, scale_ref, *refs
):
    grad_ref, square_ref = refs[-2:]
    step = pl.program_id(0)

    @pl.when(step == 0)
    def _():
        square_ref[...] = jnp.zeros_like(square_ref)

    teacher_unit = proto_units(teacher_ref[...])[2]
    rounded, scale, student_unit = proto_units(student_ref[...])
    student_z = student_z_ref[...]
    _, _, teacher_exp, student_exp = proto_terms(
        teacher_z_ref[...], student_z, teacher_unit, student_unit, centre_ref[...]
    )
    grad_logits = (student_exp * scale_ref[0:1] - teacher_exp * scale_ref[1:2]).astype(narrow)
    unit_grad = product_plain(grad_logits, student_z)
    along = jnp.sum(unit_grad * rounded, axis=-1, keepdims=True)
    grad = scale * (unit_grad - rounded * (along * scale * scale))
    grad_ref[...] = grad
    square_ref[...] += jnp.broadcast_to(jnp.sum(grad * grad), square_ref.shape)


def proto_grad_pass(teacher_z, student_z, teacher, student, centre_column, scale_lines, waits):
    rows, protos_here = teacher_z.shape[0], student.shape[0]
    block = protos_here // 4
    whole, table, column, lines = proto_specs(rows, block)
    return pl.pallas_call(
        proto_grad_kernel,
        grid=(4,),
        out_shape=[
            jax.ShapeDtypeStruct((protos_here, BOT), single),
            jax.ShapeDtypeStruct((8, 128), single),
        ],
        in_specs=[whole, whole, table, table, column, lines]
        + [pl.BlockSpec(memory_space=pl.ANY)] * len(waits),
        out_specs=[table, pl.BlockSpec((8, 128), lambda i: (0, 0))],
        compiler_params=pltpu.CompilerParams(vmem_limit_bytes=56 << 20),
        cost_estimate=pl.CostEstimate(flops=100 * 10**6, bytes_accessed=400 * 10**5, transcendentals=0),
    )(teacher_z, student_z, teacher, student, centre_column, scale_lines, *waits)


def proto_update(factor, student, moment, second, teacher, grad):
    def kernel(factor_ref, *refs):
        weight, moment, second, teacher, grad = [ref[...] for ref in refs[:5]]
        done = adam_update(weight, moment, second, grad * factor_ref[0], teacher)
        for ref, value in zip(refs[5:], done):
            ref[...] = value

    block = student.shape[0] // 4
    table = pl.BlockSpec((block, BOT), lambda i: (i, 0))
    return pl.pallas_call(
        kernel,
        grid=(4,),
        out_shape=[
            jax.ShapeDtypeStruct(student.shape, narrow if number == 3 else single) for number in range(5)
        ],
        in_specs=[pl.BlockSpec(memory_space=pltpu.SMEM)] + [table] * 5,
        out_specs=[table] * 5,
        compiler_params=pltpu.CompilerParams(vmem_limit_bytes=40 << 20),
        cost_estimate=pl.CostEstimate(flops=10**7, bytes_accessed=2 * 10**7, transcendentals=0),
    )(factor.reshape(1), student, moment, second, teacher, grad)


def head_grads_kernel(
    held, place_ref, inputs_ref, grads_ref, *refs,
):
    own_ref, partner_ref = refs[len(refs) - 9 - held :][:2] if held else refs[-9:-7]
    window_ref, rows_ref, product_ref, third_ref, bottle_ref, line_ref, sems = refs[-7:]
    slot = own_ref.shape[0]
    lead = product_ref.shape[0] - window_ref.shape[1]
    number = lax.broadcasted_iota(jnp.int32, (slot, 1), 0)
    product_ref[pl.ds(0, lead), :] = jnp.zeros((lead, ROW), single)

    def block(at, out_ref):
        column = pl.multiple_of(place_ref[at], 128)
        grad_column = pl.multiple_of(place_ref[at + 3], 128)
        copies = [
            pltpu.make_async_copy(
                inputs_ref.at[:, pl.ds(column, window_ref.shape[1])], window_ref, sems.at[0]
            ),
            pltpu.make_async_copy(grads_ref.at[:, pl.ds(grad_column, ROW)], rows_ref, sems.at[1]),
        ]
        for copy in copies:
            copy.start()
        for copy in copies:
            copy.wait()
        window = window_ref[...]
        for piece in range(4):
            spot = pl.ds(piece * (ROW // 4), ROW // 4)
            product_ref[pl.ds(lead, window.shape[1]), spot] = product_left(window, rows_ref[:, spot])
        from_row = pl.multiple_of(lead + place_ref[at + 1], 8)
        kept = jnp.where(number < place_ref[at + 2], product_ref[pl.ds(from_row, slot), :], 0.0)
        out_ref[...] = kept.astype(out_ref.dtype)

    @pl.when(place_ref[8] == 0)
    def _():
        block(0, own_ref)

    @pl.when(place_ref[8] == 1)
    def _():
        column = pl.multiple_of(place_ref[9], 128)
        copies = [
            pltpu.make_async_copy(
                inputs_ref.at[:, pl.ds(column, third_ref.shape[1])], third_ref, sems.at[0]
            ),
            pltpu.make_async_copy(grads_ref.at[:, pl.ds(2 * HID, BOT)], bottle_ref, sems.at[1]),
        ]
        for copy in copies:
            copy.start()
        for copy in copies:
            copy.wait()
        third = product_left(third_ref[...], bottle_ref[...])
        for lane in range(BOT // 128):
            line_ref[lane] = third[:, lane * 128 : (lane + 1) * 128]
        for group in range(ROW // BOT):
            for lane in range(BOT // 128):
                value = line_ref[lane, pl.ds(group, slot, stride=ROW // BOT), :]
                own_ref[:, pl.ds(group * BOT + lane * 128, 128)] = jnp.where(
                    number < place_ref[2], value, 0.0
                )

    block(4, partner_ref)


def head_grads(place, inputs_all, grads_all, slot, lead, waits, held):
    rows = inputs_all.shape[0]
    wide = slot * ROW // BOT
    return pl.pallas_call(
        lambda *refs: head_grads_kernel(len(held), *refs),
        out_shape=[jax.ShapeDtypeStruct((slot, ROW), kind) for kind in (single, narrow)]
        + [jax.ShapeDtypeStruct(array.shape, array.dtype) for array in held],
        in_specs=[pl.BlockSpec(memory_space=pltpu.SMEM)]
        + [pl.BlockSpec(memory_space=pl.ANY)] * (2 + len(waits) + len(held)),
        out_specs=[pl.BlockSpec(memory_space=pltpu.VMEM)] * 2
        + [pl.BlockSpec(memory_space=pl.ANY)] * len(held),
        input_output_aliases={3 + len(waits) + number: 2 + number for number in range(len(held))},
        scratch_shapes=[
            pltpu.VMEM((rows, 256), narrow),
            pltpu.VMEM((rows, ROW), narrow),
            pltpu.VMEM((lead + 256, ROW), single),
            pltpu.VMEM((rows, wide), narrow),
            pltpu.VMEM((rows, BOT), narrow),
            pltpu.VMEM((BOT // 128, wide, 128), single),
            pltpu.SemaphoreType.DMA((2,)),
        ],
        compiler_params=pltpu.CompilerParams(vmem_limit_bytes=56 << 20),
        cost_estimate=pl.CostEstimate(flops=100 * 10**6, bytes_accessed=370 * 10**5, transcendentals=0),
    )(place, inputs_all, grads_all, *waits, *held)


def close_local(
    patches,
    masked,
    slot_used,
    stem,
    stem_moment,
    stem_second,
    stem_teacher,
    layers,
    layer_moment,
    layer_second,
    layer_teacher,
    protos,
    proto_moment,
    proto_second,
    proto_teacher,
    centre,
):
    count = 1 << len(BITS)
    half = count // 2
    me = lax.axis_index("dev")
    across = MASKS["b"]
    student_side = me >= half
    groups = [list(range(half)), list(range(half, count))]
    quarter = half // 2
    swap = jnp.where(student_side, quarter, 0)
    side = student_side.astype(jnp.int32).reshape(1)
    images_here = patches.shape[0]
    rows_here = images_here * 17
    pair_rows = -(-2 * rows_here // 16) * 16
    more_rows = pair_rows - 2 * rows_here
    stem_piece = stem.shape[0]
    layer_piece = layers.shape[1]
    block_rows = MATRIX_ROWS // count
    block = block_rows * D
    tail = layer_piece * count - MATRIX_ROWS * D
    drift = layer_piece - block
    bounds = head_bounds(count, stem_piece)
    sizes = [bounds[i + 1] - bounds[i] for i in range(count)]
    slot = max(sizes)
    starts = [b * ROW + EMBED_FLAT - stem_piece * i for i, b in enumerate(bounds[:-1])]
    first_w2 = bounds.index(D)
    first_w3 = bounds.index(D + HID)
    row_index = jnp.concatenate([jnp.zeros((images_here, 1), jnp.int32), masked + 1], axis=1)
    masked_here = jnp.any(
        masked[:, :, None] == jnp.arange(PATCHES, dtype=jnp.int32)[None, None, :], axis=1
    )
    kept = slot_used.astype(single)

    front = 16
    early_rows = -(-stem_piece // D)
    late_start = early_rows * D - stem_piece
    embed_rows = -(-early_rows // 16) * 16
    own_layers = jnp.concatenate([layer_teacher, layers])
    own_tail = own_layers[:, layer_piece - tail :].reshape(2 * LAYERS, tail // 128, 128)
    before = lax.ppermute(own_tail, "dev", step_pairs(count, 1))
    head_span = GROUP * ROW
    stems = jnp.stack([as_lanes(stem_teacher), as_lanes(stem)])
    stems_next = lax.ppermute(stems[:, : head_span // 128], "dev", step_pairs(count, -1))
    def per_device(rows):
        return lax.dynamic_slice(jnp.array(rows, jnp.int32), (me, 0), (1, len(rows[0]))).reshape(-1)

    def spots(*values):
        return [part for value in values for part in (value // 128, value % 128)]

    place = per_device(
        [
            spots(starts[i] + front * 128, front * 128 + (0 if i == 0 else late_start), tail - drift * i)
            for i in range(count)
        ]
    )
    head_blocks, layer_blocks, embed_blocks, vector_blocks = own_blocks(
        place,
        stems,
        stems_next,
        as_lanes(own_layers),
        before,
        (front, stem_piece, layer_piece, tail),
        slot,
        block_rows,
        embed_rows,
    )

    other_layers = lax.ppermute(layer_blocks, "dev", pairs(count, across))
    both_layers = jnp.where(
        student_side,
        jnp.stack([other_layers, layer_blocks]),
        jnp.stack([layer_blocks, other_layers]),
    )
    gathered = lax.all_gather(both_layers, "dev", axis=0, axis_index_groups=groups)
    head_out = jnp.where(student_side, head_blocks[0], head_blocks[1])
    head_keep = jnp.where(student_side, head_blocks[1], head_blocks[0])
    head_got = lax.ppermute(head_out, "dev", pairs(count, across))
    both_head = jnp.where(
        student_side, jnp.stack([head_got, head_keep]), jnp.stack([head_keep, head_got])
    )

    vectors = lax.ppermute(vector_blocks, "dev", [(count - 1, 0)])
    seed = jnp.concatenate([embed_blocks.reshape(2 * embed_rows, D), vectors.reshape(8 * 2 * LAYERS, D)])
    third = -(-seed.shape[0] // 48) * 16
    spread_parts = []
    for number, order in enumerate(("xyba", "baxy", "ybax")):
        spread = seed[number * third : (number + 1) * third]
        reached = [0, 1]
        for name in order:
            moves = [(i, i ^ MASKS[name]) for i in reached]
            got = lax.ppermute(spread, "dev", moves)
            targets = [t for s, t in moves]
            is_target = jnp.array([i in targets for i in range(count)])[me]
            spread = jnp.where(is_target, got, spread)
            reached = reached + targets
        spread_parts.append(spread)
    spread = jnp.concatenate(spread_parts)
    other = lax.ppermute(spread, "dev", pairs(count, 1))
    is_even = me % 2 == 0
    even = jnp.where(is_even, spread, other)
    odd = jnp.where(is_even, other, spread)
    embed_all = [
        jnp.concatenate(
            [
                even[m * embed_rows : m * embed_rows + early_rows],
                odd[m * embed_rows : m * embed_rows + EMBED_ROWS - early_rows],
            ]
        )
        for m in range(2)
    ]
    gathered_head = lax.all_gather(after(both_head, gathered, even, odd), "dev", axis=0, axis_index_groups=groups)
    vectors_all = even[2 * embed_rows :].reshape(2, LAYERS, 8, D)

    plan = []
    for i in range(1, count):
        target = 0 if i < first_w2 else 1 if i < first_w3 else 2
        row = bounds[i] - (0, D, D + HID)[target]
        skip = max(-row, 0)
        owner = 1 if i >= half else 0
        plan.append((i ^ across if owner else i, owner, skip, sizes[i] - skip, target, row + skip))

    def embed_parts(model):
        rows = embed_all[model]
        return (rows[:PIX], rows[PIX : PIX + SEQ], rows[PIX + SEQ :], None, None, None)

    def head_rows(stream, extras):
        chosen = jnp.take_along_axis(stream, row_index[:, :, None], axis=1).reshape(rows_here, D)
        normed = layer_norm(chosen, extras[2].astype(single), extras[3].astype(single)).astype(narrow)
        return chosen, normed

    def start_rows(parts, student):
        stream = embed(parts, patches, masked_here, student)
        return jnp.pad(stream, ((0, 0), (0, PAD_SEQ - SEQ), (0, 0))).reshape(images_here * PAD_SEQ, D)

    student_parts = embed_parts(1)
    stream = start_rows(student_parts, True)
    saved_layers = []
    for layer_index in range(LAYERS):
        before_layer = stream
        stream, *saved = layer_forward(
            side, stream, vectors_all[1, layer_index], gathered, LAYERS + layer_index, True
        )
        saved_layers.append((before_layer, *saved))
    teacher_parts = embed_parts(0)
    teacher_stream = start_rows(teacher_parts, False)
    for layer_index in range(LAYERS):
        teacher_stream = layer_forward(
            side, teacher_stream, vectors_all[0, layer_index], gathered, layer_index, False
        )[0]
    stream = stream.reshape(images_here, PAD_SEQ, D)
    teacher_stream = teacher_stream.reshape(images_here, PAD_SEQ, D)
    chosen, student_normed = head_rows(stream, student_parts[2])
    teacher_normed = head_rows(teacher_stream, teacher_parts[2])[1]

    normed_got = lax.ppermute(
        jnp.where(student_side, teacher_normed, student_normed), "dev", pairs(count, across)
    )
    normed = jnp.where(
        student_side,
        jnp.concatenate([normed_got, student_normed]),
        jnp.concatenate([teacher_normed, normed_got]),
    )
    normed = jnp.pad(normed, ((0, more_rows), (0, 0)))
    all_rows = half * pair_rows
    kept_row = jnp.broadcast_to(kept[:, None], (images_here, 17)).reshape(1, rows_here)
    kept_pair = cube_gather(kept_row, "b").reshape(1, 2 * rows_here)
    kept_pair = jnp.pad(kept_pair, ((0, 0), (0, more_rows)))
    all_kept = cube_gather(kept_pair, "xygc").reshape(all_rows)
    third_end = (bounds[-2] - D - HID + slot) * (ROW // BOT)
    acts_width = D + HID + max(third_end, HID)
    unit_z, acts, bottleneck, pre_one, pre_two = head_pass(
        head_up_kernel,
        plan,
        side,
        (normed,),
        gathered_head,
        [
            jax.ShapeDtypeStruct((pair_rows, BOT), narrow),
            jax.ShapeDtypeStruct((pair_rows, acts_width), narrow),
            jax.ShapeDtypeStruct((pair_rows, BOT), single),
            jax.ShapeDtypeStruct((pair_rows, HID), single),
            jax.ShapeDtypeStruct((pair_rows, HID), single),
        ],
        (all_kept,),
    )
    inputs_all = lax.all_gather(acts, "dev", axis=0, axis_index_groups=groups).reshape(half * pair_rows, -1)

    z_pair = cube_gather(unit_z, "b")
    teacher_z_all = cube_gather(z_pair[0], "xygc").reshape(all_rows, BOT)
    student_z_all = cube_gather(z_pair[1], "gxyc").reshape((2,) * 4 + (pair_rows, BOT))
    student_z_all = jnp.transpose(student_z_all, (0, 3, 1, 2, 4, 5)).reshape(all_rows, BOT)
    protos_here = protos.shape[0]
    own_centre = lax.dynamic_slice(centre, (me * protos_here,), (protos_here,))
    centre_column = own_centre.reshape(protos_here, 1)
    spot_in_pair = jnp.arange(all_rows) % pair_rows
    is_class = (spot_in_pair % 17) == 0
    class_kept = jnp.where(is_class, all_kept, 0.0)
    row_weight = jnp.where(is_class, all_kept, all_kept * (1.0 / 16.0))
    count_total = jnp.sum(class_kept)

    def lines(*values):
        return jnp.pad(jnp.stack(values), ((0, 8 - len(values)), (0, 0)))

    mixed_rows, sums, centre_sum = logits_pass(
        teacher_z_all, student_z_all, proto_teacher, protos, centre_column, lines(class_kept)
    )
    by_pair = (2,) * 4 + (pair_rows, -1)
    mixed_own = jnp.concatenate(
        [
            cube_scatter(mixed_rows[:, :BOT].reshape(by_pair), "cgyx", "cgyx"),
            cube_scatter(mixed_rows[:, BOT:].reshape(by_pair), "cgyx", "cxyg"),
        ],
        axis=1,
    )
    mixed_own = mixed_own + lax.ppermute(
        mixed_own.astype(narrow), "dev", [(i, i ^ across) for i in range(half)]
    ).astype(single)
    stages = [sums[:3]]
    for name in "cxyab":
        stages.append(stages[-1] + lax.ppermute(stages[-1], "dev", pairs(count, MASKS[name])))
    sums = stages[-1]
    cross = jnp.log(sums[1]) - sums[2] / (sums[0] * tau_student)
    loss_total = jnp.sum(row_weight * cross)
    scale = row_weight / tau_student
    student_scale, teacher_scale = scale / sums[1], scale / sums[0]
    flags = bit_flags(me)
    pair_at = flags["c"] * 8 + flags["g"] * 4 + flags["y"] * 2 + flags["x"]
    own_scale = lax.dynamic_slice(scale, (pair_at * pair_rows,), (pair_rows,))[:, None]
    grad_unit_z = own_scale * (
        mixed_own[:, :BOT] / mixed_own[:, 2 * BOT + 1 : 2 * BOT + 2]
        - mixed_own[:, BOT : 2 * BOT] / mixed_own[:, 2 * BOT : 2 * BOT + 1]
    )
    own_new_centre = (
        centre_keep * own_centre + (1.0 - centre_keep) * centre_sum.reshape(protos_here) / count_total
    )
    new_centre = cube_gather(own_new_centre.reshape(1, protos_here), "cxyab").reshape(-1)

    grads, grad_normed = head_pass(
        head_down_kernel,
        plan,
        side,
        (grad_unit_z, bottleneck, pre_one, pre_two),
        gathered_head,
        [
            jax.ShapeDtypeStruct((pair_rows, 2 * HID + BOT), narrow),
            jax.ShapeDtypeStruct((pair_rows, D), single),
        ],
        (stages[3],),
    )
    grads_all = lax.all_gather(grads, "dev", axis=0, axis_index_groups=groups).reshape(half * pair_rows, -1)
    normed_back = lax.ppermute(
        grad_normed[:rows_here], "dev", [(i, i ^ across) for i in range(half, count)]
    )
    own_grad_normed = jnp.where(student_side, grad_normed[rows_here : 2 * rows_here], normed_back)
    extras = student_parts[2].astype(single)
    grad_chosen, grad_gain, grad_bias = jax.vjp(layer_norm, chosen, extras[2], extras[3])[1](
        own_grad_normed
    )
    image_index = jnp.arange(images_here, dtype=jnp.int32)[:, None]
    grad_stream = (
        jnp.zeros(stream.shape, single)
        .at[image_index, row_index]
        .add(grad_chosen.reshape(images_here, 17, D))
    )

    grad_stream = grad_stream.reshape(images_here * PAD_SEQ, D)
    middle_row = block_rows // 2
    vector_grads = [None] * LAYERS

    def halves(array):
        middle = array.shape[-2] // 2
        return [array[..., :middle, :], array[..., middle:, :]]

    def cuts(parts, names, order):
        return [cut(part, name, axis, 1) for part, name, axis in zip(parts, names, order)]

    def moves(pieces, order):
        return [move(sent, kept, axis) for (sent, kept, left), axis in zip(pieces, order)]

    def over_core(weight_grad, rows):
        pairs_of = weight_grad.reshape(D // 128, -1, 2, rows, 128)
        return move(*cut(pairs_of, "pc", "c", 1)[:2], "c")

    def start(late, early):
        shared_pair = 4 * D // (2 * block_rows)
        whole = jnp.concatenate(
            [
                early[:, :shared_pair],
                early[:, shared_pair:] + late[:, : early.shape[1] - shared_pair],
                late[:, early.shape[1] - shared_pair :],
            ],
            axis=1,
        )
        by_bits = whole.reshape((D // 128, 2, 2, 2, 2, block_rows, 128))
        return (cuts(halves(by_bits), ["bayx"] * 2, rounds[0]), 0)

    rounds = (("x", "b"), ("y", "a"), ("b", "x"), ("a", "y"))

    def advance(state):
        pieces, stage = state
        parts = moves(pieces, rounds[stage])
        names = [left for sent, kept, left in pieces]
        return cuts(parts, names, rounds[stage + 1]), stage + 1

    def finish(state):
        while state[1] < len(rounds) - 1:
            state = advance(state)
        return moves(state[0], rounds[-1])

    def sends(states):
        return tuple(sent for pieces, stage in states for sent, kept, left in pieces)

    started = []
    waits, later_waits = (stages[4],), (stages[5],)
    for layer_index in reversed(range(LAYERS)):
        saved, vectors = saved_layers[layer_index], vectors_all[1, layer_index]
        part = LAYERS + layer_index
        grad_stream, late_grad, late_vectors = mlp_back(
            side, grad_stream, saved, vectors, gathered, part, waits + sends(started)
        )
        late = over_core(late_grad, block_rows)
        started = [advance(state) for state in started]
        grad_stream, early_grad, early_vectors = attention_back(
            side, grad_stream, saved, vectors, gathered, part, later_waits + sends(started)
        )
        waits, later_waits = (), ()
        vector_grads[layer_index] = (late_vectors + early_vectors)[:6]
        if layer_index == LAYERS - 1:
            proto_grad, proto_square = proto_grad_pass(
                teacher_z_all,
                student_z_all,
                proto_teacher,
                protos,
                centre_column,
                lines(student_scale, teacher_scale),
                (early_vectors,),
            )
            waits = (proto_square,)
        started = [advance(state) for state in started]
        started.append(start(late, over_core(early_grad, block_rows)))
    *later_states, last = started
    small_rows = -(-(EMBED_ROWS + 6 * LAYERS) // 64) * 64
    small = embed_back(
        grad_stream,
        patches.reshape(images_here * PATCHES, PIX),
        jnp.where(masked_here, 0.0, 1.0).reshape(images_here * PATCHES, 1),
        jnp.stack([grad_gain, grad_bias]),
        jnp.concatenate(vector_grads),
        small_rows,
        sends([last]),
    )
    small_parts = halves(over_core(small, small_rows // 2)[:, 0])
    small_sends = [part.astype(narrow) for part in small_parts]
    def block_place(i):
        column = max(bounds[i], 0) // 128 * 128
        grad_column = 0 if i < first_w2 else HID
        return [column, bounds[i] - column if i else 0, sizes[i] if i else 0, grad_column]

    def third_place(i):
        return [0, 0, sizes[i], 0]

    place = per_device(
        [
            (third_place(i) if i >= first_w3 else block_place(i))
            + block_place(i ^ across)
            + [int(i >= first_w3), D + HID + max(bounds[i] - D - HID, 0) * (ROW // BOT)]
            for i in range(count)
        ]
    )
    flying = [last] + later_states
    own_block_grad, partner_block_grad, *held = head_grads(
        place,
        inputs_all,
        grads_all,
        slot,
        -min(bounds[1], 0),
        (),
        [stay for pieces, stage in flying for sent, stay, left in pieces] + small_parts,
    )
    held = iter(held)
    flying = [([(sent, next(held), left) for sent, _, left in pieces], stage) for pieces, stage in flying]
    small_parts = list(held)
    block_got = lax.ppermute(partner_block_grad, "dev", [(i, i ^ across) for i in range(half, count)])
    head_block_grad = jnp.where(student_side, own_block_grad, block_got.astype(single))
    small_parts = moves([(sent, part, "") for sent, part in zip(small_sends, small_parts)], rounds[0])
    for order in rounds[1:]:
        small_parts = [move(part.astype(narrow), part, axis) for part, axis in zip(small_parts, order)]
    small_mine = jnp.concatenate(small_parts, axis=1)
    small_other = lax.ppermute(small_mine, "dev", pairs(count, 1))
    small_sum = jnp.where(
        me % 2 == 0,
        jnp.concatenate([small_mine, small_other], axis=1),
        jnp.concatenate([small_other, small_mine], axis=1),
    )
    blocks = [jnp.concatenate(finish(state), axis=1) for state in flying]
    layer_block = jnp.stack(blocks[:1] + blocks[:0:-1])

    square_local = (
        jnp.sum(head_block_grad * head_block_grad)
        + jnp.sum(layer_block * layer_block)
        + jnp.where(me == 0, jnp.sum(small_sum * small_sum), 0.0)
        + proto_square[0, 0]
    )
    square_total = cube_sum(square_local.reshape(1, 1))[0, 0]
    behind = lax.ppermute(layer_block[:, :, :6], "dev", step_pairs(count, -1))
    last_rows = lax.dynamic_slice(
        head_block_grad, (jnp.array(sizes, jnp.int32)[me] - GROUP, 0), (GROUP, ROW)
    )
    previous = lax.ppermute(last_rows, "dev", step_pairs(count, 1))
    place = per_device([spots(head_span - starts[i], drift * i) for i in range(count)])
    stem_lines, layer_lines = own_shards(
        place, head_block_grad, previous, layer_block, behind, lane_rows(stem_piece), lane_rows(layer_piece)
    )
    small_all = jnp.swapaxes(small_sum, 0, 1).reshape(small_rows, D)
    embed_grad = small_all[:EMBED_ROWS].reshape(-1)
    vector_grad = small_all[EMBED_ROWS : EMBED_ROWS + 6 * LAYERS].reshape(LAYERS, 6 * D)
    layer_grad = layer_lines.reshape(LAYERS, -1)[:, :layer_piece]
    layer_grad = jnp.concatenate(
        [
            layer_grad[:, : layer_piece - tail],
            jnp.where(me == count - 1, vector_grad, layer_grad[:, layer_piece - tail :]),
        ],
        axis=1,
    )
    stem_grad = stem_lines.reshape(-1)[:stem_piece]
    rest = EMBED_FLAT - stem_piece
    second_part = jnp.concatenate([embed_grad[stem_piece:], stem_grad[rest:]])
    stem_grad = jnp.where(
        me == 0, embed_grad[:stem_piece], jnp.where(me == 1, second_part, stem_grad)
    )

    grad_norm = jnp.sqrt(square_total) / count_total
    factor = jnp.minimum(1.0, clip_limit / (grad_norm + 1e-06)) / count_total
    stem_set = adam_update(stem, stem_moment, stem_second, stem_grad * factor, stem_teacher)
    layer_set = adam_update(layers, layer_moment, layer_second, layer_grad * factor, layer_teacher)
    proto_set = proto_update(factor, protos, proto_moment, proto_second, proto_teacher, proto_grad)
    return (loss_total, count_total, grad_norm, new_centre) + stem_set + layer_set + tuple(proto_set)


def solution(mesh):
    count = mesh.shape["dev"]
    stem_length = -(-(EMBED_FLAT + HEAD_ROWS * ROW) // count) * count
    close = fits(count, stem_length // count, (MATRIX_ROWS + 6) * D // count)
    placed = (
        P("dev", None, None),
        P("dev", None),
        P("dev"),
        P("dev"),
        P("dev"),
        P("dev"),
        P("dev"),
        P(None, "dev"),
        P(None, "dev"),
        P(None, "dev"),
        P(None, "dev"),
        P("dev", None),
        P("dev", None),
        P("dev", None),
        P("dev", None),
        P(),
    )
    return jax.shard_map(
        close_local if close else spread_local,
        mesh=mesh,
        in_specs=placed,
        out_specs=(
            P(),
            P(),
            P(),
            P(),
            P("dev"),
            P("dev"),
            P("dev"),
            P("dev"),
            P("dev"),
            P(None, "dev"),
            P(None, "dev"),
            P(None, "dev"),
            P(None, "dev"),
            P(None, "dev"),
            P("dev", None),
            P("dev", None),
            P("dev", None),
            P("dev", None),
            P("dev", None),
        ),
        check_vma=False,
    )
```

```python
import jax
import jax.numpy as jnp
from jax import lax
from jax.experimental import pallas as pl
from jax.experimental.pallas import tpu as pltpu
from jax.sharding import PartitionSpec as P

D = 384
HEADS = 6
HEAD_DIM = 64
FF = 1536
HID = 2048
BOT = 256
PIX = 588
PATCHES = 256
LAYERS = 2
STEP = 10
SEQ = 257


tau_student = 0.1
tau_teacher = 0.04
clip_limit = 0.003
learn_rate = 0.03
beta_one = 0.9
beta_two = 0.999
adam_eps = 1e-08
decay_rate = 0.04
teacher_keep = 0.8
centre_keep = 0.9
narrow = jnp.bfloat16
single = jnp.float32


def layer_shapes():
    return ((D, 3 * D), (D, D), (D, FF), (FF, D), (6, D))


def stem_shapes():
    return ((PIX, D), (SEQ, D), (4, D), (D, HID), (HID, HID), (HID, BOT))


def cut_flat(flat_row, shape_list):
    pieces = []
    offset = 0
    for shape_pair in shape_list:
        length = shape_pair[0] * shape_pair[1]
        pieces.append(flat_row[offset : offset + length].reshape(shape_pair))
        offset = offset + length
    return pieces


def pack_flat(grad_list, total_length):
    joined = jnp.concatenate([grad_item.reshape(-1) for grad_item in grad_list])
    return jnp.concatenate([joined, jnp.zeros((total_length - joined.shape[0],), single)])


def contract(form, left_arg, right_arg):
    return jnp.einsum(form, left_arg, right_arg, preferred_element_type=single)


def layer_norm(values, gain_row, bias_row):
    centred = values - jnp.mean(values, axis=-1, keepdims=True)
    spread = jnp.mean(centred * centred, axis=-1, keepdims=True)
    return centred * lax.rsqrt(spread + 1e-06) * gain_row + bias_row


def unit_rows(values):
    return values * lax.rsqrt(jnp.sum(values * values, axis=-1, keepdims=True) + 1e-06)


def gelu_back(pre_act, grad_act):
    return jax.vjp(jax.nn.gelu, pre_act)[1](grad_act)[0]


def block_forward(stream, weights):
    w_qkv, w_proj, w_up, w_down, vectors = weights
    vectors = vectors.astype(single)
    batch_size = stream.shape[0]
    normed = layer_norm(stream, vectors[0], vectors[1]).astype(narrow)
    packed = (
        contract("bsd,de->bse", normed, w_qkv)
        .astype(narrow)
        .reshape(batch_size, SEQ, 3, HEADS, HEAD_DIM)
    )
    scores = contract("bqhe,bkhe->bhqk", packed[:, :, 0], packed[:, :, 1]) * HEAD_DIM ** (-0.5)
    top_score = jnp.max(scores, axis=-1, keepdims=True)
    exp_terms = jnp.exp(scores - top_score)
    totals = jnp.sum(exp_terms, axis=-1, keepdims=True)
    log_total = top_score + jnp.log(totals)
    mixed = contract("bhqk,bkhe->bqhe", (exp_terms / totals).astype(narrow), packed[:, :, 2])
    mixed = mixed.astype(narrow).reshape(batch_size, SEQ, D)
    attn_out = contract("bsd,de->bse", mixed, w_proj)
    middle = stream + vectors[2] * attn_out
    normed_two = layer_norm(middle, vectors[3], vectors[4]).astype(narrow)
    pre_act = contract("bsd,df->bsf", normed_two, w_up)
    hidden = jax.nn.gelu(pre_act).astype(narrow)
    mlp_out = contract("bsf,fd->bsd", hidden, w_down)
    saved = (
        stream,
        normed,
        packed,
        log_total,
        mixed,
        attn_out,
        middle,
        normed_two,
        pre_act,
        hidden,
        mlp_out,
    )
    return (middle + vectors[5] * mlp_out, saved)


def block_backward(grad_out, weights, saved):
    w_qkv, w_proj, w_up, w_down, vectors = weights
    vectors = vectors.astype(single)
    (
        stream,
        normed,
        packed,
        log_total,
        mixed,
        attn_out,
        middle,
        normed_two,
        pre_act,
        hidden,
        mlp_out,
    ) = saved
    batch_size = stream.shape[0]
    score_scale = HEAD_DIM ** (-0.5)
    grad_ls_two = jnp.sum(grad_out * mlp_out, axis=(0, 1))
    grad_mlp = (grad_out * vectors[5]).astype(narrow)
    grad_down = contract("bsf,bsd->fd", hidden, grad_mlp)
    grad_pre = gelu_back(pre_act, contract("bsd,fd->bsf", grad_mlp, w_down)).astype(narrow)
    grad_up = contract("bsd,bsf->df", normed_two, grad_pre)
    grad_normed_two = contract("bsf,df->bsd", grad_pre, w_up)
    grad_mid, grad_gain_two, grad_bias_two = jax.vjp(layer_norm, middle, vectors[3], vectors[4])[1](
        grad_normed_two
    )
    grad_mid = grad_mid + grad_out
    grad_ls_one = jnp.sum(grad_mid * attn_out, axis=(0, 1))
    grad_attn = (grad_mid * vectors[2]).astype(narrow)
    grad_proj = contract("bsd,bse->de", mixed, grad_attn)
    grad_mixed = (
        contract("bse,de->bsd", grad_attn, w_proj)
        .astype(narrow)
        .reshape(batch_size, SEQ, HEADS, HEAD_DIM)
    )
    query_rows = packed[:, :, 0]
    key_rows = packed[:, :, 1]
    value_rows = packed[:, :, 2]
    probs = jnp.exp(contract("bqhe,bkhe->bhqk", query_rows, key_rows) * score_scale - log_total)
    grad_probs = contract("bqhe,bkhe->bhqk", grad_mixed, value_rows)
    grad_values = contract("bhqk,bqhe->bkhe", probs.astype(narrow), grad_mixed)
    grad_scores = probs * (grad_probs - jnp.sum(probs * grad_probs, axis=-1, keepdims=True))
    grad_raw = (grad_scores * score_scale).astype(narrow)
    grad_queries = contract("bhqk,bkhe->bqhe", grad_raw, key_rows)
    grad_keys = contract("bhqk,bqhe->bkhe", grad_raw, query_rows)
    grad_packed = (
        jnp.stack([grad_queries, grad_keys, grad_values], axis=2)
        .astype(narrow)
        .reshape(batch_size, SEQ, 3 * D)
    )
    grad_qkv = contract("bsd,bse->de", normed, grad_packed)
    grad_normed = contract("bse,de->bsd", grad_packed, w_qkv)
    grad_in, grad_gain_one, grad_bias_one = jax.vjp(layer_norm, stream, vectors[0], vectors[1])[1](
        grad_normed
    )
    grad_vectors = jnp.stack(
        [grad_gain_one, grad_bias_one, grad_ls_one, grad_gain_two, grad_bias_two, grad_ls_two]
    )
    return (grad_in + grad_mid, (grad_qkv, grad_proj, grad_up, grad_down, grad_vectors))


def embed(stem_parts, image_rows, masked_here, student):
    patch_w, position, extras, w_first, w_second, w_third = stem_parts
    extras = extras.astype(single)
    embedded = contract("gpc,cd->gpd", image_rows, patch_w)
    if student:
        embedded = jnp.where(masked_here[:, :, None], extras[1], embedded)
    cls_rows = jnp.broadcast_to(extras[0], (image_rows.shape[0], 1, D))
    return jnp.concatenate([cls_rows, embedded], axis=1) + position.astype(single)


def embed_backward(grad_stream, image_rows, masked_here):
    grad_cls = jnp.sum(grad_stream[:, 0], axis=0)
    grad_position = jnp.sum(grad_stream, axis=0)
    grad_patch_rows = grad_stream[:, 1:]
    grad_mask_token = jnp.sum(jnp.where(masked_here[:, :, None], grad_patch_rows, 0.0), axis=(0, 1))
    grad_embedded = jnp.where(masked_here[:, :, None], 0.0, grad_patch_rows).astype(narrow)
    grad_patch_w = contract("gpc,gpd->cd", image_rows, grad_embedded)
    return (grad_patch_w, grad_position, grad_cls, grad_mask_token)


def head_forward(stem_parts, proto_rows, stream, row_index):
    patch_w, position, extras, w_first, w_second, w_third = stem_parts
    extras = extras.astype(single)
    chosen = jnp.take_along_axis(stream, row_index[:, :, None], axis=1)
    normed = layer_norm(chosen, extras[2], extras[3]).astype(narrow)
    pre_one = contract("grd,dh->grh", normed, w_first)
    hidden_one = jax.nn.gelu(pre_one).astype(narrow)
    pre_two = contract("grh,hk->grk", hidden_one, w_second)
    hidden_two = jax.nn.gelu(pre_two).astype(narrow)
    bottleneck = contract("grh,hb->grb", hidden_two, w_third)
    unit_z = unit_rows(bottleneck).astype(narrow)
    unit_protos = unit_rows(proto_rows.astype(single)).astype(narrow)
    logits = contract("grb,kb->grk", unit_z, unit_protos)
    return (
        logits,
        (chosen, normed, pre_one, hidden_one, pre_two, hidden_two, bottleneck, unit_z, unit_protos),
    )


def head_backward(grad_logits, stem_parts, saved, row_index, stream_shape):
    patch_w, position, extras, w_first, w_second, w_third = stem_parts
    extras = extras.astype(single)
    chosen, normed, pre_one, hidden_one, pre_two, hidden_two, bottleneck, unit_z, unit_protos = (
        saved
    )
    grad_rounded = grad_logits.astype(narrow)
    grad_unit_z = contract("grk,kb->grb", grad_rounded, unit_protos)
    grad_unit_protos = contract("grk,grb->kb", grad_rounded, unit_z)
    grad_bottle = jax.vjp(unit_rows, bottleneck)[1](grad_unit_z)[0].astype(narrow)
    grad_third = contract("grh,grb->hb", hidden_two, grad_bottle)
    grad_pre_two = gelu_back(pre_two, contract("grb,hb->grh", grad_bottle, w_third)).astype(narrow)
    grad_second = contract("grh,grk->hk", hidden_one, grad_pre_two)
    grad_pre_one = gelu_back(pre_one, contract("grk,hk->grh", grad_pre_two, w_second)).astype(
        narrow
    )
    grad_first = contract("grd,grh->dh", normed, grad_pre_one)
    grad_normed = contract("grh,dh->grd", grad_pre_one, w_first)
    grad_chosen, grad_gain, grad_bias = jax.vjp(layer_norm, chosen, extras[2], extras[3])[1](
        grad_normed
    )
    image_index = jnp.arange(row_index.shape[0], dtype=jnp.int32)[:, None]
    grad_stream = jnp.zeros(stream_shape, single).at[image_index, row_index].add(grad_chosen)
    return (
        grad_stream,
        (grad_first, grad_second, grad_third),
        grad_gain,
        grad_bias,
        grad_unit_protos,
    )


def adam_update(weight, moment, second, grad, teacher):
    new_moment = beta_one * moment + (1.0 - beta_one) * grad
    new_second = beta_two * second + (1.0 - beta_two) * grad * grad
    direction = (
        new_moment
        / (1.0 - beta_one**STEP)
        / (jnp.sqrt(new_second / (1.0 - beta_two**STEP)) + adam_eps)
    )
    new_weight = weight - learn_rate * (direction + decay_rate * weight)
    return (
        new_moment,
        new_second,
        new_weight,
        new_weight.astype(narrow),
        teacher_keep * teacher + (1.0 - teacher_keep) * new_weight,
    )


def spread_local(
    patches,
    masked,
    slot_used,
    stem,
    stem_moment,
    stem_second,
    stem_teacher,
    layers,
    layer_moment,
    layer_second,
    layer_teacher,
    protos,
    proto_moment,
    proto_second,
    proto_teacher,
    centre,
):
    images_here = patches.shape[0]
    row_index = jnp.concatenate([jnp.zeros((images_here, 1), jnp.int32), masked + 1], axis=1)
    masked_here = jnp.any(
        masked[:, :, None] == jnp.arange(PATCHES, dtype=jnp.int32)[None, None, :], axis=1
    )
    kept = slot_used.astype(single)
    teacher_flat, teacher_protos = (
        lax.all_gather(stem_teacher.astype(narrow), "dev", axis=0, tiled=True),
        lax.all_gather(proto_teacher.astype(narrow), "dev", axis=0, tiled=True),
    )
    teacher_parts = cut_flat(teacher_flat, stem_shapes())
    stream = embed(teacher_parts, patches, masked_here, False)
    for layer_index in range(LAYERS):
        teacher_layer = lax.all_gather(
            layer_teacher[layer_index].astype(narrow), "dev", axis=0, tiled=True
        )
        stream = block_forward(stream, cut_flat(teacher_layer, layer_shapes()))[0]
    teacher_logits = head_forward(teacher_parts, teacher_protos, stream, row_index)[0]
    teacher_probs = jax.nn.softmax((teacher_logits - centre) / tau_teacher, axis=-1)
    centre_terms = jnp.sum(kept[:, None] * teacher_logits[:, 0], axis=0)
    student_flat, student_protos = (
        lax.all_gather(stem.astype(narrow), "dev", axis=0, tiled=True),
        lax.all_gather(protos.astype(narrow), "dev", axis=0, tiled=True),
    )
    student_parts = cut_flat(student_flat, stem_shapes())
    stream = embed(student_parts, patches, masked_here, True)
    saved_layers = []
    gathered_layers = []
    for layer_index in range(LAYERS):
        layer_flat = lax.all_gather(layers[layer_index].astype(narrow), "dev", axis=0, tiled=True)
        gathered_layers.append(layer_flat)
        stream, saved = block_forward(stream, cut_flat(layer_flat, layer_shapes()))
        saved_layers.append(saved)
    logits, head_saved = head_forward(student_parts, student_protos, stream, row_index)

    def loss_piece(logit_rows):
        log_probs = jax.nn.log_softmax(logit_rows / tau_student, axis=-1)
        cross = -jnp.sum(teacher_probs * log_probs, axis=-1)
        return jnp.sum(kept * (cross[:, 0] + jnp.mean(cross[:, 1:], axis=1)))

    loss_local, loss_puller = jax.vjp(loss_piece, logits)
    grad_logits = loss_puller(jnp.float32(1.0))[0]
    count_local = jnp.sum(kept)
    loss_total, count_total, centre_total = lax.psum((loss_local, count_local, centre_terms), "dev")
    back_flat, back_protos = (
        lax.all_gather(stem.astype(narrow), "dev", axis=0, tiled=True),
        lax.all_gather(protos.astype(narrow), "dev", axis=0, tiled=True),
    )
    back_parts = cut_flat(back_flat, stem_shapes())
    grad_stream, head_grads, grad_gain, grad_bias, grad_unit_protos = head_backward(
        grad_logits, back_parts, head_saved, row_index, stream.shape
    )
    layer_grads = []
    for layer_index in reversed(range(LAYERS)):
        weight_flat = lax.all_gather(layers[layer_index].astype(narrow), "dev", axis=0, tiled=True)
        grad_stream, block_grads = block_backward(
            grad_stream, cut_flat(weight_flat, layer_shapes()), saved_layers[layer_index]
        )
        layer_grads.insert(
            0,
            lax.psum_scatter(
                pack_flat(block_grads, weight_flat.shape[0]), "dev", scatter_dimension=0, tiled=True
            ),
        )
    grad_patch_w, grad_position, grad_cls, grad_mask_token = embed_backward(
        grad_stream, patches, masked_here
    )
    grad_extras = jnp.stack([grad_cls, grad_mask_token, grad_gain, grad_bias])
    stem_flat_grad = pack_flat(
        (grad_patch_w, grad_position, grad_extras) + head_grads, back_flat.shape[0]
    )
    stem_grad, proto_row_grad = (
        lax.psum_scatter(stem_flat_grad, "dev", scatter_dimension=0, tiled=True),
        lax.psum_scatter(grad_unit_protos, "dev", scatter_dimension=0, tiled=True),
    )
    own_protos = lax.optimization_barrier(protos.astype(narrow)).astype(single)
    proto_grad = jax.vjp(unit_rows, own_protos)[1](proto_row_grad)[0]
    layer_grad = jnp.stack(layer_grads)
    square_local = (
        jnp.sum(stem_grad * stem_grad)
        + jnp.sum(layer_grad * layer_grad)
        + jnp.sum(proto_grad * proto_grad)
    )
    square_total = lax.psum(square_local, "dev")
    grad_norm = jnp.sqrt(square_total) / count_total
    factor = jnp.minimum(1.0, clip_limit / (grad_norm + 1e-06)) / count_total
    new_centre = centre_keep * centre + (1.0 - centre_keep) * centre_total / count_total
    stem_set = adam_update(stem, stem_moment, stem_second, stem_grad * factor, stem_teacher)
    layer_set = adam_update(layers, layer_moment, layer_second, layer_grad * factor, layer_teacher)
    proto_set = adam_update(protos, proto_moment, proto_second, proto_grad * factor, proto_teacher)
    return (
        loss_total,
        count_total,
        grad_norm,
        new_centre,
        stem_set[0],
        stem_set[1],
        stem_set[2],
        stem_set[3],
        stem_set[4],
        layer_set[0],
        layer_set[1],
        layer_set[2],
        layer_set[3],
        layer_set[4],
        proto_set[0],
        proto_set[1],
        proto_set[2],
        proto_set[3],
        proto_set[4],
    )


GROUP = 16
ROW = HID
MATRIX_ROWS = D * 3 + D + FF + FF
EMBED_ROWS = PIX + SEQ + 4
EMBED_FLAT = EMBED_ROWS * D
HEAD_ROWS = D + HID + BOT
BITS = ("b", "a", "y", "x", "c")
MASKS = {"c": 1, "x": 2, "y": 4, "a": 8, "b": 24, "g": 8}


def head_bounds(count, stem_piece):
    bounds = [-(-(stem_piece * device - EMBED_FLAT) // (ROW * GROUP)) * GROUP for device in range(count + 1)]
    bounds[0] = -(-EMBED_FLAT // (ROW * GROUP)) * -GROUP
    bounds[-1] = HEAD_ROWS
    return bounds


def fits(count, stem_piece, layer_piece):
    if count != 1 << len(BITS) or MATRIX_ROWS % (3 * count):
        return False
    bounds = head_bounds(count, stem_piece)
    sizes = [bounds[i + 1] - bounds[i] for i in range(count)]
    return (
        min(sizes) > GROUP
        and bounds[1] <= 0
        and stem_piece < EMBED_FLAT <= 2 * stem_piece
        and D in bounds
        and D + HID in bounds
        and stem_piece * count == EMBED_FLAT + HEAD_ROWS * ROW
    )


def pairs(count, mask):
    return [(i, i ^ mask) for i in range(count)]


def bit_flags(me):
    flags = {name: (me >> (len(BITS) - 1 - place)) & 1 for place, name in enumerate(BITS)}
    flags["g"] = flags["a"] ^ flags["b"]
    return flags


def cube_gather(part, order):
    count = 1 << len(BITS)
    flags = bit_flags(lax.axis_index("dev"))
    held = part[None]
    for name in order:
        got = lax.ppermute(held, "dev", pairs(count, MASKS[name]))
        held = jnp.where(
            flags[name] == 1,
            jnp.concatenate([got, held], axis=0),
            jnp.concatenate([held, got], axis=0),
        )
    return held


def cut(array, names, name, lead):
    flag = bit_flags(lax.axis_index("dev"))[name] == 1
    place = names.index(name) + lead
    low = lax.index_in_dim(array, 0, place, keepdims=False)
    high = lax.index_in_dim(array, 1, place, keepdims=False)
    sent = jnp.where(flag, low, high)
    return (sent if name == "c" else sent.astype(narrow)), jnp.where(flag, high, low), names.replace(name, "")


def move(sent, kept, name):
    return kept + lax.ppermute(sent, "dev", pairs(1 << len(BITS), MASKS[name])).astype(single)


def cube_scatter(array, names, order, lead=0):
    for name in order:
        sent, kept, names = cut(array, names, name, lead)
        array = move(sent, kept, name)
    return array


def cube_sum(values):
    for name in "cxyab":
        values = values + lax.ppermute(values, "dev", pairs(1 << len(BITS), MASKS[name]))
    return values


def split_bits(array, lead=0):
    return array.reshape(array.shape[:lead] + (2,) * len(BITS) + array.shape[lead + 1 :])


def step_pairs(count, step):
    return [(i, i + step) for i in range(count) if 0 <= i + step < count]


def lane_rows(length):
    return -(-length // 1024) * 8


def as_lanes(flat):
    rows = lane_rows(flat.shape[-1])
    gap = rows * 128 - flat.shape[-1]
    padded = jnp.pad(flat, [(0, 0)] * (flat.ndim - 1) + [(0, gap)])
    return padded.reshape(flat.shape[:-1] + (rows, 128))


def shifted(line_ref, row, lane, first, rows, stride):
    spots = lax.broadcasted_iota(jnp.int32, (rows, 128), 1)
    turn = lax.rem(128 - lane, 128)
    here = pltpu.roll(line_ref[pl.ds(row + first, rows, stride=stride), :], turn, 1)
    there = pltpu.roll(line_ref[pl.ds(row + first + 1, rows, stride=stride), :], turn, 1)
    return jnp.where(spots < 128 - lane, here, there)


def blocks_kernel(
    shape,
    place_ref,
    stem_ref,
    after_ref,
    layer_ref,
    before_ref,
    head_ref,
    block_ref,
    embed_ref,
    vector_ref,
    line_ref,
    flat_ref,
):
    front, stem_piece, layer_piece, tail = shape
    stem_lines = stem_ref.shape[1]
    end_row, end_lane = stem_piece // 128, stem_piece % 128
    after_lines = after_ref.shape[1]
    slot = head_ref.shape[1]
    for model in range(2):
        line_ref[pl.ds(0, front), :] = jnp.zeros((front, 128), single)
        line_ref[pl.ds(front, end_row), :] = stem_ref[model, pl.ds(0, end_row), :]
        turned = pltpu.roll(after_ref[model], end_lane, 1)
        spots = lax.broadcasted_iota(jnp.int32, (after_lines, 128), 1)
        line_ref[pl.ds(front + end_row, after_lines), :] = turned
        line_ref[pl.ds(front + end_row + after_lines, 128), :] = jnp.zeros((128, 128), single)
        lower = pltpu.roll(turned, 1, 0)
        first_line = jnp.broadcast_to(stem_ref[model, pl.ds(end_row, 1), :], (after_lines, 128))
        number = lax.broadcasted_iota(jnp.int32, (after_lines, 128), 0)
        lower = jnp.where(number == 0, first_line, lower)
        line_ref[pl.ds(front + end_row, after_lines), :] = jnp.where(spots < end_lane, lower, turned)
        per_row = ROW // 128
        for chunk in range(per_row):
            head_ref[model, :, pl.ds(chunk * 128, 128)] = shifted(
                line_ref, place_ref[0], place_ref[1], chunk, slot, per_row
            ).astype(narrow)
        for chunk in range(D // 128):
            embed_ref[model, :, pl.ds(chunk * 128, 128)] = shifted(
                line_ref, place_ref[2], place_ref[3], chunk, embed_ref.shape[1], D // 128
            ).astype(narrow)
    tail_lines = tail // 128
    layer_lines = layer_ref.shape[1]
    vector_at = tail + layer_piece - tail
    for part in range(layer_ref.shape[0]):
        flat_ref[pl.ds(0, tail_lines), :] = before_ref[part]
        flat_ref[pl.ds(tail_lines, layer_lines), :] = layer_ref[part]
        for chunk in range(D // 128):
            block_ref[part, :, pl.ds(chunk * 128, 128)] = shifted(
                flat_ref, place_ref[4], place_ref[5], chunk, block_ref.shape[1], D // 128
            ).astype(narrow)
            vector_ref[part, :, pl.ds(chunk * 128, 128)] = shifted(
                flat_ref, vector_at // 128, vector_at % 128, chunk, 8, D // 128
            ).astype(narrow)


def own_blocks(place, stems, after, layer_rows, before, shape, slot, block_rows, embed_rows):
    front, stem_piece, layer_piece, tail = shape
    lines = front + stem_piece // 128 + after.shape[1] + slot * ROW // 128
    flats = tail // 128 + layer_rows.shape[1] + 48
    return pl.pallas_call(
        lambda *refs: blocks_kernel(shape, *refs),
        out_shape=[
            jax.ShapeDtypeStruct((2, slot, ROW), narrow),
            jax.ShapeDtypeStruct((2 * LAYERS, block_rows, D), narrow),
            jax.ShapeDtypeStruct((2, embed_rows, D), narrow),
            jax.ShapeDtypeStruct((2 * LAYERS, 8, D), narrow),
        ],
        in_specs=[pl.BlockSpec(memory_space=pltpu.SMEM)] + [pl.BlockSpec(memory_space=pltpu.VMEM)] * 4,
        out_specs=[pl.BlockSpec(memory_space=pltpu.VMEM)] * 4,
        scratch_shapes=[pltpu.VMEM((lines, 128), single), pltpu.VMEM((flats, 128), single)],
        compiler_params=pltpu.CompilerParams(vmem_limit_bytes=40 << 20),
    )(place, stems, after, layer_rows, before)


def shards_kernel(held, place_ref, head_ref, previous_ref, block_ref, behind_ref, *refs):
    stem_ref, layer_ref = refs[held : held + 2]
    line_ref, flat_ref = refs[-2:]
    per_row = ROW // 128
    extra = previous_ref.shape[0]
    slot = head_ref.shape[0]
    for chunk in range(per_row):
        spot = pl.ds(chunk * 128, 128)
        line_ref[pl.ds(chunk, extra, stride=per_row), :] = previous_ref[:, spot]
        line_ref[pl.ds(extra * per_row + chunk, slot, stride=per_row), :] = head_ref[:, spot]
    stem_ref[...] = shifted(line_ref, place_ref[0], place_ref[1], 0, stem_ref.shape[0], 1)
    per_row = D // 128
    rows = block_ref.shape[2]
    for part in range(block_ref.shape[0]):
        for chunk in range(per_row):
            flat_ref[pl.ds(chunk, rows, stride=per_row), :] = block_ref[part, chunk]
            flat_ref[pl.ds(rows * per_row + chunk, 6, stride=per_row), :] = behind_ref[part, chunk]
        layer_ref[part] = shifted(flat_ref, place_ref[2], place_ref[3], 0, layer_ref.shape[1], 1)


def own_shards(place, head_grad, previous, block_grad, behind, stem_lines, layer_lines, held):
    per_row = ROW // 128
    lines = (head_grad.shape[0] + previous.shape[0]) * per_row + 256
    flats = max(block_grad.shape[2] * 3 + 18, layer_lines + 18) + 16
    return pl.pallas_call(
        lambda *refs: shards_kernel(len(held), *refs),
        out_shape=[
            jax.ShapeDtypeStruct((stem_lines, 128), single),
            jax.ShapeDtypeStruct((block_grad.shape[0], layer_lines, 128), single),
        ]
        + [jax.ShapeDtypeStruct(array.shape, array.dtype) for array in held],
        in_specs=[pl.BlockSpec(memory_space=pltpu.SMEM)]
        + [pl.BlockSpec(memory_space=pltpu.VMEM)] * 4
        + [pl.BlockSpec(memory_space=pl.ANY)] * len(held),
        out_specs=[pl.BlockSpec(memory_space=pltpu.VMEM)] * 2 + [pl.BlockSpec(memory_space=pl.ANY)] * len(held),
        input_output_aliases={5 + number: 2 + number for number in range(len(held))},
        scratch_shapes=[pltpu.VMEM((lines, 128), single), pltpu.VMEM((flats, 128), single)],
        compiler_params=pltpu.CompilerParams(vmem_limit_bytes=40 << 20),
    )(place, head_grad, previous, block_grad, behind, *held)


PAD_SEQ = 272
GELU_SCALE = 0.7978845608028654
GELU_CUBE = 0.044715


def product_plain(left, right):
    return lax.dot_general(left, right, (((1,), (0,)), ((), ())), preferred_element_type=single)


def product_right(left, right):
    return lax.dot_general(left, right, (((1,), (1,)), ((), ())), preferred_element_type=single)


def product_left(left, right):
    return lax.dot_general(left, right, (((0,), (0,)), ((), ())), preferred_element_type=single)


def norm_parts(values):
    centred = values - jnp.mean(values, axis=-1, keepdims=True)
    spread = lax.rsqrt(jnp.mean(centred * centred, axis=-1, keepdims=True) + 1e-06)
    return centred * spread, spread


def norm_back(grad, unit, spread, gain):
    grad_unit = grad * gain
    mean_one = jnp.mean(grad_unit, axis=-1, keepdims=True)
    mean_two = jnp.mean(grad_unit * unit, axis=-1, keepdims=True)
    return spread * (grad_unit - mean_one - unit * mean_two)


def gelu_tanh(values):
    return jnp.tanh(GELU_SCALE * (values + GELU_CUBE * values * values * values))


def gelu_value(values):
    return 0.5 * values * (1.0 + gelu_tanh(values))


def gelu_slope(values):
    bent = gelu_tanh(values)
    return 0.5 * (1.0 + bent) + 0.5 * values * (1.0 - bent * bent) * GELU_SCALE * (
        1.0 + 3.0 * GELU_CUBE * values * values
    )


def head_copies(plan, side_ref, gathered_ref, one_ref, two_ref, lines_ref, sems):
    quarter = gathered_ref.shape[0] // 2
    shift = side_ref[0] * quarter
    targets = (one_ref, two_ref, lines_ref)
    copies = []
    for number, (at, owner, first, rows, target, row) in enumerate(plan):
        spot = at + shift if at < quarter else at - shift
        copies.append(
            pltpu.make_async_copy(
                gathered_ref.at[spot, owner, pl.ds(first, rows)],
                targets[target].at[pl.ds(row, rows)],
                sems.at[number],
            )
        )
    for copy in copies:
        copy.start()
    return [[copy for copy, item in zip(copies, plan) if item[4] == target] for target in range(3)]


def wait_all(copies):
    for copy in copies:
        copy.wait()


def spread_third(lines_ref, wide_ref, third_ref):
    groups = ROW // BOT
    for lane in range(BOT // 128):
        for group in range(groups):
            at = group * BOT + lane * 128
            wide_ref[lane, pl.ds(group, lines_ref.shape[0], stride=groups), :] = lines_ref[
                :, at : at + 128
            ].astype(single)
        third_ref[:, pl.ds(lane * 128, 128)] = wide_ref[lane].astype(narrow)


def head_up_kernel(
    plan, side_ref, normed_ref, gathered_ref, unit_ref, acts_ref, bottle_ref, pre_one_ref, pre_two_ref,
    one_ref, two_ref, lines_ref, wide_ref, third_ref, sems,
):
    copies = head_copies(plan, side_ref, gathered_ref, one_ref, two_ref, lines_ref, sems)
    acts_ref[...] = jnp.zeros_like(acts_ref)
    normed = normed_ref[...]
    acts_ref[:, pl.ds(0, D)] = normed
    piece = HID // 4
    wait_all(copies[0])
    for number in range(4):
        spot = pl.ds(number * piece, piece)
        pre = product_plain(normed, one_ref[:, spot])
        pre_one_ref[:, spot] = pre
        acts_ref[:, pl.ds(D + number * piece, piece)] = gelu_value(pre).astype(narrow)
    wait_all(copies[2])
    spread_third(lines_ref, wide_ref, third_ref)
    wait_all(copies[1])
    hidden = acts_ref[:, pl.ds(D, HID)]
    for number in range(4):
        spot = pl.ds(number * piece, piece)
        pre = product_plain(hidden, two_ref[:, spot])
        pre_two_ref[:, spot] = pre
        acts_ref[:, pl.ds(D + HID + number * piece, piece)] = gelu_value(pre).astype(narrow)
    bottle = product_plain(acts_ref[:, pl.ds(D + HID, HID)], third_ref[...])
    bottle_ref[...] = bottle
    unit_ref[...] = (
        bottle * lax.rsqrt(jnp.sum(bottle * bottle, axis=-1, keepdims=True) + 1e-06)
    ).astype(narrow)


def head_down_kernel(
    plan, side_ref, grad_ref, bottle_ref, pre_one_ref, pre_two_ref, gathered_ref, grads_ref, normed_grad_ref,
    one_ref, two_ref, lines_ref, wide_ref, third_ref, sems,
):
    copies = head_copies(plan, side_ref, gathered_ref, one_ref, two_ref, lines_ref, sems)
    grad, bottle = grad_ref[...], bottle_ref[...]
    scale = lax.rsqrt(jnp.sum(bottle * bottle, axis=-1, keepdims=True) + 1e-06)
    along = jnp.sum(grad * bottle, axis=-1, keepdims=True)
    grad_bottle = (scale * (grad - bottle * (along * scale * scale))).astype(narrow)
    grads_ref[:, pl.ds(2 * HID, BOT)] = grad_bottle
    wait_all(copies[2])
    spread_third(lines_ref, wide_ref, third_ref)
    piece = HID // 4
    for number in range(4):
        spot = pl.ds(number * piece, piece)
        back = product_right(grad_bottle, third_ref[spot, :])
        grads_ref[:, pl.ds(HID + number * piece, piece)] = (back * gelu_slope(pre_two_ref[:, spot])).astype(narrow)
    wait_all(copies[1])
    grad_two = grads_ref[:, pl.ds(HID, HID)]
    for number in range(4):
        spot = pl.ds(number * piece, piece)
        back = product_right(grad_two, two_ref[spot, :])
        grads_ref[:, spot] = (back * gelu_slope(pre_one_ref[:, spot])).astype(narrow)
    wait_all(copies[0])
    normed_grad_ref[...] = product_right(grads_ref[:, pl.ds(0, HID)], one_ref[...])


def head_pass(kernel, plan, side, inputs, gathered, shapes, waits=()):
    read = len(inputs) + 2
    return pl.pallas_call(
        lambda *refs: kernel(plan, *refs[:read], *refs[read + len(waits) :]),
        out_shape=shapes,
        in_specs=[pl.BlockSpec(memory_space=pltpu.SMEM)]
        + [pl.BlockSpec(memory_space=pltpu.VMEM)] * len(inputs)
        + [pl.BlockSpec(memory_space=pl.ANY)] * (1 + len(waits)),
        out_specs=[pl.BlockSpec(memory_space=pltpu.VMEM)] * len(shapes),
        scratch_shapes=[
            pltpu.VMEM((D, HID), narrow),
            pltpu.VMEM((HID, HID), narrow),
            pltpu.VMEM((BOT, ROW), narrow),
            pltpu.VMEM((BOT // 128, HID, 128), single),
            pltpu.VMEM((HID, BOT), narrow),
            pltpu.SemaphoreType.DMA((len(plan),)),
        ],
        compiler_params=pltpu.CompilerParams(vmem_limit_bytes=56 << 20),
        cost_estimate=pl.CostEstimate(flops=100 * 10**6, bytes_accessed=370 * 10**5, transcendentals=0),
    )(side, *inputs, gathered, *waits)


def fetch_rows(side_ref, part, gathered_ref, flat_ref, sems):
    quarter = flat_ref.shape[0] // 4
    side = side_ref[0]
    first, second = side * quarter, (1 - side) * quarter
    copies = [
        pltpu.make_async_copy(
            gathered_ref.at[pl.ds(at, quarter), owner, part],
            flat_ref.at[pl.ds(spot * quarter, quarter)],
            sems.at[spot],
        )
        for spot, (at, owner) in enumerate(((first, 0), (second, 0), (second, 1), (first, 1)))
    ]
    for copy in copies:
        copy.start()
    for copy in copies:
        copy.wait()


def matrix_rows(flat_ref, first_row, length):
    rows = flat_ref.shape[1]
    low, high = first_row // rows, -(-(first_row + length) // rows)
    lines = flat_ref[pl.ds(low, high - low)].reshape((high - low) * rows, D)
    at = first_row - low * rows
    return lines[at : at + length]


def spread_columns(flat_ref, first_row, width, wide_ref, out_ref):
    length = width * D
    lines = matrix_rows(flat_ref, first_row, length)
    for column in range(D // 128):
        lane = slice(column * 128, (column + 1) * 128)
        wide_ref[column, pl.ds(0, length), :] = lines[:, lane].astype(single)
    for group in range(width):
        for column in range(D // 128):
            out_ref[group, :, pl.ds(column * 128, 128)] = wide_ref[
                column, pl.ds(group, D, stride=width), :
            ].astype(narrow)


def head_lanes(values, odd):
    lanes = lax.broadcasted_iota(jnp.int32, values.shape, 1)
    return jnp.where((lanes >= HEAD_DIM) == odd, values, jnp.zeros_like(values))


def join_lanes(even, odd):
    lanes = lax.broadcasted_iota(jnp.int32, even.shape, 1)
    return jnp.where(lanes >= HEAD_DIM, odd, even)


def soft_rows(query, key):
    scores = product_right(query, key) * HEAD_DIM ** (-0.5)
    spots = lax.broadcasted_iota(jnp.int32, scores.shape, 1)
    scores = jnp.where(spots < SEQ, scores, -1e30)
    terms = jnp.exp(scores - jnp.max(scores, axis=-1, keepdims=True))
    return terms / jnp.sum(terms, axis=-1, keepdims=True)


def forward_kernel(part, keep, side_ref, stream_ref, vector_ref, gathered_ref, *refs):
    out_ref = refs[0]
    if keep:
        packed_ref, mixed_ref, attn_ref, pre_ref, mlp_ref = refs[1:6]
        flat_ref, wide_ref, qkv_ref, up_ref, hidden_ref, sems = refs[6:]
    else:
        flat_ref, wide_ref, qkv_ref, up_ref, hidden_ref, packed_ref, mixed_ref, sems = refs[1:]
    fetch_rows(side_ref, part, gathered_ref, flat_ref, sems)
    spread_columns(flat_ref, 0, 3, wide_ref, qkv_ref)
    spread_columns(flat_ref, 4 * D, FF // D, wide_ref, up_ref)
    w_proj = matrix_rows(flat_ref, 3 * D, D)
    w_down = matrix_rows(flat_ref, 4 * D + FF, FF)
    vectors = vector_ref[...].astype(single)
    stream = stream_ref[...]
    normed = (norm_parts(stream)[0] * vectors[0:1] + vectors[1:2]).astype(narrow)
    for group in range(3):
        packed_ref[:, pl.ds(group * D, D)] = product_plain(normed, qkv_ref[group]).astype(narrow)
    for image in range(stream.shape[0] // PAD_SEQ):
        rows = pl.ds(image * PAD_SEQ, PAD_SEQ)
        for pair in range(HEADS // 2):
            query, key, value = [
                packed_ref[rows, pl.ds(group * D + pair * 128, 128)] for group in range(3)
            ]
            done = [
                product_plain(soft_rows(head_lanes(query, odd), key).astype(narrow), value)
                for odd in (False, True)
            ]
            mixed_ref[rows, pl.ds(pair * 128, 128)] = join_lanes(*done).astype(narrow)
    attn = product_plain(mixed_ref[...], w_proj)
    middle = stream + vectors[2:3] * attn
    normed_two = (norm_parts(middle)[0] * vectors[3:4] + vectors[4:5]).astype(narrow)
    for group in range(FF // D):
        spot = pl.ds(group * D, D)
        pre = product_plain(normed_two, up_ref[group])
        if keep:
            pre_ref[:, spot] = pre
        hidden_ref[:, spot] = (0.5 * pre * (1.0 + gelu_tanh(pre))).astype(narrow)
    mlp = product_plain(hidden_ref[...], w_down)
    out_ref[...] = middle + vectors[5:6] * mlp
    if keep:
        attn_ref[...] = attn
        mlp_ref[...] = mlp


def layer_scratch(gathered):
    rows, blocks = gathered.shape[3], 2 * gathered.shape[0]
    return [
        pltpu.VMEM((blocks, rows, D), narrow),
        pltpu.VMEM((D // 128, FF, 128), single),
        pltpu.VMEM((3, D, D), narrow),
        pltpu.VMEM((FF // D, D, D), narrow),
    ]


def layer_specs_in(count):
    return (
        [pl.BlockSpec(memory_space=pltpu.SMEM)]
        + [pl.BlockSpec(memory_space=pltpu.VMEM)] * (count - 2)
        + [pl.BlockSpec(memory_space=pl.ANY)]
    )


def layer_forward(side, stream, vectors, gathered, part, keep):
    tokens = stream.shape[0]
    shapes = [jax.ShapeDtypeStruct((tokens, D), single)]
    extra = [
        jax.ShapeDtypeStruct((tokens, 3 * D), narrow),
        jax.ShapeDtypeStruct((tokens, D), narrow),
        jax.ShapeDtypeStruct((tokens, D), single),
        jax.ShapeDtypeStruct((tokens, FF), single),
        jax.ShapeDtypeStruct((tokens, D), single),
    ]
    scratch = layer_scratch(gathered) + [pltpu.VMEM((tokens, FF), narrow)]
    if keep:
        shapes = shapes + extra
    else:
        scratch = scratch + [pltpu.VMEM((tokens, 3 * D), narrow), pltpu.VMEM((tokens, D), narrow)]
    scratch.append(pltpu.SemaphoreType.DMA((4,)))
    return pl.pallas_call(
        lambda *refs: forward_kernel(part, keep, *refs),
        out_shape=shapes,
        in_specs=layer_specs_in(4),
        out_specs=[pl.BlockSpec(memory_space=pltpu.VMEM)] * len(shapes),
        scratch_shapes=scratch,
        compiler_params=pltpu.CompilerParams(vmem_limit_bytes=56 << 20),
        cost_estimate=pl.CostEstimate(flops=100 * 10**6, bytes_accessed=430 * 10**5, transcendentals=0),
    )(side, stream, vectors, gathered)


def mlp_back_kernel(
    part,
    side_ref,
    grad_ref,
    stream_ref,
    attn_ref,
    pre_ref,
    mlp_ref,
    vector_ref,
    gathered_ref,
    *refs,
):
    grad_mid_ref, weight_grad_ref, vector_grad_ref = refs[-9:-6]
    flat_ref, wide_ref, up_ref, hidden_ref, grad_pre_ref, sems = refs[-6:]
    lead = weight_grad_ref.shape[1] - 2 * FF
    weight_grad_ref[:, pl.ds(0, lead), :] = jnp.zeros((D // 128, lead, 128), single)
    fetch_rows(side_ref, part, gathered_ref, flat_ref, sems)
    spread_columns(flat_ref, 4 * D, FF // D, wide_ref, up_ref)
    w_down = matrix_rows(flat_ref, 4 * D + FF, FF)
    vectors = vector_ref[...].astype(single)
    grad_out = grad_ref[...]
    vector_grad_ref[...] = jnp.zeros_like(vector_grad_ref)
    attn = attn_ref[...]
    middle = stream_ref[...] + vectors[2:3] * attn
    unit_two, spread_two = norm_parts(middle)
    normed_two = (unit_two * vectors[3:4] + vectors[4:5]).astype(narrow)
    vector_grad_ref[pl.ds(5, 1), :] = jnp.sum(grad_out * mlp_ref[...], axis=0, keepdims=True)
    grad_mlp = (grad_out * vectors[5:6]).astype(narrow)
    grad_normed_two = jnp.zeros_like(grad_out)
    for group in range(FF // D):
        spot = pl.ds(group * D, D)
        pre = pre_ref[:, spot]
        bent = gelu_tanh(pre)
        hidden_ref[:, spot] = (0.5 * pre * (1.0 + bent)).astype(narrow)
        slope = 0.5 * (1.0 + bent) + 0.5 * pre * (1.0 - bent * bent) * GELU_SCALE * (
            1.0 + 3.0 * GELU_CUBE * pre * pre
        )
        grad_hidden = product_right(grad_mlp, w_down[group * D : (group + 1) * D])
        grad_pre = (grad_hidden * slope).astype(narrow)
        grad_pre_ref[:, spot] = grad_pre
        grad_normed_two = grad_normed_two + product_right(grad_pre, up_ref[group])
    for group in range(FF // D):
        spot = pl.ds(group * D, D)
        up_grad = product_left(normed_two, grad_pre_ref[:, spot])
        down_grad = product_left(hidden_ref[:, spot], grad_mlp)
        for column in range(D // 128):
            lane = slice(column * 128, (column + 1) * 128)
            weight_grad_ref[column, pl.ds(lead + group, D, stride=FF // D), :] = up_grad[:, lane]
            weight_grad_ref[column, pl.ds(lead + FF + group * D, D), :] = down_grad[:, lane]
    vector_grad_ref[pl.ds(3, 1), :] = jnp.sum(grad_normed_two * unit_two, axis=0, keepdims=True)
    vector_grad_ref[pl.ds(4, 1), :] = jnp.sum(grad_normed_two, axis=0, keepdims=True)
    grad_mid = grad_out + norm_back(grad_normed_two, unit_two, spread_two, vectors[3:4])
    vector_grad_ref[pl.ds(2, 1), :] = jnp.sum(grad_mid * attn, axis=0, keepdims=True)
    grad_mid_ref[...] = grad_mid


def attention_back_kernel(
    part,
    side_ref,
    grad_ref,
    stream_ref,
    packed_ref,
    mixed_ref,
    vector_ref,
    gathered_ref,
    *refs,
):
    grad_in_ref, weight_grad_ref, vector_grad_ref = refs[-9:-6]
    flat_ref, wide_ref, qkv_ref, grad_mixed_ref, grad_packed_ref, sems = refs[-6:]
    rest = weight_grad_ref.shape[1] - 4 * D
    weight_grad_ref[:, pl.ds(4 * D, rest), :] = jnp.zeros((D // 128, rest, 128), single)
    fetch_rows(side_ref, part, gathered_ref, flat_ref, sems)
    spread_columns(flat_ref, 0, 3, wide_ref, qkv_ref)
    w_proj = matrix_rows(flat_ref, 3 * D, D)
    vectors = vector_ref[...].astype(single)
    vector_grad_ref[...] = jnp.zeros_like(vector_grad_ref)
    grad_mid = grad_ref[...]
    stream = stream_ref[...]
    grad_attn = (grad_mid * vectors[2:3]).astype(narrow)
    proj_grad = product_left(mixed_ref[...], grad_attn)
    for column in range(D // 128):
        weight_grad_ref[column, pl.ds(3 * D, D), :] = proj_grad[:, column * 128 : (column + 1) * 128]
    grad_mixed_ref[...] = product_right(grad_attn, w_proj).astype(narrow)
    for image in range(stream.shape[0] // PAD_SEQ):
        rows = pl.ds(image * PAD_SEQ, PAD_SEQ)
        for pair in range(HEADS // 2):
            query, key, value = [
                packed_ref[rows, pl.ds(group * D + pair * 128, 128)] for group in range(3)
            ]
            grad_mixed = grad_mixed_ref[rows, pl.ds(pair * 128, 128)]
            parts = []
            for odd in (False, True):
                probs = soft_rows(head_lanes(query, odd), key)
                grad_probs = product_right(head_lanes(grad_mixed, odd), value)
                grad_value = product_left(probs.astype(narrow), grad_mixed)
                grad_scores = probs * (grad_probs - jnp.sum(probs * grad_probs, axis=-1, keepdims=True))
                grad_raw = (grad_scores * HEAD_DIM ** (-0.5)).astype(narrow)
                parts.append((product_plain(grad_raw, key), product_left(grad_raw, query), grad_value))
            for group in range(3):
                grad_packed_ref[rows, pl.ds(group * D + pair * 128, 128)] = join_lanes(
                    parts[0][group], parts[1][group]
                ).astype(narrow)
    unit_one, spread_one = norm_parts(stream)
    normed = (unit_one * vectors[0:1] + vectors[1:2]).astype(narrow)
    grad_normed = jnp.zeros_like(grad_mid)
    for group in range(3):
        grad_part = grad_packed_ref[:, pl.ds(group * D, D)]
        grad_normed = grad_normed + product_right(grad_part, qkv_ref[group])
        qkv_grad = product_left(normed, grad_part)
        for column in range(D // 128):
            lane = slice(column * 128, (column + 1) * 128)
            weight_grad_ref[column, pl.ds(group, D, stride=3), :] = qkv_grad[:, lane]
    vector_grad_ref[pl.ds(0, 1), :] = jnp.sum(grad_normed * unit_one, axis=0, keepdims=True)
    vector_grad_ref[pl.ds(1, 1), :] = jnp.sum(grad_normed, axis=0, keepdims=True)
    grad_in_ref[...] = grad_mid + norm_back(grad_normed, unit_one, spread_one, vectors[0:1])


def layer_back(kernel, part, weight_rows, side, inputs, vectors, gathered, waits, columns, buffers):
    tokens = inputs[0].shape[0]
    rows, blocks = gathered.shape[3], 2 * gathered.shape[0]
    return pl.pallas_call(
        lambda *refs: kernel(part, *refs),
        out_shape=[
            jax.ShapeDtypeStruct((tokens, D), single),
            jax.ShapeDtypeStruct((D // 128, weight_rows, 128), single),
            jax.ShapeDtypeStruct((8, D), single),
        ],
        in_specs=layer_specs_in(len(inputs) + 3) + [pl.BlockSpec(memory_space=pl.ANY)] * len(waits),
        out_specs=[pl.BlockSpec(memory_space=pltpu.VMEM)] * 3,
        scratch_shapes=[
            pltpu.VMEM((blocks, rows, D), narrow),
            pltpu.VMEM((D // 128, columns * D, 128), single),
            pltpu.VMEM((columns, D, D), narrow),
        ]
        + [pltpu.VMEM((tokens, width), narrow) for width in buffers]
        + [pltpu.SemaphoreType.DMA((4,))],
        compiler_params=pltpu.CompilerParams(vmem_limit_bytes=56 << 20),
        cost_estimate=pl.CostEstimate(flops=100 * 10**6, bytes_accessed=600 * 10**5, transcendentals=0),
    )(side, *inputs, vectors, gathered, *waits)


def pair_rows_of(block_rows):
    pair = 2 * block_rows
    return 4 * D // pair * pair, -(-4 * D // pair) * pair


def mlp_back(side, grad_out, saved, vectors, gathered, part, waits):
    stream, packed, mixed, attn, pre, mlp = saved
    return layer_back(
        mlp_back_kernel, part, MATRIX_ROWS - pair_rows_of(gathered.shape[3])[0], side,
        (grad_out, stream, attn, pre, mlp), vectors, gathered, waits,
        FF // D, (FF, FF),
    )


def attention_back(side, grad_mid, saved, vectors, gathered, part, waits):
    stream, packed, mixed, attn, pre, mlp = saved
    return layer_back(
        attention_back_kernel, part, pair_rows_of(gathered.shape[3])[1], side,
        (grad_mid, stream, packed, mixed), vectors, gathered, waits,
        3, (D, 3 * D),
    )


def after(value, *tokens):
    def kernel(*refs):
        refs[-1][...] = refs[0][...]

    return pl.pallas_call(
        kernel,
        out_shape=jax.ShapeDtypeStruct(value.shape, value.dtype),
        in_specs=[pl.BlockSpec(memory_space=pltpu.VMEM)] + [pl.BlockSpec(memory_space=pl.ANY)] * len(tokens),
        out_specs=pl.BlockSpec(memory_space=pltpu.VMEM),
    )(value, *tokens)


def embed_back_kernel(grad_ref, patch_ref, shown_ref, gain_ref, vector_ref, *refs):
    out_ref = refs[-1]
    grad = grad_ref[...]
    images = grad.shape[0] // PAD_SEQ
    shown = shown_ref[...]
    position = jnp.zeros((PAD_SEQ, D), single)
    token = jnp.zeros((1, D), single)
    patch_grads = []
    for image in range(images):
        here = grad[image * PAD_SEQ : (image + 1) * PAD_SEQ]
        position = position + here
        rows = here[1:SEQ]
        seen = shown[image * PATCHES : (image + 1) * PATCHES]
        token = token + jnp.sum(rows * (1.0 - seen), axis=0, keepdims=True)
        patch_grads.append((rows * seen).astype(narrow))
    patch_grad = product_left(patch_ref[...], jnp.concatenate(patch_grads))
    out_ref[...] = jnp.zeros_like(out_ref)
    for column in range(D // 128):
        lane = slice(column * 128, (column + 1) * 128)
        out_ref[column, pl.ds(0, PIX), :] = patch_grad[:, lane]
        out_ref[column, pl.ds(PIX, SEQ), :] = position[:SEQ, lane]
        out_ref[column, pl.ds(PIX + SEQ, 1), :] = position[0:1, lane]
        out_ref[column, pl.ds(PIX + SEQ + 1, 1), :] = token[:, lane]
        out_ref[column, pl.ds(PIX + SEQ + 2, 2), :] = gain_ref[:, lane]
        out_ref[column, pl.ds(EMBED_ROWS, vector_ref.shape[0]), :] = vector_ref[:, lane]


def embed_back(grad, patch_rows, shown, gains, vector_grads, rows, waits):
    return pl.pallas_call(
        embed_back_kernel,
        out_shape=jax.ShapeDtypeStruct((D // 128, rows, 128), single),
        in_specs=[pl.BlockSpec(memory_space=pltpu.VMEM)] * 5 + [pl.BlockSpec(memory_space=pl.ANY)] * len(waits),
        out_specs=pl.BlockSpec(memory_space=pltpu.VMEM),
        compiler_params=pltpu.CompilerParams(vmem_limit_bytes=40 << 20),
        cost_estimate=pl.CostEstimate(flops=100 * 10**6, bytes_accessed=37 * 10**5, transcendentals=0),
    )(grad, patch_rows, shown, gains, vector_grads, *waits)


def proto_units(values):
    rounded = values.astype(narrow).astype(single)
    scale = lax.rsqrt(jnp.sum(rounded * rounded, axis=-1, keepdims=True) + 1e-06)
    return rounded, scale, (rounded * scale).astype(narrow)


def proto_terms(teacher_z, student_z, teacher_unit, student_unit, centre_column):
    teacher_logits = product_right(teacher_unit, teacher_z)
    logits = product_right(student_unit, student_z)
    teacher_exp = jnp.exp((teacher_logits - centre_column) * (1.0 / tau_teacher))
    student_exp = jnp.exp(logits * (1.0 / tau_student))
    return teacher_logits, logits, teacher_exp, student_exp


def logits_kernel(
    teacher_z_ref,
    student_z_ref,
    teacher_ref,
    student_ref,
    centre_ref,
    class_ref,
    mixed_ref,
    sums_ref,
    centre_sum_ref,
    student_mix_ref,
    teacher_mix_ref,
    totals_ref,
):
    step = pl.program_id(0)

    @pl.when(step == 0)
    def _():
        student_mix_ref[...] = jnp.zeros_like(student_mix_ref)
        teacher_mix_ref[...] = jnp.zeros_like(teacher_mix_ref)
        totals_ref[...] = jnp.zeros_like(totals_ref)

    teacher_unit = proto_units(teacher_ref[...])[2]
    student_unit = proto_units(student_ref[...])[2]
    teacher_logits, logits, teacher_exp, student_exp = proto_terms(
        teacher_z_ref[...], student_z_ref[...], teacher_unit, student_unit, centre_ref[...]
    )
    totals_ref[pl.ds(0, 1), :] += jnp.sum(teacher_exp, axis=0, keepdims=True)
    totals_ref[pl.ds(1, 1), :] += jnp.sum(student_exp, axis=0, keepdims=True)
    totals_ref[pl.ds(2, 1), :] += jnp.sum(teacher_exp * logits, axis=0, keepdims=True)
    centre_sum_ref[...] = jnp.sum(teacher_logits * class_ref[0:1], axis=1, keepdims=True)
    student_mix_ref[...] += product_left(student_unit, student_exp.astype(narrow))
    teacher_mix_ref[...] += product_left(student_unit, teacher_exp.astype(narrow))

    @pl.when(step == pl.num_programs(0) - 1)
    def _():
        mixed_ref[:, pl.ds(0, BOT)] = student_mix_ref[...].T
        mixed_ref[:, pl.ds(BOT, BOT)] = teacher_mix_ref[...].T
        lower = jnp.zeros((128 - totals_ref.shape[0], totals_ref.shape[1]), single)
        mixed_ref[:, pl.ds(2 * BOT, 128)] = jnp.concatenate([totals_ref[...], lower]).T
        sums_ref[...] = totals_ref[...]


def proto_specs(rows, block):
    whole = pl.BlockSpec((rows, BOT), lambda i: (0, 0))
    table = pl.BlockSpec((block, BOT), lambda i: (i, 0))
    column = pl.BlockSpec((block, 1), lambda i: (i, 0))
    lines = pl.BlockSpec((8, rows), lambda i: (0, 0))
    return whole, table, column, lines


def logits_pass(teacher_z, student_z, teacher, student, centre_column, class_lines):
    rows, protos_here = teacher_z.shape[0], student.shape[0]
    block = protos_here // 4
    whole, table, column, lines = proto_specs(rows, block)
    return pl.pallas_call(
        logits_kernel,
        grid=(4,),
        out_shape=[
            jax.ShapeDtypeStruct((rows, 2 * BOT + 128), single),
            jax.ShapeDtypeStruct((8, rows), single),
            jax.ShapeDtypeStruct((protos_here, 1), single),
        ],
        in_specs=[whole, whole, table, table, column, lines],
        out_specs=[pl.BlockSpec((rows, 2 * BOT + 128), lambda i: (0, 0)), lines, column],
        scratch_shapes=[
            pltpu.VMEM((BOT, rows), single),
            pltpu.VMEM((BOT, rows), single),
            pltpu.VMEM((8, rows), single),
        ],
        compiler_params=pltpu.CompilerParams(vmem_limit_bytes=56 << 20),
        cost_estimate=pl.CostEstimate(flops=100 * 10**6, bytes_accessed=520 * 10**5, transcendentals=0),
    )(teacher_z, student_z, teacher, student, centre_column, class_lines)


def proto_grad_kernel(
    held, teacher_z_ref, student_z_ref, teacher_ref, student_ref, centre_ref, scale_ref, *refs
):
    grad_ref, square_ref = refs[held : held + 2]
    step = pl.program_id(0)

    @pl.when(step == 0)
    def _():
        square_ref[...] = jnp.zeros_like(square_ref)

    teacher_unit = proto_units(teacher_ref[...])[2]
    rounded, scale, student_unit = proto_units(student_ref[...])
    student_z = student_z_ref[...]
    _, _, teacher_exp, student_exp = proto_terms(
        teacher_z_ref[...], student_z, teacher_unit, student_unit, centre_ref[...]
    )
    grad_logits = (student_exp * scale_ref[0:1] - teacher_exp * scale_ref[1:2]).astype(narrow)
    unit_grad = product_plain(grad_logits, student_z)
    along = jnp.sum(unit_grad * rounded, axis=-1, keepdims=True)
    grad = scale * (unit_grad - rounded * (along * scale * scale))
    grad_ref[...] = grad
    square_ref[...] += jnp.broadcast_to(jnp.sum(grad * grad), square_ref.shape)


def proto_grad_pass(teacher_z, student_z, teacher, student, centre_column, scale_lines, held):
    rows, protos_here = teacher_z.shape[0], student.shape[0]
    block = protos_here // 4
    whole, table, column, lines = proto_specs(rows, block)
    return pl.pallas_call(
        lambda *refs: proto_grad_kernel(len(held), *refs),
        grid=(4,),
        out_shape=[
            jax.ShapeDtypeStruct((protos_here, BOT), single),
            jax.ShapeDtypeStruct((8, 128), single),
        ]
        + [jax.ShapeDtypeStruct(array.shape, array.dtype) for array in held],
        in_specs=[whole, whole, table, table, column, lines]
        + [pl.BlockSpec(memory_space=pl.ANY)] * len(held),
        out_specs=[table, pl.BlockSpec((8, 128), lambda i: (0, 0))]
        + [pl.BlockSpec(memory_space=pl.ANY)] * len(held),
        input_output_aliases={6 + number: 2 + number for number in range(len(held))},
        compiler_params=pltpu.CompilerParams(vmem_limit_bytes=56 << 20),
        cost_estimate=pl.CostEstimate(flops=100 * 10**6, bytes_accessed=400 * 10**5, transcendentals=0),
    )(teacher_z, student_z, teacher, student, centre_column, scale_lines, *held)


def proto_update(factor, student, moment, second, teacher, grad):
    def kernel(factor_ref, *refs):
        weight, moment, second, teacher, grad = [ref[...] for ref in refs[:5]]
        done = adam_update(weight, moment, second, grad * factor_ref[0], teacher)
        for ref, value in zip(refs[5:], done):
            ref[...] = value

    block = student.shape[0] // 4
    table = pl.BlockSpec((block, BOT), lambda i: (i, 0))
    return pl.pallas_call(
        kernel,
        grid=(4,),
        out_shape=[
            jax.ShapeDtypeStruct(student.shape, narrow if number == 3 else single) for number in range(5)
        ],
        in_specs=[pl.BlockSpec(memory_space=pltpu.SMEM)] + [table] * 5,
        out_specs=[table] * 5,
        compiler_params=pltpu.CompilerParams(vmem_limit_bytes=40 << 20),
        cost_estimate=pl.CostEstimate(flops=10**7, bytes_accessed=2 * 10**7, transcendentals=0),
    )(factor.reshape(1), student, moment, second, teacher, grad)


def head_grads_kernel(
    held, place_ref, inputs_ref, grads_ref, *refs,
):
    own_ref, partner_ref = refs[len(refs) - 9 - held :][:2] if held else refs[-9:-7]
    window_ref, rows_ref, product_ref, third_ref, bottle_ref, line_ref, sems = refs[-7:]
    slot = own_ref.shape[0]
    lead = product_ref.shape[0] - window_ref.shape[1]
    number = lax.broadcasted_iota(jnp.int32, (slot, 1), 0)
    product_ref[pl.ds(0, lead), :] = jnp.zeros((lead, ROW), single)

    def block(at, out_ref):
        column = pl.multiple_of(place_ref[at], 128)
        grad_column = pl.multiple_of(place_ref[at + 3], 128)
        copies = [
            pltpu.make_async_copy(
                inputs_ref.at[:, pl.ds(column, window_ref.shape[1])], window_ref, sems.at[0]
            ),
            pltpu.make_async_copy(grads_ref.at[:, pl.ds(grad_column, ROW)], rows_ref, sems.at[1]),
        ]
        for copy in copies:
            copy.start()
        for copy in copies:
            copy.wait()
        window = window_ref[...]
        for piece in range(4):
            spot = pl.ds(piece * (ROW // 4), ROW // 4)
            product_ref[pl.ds(lead, window.shape[1]), spot] = product_left(window, rows_ref[:, spot])
        from_row = pl.multiple_of(lead + place_ref[at + 1], 8)
        kept = jnp.where(number < place_ref[at + 2], product_ref[pl.ds(from_row, slot), :], 0.0)
        out_ref[...] = kept.astype(out_ref.dtype)

    @pl.when(place_ref[8] == 0)
    def _():
        block(0, own_ref)

    @pl.when(place_ref[8] == 1)
    def _():
        column = pl.multiple_of(place_ref[9], 128)
        copies = [
            pltpu.make_async_copy(
                inputs_ref.at[:, pl.ds(column, third_ref.shape[1])], third_ref, sems.at[0]
            ),
            pltpu.make_async_copy(grads_ref.at[:, pl.ds(2 * HID, BOT)], bottle_ref, sems.at[1]),
        ]
        for copy in copies:
            copy.start()
        for copy in copies:
            copy.wait()
        third = product_left(third_ref[...], bottle_ref[...])
        for lane in range(BOT // 128):
            line_ref[lane] = third[:, lane * 128 : (lane + 1) * 128]
        for group in range(ROW // BOT):
            for lane in range(BOT // 128):
                value = line_ref[lane, pl.ds(group, slot, stride=ROW // BOT), :]
                own_ref[:, pl.ds(group * BOT + lane * 128, 128)] = jnp.where(
                    number < place_ref[2], value, 0.0
                )

    block(4, partner_ref)


def head_grads(place, inputs_all, grads_all, slot, lead, waits, held):
    rows = inputs_all.shape[0]
    wide = slot * ROW // BOT
    return pl.pallas_call(
        lambda *refs: head_grads_kernel(len(held), *refs),
        out_shape=[jax.ShapeDtypeStruct((slot, ROW), kind) for kind in (single, narrow)]
        + [jax.ShapeDtypeStruct(array.shape, array.dtype) for array in held],
        in_specs=[pl.BlockSpec(memory_space=pltpu.SMEM)]
        + [pl.BlockSpec(memory_space=pl.ANY)] * (2 + len(waits) + len(held)),
        out_specs=[pl.BlockSpec(memory_space=pltpu.VMEM)] * 2
        + [pl.BlockSpec(memory_space=pl.ANY)] * len(held),
        input_output_aliases={3 + len(waits) + number: 2 + number for number in range(len(held))},
        scratch_shapes=[
            pltpu.VMEM((rows, 256), narrow),
            pltpu.VMEM((rows, ROW), narrow),
            pltpu.VMEM((lead + 256, ROW), single),
            pltpu.VMEM((rows, wide), narrow),
            pltpu.VMEM((rows, BOT), narrow),
            pltpu.VMEM((BOT // 128, wide, 128), single),
            pltpu.SemaphoreType.DMA((2,)),
        ],
        compiler_params=pltpu.CompilerParams(vmem_limit_bytes=56 << 20),
        cost_estimate=pl.CostEstimate(flops=100 * 10**6, bytes_accessed=370 * 10**5, transcendentals=0),
    )(place, inputs_all, grads_all, *waits, *held)


def close_local(
    patches,
    masked,
    slot_used,
    stem,
    stem_moment,
    stem_second,
    stem_teacher,
    layers,
    layer_moment,
    layer_second,
    layer_teacher,
    protos,
    proto_moment,
    proto_second,
    proto_teacher,
    centre,
):
    count = 1 << len(BITS)
    half = count // 2
    me = lax.axis_index("dev")
    across = MASKS["b"]
    student_side = me >= half
    groups = [list(range(half)), list(range(half, count))]
    quarter = half // 2
    swap = jnp.where(student_side, quarter, 0)
    side = student_side.astype(jnp.int32).reshape(1)
    images_here = patches.shape[0]
    rows_here = images_here * 17
    pair_rows = -(-2 * rows_here // 16) * 16
    more_rows = pair_rows - 2 * rows_here
    stem_piece = stem.shape[0]
    layer_piece = layers.shape[1]
    block_rows = MATRIX_ROWS // count
    block = block_rows * D
    tail = layer_piece * count - MATRIX_ROWS * D
    drift = layer_piece - block
    bounds = head_bounds(count, stem_piece)
    sizes = [bounds[i + 1] - bounds[i] for i in range(count)]
    slot = max(sizes)
    starts = [b * ROW + EMBED_FLAT - stem_piece * i for i, b in enumerate(bounds[:-1])]
    first_w2 = bounds.index(D)
    first_w3 = bounds.index(D + HID)
    row_index = jnp.concatenate([jnp.zeros((images_here, 1), jnp.int32), masked + 1], axis=1)
    masked_here = jnp.any(
        masked[:, :, None] == jnp.arange(PATCHES, dtype=jnp.int32)[None, None, :], axis=1
    )
    kept = slot_used.astype(single)

    front = 16
    early_rows = -(-stem_piece // D)
    late_start = early_rows * D - stem_piece
    embed_rows = -(-early_rows // 16) * 16
    own_layers = jnp.concatenate([layer_teacher, layers])
    own_tail = own_layers[:, layer_piece - tail :].reshape(2 * LAYERS, tail // 128, 128)
    before = lax.ppermute(own_tail, "dev", step_pairs(count, 1))
    head_span = GROUP * ROW
    stems = jnp.stack([as_lanes(stem_teacher), as_lanes(stem)])
    stems_next = lax.ppermute(stems[:, : head_span // 128], "dev", step_pairs(count, -1))
    def per_device(rows):
        return lax.dynamic_slice(jnp.array(rows, jnp.int32), (me, 0), (1, len(rows[0]))).reshape(-1)

    def spots(*values):
        return [part for value in values for part in (value // 128, value % 128)]

    place = per_device(
        [
            spots(starts[i] + front * 128, front * 128 + (0 if i == 0 else late_start), tail - drift * i)
            for i in range(count)
        ]
    )
    head_blocks, layer_blocks, embed_blocks, vector_blocks = own_blocks(
        place,
        stems,
        stems_next,
        as_lanes(own_layers),
        before,
        (front, stem_piece, layer_piece, tail),
        slot,
        block_rows,
        embed_rows,
    )

    other_layers = lax.ppermute(layer_blocks, "dev", pairs(count, across))
    both_layers = jnp.where(
        student_side,
        jnp.stack([other_layers, layer_blocks]),
        jnp.stack([layer_blocks, other_layers]),
    )
    gathered = lax.all_gather(both_layers, "dev", axis=0, axis_index_groups=groups)
    head_out = jnp.where(student_side, head_blocks[0], head_blocks[1])
    head_keep = jnp.where(student_side, head_blocks[1], head_blocks[0])
    head_got = lax.ppermute(head_out, "dev", pairs(count, across))
    both_head = jnp.where(
        student_side, jnp.stack([head_got, head_keep]), jnp.stack([head_keep, head_got])
    )

    vectors = lax.ppermute(vector_blocks, "dev", [(count - 1, 0)])
    seed = jnp.concatenate([embed_blocks.reshape(2 * embed_rows, D), vectors.reshape(8 * 2 * LAYERS, D)])
    third = -(-seed.shape[0] // 48) * 16
    spread_parts = []
    for number, order in enumerate(("xyba", "baxy", "ybax")):
        spread = seed[number * third : (number + 1) * third]
        reached = [0, 1]
        for name in order:
            moves = [(i, i ^ MASKS[name]) for i in reached]
            got = lax.ppermute(spread, "dev", moves)
            targets = [t for s, t in moves]
            is_target = jnp.array([i in targets for i in range(count)])[me]
            spread = jnp.where(is_target, got, spread)
            reached = reached + targets
        spread_parts.append(spread)
    spread = jnp.concatenate(spread_parts)
    other = lax.ppermute(spread, "dev", pairs(count, 1))
    is_even = me % 2 == 0
    even = jnp.where(is_even, spread, other)
    odd = jnp.where(is_even, other, spread)
    embed_all = [
        jnp.concatenate(
            [
                even[m * embed_rows : m * embed_rows + early_rows],
                odd[m * embed_rows : m * embed_rows + EMBED_ROWS - early_rows],
            ]
        )
        for m in range(2)
    ]
    gathered_head = lax.all_gather(after(both_head, gathered, even, odd), "dev", axis=0, axis_index_groups=groups)
    vectors_all = even[2 * embed_rows :].reshape(2, LAYERS, 8, D)

    plan = []
    for i in range(1, count):
        target = 0 if i < first_w2 else 1 if i < first_w3 else 2
        row = bounds[i] - (0, D, D + HID)[target]
        skip = max(-row, 0)
        owner = 1 if i >= half else 0
        plan.append((i ^ across if owner else i, owner, skip, sizes[i] - skip, target, row + skip))

    def embed_parts(model):
        rows = embed_all[model]
        return (rows[:PIX], rows[PIX : PIX + SEQ], rows[PIX + SEQ :], None, None, None)

    def head_rows(stream, extras):
        chosen = jnp.take_along_axis(stream, row_index[:, :, None], axis=1).reshape(rows_here, D)
        normed = layer_norm(chosen, extras[2].astype(single), extras[3].astype(single)).astype(narrow)
        return chosen, normed

    def start_rows(parts, student):
        stream = embed(parts, patches, masked_here, student)
        return jnp.pad(stream, ((0, 0), (0, PAD_SEQ - SEQ), (0, 0))).reshape(images_here * PAD_SEQ, D)

    student_parts = embed_parts(1)
    stream = start_rows(student_parts, True)
    saved_layers = []
    for layer_index in range(LAYERS):
        before_layer = stream
        stream, *saved = layer_forward(
            side, stream, vectors_all[1, layer_index], gathered, LAYERS + layer_index, True
        )
        saved_layers.append((before_layer, *saved))
    teacher_parts = embed_parts(0)
    teacher_stream = start_rows(teacher_parts, False)
    for layer_index in range(LAYERS):
        teacher_stream = layer_forward(
            side, teacher_stream, vectors_all[0, layer_index], gathered, layer_index, False
        )[0]
    stream = stream.reshape(images_here, PAD_SEQ, D)
    teacher_stream = teacher_stream.reshape(images_here, PAD_SEQ, D)
    chosen, student_normed = head_rows(stream, student_parts[2])
    teacher_normed = head_rows(teacher_stream, teacher_parts[2])[1]

    normed_got = lax.ppermute(
        jnp.where(student_side, teacher_normed, student_normed), "dev", pairs(count, across)
    )
    normed = jnp.where(
        student_side,
        jnp.concatenate([normed_got, student_normed]),
        jnp.concatenate([teacher_normed, normed_got]),
    )
    normed = jnp.pad(normed, ((0, more_rows), (0, 0)))
    all_rows = half * pair_rows
    kept_row = jnp.broadcast_to(kept[:, None], (images_here, 17)).reshape(1, rows_here)
    kept_pair = cube_gather(kept_row, "b").reshape(1, 2 * rows_here)
    kept_pair = jnp.pad(kept_pair, ((0, 0), (0, more_rows)))
    all_kept = cube_gather(kept_pair, "xygc").reshape(all_rows)
    third_end = (bounds[-2] - D - HID + slot) * (ROW // BOT)
    acts_width = D + HID + max(third_end, HID)
    unit_z, acts, bottleneck, pre_one, pre_two = head_pass(
        head_up_kernel,
        plan,
        side,
        (normed,),
        gathered_head,
        [
            jax.ShapeDtypeStruct((pair_rows, BOT), narrow),
            jax.ShapeDtypeStruct((pair_rows, acts_width), narrow),
            jax.ShapeDtypeStruct((pair_rows, BOT), single),
            jax.ShapeDtypeStruct((pair_rows, HID), single),
            jax.ShapeDtypeStruct((pair_rows, HID), single),
        ],
        (all_kept,),
    )
    inputs_all = lax.all_gather(acts, "dev", axis=0, axis_index_groups=groups).reshape(half * pair_rows, -1)

    z_pair = cube_gather(unit_z, "b")
    teacher_z_all = cube_gather(z_pair[0], "xygc").reshape(all_rows, BOT)
    student_z_all = cube_gather(z_pair[1], "gxyc").reshape((2,) * 4 + (pair_rows, BOT))
    student_z_all = jnp.transpose(student_z_all, (0, 3, 1, 2, 4, 5)).reshape(all_rows, BOT)
    protos_here = protos.shape[0]
    own_centre = lax.dynamic_slice(centre, (me * protos_here,), (protos_here,))
    centre_column = own_centre.reshape(protos_here, 1)
    spot_in_pair = jnp.arange(all_rows) % pair_rows
    is_class = (spot_in_pair % 17) == 0
    class_kept = jnp.where(is_class, all_kept, 0.0)
    row_weight = jnp.where(is_class, all_kept, all_kept * (1.0 / 16.0))
    count_total = jnp.sum(class_kept)

    def lines(*values):
        return jnp.pad(jnp.stack(values), ((0, 8 - len(values)), (0, 0)))

    mixed_rows, sums, centre_sum = logits_pass(
        teacher_z_all, student_z_all, proto_teacher, protos, centre_column, lines(class_kept)
    )
    by_pair = (2,) * 4 + (pair_rows, -1)
    mixed_own = jnp.concatenate(
        [
            cube_scatter(mixed_rows[:, :BOT].reshape(by_pair), "cgyx", "cgyx"),
            cube_scatter(mixed_rows[:, BOT:].reshape(by_pair), "cgyx", "cxyg"),
        ],
        axis=1,
    )
    mixed_own = mixed_own + lax.ppermute(
        mixed_own.astype(narrow), "dev", [(i, i ^ across) for i in range(half)]
    ).astype(single)
    stages = [sums[:3]]
    for name in "cxyab":
        stages.append(stages[-1] + lax.ppermute(stages[-1], "dev", pairs(count, MASKS[name])))
    sums = stages[-1]
    cross = jnp.log(sums[1]) - sums[2] / (sums[0] * tau_student)
    loss_total = jnp.sum(row_weight * cross)
    scale = row_weight / tau_student
    student_scale, teacher_scale = scale / sums[1], scale / sums[0]
    flags = bit_flags(me)
    pair_at = flags["c"] * 8 + flags["g"] * 4 + flags["y"] * 2 + flags["x"]
    own_scale = lax.dynamic_slice(scale, (pair_at * pair_rows,), (pair_rows,))[:, None]
    grad_unit_z = own_scale * (
        mixed_own[:, :BOT] / mixed_own[:, 2 * BOT + 1 : 2 * BOT + 2]
        - mixed_own[:, BOT : 2 * BOT] / mixed_own[:, 2 * BOT : 2 * BOT + 1]
    )
    own_new_centre = (
        centre_keep * own_centre + (1.0 - centre_keep) * centre_sum.reshape(protos_here) / count_total
    )
    new_centre = cube_gather(own_new_centre.reshape(1, protos_here), "cxyab").reshape(-1)

    grads, grad_normed = head_pass(
        head_down_kernel,
        plan,
        side,
        (grad_unit_z, bottleneck, pre_one, pre_two),
        gathered_head,
        [
            jax.ShapeDtypeStruct((pair_rows, 2 * HID + BOT), narrow),
            jax.ShapeDtypeStruct((pair_rows, D), single),
        ],
        (stages[3],),
    )
    grads_all = lax.all_gather(grads, "dev", axis=0, axis_index_groups=groups).reshape(half * pair_rows, -1)
    normed_back = lax.ppermute(
        grad_normed[:rows_here], "dev", [(i, i ^ across) for i in range(half, count)]
    )
    own_grad_normed = jnp.where(student_side, grad_normed[rows_here : 2 * rows_here], normed_back)
    extras = student_parts[2].astype(single)
    grad_chosen, grad_gain, grad_bias = jax.vjp(layer_norm, chosen, extras[2], extras[3])[1](
        own_grad_normed
    )
    image_index = jnp.arange(images_here, dtype=jnp.int32)[:, None]
    grad_stream = (
        jnp.zeros(stream.shape, single)
        .at[image_index, row_index]
        .add(grad_chosen.reshape(images_here, 17, D))
    )

    grad_stream = grad_stream.reshape(images_here * PAD_SEQ, D)
    middle_row = block_rows // 2
    vector_grads = [None] * LAYERS

    def halves(array):
        middle = array.shape[-2] // 2
        return [array[..., :middle, :], array[..., middle:, :]]

    def cuts(parts, names, order):
        return [cut(part, name, axis, 1) for part, name, axis in zip(parts, names, order)]

    def moves(pieces, order):
        return [move(sent, kept, axis) for (sent, kept, left), axis in zip(pieces, order)]

    def over_core(weight_grad, rows):
        pairs_of = weight_grad.reshape(D // 128, -1, 2, rows, 128)
        return move(*cut(pairs_of, "pc", "c", 1)[:2], "c")

    def core_cut(weight_grad, rows):
        return cut(weight_grad.reshape(D // 128, -1, 2, rows, 128), "pc", "c", 1)[:2]

    def start(late, early, *others):
        shared_pair = 4 * D // (2 * block_rows)
        whole = jnp.concatenate(
            [
                early[:, :shared_pair],
                early[:, shared_pair:] + late[:, : early.shape[1] - shared_pair],
                late[:, early.shape[1] - shared_pair :],
            ],
            axis=1,
        )
        parts = [jnp.concatenate(pieces, axis=2) for pieces in zip(*[halves(array) for array in (whole, *others)])]
        by_bits = [part.reshape((D // 128, 2, 2, 2, 2) + part.shape[2:]) for part in parts]
        return (cuts(by_bits, ["bayx"] * 2, rounds[0]), 0)

    rounds = (("x", "b"), ("y", "a"), ("b", "x"), ("a", "y"))

    def advance(state):
        pieces, stage = state
        parts = moves(pieces, rounds[stage])
        names = [left for sent, kept, left in pieces]
        return cuts(parts, names, rounds[stage + 1]), stage + 1

    def finish(state):
        while state[1] < len(rounds) - 1:
            state = advance(state)
        return moves(state[0], rounds[-1])

    def sends(states):
        return tuple(sent for pieces, stage in states for sent, kept, left in pieces)

    def block_place(i):
        column = max(bounds[i], 0) // 128 * 128
        grad_column = 0 if i < first_w2 else HID
        return [column, bounds[i] - column if i else 0, sizes[i] if i else 0, grad_column]

    def third_place(i):
        return [0, 0, sizes[i], 0]

    place = per_device(
        [
            (third_place(i) if i >= first_w3 else block_place(i))
            + block_place(i ^ across)
            + [int(i >= first_w3), D + HID + max(bounds[i] - D - HID, 0) * (ROW // BOT)]
            for i in range(count)
        ]
    )
    started = []
    waits, later_waits = (), ()
    for layer_index in reversed(range(LAYERS)):
        saved, vectors = saved_layers[layer_index], vectors_all[1, layer_index]
        part = LAYERS + layer_index
        grad_stream, late_grad, late_vectors = mlp_back(
            side, grad_stream, saved, vectors, gathered, part, waits + sends(started)
        )
        late = over_core(late_grad, block_rows)
        started = [advance(state) for state in started]
        grad_stream, early_grad, early_vectors = attention_back(
            side, grad_stream, saved, vectors, gathered, part, later_waits + sends(started)
        )
        vector_grads[layer_index] = (late_vectors + early_vectors)[:6]
        if layer_index == LAYERS - 1:
            sent, stay = core_cut(early_grad, block_rows)
            own_block_grad, partner_block_grad, stay = head_grads(
                place, inputs_all, grads_all, slot, -min(bounds[1], 0), (early_vectors,), [stay]
            )
            block_got = lax.ppermute(partner_block_grad, "dev", [(i, i ^ across) for i in range(half, count)])
            waits, later_waits = (own_block_grad, stages[4]), (stages[5], block_got, new_centre)
        started = [advance(state) for state in started]
        if layer_index > 0:
            started.append(start(late, move(sent, stay, "c")))
    head_block_grad = jnp.where(student_side, own_block_grad, block_got.astype(single))
    early = over_core(early_grad, block_rows)
    small_rows = -(-(EMBED_ROWS + 6 * LAYERS) // (16 * count)) * 16
    small = embed_back(
        grad_stream,
        patches.reshape(images_here * PATCHES, PIX),
        jnp.where(masked_here, 0.0, 1.0).reshape(images_here * PATCHES, 1),
        jnp.stack([grad_gain, grad_bias]),
        jnp.concatenate(vector_grads),
        small_rows * count,
        (),
    )
    started.append(start(late, early, over_core(small, small_rows)))
    last_rows = lax.dynamic_slice(
        head_block_grad, (jnp.array(sizes, jnp.int32)[me] - GROUP, 0), (GROUP, ROW)
    )
    previous = lax.ppermute(last_rows, "dev", step_pairs(count, 1))
    proto_grad, proto_square, *held = proto_grad_pass(
        teacher_z_all,
        student_z_all,
        proto_teacher,
        protos,
        centre_column,
        lines(student_scale, teacher_scale),
        [previous] + [stay for pieces, stage in started for sent, stay, left in pieces],
    )
    previous, *held = held
    held = iter(held)
    started = [([(sent, next(held), left) for sent, _, left in pieces], stage) for pieces, stage in started]
    blocks = [finish(state) for state in started][::-1]
    middle_row = block_rows // 2
    layer_block = jnp.stack([jnp.concatenate([part[:, :middle_row] for part in parts], axis=1) for parts in blocks])
    small_block = jnp.concatenate([part[:, middle_row:] for part in blocks[0]], axis=1)

    square_local = (
        jnp.sum(head_block_grad * head_block_grad)
        + jnp.sum(layer_block * layer_block)
        + jnp.sum(small_block * small_block)
        + proto_square[0, 0]
    )
    high = square_local.astype(narrow)
    middle = (square_local - high.astype(single)).astype(narrow)
    low = (square_local - high.astype(single) - middle.astype(single)).astype(narrow)
    tile = jnp.pad(jnp.stack([high, middle, low]).reshape(1, 1, 3), ((0, 0), (0, 15), (0, 125)))
    first_rows = small_block[:2].astype(narrow)
    other_rows = jnp.concatenate([small_block[2:].astype(narrow), tile], axis=1)
    first_rows = cube_gather(first_rows, "xya")
    other_rows = cube_gather(other_rows, "abx")
    behind = lax.ppermute(layer_block[:, :, :6], "dev", step_pairs(count, -1))
    place = per_device([spots(head_span - starts[i], drift * i) for i in range(count)])
    stem_lines, layer_lines, first_rows, other_rows = own_shards(
        place, head_block_grad, previous, layer_block, behind, lane_rows(stem_piece), lane_rows(layer_piece),
        [first_rows, other_rows],
    )
    first_rows = jnp.moveaxis(cube_gather(first_rows, "bc").reshape((2, 2, 8) + first_rows.shape[1:]), 0, 2)
    other_rows = cube_gather(other_rows, "yc")
    other_rows = other_rows.reshape((2,) * 5 + other_rows.shape[2:])
    other_rows = jnp.transpose(other_rows, (3, 4, 1, 2, 0, 5, 6, 7))
    first_rows = first_rows.reshape((count,) + first_rows.shape[3:])
    other_rows = other_rows.reshape((count,) + other_rows.shape[5:])
    square_total = jnp.sum(other_rows[:, 0, small_rows, :3].astype(single))
    small_all = jnp.concatenate([first_rows, other_rows[:, :, :small_rows]], axis=1).astype(single)
    small_all = jnp.transpose(small_all, (0, 2, 1, 3)).reshape(small_rows * count, D)
    embed_grad = small_all[:EMBED_ROWS].reshape(-1)
    vector_grad = small_all[EMBED_ROWS : EMBED_ROWS + 6 * LAYERS].reshape(LAYERS, 6 * D)
    layer_grad = layer_lines.reshape(LAYERS, -1)[:, :layer_piece]
    layer_grad = jnp.concatenate(
        [
            layer_grad[:, : layer_piece - tail],
            jnp.where(me == count - 1, vector_grad, layer_grad[:, layer_piece - tail :]),
        ],
        axis=1,
    )
    stem_grad = stem_lines.reshape(-1)[:stem_piece]
    rest = EMBED_FLAT - stem_piece
    second_part = jnp.concatenate([embed_grad[stem_piece:], stem_grad[rest:]])
    stem_grad = jnp.where(
        me == 0, embed_grad[:stem_piece], jnp.where(me == 1, second_part, stem_grad)
    )

    grad_norm = jnp.sqrt(square_total) / count_total
    factor = jnp.minimum(1.0, clip_limit / (grad_norm + 1e-06)) / count_total
    stem_set = adam_update(stem, stem_moment, stem_second, stem_grad * factor, stem_teacher)
    layer_set = adam_update(layers, layer_moment, layer_second, layer_grad * factor, layer_teacher)
    proto_set = proto_update(factor, protos, proto_moment, proto_second, proto_teacher, proto_grad)
    return (loss_total, count_total, grad_norm, new_centre) + stem_set + layer_set + tuple(proto_set)


def solution(mesh):
    count = mesh.shape["dev"]
    stem_length = -(-(EMBED_FLAT + HEAD_ROWS * ROW) // count) * count
    close = fits(count, stem_length // count, (MATRIX_ROWS + 6) * D // count)
    placed = (
        P("dev", None, None),
        P("dev", None),
        P("dev"),
        P("dev"),
        P("dev"),
        P("dev"),
        P("dev"),
        P(None, "dev"),
        P(None, "dev"),
        P(None, "dev"),
        P(None, "dev"),
        P("dev", None),
        P("dev", None),
        P("dev", None),
        P("dev", None),
        P(),
    )
    return jax.shard_map(
        close_local if close else spread_local,
        mesh=mesh,
        in_specs=placed,
        out_specs=(
            P(),
            P(),
            P(),
            P(),
            P("dev"),
            P("dev"),
            P("dev"),
            P("dev"),
            P("dev"),
            P(None, "dev"),
            P(None, "dev"),
            P(None, "dev"),
            P(None, "dev"),
            P(None, "dev"),
            P("dev", None),
            P("dev", None),
            P("dev", None),
            P("dev", None),
            P("dev", None),
        ),
        check_vma=False,
    )
```

```python
import jax
import jax.numpy as jnp
from jax import lax
from jax.experimental import pallas as pl
from jax.experimental.pallas import tpu as pltpu
from jax.sharding import PartitionSpec as P

D = 384
HEADS = 6
HEAD_DIM = 64
FF = 1536
HID = 2048
BOT = 256
PIX = 588
PATCHES = 256
LAYERS = 2
STEP = 10
SEQ = 257


tau_student = 0.1
tau_teacher = 0.04
clip_limit = 0.003
learn_rate = 0.03
beta_one = 0.9
beta_two = 0.999
adam_eps = 1e-08
decay_rate = 0.04
teacher_keep = 0.8
centre_keep = 0.9
narrow = jnp.bfloat16
single = jnp.float32


def layer_shapes():
    return ((D, 3 * D), (D, D), (D, FF), (FF, D), (6, D))


def stem_shapes():
    return ((PIX, D), (SEQ, D), (4, D), (D, HID), (HID, HID), (HID, BOT))


def cut_flat(flat_row, shape_list):
    pieces = []
    offset = 0
    for shape_pair in shape_list:
        length = shape_pair[0] * shape_pair[1]
        pieces.append(flat_row[offset : offset + length].reshape(shape_pair))
        offset = offset + length
    return pieces


def pack_flat(grad_list, total_length):
    joined = jnp.concatenate([grad_item.reshape(-1) for grad_item in grad_list])
    return jnp.concatenate([joined, jnp.zeros((total_length - joined.shape[0],), single)])


def contract(form, left_arg, right_arg):
    return jnp.einsum(form, left_arg, right_arg, preferred_element_type=single)


def layer_norm(values, gain_row, bias_row):
    centred = values - jnp.mean(values, axis=-1, keepdims=True)
    spread = jnp.mean(centred * centred, axis=-1, keepdims=True)
    return centred * lax.rsqrt(spread + 1e-06) * gain_row + bias_row


def unit_rows(values):
    return values * lax.rsqrt(jnp.sum(values * values, axis=-1, keepdims=True) + 1e-06)


def gelu_back(pre_act, grad_act):
    return jax.vjp(jax.nn.gelu, pre_act)[1](grad_act)[0]


def block_forward(stream, weights):
    w_qkv, w_proj, w_up, w_down, vectors = weights
    vectors = vectors.astype(single)
    batch_size = stream.shape[0]
    normed = layer_norm(stream, vectors[0], vectors[1]).astype(narrow)
    packed = (
        contract("bsd,de->bse", normed, w_qkv)
        .astype(narrow)
        .reshape(batch_size, SEQ, 3, HEADS, HEAD_DIM)
    )
    scores = contract("bqhe,bkhe->bhqk", packed[:, :, 0], packed[:, :, 1]) * HEAD_DIM ** (-0.5)
    top_score = jnp.max(scores, axis=-1, keepdims=True)
    exp_terms = jnp.exp(scores - top_score)
    totals = jnp.sum(exp_terms, axis=-1, keepdims=True)
    log_total = top_score + jnp.log(totals)
    mixed = contract("bhqk,bkhe->bqhe", (exp_terms / totals).astype(narrow), packed[:, :, 2])
    mixed = mixed.astype(narrow).reshape(batch_size, SEQ, D)
    attn_out = contract("bsd,de->bse", mixed, w_proj)
    middle = stream + vectors[2] * attn_out
    normed_two = layer_norm(middle, vectors[3], vectors[4]).astype(narrow)
    pre_act = contract("bsd,df->bsf", normed_two, w_up)
    hidden = jax.nn.gelu(pre_act).astype(narrow)
    mlp_out = contract("bsf,fd->bsd", hidden, w_down)
    saved = (
        stream,
        normed,
        packed,
        log_total,
        mixed,
        attn_out,
        middle,
        normed_two,
        pre_act,
        hidden,
        mlp_out,
    )
    return (middle + vectors[5] * mlp_out, saved)


def block_backward(grad_out, weights, saved):
    w_qkv, w_proj, w_up, w_down, vectors = weights
    vectors = vectors.astype(single)
    (
        stream,
        normed,
        packed,
        log_total,
        mixed,
        attn_out,
        middle,
        normed_two,
        pre_act,
        hidden,
        mlp_out,
    ) = saved
    batch_size = stream.shape[0]
    score_scale = HEAD_DIM ** (-0.5)
    grad_ls_two = jnp.sum(grad_out * mlp_out, axis=(0, 1))
    grad_mlp = (grad_out * vectors[5]).astype(narrow)
    grad_down = contract("bsf,bsd->fd", hidden, grad_mlp)
    grad_pre = gelu_back(pre_act, contract("bsd,fd->bsf", grad_mlp, w_down)).astype(narrow)
    grad_up = contract("bsd,bsf->df", normed_two, grad_pre)
    grad_normed_two = contract("bsf,df->bsd", grad_pre, w_up)
    grad_mid, grad_gain_two, grad_bias_two = jax.vjp(layer_norm, middle, vectors[3], vectors[4])[1](
        grad_normed_two
    )
    grad_mid = grad_mid + grad_out
    grad_ls_one = jnp.sum(grad_mid * attn_out, axis=(0, 1))
    grad_attn = (grad_mid * vectors[2]).astype(narrow)
    grad_proj = contract("bsd,bse->de", mixed, grad_attn)
    grad_mixed = (
        contract("bse,de->bsd", grad_attn, w_proj)
        .astype(narrow)
        .reshape(batch_size, SEQ, HEADS, HEAD_DIM)
    )
    query_rows = packed[:, :, 0]
    key_rows = packed[:, :, 1]
    value_rows = packed[:, :, 2]
    probs = jnp.exp(contract("bqhe,bkhe->bhqk", query_rows, key_rows) * score_scale - log_total)
    grad_probs = contract("bqhe,bkhe->bhqk", grad_mixed, value_rows)
    grad_values = contract("bhqk,bqhe->bkhe", probs.astype(narrow), grad_mixed)
    grad_scores = probs * (grad_probs - jnp.sum(probs * grad_probs, axis=-1, keepdims=True))
    grad_raw = (grad_scores * score_scale).astype(narrow)
    grad_queries = contract("bhqk,bkhe->bqhe", grad_raw, key_rows)
    grad_keys = contract("bhqk,bqhe->bkhe", grad_raw, query_rows)
    grad_packed = (
        jnp.stack([grad_queries, grad_keys, grad_values], axis=2)
        .astype(narrow)
        .reshape(batch_size, SEQ, 3 * D)
    )
    grad_qkv = contract("bsd,bse->de", normed, grad_packed)
    grad_normed = contract("bse,de->bsd", grad_packed, w_qkv)
    grad_in, grad_gain_one, grad_bias_one = jax.vjp(layer_norm, stream, vectors[0], vectors[1])[1](
        grad_normed
    )
    grad_vectors = jnp.stack(
        [grad_gain_one, grad_bias_one, grad_ls_one, grad_gain_two, grad_bias_two, grad_ls_two]
    )
    return (grad_in + grad_mid, (grad_qkv, grad_proj, grad_up, grad_down, grad_vectors))


def embed(stem_parts, image_rows, masked_here, student):
    patch_w, position, extras, w_first, w_second, w_third = stem_parts
    extras = extras.astype(single)
    embedded = contract("gpc,cd->gpd", image_rows, patch_w)
    if student:
        embedded = jnp.where(masked_here[:, :, None], extras[1], embedded)
    cls_rows = jnp.broadcast_to(extras[0], (image_rows.shape[0], 1, D))
    return jnp.concatenate([cls_rows, embedded], axis=1) + position.astype(single)


def embed_backward(grad_stream, image_rows, masked_here):
    grad_cls = jnp.sum(grad_stream[:, 0], axis=0)
    grad_position = jnp.sum(grad_stream, axis=0)
    grad_patch_rows = grad_stream[:, 1:]
    grad_mask_token = jnp.sum(jnp.where(masked_here[:, :, None], grad_patch_rows, 0.0), axis=(0, 1))
    grad_embedded = jnp.where(masked_here[:, :, None], 0.0, grad_patch_rows).astype(narrow)
    grad_patch_w = contract("gpc,gpd->cd", image_rows, grad_embedded)
    return (grad_patch_w, grad_position, grad_cls, grad_mask_token)


def head_forward(stem_parts, proto_rows, stream, row_index):
    patch_w, position, extras, w_first, w_second, w_third = stem_parts
    extras = extras.astype(single)
    chosen = jnp.take_along_axis(stream, row_index[:, :, None], axis=1)
    normed = layer_norm(chosen, extras[2], extras[3]).astype(narrow)
    pre_one = contract("grd,dh->grh", normed, w_first)
    hidden_one = jax.nn.gelu(pre_one).astype(narrow)
    pre_two = contract("grh,hk->grk", hidden_one, w_second)
    hidden_two = jax.nn.gelu(pre_two).astype(narrow)
    bottleneck = contract("grh,hb->grb", hidden_two, w_third)
    unit_z = unit_rows(bottleneck).astype(narrow)
    unit_protos = unit_rows(proto_rows.astype(single)).astype(narrow)
    logits = contract("grb,kb->grk", unit_z, unit_protos)
    return (
        logits,
        (chosen, normed, pre_one, hidden_one, pre_two, hidden_two, bottleneck, unit_z, unit_protos),
    )


def head_backward(grad_logits, stem_parts, saved, row_index, stream_shape):
    patch_w, position, extras, w_first, w_second, w_third = stem_parts
    extras = extras.astype(single)
    chosen, normed, pre_one, hidden_one, pre_two, hidden_two, bottleneck, unit_z, unit_protos = (
        saved
    )
    grad_rounded = grad_logits.astype(narrow)
    grad_unit_z = contract("grk,kb->grb", grad_rounded, unit_protos)
    grad_unit_protos = contract("grk,grb->kb", grad_rounded, unit_z)
    grad_bottle = jax.vjp(unit_rows, bottleneck)[1](grad_unit_z)[0].astype(narrow)
    grad_third = contract("grh,grb->hb", hidden_two, grad_bottle)
    grad_pre_two = gelu_back(pre_two, contract("grb,hb->grh", grad_bottle, w_third)).astype(narrow)
    grad_second = contract("grh,grk->hk", hidden_one, grad_pre_two)
    grad_pre_one = gelu_back(pre_one, contract("grk,hk->grh", grad_pre_two, w_second)).astype(
        narrow
    )
    grad_first = contract("grd,grh->dh", normed, grad_pre_one)
    grad_normed = contract("grh,dh->grd", grad_pre_one, w_first)
    grad_chosen, grad_gain, grad_bias = jax.vjp(layer_norm, chosen, extras[2], extras[3])[1](
        grad_normed
    )
    image_index = jnp.arange(row_index.shape[0], dtype=jnp.int32)[:, None]
    grad_stream = jnp.zeros(stream_shape, single).at[image_index, row_index].add(grad_chosen)
    return (
        grad_stream,
        (grad_first, grad_second, grad_third),
        grad_gain,
        grad_bias,
        grad_unit_protos,
    )


def adam_update(weight, moment, second, grad, teacher):
    new_moment = beta_one * moment + (1.0 - beta_one) * grad
    new_second = beta_two * second + (1.0 - beta_two) * grad * grad
    direction = (
        new_moment
        / (1.0 - beta_one**STEP)
        / (jnp.sqrt(new_second / (1.0 - beta_two**STEP)) + adam_eps)
    )
    new_weight = weight - learn_rate * (direction + decay_rate * weight)
    return (
        new_moment,
        new_second,
        new_weight,
        new_weight.astype(narrow),
        teacher_keep * teacher + (1.0 - teacher_keep) * new_weight,
    )


def spread_local(
    patches,
    masked,
    slot_used,
    stem,
    stem_moment,
    stem_second,
    stem_teacher,
    layers,
    layer_moment,
    layer_second,
    layer_teacher,
    protos,
    proto_moment,
    proto_second,
    proto_teacher,
    centre,
):
    images_here = patches.shape[0]
    row_index = jnp.concatenate([jnp.zeros((images_here, 1), jnp.int32), masked + 1], axis=1)
    masked_here = jnp.any(
        masked[:, :, None] == jnp.arange(PATCHES, dtype=jnp.int32)[None, None, :], axis=1
    )
    kept = slot_used.astype(single)
    teacher_flat, teacher_protos = (
        lax.all_gather(stem_teacher.astype(narrow), "dev", axis=0, tiled=True),
        lax.all_gather(proto_teacher.astype(narrow), "dev", axis=0, tiled=True),
    )
    teacher_parts = cut_flat(teacher_flat, stem_shapes())
    stream = embed(teacher_parts, patches, masked_here, False)
    for layer_index in range(LAYERS):
        teacher_layer = lax.all_gather(
            layer_teacher[layer_index].astype(narrow), "dev", axis=0, tiled=True
        )
        stream = block_forward(stream, cut_flat(teacher_layer, layer_shapes()))[0]
    teacher_logits = head_forward(teacher_parts, teacher_protos, stream, row_index)[0]
    teacher_probs = jax.nn.softmax((teacher_logits - centre) / tau_teacher, axis=-1)
    centre_terms = jnp.sum(kept[:, None] * teacher_logits[:, 0], axis=0)
    student_flat, student_protos = (
        lax.all_gather(stem.astype(narrow), "dev", axis=0, tiled=True),
        lax.all_gather(protos.astype(narrow), "dev", axis=0, tiled=True),
    )
    student_parts = cut_flat(student_flat, stem_shapes())
    stream = embed(student_parts, patches, masked_here, True)
    saved_layers = []
    gathered_layers = []
    for layer_index in range(LAYERS):
        layer_flat = lax.all_gather(layers[layer_index].astype(narrow), "dev", axis=0, tiled=True)
        gathered_layers.append(layer_flat)
        stream, saved = block_forward(stream, cut_flat(layer_flat, layer_shapes()))
        saved_layers.append(saved)
    logits, head_saved = head_forward(student_parts, student_protos, stream, row_index)

    def loss_piece(logit_rows):
        log_probs = jax.nn.log_softmax(logit_rows / tau_student, axis=-1)
        cross = -jnp.sum(teacher_probs * log_probs, axis=-1)
        return jnp.sum(kept * (cross[:, 0] + jnp.mean(cross[:, 1:], axis=1)))

    loss_local, loss_puller = jax.vjp(loss_piece, logits)
    grad_logits = loss_puller(jnp.float32(1.0))[0]
    count_local = jnp.sum(kept)
    loss_total, count_total, centre_total = lax.psum((loss_local, count_local, centre_terms), "dev")
    back_flat, back_protos = (
        lax.all_gather(stem.astype(narrow), "dev", axis=0, tiled=True),
        lax.all_gather(protos.astype(narrow), "dev", axis=0, tiled=True),
    )
    back_parts = cut_flat(back_flat, stem_shapes())
    grad_stream, head_grads, grad_gain, grad_bias, grad_unit_protos = head_backward(
        grad_logits, back_parts, head_saved, row_index, stream.shape
    )
    layer_grads = []
    for layer_index in reversed(range(LAYERS)):
        weight_flat = lax.all_gather(layers[layer_index].astype(narrow), "dev", axis=0, tiled=True)
        grad_stream, block_grads = block_backward(
            grad_stream, cut_flat(weight_flat, layer_shapes()), saved_layers[layer_index]
        )
        layer_grads.insert(
            0,
            lax.psum_scatter(
                pack_flat(block_grads, weight_flat.shape[0]), "dev", scatter_dimension=0, tiled=True
            ),
        )
    grad_patch_w, grad_position, grad_cls, grad_mask_token = embed_backward(
        grad_stream, patches, masked_here
    )
    grad_extras = jnp.stack([grad_cls, grad_mask_token, grad_gain, grad_bias])
    stem_flat_grad = pack_flat(
        (grad_patch_w, grad_position, grad_extras) + head_grads, back_flat.shape[0]
    )
    stem_grad, proto_row_grad = (
        lax.psum_scatter(stem_flat_grad, "dev", scatter_dimension=0, tiled=True),
        lax.psum_scatter(grad_unit_protos, "dev", scatter_dimension=0, tiled=True),
    )
    own_protos = lax.optimization_barrier(protos.astype(narrow)).astype(single)
    proto_grad = jax.vjp(unit_rows, own_protos)[1](proto_row_grad)[0]
    layer_grad = jnp.stack(layer_grads)
    square_local = (
        jnp.sum(stem_grad * stem_grad)
        + jnp.sum(layer_grad * layer_grad)
        + jnp.sum(proto_grad * proto_grad)
    )
    square_total = lax.psum(square_local, "dev")
    grad_norm = jnp.sqrt(square_total) / count_total
    factor = jnp.minimum(1.0, clip_limit / (grad_norm + 1e-06)) / count_total
    new_centre = centre_keep * centre + (1.0 - centre_keep) * centre_total / count_total
    stem_set = adam_update(stem, stem_moment, stem_second, stem_grad * factor, stem_teacher)
    layer_set = adam_update(layers, layer_moment, layer_second, layer_grad * factor, layer_teacher)
    proto_set = adam_update(protos, proto_moment, proto_second, proto_grad * factor, proto_teacher)
    return (
        loss_total,
        count_total,
        grad_norm,
        new_centre,
        stem_set[0],
        stem_set[1],
        stem_set[2],
        stem_set[3],
        stem_set[4],
        layer_set[0],
        layer_set[1],
        layer_set[2],
        layer_set[3],
        layer_set[4],
        proto_set[0],
        proto_set[1],
        proto_set[2],
        proto_set[3],
        proto_set[4],
    )


GROUP = 16
ROW = HID
MATRIX_ROWS = D * 3 + D + FF + FF
EMBED_ROWS = PIX + SEQ + 4
EMBED_FLAT = EMBED_ROWS * D
HEAD_ROWS = D + HID + BOT
BITS = ("b", "a", "y", "x", "c")
MASKS = {"c": 1, "x": 2, "y": 4, "a": 8, "b": 24, "g": 8}


def head_bounds(count, stem_piece):
    bounds = [-(-(stem_piece * device - EMBED_FLAT) // (ROW * GROUP)) * GROUP for device in range(count + 1)]
    bounds[0] = -(-EMBED_FLAT // (ROW * GROUP)) * -GROUP
    bounds[-1] = HEAD_ROWS
    return bounds


def fits(count, stem_piece, layer_piece):
    if count != 1 << len(BITS) or MATRIX_ROWS % (3 * count):
        return False
    bounds = head_bounds(count, stem_piece)
    sizes = [bounds[i + 1] - bounds[i] for i in range(count)]
    return (
        min(sizes) > GROUP
        and bounds[1] <= 0
        and stem_piece < EMBED_FLAT <= 2 * stem_piece
        and D in bounds
        and D + HID in bounds
        and stem_piece * count == EMBED_FLAT + HEAD_ROWS * ROW
    )


def pairs(count, mask):
    return [(i, i ^ mask) for i in range(count)]


def bit_flags(me):
    flags = {name: (me >> (len(BITS) - 1 - place)) & 1 for place, name in enumerate(BITS)}
    flags["g"] = flags["a"] ^ flags["b"]
    return flags


def cube_gather(part, order):
    count = 1 << len(BITS)
    flags = bit_flags(lax.axis_index("dev"))
    held = part[None]
    for name in order:
        got = lax.ppermute(held, "dev", pairs(count, MASKS[name]))
        held = jnp.where(
            flags[name] == 1,
            jnp.concatenate([got, held], axis=0),
            jnp.concatenate([held, got], axis=0),
        )
    return held


def cut(array, names, name, lead):
    mine = bit_flags(lax.axis_index("dev"))[name]
    place = names.index(name) + lead
    sent = lax.dynamic_index_in_dim(array, 1 - mine, place, keepdims=False)
    kept = lax.dynamic_index_in_dim(array, mine, place, keepdims=False)
    return (sent if name == "c" else sent.astype(narrow)), kept, names.replace(name, "")


def move(sent, kept, name):
    return kept + lax.ppermute(sent, "dev", pairs(1 << len(BITS), MASKS[name])).astype(single)


def cube_scatter(array, names, order, lead=0):
    for name in order:
        sent, kept, names = cut(array, names, name, lead)
        array = move(sent, kept, name)
    return array


def cube_sum(values):
    for name in "cxyab":
        values = values + lax.ppermute(values, "dev", pairs(1 << len(BITS), MASKS[name]))
    return values


def split_bits(array, lead=0):
    return array.reshape(array.shape[:lead] + (2,) * len(BITS) + array.shape[lead + 1 :])


def step_pairs(count, step):
    return [(i, i + step) for i in range(count) if 0 <= i + step < count]


def lane_rows(length):
    return -(-length // 1024) * 8


def as_lanes(flat):
    rows = lane_rows(flat.shape[-1])
    gap = rows * 128 - flat.shape[-1]
    padded = jnp.pad(flat, [(0, 0)] * (flat.ndim - 1) + [(0, gap)])
    return padded.reshape(flat.shape[:-1] + (rows, 128))


def shifted(line_ref, row, lane, first, rows, stride):
    spots = lax.broadcasted_iota(jnp.int32, (rows, 128), 1)
    turn = lax.rem(128 - lane, 128)
    here = pltpu.roll(line_ref[pl.ds(row + first, rows, stride=stride), :], turn, 1)
    there = pltpu.roll(line_ref[pl.ds(row + first + 1, rows, stride=stride), :], turn, 1)
    return jnp.where(spots < 128 - lane, here, there)


def blocks_kernel(
    shape,
    place_ref,
    stem_ref,
    after_ref,
    layer_ref,
    before_ref,
    head_ref,
    block_ref,
    embed_ref,
    vector_ref,
    line_ref,
    flat_ref,
):
    front, stem_piece, layer_piece, tail = shape
    stem_lines = stem_ref.shape[1]
    end_row, end_lane = stem_piece // 128, stem_piece % 128
    after_lines = after_ref.shape[1]
    slot = head_ref.shape[1]
    for model in range(2):
        line_ref[pl.ds(0, front), :] = jnp.zeros((front, 128), single)
        line_ref[pl.ds(front, end_row), :] = stem_ref[model, pl.ds(0, end_row), :]
        turned = pltpu.roll(after_ref[model], end_lane, 1)
        spots = lax.broadcasted_iota(jnp.int32, (after_lines, 128), 1)
        line_ref[pl.ds(front + end_row, after_lines), :] = turned
        line_ref[pl.ds(front + end_row + after_lines, 128), :] = jnp.zeros((128, 128), single)
        lower = pltpu.roll(turned, 1, 0)
        first_line = jnp.broadcast_to(stem_ref[model, pl.ds(end_row, 1), :], (after_lines, 128))
        number = lax.broadcasted_iota(jnp.int32, (after_lines, 128), 0)
        lower = jnp.where(number == 0, first_line, lower)
        line_ref[pl.ds(front + end_row, after_lines), :] = jnp.where(spots < end_lane, lower, turned)
        per_row = ROW // 128
        for chunk in range(per_row):
            head_ref[model, :, pl.ds(chunk * 128, 128)] = shifted(
                line_ref, place_ref[0], place_ref[1], chunk, slot, per_row
            ).astype(narrow)
        for chunk in range(D // 128):
            embed_ref[model, :, pl.ds(chunk * 128, 128)] = shifted(
                line_ref, place_ref[2], place_ref[3], chunk, embed_ref.shape[1], D // 128
            ).astype(narrow)
    tail_lines = tail // 128
    layer_lines = layer_ref.shape[1]
    vector_at = tail + layer_piece - tail
    for part in range(layer_ref.shape[0]):
        flat_ref[pl.ds(0, tail_lines), :] = before_ref[part]
        flat_ref[pl.ds(tail_lines, layer_lines), :] = layer_ref[part]
        for chunk in range(D // 128):
            block_ref[part, :, pl.ds(chunk * 128, 128)] = shifted(
                flat_ref, place_ref[4], place_ref[5], chunk, block_ref.shape[1], D // 128
            ).astype(narrow)
            vector_ref[part, :, pl.ds(chunk * 128, 128)] = shifted(
                flat_ref, vector_at // 128, vector_at % 128, chunk, 8, D // 128
            ).astype(narrow)


def own_blocks(place, stems, after, layer_rows, before, shape, slot, block_rows, embed_rows):
    front, stem_piece, layer_piece, tail = shape
    lines = front + stem_piece // 128 + after.shape[1] + slot * ROW // 128
    flats = tail // 128 + layer_rows.shape[1] + 48
    return pl.pallas_call(
        lambda *refs: blocks_kernel(shape, *refs),
        out_shape=[
            jax.ShapeDtypeStruct((2, slot, ROW), narrow),
            jax.ShapeDtypeStruct((2 * LAYERS, block_rows, D), narrow),
            jax.ShapeDtypeStruct((2, embed_rows, D), narrow),
            jax.ShapeDtypeStruct((2 * LAYERS, 8, D), narrow),
        ],
        in_specs=[pl.BlockSpec(memory_space=pltpu.SMEM)] + [pl.BlockSpec(memory_space=pltpu.VMEM)] * 4,
        out_specs=[pl.BlockSpec(memory_space=pltpu.VMEM)] * 4,
        scratch_shapes=[pltpu.VMEM((lines, 128), single), pltpu.VMEM((flats, 128), single)],
        compiler_params=pltpu.CompilerParams(vmem_limit_bytes=40 << 20),
    )(place, stems, after, layer_rows, before)


def shards_kernel(held, place_ref, head_ref, previous_ref, block_ref, behind_ref, *refs):
    stem_ref, layer_ref = refs[held : held + 2]
    line_ref, flat_ref = refs[-2:]
    per_row = ROW // 128
    extra = previous_ref.shape[0]
    slot = head_ref.shape[0]
    for chunk in range(per_row):
        spot = pl.ds(chunk * 128, 128)
        line_ref[pl.ds(chunk, extra, stride=per_row), :] = previous_ref[:, spot]
        line_ref[pl.ds(extra * per_row + chunk, slot, stride=per_row), :] = head_ref[:, spot]
    stem_ref[...] = shifted(line_ref, place_ref[0], place_ref[1], 0, stem_ref.shape[0], 1)
    per_row = D // 128
    rows = block_ref.shape[2]
    for part in range(block_ref.shape[0]):
        for chunk in range(per_row):
            flat_ref[pl.ds(chunk, rows, stride=per_row), :] = block_ref[part, chunk]
            flat_ref[pl.ds(rows * per_row + chunk, 6, stride=per_row), :] = behind_ref[part, chunk]
        layer_ref[part] = shifted(flat_ref, place_ref[2], place_ref[3], 0, layer_ref.shape[1], 1)


def own_shards(place, head_grad, previous, block_grad, behind, stem_lines, layer_lines, held):
    per_row = ROW // 128
    lines = (head_grad.shape[0] + previous.shape[0]) * per_row + 256
    flats = max(block_grad.shape[2] * 3 + 18, layer_lines + 18) + 16
    return pl.pallas_call(
        lambda *refs: shards_kernel(len(held), *refs),
        out_shape=[
            jax.ShapeDtypeStruct((stem_lines, 128), single),
            jax.ShapeDtypeStruct((block_grad.shape[0], layer_lines, 128), single),
        ]
        + [jax.ShapeDtypeStruct(array.shape, array.dtype) for array in held],
        in_specs=[pl.BlockSpec(memory_space=pltpu.SMEM)]
        + [pl.BlockSpec(memory_space=pltpu.VMEM)] * 4
        + [pl.BlockSpec(memory_space=pl.ANY)] * len(held),
        out_specs=[pl.BlockSpec(memory_space=pltpu.VMEM)] * 2 + [pl.BlockSpec(memory_space=pl.ANY)] * len(held),
        input_output_aliases={5 + number: 2 + number for number in range(len(held))},
        scratch_shapes=[pltpu.VMEM((lines, 128), single), pltpu.VMEM((flats, 128), single)],
        compiler_params=pltpu.CompilerParams(vmem_limit_bytes=40 << 20),
    )(place, head_grad, previous, block_grad, behind, *held)


PAD_SEQ = 272
GELU_SCALE = 0.7978845608028654
GELU_CUBE = 0.044715


def product_plain(left, right):
    return lax.dot_general(left, right, (((1,), (0,)), ((), ())), preferred_element_type=single)


def product_right(left, right):
    return lax.dot_general(left, right, (((1,), (1,)), ((), ())), preferred_element_type=single)


def product_left(left, right):
    return lax.dot_general(left, right, (((0,), (0,)), ((), ())), preferred_element_type=single)


def norm_parts(values):
    centred = values - jnp.mean(values, axis=-1, keepdims=True)
    spread = lax.rsqrt(jnp.mean(centred * centred, axis=-1, keepdims=True) + 1e-06)
    return centred * spread, spread


def norm_back(grad, unit, spread, gain):
    grad_unit = grad * gain
    mean_one = jnp.mean(grad_unit, axis=-1, keepdims=True)
    mean_two = jnp.mean(grad_unit * unit, axis=-1, keepdims=True)
    return spread * (grad_unit - mean_one - unit * mean_two)


def gelu_tanh(values):
    return jnp.tanh(GELU_SCALE * (values + GELU_CUBE * values * values * values))


def gelu_value(values):
    return 0.5 * values * (1.0 + gelu_tanh(values))


def gelu_slope(values):
    bent = gelu_tanh(values)
    return 0.5 * (1.0 + bent) + 0.5 * values * (1.0 - bent * bent) * GELU_SCALE * (
        1.0 + 3.0 * GELU_CUBE * values * values
    )


def head_copies(plan, side_ref, gathered_ref, one_ref, two_ref, lines_ref, sems):
    quarter = gathered_ref.shape[0] // 2
    shift = side_ref[0] * quarter
    targets = (one_ref, two_ref, lines_ref)
    copies = []
    for number, (at, owner, first, rows, target, row) in enumerate(plan):
        spot = at + shift if at < quarter else at - shift
        copies.append(
            pltpu.make_async_copy(
                gathered_ref.at[spot, owner, pl.ds(first, rows)],
                targets[target].at[pl.ds(row, rows)],
                sems.at[number],
            )
        )
    for copy in copies:
        copy.start()
    return [[copy for copy, item in zip(copies, plan) if item[4] == target] for target in range(3)]


def wait_all(copies):
    for copy in copies:
        copy.wait()


def spread_third(lines_ref, wide_ref, third_ref):
    groups = ROW // BOT
    for lane in range(BOT // 128):
        for group in range(groups):
            at = group * BOT + lane * 128
            wide_ref[lane, pl.ds(group, lines_ref.shape[0], stride=groups), :] = lines_ref[
                :, at : at + 128
            ].astype(single)
        third_ref[:, pl.ds(lane * 128, 128)] = wide_ref[lane].astype(narrow)


def head_up_kernel(
    plan, side_ref, normed_ref, gathered_ref, unit_ref, acts_ref, bottle_ref, pre_one_ref, pre_two_ref,
    one_ref, two_ref, lines_ref, wide_ref, third_ref, sems,
):
    copies = head_copies(plan, side_ref, gathered_ref, one_ref, two_ref, lines_ref, sems)
    acts_ref[...] = jnp.zeros_like(acts_ref)
    normed = normed_ref[...]
    acts_ref[:, pl.ds(0, D)] = normed
    piece = HID // 4
    wait_all(copies[0])
    for number in range(4):
        spot = pl.ds(number * piece, piece)
        pre = product_plain(normed, one_ref[:, spot])
        pre_one_ref[:, spot] = pre
        acts_ref[:, pl.ds(D + number * piece, piece)] = gelu_value(pre).astype(narrow)
    wait_all(copies[2])
    spread_third(lines_ref, wide_ref, third_ref)
    wait_all(copies[1])
    hidden = acts_ref[:, pl.ds(D, HID)]
    for number in range(4):
        spot = pl.ds(number * piece, piece)
        pre = product_plain(hidden, two_ref[:, spot])
        pre_two_ref[:, spot] = pre
        acts_ref[:, pl.ds(D + HID + number * piece, piece)] = gelu_value(pre).astype(narrow)
    bottle = product_plain(acts_ref[:, pl.ds(D + HID, HID)], third_ref[...])
    bottle_ref[...] = bottle
    unit_ref[...] = (
        bottle * lax.rsqrt(jnp.sum(bottle * bottle, axis=-1, keepdims=True) + 1e-06)
    ).astype(narrow)


def head_down_kernel(
    plan, side_ref, grad_ref, bottle_ref, pre_one_ref, pre_two_ref, gathered_ref, grads_ref, normed_grad_ref,
    one_ref, two_ref, lines_ref, wide_ref, third_ref, sems,
):
    copies = head_copies(plan, side_ref, gathered_ref, one_ref, two_ref, lines_ref, sems)
    grad, bottle = grad_ref[...], bottle_ref[...]
    scale = lax.rsqrt(jnp.sum(bottle * bottle, axis=-1, keepdims=True) + 1e-06)
    along = jnp.sum(grad * bottle, axis=-1, keepdims=True)
    grad_bottle = (scale * (grad - bottle * (along * scale * scale))).astype(narrow)
    grads_ref[:, pl.ds(2 * HID, BOT)] = grad_bottle
    wait_all(copies[2])
    spread_third(lines_ref, wide_ref, third_ref)
    piece = HID // 4
    for number in range(4):
        spot = pl.ds(number * piece, piece)
        back = product_right(grad_bottle, third_ref[spot, :])
        grads_ref[:, pl.ds(HID + number * piece, piece)] = (back * gelu_slope(pre_two_ref[:, spot])).astype(narrow)
    wait_all(copies[1])
    grad_two = grads_ref[:, pl.ds(HID, HID)]
    for number in range(4):
        spot = pl.ds(number * piece, piece)
        back = product_right(grad_two, two_ref[spot, :])
        grads_ref[:, spot] = (back * gelu_slope(pre_one_ref[:, spot])).astype(narrow)
    wait_all(copies[0])
    normed_grad_ref[...] = product_right(grads_ref[:, pl.ds(0, HID)], one_ref[...])


def head_pass(kernel, plan, side, inputs, gathered, shapes, waits=()):
    read = len(inputs) + 2
    return pl.pallas_call(
        lambda *refs: kernel(plan, *refs[:read], *refs[read + len(waits) :]),
        out_shape=shapes,
        in_specs=[pl.BlockSpec(memory_space=pltpu.SMEM)]
        + [pl.BlockSpec(memory_space=pltpu.VMEM)] * len(inputs)
        + [pl.BlockSpec(memory_space=pl.ANY)] * (1 + len(waits)),
        out_specs=[pl.BlockSpec(memory_space=pltpu.VMEM)] * len(shapes),
        scratch_shapes=[
            pltpu.VMEM((D, HID), narrow),
            pltpu.VMEM((HID, HID), narrow),
            pltpu.VMEM((BOT, ROW), narrow),
            pltpu.VMEM((BOT // 128, HID, 128), single),
            pltpu.VMEM((HID, BOT), narrow),
            pltpu.SemaphoreType.DMA((len(plan),)),
        ],
        compiler_params=pltpu.CompilerParams(vmem_limit_bytes=56 << 20),
        cost_estimate=pl.CostEstimate(flops=100 * 10**6, bytes_accessed=370 * 10**5, transcendentals=0),
    )(side, *inputs, gathered, *waits)


def fetch_rows(side_ref, part, gathered_ref, flat_ref, sems):
    quarter = flat_ref.shape[0] // 4
    side = side_ref[0]
    first, second = side * quarter, (1 - side) * quarter
    copies = [
        pltpu.make_async_copy(
            gathered_ref.at[pl.ds(at, quarter), owner, part],
            flat_ref.at[pl.ds(spot * quarter, quarter)],
            sems.at[spot],
        )
        for spot, (at, owner) in enumerate(((first, 0), (second, 0), (second, 1), (first, 1)))
    ]
    for copy in copies:
        copy.start()
    for copy in copies:
        copy.wait()


def matrix_rows(flat_ref, first_row, length):
    rows = flat_ref.shape[1]
    low, high = first_row // rows, -(-(first_row + length) // rows)
    lines = flat_ref[pl.ds(low, high - low)].reshape((high - low) * rows, D)
    at = first_row - low * rows
    return lines[at : at + length]


def spread_columns(flat_ref, first_row, width, wide_ref, out_ref):
    length = width * D
    lines = matrix_rows(flat_ref, first_row, length)
    for column in range(D // 128):
        lane = slice(column * 128, (column + 1) * 128)
        wide_ref[column, pl.ds(0, length), :] = lines[:, lane].astype(single)
    for group in range(width):
        for column in range(D // 128):
            out_ref[group, :, pl.ds(column * 128, 128)] = wide_ref[
                column, pl.ds(group, D, stride=width), :
            ].astype(narrow)


def head_lanes(values, odd):
    lanes = lax.broadcasted_iota(jnp.int32, values.shape, 1)
    return jnp.where((lanes >= HEAD_DIM) == odd, values, jnp.zeros_like(values))


def join_lanes(even, odd):
    lanes = lax.broadcasted_iota(jnp.int32, even.shape, 1)
    return jnp.where(lanes >= HEAD_DIM, odd, even)


def soft_rows(query, key):
    scores = product_right(query, key) * HEAD_DIM ** (-0.5)
    spots = lax.broadcasted_iota(jnp.int32, scores.shape, 1)
    scores = jnp.where(spots < SEQ, scores, -1e30)
    terms = jnp.exp(scores - jnp.max(scores, axis=-1, keepdims=True))
    return terms / jnp.sum(terms, axis=-1, keepdims=True)


def forward_kernel(part, keep, side_ref, stream_ref, vector_ref, gathered_ref, *refs):
    out_ref = refs[0]
    if keep:
        packed_ref, mixed_ref, attn_ref, pre_ref, mlp_ref = refs[1:6]
        flat_ref, wide_ref, qkv_ref, up_ref, hidden_ref, sems = refs[6:]
    else:
        flat_ref, wide_ref, qkv_ref, up_ref, hidden_ref, packed_ref, mixed_ref, sems = refs[1:]
    fetch_rows(side_ref, part, gathered_ref, flat_ref, sems)
    spread_columns(flat_ref, 0, 3, wide_ref, qkv_ref)
    spread_columns(flat_ref, 4 * D, FF // D, wide_ref, up_ref)
    w_proj = matrix_rows(flat_ref, 3 * D, D)
    w_down = matrix_rows(flat_ref, 4 * D + FF, FF)
    vectors = vector_ref[...].astype(single)
    stream = stream_ref[...]
    normed = (norm_parts(stream)[0] * vectors[0:1] + vectors[1:2]).astype(narrow)
    for group in range(3):
        packed_ref[:, pl.ds(group * D, D)] = product_plain(normed, qkv_ref[group]).astype(narrow)
    for image in range(stream.shape[0] // PAD_SEQ):
        rows = pl.ds(image * PAD_SEQ, PAD_SEQ)
        for pair in range(HEADS // 2):
            query, key, value = [
                packed_ref[rows, pl.ds(group * D + pair * 128, 128)] for group in range(3)
            ]
            done = [
                product_plain(soft_rows(head_lanes(query, odd), key).astype(narrow), value)
                for odd in (False, True)
            ]
            mixed_ref[rows, pl.ds(pair * 128, 128)] = join_lanes(*done).astype(narrow)
    attn = product_plain(mixed_ref[...], w_proj)
    middle = stream + vectors[2:3] * attn
    normed_two = (norm_parts(middle)[0] * vectors[3:4] + vectors[4:5]).astype(narrow)
    for group in range(FF // D):
        spot = pl.ds(group * D, D)
        pre = product_plain(normed_two, up_ref[group])
        if keep:
            pre_ref[:, spot] = pre
        hidden_ref[:, spot] = (0.5 * pre * (1.0 + gelu_tanh(pre))).astype(narrow)
    mlp = product_plain(hidden_ref[...], w_down)
    out_ref[...] = middle + vectors[5:6] * mlp
    if keep:
        attn_ref[...] = attn
        mlp_ref[...] = mlp


def layer_scratch(gathered):
    rows, blocks = gathered.shape[3], 2 * gathered.shape[0]
    return [
        pltpu.VMEM((blocks, rows, D), narrow),
        pltpu.VMEM((D // 128, FF, 128), single),
        pltpu.VMEM((3, D, D), narrow),
        pltpu.VMEM((FF // D, D, D), narrow),
    ]


def layer_specs_in(count):
    return (
        [pl.BlockSpec(memory_space=pltpu.SMEM)]
        + [pl.BlockSpec(memory_space=pltpu.VMEM)] * (count - 2)
        + [pl.BlockSpec(memory_space=pl.ANY)]
    )


def layer_forward(side, stream, vectors, gathered, part, keep):
    tokens = stream.shape[0]
    shapes = [jax.ShapeDtypeStruct((tokens, D), single)]
    extra = [
        jax.ShapeDtypeStruct((tokens, 3 * D), narrow),
        jax.ShapeDtypeStruct((tokens, D), narrow),
        jax.ShapeDtypeStruct((tokens, D), single),
        jax.ShapeDtypeStruct((tokens, FF), single),
        jax.ShapeDtypeStruct((tokens, D), single),
    ]
    scratch = layer_scratch(gathered) + [pltpu.VMEM((tokens, FF), narrow)]
    if keep:
        shapes = shapes + extra
    else:
        scratch = scratch + [pltpu.VMEM((tokens, 3 * D), narrow), pltpu.VMEM((tokens, D), narrow)]
    scratch.append(pltpu.SemaphoreType.DMA((4,)))
    return pl.pallas_call(
        lambda *refs: forward_kernel(part, keep, *refs),
        out_shape=shapes,
        in_specs=layer_specs_in(4),
        out_specs=[pl.BlockSpec(memory_space=pltpu.VMEM)] * len(shapes),
        scratch_shapes=scratch,
        compiler_params=pltpu.CompilerParams(vmem_limit_bytes=56 << 20),
        cost_estimate=pl.CostEstimate(flops=100 * 10**6, bytes_accessed=430 * 10**5, transcendentals=0),
    )(side, stream, vectors, gathered)


def mlp_back_kernel(
    part,
    side_ref,
    grad_ref,
    stream_ref,
    attn_ref,
    pre_ref,
    mlp_ref,
    vector_ref,
    gathered_ref,
    *refs,
):
    grad_mid_ref, weight_grad_ref, vector_grad_ref = refs[-9:-6]
    flat_ref, wide_ref, up_ref, hidden_ref, grad_pre_ref, sems = refs[-6:]
    lead = weight_grad_ref.shape[1] - 2 * FF
    weight_grad_ref[:, pl.ds(0, lead), :] = jnp.zeros((D // 128, lead, 128), single)
    fetch_rows(side_ref, part, gathered_ref, flat_ref, sems)
    spread_columns(flat_ref, 4 * D, FF // D, wide_ref, up_ref)
    w_down = matrix_rows(flat_ref, 4 * D + FF, FF)
    vectors = vector_ref[...].astype(single)
    grad_out = grad_ref[...]
    vector_grad_ref[...] = jnp.zeros_like(vector_grad_ref)
    attn = attn_ref[...]
    middle = stream_ref[...] + vectors[2:3] * attn
    unit_two, spread_two = norm_parts(middle)
    normed_two = (unit_two * vectors[3:4] + vectors[4:5]).astype(narrow)
    vector_grad_ref[pl.ds(5, 1), :] = jnp.sum(grad_out * mlp_ref[...], axis=0, keepdims=True)
    grad_mlp = (grad_out * vectors[5:6]).astype(narrow)
    grad_normed_two = jnp.zeros_like(grad_out)
    for group in range(FF // D):
        spot = pl.ds(group * D, D)
        pre = pre_ref[:, spot]
        bent = gelu_tanh(pre)
        hidden_ref[:, spot] = (0.5 * pre * (1.0 + bent)).astype(narrow)
        slope = 0.5 * (1.0 + bent) + 0.5 * pre * (1.0 - bent * bent) * GELU_SCALE * (
            1.0 + 3.0 * GELU_CUBE * pre * pre
        )
        grad_hidden = product_right(grad_mlp, w_down[group * D : (group + 1) * D])
        grad_pre = (grad_hidden * slope).astype(narrow)
        grad_pre_ref[:, spot] = grad_pre
        grad_normed_two = grad_normed_two + product_right(grad_pre, up_ref[group])
    for group in range(FF // D):
        spot = pl.ds(group * D, D)
        up_grad = product_left(normed_two, grad_pre_ref[:, spot])
        down_grad = product_left(hidden_ref[:, spot], grad_mlp)
        for column in range(D // 128):
            lane = slice(column * 128, (column + 1) * 128)
            weight_grad_ref[column, pl.ds(lead + group, D, stride=FF // D), :] = up_grad[:, lane]
            weight_grad_ref[column, pl.ds(lead + FF + group * D, D), :] = down_grad[:, lane]
    vector_grad_ref[pl.ds(3, 1), :] = jnp.sum(grad_normed_two * unit_two, axis=0, keepdims=True)
    vector_grad_ref[pl.ds(4, 1), :] = jnp.sum(grad_normed_two, axis=0, keepdims=True)
    grad_mid = grad_out + norm_back(grad_normed_two, unit_two, spread_two, vectors[3:4])
    vector_grad_ref[pl.ds(2, 1), :] = jnp.sum(grad_mid * attn, axis=0, keepdims=True)
    grad_mid_ref[...] = grad_mid


def attention_back_kernel(
    part,
    side_ref,
    grad_ref,
    stream_ref,
    packed_ref,
    mixed_ref,
    vector_ref,
    gathered_ref,
    *refs,
):
    grad_in_ref, weight_grad_ref, vector_grad_ref = refs[-9:-6]
    flat_ref, wide_ref, qkv_ref, grad_mixed_ref, grad_packed_ref, sems = refs[-6:]
    rest = weight_grad_ref.shape[1] - 4 * D
    weight_grad_ref[:, pl.ds(4 * D, rest), :] = jnp.zeros((D // 128, rest, 128), single)
    fetch_rows(side_ref, part, gathered_ref, flat_ref, sems)
    spread_columns(flat_ref, 0, 3, wide_ref, qkv_ref)
    w_proj = matrix_rows(flat_ref, 3 * D, D)
    vectors = vector_ref[...].astype(single)
    vector_grad_ref[...] = jnp.zeros_like(vector_grad_ref)
    grad_mid = grad_ref[...]
    stream = stream_ref[...]
    grad_attn = (grad_mid * vectors[2:3]).astype(narrow)
    proj_grad = product_left(mixed_ref[...], grad_attn)
    for column in range(D // 128):
        weight_grad_ref[column, pl.ds(3 * D, D), :] = proj_grad[:, column * 128 : (column + 1) * 128]
    grad_mixed_ref[...] = product_right(grad_attn, w_proj).astype(narrow)
    for image in range(stream.shape[0] // PAD_SEQ):
        rows = pl.ds(image * PAD_SEQ, PAD_SEQ)
        for pair in range(HEADS // 2):
            query, key, value = [
                packed_ref[rows, pl.ds(group * D + pair * 128, 128)] for group in range(3)
            ]
            grad_mixed = grad_mixed_ref[rows, pl.ds(pair * 128, 128)]
            parts = []
            for odd in (False, True):
                probs = soft_rows(head_lanes(query, odd), key)
                grad_probs = product_right(head_lanes(grad_mixed, odd), value)
                grad_value = product_left(probs.astype(narrow), grad_mixed)
                grad_scores = probs * (grad_probs - jnp.sum(probs * grad_probs, axis=-1, keepdims=True))
                grad_raw = (grad_scores * HEAD_DIM ** (-0.5)).astype(narrow)
                parts.append((product_plain(grad_raw, key), product_left(grad_raw, query), grad_value))
            for group in range(3):
                grad_packed_ref[rows, pl.ds(group * D + pair * 128, 128)] = join_lanes(
                    parts[0][group], parts[1][group]
                ).astype(narrow)
    unit_one, spread_one = norm_parts(stream)
    normed = (unit_one * vectors[0:1] + vectors[1:2]).astype(narrow)
    grad_normed = jnp.zeros_like(grad_mid)
    for group in range(3):
        grad_part = grad_packed_ref[:, pl.ds(group * D, D)]
        grad_normed = grad_normed + product_right(grad_part, qkv_ref[group])
        qkv_grad = product_left(normed, grad_part)
        for column in range(D // 128):
            lane = slice(column * 128, (column + 1) * 128)
            weight_grad_ref[column, pl.ds(group, D, stride=3), :] = qkv_grad[:, lane]
    vector_grad_ref[pl.ds(0, 1), :] = jnp.sum(grad_normed * unit_one, axis=0, keepdims=True)
    vector_grad_ref[pl.ds(1, 1), :] = jnp.sum(grad_normed, axis=0, keepdims=True)
    grad_in_ref[...] = grad_mid + norm_back(grad_normed, unit_one, spread_one, vectors[0:1])


def layer_back(kernel, part, weight_rows, side, inputs, vectors, gathered, waits, held, columns, buffers):
    tokens = inputs[0].shape[0]
    rows, blocks = gathered.shape[3], 2 * gathered.shape[0]
    return pl.pallas_call(
        lambda *refs: kernel(part, *refs[: len(refs) - 6 - len(held)], *refs[len(refs) - 6 :]),
        out_shape=[
            jax.ShapeDtypeStruct((tokens, D), single),
            jax.ShapeDtypeStruct((D // 128, weight_rows, 128), single),
            jax.ShapeDtypeStruct((8, D), single),
        ]
        + [jax.ShapeDtypeStruct(array.shape, array.dtype) for array in held],
        in_specs=layer_specs_in(len(inputs) + 3) + [pl.BlockSpec(memory_space=pl.ANY)] * (len(waits) + len(held)),
        out_specs=[pl.BlockSpec(memory_space=pltpu.VMEM)] * 3 + [pl.BlockSpec(memory_space=pl.ANY)] * len(held),
        input_output_aliases={len(inputs) + 3 + len(waits) + number: 3 + number for number in range(len(held))},
        scratch_shapes=[
            pltpu.VMEM((blocks, rows, D), narrow),
            pltpu.VMEM((D // 128, columns * D, 128), single),
            pltpu.VMEM((columns, D, D), narrow),
        ]
        + [pltpu.VMEM((tokens, width), narrow) for width in buffers]
        + [pltpu.SemaphoreType.DMA((4,))],
        compiler_params=pltpu.CompilerParams(vmem_limit_bytes=56 << 20),
        cost_estimate=pl.CostEstimate(flops=100 * 10**6, bytes_accessed=600 * 10**5, transcendentals=0),
    )(side, *inputs, vectors, gathered, *waits, *held)


def pair_rows_of(block_rows):
    pair = 2 * block_rows
    return 4 * D // pair * pair, -(-4 * D // pair) * pair


def mlp_back(side, grad_out, saved, vectors, gathered, part, waits, held):
    stream, packed, mixed, attn, pre, mlp = saved
    return layer_back(
        mlp_back_kernel, part, MATRIX_ROWS - pair_rows_of(gathered.shape[3])[0], side,
        (grad_out, stream, attn, pre, mlp), vectors, gathered, waits, held,
        FF // D, (FF, FF),
    )


def attention_back(side, grad_mid, saved, vectors, gathered, part, waits, held):
    stream, packed, mixed, attn, pre, mlp = saved
    return layer_back(
        attention_back_kernel, part, pair_rows_of(gathered.shape[3])[1], side,
        (grad_mid, stream, packed, mixed), vectors, gathered, waits, held,
        3, (D, 3 * D),
    )


def after(value, *tokens):
    def kernel(*refs):
        refs[-1][...] = refs[0][...]

    return pl.pallas_call(
        kernel,
        out_shape=jax.ShapeDtypeStruct(value.shape, value.dtype),
        in_specs=[pl.BlockSpec(memory_space=pltpu.VMEM)] + [pl.BlockSpec(memory_space=pl.ANY)] * len(tokens),
        out_specs=pl.BlockSpec(memory_space=pltpu.VMEM),
    )(value, *tokens)


def embed_back_kernel(grad_ref, patch_ref, shown_ref, gain_ref, vector_ref, *refs):
    out_ref = refs[-1]
    grad = grad_ref[...]
    images = grad.shape[0] // PAD_SEQ
    shown = shown_ref[...]
    position = jnp.zeros((PAD_SEQ, D), single)
    token = jnp.zeros((1, D), single)
    patch_grads = []
    for image in range(images):
        here = grad[image * PAD_SEQ : (image + 1) * PAD_SEQ]
        position = position + here
        rows = here[1:SEQ]
        seen = shown[image * PATCHES : (image + 1) * PATCHES]
        token = token + jnp.sum(rows * (1.0 - seen), axis=0, keepdims=True)
        patch_grads.append((rows * seen).astype(narrow))
    patch_grad = product_left(patch_ref[...], jnp.concatenate(patch_grads))
    out_ref[...] = jnp.zeros_like(out_ref)
    for column in range(D // 128):
        lane = slice(column * 128, (column + 1) * 128)
        out_ref[column, pl.ds(0, PIX), :] = patch_grad[:, lane]
        out_ref[column, pl.ds(PIX, SEQ), :] = position[:SEQ, lane]
        out_ref[column, pl.ds(PIX + SEQ, 1), :] = position[0:1, lane]
        out_ref[column, pl.ds(PIX + SEQ + 1, 1), :] = token[:, lane]
        out_ref[column, pl.ds(PIX + SEQ + 2, 2), :] = gain_ref[:, lane]
        out_ref[column, pl.ds(EMBED_ROWS, vector_ref.shape[0]), :] = vector_ref[:, lane]


def embed_back(grad, patch_rows, shown, gains, vector_grads, rows, waits):
    return pl.pallas_call(
        embed_back_kernel,
        out_shape=jax.ShapeDtypeStruct((D // 128, rows, 128), single),
        in_specs=[pl.BlockSpec(memory_space=pltpu.VMEM)] * 5 + [pl.BlockSpec(memory_space=pl.ANY)] * len(waits),
        out_specs=pl.BlockSpec(memory_space=pltpu.VMEM),
        compiler_params=pltpu.CompilerParams(vmem_limit_bytes=40 << 20),
        cost_estimate=pl.CostEstimate(flops=100 * 10**6, bytes_accessed=37 * 10**5, transcendentals=0),
    )(grad, patch_rows, shown, gains, vector_grads, *waits)


def proto_units(values):
    rounded = values.astype(narrow).astype(single)
    scale = lax.rsqrt(jnp.sum(rounded * rounded, axis=-1, keepdims=True) + 1e-06)
    return rounded, scale, (rounded * scale).astype(narrow)


def proto_terms(teacher_z, student_z, teacher_unit, student_unit, centre_column):
    teacher_logits = product_right(teacher_unit, teacher_z)
    logits = product_right(student_unit, student_z)
    teacher_exp = jnp.exp((teacher_logits - centre_column) * (1.0 / tau_teacher))
    student_exp = jnp.exp(logits * (1.0 / tau_student))
    return teacher_logits, logits, teacher_exp, student_exp


def logits_kernel(
    teacher_z_ref,
    student_z_ref,
    teacher_ref,
    student_ref,
    centre_ref,
    class_ref,
    mixed_ref,
    sums_ref,
    centre_sum_ref,
    student_mix_ref,
    teacher_mix_ref,
    totals_ref,
):
    step = pl.program_id(0)

    @pl.when(step == 0)
    def _():
        student_mix_ref[...] = jnp.zeros_like(student_mix_ref)
        teacher_mix_ref[...] = jnp.zeros_like(teacher_mix_ref)
        totals_ref[...] = jnp.zeros_like(totals_ref)

    teacher_unit = proto_units(teacher_ref[...])[2]
    student_unit = proto_units(student_ref[...])[2]
    teacher_logits, logits, teacher_exp, student_exp = proto_terms(
        teacher_z_ref[...], student_z_ref[...], teacher_unit, student_unit, centre_ref[...]
    )
    totals_ref[pl.ds(0, 1), :] += jnp.sum(teacher_exp, axis=0, keepdims=True)
    totals_ref[pl.ds(1, 1), :] += jnp.sum(student_exp, axis=0, keepdims=True)
    totals_ref[pl.ds(2, 1), :] += jnp.sum(teacher_exp * logits, axis=0, keepdims=True)
    centre_sum_ref[...] = jnp.sum(teacher_logits * class_ref[0:1], axis=1, keepdims=True)
    student_mix_ref[...] += product_left(student_unit, student_exp.astype(narrow))
    teacher_mix_ref[...] += product_left(student_unit, teacher_exp.astype(narrow))

    @pl.when(step == pl.num_programs(0) - 1)
    def _():
        mixed_ref[:, pl.ds(0, BOT)] = student_mix_ref[...].T
        mixed_ref[:, pl.ds(BOT, BOT)] = teacher_mix_ref[...].T
        lower = jnp.zeros((128 - totals_ref.shape[0], totals_ref.shape[1]), single)
        mixed_ref[:, pl.ds(2 * BOT, 128)] = jnp.concatenate([totals_ref[...], lower]).T
        sums_ref[...] = totals_ref[...]


def proto_specs(rows, block):
    whole = pl.BlockSpec((rows, BOT), lambda i: (0, 0))
    table = pl.BlockSpec((block, BOT), lambda i: (i, 0))
    column = pl.BlockSpec((block, 1), lambda i: (i, 0))
    lines = pl.BlockSpec((8, rows), lambda i: (0, 0))
    return whole, table, column, lines


def logits_pass(teacher_z, student_z, teacher, student, centre_column, class_lines):
    rows, protos_here = teacher_z.shape[0], student.shape[0]
    block = protos_here // 4
    whole, table, column, lines = proto_specs(rows, block)
    return pl.pallas_call(
        logits_kernel,
        grid=(4,),
        out_shape=[
            jax.ShapeDtypeStruct((rows, 2 * BOT + 128), single),
            jax.ShapeDtypeStruct((8, rows), single),
            jax.ShapeDtypeStruct((protos_here, 1), single),
        ],
        in_specs=[whole, whole, table, table, column, lines],
        out_specs=[pl.BlockSpec((rows, 2 * BOT + 128), lambda i: (0, 0)), lines, column],
        scratch_shapes=[
            pltpu.VMEM((BOT, rows), single),
            pltpu.VMEM((BOT, rows), single),
            pltpu.VMEM((8, rows), single),
        ],
        compiler_params=pltpu.CompilerParams(vmem_limit_bytes=56 << 20),
        cost_estimate=pl.CostEstimate(flops=100 * 10**6, bytes_accessed=520 * 10**5, transcendentals=0),
    )(teacher_z, student_z, teacher, student, centre_column, class_lines)


def proto_grad_kernel(
    held, teacher_z_ref, student_z_ref, teacher_ref, student_ref, centre_ref, scale_ref, *refs
):
    grad_ref, square_ref = refs[held : held + 2]
    step = pl.program_id(0)

    @pl.when(step == 0)
    def _():
        square_ref[...] = jnp.zeros_like(square_ref)

    teacher_unit = proto_units(teacher_ref[...])[2]
    rounded, scale, student_unit = proto_units(student_ref[...])
    student_z = student_z_ref[...]
    _, _, teacher_exp, student_exp = proto_terms(
        teacher_z_ref[...], student_z, teacher_unit, student_unit, centre_ref[...]
    )
    grad_logits = (student_exp * scale_ref[0:1] - teacher_exp * scale_ref[1:2]).astype(narrow)
    unit_grad = product_plain(grad_logits, student_z)
    along = jnp.sum(unit_grad * rounded, axis=-1, keepdims=True)
    grad = scale * (unit_grad - rounded * (along * scale * scale))
    grad_ref[...] = grad
    square_ref[...] += jnp.broadcast_to(jnp.sum(grad * grad), square_ref.shape)


def proto_grad_pass(teacher_z, student_z, teacher, student, centre_column, scale_lines, held):
    rows, protos_here = teacher_z.shape[0], student.shape[0]
    block = protos_here // 4
    whole, table, column, lines = proto_specs(rows, block)
    return pl.pallas_call(
        lambda *refs: proto_grad_kernel(len(held), *refs),
        grid=(4,),
        out_shape=[
            jax.ShapeDtypeStruct((protos_here, BOT), single),
            jax.ShapeDtypeStruct((8, 128), single),
        ]
        + [jax.ShapeDtypeStruct(array.shape, array.dtype) for array in held],
        in_specs=[whole, whole, table, table, column, lines]
        + [pl.BlockSpec(memory_space=pl.ANY)] * len(held),
        out_specs=[table, pl.BlockSpec((8, 128), lambda i: (0, 0))]
        + [pl.BlockSpec(memory_space=pl.ANY)] * len(held),
        input_output_aliases={6 + number: 2 + number for number in range(len(held))},
        compiler_params=pltpu.CompilerParams(vmem_limit_bytes=56 << 20),
        cost_estimate=pl.CostEstimate(flops=100 * 10**6, bytes_accessed=400 * 10**5, transcendentals=0),
    )(teacher_z, student_z, teacher, student, centre_column, scale_lines, *held)


def proto_update(factor, student, moment, second, teacher, grad):
    def kernel(factor_ref, *refs):
        weight, moment, second, teacher, grad = [ref[...] for ref in refs[:5]]
        done = adam_update(weight, moment, second, grad * factor_ref[0], teacher)
        for ref, value in zip(refs[5:], done):
            ref[...] = value

    block = student.shape[0] // 4
    table = pl.BlockSpec((block, BOT), lambda i: (i, 0))
    return pl.pallas_call(
        kernel,
        grid=(4,),
        out_shape=[
            jax.ShapeDtypeStruct(student.shape, narrow if number == 3 else single) for number in range(5)
        ],
        in_specs=[pl.BlockSpec(memory_space=pltpu.SMEM)] + [table] * 5,
        out_specs=[table] * 5,
        compiler_params=pltpu.CompilerParams(vmem_limit_bytes=60 << 20),
        cost_estimate=pl.CostEstimate(flops=10**7, bytes_accessed=2 * 10**7, transcendentals=0),
    )(factor.reshape(1), student, moment, second, teacher, grad)


def head_grads_kernel(
    held, place_ref, inputs_ref, grads_ref, *refs,
):
    own_ref, partner_ref = refs[len(refs) - 9 - held :][:2] if held else refs[-9:-7]
    window_ref, rows_ref, product_ref, third_ref, bottle_ref, line_ref, sems = refs[-7:]
    slot = own_ref.shape[0]
    lead = product_ref.shape[0] - window_ref.shape[1]
    number = lax.broadcasted_iota(jnp.int32, (slot, 1), 0)
    product_ref[pl.ds(0, lead), :] = jnp.zeros((lead, ROW), single)

    def block(at, out_ref):
        column = pl.multiple_of(place_ref[at], 128)
        grad_column = pl.multiple_of(place_ref[at + 3], 128)
        copies = [
            pltpu.make_async_copy(
                inputs_ref.at[:, pl.ds(column, window_ref.shape[1])], window_ref, sems.at[0]
            ),
            pltpu.make_async_copy(grads_ref.at[:, pl.ds(grad_column, ROW)], rows_ref, sems.at[1]),
        ]
        for copy in copies:
            copy.start()
        for copy in copies:
            copy.wait()
        window = window_ref[...]
        for piece in range(4):
            spot = pl.ds(piece * (ROW // 4), ROW // 4)
            product_ref[pl.ds(lead, window.shape[1]), spot] = product_left(window, rows_ref[:, spot])
        from_row = pl.multiple_of(lead + place_ref[at + 1], 8)
        kept = jnp.where(number < place_ref[at + 2], product_ref[pl.ds(from_row, slot), :], 0.0)
        out_ref[...] = kept.astype(out_ref.dtype)

    @pl.when(place_ref[8] == 0)
    def _():
        block(0, own_ref)

    @pl.when(place_ref[8] == 1)
    def _():
        column = pl.multiple_of(place_ref[9], 128)
        copies = [
            pltpu.make_async_copy(
                inputs_ref.at[:, pl.ds(column, third_ref.shape[1])], third_ref, sems.at[0]
            ),
            pltpu.make_async_copy(grads_ref.at[:, pl.ds(2 * HID, BOT)], bottle_ref, sems.at[1]),
        ]
        for copy in copies:
            copy.start()
        for copy in copies:
            copy.wait()
        third = product_left(third_ref[...], bottle_ref[...])
        for lane in range(BOT // 128):
            line_ref[lane] = third[:, lane * 128 : (lane + 1) * 128]
        for group in range(ROW // BOT):
            for lane in range(BOT // 128):
                value = line_ref[lane, pl.ds(group, slot, stride=ROW // BOT), :]
                own_ref[:, pl.ds(group * BOT + lane * 128, 128)] = jnp.where(
                    number < place_ref[2], value, 0.0
                )

    block(4, partner_ref)


def head_grads(place, inputs_all, grads_all, slot, lead, waits, held):
    rows = inputs_all.shape[0]
    wide = slot * ROW // BOT
    return pl.pallas_call(
        lambda *refs: head_grads_kernel(len(held), *refs),
        out_shape=[jax.ShapeDtypeStruct((slot, ROW), kind) for kind in (single, narrow)]
        + [jax.ShapeDtypeStruct(array.shape, array.dtype) for array in held],
        in_specs=[pl.BlockSpec(memory_space=pltpu.SMEM)]
        + [pl.BlockSpec(memory_space=pl.ANY)] * (2 + len(waits) + len(held)),
        out_specs=[pl.BlockSpec(memory_space=pltpu.VMEM)] * 2
        + [pl.BlockSpec(memory_space=pl.ANY)] * len(held),
        input_output_aliases={3 + len(waits) + number: 2 + number for number in range(len(held))},
        scratch_shapes=[
            pltpu.VMEM((rows, 256), narrow),
            pltpu.VMEM((rows, ROW), narrow),
            pltpu.VMEM((lead + 256, ROW), single),
            pltpu.VMEM((rows, wide), narrow),
            pltpu.VMEM((rows, BOT), narrow),
            pltpu.VMEM((BOT // 128, wide, 128), single),
            pltpu.SemaphoreType.DMA((2,)),
        ],
        compiler_params=pltpu.CompilerParams(vmem_limit_bytes=56 << 20),
        cost_estimate=pl.CostEstimate(flops=100 * 10**6, bytes_accessed=370 * 10**5, transcendentals=0),
    )(place, inputs_all, grads_all, *waits, *held)


def close_local(
    patches,
    masked,
    slot_used,
    stem,
    stem_moment,
    stem_second,
    stem_teacher,
    layers,
    layer_moment,
    layer_second,
    layer_teacher,
    protos,
    proto_moment,
    proto_second,
    proto_teacher,
    centre,
):
    count = 1 << len(BITS)
    half = count // 2
    me = lax.axis_index("dev")
    across = MASKS["b"]
    student_side = me >= half
    groups = [list(range(half)), list(range(half, count))]
    quarter = half // 2
    swap = jnp.where(student_side, quarter, 0)
    side = student_side.astype(jnp.int32).reshape(1)
    images_here = patches.shape[0]
    rows_here = images_here * 17
    pair_rows = -(-2 * rows_here // 16) * 16
    more_rows = pair_rows - 2 * rows_here
    stem_piece = stem.shape[0]
    layer_piece = layers.shape[1]
    block_rows = MATRIX_ROWS // count
    block = block_rows * D
    tail = layer_piece * count - MATRIX_ROWS * D
    drift = layer_piece - block
    bounds = head_bounds(count, stem_piece)
    sizes = [bounds[i + 1] - bounds[i] for i in range(count)]
    slot = max(sizes)
    starts = [b * ROW + EMBED_FLAT - stem_piece * i for i, b in enumerate(bounds[:-1])]
    first_w2 = bounds.index(D)
    first_w3 = bounds.index(D + HID)
    row_index = jnp.concatenate([jnp.zeros((images_here, 1), jnp.int32), masked + 1], axis=1)
    masked_here = jnp.any(
        masked[:, :, None] == jnp.arange(PATCHES, dtype=jnp.int32)[None, None, :], axis=1
    )
    kept = slot_used.astype(single)

    front = 16
    early_rows = -(-stem_piece // D)
    late_start = early_rows * D - stem_piece
    embed_rows = -(-early_rows // 16) * 16
    own_layers = jnp.concatenate([layer_teacher, layers])
    own_tail = own_layers[:, layer_piece - tail :].reshape(2 * LAYERS, tail // 128, 128)
    before = lax.ppermute(own_tail, "dev", step_pairs(count, 1))
    head_span = GROUP * ROW
    stems = jnp.stack([as_lanes(stem_teacher), as_lanes(stem)])
    stems_next = lax.ppermute(stems[:, : head_span // 128], "dev", step_pairs(count, -1))
    def per_device(rows):
        return lax.dynamic_slice(jnp.array(rows, jnp.int32), (me, 0), (1, len(rows[0]))).reshape(-1)

    def spots(*values):
        return [part for value in values for part in (value // 128, value % 128)]

    place = per_device(
        [
            spots(starts[i] + front * 128, front * 128 + (0 if i == 0 else late_start), tail - drift * i)
            for i in range(count)
        ]
    )
    head_blocks, layer_blocks, embed_blocks, vector_blocks = own_blocks(
        place,
        stems,
        stems_next,
        as_lanes(own_layers),
        before,
        (front, stem_piece, layer_piece, tail),
        slot,
        block_rows,
        embed_rows,
    )

    other_layers = lax.ppermute(layer_blocks, "dev", pairs(count, across))
    both_layers = jnp.where(
        student_side,
        jnp.stack([other_layers, layer_blocks]),
        jnp.stack([layer_blocks, other_layers]),
    )
    gathered = lax.all_gather(both_layers, "dev", axis=0, axis_index_groups=groups)
    head_out = jnp.where(student_side, head_blocks[0], head_blocks[1])
    head_keep = jnp.where(student_side, head_blocks[1], head_blocks[0])
    head_got = lax.ppermute(head_out, "dev", pairs(count, across))
    both_head = jnp.where(
        student_side, jnp.stack([head_got, head_keep]), jnp.stack([head_keep, head_got])
    )

    vectors = lax.ppermute(vector_blocks, "dev", [(count - 1, 0)])
    seed = jnp.concatenate([embed_blocks.reshape(2 * embed_rows, D), vectors.reshape(8 * 2 * LAYERS, D)])
    third = -(-seed.shape[0] // 48) * 16
    spread_parts = []
    for number, order in enumerate(("xyba", "baxy", "ybax")):
        spread = seed[number * third : (number + 1) * third]
        reached = [0, 1]
        for name in order:
            moves = [(i, i ^ MASKS[name]) for i in reached]
            got = lax.ppermute(spread, "dev", moves)
            targets = [t for s, t in moves]
            is_target = jnp.array([i in targets for i in range(count)])[me]
            spread = jnp.where(is_target, got, spread)
            reached = reached + targets
        spread_parts.append(spread)
    spread = jnp.concatenate(spread_parts)
    other = lax.ppermute(spread, "dev", pairs(count, 1))
    is_even = me % 2 == 0
    even = jnp.where(is_even, spread, other)
    odd = jnp.where(is_even, other, spread)
    embed_all = [
        jnp.concatenate(
            [
                even[m * embed_rows : m * embed_rows + early_rows],
                odd[m * embed_rows : m * embed_rows + EMBED_ROWS - early_rows],
            ]
        )
        for m in range(2)
    ]
    all_rows = half * pair_rows
    kept_row = jnp.broadcast_to(kept[:, None], (images_here, 17)).reshape(1, rows_here)
    kept_pair = cube_gather(kept_row, "b").reshape(1, 2 * rows_here)
    kept_pair = jnp.pad(kept_pair, ((0, 0), (0, more_rows)))
    all_kept = cube_gather(kept_pair, "xygc").reshape(all_rows)
    gathered_head = lax.all_gather(after(both_head, gathered, even, odd, all_kept), "dev", axis=0, axis_index_groups=groups)
    vectors_all = even[2 * embed_rows :].reshape(2, LAYERS, 8, D)

    plan = []
    for i in range(1, count):
        target = 0 if i < first_w2 else 1 if i < first_w3 else 2
        row = bounds[i] - (0, D, D + HID)[target]
        skip = max(-row, 0)
        owner = 1 if i >= half else 0
        plan.append((i ^ across if owner else i, owner, skip, sizes[i] - skip, target, row + skip))

    def embed_parts(model):
        rows = embed_all[model]
        return (rows[:PIX], rows[PIX : PIX + SEQ], rows[PIX + SEQ :], None, None, None)

    def head_rows(stream, extras):
        chosen = jnp.take_along_axis(stream, row_index[:, :, None], axis=1).reshape(rows_here, D)
        normed = layer_norm(chosen, extras[2].astype(single), extras[3].astype(single)).astype(narrow)
        return chosen, normed

    def start_rows(parts, student):
        stream = embed(parts, patches, masked_here, student)
        return jnp.pad(stream, ((0, 0), (0, PAD_SEQ - SEQ), (0, 0))).reshape(images_here * PAD_SEQ, D)

    student_parts = embed_parts(1)
    stream = start_rows(student_parts, True)
    saved_layers = []
    for layer_index in range(LAYERS):
        before_layer = stream
        stream, *saved = layer_forward(
            side, stream, vectors_all[1, layer_index], gathered, LAYERS + layer_index, True
        )
        saved_layers.append((before_layer, *saved))
    teacher_parts = embed_parts(0)
    teacher_stream = start_rows(teacher_parts, False)
    for layer_index in range(LAYERS):
        teacher_stream = layer_forward(
            side, teacher_stream, vectors_all[0, layer_index], gathered, layer_index, False
        )[0]
    stream = stream.reshape(images_here, PAD_SEQ, D)
    teacher_stream = teacher_stream.reshape(images_here, PAD_SEQ, D)
    chosen, student_normed = head_rows(stream, student_parts[2])
    teacher_normed = head_rows(teacher_stream, teacher_parts[2])[1]

    normed_got = lax.ppermute(
        jnp.where(student_side, teacher_normed, student_normed), "dev", pairs(count, across)
    )
    normed = jnp.where(
        student_side,
        jnp.concatenate([normed_got, student_normed]),
        jnp.concatenate([teacher_normed, normed_got]),
    )
    normed = jnp.pad(normed, ((0, more_rows), (0, 0)))
    third_end = (bounds[-2] - D - HID + slot) * (ROW // BOT)
    acts_width = D + HID + max(third_end, HID)
    unit_z, acts, bottleneck, pre_one, pre_two = head_pass(
        head_up_kernel,
        plan,
        side,
        (normed,),
        gathered_head,
        [
            jax.ShapeDtypeStruct((pair_rows, BOT), narrow),
            jax.ShapeDtypeStruct((pair_rows, acts_width), narrow),
            jax.ShapeDtypeStruct((pair_rows, BOT), single),
            jax.ShapeDtypeStruct((pair_rows, HID), single),
            jax.ShapeDtypeStruct((pair_rows, HID), single),
        ],
    )
    inputs_all = lax.all_gather(acts, "dev", axis=0, axis_index_groups=groups).reshape(half * pair_rows, -1)

    z_pair = cube_gather(unit_z, "b")
    teacher_z_all = cube_gather(z_pair[0], "xygc").reshape(all_rows, BOT)
    student_z_all = cube_gather(z_pair[1], "gxyc").reshape((2,) * 4 + (pair_rows, BOT))
    student_z_all = jnp.transpose(student_z_all, (0, 3, 1, 2, 4, 5)).reshape(all_rows, BOT)
    protos_here = protos.shape[0]
    own_centre = lax.dynamic_slice(centre, (me * protos_here,), (protos_here,))
    centre_column = own_centre.reshape(protos_here, 1)
    spot_in_pair = jnp.arange(all_rows) % pair_rows
    is_class = (spot_in_pair % 17) == 0
    class_kept = jnp.where(is_class, all_kept, 0.0)
    row_weight = jnp.where(is_class, all_kept, all_kept * (1.0 / 16.0))
    count_total = jnp.sum(class_kept)

    def lines(*values):
        return jnp.pad(jnp.stack(values), ((0, 8 - len(values)), (0, 0)))

    mixed_rows, sums, centre_sum = logits_pass(
        teacher_z_all, student_z_all, proto_teacher, protos, centre_column, lines(class_kept)
    )
    by_pair = (2,) * 4 + (pair_rows, -1)
    mixed_own = jnp.concatenate(
        [
            cube_scatter(mixed_rows[:, :BOT].reshape(by_pair), "cgyx", "cgyx"),
            cube_scatter(mixed_rows[:, BOT:].reshape(by_pair), "cgyx", "cxyg"),
        ],
        axis=1,
    )
    mixed_own = mixed_own + lax.ppermute(
        mixed_own.astype(narrow), "dev", [(i, i ^ across) for i in range(half)]
    ).astype(single)
    scale = row_weight / tau_student
    flags = bit_flags(me)
    pair_at = flags["c"] * 8 + flags["g"] * 4 + flags["y"] * 2 + flags["x"]
    own_scale = lax.dynamic_slice(scale, (pair_at * pair_rows,), (pair_rows,))[:, None]
    grad_unit_z = own_scale * (
        mixed_own[:, :BOT] / mixed_own[:, 2 * BOT + 1 : 2 * BOT + 2]
        - mixed_own[:, BOT : 2 * BOT] / mixed_own[:, 2 * BOT : 2 * BOT + 1]
    )
    own_new_centre = (
        centre_keep * own_centre + (1.0 - centre_keep) * centre_sum.reshape(protos_here) / count_total
    )

    grads, grad_normed = head_pass(
        head_down_kernel,
        plan,
        side,
        (grad_unit_z, bottleneck, pre_one, pre_two),
        gathered_head,
        [
            jax.ShapeDtypeStruct((pair_rows, 2 * HID + BOT), narrow),
            jax.ShapeDtypeStruct((pair_rows, D), single),
        ],
    )
    grads_all = lax.all_gather(grads, "dev", axis=0, axis_index_groups=groups).reshape(half * pair_rows, -1)
    normed_back = lax.ppermute(
        grad_normed[:rows_here], "dev", [(i, i ^ across) for i in range(half, count)]
    )
    own_grad_normed = jnp.where(student_side, grad_normed[rows_here : 2 * rows_here], normed_back)
    extras = student_parts[2].astype(single)
    grad_chosen, grad_gain, grad_bias = jax.vjp(layer_norm, chosen, extras[2], extras[3])[1](
        own_grad_normed
    )
    image_index = jnp.arange(images_here, dtype=jnp.int32)[:, None]
    grad_stream = (
        jnp.zeros(stream.shape, single)
        .at[image_index, row_index]
        .add(grad_chosen.reshape(images_here, 17, D))
    )

    grad_stream = grad_stream.reshape(images_here * PAD_SEQ, D)
    middle_row = block_rows // 2
    vector_grads = [None] * LAYERS

    def halves(array):
        middle = array.shape[-2] // 2
        return [array[..., :middle, :], array[..., middle:, :]]

    def cuts(parts, names, order):
        return [cut(part, name, axis, 1) for part, name, axis in zip(parts, names, order)]

    def moves(pieces, order):
        return [move(sent, kept, axis) for (sent, kept, left), axis in zip(pieces, order)]

    def over_core(weight_grad, rows):
        pairs_of = weight_grad.reshape(D // 128, -1, 2, rows, 128)
        return move(*cut(pairs_of, "pc", "c", 1)[:2], "c")

    def core_cut(weight_grad, rows):
        return cut(weight_grad.reshape(D // 128, -1, 2, rows, 128), "pc", "c", 1)[:2]

    def start(late, early, *others):
        shared_pair = 4 * D // (2 * block_rows)
        whole = jnp.concatenate(
            [
                early[:, :shared_pair],
                early[:, shared_pair:] + late[:, : early.shape[1] - shared_pair],
                late[:, early.shape[1] - shared_pair :],
            ],
            axis=1,
        )
        parts = [jnp.concatenate(pieces, axis=2) for pieces in zip(*[halves(array) for array in (whole, *others)])]
        by_bits = [part.reshape((D // 128, 2, 2, 2, 2) + part.shape[2:]) for part in parts]
        return (cuts(by_bits, ["bayx"] * 2, rounds[0]), 0)

    rounds = (("x", "b"), ("y", "a"), ("b", "x"), ("a", "y"))

    def advance(state):
        pieces, stage = state
        parts = moves(pieces, rounds[stage])
        names = [left for sent, kept, left in pieces]
        return cuts(parts, names, rounds[stage + 1]), stage + 1

    def finish(state):
        while state[1] < len(rounds) - 1:
            state = advance(state)
        return moves(state[0], rounds[-1])

    def sends(states):
        return tuple(sent for pieces, stage in states for sent, kept, left in pieces)

    def block_place(i):
        column = max(bounds[i], 0) // 128 * 128
        grad_column = 0 if i < first_w2 else HID
        return [column, bounds[i] - column if i else 0, sizes[i] if i else 0, grad_column]

    def third_place(i):
        return [0, 0, sizes[i], 0]

    place = per_device(
        [
            (third_place(i) if i >= first_w3 else block_place(i))
            + block_place(i ^ across)
            + [int(i >= first_w3), D + HID + max(bounds[i] - D - HID, 0) * (ROW // BOT)]
            for i in range(count)
        ]
    )
    slow = [own_new_centre.reshape(1, protos_here), sums[:3]]
    slow_order = ["c", "x", "y", "a", "b"]

    def slow_round(sent, stay):
        name = slow_order.pop(0)
        got = [lax.ppermute(array, "dev", pairs(count, MASKS[name])) for array in sent]
        joined = jnp.where(
            flags[name] == 1,
            jnp.concatenate([got[0], stay[0]], axis=0),
            jnp.concatenate([stay[0], got[0]], axis=0),
        )
        return [joined, stay[1] + got[1]]

    started = []
    held_block = None
    waits = ()
    for layer_index in reversed(range(LAYERS)):
        saved, vectors = saved_layers[layer_index], vectors_all[1, layer_index]
        part = LAYERS + layer_index
        grad_stream, late_grad, late_vectors, stay_one, stay_two, *held_block = mlp_back(
            side,
            grad_stream,
            saved,
            vectors,
            gathered,
            part,
            waits + sends(started),
            slow + ([partner_block_grad] if started else []),
        )
        slow = slow_round(slow, [stay_one, stay_two])
        late = over_core(late_grad, block_rows)
        started = [advance(state) for state in started]
        if started:
            block_got = lax.ppermute(held_block[0], "dev", [(i, i ^ across) for i in range(half, count)])
        grad_stream, early_grad, early_vectors, stay_one, stay_two, *held_block = attention_back(
            side,
            grad_stream,
            saved,
            vectors,
            gathered,
            part,
            sends(started),
            slow + ([own_block_grad] if started else []),
        )
        slow = slow_round(slow, [stay_one, stay_two])
        vector_grads[layer_index] = (late_vectors + early_vectors)[:6]
        if layer_index == LAYERS - 1:
            sent, stay = core_cut(early_grad, block_rows)
            own_block_grad, partner_block_grad, stay, stay_one, stay_two = head_grads(
                place, inputs_all, grads_all, slot, -min(bounds[1], 0), (early_vectors,), [stay] + slow
            )
            slow = slow_round(slow, [stay_one, stay_two])
            waits = (own_block_grad,)
        started = [advance(state) for state in started]
        if layer_index > 0:
            started.append(start(late, move(sent, stay, "c")))
    own_block_grad = held_block[0]
    new_centre = slow[0].reshape(-1)
    sums = slow[1]
    cross = jnp.log(sums[1]) - sums[2] / (sums[0] * tau_student)
    loss_total = jnp.sum(row_weight * cross)
    student_scale, teacher_scale = scale / sums[1], scale / sums[0]
    head_block_grad = jnp.where(student_side, own_block_grad, block_got.astype(single))
    early = over_core(early_grad, block_rows)
    small_rows = -(-(EMBED_ROWS + 6 * LAYERS) // (16 * count)) * 16
    small = embed_back(
        grad_stream,
        patches.reshape(images_here * PATCHES, PIX),
        jnp.where(masked_here, 0.0, 1.0).reshape(images_here * PATCHES, 1),
        jnp.stack([grad_gain, grad_bias]),
        jnp.concatenate(vector_grads),
        small_rows * count,
        (),
    )
    started.append(start(late, early, over_core(small, small_rows)))
    last_rows = lax.dynamic_slice(
        head_block_grad, (jnp.array(sizes, jnp.int32)[me] - GROUP, 0), (GROUP, ROW)
    )
    previous = lax.ppermute(last_rows, "dev", step_pairs(count, 1))
    proto_grad, proto_square, *held = proto_grad_pass(
        teacher_z_all,
        student_z_all,
        proto_teacher,
        protos,
        centre_column,
        lines(student_scale, teacher_scale),
        [stay for pieces, stage in started for sent, stay, left in pieces],
    )
    held = iter(held)
    started = [([(sent, next(held), left) for sent, _, left in pieces], stage) for pieces, stage in started]
    blocks = [finish(state) for state in started][::-1]
    middle_row = block_rows // 2
    layer_block = jnp.stack([jnp.concatenate([part[:, :middle_row] for part in parts], axis=1) for parts in blocks])
    small_block = jnp.concatenate([part[:, middle_row:] for part in blocks[0]], axis=1)

    square_local = (
        jnp.sum(head_block_grad * head_block_grad)
        + jnp.sum(layer_block * layer_block)
        + jnp.sum(small_block * small_block)
        + proto_square[0, 0]
    )
    high = square_local.astype(narrow)
    middle = (square_local - high.astype(single)).astype(narrow)
    low = (square_local - high.astype(single) - middle.astype(single)).astype(narrow)
    tile = jnp.pad(jnp.stack([high, middle, low]).reshape(1, 1, 3), ((0, 0), (0, 15), (0, 125)))
    first_rows = small_block[:2].astype(narrow)
    other_rows = jnp.concatenate([small_block[2:].astype(narrow), tile], axis=1)
    first_rows = cube_gather(first_rows, "xya")
    other_rows = cube_gather(other_rows, "abx")
    behind = lax.ppermute(layer_block[:, :, :6], "dev", step_pairs(count, -1))
    place = per_device([spots(head_span - starts[i], drift * i) for i in range(count)])
    stem_lines, layer_lines, first_rows, other_rows = own_shards(
        place, head_block_grad, previous, layer_block, behind, lane_rows(stem_piece), lane_rows(layer_piece),
        [first_rows, other_rows],
    )
    first_rows = jnp.moveaxis(cube_gather(first_rows, "bc").reshape((2, 2, 8) + first_rows.shape[1:]), 0, 2)
    other_rows = cube_gather(other_rows, "yc")
    other_rows = other_rows.reshape((2,) * 5 + other_rows.shape[2:])
    other_rows = jnp.transpose(other_rows, (3, 4, 1, 2, 0, 5, 6, 7))
    first_rows = first_rows.reshape((count,) + first_rows.shape[3:])
    other_rows = other_rows.reshape((count,) + other_rows.shape[5:])
    square_total = jnp.sum(other_rows[:, 0, small_rows, :3].astype(single))
    small_all = jnp.concatenate([first_rows, other_rows[:, :, :small_rows]], axis=1).astype(single)
    small_all = jnp.transpose(small_all, (0, 2, 1, 3)).reshape(small_rows * count, D)
    embed_grad = small_all[:EMBED_ROWS].reshape(-1)
    vector_grad = small_all[EMBED_ROWS : EMBED_ROWS + 6 * LAYERS].reshape(LAYERS, 6 * D)
    layer_grad = layer_lines.reshape(LAYERS, -1)[:, :layer_piece]
    layer_grad = jnp.concatenate(
        [
            layer_grad[:, : layer_piece - tail],
            jnp.where(me == count - 1, vector_grad, layer_grad[:, layer_piece - tail :]),
        ],
        axis=1,
    )
    stem_grad = stem_lines.reshape(-1)[:stem_piece]
    rest = EMBED_FLAT - stem_piece
    second_part = jnp.concatenate([embed_grad[stem_piece:], stem_grad[rest:]])
    stem_grad = jnp.where(
        me == 0, embed_grad[:stem_piece], jnp.where(me == 1, second_part, stem_grad)
    )

    grad_norm = jnp.sqrt(square_total) / count_total
    factor = jnp.minimum(1.0, clip_limit / (grad_norm + 1e-06)) / count_total
    stem_set = adam_update(stem, stem_moment, stem_second, stem_grad * factor, stem_teacher)
    layer_set = adam_update(layers, layer_moment, layer_second, layer_grad * factor, layer_teacher)
    proto_set = proto_update(factor, protos, proto_moment, proto_second, proto_teacher, proto_grad)
    return (loss_total, count_total, grad_norm, new_centre) + stem_set + layer_set + tuple(proto_set)


def solution(mesh):
    count = mesh.shape["dev"]
    stem_length = -(-(EMBED_FLAT + HEAD_ROWS * ROW) // count) * count
    close = fits(count, stem_length // count, (MATRIX_ROWS + 6) * D // count)
    placed = (
        P("dev", None, None),
        P("dev", None),
        P("dev"),
        P("dev"),
        P("dev"),
        P("dev"),
        P("dev"),
        P(None, "dev"),
        P(None, "dev"),
        P(None, "dev"),
        P(None, "dev"),
        P("dev", None),
        P("dev", None),
        P("dev", None),
        P("dev", None),
        P(),
    )
    return jax.shard_map(
        close_local if close else spread_local,
        mesh=mesh,
        in_specs=placed,
        out_specs=(
            P(),
            P(),
            P(),
            P(),
            P("dev"),
            P("dev"),
            P("dev"),
            P("dev"),
            P("dev"),
            P(None, "dev"),
            P(None, "dev"),
            P(None, "dev"),
            P(None, "dev"),
            P(None, "dev"),
            P("dev", None),
            P("dev", None),
            P("dev", None),
            P("dev", None),
            P("dev", None),
        ),
        check_vma=False,
    )
```

```python
import jax
import jax.numpy as jnp
from jax import lax
from jax.experimental import pallas as pl
from jax.experimental.pallas import tpu as pltpu
from jax.sharding import PartitionSpec as P

D = 384
HEADS = 6
HEAD_DIM = 64
FF = 1536
HID = 2048
BOT = 256
PIX = 588
PATCHES = 256
LAYERS = 2
STEP = 10
SEQ = 257


tau_student = 0.1
tau_teacher = 0.04
clip_limit = 0.003
learn_rate = 0.03
beta_one = 0.9
beta_two = 0.999
adam_eps = 1e-08
decay_rate = 0.04
teacher_keep = 0.8
centre_keep = 0.9
narrow = jnp.bfloat16
single = jnp.float32


def layer_shapes():
    return ((D, 3 * D), (D, D), (D, FF), (FF, D), (6, D))


def stem_shapes():
    return ((PIX, D), (SEQ, D), (4, D), (D, HID), (HID, HID), (HID, BOT))


def cut_flat(flat_row, shape_list):
    pieces = []
    offset = 0
    for shape_pair in shape_list:
        length = shape_pair[0] * shape_pair[1]
        pieces.append(flat_row[offset : offset + length].reshape(shape_pair))
        offset = offset + length
    return pieces


def pack_flat(grad_list, total_length):
    joined = jnp.concatenate([grad_item.reshape(-1) for grad_item in grad_list])
    return jnp.concatenate([joined, jnp.zeros((total_length - joined.shape[0],), single)])


def contract(form, left_arg, right_arg):
    return jnp.einsum(form, left_arg, right_arg, preferred_element_type=single)


def layer_norm(values, gain_row, bias_row):
    centred = values - jnp.mean(values, axis=-1, keepdims=True)
    spread = jnp.mean(centred * centred, axis=-1, keepdims=True)
    return centred * lax.rsqrt(spread + 1e-06) * gain_row + bias_row


def unit_rows(values):
    return values * lax.rsqrt(jnp.sum(values * values, axis=-1, keepdims=True) + 1e-06)


def gelu_back(pre_act, grad_act):
    return jax.vjp(jax.nn.gelu, pre_act)[1](grad_act)[0]


def block_forward(stream, weights):
    w_qkv, w_proj, w_up, w_down, vectors = weights
    vectors = vectors.astype(single)
    batch_size = stream.shape[0]
    normed = layer_norm(stream, vectors[0], vectors[1]).astype(narrow)
    packed = (
        contract("bsd,de->bse", normed, w_qkv)
        .astype(narrow)
        .reshape(batch_size, SEQ, 3, HEADS, HEAD_DIM)
    )
    scores = contract("bqhe,bkhe->bhqk", packed[:, :, 0], packed[:, :, 1]) * HEAD_DIM ** (-0.5)
    top_score = jnp.max(scores, axis=-1, keepdims=True)
    exp_terms = jnp.exp(scores - top_score)
    totals = jnp.sum(exp_terms, axis=-1, keepdims=True)
    log_total = top_score + jnp.log(totals)
    mixed = contract("bhqk,bkhe->bqhe", (exp_terms / totals).astype(narrow), packed[:, :, 2])
    mixed = mixed.astype(narrow).reshape(batch_size, SEQ, D)
    attn_out = contract("bsd,de->bse", mixed, w_proj)
    middle = stream + vectors[2] * attn_out
    normed_two = layer_norm(middle, vectors[3], vectors[4]).astype(narrow)
    pre_act = contract("bsd,df->bsf", normed_two, w_up)
    hidden = jax.nn.gelu(pre_act).astype(narrow)
    mlp_out = contract("bsf,fd->bsd", hidden, w_down)
    saved = (
        stream,
        normed,
        packed,
        log_total,
        mixed,
        attn_out,
        middle,
        normed_two,
        pre_act,
        hidden,
        mlp_out,
    )
    return (middle + vectors[5] * mlp_out, saved)


def block_backward(grad_out, weights, saved):
    w_qkv, w_proj, w_up, w_down, vectors = weights
    vectors = vectors.astype(single)
    (
        stream,
        normed,
        packed,
        log_total,
        mixed,
        attn_out,
        middle,
        normed_two,
        pre_act,
        hidden,
        mlp_out,
    ) = saved
    batch_size = stream.shape[0]
    score_scale = HEAD_DIM ** (-0.5)
    grad_ls_two = jnp.sum(grad_out * mlp_out, axis=(0, 1))
    grad_mlp = (grad_out * vectors[5]).astype(narrow)
    grad_down = contract("bsf,bsd->fd", hidden, grad_mlp)
    grad_pre = gelu_back(pre_act, contract("bsd,fd->bsf", grad_mlp, w_down)).astype(narrow)
    grad_up = contract("bsd,bsf->df", normed_two, grad_pre)
    grad_normed_two = contract("bsf,df->bsd", grad_pre, w_up)
    grad_mid, grad_gain_two, grad_bias_two = jax.vjp(layer_norm, middle, vectors[3], vectors[4])[1](
        grad_normed_two
    )
    grad_mid = grad_mid + grad_out
    grad_ls_one = jnp.sum(grad_mid * attn_out, axis=(0, 1))
    grad_attn = (grad_mid * vectors[2]).astype(narrow)
    grad_proj = contract("bsd,bse->de", mixed, grad_attn)
    grad_mixed = (
        contract("bse,de->bsd", grad_attn, w_proj)
        .astype(narrow)
        .reshape(batch_size, SEQ, HEADS, HEAD_DIM)
    )
    query_rows = packed[:, :, 0]
    key_rows = packed[:, :, 1]
    value_rows = packed[:, :, 2]
    probs = jnp.exp(contract("bqhe,bkhe->bhqk", query_rows, key_rows) * score_scale - log_total)
    grad_probs = contract("bqhe,bkhe->bhqk", grad_mixed, value_rows)
    grad_values = contract("bhqk,bqhe->bkhe", probs.astype(narrow), grad_mixed)
    grad_scores = probs * (grad_probs - jnp.sum(probs * grad_probs, axis=-1, keepdims=True))
    grad_raw = (grad_scores * score_scale).astype(narrow)
    grad_queries = contract("bhqk,bkhe->bqhe", grad_raw, key_rows)
    grad_keys = contract("bhqk,bqhe->bkhe", grad_raw, query_rows)
    grad_packed = (
        jnp.stack([grad_queries, grad_keys, grad_values], axis=2)
        .astype(narrow)
        .reshape(batch_size, SEQ, 3 * D)
    )
    grad_qkv = contract("bsd,bse->de", normed, grad_packed)
    grad_normed = contract("bse,de->bsd", grad_packed, w_qkv)
    grad_in, grad_gain_one, grad_bias_one = jax.vjp(layer_norm, stream, vectors[0], vectors[1])[1](
        grad_normed
    )
    grad_vectors = jnp.stack(
        [grad_gain_one, grad_bias_one, grad_ls_one, grad_gain_two, grad_bias_two, grad_ls_two]
    )
    return (grad_in + grad_mid, (grad_qkv, grad_proj, grad_up, grad_down, grad_vectors))


def embed(stem_parts, image_rows, masked_here, student):
    patch_w, position, extras, w_first, w_second, w_third = stem_parts
    extras = extras.astype(single)
    embedded = contract("gpc,cd->gpd", image_rows, patch_w)
    if student:
        embedded = jnp.where(masked_here[:, :, None], extras[1], embedded)
    cls_rows = jnp.broadcast_to(extras[0], (image_rows.shape[0], 1, D))
    return jnp.concatenate([cls_rows, embedded], axis=1) + position.astype(single)


def embed_backward(grad_stream, image_rows, masked_here):
    grad_cls = jnp.sum(grad_stream[:, 0], axis=0)
    grad_position = jnp.sum(grad_stream, axis=0)
    grad_patch_rows = grad_stream[:, 1:]
    grad_mask_token = jnp.sum(jnp.where(masked_here[:, :, None], grad_patch_rows, 0.0), axis=(0, 1))
    grad_embedded = jnp.where(masked_here[:, :, None], 0.0, grad_patch_rows).astype(narrow)
    grad_patch_w = contract("gpc,gpd->cd", image_rows, grad_embedded)
    return (grad_patch_w, grad_position, grad_cls, grad_mask_token)


def head_forward(stem_parts, proto_rows, stream, row_index):
    patch_w, position, extras, w_first, w_second, w_third = stem_parts
    extras = extras.astype(single)
    chosen = jnp.take_along_axis(stream, row_index[:, :, None], axis=1)
    normed = layer_norm(chosen, extras[2], extras[3]).astype(narrow)
    pre_one = contract("grd,dh->grh", normed, w_first)
    hidden_one = jax.nn.gelu(pre_one).astype(narrow)
    pre_two = contract("grh,hk->grk", hidden_one, w_second)
    hidden_two = jax.nn.gelu(pre_two).astype(narrow)
    bottleneck = contract("grh,hb->grb", hidden_two, w_third)
    unit_z = unit_rows(bottleneck).astype(narrow)
    unit_protos = unit_rows(proto_rows.astype(single)).astype(narrow)
    logits = contract("grb,kb->grk", unit_z, unit_protos)
    return (
        logits,
        (chosen, normed, pre_one, hidden_one, pre_two, hidden_two, bottleneck, unit_z, unit_protos),
    )


def head_backward(grad_logits, stem_parts, saved, row_index, stream_shape):
    patch_w, position, extras, w_first, w_second, w_third = stem_parts
    extras = extras.astype(single)
    chosen, normed, pre_one, hidden_one, pre_two, hidden_two, bottleneck, unit_z, unit_protos = (
        saved
    )
    grad_rounded = grad_logits.astype(narrow)
    grad_unit_z = contract("grk,kb->grb", grad_rounded, unit_protos)
    grad_unit_protos = contract("grk,grb->kb", grad_rounded, unit_z)
    grad_bottle = jax.vjp(unit_rows, bottleneck)[1](grad_unit_z)[0].astype(narrow)
    grad_third = contract("grh,grb->hb", hidden_two, grad_bottle)
    grad_pre_two = gelu_back(pre_two, contract("grb,hb->grh", grad_bottle, w_third)).astype(narrow)
    grad_second = contract("grh,grk->hk", hidden_one, grad_pre_two)
    grad_pre_one = gelu_back(pre_one, contract("grk,hk->grh", grad_pre_two, w_second)).astype(
        narrow
    )
    grad_first = contract("grd,grh->dh", normed, grad_pre_one)
    grad_normed = contract("grh,dh->grd", grad_pre_one, w_first)
    grad_chosen, grad_gain, grad_bias = jax.vjp(layer_norm, chosen, extras[2], extras[3])[1](
        grad_normed
    )
    image_index = jnp.arange(row_index.shape[0], dtype=jnp.int32)[:, None]
    grad_stream = jnp.zeros(stream_shape, single).at[image_index, row_index].add(grad_chosen)
    return (
        grad_stream,
        (grad_first, grad_second, grad_third),
        grad_gain,
        grad_bias,
        grad_unit_protos,
    )


def adam_update(weight, moment, second, grad, teacher):
    new_moment = beta_one * moment + (1.0 - beta_one) * grad
    new_second = beta_two * second + (1.0 - beta_two) * grad * grad
    direction = (
        new_moment
        / (1.0 - beta_one**STEP)
        / (jnp.sqrt(new_second / (1.0 - beta_two**STEP)) + adam_eps)
    )
    new_weight = weight - learn_rate * (direction + decay_rate * weight)
    return (
        new_moment,
        new_second,
        new_weight,
        new_weight.astype(narrow),
        teacher_keep * teacher + (1.0 - teacher_keep) * new_weight,
    )


def spread_local(
    patches,
    masked,
    slot_used,
    stem,
    stem_moment,
    stem_second,
    stem_teacher,
    layers,
    layer_moment,
    layer_second,
    layer_teacher,
    protos,
    proto_moment,
    proto_second,
    proto_teacher,
    centre,
):
    images_here = patches.shape[0]
    row_index = jnp.concatenate([jnp.zeros((images_here, 1), jnp.int32), masked + 1], axis=1)
    masked_here = jnp.any(
        masked[:, :, None] == jnp.arange(PATCHES, dtype=jnp.int32)[None, None, :], axis=1
    )
    kept = slot_used.astype(single)
    teacher_flat, teacher_protos = (
        lax.all_gather(stem_teacher.astype(narrow), "dev", axis=0, tiled=True),
        lax.all_gather(proto_teacher.astype(narrow), "dev", axis=0, tiled=True),
    )
    teacher_parts = cut_flat(teacher_flat, stem_shapes())
    stream = embed(teacher_parts, patches, masked_here, False)
    for layer_index in range(LAYERS):
        teacher_layer = lax.all_gather(
            layer_teacher[layer_index].astype(narrow), "dev", axis=0, tiled=True
        )
        stream = block_forward(stream, cut_flat(teacher_layer, layer_shapes()))[0]
    teacher_logits = head_forward(teacher_parts, teacher_protos, stream, row_index)[0]
    teacher_probs = jax.nn.softmax((teacher_logits - centre) / tau_teacher, axis=-1)
    centre_terms = jnp.sum(kept[:, None] * teacher_logits[:, 0], axis=0)
    student_flat, student_protos = (
        lax.all_gather(stem.astype(narrow), "dev", axis=0, tiled=True),
        lax.all_gather(protos.astype(narrow), "dev", axis=0, tiled=True),
    )
    student_parts = cut_flat(student_flat, stem_shapes())
    stream = embed(student_parts, patches, masked_here, True)
    saved_layers = []
    gathered_layers = []
    for layer_index in range(LAYERS):
        layer_flat = lax.all_gather(layers[layer_index].astype(narrow), "dev", axis=0, tiled=True)
        gathered_layers.append(layer_flat)
        stream, saved = block_forward(stream, cut_flat(layer_flat, layer_shapes()))
        saved_layers.append(saved)
    logits, head_saved = head_forward(student_parts, student_protos, stream, row_index)

    def loss_piece(logit_rows):
        log_probs = jax.nn.log_softmax(logit_rows / tau_student, axis=-1)
        cross = -jnp.sum(teacher_probs * log_probs, axis=-1)
        return jnp.sum(kept * (cross[:, 0] + jnp.mean(cross[:, 1:], axis=1)))

    loss_local, loss_puller = jax.vjp(loss_piece, logits)
    grad_logits = loss_puller(jnp.float32(1.0))[0]
    count_local = jnp.sum(kept)
    loss_total, count_total, centre_total = lax.psum((loss_local, count_local, centre_terms), "dev")
    back_flat, back_protos = (
        lax.all_gather(stem.astype(narrow), "dev", axis=0, tiled=True),
        lax.all_gather(protos.astype(narrow), "dev", axis=0, tiled=True),
    )
    back_parts = cut_flat(back_flat, stem_shapes())
    grad_stream, head_grads, grad_gain, grad_bias, grad_unit_protos = head_backward(
        grad_logits, back_parts, head_saved, row_index, stream.shape
    )
    layer_grads = []
    for layer_index in reversed(range(LAYERS)):
        weight_flat = lax.all_gather(layers[layer_index].astype(narrow), "dev", axis=0, tiled=True)
        grad_stream, block_grads = block_backward(
            grad_stream, cut_flat(weight_flat, layer_shapes()), saved_layers[layer_index]
        )
        layer_grads.insert(
            0,
            lax.psum_scatter(
                pack_flat(block_grads, weight_flat.shape[0]), "dev", scatter_dimension=0, tiled=True
            ),
        )
    grad_patch_w, grad_position, grad_cls, grad_mask_token = embed_backward(
        grad_stream, patches, masked_here
    )
    grad_extras = jnp.stack([grad_cls, grad_mask_token, grad_gain, grad_bias])
    stem_flat_grad = pack_flat(
        (grad_patch_w, grad_position, grad_extras) + head_grads, back_flat.shape[0]
    )
    stem_grad, proto_row_grad = (
        lax.psum_scatter(stem_flat_grad, "dev", scatter_dimension=0, tiled=True),
        lax.psum_scatter(grad_unit_protos, "dev", scatter_dimension=0, tiled=True),
    )
    own_protos = lax.optimization_barrier(protos.astype(narrow)).astype(single)
    proto_grad = jax.vjp(unit_rows, own_protos)[1](proto_row_grad)[0]
    layer_grad = jnp.stack(layer_grads)
    square_local = (
        jnp.sum(stem_grad * stem_grad)
        + jnp.sum(layer_grad * layer_grad)
        + jnp.sum(proto_grad * proto_grad)
    )
    square_total = lax.psum(square_local, "dev")
    grad_norm = jnp.sqrt(square_total) / count_total
    factor = jnp.minimum(1.0, clip_limit / (grad_norm + 1e-06)) / count_total
    new_centre = centre_keep * centre + (1.0 - centre_keep) * centre_total / count_total
    stem_set = adam_update(stem, stem_moment, stem_second, stem_grad * factor, stem_teacher)
    layer_set = adam_update(layers, layer_moment, layer_second, layer_grad * factor, layer_teacher)
    proto_set = adam_update(protos, proto_moment, proto_second, proto_grad * factor, proto_teacher)
    return (
        loss_total,
        count_total,
        grad_norm,
        new_centre,
        stem_set[0],
        stem_set[1],
        stem_set[2],
        stem_set[3],
        stem_set[4],
        layer_set[0],
        layer_set[1],
        layer_set[2],
        layer_set[3],
        layer_set[4],
        proto_set[0],
        proto_set[1],
        proto_set[2],
        proto_set[3],
        proto_set[4],
    )


GROUP = 16
ROW = HID
MATRIX_ROWS = D * 3 + D + FF + FF
EMBED_ROWS = PIX + SEQ + 4
EMBED_FLAT = EMBED_ROWS * D
HEAD_ROWS = D + HID + BOT
BITS = ("b", "a", "y", "x", "c")
MASKS = {"c": 1, "x": 2, "y": 4, "a": 8, "b": 24, "g": 8}


def head_bounds(count, stem_piece):
    bounds = [-(-(stem_piece * device - EMBED_FLAT) // (ROW * GROUP)) * GROUP for device in range(count + 1)]
    bounds[0] = -(-EMBED_FLAT // (ROW * GROUP)) * -GROUP
    bounds[-1] = HEAD_ROWS
    return bounds


def fits(count, stem_piece, layer_piece):
    if count != 1 << len(BITS) or MATRIX_ROWS % (3 * count):
        return False
    bounds = head_bounds(count, stem_piece)
    sizes = [bounds[i + 1] - bounds[i] for i in range(count)]
    return (
        min(sizes) > GROUP
        and bounds[1] <= 0
        and stem_piece < EMBED_FLAT <= 2 * stem_piece
        and D in bounds
        and D + HID in bounds
        and stem_piece * count == EMBED_FLAT + HEAD_ROWS * ROW
    )


def pairs(count, mask):
    return [(i, i ^ mask) for i in range(count)]


def bit_flags(me):
    flags = {name: (me >> (len(BITS) - 1 - place)) & 1 for place, name in enumerate(BITS)}
    flags["g"] = flags["a"] ^ flags["b"]
    return flags


def cube_gather(part, order):
    count = 1 << len(BITS)
    flags = bit_flags(lax.axis_index("dev"))
    held = part[None]
    for name in order:
        got = lax.ppermute(held, "dev", pairs(count, MASKS[name]))
        held = jnp.where(
            flags[name] == 1,
            jnp.concatenate([got, held], axis=0),
            jnp.concatenate([held, got], axis=0),
        )
    return held


def cut(array, names, name, lead):
    mine = bit_flags(lax.axis_index("dev"))[name]
    place = names.index(name) + lead
    sent = lax.dynamic_index_in_dim(array, 1 - mine, place, keepdims=False)
    kept = lax.dynamic_index_in_dim(array, mine, place, keepdims=False)
    return (sent if name == "c" else sent.astype(narrow)), kept, names.replace(name, "")


def move(sent, kept, name):
    return kept + lax.ppermute(sent, "dev", pairs(1 << len(BITS), MASKS[name])).astype(single)


def cube_scatter(array, names, order, lead=0):
    for name in order:
        sent, kept, names = cut(array, names, name, lead)
        array = move(sent, kept, name)
    return array


def cube_sum(values):
    for name in "cxyab":
        values = values + lax.ppermute(values, "dev", pairs(1 << len(BITS), MASKS[name]))
    return values


def split_bits(array, lead=0):
    return array.reshape(array.shape[:lead] + (2,) * len(BITS) + array.shape[lead + 1 :])


def step_pairs(count, step):
    return [(i, i + step) for i in range(count) if 0 <= i + step < count]


def lane_rows(length):
    return -(-length // 1024) * 8


def as_lanes(flat):
    rows = lane_rows(flat.shape[-1])
    gap = rows * 128 - flat.shape[-1]
    padded = jnp.pad(flat, [(0, 0)] * (flat.ndim - 1) + [(0, gap)])
    return padded.reshape(flat.shape[:-1] + (rows, 128))


def shifted(line_ref, row, lane, first, rows, stride):
    spots = lax.broadcasted_iota(jnp.int32, (rows, 128), 1)
    turn = lax.rem(128 - lane, 128)
    here = pltpu.roll(line_ref[pl.ds(row + first, rows, stride=stride), :], turn, 1)
    there = pltpu.roll(line_ref[pl.ds(row + first + 1, rows, stride=stride), :], turn, 1)
    return jnp.where(spots < 128 - lane, here, there)


def blocks_kernel(
    shape,
    place_ref,
    stem_ref,
    after_ref,
    layer_ref,
    before_ref,
    last_ref,
    head_ref,
    block_ref,
    embed_ref,
    vector_ref,
    line_ref,
    flat_ref,
):
    front, stem_piece, layer_piece, tail = shape
    stem_lines = stem_ref.shape[1]
    end_row, end_lane = stem_piece // 128, stem_piece % 128
    after_lines = after_ref.shape[1]
    slot = head_ref.shape[1]
    for model in range(2):
        line_ref[pl.ds(0, front), :] = jnp.zeros((front, 128), single)
        line_ref[pl.ds(front, end_row), :] = stem_ref[model, pl.ds(0, end_row), :]
        turned = pltpu.roll(after_ref[model], end_lane, 1)
        spots = lax.broadcasted_iota(jnp.int32, (after_lines, 128), 1)
        line_ref[pl.ds(front + end_row, after_lines), :] = turned
        line_ref[pl.ds(front + end_row + after_lines, 128), :] = jnp.zeros((128, 128), single)
        lower = pltpu.roll(turned, 1, 0)
        first_line = jnp.broadcast_to(stem_ref[model, pl.ds(end_row, 1), :], (after_lines, 128))
        number = lax.broadcasted_iota(jnp.int32, (after_lines, 128), 0)
        lower = jnp.where(number == 0, first_line, lower)
        line_ref[pl.ds(front + end_row, after_lines), :] = jnp.where(spots < end_lane, lower, turned)
        per_row = ROW // 128
        for chunk in range(per_row):
            head_ref[model, :, pl.ds(chunk * 128, 128)] = shifted(
                line_ref, place_ref[0], place_ref[1], chunk, slot, per_row
            ).astype(narrow)
        for chunk in range(D // 128):
            embed_ref[model, :, pl.ds(chunk * 128, 128)] = shifted(
                line_ref, place_ref[2], place_ref[3], chunk, embed_ref.shape[1], D // 128
            ).astype(narrow)
    tail_lines = tail // 128
    layer_lines = layer_ref.shape[1]
    for part in range(layer_ref.shape[0]):
        flat_ref[pl.ds(0, tail_lines), :] = before_ref[part]
        flat_ref[pl.ds(tail_lines, layer_lines), :] = layer_ref[part]
        for chunk in range(D // 128):
            block_ref[part, :, pl.ds(chunk * 128, 128)] = shifted(
                flat_ref, place_ref[4], place_ref[5], chunk, block_ref.shape[1], D // 128
            ).astype(narrow)
            vector_ref[part, :, pl.ds(chunk * 128, 128)] = last_ref[
                part, pl.ds(chunk, 8, stride=D // 128), :
            ].astype(narrow)


def own_blocks(place, stems, after, layer_rows, before, last_lines, shape, slot, block_rows, embed_rows):
    front, stem_piece, layer_piece, tail = shape
    lines = front + stem_piece // 128 + after.shape[1] + slot * ROW // 128
    flats = tail // 128 + layer_rows.shape[1] + 48
    return pl.pallas_call(
        lambda *refs: blocks_kernel(shape, *refs),
        out_shape=[
            jax.ShapeDtypeStruct((2, slot, ROW), narrow),
            jax.ShapeDtypeStruct((2 * LAYERS, block_rows, D), narrow),
            jax.ShapeDtypeStruct((2, embed_rows, D), narrow),
            jax.ShapeDtypeStruct((2 * LAYERS, 8, D), narrow),
        ],
        in_specs=[pl.BlockSpec(memory_space=pltpu.SMEM)] + [pl.BlockSpec(memory_space=pltpu.VMEM)] * 5,
        out_specs=[pl.BlockSpec(memory_space=pltpu.VMEM)] * 4,
        scratch_shapes=[pltpu.VMEM((lines, 128), single), pltpu.VMEM((flats, 128), single)],
        compiler_params=pltpu.CompilerParams(vmem_limit_bytes=40 << 20),
    )(place, stems, after, layer_rows, before, last_lines)


def shards_kernel(held, place_ref, head_ref, previous_ref, block_ref, behind_ref, *refs):
    stem_ref, layer_ref = refs[held : held + 2]
    line_ref, flat_ref = refs[-2:]
    per_row = ROW // 128
    extra = previous_ref.shape[0]
    slot = head_ref.shape[0]
    for chunk in range(per_row):
        spot = pl.ds(chunk * 128, 128)
        line_ref[pl.ds(chunk, extra, stride=per_row), :] = previous_ref[:, spot]
        line_ref[pl.ds(extra * per_row + chunk, slot, stride=per_row), :] = head_ref[:, spot]
    stem_ref[...] = shifted(line_ref, place_ref[0], place_ref[1], 0, stem_ref.shape[0], 1)
    per_row = D // 128
    rows = block_ref.shape[2]
    for part in range(block_ref.shape[0]):
        for chunk in range(per_row):
            flat_ref[pl.ds(chunk, rows, stride=per_row), :] = block_ref[part, chunk]
            flat_ref[pl.ds(rows * per_row + chunk, 6, stride=per_row), :] = behind_ref[part, chunk]
        layer_ref[part] = shifted(flat_ref, place_ref[2], place_ref[3], 0, layer_ref.shape[1], 1)


def own_shards(place, head_grad, previous, block_grad, behind, stem_lines, layer_lines, held):
    per_row = ROW // 128
    lines = (head_grad.shape[0] + previous.shape[0]) * per_row + 256
    flats = max(block_grad.shape[2] * 3 + 18, layer_lines + 18) + 16
    return pl.pallas_call(
        lambda *refs: shards_kernel(len(held), *refs),
        out_shape=[
            jax.ShapeDtypeStruct((stem_lines, 128), single),
            jax.ShapeDtypeStruct((block_grad.shape[0], layer_lines, 128), single),
        ]
        + [jax.ShapeDtypeStruct(array.shape, array.dtype) for array in held],
        in_specs=[pl.BlockSpec(memory_space=pltpu.SMEM)]
        + [pl.BlockSpec(memory_space=pltpu.VMEM)] * 4
        + [pl.BlockSpec(memory_space=pl.ANY)] * len(held),
        out_specs=[pl.BlockSpec(memory_space=pltpu.VMEM)] * 2 + [pl.BlockSpec(memory_space=pl.ANY)] * len(held),
        input_output_aliases={5 + number: 2 + number for number in range(len(held))},
        scratch_shapes=[pltpu.VMEM((lines, 128), single), pltpu.VMEM((flats, 128), single)],
        compiler_params=pltpu.CompilerParams(vmem_limit_bytes=40 << 20),
    )(place, head_grad, previous, block_grad, behind, *held)


PAD_SEQ = 272
GELU_SCALE = 0.7978845608028654
GELU_CUBE = 0.044715


def product_plain(left, right):
    return lax.dot_general(left, right, (((1,), (0,)), ((), ())), preferred_element_type=single)


def product_right(left, right):
    return lax.dot_general(left, right, (((1,), (1,)), ((), ())), preferred_element_type=single)


def product_left(left, right):
    return lax.dot_general(left, right, (((0,), (0,)), ((), ())), preferred_element_type=single)


def norm_parts(values):
    centred = values - jnp.mean(values, axis=-1, keepdims=True)
    spread = lax.rsqrt(jnp.mean(centred * centred, axis=-1, keepdims=True) + 1e-06)
    return centred * spread, spread


def norm_back(grad, unit, spread, gain):
    grad_unit = grad * gain
    mean_one = jnp.mean(grad_unit, axis=-1, keepdims=True)
    mean_two = jnp.mean(grad_unit * unit, axis=-1, keepdims=True)
    return spread * (grad_unit - mean_one - unit * mean_two)


def gelu_tanh(values):
    return jnp.tanh(GELU_SCALE * (values + GELU_CUBE * values * values * values))


def gelu_value(values):
    return 0.5 * values * (1.0 + gelu_tanh(values))


def gelu_slope(values):
    bent = gelu_tanh(values)
    return 0.5 * (1.0 + bent) + 0.5 * values * (1.0 - bent * bent) * GELU_SCALE * (
        1.0 + 3.0 * GELU_CUBE * values * values
    )


def head_copies(plan, side_ref, gathered_ref, one_ref, two_ref, lines_ref, sems):
    quarter = gathered_ref.shape[0] // 2
    shift = side_ref[0] * quarter
    targets = (one_ref, two_ref, lines_ref)
    copies = []
    for number, (at, owner, first, rows, target, row) in enumerate(plan):
        spot = at + shift if at < quarter else at - shift
        copies.append(
            pltpu.make_async_copy(
                gathered_ref.at[spot, owner, pl.ds(first, rows)],
                targets[target].at[pl.ds(row, rows)],
                sems.at[number],
            )
        )
    for copy in copies:
        copy.start()
    return [[copy for copy, item in zip(copies, plan) if item[4] == target] for target in range(3)]


def wait_all(copies):
    for copy in copies:
        copy.wait()


def spread_third(lines_ref, wide_ref, third_ref):
    groups = ROW // BOT
    for lane in range(BOT // 128):
        for group in range(groups):
            at = group * BOT + lane * 128
            wide_ref[lane, pl.ds(group, lines_ref.shape[0], stride=groups), :] = lines_ref[
                :, at : at + 128
            ].astype(single)
        third_ref[:, pl.ds(lane * 128, 128)] = wide_ref[lane].astype(narrow)


def head_up_kernel(
    plan, side_ref, normed_ref, gathered_ref, unit_ref, acts_ref, bottle_ref, pre_one_ref, pre_two_ref,
    one_ref, two_ref, lines_ref, wide_ref, third_ref, sems,
):
    copies = head_copies(plan, side_ref, gathered_ref, one_ref, two_ref, lines_ref, sems)
    acts_ref[...] = jnp.zeros_like(acts_ref)
    normed = normed_ref[...]
    acts_ref[:, pl.ds(0, D)] = normed
    piece = HID // 4
    wait_all(copies[0])
    for number in range(4):
        spot = pl.ds(number * piece, piece)
        pre = product_plain(normed, one_ref[:, spot])
        pre_one_ref[:, spot] = pre
        acts_ref[:, pl.ds(D + number * piece, piece)] = gelu_value(pre).astype(narrow)
    wait_all(copies[2])
    spread_third(lines_ref, wide_ref, third_ref)
    wait_all(copies[1])
    hidden = acts_ref[:, pl.ds(D, HID)]
    for number in range(4):
        spot = pl.ds(number * piece, piece)
        pre = product_plain(hidden, two_ref[:, spot])
        pre_two_ref[:, spot] = pre
        acts_ref[:, pl.ds(D + HID + number * piece, piece)] = gelu_value(pre).astype(narrow)
    bottle = product_plain(acts_ref[:, pl.ds(D + HID, HID)], third_ref[...])
    bottle_ref[...] = bottle
    unit_ref[...] = (
        bottle * lax.rsqrt(jnp.sum(bottle * bottle, axis=-1, keepdims=True) + 1e-06)
    ).astype(narrow)


def head_down_kernel(
    plan, side_ref, grad_ref, bottle_ref, pre_one_ref, pre_two_ref, gathered_ref, grads_ref, normed_grad_ref,
    one_ref, two_ref, lines_ref, wide_ref, third_ref, sems,
):
    copies = head_copies(plan, side_ref, gathered_ref, one_ref, two_ref, lines_ref, sems)
    grad, bottle = grad_ref[...], bottle_ref[...]
    scale = lax.rsqrt(jnp.sum(bottle * bottle, axis=-1, keepdims=True) + 1e-06)
    along = jnp.sum(grad * bottle, axis=-1, keepdims=True)
    grad_bottle = (scale * (grad - bottle * (along * scale * scale))).astype(narrow)
    grads_ref[:, pl.ds(2 * HID, BOT)] = grad_bottle
    wait_all(copies[2])
    spread_third(lines_ref, wide_ref, third_ref)
    piece = HID // 4
    for number in range(4):
        spot = pl.ds(number * piece, piece)
        back = product_right(grad_bottle, third_ref[spot, :])
        grads_ref[:, pl.ds(HID + number * piece, piece)] = (back * gelu_slope(pre_two_ref[:, spot])).astype(narrow)
    wait_all(copies[1])
    grad_two = grads_ref[:, pl.ds(HID, HID)]
    for number in range(4):
        spot = pl.ds(number * piece, piece)
        back = product_right(grad_two, two_ref[spot, :])
        grads_ref[:, spot] = (back * gelu_slope(pre_one_ref[:, spot])).astype(narrow)
    wait_all(copies[0])
    normed_grad_ref[...] = product_right(grads_ref[:, pl.ds(0, HID)], one_ref[...])


def head_pass(kernel, plan, side, inputs, gathered, shapes, waits=()):
    read = len(inputs) + 2
    return pl.pallas_call(
        lambda *refs: kernel(plan, *refs[:read], *refs[read + len(waits) :]),
        out_shape=shapes,
        in_specs=[pl.BlockSpec(memory_space=pltpu.SMEM)]
        + [pl.BlockSpec(memory_space=pltpu.VMEM)] * len(inputs)
        + [pl.BlockSpec(memory_space=pl.ANY)] * (1 + len(waits)),
        out_specs=[pl.BlockSpec(memory_space=pltpu.VMEM)] * len(shapes),
        scratch_shapes=[
            pltpu.VMEM((D, HID), narrow),
            pltpu.VMEM((HID, HID), narrow),
            pltpu.VMEM((BOT, ROW), narrow),
            pltpu.VMEM((BOT // 128, HID, 128), single),
            pltpu.VMEM((HID, BOT), narrow),
            pltpu.SemaphoreType.DMA((len(plan),)),
        ],
        compiler_params=pltpu.CompilerParams(vmem_limit_bytes=56 << 20),
        cost_estimate=pl.CostEstimate(flops=100 * 10**6, bytes_accessed=370 * 10**5, transcendentals=0),
    )(side, *inputs, gathered, *waits)


def fetch_rows(side_ref, part, gathered_ref, flat_ref, sems):
    quarter = flat_ref.shape[0] // 4
    side = side_ref[0]
    first, second = side * quarter, (1 - side) * quarter
    copies = [
        pltpu.make_async_copy(
            gathered_ref.at[pl.ds(at, quarter), owner, part],
            flat_ref.at[pl.ds(spot * quarter, quarter)],
            sems.at[spot],
        )
        for spot, (at, owner) in enumerate(((first, 0), (second, 0), (second, 1), (first, 1)))
    ]
    for copy in copies:
        copy.start()
    for copy in copies:
        copy.wait()


def matrix_rows(flat_ref, first_row, length):
    rows = flat_ref.shape[1]
    low, high = first_row // rows, -(-(first_row + length) // rows)
    lines = flat_ref[pl.ds(low, high - low)].reshape((high - low) * rows, D)
    at = first_row - low * rows
    return lines[at : at + length]


def spread_columns(flat_ref, first_row, width, wide_ref, out_ref):
    length = width * D
    lines = matrix_rows(flat_ref, first_row, length)
    for column in range(D // 128):
        lane = slice(column * 128, (column + 1) * 128)
        wide_ref[column, pl.ds(0, length), :] = lines[:, lane].astype(single)
    for group in range(width):
        for column in range(D // 128):
            out_ref[group, :, pl.ds(column * 128, 128)] = wide_ref[
                column, pl.ds(group, D, stride=width), :
            ].astype(narrow)


def head_lanes(values, odd):
    lanes = lax.broadcasted_iota(jnp.int32, values.shape, 1)
    return jnp.where((lanes >= HEAD_DIM) == odd, values, jnp.zeros_like(values))


def join_lanes(even, odd):
    lanes = lax.broadcasted_iota(jnp.int32, even.shape, 1)
    return jnp.where(lanes >= HEAD_DIM, odd, even)


def soft_rows(query, key):
    scores = product_right(query, key) * HEAD_DIM ** (-0.5)
    spots = lax.broadcasted_iota(jnp.int32, scores.shape, 1)
    scores = jnp.where(spots < SEQ, scores, -1e30)
    terms = jnp.exp(scores - jnp.max(scores, axis=-1, keepdims=True))
    return terms / jnp.sum(terms, axis=-1, keepdims=True)


def forward_kernel(part, keep, side_ref, stream_ref, vector_ref, gathered_ref, *refs):
    out_ref = refs[0]
    if keep:
        packed_ref, mixed_ref, attn_ref, pre_ref, mlp_ref = refs[1:6]
        flat_ref, wide_ref, qkv_ref, up_ref, hidden_ref, sems = refs[6:]
    else:
        flat_ref, wide_ref, qkv_ref, up_ref, hidden_ref, packed_ref, mixed_ref, sems = refs[1:]
    fetch_rows(side_ref, part, gathered_ref, flat_ref, sems)
    spread_columns(flat_ref, 0, 3, wide_ref, qkv_ref)
    spread_columns(flat_ref, 4 * D, FF // D, wide_ref, up_ref)
    w_proj = matrix_rows(flat_ref, 3 * D, D)
    w_down = matrix_rows(flat_ref, 4 * D + FF, FF)
    vectors = vector_ref[...].astype(single)
    stream = stream_ref[...]
    normed = (norm_parts(stream)[0] * vectors[0:1] + vectors[1:2]).astype(narrow)
    for group in range(3):
        packed_ref[:, pl.ds(group * D, D)] = product_plain(normed, qkv_ref[group]).astype(narrow)
    for image in range(stream.shape[0] // PAD_SEQ):
        rows = pl.ds(image * PAD_SEQ, PAD_SEQ)
        for pair in range(HEADS // 2):
            query, key, value = [
                packed_ref[rows, pl.ds(group * D + pair * 128, 128)] for group in range(3)
            ]
            done = [
                product_plain(soft_rows(head_lanes(query, odd), key).astype(narrow), value)
                for odd in (False, True)
            ]
            mixed_ref[rows, pl.ds(pair * 128, 128)] = join_lanes(*done).astype(narrow)
    attn = product_plain(mixed_ref[...], w_proj)
    middle = stream + vectors[2:3] * attn
    normed_two = (norm_parts(middle)[0] * vectors[3:4] + vectors[4:5]).astype(narrow)
    for group in range(FF // D):
        spot = pl.ds(group * D, D)
        pre = product_plain(normed_two, up_ref[group])
        if keep:
            pre_ref[:, spot] = pre
        hidden_ref[:, spot] = (0.5 * pre * (1.0 + gelu_tanh(pre))).astype(narrow)
    mlp = product_plain(hidden_ref[...], w_down)
    out_ref[...] = middle + vectors[5:6] * mlp
    if keep:
        attn_ref[...] = attn
        mlp_ref[...] = mlp


def layer_scratch(gathered):
    rows, blocks = gathered.shape[3], 2 * gathered.shape[0]
    return [
        pltpu.VMEM((blocks, rows, D), narrow),
        pltpu.VMEM((D // 128, FF, 128), single),
        pltpu.VMEM((3, D, D), narrow),
        pltpu.VMEM((FF // D, D, D), narrow),
    ]


def layer_specs_in(count):
    return (
        [pl.BlockSpec(memory_space=pltpu.SMEM)]
        + [pl.BlockSpec(memory_space=pltpu.VMEM)] * (count - 2)
        + [pl.BlockSpec(memory_space=pl.ANY)]
    )


def layer_forward(side, stream, vectors, gathered, part, keep):
    tokens = stream.shape[0]
    shapes = [jax.ShapeDtypeStruct((tokens, D), single)]
    extra = [
        jax.ShapeDtypeStruct((tokens, 3 * D), narrow),
        jax.ShapeDtypeStruct((tokens, D), narrow),
        jax.ShapeDtypeStruct((tokens, D), single),
        jax.ShapeDtypeStruct((tokens, FF), single),
        jax.ShapeDtypeStruct((tokens, D), single),
    ]
    scratch = layer_scratch(gathered) + [pltpu.VMEM((tokens, FF), narrow)]
    if keep:
        shapes = shapes + extra
    else:
        scratch = scratch + [pltpu.VMEM((tokens, 3 * D), narrow), pltpu.VMEM((tokens, D), narrow)]
    scratch.append(pltpu.SemaphoreType.DMA((4,)))
    return pl.pallas_call(
        lambda *refs: forward_kernel(part, keep, *refs),
        out_shape=shapes,
        in_specs=layer_specs_in(4),
        out_specs=[pl.BlockSpec(memory_space=pltpu.VMEM)] * len(shapes),
        scratch_shapes=scratch,
        compiler_params=pltpu.CompilerParams(vmem_limit_bytes=56 << 20),
        cost_estimate=pl.CostEstimate(flops=100 * 10**6, bytes_accessed=430 * 10**5, transcendentals=0),
    )(side, stream, vectors, gathered)


def mlp_back_kernel(
    part,
    side_ref,
    grad_ref,
    stream_ref,
    attn_ref,
    pre_ref,
    mlp_ref,
    vector_ref,
    gathered_ref,
    *refs,
):
    grad_mid_ref, weight_grad_ref, vector_grad_ref = refs[-9:-6]
    flat_ref, wide_ref, up_ref, hidden_ref, grad_pre_ref, sems = refs[-6:]
    lead = weight_grad_ref.shape[1] - 2 * FF
    weight_grad_ref[:, pl.ds(0, lead), :] = jnp.zeros((D // 128, lead, 128), single)
    fetch_rows(side_ref, part, gathered_ref, flat_ref, sems)
    spread_columns(flat_ref, 4 * D, FF // D, wide_ref, up_ref)
    w_down = matrix_rows(flat_ref, 4 * D + FF, FF)
    vectors = vector_ref[...].astype(single)
    grad_out = grad_ref[...]
    vector_grad_ref[...] = jnp.zeros_like(vector_grad_ref)
    attn = attn_ref[...]
    middle = stream_ref[...] + vectors[2:3] * attn
    unit_two, spread_two = norm_parts(middle)
    normed_two = (unit_two * vectors[3:4] + vectors[4:5]).astype(narrow)
    vector_grad_ref[pl.ds(5, 1), :] = jnp.sum(grad_out * mlp_ref[...], axis=0, keepdims=True)
    grad_mlp = (grad_out * vectors[5:6]).astype(narrow)
    grad_normed_two = jnp.zeros_like(grad_out)
    for group in range(FF // D):
        spot = pl.ds(group * D, D)
        pre = pre_ref[:, spot]
        bent = gelu_tanh(pre)
        hidden_ref[:, spot] = (0.5 * pre * (1.0 + bent)).astype(narrow)
        slope = 0.5 * (1.0 + bent) + 0.5 * pre * (1.0 - bent * bent) * GELU_SCALE * (
            1.0 + 3.0 * GELU_CUBE * pre * pre
        )
        grad_hidden = product_right(grad_mlp, w_down[group * D : (group + 1) * D])
        grad_pre = (grad_hidden * slope).astype(narrow)
        grad_pre_ref[:, spot] = grad_pre
        grad_normed_two = grad_normed_two + product_right(grad_pre, up_ref[group])
    for group in range(FF // D):
        spot = pl.ds(group * D, D)
        up_grad = product_left(normed_two, grad_pre_ref[:, spot])
        down_grad = product_left(hidden_ref[:, spot], grad_mlp)
        for column in range(D // 128):
            lane = slice(column * 128, (column + 1) * 128)
            weight_grad_ref[column, pl.ds(lead + group, D, stride=FF // D), :] = up_grad[:, lane]
            weight_grad_ref[column, pl.ds(lead + FF + group * D, D), :] = down_grad[:, lane]
    vector_grad_ref[pl.ds(3, 1), :] = jnp.sum(grad_normed_two * unit_two, axis=0, keepdims=True)
    vector_grad_ref[pl.ds(4, 1), :] = jnp.sum(grad_normed_two, axis=0, keepdims=True)
    grad_mid = grad_out + norm_back(grad_normed_two, unit_two, spread_two, vectors[3:4])
    vector_grad_ref[pl.ds(2, 1), :] = jnp.sum(grad_mid * attn, axis=0, keepdims=True)
    grad_mid_ref[...] = grad_mid


def attention_back_kernel(
    part,
    side_ref,
    grad_ref,
    stream_ref,
    packed_ref,
    mixed_ref,
    vector_ref,
    gathered_ref,
    *refs,
):
    grad_in_ref, weight_grad_ref, vector_grad_ref = refs[-9:-6]
    flat_ref, wide_ref, qkv_ref, grad_mixed_ref, grad_packed_ref, sems = refs[-6:]
    rest = weight_grad_ref.shape[1] - 4 * D
    weight_grad_ref[:, pl.ds(4 * D, rest), :] = jnp.zeros((D // 128, rest, 128), single)
    fetch_rows(side_ref, part, gathered_ref, flat_ref, sems)
    spread_columns(flat_ref, 0, 3, wide_ref, qkv_ref)
    w_proj = matrix_rows(flat_ref, 3 * D, D)
    vectors = vector_ref[...].astype(single)
    vector_grad_ref[...] = jnp.zeros_like(vector_grad_ref)
    grad_mid = grad_ref[...]
    stream = stream_ref[...]
    grad_attn = (grad_mid * vectors[2:3]).astype(narrow)
    proj_grad = product_left(mixed_ref[...], grad_attn)
    for column in range(D // 128):
        weight_grad_ref[column, pl.ds(3 * D, D), :] = proj_grad[:, column * 128 : (column + 1) * 128]
    grad_mixed_ref[...] = product_right(grad_attn, w_proj).astype(narrow)
    for image in range(stream.shape[0] // PAD_SEQ):
        rows = pl.ds(image * PAD_SEQ, PAD_SEQ)
        for pair in range(HEADS // 2):
            query, key, value = [
                packed_ref[rows, pl.ds(group * D + pair * 128, 128)] for group in range(3)
            ]
            grad_mixed = grad_mixed_ref[rows, pl.ds(pair * 128, 128)]
            parts = []
            for odd in (False, True):
                probs = soft_rows(head_lanes(query, odd), key)
                grad_probs = product_right(head_lanes(grad_mixed, odd), value)
                grad_value = product_left(probs.astype(narrow), grad_mixed)
                grad_scores = probs * (grad_probs - jnp.sum(probs * grad_probs, axis=-1, keepdims=True))
                grad_raw = (grad_scores * HEAD_DIM ** (-0.5)).astype(narrow)
                parts.append((product_plain(grad_raw, key), product_left(grad_raw, query), grad_value))
            for group in range(3):
                grad_packed_ref[rows, pl.ds(group * D + pair * 128, 128)] = join_lanes(
                    parts[0][group], parts[1][group]
                ).astype(narrow)
    unit_one, spread_one = norm_parts(stream)
    normed = (unit_one * vectors[0:1] + vectors[1:2]).astype(narrow)
    grad_normed = jnp.zeros_like(grad_mid)
    for group in range(3):
        grad_part = grad_packed_ref[:, pl.ds(group * D, D)]
        grad_normed = grad_normed + product_right(grad_part, qkv_ref[group])
        qkv_grad = product_left(normed, grad_part)
        for column in range(D // 128):
            lane = slice(column * 128, (column + 1) * 128)
            weight_grad_ref[column, pl.ds(group, D, stride=3), :] = qkv_grad[:, lane]
    vector_grad_ref[pl.ds(0, 1), :] = jnp.sum(grad_normed * unit_one, axis=0, keepdims=True)
    vector_grad_ref[pl.ds(1, 1), :] = jnp.sum(grad_normed, axis=0, keepdims=True)
    grad_in_ref[...] = grad_mid + norm_back(grad_normed, unit_one, spread_one, vectors[0:1])


def layer_back(kernel, part, weight_rows, side, inputs, vectors, gathered, waits, held, columns, buffers):
    tokens = inputs[0].shape[0]
    rows, blocks = gathered.shape[3], 2 * gathered.shape[0]
    return pl.pallas_call(
        lambda *refs: kernel(part, *refs[: len(refs) - 6 - len(held)], *refs[len(refs) - 6 :]),
        out_shape=[
            jax.ShapeDtypeStruct((tokens, D), single),
            jax.ShapeDtypeStruct((D // 128, weight_rows, 128), single),
            jax.ShapeDtypeStruct((8, D), single),
        ]
        + [jax.ShapeDtypeStruct(array.shape, array.dtype) for array in held],
        in_specs=layer_specs_in(len(inputs) + 3) + [pl.BlockSpec(memory_space=pl.ANY)] * (len(waits) + len(held)),
        out_specs=[pl.BlockSpec(memory_space=pltpu.VMEM)] * 3 + [pl.BlockSpec(memory_space=pl.ANY)] * len(held),
        input_output_aliases={len(inputs) + 3 + len(waits) + number: 3 + number for number in range(len(held))},
        scratch_shapes=[
            pltpu.VMEM((blocks, rows, D), narrow),
            pltpu.VMEM((D // 128, columns * D, 128), single),
            pltpu.VMEM((columns, D, D), narrow),
        ]
        + [pltpu.VMEM((tokens, width), narrow) for width in buffers]
        + [pltpu.SemaphoreType.DMA((4,))],
        compiler_params=pltpu.CompilerParams(vmem_limit_bytes=56 << 20),
        cost_estimate=pl.CostEstimate(flops=100 * 10**6, bytes_accessed=600 * 10**5, transcendentals=0),
    )(side, *inputs, vectors, gathered, *waits, *held)


def pair_rows_of(block_rows):
    pair = 2 * block_rows
    return 4 * D // pair * pair, -(-4 * D // pair) * pair


def mlp_back(side, grad_out, saved, vectors, gathered, part, waits, held):
    stream, packed, mixed, attn, pre, mlp = saved
    return layer_back(
        mlp_back_kernel, part, MATRIX_ROWS - pair_rows_of(gathered.shape[3])[0], side,
        (grad_out, stream, attn, pre, mlp), vectors, gathered, waits, held,
        FF // D, (FF, FF),
    )


def attention_back(side, grad_mid, saved, vectors, gathered, part, waits, held):
    stream, packed, mixed, attn, pre, mlp = saved
    return layer_back(
        attention_back_kernel, part, pair_rows_of(gathered.shape[3])[1], side,
        (grad_mid, stream, packed, mixed), vectors, gathered, waits, held,
        3, (D, 3 * D),
    )


def after(value, *tokens):
    def kernel(*refs):
        refs[-1][...] = refs[0][...]

    return pl.pallas_call(
        kernel,
        out_shape=jax.ShapeDtypeStruct(value.shape, value.dtype),
        in_specs=[pl.BlockSpec(memory_space=pltpu.VMEM)] + [pl.BlockSpec(memory_space=pl.ANY)] * len(tokens),
        out_specs=pl.BlockSpec(memory_space=pltpu.VMEM),
    )(value, *tokens)


def embed_back_kernel(grad_ref, patch_ref, shown_ref, gain_ref, vector_ref, *refs):
    out_ref = refs[-1]
    grad = grad_ref[...]
    images = grad.shape[0] // PAD_SEQ
    shown = shown_ref[...]
    position = jnp.zeros((PAD_SEQ, D), single)
    token = jnp.zeros((1, D), single)
    patch_grads = []
    for image in range(images):
        here = grad[image * PAD_SEQ : (image + 1) * PAD_SEQ]
        position = position + here
        rows = here[1:SEQ]
        seen = shown[image * PATCHES : (image + 1) * PATCHES]
        token = token + jnp.sum(rows * (1.0 - seen), axis=0, keepdims=True)
        patch_grads.append((rows * seen).astype(narrow))
    patch_grad = product_left(patch_ref[...], jnp.concatenate(patch_grads))
    out_ref[...] = jnp.zeros_like(out_ref)
    for column in range(D // 128):
        lane = slice(column * 128, (column + 1) * 128)
        out_ref[column, pl.ds(0, PIX), :] = patch_grad[:, lane]
        out_ref[column, pl.ds(PIX, SEQ), :] = position[:SEQ, lane]
        out_ref[column, pl.ds(PIX + SEQ, 1), :] = position[0:1, lane]
        out_ref[column, pl.ds(PIX + SEQ + 1, 1), :] = token[:, lane]
        out_ref[column, pl.ds(PIX + SEQ + 2, 2), :] = gain_ref[:, lane]
        out_ref[column, pl.ds(EMBED_ROWS, vector_ref.shape[0]), :] = vector_ref[:, lane]


def embed_back(grad, patch_rows, shown, gains, vector_grads, rows, waits):
    return pl.pallas_call(
        embed_back_kernel,
        out_shape=jax.ShapeDtypeStruct((D // 128, rows, 128), single),
        in_specs=[pl.BlockSpec(memory_space=pltpu.VMEM)] * 5 + [pl.BlockSpec(memory_space=pl.ANY)] * len(waits),
        out_specs=pl.BlockSpec(memory_space=pltpu.VMEM),
        compiler_params=pltpu.CompilerParams(vmem_limit_bytes=40 << 20),
        cost_estimate=pl.CostEstimate(flops=100 * 10**6, bytes_accessed=37 * 10**5, transcendentals=0),
    )(grad, patch_rows, shown, gains, vector_grads, *waits)


def proto_units(values):
    rounded = values.astype(narrow).astype(single)
    scale = lax.rsqrt(jnp.sum(rounded * rounded, axis=-1, keepdims=True) + 1e-06)
    return rounded, scale, (rounded * scale).astype(narrow)


def proto_terms(teacher_z, student_z, teacher_unit, student_unit, centre_column):
    teacher_logits = product_right(teacher_unit, teacher_z)
    logits = product_right(student_unit, student_z)
    teacher_exp = jnp.exp((teacher_logits - centre_column) * (1.0 / tau_teacher))
    student_exp = jnp.exp(logits * (1.0 / tau_student))
    return teacher_logits, logits, teacher_exp, student_exp


def logits_kernel(
    teacher_z_ref,
    student_z_ref,
    teacher_ref,
    student_ref,
    centre_ref,
    class_ref,
    mixed_ref,
    mixed_teacher_ref,
    sums_ref,
    centre_sum_ref,
    student_mix_ref,
    teacher_mix_ref,
    totals_ref,
):
    step = pl.program_id(0)

    @pl.when(step == 0)
    def _():
        student_mix_ref[...] = jnp.zeros_like(student_mix_ref)
        teacher_mix_ref[...] = jnp.zeros_like(teacher_mix_ref)
        totals_ref[...] = jnp.zeros_like(totals_ref)

    teacher_unit = proto_units(teacher_ref[...])[2]
    student_unit = proto_units(student_ref[...])[2]
    teacher_logits, logits, teacher_exp, student_exp = proto_terms(
        teacher_z_ref[...], student_z_ref[...], teacher_unit, student_unit, centre_ref[...]
    )
    totals_ref[pl.ds(0, 1), :] += jnp.sum(teacher_exp, axis=0, keepdims=True)
    totals_ref[pl.ds(1, 1), :] += jnp.sum(student_exp, axis=0, keepdims=True)
    totals_ref[pl.ds(2, 1), :] += jnp.sum(teacher_exp * logits, axis=0, keepdims=True)
    centre_sum_ref[...] = jnp.sum(teacher_logits * class_ref[0:1], axis=1, keepdims=True)
    student_mix_ref[...] += product_left(student_unit, student_exp.astype(narrow))
    teacher_mix_ref[...] += product_left(student_unit, teacher_exp.astype(narrow))

    @pl.when(step == pl.num_programs(0) - 1)
    def _():
        mixed_ref[...] = student_mix_ref[...].T
        mixed_teacher_ref[:, pl.ds(0, BOT)] = teacher_mix_ref[...].T
        lower = jnp.zeros((128 - totals_ref.shape[0], totals_ref.shape[1]), single)
        mixed_teacher_ref[:, pl.ds(BOT, 128)] = jnp.concatenate([totals_ref[...], lower]).T
        sums_ref[...] = totals_ref[...]


def proto_specs(rows, block):
    whole = pl.BlockSpec((rows, BOT), lambda i: (0, 0))
    table = pl.BlockSpec((block, BOT), lambda i: (i, 0))
    column = pl.BlockSpec((block, 1), lambda i: (i, 0))
    lines = pl.BlockSpec((8, rows), lambda i: (0, 0))
    return whole, table, column, lines


def logits_pass(teacher_z, student_z, teacher, student, centre_column, class_lines):
    rows, protos_here = teacher_z.shape[0], student.shape[0]
    block = protos_here // 4
    whole, table, column, lines = proto_specs(rows, block)
    return pl.pallas_call(
        logits_kernel,
        grid=(4,),
        out_shape=[
            jax.ShapeDtypeStruct((rows, BOT), single),
            jax.ShapeDtypeStruct((rows, BOT + 128), single),
            jax.ShapeDtypeStruct((8, rows), single),
            jax.ShapeDtypeStruct((protos_here, 1), single),
        ],
        in_specs=[whole, whole, table, table, column, lines],
        out_specs=[whole, pl.BlockSpec((rows, BOT + 128), lambda i: (0, 0)), lines, column],
        scratch_shapes=[
            pltpu.VMEM((BOT, rows), single),
            pltpu.VMEM((BOT, rows), single),
            pltpu.VMEM((8, rows), single),
        ],
        compiler_params=pltpu.CompilerParams(vmem_limit_bytes=56 << 20),
        cost_estimate=pl.CostEstimate(flops=100 * 10**6, bytes_accessed=520 * 10**5, transcendentals=0),
    )(teacher_z, student_z, teacher, student, centre_column, class_lines)


def proto_grad_kernel(
    held, teacher_z_ref, student_z_ref, teacher_ref, student_ref, centre_ref, scale_ref, *refs
):
    grad_ref, square_ref = refs[held : held + 2]
    step = pl.program_id(0)

    @pl.when(step == 0)
    def _():
        square_ref[...] = jnp.zeros_like(square_ref)

    teacher_unit = proto_units(teacher_ref[...])[2]
    rounded, scale, student_unit = proto_units(student_ref[...])
    student_z = student_z_ref[...]
    _, _, teacher_exp, student_exp = proto_terms(
        teacher_z_ref[...], student_z, teacher_unit, student_unit, centre_ref[...]
    )
    grad_logits = (student_exp * scale_ref[0:1] - teacher_exp * scale_ref[1:2]).astype(narrow)
    unit_grad = product_plain(grad_logits, student_z)
    along = jnp.sum(unit_grad * rounded, axis=-1, keepdims=True)
    grad = scale * (unit_grad - rounded * (along * scale * scale))
    grad_ref[...] = grad
    square_ref[...] += jnp.broadcast_to(jnp.sum(grad * grad), square_ref.shape)


def proto_grad_pass(teacher_z, student_z, teacher, student, centre_column, scale_lines, held):
    rows, protos_here = teacher_z.shape[0], student.shape[0]
    block = protos_here // 4
    whole, table, column, lines = proto_specs(rows, block)
    return pl.pallas_call(
        lambda *refs: proto_grad_kernel(len(held), *refs),
        grid=(4,),
        out_shape=[
            jax.ShapeDtypeStruct((protos_here, BOT), single),
            jax.ShapeDtypeStruct((8, 128), single),
        ]
        + [jax.ShapeDtypeStruct(array.shape, array.dtype) for array in held],
        in_specs=[whole, whole, table, table, column, lines]
        + [pl.BlockSpec(memory_space=pl.ANY)] * len(held),
        out_specs=[table, pl.BlockSpec((8, 128), lambda i: (0, 0))]
        + [pl.BlockSpec(memory_space=pl.ANY)] * len(held),
        input_output_aliases={6 + number: 2 + number for number in range(len(held))},
        compiler_params=pltpu.CompilerParams(vmem_limit_bytes=56 << 20),
        cost_estimate=pl.CostEstimate(flops=100 * 10**6, bytes_accessed=400 * 10**5, transcendentals=0),
    )(teacher_z, student_z, teacher, student, centre_column, scale_lines, *held)


def proto_update(factor, student, moment, second, teacher, grad):
    def kernel(factor_ref, *refs):
        weight, moment, second, teacher, grad = [ref[...] for ref in refs[:5]]
        done = adam_update(weight, moment, second, grad * factor_ref[0], teacher)
        for ref, value in zip(refs[5:], done):
            ref[...] = value

    block = student.shape[0] // 4
    table = pl.BlockSpec((block, BOT), lambda i: (i, 0))
    return pl.pallas_call(
        kernel,
        grid=(4,),
        out_shape=[
            jax.ShapeDtypeStruct(student.shape, narrow if number == 3 else single) for number in range(5)
        ],
        in_specs=[pl.BlockSpec(memory_space=pltpu.SMEM)] + [table] * 5,
        out_specs=[table] * 5,
        compiler_params=pltpu.CompilerParams(vmem_limit_bytes=60 << 20),
        cost_estimate=pl.CostEstimate(flops=10**7, bytes_accessed=2 * 10**7, transcendentals=0),
    )(factor.reshape(1), student, moment, second, teacher, grad)


def head_grads_kernel(
    held, place_ref, inputs_ref, grads_ref, *refs,
):
    own_ref, partner_ref = refs[len(refs) - 9 - held :][:2] if held else refs[-9:-7]
    window_ref, rows_ref, product_ref, third_ref, bottle_ref, line_ref, sems = refs[-7:]
    slot = own_ref.shape[0]
    lead = product_ref.shape[0] - window_ref.shape[1]
    number = lax.broadcasted_iota(jnp.int32, (slot, 1), 0)
    product_ref[pl.ds(0, lead), :] = jnp.zeros((lead, ROW), single)

    def block(at, out_ref):
        column = pl.multiple_of(place_ref[at], 128)
        grad_column = pl.multiple_of(place_ref[at + 3], 128)
        copies = [
            pltpu.make_async_copy(
                inputs_ref.at[:, pl.ds(column, window_ref.shape[1])], window_ref, sems.at[0]
            ),
            pltpu.make_async_copy(grads_ref.at[:, pl.ds(grad_column, ROW)], rows_ref, sems.at[1]),
        ]
        for copy in copies:
            copy.start()
        for copy in copies:
            copy.wait()
        window = window_ref[...]
        for piece in range(4):
            spot = pl.ds(piece * (ROW // 4), ROW // 4)
            product_ref[pl.ds(lead, window.shape[1]), spot] = product_left(window, rows_ref[:, spot])
        from_row = pl.multiple_of(lead + place_ref[at + 1], 8)
        kept = jnp.where(number < place_ref[at + 2], product_ref[pl.ds(from_row, slot), :], 0.0)
        out_ref[...] = kept.astype(out_ref.dtype)

    @pl.when(place_ref[8] == 0)
    def _():
        block(0, own_ref)

    @pl.when(place_ref[8] == 1)
    def _():
        column = pl.multiple_of(place_ref[9], 128)
        copies = [
            pltpu.make_async_copy(
                inputs_ref.at[:, pl.ds(column, third_ref.shape[1])], third_ref, sems.at[0]
            ),
            pltpu.make_async_copy(grads_ref.at[:, pl.ds(2 * HID, BOT)], bottle_ref, sems.at[1]),
        ]
        for copy in copies:
            copy.start()
        for copy in copies:
            copy.wait()
        third = product_left(third_ref[...], bottle_ref[...])
        for lane in range(BOT // 128):
            line_ref[lane] = third[:, lane * 128 : (lane + 1) * 128]
        for group in range(ROW // BOT):
            for lane in range(BOT // 128):
                value = line_ref[lane, pl.ds(group, slot, stride=ROW // BOT), :]
                own_ref[:, pl.ds(group * BOT + lane * 128, 128)] = jnp.where(
                    number < place_ref[2], value, 0.0
                )

    block(4, partner_ref)


def head_grads(place, inputs_all, grads_all, slot, lead, waits, held):
    rows = inputs_all.shape[0]
    wide = slot * ROW // BOT
    return pl.pallas_call(
        lambda *refs: head_grads_kernel(len(held), *refs),
        out_shape=[jax.ShapeDtypeStruct((slot, ROW), kind) for kind in (single, narrow)]
        + [jax.ShapeDtypeStruct(array.shape, array.dtype) for array in held],
        in_specs=[pl.BlockSpec(memory_space=pltpu.SMEM)]
        + [pl.BlockSpec(memory_space=pl.ANY)] * (2 + len(waits) + len(held)),
        out_specs=[pl.BlockSpec(memory_space=pltpu.VMEM)] * 2
        + [pl.BlockSpec(memory_space=pl.ANY)] * len(held),
        input_output_aliases={3 + len(waits) + number: 2 + number for number in range(len(held))},
        scratch_shapes=[
            pltpu.VMEM((rows, 256), narrow),
            pltpu.VMEM((rows, ROW), narrow),
            pltpu.VMEM((lead + 256, ROW), single),
            pltpu.VMEM((rows, wide), narrow),
            pltpu.VMEM((rows, BOT), narrow),
            pltpu.VMEM((BOT // 128, wide, 128), single),
            pltpu.SemaphoreType.DMA((2,)),
        ],
        compiler_params=pltpu.CompilerParams(vmem_limit_bytes=56 << 20),
        cost_estimate=pl.CostEstimate(flops=100 * 10**6, bytes_accessed=370 * 10**5, transcendentals=0),
    )(place, inputs_all, grads_all, *waits, *held)


def close_local(
    patches,
    masked,
    slot_used,
    stem,
    stem_moment,
    stem_second,
    stem_teacher,
    layers,
    layer_moment,
    layer_second,
    layer_teacher,
    protos,
    proto_moment,
    proto_second,
    proto_teacher,
    centre,
):
    count = 1 << len(BITS)
    half = count // 2
    me = lax.axis_index("dev")
    across = MASKS["b"]
    student_side = me >= half
    groups = [list(range(half)), list(range(half, count))]
    quarter = half // 2
    swap = jnp.where(student_side, quarter, 0)
    side = student_side.astype(jnp.int32).reshape(1)
    images_here = patches.shape[0]
    rows_here = images_here * 17
    pair_rows = -(-2 * rows_here // 16) * 16
    more_rows = pair_rows - 2 * rows_here
    stem_piece = stem.shape[0]
    layer_piece = layers.shape[1]
    block_rows = MATRIX_ROWS // count
    block = block_rows * D
    tail = layer_piece * count - MATRIX_ROWS * D
    drift = layer_piece - block
    bounds = head_bounds(count, stem_piece)
    sizes = [bounds[i + 1] - bounds[i] for i in range(count)]
    slot = max(sizes)
    starts = [b * ROW + EMBED_FLAT - stem_piece * i for i, b in enumerate(bounds[:-1])]
    first_w2 = bounds.index(D)
    first_w3 = bounds.index(D + HID)
    row_index = jnp.concatenate([jnp.zeros((images_here, 1), jnp.int32), masked + 1], axis=1)
    masked_here = jnp.any(
        masked[:, :, None] == jnp.arange(PATCHES, dtype=jnp.int32)[None, None, :], axis=1
    )
    kept = slot_used.astype(single)

    front = 16
    early_rows = -(-stem_piece // D)
    late_start = early_rows * D - stem_piece
    embed_rows = -(-early_rows // 16) * 16
    own_layers = jnp.concatenate([layer_teacher, layers])
    own_tail = own_layers[:, layer_piece - tail :].reshape(2 * LAYERS, tail // 128, 128)
    before = lax.ppermute(own_tail, "dev", step_pairs(count, 1))
    last_lines = lax.ppermute(
        jnp.pad(own_tail, ((0, 0), (0, 24 - tail // 128), (0, 0))), "dev", [(count - 1, 0)]
    )
    head_span = GROUP * ROW
    stems = jnp.stack([as_lanes(stem_teacher), as_lanes(stem)])
    stems_next = lax.ppermute(stems[:, : head_span // 128], "dev", step_pairs(count, -1))
    def per_device(rows):
        return lax.dynamic_slice(jnp.array(rows, jnp.int32), (me, 0), (1, len(rows[0]))).reshape(-1)

    def spots(*values):
        return [part for value in values for part in (value // 128, value % 128)]

    place = per_device(
        [
            spots(starts[i] + front * 128, front * 128 + (0 if i == 0 else late_start), tail - drift * i)
            for i in range(count)
        ]
    )
    head_blocks, layer_blocks, embed_blocks, vector_blocks = own_blocks(
        place,
        stems,
        stems_next,
        as_lanes(own_layers),
        before,
        last_lines,
        (front, stem_piece, layer_piece, tail),
        slot,
        block_rows,
        embed_rows,
    )

    other_layers = lax.ppermute(layer_blocks, "dev", pairs(count, across))
    both_layers = jnp.where(
        student_side,
        jnp.stack([other_layers, layer_blocks]),
        jnp.stack([layer_blocks, other_layers]),
    )
    gathered = lax.all_gather(both_layers, "dev", axis=0, axis_index_groups=groups)
    head_out = jnp.where(student_side, head_blocks[0], head_blocks[1])
    head_keep = jnp.where(student_side, head_blocks[1], head_blocks[0])
    head_got = lax.ppermute(head_out, "dev", pairs(count, across))
    both_head = jnp.where(
        student_side, jnp.stack([head_got, head_keep]), jnp.stack([head_keep, head_got])
    )

    seed = jnp.concatenate([embed_blocks.reshape(2 * embed_rows, D), vector_blocks.reshape(8 * 2 * LAYERS, D)])
    third = -(-seed.shape[0] // 48) * 16
    spread_parts = []
    for number, order in enumerate(("xyba", "baxy", "ybax")):
        spread = seed[number * third : (number + 1) * third]
        reached = [0, 1]
        for name in order:
            moves = [(i, i ^ MASKS[name]) for i in reached]
            got = lax.ppermute(spread, "dev", moves)
            targets = [t for s, t in moves]
            is_target = jnp.array([i in targets for i in range(count)])[me]
            spread = jnp.where(is_target, got, spread)
            reached = reached + targets
        spread_parts.append(spread)
    spread = jnp.concatenate(spread_parts)
    other = lax.ppermute(spread, "dev", pairs(count, 1))
    is_even = me % 2 == 0
    even = jnp.where(is_even, spread, other)
    odd = jnp.where(is_even, other, spread)
    embed_all = [
        jnp.concatenate(
            [
                even[m * embed_rows : m * embed_rows + early_rows],
                odd[m * embed_rows : m * embed_rows + EMBED_ROWS - early_rows],
            ]
        )
        for m in range(2)
    ]
    gathered_head = lax.all_gather(after(both_head, gathered, even, odd), "dev", axis=0, axis_index_groups=groups)
    vectors_all = even[2 * embed_rows :].reshape(2, LAYERS, 8, D)

    plan = []
    for i in range(1, count):
        target = 0 if i < first_w2 else 1 if i < first_w3 else 2
        row = bounds[i] - (0, D, D + HID)[target]
        skip = max(-row, 0)
        owner = 1 if i >= half else 0
        plan.append((i ^ across if owner else i, owner, skip, sizes[i] - skip, target, row + skip))

    def embed_parts(model):
        rows = embed_all[model]
        return (rows[:PIX], rows[PIX : PIX + SEQ], rows[PIX + SEQ :], None, None, None)

    def head_rows(stream, extras):
        chosen = jnp.take_along_axis(stream, row_index[:, :, None], axis=1).reshape(rows_here, D)
        normed = layer_norm(chosen, extras[2].astype(single), extras[3].astype(single)).astype(narrow)
        return chosen, normed

    def start_rows(parts, student):
        stream = embed(parts, patches, masked_here, student)
        return jnp.pad(stream, ((0, 0), (0, PAD_SEQ - SEQ), (0, 0))).reshape(images_here * PAD_SEQ, D)

    student_parts = embed_parts(1)
    stream = start_rows(student_parts, True)
    saved_layers = []
    for layer_index in range(LAYERS):
        before_layer = stream
        stream, *saved = layer_forward(
            side, stream, vectors_all[1, layer_index], gathered, LAYERS + layer_index, True
        )
        saved_layers.append((before_layer, *saved))
    teacher_parts = embed_parts(0)
    teacher_stream = start_rows(teacher_parts, False)
    for layer_index in range(LAYERS):
        teacher_stream = layer_forward(
            side, teacher_stream, vectors_all[0, layer_index], gathered, layer_index, False
        )[0]
    stream = stream.reshape(images_here, PAD_SEQ, D)
    teacher_stream = teacher_stream.reshape(images_here, PAD_SEQ, D)
    chosen, student_normed = head_rows(stream, student_parts[2])
    teacher_normed = head_rows(teacher_stream, teacher_parts[2])[1]

    normed_got = lax.ppermute(
        jnp.where(student_side, teacher_normed, student_normed), "dev", pairs(count, across)
    )
    normed = jnp.where(
        student_side,
        jnp.concatenate([normed_got, student_normed]),
        jnp.concatenate([teacher_normed, normed_got]),
    )
    normed = jnp.pad(normed, ((0, more_rows), (0, 0)))
    third_end = (bounds[-2] - D - HID + slot) * (ROW // BOT)
    acts_width = D + HID + max(third_end, HID)
    unit_z, acts, bottleneck, pre_one, pre_two = head_pass(
        head_up_kernel,
        plan,
        side,
        (normed,),
        gathered_head,
        [
            jax.ShapeDtypeStruct((pair_rows, BOT), narrow),
            jax.ShapeDtypeStruct((pair_rows, acts_width), narrow),
            jax.ShapeDtypeStruct((pair_rows, BOT), single),
            jax.ShapeDtypeStruct((pair_rows, HID), single),
            jax.ShapeDtypeStruct((pair_rows, HID), single),
        ],
    )
    inputs_all = lax.all_gather(acts, "dev", axis=0, axis_index_groups=groups).reshape(half * pair_rows, -1)

    all_rows = half * pair_rows
    flag_row = 2 * rows_here
    kept_row = jnp.broadcast_to(kept[:, None] * (1.0 / 128.0), (images_here, 17)).reshape(1, rows_here)
    kept_row = jnp.pad(kept_row.astype(narrow), ((0, 0), (0, BOT - rows_here)))
    z_pair = cube_gather(jnp.concatenate([unit_z[:flag_row], kept_row, unit_z[flag_row + 1 :]]), "b")
    teacher_z_all = cube_gather(z_pair[0], "xygc")
    student_z_all = cube_gather(z_pair[1], "gxyc").reshape((2,) * 4 + (pair_rows, BOT))
    student_z_all = jnp.transpose(student_z_all, (0, 3, 1, 2, 4, 5)).reshape(half, pair_rows, BOT)
    all_kept = jnp.concatenate(
        [
            teacher_z_all[:, flag_row, :rows_here],
            student_z_all[:, flag_row, :rows_here],
            jnp.zeros((half, more_rows), narrow),
        ],
        axis=1,
    )
    all_kept = all_kept.astype(single).reshape(all_rows) * 128.0
    teacher_z_all = teacher_z_all.reshape(all_rows, BOT)
    student_z_all = student_z_all.reshape(all_rows, BOT)
    protos_here = protos.shape[0]
    own_centre = lax.dynamic_slice(centre, (me * protos_here,), (protos_here,))
    centre_column = own_centre.reshape(protos_here, 1)
    spot_in_pair = jnp.arange(all_rows) % pair_rows
    is_class = (spot_in_pair % 17) == 0
    class_kept = jnp.where(is_class, all_kept, 0.0)
    row_weight = jnp.where(is_class, all_kept, all_kept * (1.0 / 16.0))
    count_total = jnp.sum(class_kept)

    def lines(*values):
        return jnp.pad(jnp.stack(values), ((0, 8 - len(values)), (0, 0)))

    mixed_student, mixed_teacher, sums, centre_sum = logits_pass(
        teacher_z_all, student_z_all, proto_teacher, protos, centre_column, lines(class_kept)
    )
    by_pair = (2,) * 4 + (pair_rows, -1)
    mixed_own = jnp.concatenate(
        [
            cube_scatter(mixed_student.reshape(by_pair), "cgyx", "cgyx"),
            cube_scatter(mixed_teacher.reshape(by_pair), "cgyx", "cxyg"),
        ],
        axis=1,
    )
    mixed_own = mixed_own + lax.ppermute(
        mixed_own.astype(narrow), "dev", [(i, i ^ across) for i in range(half)]
    ).astype(single)
    scale = row_weight / tau_student
    flags = bit_flags(me)
    pair_at = flags["c"] * 8 + flags["g"] * 4 + flags["y"] * 2 + flags["x"]
    own_scale = lax.dynamic_slice(scale, (pair_at * pair_rows,), (pair_rows,))[:, None]
    grad_unit_z = own_scale * (
        mixed_own[:, :BOT] / mixed_own[:, 2 * BOT + 1 : 2 * BOT + 2]
        - mixed_own[:, BOT : 2 * BOT] / mixed_own[:, 2 * BOT : 2 * BOT + 1]
    )
    own_new_centre = (
        centre_keep * own_centre + (1.0 - centre_keep) * centre_sum.reshape(protos_here) / count_total
    )

    grads, grad_normed = head_pass(
        head_down_kernel,
        plan,
        side,
        (grad_unit_z, bottleneck, pre_one, pre_two),
        gathered_head,
        [
            jax.ShapeDtypeStruct((pair_rows, 2 * HID + BOT), narrow),
            jax.ShapeDtypeStruct((pair_rows, D), single),
        ],
    )
    carried = jnp.concatenate([own_new_centre, sums[:3].reshape(-1)])
    carried_size = carried.shape[0]
    width = grads.shape[1]
    carried_rows = -(-3 * carried_size // width)
    assert carried_rows <= more_rows
    high = carried.astype(narrow)
    middle = (carried - high.astype(single)).astype(narrow)
    low = (carried - high.astype(single) - middle.astype(single)).astype(narrow)
    carried = jnp.pad(jnp.concatenate([high, middle, low]), (0, carried_rows * width - 3 * carried_size))
    grads = jnp.concatenate(
        [
            grads[: 2 * rows_here],
            carried.reshape(carried_rows, width),
            grads[2 * rows_here + carried_rows :],
        ]
    )
    grads_all = lax.all_gather(grads, "dev", axis=0, axis_index_groups=groups).reshape(half * pair_rows, -1)
    normed_back = lax.ppermute(
        grad_normed[:rows_here], "dev", [(i, i ^ across) for i in range(half, count)]
    )
    own_grad_normed = jnp.where(student_side, grad_normed[rows_here : 2 * rows_here], normed_back)
    extras = student_parts[2].astype(single)
    grad_chosen, grad_gain, grad_bias = jax.vjp(layer_norm, chosen, extras[2], extras[3])[1](
        own_grad_normed
    )
    image_index = jnp.arange(images_here, dtype=jnp.int32)[:, None]
    grad_stream = (
        jnp.zeros(stream.shape, single)
        .at[image_index, row_index]
        .add(grad_chosen.reshape(images_here, 17, D))
    )

    grad_stream = grad_stream.reshape(images_here * PAD_SEQ, D)
    middle_row = block_rows // 2
    vector_grads = [None] * LAYERS

    def halves(array):
        middle = array.shape[-2] // 2
        return [array[..., :middle, :], array[..., middle:, :]]

    def cuts(parts, names, order):
        return [cut(part, name, axis, 1) for part, name, axis in zip(parts, names, order)]

    def moves(pieces, order):
        return [move(sent, kept, axis) for (sent, kept, left), axis in zip(pieces, order)]

    def over_core(weight_grad, rows):
        pairs_of = weight_grad.reshape(D // 128, -1, 2, rows, 128)
        return move(*cut(pairs_of, "pc", "c", 1)[:2], "c")

    def core_cut(weight_grad, rows):
        return cut(weight_grad.reshape(D // 128, -1, 2, rows, 128), "pc", "c", 1)[:2]

    def start(late, early, *others):
        shared_pair = 4 * D // (2 * block_rows)
        whole = jnp.concatenate(
            [
                early[:, :shared_pair],
                early[:, shared_pair:] + late[:, : early.shape[1] - shared_pair],
                late[:, early.shape[1] - shared_pair :],
            ],
            axis=1,
        )
        parts = [jnp.concatenate(pieces, axis=2) for pieces in zip(*[halves(array) for array in (whole, *others)])]
        by_bits = [part.reshape((D // 128, 2, 2, 2, 2) + part.shape[2:]) for part in parts]
        return (cuts(by_bits, ["bayx"] * 2, rounds[0]), 0)

    rounds = (("x", "b"), ("y", "a"), ("b", "x"), ("a", "y"))

    def advance(state):
        pieces, stage = state
        parts = moves(pieces, rounds[stage])
        names = [left for sent, kept, left in pieces]
        return cuts(parts, names, rounds[stage + 1]), stage + 1

    def finish(state):
        while state[1] < len(rounds) - 1:
            state = advance(state)
        return moves(state[0], rounds[-1])

    def sends(states):
        return tuple(sent for pieces, stage in states for sent, kept, left in pieces)

    def block_place(i):
        column = max(bounds[i], 0) // 128 * 128
        grad_column = 0 if i < first_w2 else HID
        return [column, bounds[i] - column if i else 0, sizes[i] if i else 0, grad_column]

    def third_place(i):
        return [0, 0, sizes[i], 0]

    place = per_device(
        [
            (third_place(i) if i >= first_w3 else block_place(i))
            + block_place(i ^ across)
            + [int(i >= first_w3), D + HID + max(bounds[i] - D - HID, 0) * (ROW // BOT)]
            for i in range(count)
        ]
    )
    started = []
    held_block = None
    waits = ()
    for layer_index in reversed(range(LAYERS)):
        saved, vectors = saved_layers[layer_index], vectors_all[1, layer_index]
        part = LAYERS + layer_index
        grad_stream, late_grad, late_vectors, *held_block = mlp_back(
            side,
            grad_stream,
            saved,
            vectors,
            gathered,
            part,
            waits + sends(started),
            [partner_block_grad] if started else [],
        )
        late = over_core(late_grad, block_rows)
        started = [advance(state) for state in started]
        if started:
            block_got = lax.ppermute(held_block[0], "dev", [(i, i ^ across) for i in range(half, count)])
        grad_stream, early_grad, early_vectors, *held_block = attention_back(
            side,
            grad_stream,
            saved,
            vectors,
            gathered,
            part,
            sends(started),
            [own_block_grad] if started else [],
        )
        vector_grads[layer_index] = (late_vectors + early_vectors)[:6]
        if layer_index == LAYERS - 1:
            sent, stay = core_cut(early_grad, block_rows)
            own_block_grad, partner_block_grad, stay = head_grads(
                place, inputs_all, grads_all, slot, -min(bounds[1], 0), (early_vectors,), [stay]
            )
            waits = (own_block_grad,)
        started = [advance(state) for state in started]
        if layer_index > 0:
            started.append(start(late, move(sent, stay, "c")))
    own_block_grad = held_block[0]
    rows = grads_all.reshape(half, pair_rows, width)[:, 2 * rows_here : 2 * rows_here + carried_rows]
    rows = rows.reshape(half, -1)[:, : 3 * carried_size].reshape(half, 3, carried_size).astype(single)
    rows = rows[:, 0] + rows[:, 1] + rows[:, 2]
    half_centre = rows[:, :protos_here].reshape(-1)
    half_sums = jnp.sum(rows[:, protos_here:], axis=0)
    other = lax.ppermute(jnp.concatenate([half_centre, half_sums]), "dev", pairs(count, across))
    other_centre, other_sums = other[: half * protos_here], other[half * protos_here :]
    new_centre = jnp.where(
        student_side,
        jnp.concatenate([other_centre, half_centre]),
        jnp.concatenate([half_centre, other_centre]),
    )
    sums = (half_sums + other_sums).reshape(3, all_rows)
    cross = jnp.log(sums[1]) - sums[2] / (sums[0] * tau_student)
    loss_total = jnp.sum(row_weight * cross)
    student_scale, teacher_scale = scale / sums[1], scale / sums[0]
    head_block_grad = jnp.where(student_side, own_block_grad, block_got.astype(single))
    early = over_core(early_grad, block_rows)
    small_rows = -(-(EMBED_ROWS + 6 * LAYERS) // (16 * count)) * 16
    small = embed_back(
        grad_stream,
        patches.reshape(images_here * PATCHES, PIX),
        jnp.where(masked_here, 0.0, 1.0).reshape(images_here * PATCHES, 1),
        jnp.stack([grad_gain, grad_bias]),
        jnp.concatenate(vector_grads),
        small_rows * count,
        (),
    )
    started.append(start(late, early, over_core(small, small_rows)))
    last_rows = lax.dynamic_slice(
        head_block_grad, (jnp.array(sizes, jnp.int32)[me] - GROUP, 0), (GROUP, ROW)
    )
    previous = lax.ppermute(last_rows, "dev", step_pairs(count, 1))
    proto_grad, proto_square, *held = proto_grad_pass(
        teacher_z_all,
        student_z_all,
        proto_teacher,
        protos,
        centre_column,
        lines(student_scale, teacher_scale),
        [stay for pieces, stage in started for sent, stay, left in pieces],
    )
    held = iter(held)
    started = [([(sent, next(held), left) for sent, _, left in pieces], stage) for pieces, stage in started]
    blocks = [finish(state) for state in started][::-1]
    middle_row = block_rows // 2
    layer_block = jnp.stack([jnp.concatenate([part[:, :middle_row] for part in parts], axis=1) for parts in blocks])
    small_block = jnp.concatenate([part[:, middle_row:] for part in blocks[0]], axis=1)

    square_local = (
        jnp.sum(head_block_grad * head_block_grad)
        + jnp.sum(layer_block * layer_block)
        + jnp.sum(small_block * small_block)
        + proto_square[0, 0]
    )
    high = square_local.astype(narrow)
    middle = (square_local - high.astype(single)).astype(narrow)
    low = (square_local - high.astype(single) - middle.astype(single)).astype(narrow)
    tile = jnp.pad(jnp.stack([high, middle, low]).reshape(1, 1, 3), ((0, 0), (0, 15), (0, 125)))
    first_rows = small_block[:2].astype(narrow)
    other_rows = jnp.concatenate([small_block[2:].astype(narrow), tile], axis=1)
    first_rows = cube_gather(first_rows, "xya")
    other_rows = cube_gather(other_rows, "abx")
    behind = lax.ppermute(layer_block[:, :, :6], "dev", step_pairs(count, -1))
    place = per_device([spots(head_span - starts[i], drift * i) for i in range(count)])
    stem_lines, layer_lines, first_rows, other_rows = own_shards(
        place, head_block_grad, previous, layer_block, behind, lane_rows(stem_piece), lane_rows(layer_piece),
        [first_rows, other_rows],
    )
    first_rows = jnp.moveaxis(cube_gather(first_rows, "bc").reshape((2, 2, 8) + first_rows.shape[1:]), 0, 2)
    other_rows = cube_gather(other_rows, "yc")
    other_rows = other_rows.reshape((2,) * 5 + other_rows.shape[2:])
    other_rows = jnp.transpose(other_rows, (3, 4, 1, 2, 0, 5, 6, 7))
    first_rows = first_rows.reshape((count,) + first_rows.shape[3:])
    other_rows = other_rows.reshape((count,) + other_rows.shape[5:])
    square_total = jnp.sum(other_rows[:, 0, small_rows, :3].astype(single))
    small_all = jnp.concatenate([first_rows, other_rows[:, :, :small_rows]], axis=1).astype(single)
    small_all = jnp.transpose(small_all, (0, 2, 1, 3)).reshape(small_rows * count, D)
    embed_grad = small_all[:EMBED_ROWS].reshape(-1)
    vector_grad = small_all[EMBED_ROWS : EMBED_ROWS + 6 * LAYERS].reshape(LAYERS, 6 * D)
    layer_grad = layer_lines.reshape(LAYERS, -1)[:, :layer_piece]
    layer_grad = jnp.concatenate(
        [
            layer_grad[:, : layer_piece - tail],
            jnp.where(me == count - 1, vector_grad, layer_grad[:, layer_piece - tail :]),
        ],
        axis=1,
    )
    stem_grad = stem_lines.reshape(-1)[:stem_piece]
    rest = EMBED_FLAT - stem_piece
    second_part = jnp.concatenate([embed_grad[stem_piece:], stem_grad[rest:]])
    stem_grad = jnp.where(
        me == 0, embed_grad[:stem_piece], jnp.where(me == 1, second_part, stem_grad)
    )

    grad_norm = jnp.sqrt(square_total) / count_total
    factor = jnp.minimum(1.0, clip_limit / (grad_norm + 1e-06)) / count_total
    stem_set = adam_update(stem, stem_moment, stem_second, stem_grad * factor, stem_teacher)
    layer_set = adam_update(layers, layer_moment, layer_second, layer_grad * factor, layer_teacher)
    proto_set = proto_update(factor, protos, proto_moment, proto_second, proto_teacher, proto_grad)
    return (loss_total, count_total, grad_norm, new_centre) + stem_set + layer_set + tuple(proto_set)


def solution(mesh):
    count = mesh.shape["dev"]
    stem_length = -(-(EMBED_FLAT + HEAD_ROWS * ROW) // count) * count
    close = fits(count, stem_length // count, (MATRIX_ROWS + 6) * D // count)
    placed = (
        P("dev", None, None),
        P("dev", None),
        P("dev"),
        P("dev"),
        P("dev"),
        P("dev"),
        P("dev"),
        P(None, "dev"),
        P(None, "dev"),
        P(None, "dev"),
        P(None, "dev"),
        P("dev", None),
        P("dev", None),
        P("dev", None),
        P("dev", None),
        P(),
    )
    return jax.shard_map(
        close_local if close else spread_local,
        mesh=mesh,
        in_specs=placed,
        out_specs=(
            P(),
            P(),
            P(),
            P(),
            P("dev"),
            P("dev"),
            P("dev"),
            P("dev"),
            P("dev"),
            P(None, "dev"),
            P(None, "dev"),
            P(None, "dev"),
            P(None, "dev"),
            P(None, "dev"),
            P("dev", None),
            P("dev", None),
            P("dev", None),
            P("dev", None),
            P("dev", None),
        ),
        check_vma=False,
    )
```

```python
import jax
import jax.numpy as jnp
from jax import lax
from jax.experimental import pallas as pl
from jax.experimental.pallas import tpu as pltpu
from jax.sharding import PartitionSpec as P

D = 384
HEADS = 6
HEAD_DIM = 64
FF = 1536
HID = 2048
BOT = 256
PIX = 588
PATCHES = 256
LAYERS = 2
STEP = 10
SEQ = 257


tau_student = 0.1
tau_teacher = 0.04
clip_limit = 0.003
learn_rate = 0.03
beta_one = 0.9
beta_two = 0.999
adam_eps = 1e-08
decay_rate = 0.04
teacher_keep = 0.8
centre_keep = 0.9
narrow = jnp.bfloat16
single = jnp.float32


def layer_shapes():
    return ((D, 3 * D), (D, D), (D, FF), (FF, D), (6, D))


def stem_shapes():
    return ((PIX, D), (SEQ, D), (4, D), (D, HID), (HID, HID), (HID, BOT))


def cut_flat(flat_row, shape_list):
    pieces = []
    offset = 0
    for shape_pair in shape_list:
        length = shape_pair[0] * shape_pair[1]
        pieces.append(flat_row[offset : offset + length].reshape(shape_pair))
        offset = offset + length
    return pieces


def pack_flat(grad_list, total_length):
    joined = jnp.concatenate([grad_item.reshape(-1) for grad_item in grad_list])
    return jnp.concatenate([joined, jnp.zeros((total_length - joined.shape[0],), single)])


def contract(form, left_arg, right_arg):
    return jnp.einsum(form, left_arg, right_arg, preferred_element_type=single)


def layer_norm(values, gain_row, bias_row):
    centred = values - jnp.mean(values, axis=-1, keepdims=True)
    spread = jnp.mean(centred * centred, axis=-1, keepdims=True)
    return centred * lax.rsqrt(spread + 1e-06) * gain_row + bias_row


def unit_rows(values):
    return values * lax.rsqrt(jnp.sum(values * values, axis=-1, keepdims=True) + 1e-06)


def gelu_back(pre_act, grad_act):
    return jax.vjp(jax.nn.gelu, pre_act)[1](grad_act)[0]


def block_forward(stream, weights):
    w_qkv, w_proj, w_up, w_down, vectors = weights
    vectors = vectors.astype(single)
    batch_size = stream.shape[0]
    normed = layer_norm(stream, vectors[0], vectors[1]).astype(narrow)
    packed = (
        contract("bsd,de->bse", normed, w_qkv)
        .astype(narrow)
        .reshape(batch_size, SEQ, 3, HEADS, HEAD_DIM)
    )
    scores = contract("bqhe,bkhe->bhqk", packed[:, :, 0], packed[:, :, 1]) * HEAD_DIM ** (-0.5)
    top_score = jnp.max(scores, axis=-1, keepdims=True)
    exp_terms = jnp.exp(scores - top_score)
    totals = jnp.sum(exp_terms, axis=-1, keepdims=True)
    log_total = top_score + jnp.log(totals)
    mixed = contract("bhqk,bkhe->bqhe", (exp_terms / totals).astype(narrow), packed[:, :, 2])
    mixed = mixed.astype(narrow).reshape(batch_size, SEQ, D)
    attn_out = contract("bsd,de->bse", mixed, w_proj)
    middle = stream + vectors[2] * attn_out
    normed_two = layer_norm(middle, vectors[3], vectors[4]).astype(narrow)
    pre_act = contract("bsd,df->bsf", normed_two, w_up)
    hidden = jax.nn.gelu(pre_act).astype(narrow)
    mlp_out = contract("bsf,fd->bsd", hidden, w_down)
    saved = (
        stream,
        normed,
        packed,
        log_total,
        mixed,
        attn_out,
        middle,
        normed_two,
        pre_act,
        hidden,
        mlp_out,
    )
    return (middle + vectors[5] * mlp_out, saved)


def block_backward(grad_out, weights, saved):
    w_qkv, w_proj, w_up, w_down, vectors = weights
    vectors = vectors.astype(single)
    (
        stream,
        normed,
        packed,
        log_total,
        mixed,
        attn_out,
        middle,
        normed_two,
        pre_act,
        hidden,
        mlp_out,
    ) = saved
    batch_size = stream.shape[0]
    score_scale = HEAD_DIM ** (-0.5)
    grad_ls_two = jnp.sum(grad_out * mlp_out, axis=(0, 1))
    grad_mlp = (grad_out * vectors[5]).astype(narrow)
    grad_down = contract("bsf,bsd->fd", hidden, grad_mlp)
    grad_pre = gelu_back(pre_act, contract("bsd,fd->bsf", grad_mlp, w_down)).astype(narrow)
    grad_up = contract("bsd,bsf->df", normed_two, grad_pre)
    grad_normed_two = contract("bsf,df->bsd", grad_pre, w_up)
    grad_mid, grad_gain_two, grad_bias_two = jax.vjp(layer_norm, middle, vectors[3], vectors[4])[1](
        grad_normed_two
    )
    grad_mid = grad_mid + grad_out
    grad_ls_one = jnp.sum(grad_mid * attn_out, axis=(0, 1))
    grad_attn = (grad_mid * vectors[2]).astype(narrow)
    grad_proj = contract("bsd,bse->de", mixed, grad_attn)
    grad_mixed = (
        contract("bse,de->bsd", grad_attn, w_proj)
        .astype(narrow)
        .reshape(batch_size, SEQ, HEADS, HEAD_DIM)
    )
    query_rows = packed[:, :, 0]
    key_rows = packed[:, :, 1]
    value_rows = packed[:, :, 2]
    probs = jnp.exp(contract("bqhe,bkhe->bhqk", query_rows, key_rows) * score_scale - log_total)
    grad_probs = contract("bqhe,bkhe->bhqk", grad_mixed, value_rows)
    grad_values = contract("bhqk,bqhe->bkhe", probs.astype(narrow), grad_mixed)
    grad_scores = probs * (grad_probs - jnp.sum(probs * grad_probs, axis=-1, keepdims=True))
    grad_raw = (grad_scores * score_scale).astype(narrow)
    grad_queries = contract("bhqk,bkhe->bqhe", grad_raw, key_rows)
    grad_keys = contract("bhqk,bqhe->bkhe", grad_raw, query_rows)
    grad_packed = (
        jnp.stack([grad_queries, grad_keys, grad_values], axis=2)
        .astype(narrow)
        .reshape(batch_size, SEQ, 3 * D)
    )
    grad_qkv = contract("bsd,bse->de", normed, grad_packed)
    grad_normed = contract("bse,de->bsd", grad_packed, w_qkv)
    grad_in, grad_gain_one, grad_bias_one = jax.vjp(layer_norm, stream, vectors[0], vectors[1])[1](
        grad_normed
    )
    grad_vectors = jnp.stack(
        [grad_gain_one, grad_bias_one, grad_ls_one, grad_gain_two, grad_bias_two, grad_ls_two]
    )
    return (grad_in + grad_mid, (grad_qkv, grad_proj, grad_up, grad_down, grad_vectors))


def embed(stem_parts, image_rows, masked_here, student):
    patch_w, position, extras, w_first, w_second, w_third = stem_parts
    extras = extras.astype(single)
    embedded = contract("gpc,cd->gpd", image_rows, patch_w)
    if student:
        embedded = jnp.where(masked_here[:, :, None], extras[1], embedded)
    cls_rows = jnp.broadcast_to(extras[0], (image_rows.shape[0], 1, D))
    return jnp.concatenate([cls_rows, embedded], axis=1) + position.astype(single)


def embed_backward(grad_stream, image_rows, masked_here):
    grad_cls = jnp.sum(grad_stream[:, 0], axis=0)
    grad_position = jnp.sum(grad_stream, axis=0)
    grad_patch_rows = grad_stream[:, 1:]
    grad_mask_token = jnp.sum(jnp.where(masked_here[:, :, None], grad_patch_rows, 0.0), axis=(0, 1))
    grad_embedded = jnp.where(masked_here[:, :, None], 0.0, grad_patch_rows).astype(narrow)
    grad_patch_w = contract("gpc,gpd->cd", image_rows, grad_embedded)
    return (grad_patch_w, grad_position, grad_cls, grad_mask_token)


def head_forward(stem_parts, proto_rows, stream, row_index):
    patch_w, position, extras, w_first, w_second, w_third = stem_parts
    extras = extras.astype(single)
    chosen = jnp.take_along_axis(stream, row_index[:, :, None], axis=1)
    normed = layer_norm(chosen, extras[2], extras[3]).astype(narrow)
    pre_one = contract("grd,dh->grh", normed, w_first)
    hidden_one = jax.nn.gelu(pre_one).astype(narrow)
    pre_two = contract("grh,hk->grk", hidden_one, w_second)
    hidden_two = jax.nn.gelu(pre_two).astype(narrow)
    bottleneck = contract("grh,hb->grb", hidden_two, w_third)
    unit_z = unit_rows(bottleneck).astype(narrow)
    unit_protos = unit_rows(proto_rows.astype(single)).astype(narrow)
    logits = contract("grb,kb->grk", unit_z, unit_protos)
    return (
        logits,
        (chosen, normed, pre_one, hidden_one, pre_two, hidden_two, bottleneck, unit_z, unit_protos),
    )


def head_backward(grad_logits, stem_parts, saved, row_index, stream_shape):
    patch_w, position, extras, w_first, w_second, w_third = stem_parts
    extras = extras.astype(single)
    chosen, normed, pre_one, hidden_one, pre_two, hidden_two, bottleneck, unit_z, unit_protos = (
        saved
    )
    grad_rounded = grad_logits.astype(narrow)
    grad_unit_z = contract("grk,kb->grb", grad_rounded, unit_protos)
    grad_unit_protos = contract("grk,grb->kb", grad_rounded, unit_z)
    grad_bottle = jax.vjp(unit_rows, bottleneck)[1](grad_unit_z)[0].astype(narrow)
    grad_third = contract("grh,grb->hb", hidden_two, grad_bottle)
    grad_pre_two = gelu_back(pre_two, contract("grb,hb->grh", grad_bottle, w_third)).astype(narrow)
    grad_second = contract("grh,grk->hk", hidden_one, grad_pre_two)
    grad_pre_one = gelu_back(pre_one, contract("grk,hk->grh", grad_pre_two, w_second)).astype(
        narrow
    )
    grad_first = contract("grd,grh->dh", normed, grad_pre_one)
    grad_normed = contract("grh,dh->grd", grad_pre_one, w_first)
    grad_chosen, grad_gain, grad_bias = jax.vjp(layer_norm, chosen, extras[2], extras[3])[1](
        grad_normed
    )
    image_index = jnp.arange(row_index.shape[0], dtype=jnp.int32)[:, None]
    grad_stream = jnp.zeros(stream_shape, single).at[image_index, row_index].add(grad_chosen)
    return (
        grad_stream,
        (grad_first, grad_second, grad_third),
        grad_gain,
        grad_bias,
        grad_unit_protos,
    )


def adam_update(weight, moment, second, grad, teacher):
    new_moment = beta_one * moment + (1.0 - beta_one) * grad
    new_second = beta_two * second + (1.0 - beta_two) * grad * grad
    direction = (
        new_moment
        / (1.0 - beta_one**STEP)
        / (jnp.sqrt(new_second / (1.0 - beta_two**STEP)) + adam_eps)
    )
    new_weight = weight - learn_rate * (direction + decay_rate * weight)
    return (
        new_moment,
        new_second,
        new_weight,
        new_weight.astype(narrow),
        teacher_keep * teacher + (1.0 - teacher_keep) * new_weight,
    )


def spread_local(
    patches,
    masked,
    slot_used,
    stem,
    stem_moment,
    stem_second,
    stem_teacher,
    layers,
    layer_moment,
    layer_second,
    layer_teacher,
    protos,
    proto_moment,
    proto_second,
    proto_teacher,
    centre,
):
    images_here = patches.shape[0]
    row_index = jnp.concatenate([jnp.zeros((images_here, 1), jnp.int32), masked + 1], axis=1)
    masked_here = jnp.any(
        masked[:, :, None] == jnp.arange(PATCHES, dtype=jnp.int32)[None, None, :], axis=1
    )
    kept = slot_used.astype(single)
    teacher_flat, teacher_protos = (
        lax.all_gather(stem_teacher.astype(narrow), "dev", axis=0, tiled=True),
        lax.all_gather(proto_teacher.astype(narrow), "dev", axis=0, tiled=True),
    )
    teacher_parts = cut_flat(teacher_flat, stem_shapes())
    stream = embed(teacher_parts, patches, masked_here, False)
    for layer_index in range(LAYERS):
        teacher_layer = lax.all_gather(
            layer_teacher[layer_index].astype(narrow), "dev", axis=0, tiled=True
        )
        stream = block_forward(stream, cut_flat(teacher_layer, layer_shapes()))[0]
    teacher_logits = head_forward(teacher_parts, teacher_protos, stream, row_index)[0]
    teacher_probs = jax.nn.softmax((teacher_logits - centre) / tau_teacher, axis=-1)
    centre_terms = jnp.sum(kept[:, None] * teacher_logits[:, 0], axis=0)
    student_flat, student_protos = (
        lax.all_gather(stem.astype(narrow), "dev", axis=0, tiled=True),
        lax.all_gather(protos.astype(narrow), "dev", axis=0, tiled=True),
    )
    student_parts = cut_flat(student_flat, stem_shapes())
    stream = embed(student_parts, patches, masked_here, True)
    saved_layers = []
    gathered_layers = []
    for layer_index in range(LAYERS):
        layer_flat = lax.all_gather(layers[layer_index].astype(narrow), "dev", axis=0, tiled=True)
        gathered_layers.append(layer_flat)
        stream, saved = block_forward(stream, cut_flat(layer_flat, layer_shapes()))
        saved_layers.append(saved)
    logits, head_saved = head_forward(student_parts, student_protos, stream, row_index)

    def loss_piece(logit_rows):
        log_probs = jax.nn.log_softmax(logit_rows / tau_student, axis=-1)
        cross = -jnp.sum(teacher_probs * log_probs, axis=-1)
        return jnp.sum(kept * (cross[:, 0] + jnp.mean(cross[:, 1:], axis=1)))

    loss_local, loss_puller = jax.vjp(loss_piece, logits)
    grad_logits = loss_puller(jnp.float32(1.0))[0]
    count_local = jnp.sum(kept)
    loss_total, count_total, centre_total = lax.psum((loss_local, count_local, centre_terms), "dev")
    back_flat, back_protos = (
        lax.all_gather(stem.astype(narrow), "dev", axis=0, tiled=True),
        lax.all_gather(protos.astype(narrow), "dev", axis=0, tiled=True),
    )
    back_parts = cut_flat(back_flat, stem_shapes())
    grad_stream, head_grads, grad_gain, grad_bias, grad_unit_protos = head_backward(
        grad_logits, back_parts, head_saved, row_index, stream.shape
    )
    layer_grads = []
    for layer_index in reversed(range(LAYERS)):
        weight_flat = lax.all_gather(layers[layer_index].astype(narrow), "dev", axis=0, tiled=True)
        grad_stream, block_grads = block_backward(
            grad_stream, cut_flat(weight_flat, layer_shapes()), saved_layers[layer_index]
        )
        layer_grads.insert(
            0,
            lax.psum_scatter(
                pack_flat(block_grads, weight_flat.shape[0]), "dev", scatter_dimension=0, tiled=True
            ),
        )
    grad_patch_w, grad_position, grad_cls, grad_mask_token = embed_backward(
        grad_stream, patches, masked_here
    )
    grad_extras = jnp.stack([grad_cls, grad_mask_token, grad_gain, grad_bias])
    stem_flat_grad = pack_flat(
        (grad_patch_w, grad_position, grad_extras) + head_grads, back_flat.shape[0]
    )
    stem_grad, proto_row_grad = (
        lax.psum_scatter(stem_flat_grad, "dev", scatter_dimension=0, tiled=True),
        lax.psum_scatter(grad_unit_protos, "dev", scatter_dimension=0, tiled=True),
    )
    own_protos = lax.optimization_barrier(protos.astype(narrow)).astype(single)
    proto_grad = jax.vjp(unit_rows, own_protos)[1](proto_row_grad)[0]
    layer_grad = jnp.stack(layer_grads)
    square_local = (
        jnp.sum(stem_grad * stem_grad)
        + jnp.sum(layer_grad * layer_grad)
        + jnp.sum(proto_grad * proto_grad)
    )
    square_total = lax.psum(square_local, "dev")
    grad_norm = jnp.sqrt(square_total) / count_total
    factor = jnp.minimum(1.0, clip_limit / (grad_norm + 1e-06)) / count_total
    new_centre = centre_keep * centre + (1.0 - centre_keep) * centre_total / count_total
    stem_set = adam_update(stem, stem_moment, stem_second, stem_grad * factor, stem_teacher)
    layer_set = adam_update(layers, layer_moment, layer_second, layer_grad * factor, layer_teacher)
    proto_set = adam_update(protos, proto_moment, proto_second, proto_grad * factor, proto_teacher)
    return (
        loss_total,
        count_total,
        grad_norm,
        new_centre,
        stem_set[0],
        stem_set[1],
        stem_set[2],
        stem_set[3],
        stem_set[4],
        layer_set[0],
        layer_set[1],
        layer_set[2],
        layer_set[3],
        layer_set[4],
        proto_set[0],
        proto_set[1],
        proto_set[2],
        proto_set[3],
        proto_set[4],
    )


GROUP = 16
ROW = HID
MATRIX_ROWS = D * 3 + D + FF + FF
EMBED_ROWS = PIX + SEQ + 4
EMBED_FLAT = EMBED_ROWS * D
HEAD_ROWS = D + HID + BOT
BITS = ("b", "a", "y", "x", "c")
MASKS = {"c": 1, "x": 2, "y": 4, "a": 8, "b": 24, "g": 8}


def head_bounds(count, stem_piece):
    bounds = [-(-(stem_piece * device - EMBED_FLAT) // (ROW * GROUP)) * GROUP for device in range(count + 1)]
    bounds[0] = -(-EMBED_FLAT // (ROW * GROUP)) * -GROUP
    bounds[-1] = HEAD_ROWS
    return bounds


def fits(count, stem_piece, layer_piece):
    if count != 1 << len(BITS) or MATRIX_ROWS % (3 * count):
        return False
    bounds = head_bounds(count, stem_piece)
    sizes = [bounds[i + 1] - bounds[i] for i in range(count)]
    return (
        min(sizes) > GROUP
        and bounds[1] <= 0
        and stem_piece < EMBED_FLAT <= 2 * stem_piece
        and D in bounds
        and D + HID in bounds
        and stem_piece * count == EMBED_FLAT + HEAD_ROWS * ROW
    )


def pairs(count, mask):
    return [(i, i ^ mask) for i in range(count)]


def bit_flags(me):
    flags = {name: (me >> (len(BITS) - 1 - place)) & 1 for place, name in enumerate(BITS)}
    flags["g"] = flags["a"] ^ flags["b"]
    return flags


def cube_gather(part, order):
    count = 1 << len(BITS)
    flags = bit_flags(lax.axis_index("dev"))
    held = part[None]
    for name in order:
        got = lax.ppermute(held, "dev", pairs(count, MASKS[name]))
        held = jnp.where(
            flags[name] == 1,
            jnp.concatenate([got, held], axis=0),
            jnp.concatenate([held, got], axis=0),
        )
    return held


def cut(array, names, name, lead):
    mine = bit_flags(lax.axis_index("dev"))[name]
    place = names.index(name) + lead
    sent = lax.dynamic_index_in_dim(array, 1 - mine, place, keepdims=False)
    kept = lax.dynamic_index_in_dim(array, mine, place, keepdims=False)
    return (sent if name == "c" else sent.astype(narrow)), kept, names.replace(name, "")


def move(sent, kept, name):
    return kept + lax.ppermute(sent, "dev", pairs(1 << len(BITS), MASKS[name])).astype(single)


def cube_scatter(array, names, order, lead=0):
    for name in order:
        sent, kept, names = cut(array, names, name, lead)
        array = move(sent, kept, name)
    return array


def cube_sum(values):
    for name in "cxyab":
        values = values + lax.ppermute(values, "dev", pairs(1 << len(BITS), MASKS[name]))
    return values


def split_bits(array, lead=0):
    return array.reshape(array.shape[:lead] + (2,) * len(BITS) + array.shape[lead + 1 :])


def step_pairs(count, step):
    return [(i, i + step) for i in range(count) if 0 <= i + step < count]


def lane_rows(length):
    return -(-length // 1024) * 8


def as_lanes(flat):
    rows = lane_rows(flat.shape[-1])
    gap = rows * 128 - flat.shape[-1]
    padded = jnp.pad(flat, [(0, 0)] * (flat.ndim - 1) + [(0, gap)])
    return padded.reshape(flat.shape[:-1] + (rows, 128))


def shifted(line_ref, row, lane, first, rows, stride):
    spots = lax.broadcasted_iota(jnp.int32, (rows, 128), 1)
    turn = lax.rem(128 - lane, 128)
    here = pltpu.roll(line_ref[pl.ds(row + first, rows, stride=stride), :], turn, 1)
    there = pltpu.roll(line_ref[pl.ds(row + first + 1, rows, stride=stride), :], turn, 1)
    return jnp.where(spots < 128 - lane, here, there)


def blocks_kernel(
    shape,
    place_ref,
    stem_ref,
    after_ref,
    layer_ref,
    before_ref,
    last_ref,
    head_ref,
    block_ref,
    embed_ref,
    vector_ref,
    line_ref,
    flat_ref,
):
    front, stem_piece, layer_piece, tail = shape
    stem_lines = stem_ref.shape[1]
    end_row, end_lane = stem_piece // 128, stem_piece % 128
    after_lines = after_ref.shape[1]
    slot = head_ref.shape[1]
    for model in range(2):
        line_ref[pl.ds(0, front), :] = jnp.zeros((front, 128), single)
        line_ref[pl.ds(front, end_row), :] = stem_ref[model, pl.ds(0, end_row), :]
        turned = pltpu.roll(after_ref[model], end_lane, 1)
        spots = lax.broadcasted_iota(jnp.int32, (after_lines, 128), 1)
        line_ref[pl.ds(front + end_row, after_lines), :] = turned
        line_ref[pl.ds(front + end_row + after_lines, 128), :] = jnp.zeros((128, 128), single)
        lower = pltpu.roll(turned, 1, 0)
        first_line = jnp.broadcast_to(stem_ref[model, pl.ds(end_row, 1), :], (after_lines, 128))
        number = lax.broadcasted_iota(jnp.int32, (after_lines, 128), 0)
        lower = jnp.where(number == 0, first_line, lower)
        line_ref[pl.ds(front + end_row, after_lines), :] = jnp.where(spots < end_lane, lower, turned)
        per_row = ROW // 128
        for chunk in range(per_row):
            head_ref[model, :, pl.ds(chunk * 128, 128)] = shifted(
                line_ref, place_ref[0], place_ref[1], chunk, slot, per_row
            ).astype(narrow)
        for chunk in range(D // 128):
            embed_ref[model, :, pl.ds(chunk * 128, 128)] = shifted(
                line_ref, place_ref[2], place_ref[3], chunk, embed_ref.shape[1], D // 128
            ).astype(narrow)
    tail_lines = tail // 128
    layer_lines = layer_ref.shape[1]
    for part in range(layer_ref.shape[0]):
        flat_ref[pl.ds(0, tail_lines), :] = before_ref[part]
        flat_ref[pl.ds(tail_lines, layer_lines), :] = layer_ref[part]
        for chunk in range(D // 128):
            block_ref[part, :, pl.ds(chunk * 128, 128)] = shifted(
                flat_ref, place_ref[4], place_ref[5], chunk, block_ref.shape[1], D // 128
            ).astype(narrow)
            vector_ref[part, :, pl.ds(chunk * 128, 128)] = last_ref[
                part, pl.ds(chunk, 8, stride=D // 128), :
            ].astype(narrow)


def own_blocks(place, stems, after, layer_rows, before, last_lines, shape, slot, block_rows, embed_rows):
    front, stem_piece, layer_piece, tail = shape
    lines = front + stem_piece // 128 + after.shape[1] + slot * ROW // 128
    flats = tail // 128 + layer_rows.shape[1] + 48
    return pl.pallas_call(
        lambda *refs: blocks_kernel(shape, *refs),
        out_shape=[
            jax.ShapeDtypeStruct((2, slot, ROW), narrow),
            jax.ShapeDtypeStruct((2 * LAYERS, block_rows, D), narrow),
            jax.ShapeDtypeStruct((2, embed_rows, D), narrow),
            jax.ShapeDtypeStruct((2 * LAYERS, 8, D), narrow),
        ],
        in_specs=[pl.BlockSpec(memory_space=pltpu.SMEM)] + [pl.BlockSpec(memory_space=pltpu.VMEM)] * 5,
        out_specs=[pl.BlockSpec(memory_space=pltpu.VMEM)] * 4,
        scratch_shapes=[pltpu.VMEM((lines, 128), single), pltpu.VMEM((flats, 128), single)],
        compiler_params=pltpu.CompilerParams(vmem_limit_bytes=40 << 20),
    )(place, stems, after, layer_rows, before, last_lines)


def shards_kernel(held, place_ref, head_ref, previous_ref, block_ref, behind_ref, *refs):
    stem_ref, layer_ref = refs[held : held + 2]
    line_ref, flat_ref = refs[-2:]
    per_row = ROW // 128
    extra = previous_ref.shape[0]
    slot = head_ref.shape[0]
    for chunk in range(per_row):
        spot = pl.ds(chunk * 128, 128)
        line_ref[pl.ds(chunk, extra, stride=per_row), :] = previous_ref[:, spot]
        line_ref[pl.ds(extra * per_row + chunk, slot, stride=per_row), :] = head_ref[:, spot]
    stem_ref[...] = shifted(line_ref, place_ref[0], place_ref[1], 0, stem_ref.shape[0], 1)
    per_row = D // 128
    rows = block_ref.shape[2]
    for part in range(block_ref.shape[0]):
        for chunk in range(per_row):
            flat_ref[pl.ds(chunk, rows, stride=per_row), :] = block_ref[part, chunk]
            flat_ref[pl.ds(rows * per_row + chunk, 6, stride=per_row), :] = behind_ref[part, chunk]
        layer_ref[part] = shifted(flat_ref, place_ref[2], place_ref[3], 0, layer_ref.shape[1], 1)


def own_shards(place, head_grad, previous, block_grad, behind, stem_lines, layer_lines, held):
    per_row = ROW // 128
    lines = (head_grad.shape[0] + previous.shape[0]) * per_row + 256
    flats = max(block_grad.shape[2] * 3 + 18, layer_lines + 18) + 16
    return pl.pallas_call(
        lambda *refs: shards_kernel(len(held), *refs),
        out_shape=[
            jax.ShapeDtypeStruct((stem_lines, 128), single),
            jax.ShapeDtypeStruct((block_grad.shape[0], layer_lines, 128), single),
        ]
        + [jax.ShapeDtypeStruct(array.shape, array.dtype) for array in held],
        in_specs=[pl.BlockSpec(memory_space=pltpu.SMEM)]
        + [pl.BlockSpec(memory_space=pltpu.VMEM)] * 4
        + [pl.BlockSpec(memory_space=pl.ANY)] * len(held),
        out_specs=[pl.BlockSpec(memory_space=pltpu.VMEM)] * 2 + [pl.BlockSpec(memory_space=pl.ANY)] * len(held),
        input_output_aliases={5 + number: 2 + number for number in range(len(held))},
        scratch_shapes=[pltpu.VMEM((lines, 128), single), pltpu.VMEM((flats, 128), single)],
        compiler_params=pltpu.CompilerParams(vmem_limit_bytes=40 << 20),
    )(place, head_grad, previous, block_grad, behind, *held)


PAD_SEQ = 272
GELU_SCALE = 0.7978845608028654
GELU_CUBE = 0.044715


def product_plain(left, right):
    return lax.dot_general(left, right, (((1,), (0,)), ((), ())), preferred_element_type=single)


def product_right(left, right):
    return lax.dot_general(left, right, (((1,), (1,)), ((), ())), preferred_element_type=single)


def product_left(left, right):
    return lax.dot_general(left, right, (((0,), (0,)), ((), ())), preferred_element_type=single)


def norm_parts(values):
    centred = values - jnp.mean(values, axis=-1, keepdims=True)
    spread = lax.rsqrt(jnp.mean(centred * centred, axis=-1, keepdims=True) + 1e-06)
    return centred * spread, spread


def norm_back(grad, unit, spread, gain):
    grad_unit = grad * gain
    mean_one = jnp.mean(grad_unit, axis=-1, keepdims=True)
    mean_two = jnp.mean(grad_unit * unit, axis=-1, keepdims=True)
    return spread * (grad_unit - mean_one - unit * mean_two)


def gelu_tanh(values):
    return jnp.tanh(GELU_SCALE * (values + GELU_CUBE * values * values * values))


def gelu_value(values):
    return 0.5 * values * (1.0 + gelu_tanh(values))


def gelu_slope(values):
    bent = gelu_tanh(values)
    return 0.5 * (1.0 + bent) + 0.5 * values * (1.0 - bent * bent) * GELU_SCALE * (
        1.0 + 3.0 * GELU_CUBE * values * values
    )


def head_copies(plan, side_ref, gathered_ref, one_ref, two_ref, lines_ref, sems):
    quarter = gathered_ref.shape[0] // 2
    shift = side_ref[0] * quarter
    targets = (one_ref, two_ref, lines_ref)
    copies = []
    for number, (at, owner, first, rows, target, row) in enumerate(plan):
        spot = at + shift if at < quarter else at - shift
        copies.append(
            pltpu.make_async_copy(
                gathered_ref.at[spot, owner, pl.ds(first, rows)],
                targets[target].at[pl.ds(row, rows)],
                sems.at[number],
            )
        )
    for copy in copies:
        copy.start()
    return [[copy for copy, item in zip(copies, plan) if item[4] == target] for target in range(3)]


def wait_all(copies):
    for copy in copies:
        copy.wait()


def spread_third(lines_ref, wide_ref, third_ref):
    groups = ROW // BOT
    for lane in range(BOT // 128):
        for group in range(groups):
            at = group * BOT + lane * 128
            wide_ref[lane, pl.ds(group, lines_ref.shape[0], stride=groups), :] = lines_ref[
                :, at : at + 128
            ].astype(single)
        third_ref[:, pl.ds(lane * 128, 128)] = wide_ref[lane].astype(narrow)


def head_up_kernel(
    plan, side_ref, normed_ref, gathered_ref, unit_ref, acts_ref, bottle_ref, pre_one_ref, pre_two_ref,
    one_ref, two_ref, lines_ref, wide_ref, third_ref, sems,
):
    copies = head_copies(plan, side_ref, gathered_ref, one_ref, two_ref, lines_ref, sems)
    acts_ref[...] = jnp.zeros_like(acts_ref)
    normed = normed_ref[...]
    acts_ref[:, pl.ds(0, D)] = normed
    piece = HID // 4
    wait_all(copies[0])
    for number in range(4):
        spot = pl.ds(number * piece, piece)
        pre = product_plain(normed, one_ref[:, spot])
        pre_one_ref[:, spot] = pre
        acts_ref[:, pl.ds(D + number * piece, piece)] = gelu_value(pre).astype(narrow)
    wait_all(copies[2])
    spread_third(lines_ref, wide_ref, third_ref)
    wait_all(copies[1])
    hidden = acts_ref[:, pl.ds(D, HID)]
    for number in range(4):
        spot = pl.ds(number * piece, piece)
        pre = product_plain(hidden, two_ref[:, spot])
        pre_two_ref[:, spot] = pre
        acts_ref[:, pl.ds(D + HID + number * piece, piece)] = gelu_value(pre).astype(narrow)
    bottle = product_plain(acts_ref[:, pl.ds(D + HID, HID)], third_ref[...])
    bottle_ref[...] = bottle
    unit_ref[...] = (
        bottle * lax.rsqrt(jnp.sum(bottle * bottle, axis=-1, keepdims=True) + 1e-06)
    ).astype(narrow)


def head_down_kernel(
    plan, side_ref, grad_ref, bottle_ref, pre_one_ref, pre_two_ref, gathered_ref, grads_ref, normed_grad_ref,
    one_ref, two_ref, lines_ref, wide_ref, third_ref, sems,
):
    copies = head_copies(plan, side_ref, gathered_ref, one_ref, two_ref, lines_ref, sems)
    grad, bottle = grad_ref[...], bottle_ref[...]
    scale = lax.rsqrt(jnp.sum(bottle * bottle, axis=-1, keepdims=True) + 1e-06)
    along = jnp.sum(grad * bottle, axis=-1, keepdims=True)
    grad_bottle = (scale * (grad - bottle * (along * scale * scale))).astype(narrow)
    grads_ref[:, pl.ds(2 * HID, BOT)] = grad_bottle
    wait_all(copies[2])
    spread_third(lines_ref, wide_ref, third_ref)
    piece = HID // 4
    for number in range(4):
        spot = pl.ds(number * piece, piece)
        back = product_right(grad_bottle, third_ref[spot, :])
        grads_ref[:, pl.ds(HID + number * piece, piece)] = (back * gelu_slope(pre_two_ref[:, spot])).astype(narrow)
    wait_all(copies[1])
    grad_two = grads_ref[:, pl.ds(HID, HID)]
    for number in range(4):
        spot = pl.ds(number * piece, piece)
        back = product_right(grad_two, two_ref[spot, :])
        grads_ref[:, spot] = (back * gelu_slope(pre_one_ref[:, spot])).astype(narrow)
    wait_all(copies[0])
    normed_grad_ref[...] = product_right(grads_ref[:, pl.ds(0, HID)], one_ref[...])


def head_pass(kernel, plan, side, inputs, gathered, shapes, waits=()):
    read = len(inputs) + 2
    return pl.pallas_call(
        lambda *refs: kernel(plan, *refs[:read], *refs[read + len(waits) :]),
        out_shape=shapes,
        in_specs=[pl.BlockSpec(memory_space=pltpu.SMEM)]
        + [pl.BlockSpec(memory_space=pltpu.VMEM)] * len(inputs)
        + [pl.BlockSpec(memory_space=pl.ANY)] * (1 + len(waits)),
        out_specs=[pl.BlockSpec(memory_space=pltpu.VMEM)] * len(shapes),
        scratch_shapes=[
            pltpu.VMEM((D, HID), narrow),
            pltpu.VMEM((HID, HID), narrow),
            pltpu.VMEM((BOT, ROW), narrow),
            pltpu.VMEM((BOT // 128, HID, 128), single),
            pltpu.VMEM((HID, BOT), narrow),
            pltpu.SemaphoreType.DMA((len(plan),)),
        ],
        compiler_params=pltpu.CompilerParams(vmem_limit_bytes=56 << 20),
        cost_estimate=pl.CostEstimate(flops=100 * 10**6, bytes_accessed=370 * 10**5, transcendentals=0),
    )(side, *inputs, gathered, *waits)


def fetch_rows(side_ref, part, gathered_ref, flat_ref, sems, first_row, last_row):
    quarter = flat_ref.shape[0] // 4
    side = side_ref[0]
    first, second = side * quarter, (1 - side) * quarter
    copies = [
        pltpu.make_async_copy(
            gathered_ref.at[pl.ds(at, quarter), owner, part],
            flat_ref.at[pl.ds(spot * quarter, quarter)],
            sems.at[spot],
        )
        for spot, (at, owner) in enumerate(((first, 0), (second, 0), (second, 1), (first, 1)))
        if spot * quarter * flat_ref.shape[1] < last_row and first_row < (spot + 1) * quarter * flat_ref.shape[1]
    ]
    for copy in copies:
        copy.start()
    return copies


def matrix_rows(flat_ref, first_row, length):
    rows = flat_ref.shape[1]
    low, high = first_row // rows, -(-(first_row + length) // rows)
    lines = flat_ref[pl.ds(low, high - low)].reshape((high - low) * rows, D)
    at = first_row - low * rows
    return lines[at : at + length]


def spread_columns(flat_ref, first_row, width, wide_ref, out_ref):
    length = width * D
    lines = matrix_rows(flat_ref, first_row, length)
    for column in range(D // 128):
        lane = slice(column * 128, (column + 1) * 128)
        wide_ref[column, pl.ds(0, length), :] = lines[:, lane].astype(single)
    for group in range(width):
        for column in range(D // 128):
            out_ref[group, :, pl.ds(column * 128, 128)] = wide_ref[
                column, pl.ds(group, D, stride=width), :
            ].astype(narrow)


def head_lanes(values, odd):
    lanes = lax.broadcasted_iota(jnp.int32, values.shape, 1)
    return jnp.where((lanes >= HEAD_DIM) == odd, values, jnp.zeros_like(values))


def join_lanes(even, odd):
    lanes = lax.broadcasted_iota(jnp.int32, even.shape, 1)
    return jnp.where(lanes >= HEAD_DIM, odd, even)


def soft_rows(query, key):
    scores = product_right(query, key) * HEAD_DIM ** (-0.5)
    spots = lax.broadcasted_iota(jnp.int32, scores.shape, 1)
    scores = jnp.where(spots < SEQ, scores, -1e30)
    terms = jnp.exp(scores - jnp.max(scores, axis=-1, keepdims=True))
    return terms / jnp.sum(terms, axis=-1, keepdims=True)


def forward_kernel(part, keep, side_ref, stream_ref, vector_ref, gathered_ref, *refs):
    out_ref = refs[0]
    if keep:
        packed_ref, mixed_ref, attn_ref, pre_ref, mlp_ref = refs[1:6]
        flat_ref, wide_ref, qkv_ref, up_ref, hidden_ref, sems = refs[6:]
    else:
        flat_ref, wide_ref, qkv_ref, up_ref, hidden_ref, packed_ref, mixed_ref, sems = refs[1:]
    copies = fetch_rows(side_ref, part, gathered_ref, flat_ref, sems, 0, MATRIX_ROWS)
    vectors = vector_ref[...].astype(single)
    stream = stream_ref[...]
    normed = (norm_parts(stream)[0] * vectors[0:1] + vectors[1:2]).astype(narrow)
    wait_all(copies)
    spread_columns(flat_ref, 0, 3, wide_ref, qkv_ref)
    spread_columns(flat_ref, 4 * D, FF // D, wide_ref, up_ref)
    w_proj = matrix_rows(flat_ref, 3 * D, D)
    w_down = matrix_rows(flat_ref, 4 * D + FF, FF)
    for group in range(3):
        packed_ref[:, pl.ds(group * D, D)] = product_plain(normed, qkv_ref[group]).astype(narrow)
    for image in range(stream.shape[0] // PAD_SEQ):
        rows = pl.ds(image * PAD_SEQ, PAD_SEQ)
        for pair in range(HEADS // 2):
            query, key, value = [
                packed_ref[rows, pl.ds(group * D + pair * 128, 128)] for group in range(3)
            ]
            done = [
                product_plain(soft_rows(head_lanes(query, odd), key).astype(narrow), value)
                for odd in (False, True)
            ]
            mixed_ref[rows, pl.ds(pair * 128, 128)] = join_lanes(*done).astype(narrow)
    attn = product_plain(mixed_ref[...], w_proj)
    middle = stream + vectors[2:3] * attn
    normed_two = (norm_parts(middle)[0] * vectors[3:4] + vectors[4:5]).astype(narrow)
    for group in range(FF // D):
        spot = pl.ds(group * D, D)
        pre = product_plain(normed_two, up_ref[group])
        if keep:
            pre_ref[:, spot] = pre
        hidden_ref[:, spot] = (0.5 * pre * (1.0 + gelu_tanh(pre))).astype(narrow)
    mlp = product_plain(hidden_ref[...], w_down)
    out_ref[...] = middle + vectors[5:6] * mlp
    if keep:
        attn_ref[...] = attn
        mlp_ref[...] = mlp


def layer_scratch(gathered):
    rows, blocks = gathered.shape[3], 2 * gathered.shape[0]
    return [
        pltpu.VMEM((blocks, rows, D), narrow),
        pltpu.VMEM((D // 128, FF, 128), single),
        pltpu.VMEM((3, D, D), narrow),
        pltpu.VMEM((FF // D, D, D), narrow),
    ]


def layer_specs_in(count):
    return (
        [pl.BlockSpec(memory_space=pltpu.SMEM)]
        + [pl.BlockSpec(memory_space=pltpu.VMEM)] * (count - 2)
        + [pl.BlockSpec(memory_space=pl.ANY)]
    )


def layer_forward(side, stream, vectors, gathered, part, keep):
    tokens = stream.shape[0]
    shapes = [jax.ShapeDtypeStruct((tokens, D), single)]
    extra = [
        jax.ShapeDtypeStruct((tokens, 3 * D), narrow),
        jax.ShapeDtypeStruct((tokens, D), narrow),
        jax.ShapeDtypeStruct((tokens, D), single),
        jax.ShapeDtypeStruct((tokens, FF), single),
        jax.ShapeDtypeStruct((tokens, D), single),
    ]
    scratch = layer_scratch(gathered) + [pltpu.VMEM((tokens, FF), narrow)]
    if keep:
        shapes = shapes + extra
    else:
        scratch = scratch + [pltpu.VMEM((tokens, 3 * D), narrow), pltpu.VMEM((tokens, D), narrow)]
    scratch.append(pltpu.SemaphoreType.DMA((4,)))
    return pl.pallas_call(
        lambda *refs: forward_kernel(part, keep, *refs),
        out_shape=shapes,
        in_specs=layer_specs_in(4),
        out_specs=[pl.BlockSpec(memory_space=pltpu.VMEM)] * len(shapes),
        scratch_shapes=scratch,
        compiler_params=pltpu.CompilerParams(vmem_limit_bytes=56 << 20),
        cost_estimate=pl.CostEstimate(flops=100 * 10**6, bytes_accessed=430 * 10**5, transcendentals=0),
    )(side, stream, vectors, gathered)


def mlp_back_kernel(
    part,
    side_ref,
    grad_ref,
    stream_ref,
    attn_ref,
    pre_ref,
    mlp_ref,
    vector_ref,
    gathered_ref,
    *refs,
):
    grad_mid_ref, weight_grad_ref, vector_grad_ref = refs[-9:-6]
    flat_ref, wide_ref, up_ref, hidden_ref, grad_pre_ref, sems = refs[-6:]
    lead = weight_grad_ref.shape[1] - 2 * FF
    weight_grad_ref[:, pl.ds(0, lead), :] = jnp.zeros((D // 128, lead, 128), single)
    copies = fetch_rows(side_ref, part, gathered_ref, flat_ref, sems, 4 * D, MATRIX_ROWS)
    vectors = vector_ref[...].astype(single)
    grad_out = grad_ref[...]
    vector_grad_ref[...] = jnp.zeros_like(vector_grad_ref)
    attn = attn_ref[...]
    middle = stream_ref[...] + vectors[2:3] * attn
    unit_two, spread_two = norm_parts(middle)
    normed_two = (unit_two * vectors[3:4] + vectors[4:5]).astype(narrow)
    vector_grad_ref[pl.ds(5, 1), :] = jnp.sum(grad_out * mlp_ref[...], axis=0, keepdims=True)
    grad_mlp = (grad_out * vectors[5:6]).astype(narrow)
    wait_all(copies)
    spread_columns(flat_ref, 4 * D, FF // D, wide_ref, up_ref)
    w_down = matrix_rows(flat_ref, 4 * D + FF, FF)
    grad_normed_two = jnp.zeros_like(grad_out)
    for group in range(FF // D):
        spot = pl.ds(group * D, D)
        pre = pre_ref[:, spot]
        bent = gelu_tanh(pre)
        hidden_ref[:, spot] = (0.5 * pre * (1.0 + bent)).astype(narrow)
        slope = 0.5 * (1.0 + bent) + 0.5 * pre * (1.0 - bent * bent) * GELU_SCALE * (
            1.0 + 3.0 * GELU_CUBE * pre * pre
        )
        grad_hidden = product_right(grad_mlp, w_down[group * D : (group + 1) * D])
        grad_pre = (grad_hidden * slope).astype(narrow)
        grad_pre_ref[:, spot] = grad_pre
        grad_normed_two = grad_normed_two + product_right(grad_pre, up_ref[group])
    for group in range(FF // D):
        spot = pl.ds(group * D, D)
        up_grad = product_left(normed_two, grad_pre_ref[:, spot])
        down_grad = product_left(hidden_ref[:, spot], grad_mlp)
        for column in range(D // 128):
            lane = slice(column * 128, (column + 1) * 128)
            weight_grad_ref[column, pl.ds(lead + group, D, stride=FF // D), :] = up_grad[:, lane]
            weight_grad_ref[column, pl.ds(lead + FF + group * D, D), :] = down_grad[:, lane]
    vector_grad_ref[pl.ds(3, 1), :] = jnp.sum(grad_normed_two * unit_two, axis=0, keepdims=True)
    vector_grad_ref[pl.ds(4, 1), :] = jnp.sum(grad_normed_two, axis=0, keepdims=True)
    grad_mid = grad_out + norm_back(grad_normed_two, unit_two, spread_two, vectors[3:4])
    vector_grad_ref[pl.ds(2, 1), :] = jnp.sum(grad_mid * attn, axis=0, keepdims=True)
    grad_mid_ref[...] = grad_mid


def attention_back_kernel(
    part,
    side_ref,
    grad_ref,
    stream_ref,
    packed_ref,
    mixed_ref,
    vector_ref,
    gathered_ref,
    *refs,
):
    grad_in_ref, weight_grad_ref, vector_grad_ref = refs[-9:-6]
    flat_ref, wide_ref, qkv_ref, grad_mixed_ref, grad_packed_ref, sems = refs[-6:]
    rest = weight_grad_ref.shape[1] - 4 * D
    weight_grad_ref[:, pl.ds(4 * D, rest), :] = jnp.zeros((D // 128, rest, 128), single)
    copies = fetch_rows(side_ref, part, gathered_ref, flat_ref, sems, 0, 4 * D)
    vectors = vector_ref[...].astype(single)
    vector_grad_ref[...] = jnp.zeros_like(vector_grad_ref)
    grad_mid = grad_ref[...]
    stream = stream_ref[...]
    grad_attn = (grad_mid * vectors[2:3]).astype(narrow)
    proj_grad = product_left(mixed_ref[...], grad_attn)
    for column in range(D // 128):
        weight_grad_ref[column, pl.ds(3 * D, D), :] = proj_grad[:, column * 128 : (column + 1) * 128]
    wait_all(copies)
    spread_columns(flat_ref, 0, 3, wide_ref, qkv_ref)
    w_proj = matrix_rows(flat_ref, 3 * D, D)
    grad_mixed_ref[...] = product_right(grad_attn, w_proj).astype(narrow)
    for image in range(stream.shape[0] // PAD_SEQ):
        rows = pl.ds(image * PAD_SEQ, PAD_SEQ)
        for pair in range(HEADS // 2):
            query, key, value = [
                packed_ref[rows, pl.ds(group * D + pair * 128, 128)] for group in range(3)
            ]
            grad_mixed = grad_mixed_ref[rows, pl.ds(pair * 128, 128)]
            parts = []
            for odd in (False, True):
                probs = soft_rows(head_lanes(query, odd), key)
                grad_probs = product_right(head_lanes(grad_mixed, odd), value)
                grad_value = product_left(probs.astype(narrow), grad_mixed)
                grad_scores = probs * (grad_probs - jnp.sum(probs * grad_probs, axis=-1, keepdims=True))
                grad_raw = (grad_scores * HEAD_DIM ** (-0.5)).astype(narrow)
                parts.append((product_plain(grad_raw, key), product_left(grad_raw, query), grad_value))
            for group in range(3):
                grad_packed_ref[rows, pl.ds(group * D + pair * 128, 128)] = join_lanes(
                    parts[0][group], parts[1][group]
                ).astype(narrow)
    unit_one, spread_one = norm_parts(stream)
    normed = (unit_one * vectors[0:1] + vectors[1:2]).astype(narrow)
    grad_normed = jnp.zeros_like(grad_mid)
    for group in range(3):
        grad_part = grad_packed_ref[:, pl.ds(group * D, D)]
        grad_normed = grad_normed + product_right(grad_part, qkv_ref[group])
        qkv_grad = product_left(normed, grad_part)
        for column in range(D // 128):
            lane = slice(column * 128, (column + 1) * 128)
            weight_grad_ref[column, pl.ds(group, D, stride=3), :] = qkv_grad[:, lane]
    vector_grad_ref[pl.ds(0, 1), :] = jnp.sum(grad_normed * unit_one, axis=0, keepdims=True)
    vector_grad_ref[pl.ds(1, 1), :] = jnp.sum(grad_normed, axis=0, keepdims=True)
    grad_in_ref[...] = grad_mid + norm_back(grad_normed, unit_one, spread_one, vectors[0:1])


def layer_back(kernel, part, weight_rows, side, inputs, vectors, gathered, waits, held, columns, buffers):
    tokens = inputs[0].shape[0]
    rows, blocks = gathered.shape[3], 2 * gathered.shape[0]
    return pl.pallas_call(
        lambda *refs: kernel(part, *refs[: len(refs) - 6 - len(held)], *refs[len(refs) - 6 :]),
        out_shape=[
            jax.ShapeDtypeStruct((tokens, D), single),
            jax.ShapeDtypeStruct((D // 128, weight_rows, 128), single),
            jax.ShapeDtypeStruct((8, D), single),
        ]
        + [jax.ShapeDtypeStruct(array.shape, array.dtype) for array in held],
        in_specs=layer_specs_in(len(inputs) + 3) + [pl.BlockSpec(memory_space=pl.ANY)] * (len(waits) + len(held)),
        out_specs=[pl.BlockSpec(memory_space=pltpu.VMEM)] * 3 + [pl.BlockSpec(memory_space=pl.ANY)] * len(held),
        input_output_aliases={len(inputs) + 3 + len(waits) + number: 3 + number for number in range(len(held))},
        scratch_shapes=[
            pltpu.VMEM((blocks, rows, D), narrow),
            pltpu.VMEM((D // 128, columns * D, 128), single),
            pltpu.VMEM((columns, D, D), narrow),
        ]
        + [pltpu.VMEM((tokens, width), narrow) for width in buffers]
        + [pltpu.SemaphoreType.DMA((4,))],
        compiler_params=pltpu.CompilerParams(vmem_limit_bytes=56 << 20),
        cost_estimate=pl.CostEstimate(flops=100 * 10**6, bytes_accessed=600 * 10**5, transcendentals=0),
    )(side, *inputs, vectors, gathered, *waits, *held)


def pair_rows_of(block_rows):
    pair = 2 * block_rows
    return 4 * D // pair * pair, -(-4 * D // pair) * pair


def mlp_back(side, grad_out, saved, vectors, gathered, part, waits, held):
    stream, packed, mixed, attn, pre, mlp = saved
    return layer_back(
        mlp_back_kernel, part, MATRIX_ROWS - pair_rows_of(gathered.shape[3])[0], side,
        (grad_out, stream, attn, pre, mlp), vectors, gathered, waits, held,
        FF // D, (FF, FF),
    )


def attention_back(side, grad_mid, saved, vectors, gathered, part, waits, held):
    stream, packed, mixed, attn, pre, mlp = saved
    return layer_back(
        attention_back_kernel, part, pair_rows_of(gathered.shape[3])[1], side,
        (grad_mid, stream, packed, mixed), vectors, gathered, waits, held,
        3, (D, 3 * D),
    )


def after(value, *tokens):
    def kernel(*refs):
        refs[-1][...] = refs[0][...]

    return pl.pallas_call(
        kernel,
        out_shape=jax.ShapeDtypeStruct(value.shape, value.dtype),
        in_specs=[pl.BlockSpec(memory_space=pltpu.VMEM)] + [pl.BlockSpec(memory_space=pl.ANY)] * len(tokens),
        out_specs=pl.BlockSpec(memory_space=pltpu.VMEM),
    )(value, *tokens)


def embed_back_kernel(grad_ref, patch_ref, shown_ref, gain_ref, vector_ref, *refs):
    out_ref = refs[-1]
    grad = grad_ref[...]
    images = grad.shape[0] // PAD_SEQ
    shown = shown_ref[...]
    position = jnp.zeros((PAD_SEQ, D), single)
    token = jnp.zeros((1, D), single)
    patch_grads = []
    for image in range(images):
        here = grad[image * PAD_SEQ : (image + 1) * PAD_SEQ]
        position = position + here
        rows = here[1:SEQ]
        seen = shown[image * PATCHES : (image + 1) * PATCHES]
        token = token + jnp.sum(rows * (1.0 - seen), axis=0, keepdims=True)
        patch_grads.append((rows * seen).astype(narrow))
    patch_grad = product_left(patch_ref[...], jnp.concatenate(patch_grads))
    out_ref[...] = jnp.zeros_like(out_ref)
    for column in range(D // 128):
        lane = slice(column * 128, (column + 1) * 128)
        out_ref[column, pl.ds(0, PIX), :] = patch_grad[:, lane]
        out_ref[column, pl.ds(PIX, SEQ), :] = position[:SEQ, lane]
        out_ref[column, pl.ds(PIX + SEQ, 1), :] = position[0:1, lane]
        out_ref[column, pl.ds(PIX + SEQ + 1, 1), :] = token[:, lane]
        out_ref[column, pl.ds(PIX + SEQ + 2, 2), :] = gain_ref[:, lane]
        out_ref[column, pl.ds(EMBED_ROWS, vector_ref.shape[0]), :] = vector_ref[:, lane]


def embed_back(grad, patch_rows, shown, gains, vector_grads, rows, waits):
    return pl.pallas_call(
        embed_back_kernel,
        out_shape=jax.ShapeDtypeStruct((D // 128, rows, 128), single),
        in_specs=[pl.BlockSpec(memory_space=pltpu.VMEM)] * 5 + [pl.BlockSpec(memory_space=pl.ANY)] * len(waits),
        out_specs=pl.BlockSpec(memory_space=pltpu.VMEM),
        compiler_params=pltpu.CompilerParams(vmem_limit_bytes=40 << 20),
        cost_estimate=pl.CostEstimate(flops=100 * 10**6, bytes_accessed=37 * 10**5, transcendentals=0),
    )(grad, patch_rows, shown, gains, vector_grads, *waits)


def proto_units(values):
    rounded = values.astype(narrow).astype(single)
    scale = lax.rsqrt(jnp.sum(rounded * rounded, axis=-1, keepdims=True) + 1e-06)
    return rounded, scale, (rounded * scale).astype(narrow)


def proto_terms(teacher_z, student_z, teacher_unit, student_unit, centre_column):
    teacher_logits = product_right(teacher_unit, teacher_z)
    logits = product_right(student_unit, student_z)
    teacher_exp = jnp.exp((teacher_logits - centre_column) * (1.0 / tau_teacher))
    student_exp = jnp.exp(logits * (1.0 / tau_student))
    return teacher_logits, logits, teacher_exp, student_exp


def logits_kernel(
    teacher_z_ref,
    student_z_ref,
    teacher_ref,
    student_ref,
    centre_ref,
    class_ref,
    mixed_ref,
    mixed_teacher_ref,
    sums_ref,
    centre_sum_ref,
    student_mix_ref,
    teacher_mix_ref,
    totals_ref,
):
    step = pl.program_id(0)

    @pl.when(step == 0)
    def _():
        student_mix_ref[...] = jnp.zeros_like(student_mix_ref)
        teacher_mix_ref[...] = jnp.zeros_like(teacher_mix_ref)
        totals_ref[...] = jnp.zeros_like(totals_ref)

    teacher_unit = proto_units(teacher_ref[...])[2]
    student_unit = proto_units(student_ref[...])[2]
    teacher_logits, logits, teacher_exp, student_exp = proto_terms(
        teacher_z_ref[...], student_z_ref[...], teacher_unit, student_unit, centre_ref[...]
    )
    totals_ref[pl.ds(0, 1), :] += jnp.sum(teacher_exp, axis=0, keepdims=True)
    totals_ref[pl.ds(1, 1), :] += jnp.sum(student_exp, axis=0, keepdims=True)
    totals_ref[pl.ds(2, 1), :] += jnp.sum(teacher_exp * logits, axis=0, keepdims=True)
    centre_sum_ref[...] = jnp.sum(teacher_logits * class_ref[0:1], axis=1, keepdims=True)
    student_mix_ref[...] += product_left(student_unit, student_exp.astype(narrow))
    teacher_mix_ref[...] += product_left(student_unit, teacher_exp.astype(narrow))

    @pl.when(step == pl.num_programs(0) - 1)
    def _():
        mixed_ref[...] = student_mix_ref[...].T
        mixed_teacher_ref[:, pl.ds(0, BOT)] = teacher_mix_ref[...].T
        lower = jnp.zeros((128 - totals_ref.shape[0], totals_ref.shape[1]), single)
        mixed_teacher_ref[:, pl.ds(BOT, 128)] = jnp.concatenate([totals_ref[...], lower]).T
        sums_ref[...] = totals_ref[...]


def proto_specs(rows, block):
    whole = pl.BlockSpec((rows, BOT), lambda i: (0, 0))
    table = pl.BlockSpec((block, BOT), lambda i: (i, 0))
    column = pl.BlockSpec((block, 1), lambda i: (i, 0))
    lines = pl.BlockSpec((8, rows), lambda i: (0, 0))
    return whole, table, column, lines


def logits_pass(teacher_z, student_z, teacher, student, centre_column, class_lines):
    rows, protos_here = teacher_z.shape[0], student.shape[0]
    block = protos_here // 4
    whole, table, column, lines = proto_specs(rows, block)
    return pl.pallas_call(
        logits_kernel,
        grid=(4,),
        out_shape=[
            jax.ShapeDtypeStruct((rows, BOT), single),
            jax.ShapeDtypeStruct((rows, BOT + 128), single),
            jax.ShapeDtypeStruct((8, rows), single),
            jax.ShapeDtypeStruct((protos_here, 1), single),
        ],
        in_specs=[whole, whole, table, table, column, lines],
        out_specs=[whole, pl.BlockSpec((rows, BOT + 128), lambda i: (0, 0)), lines, column],
        scratch_shapes=[
            pltpu.VMEM((BOT, rows), single),
            pltpu.VMEM((BOT, rows), single),
            pltpu.VMEM((8, rows), single),
        ],
        compiler_params=pltpu.CompilerParams(vmem_limit_bytes=56 << 20),
        cost_estimate=pl.CostEstimate(flops=100 * 10**6, bytes_accessed=520 * 10**5, transcendentals=0),
    )(teacher_z, student_z, teacher, student, centre_column, class_lines)


def proto_grad_kernel(
    held, teacher_z_ref, student_z_ref, teacher_ref, student_ref, centre_ref, scale_ref, *refs
):
    grad_ref, square_ref = refs[held : held + 2]
    step = pl.program_id(0)

    @pl.when(step == 0)
    def _():
        square_ref[...] = jnp.zeros_like(square_ref)

    teacher_unit = proto_units(teacher_ref[...])[2]
    rounded, scale, student_unit = proto_units(student_ref[...])
    student_z = student_z_ref[...]
    _, _, teacher_exp, student_exp = proto_terms(
        teacher_z_ref[...], student_z, teacher_unit, student_unit, centre_ref[...]
    )
    grad_logits = (student_exp * scale_ref[0:1] - teacher_exp * scale_ref[1:2]).astype(narrow)
    unit_grad = product_plain(grad_logits, student_z)
    along = jnp.sum(unit_grad * rounded, axis=-1, keepdims=True)
    grad = scale * (unit_grad - rounded * (along * scale * scale))
    grad_ref[...] = grad
    square_ref[...] += jnp.broadcast_to(jnp.sum(grad * grad), square_ref.shape)


def proto_grad_pass(teacher_z, student_z, teacher, student, centre_column, scale_lines, held):
    rows, protos_here = teacher_z.shape[0], student.shape[0]
    block = protos_here // 4
    whole, table, column, lines = proto_specs(rows, block)
    return pl.pallas_call(
        lambda *refs: proto_grad_kernel(len(held), *refs),
        grid=(4,),
        out_shape=[
            jax.ShapeDtypeStruct((protos_here, BOT), single),
            jax.ShapeDtypeStruct((8, 128), single),
        ]
        + [jax.ShapeDtypeStruct(array.shape, array.dtype) for array in held],
        in_specs=[whole, whole, table, table, column, lines]
        + [pl.BlockSpec(memory_space=pl.ANY)] * len(held),
        out_specs=[table, pl.BlockSpec((8, 128), lambda i: (0, 0))]
        + [pl.BlockSpec(memory_space=pl.ANY)] * len(held),
        input_output_aliases={6 + number: 2 + number for number in range(len(held))},
        compiler_params=pltpu.CompilerParams(vmem_limit_bytes=56 << 20),
        cost_estimate=pl.CostEstimate(flops=100 * 10**6, bytes_accessed=400 * 10**5, transcendentals=0),
    )(teacher_z, student_z, teacher, student, centre_column, scale_lines, *held)


def proto_update(factor, student, moment, second, teacher, grad):
    def kernel(factor_ref, *refs):
        weight, moment, second, teacher, grad = [ref[...] for ref in refs[:5]]
        done = adam_update(weight, moment, second, grad * factor_ref[0], teacher)
        for ref, value in zip(refs[5:], done):
            ref[...] = value

    block = student.shape[0] // 4
    table = pl.BlockSpec((block, BOT), lambda i: (i, 0))
    return pl.pallas_call(
        kernel,
        grid=(4,),
        out_shape=[
            jax.ShapeDtypeStruct(student.shape, narrow if number == 3 else single) for number in range(5)
        ],
        in_specs=[pl.BlockSpec(memory_space=pltpu.SMEM)] + [table] * 5,
        out_specs=[table] * 5,
        compiler_params=pltpu.CompilerParams(vmem_limit_bytes=60 << 20),
        cost_estimate=pl.CostEstimate(flops=10**7, bytes_accessed=2 * 10**7, transcendentals=0),
    )(factor.reshape(1), student, moment, second, teacher, grad)


def head_grads_kernel(
    held, place_ref, inputs_ref, grads_ref, *refs,
):
    own_ref, partner_ref = refs[len(refs) - 9 - held :][:2] if held else refs[-9:-7]
    window_ref, rows_ref, product_ref, third_ref, bottle_ref, line_ref, sems = refs[-7:]
    slot = own_ref.shape[0]
    lead = product_ref.shape[0] - window_ref.shape[1]
    number = lax.broadcasted_iota(jnp.int32, (slot, 1), 0)
    product_ref[pl.ds(0, lead), :] = jnp.zeros((lead, ROW), single)

    def block(at, out_ref):
        column = pl.multiple_of(place_ref[at], 128)
        grad_column = pl.multiple_of(place_ref[at + 3], 128)
        copies = [
            pltpu.make_async_copy(
                inputs_ref.at[:, pl.ds(column, window_ref.shape[1])], window_ref, sems.at[0]
            ),
            pltpu.make_async_copy(grads_ref.at[:, pl.ds(grad_column, ROW)], rows_ref, sems.at[1]),
        ]
        for copy in copies:
            copy.start()
        for copy in copies:
            copy.wait()
        window = window_ref[...]
        for piece in range(4):
            spot = pl.ds(piece * (ROW // 4), ROW // 4)
            product_ref[pl.ds(lead, window.shape[1]), spot] = product_left(window, rows_ref[:, spot])
        from_row = pl.multiple_of(lead + place_ref[at + 1], 8)
        kept = jnp.where(number < place_ref[at + 2], product_ref[pl.ds(from_row, slot), :], 0.0)
        out_ref[...] = kept.astype(out_ref.dtype)

    @pl.when(place_ref[8] == 0)
    def _():
        block(0, own_ref)

    @pl.when(place_ref[8] == 1)
    def _():
        column = pl.multiple_of(place_ref[9], 128)
        copies = [
            pltpu.make_async_copy(
                inputs_ref.at[:, pl.ds(column, third_ref.shape[1])], third_ref, sems.at[0]
            ),
            pltpu.make_async_copy(grads_ref.at[:, pl.ds(2 * HID, BOT)], bottle_ref, sems.at[1]),
        ]
        for copy in copies:
            copy.start()
        for copy in copies:
            copy.wait()
        third = product_left(third_ref[...], bottle_ref[...])
        for lane in range(BOT // 128):
            line_ref[lane] = third[:, lane * 128 : (lane + 1) * 128]
        for group in range(ROW // BOT):
            for lane in range(BOT // 128):
                value = line_ref[lane, pl.ds(group, slot, stride=ROW // BOT), :]
                own_ref[:, pl.ds(group * BOT + lane * 128, 128)] = jnp.where(
                    number < place_ref[2], value, 0.0
                )

    block(4, partner_ref)


def head_grads(place, inputs_all, grads_all, slot, lead, waits, held):
    rows = inputs_all.shape[0]
    wide = slot * ROW // BOT
    return pl.pallas_call(
        lambda *refs: head_grads_kernel(len(held), *refs),
        out_shape=[jax.ShapeDtypeStruct((slot, ROW), kind) for kind in (single, narrow)]
        + [jax.ShapeDtypeStruct(array.shape, array.dtype) for array in held],
        in_specs=[pl.BlockSpec(memory_space=pltpu.SMEM)]
        + [pl.BlockSpec(memory_space=pl.ANY)] * (2 + len(waits) + len(held)),
        out_specs=[pl.BlockSpec(memory_space=pltpu.VMEM)] * 2
        + [pl.BlockSpec(memory_space=pl.ANY)] * len(held),
        input_output_aliases={3 + len(waits) + number: 2 + number for number in range(len(held))},
        scratch_shapes=[
            pltpu.VMEM((rows, 256), narrow),
            pltpu.VMEM((rows, ROW), narrow),
            pltpu.VMEM((lead + 256, ROW), single),
            pltpu.VMEM((rows, wide), narrow),
            pltpu.VMEM((rows, BOT), narrow),
            pltpu.VMEM((BOT // 128, wide, 128), single),
            pltpu.SemaphoreType.DMA((2,)),
        ],
        compiler_params=pltpu.CompilerParams(vmem_limit_bytes=56 << 20),
        cost_estimate=pl.CostEstimate(flops=100 * 10**6, bytes_accessed=370 * 10**5, transcendentals=0),
    )(place, inputs_all, grads_all, *waits, *held)


def close_local(
    patches,
    masked,
    slot_used,
    stem,
    stem_moment,
    stem_second,
    stem_teacher,
    layers,
    layer_moment,
    layer_second,
    layer_teacher,
    protos,
    proto_moment,
    proto_second,
    proto_teacher,
    centre,
):
    count = 1 << len(BITS)
    half = count // 2
    me = lax.axis_index("dev")
    across = MASKS["b"]
    student_side = me >= half
    groups = [list(range(half)), list(range(half, count))]
    quarter = half // 2
    swap = jnp.where(student_side, quarter, 0)
    side = student_side.astype(jnp.int32).reshape(1)
    images_here = patches.shape[0]
    rows_here = images_here * 17
    pair_rows = -(-2 * rows_here // 16) * 16
    more_rows = pair_rows - 2 * rows_here
    stem_piece = stem.shape[0]
    layer_piece = layers.shape[1]
    block_rows = MATRIX_ROWS // count
    block = block_rows * D
    tail = layer_piece * count - MATRIX_ROWS * D
    drift = layer_piece - block
    bounds = head_bounds(count, stem_piece)
    sizes = [bounds[i + 1] - bounds[i] for i in range(count)]
    slot = max(sizes)
    starts = [b * ROW + EMBED_FLAT - stem_piece * i for i, b in enumerate(bounds[:-1])]
    first_w2 = bounds.index(D)
    first_w3 = bounds.index(D + HID)
    row_index = jnp.concatenate([jnp.zeros((images_here, 1), jnp.int32), masked + 1], axis=1)
    masked_here = jnp.any(
        masked[:, :, None] == jnp.arange(PATCHES, dtype=jnp.int32)[None, None, :], axis=1
    )
    kept = slot_used.astype(single)

    front = 16
    early_rows = -(-stem_piece // D)
    late_start = early_rows * D - stem_piece
    embed_rows = -(-early_rows // 16) * 16
    own_layers = jnp.concatenate([layer_teacher, layers])
    own_tail = own_layers[:, layer_piece - tail :].reshape(2 * LAYERS, tail // 128, 128)
    before = lax.ppermute(own_tail, "dev", step_pairs(count, 1))
    last_lines = lax.ppermute(
        jnp.pad(own_tail, ((0, 0), (0, 24 - tail // 128), (0, 0))), "dev", [(count - 1, 0)]
    )
    head_span = GROUP * ROW
    stems = jnp.stack([as_lanes(stem_teacher), as_lanes(stem)])
    stems_next = lax.ppermute(stems[:, : head_span // 128], "dev", step_pairs(count, -1))
    def per_device(rows):
        return lax.dynamic_slice(jnp.array(rows, jnp.int32), (me, 0), (1, len(rows[0]))).reshape(-1)

    def spots(*values):
        return [part for value in values for part in (value // 128, value % 128)]

    place = per_device(
        [
            spots(starts[i] + front * 128, front * 128 + (0 if i == 0 else late_start), tail - drift * i)
            for i in range(count)
        ]
    )
    head_blocks, layer_blocks, embed_blocks, vector_blocks = own_blocks(
        place,
        stems,
        stems_next,
        as_lanes(own_layers),
        before,
        last_lines,
        (front, stem_piece, layer_piece, tail),
        slot,
        block_rows,
        embed_rows,
    )

    other_layers = lax.ppermute(layer_blocks, "dev", pairs(count, across))
    both_layers = jnp.where(
        student_side,
        jnp.stack([other_layers, layer_blocks]),
        jnp.stack([layer_blocks, other_layers]),
    )
    gathered = lax.all_gather(both_layers, "dev", axis=0, axis_index_groups=groups)
    head_out = jnp.where(student_side, head_blocks[0], head_blocks[1])
    head_keep = jnp.where(student_side, head_blocks[1], head_blocks[0])
    head_got = lax.ppermute(head_out, "dev", pairs(count, across))
    both_head = jnp.where(
        student_side, jnp.stack([head_got, head_keep]), jnp.stack([head_keep, head_got])
    )

    seed = jnp.concatenate([embed_blocks.reshape(2 * embed_rows, D), vector_blocks.reshape(8 * 2 * LAYERS, D)])
    third = -(-seed.shape[0] // 48) * 16
    spread_parts = []
    for number, order in enumerate(("xyba", "baxy", "ybax")):
        spread = seed[number * third : (number + 1) * third]
        reached = [0, 1]
        for name in order:
            moves = [(i, i ^ MASKS[name]) for i in reached]
            got = lax.ppermute(spread, "dev", moves)
            targets = [t for s, t in moves]
            is_target = jnp.array([i in targets for i in range(count)])[me]
            spread = jnp.where(is_target, got, spread)
            reached = reached + targets
        spread_parts.append(spread)
    spread = jnp.concatenate(spread_parts)
    other = lax.ppermute(spread, "dev", pairs(count, 1))
    is_even = me % 2 == 0
    even = jnp.where(is_even, spread, other)
    odd = jnp.where(is_even, other, spread)
    embed_all = [
        jnp.concatenate(
            [
                even[m * embed_rows : m * embed_rows + early_rows],
                odd[m * embed_rows : m * embed_rows + EMBED_ROWS - early_rows],
            ]
        )
        for m in range(2)
    ]
    gathered_head = lax.all_gather(after(both_head, gathered, even, odd), "dev", axis=0, axis_index_groups=groups)
    vectors_all = even[2 * embed_rows :].reshape(2, LAYERS, 8, D)

    plan = []
    for i in range(1, count):
        target = 0 if i < first_w2 else 1 if i < first_w3 else 2
        row = bounds[i] - (0, D, D + HID)[target]
        skip = max(-row, 0)
        owner = 1 if i >= half else 0
        plan.append((i ^ across if owner else i, owner, skip, sizes[i] - skip, target, row + skip))

    def embed_parts(model):
        rows = embed_all[model]
        return (rows[:PIX], rows[PIX : PIX + SEQ], rows[PIX + SEQ :], None, None, None)

    def head_rows(stream, extras):
        chosen = jnp.take_along_axis(stream, row_index[:, :, None], axis=1).reshape(rows_here, D)
        normed = layer_norm(chosen, extras[2].astype(single), extras[3].astype(single)).astype(narrow)
        return chosen, normed

    def start_rows(parts, student):
        stream = embed(parts, patches, masked_here, student)
        return jnp.pad(stream, ((0, 0), (0, PAD_SEQ - SEQ), (0, 0))).reshape(images_here * PAD_SEQ, D)

    student_parts = embed_parts(1)
    stream = start_rows(student_parts, True)
    saved_layers = []
    for layer_index in range(LAYERS):
        before_layer = stream
        stream, *saved = layer_forward(
            side, stream, vectors_all[1, layer_index], gathered, LAYERS + layer_index, True
        )
        saved_layers.append((before_layer, *saved))
    teacher_parts = embed_parts(0)
    teacher_stream = start_rows(teacher_parts, False)
    for layer_index in range(LAYERS):
        teacher_stream = layer_forward(
            side, teacher_stream, vectors_all[0, layer_index], gathered, layer_index, False
        )[0]
    stream = stream.reshape(images_here, PAD_SEQ, D)
    teacher_stream = teacher_stream.reshape(images_here, PAD_SEQ, D)
    chosen, student_normed = head_rows(stream, student_parts[2])
    teacher_normed = head_rows(teacher_stream, teacher_parts[2])[1]

    normed_got = lax.ppermute(
        jnp.where(student_side, teacher_normed, student_normed), "dev", pairs(count, across)
    )
    normed = jnp.where(
        student_side,
        jnp.concatenate([normed_got, student_normed]),
        jnp.concatenate([teacher_normed, normed_got]),
    )
    normed = jnp.pad(normed, ((0, more_rows), (0, 0)))
    third_end = (bounds[-2] - D - HID + slot) * (ROW // BOT)
    acts_width = D + HID + max(third_end, HID)
    unit_z, acts, bottleneck, pre_one, pre_two = head_pass(
        head_up_kernel,
        plan,
        side,
        (normed,),
        gathered_head,
        [
            jax.ShapeDtypeStruct((pair_rows, BOT), narrow),
            jax.ShapeDtypeStruct((pair_rows, acts_width), narrow),
            jax.ShapeDtypeStruct((pair_rows, BOT), single),
            jax.ShapeDtypeStruct((pair_rows, HID), single),
            jax.ShapeDtypeStruct((pair_rows, HID), single),
        ],
    )
    inputs_all = lax.all_gather(acts, "dev", axis=0, axis_index_groups=groups).reshape(half * pair_rows, -1)

    all_rows = half * pair_rows
    flag_row = 2 * rows_here
    kept_row = jnp.broadcast_to(kept[:, None] * (1.0 / 128.0), (images_here, 17)).reshape(1, rows_here)
    kept_row = jnp.pad(kept_row.astype(narrow), ((0, 0), (0, BOT - rows_here)))
    z_pair = cube_gather(jnp.concatenate([unit_z[:flag_row], kept_row, unit_z[flag_row + 1 :]]), "b")
    teacher_z_all = cube_gather(z_pair[0], "xygc")
    student_z_all = cube_gather(z_pair[1], "gxyc").reshape((2,) * 4 + (pair_rows, BOT))
    student_z_all = jnp.transpose(student_z_all, (0, 3, 1, 2, 4, 5)).reshape(half, pair_rows, BOT)
    all_kept = jnp.concatenate(
        [
            teacher_z_all[:, flag_row, :rows_here],
            student_z_all[:, flag_row, :rows_here],
            jnp.zeros((half, more_rows), narrow),
        ],
        axis=1,
    )
    all_kept = all_kept.astype(single).reshape(all_rows) * 128.0
    teacher_z_all = teacher_z_all.reshape(all_rows, BOT)
    student_z_all = student_z_all.reshape(all_rows, BOT)
    protos_here = protos.shape[0]
    own_centre = lax.dynamic_slice(centre, (me * protos_here,), (protos_here,))
    centre_column = own_centre.reshape(protos_here, 1)
    spot_in_pair = jnp.arange(all_rows) % pair_rows
    is_class = (spot_in_pair % 17) == 0
    class_kept = jnp.where(is_class, all_kept, 0.0)
    row_weight = jnp.where(is_class, all_kept, all_kept * (1.0 / 16.0))
    count_total = jnp.sum(class_kept)

    def lines(*values):
        return jnp.pad(jnp.stack(values), ((0, 8 - len(values)), (0, 0)))

    mixed_student, mixed_teacher, sums, centre_sum = logits_pass(
        teacher_z_all, student_z_all, proto_teacher, protos, centre_column, lines(class_kept)
    )
    by_pair = (2,) * 4 + (pair_rows, -1)
    mixed_own = jnp.concatenate(
        [
            cube_scatter(mixed_student.reshape(by_pair), "cgyx", "cgyx"),
            cube_scatter(mixed_teacher.reshape(by_pair), "cgyx", "cxyg"),
        ],
        axis=1,
    )
    mixed_own = mixed_own + lax.ppermute(
        mixed_own.astype(narrow), "dev", [(i, i ^ across) for i in range(half)]
    ).astype(single)
    scale = row_weight / tau_student
    flags = bit_flags(me)
    pair_at = flags["c"] * 8 + flags["g"] * 4 + flags["y"] * 2 + flags["x"]
    own_scale = lax.dynamic_slice(scale, (pair_at * pair_rows,), (pair_rows,))[:, None]
    grad_unit_z = own_scale * (
        mixed_own[:, :BOT] / mixed_own[:, 2 * BOT + 1 : 2 * BOT + 2]
        - mixed_own[:, BOT : 2 * BOT] / mixed_own[:, 2 * BOT : 2 * BOT + 1]
    )
    own_new_centre = (
        centre_keep * own_centre + (1.0 - centre_keep) * centre_sum.reshape(protos_here) / count_total
    )

    grads, grad_normed = head_pass(
        head_down_kernel,
        plan,
        side,
        (grad_unit_z, bottleneck, pre_one, pre_two),
        gathered_head,
        [
            jax.ShapeDtypeStruct((pair_rows, 2 * HID + BOT), narrow),
            jax.ShapeDtypeStruct((pair_rows, D), single),
        ],
    )
    width = grads.shape[1]
    wide = max(protos_here, all_rows)
    carried = jnp.stack(
        [jnp.pad(row, (0, wide - row.shape[0])) for row in (own_new_centre, sums[0], sums[1], sums[2])]
    )
    carried_rows = 3 * carried.shape[0]
    assert carried_rows <= more_rows and wide <= width
    high = carried.astype(narrow)
    middle = (carried - high.astype(single)).astype(narrow)
    low = (carried - high.astype(single) - middle.astype(single)).astype(narrow)
    carried = jnp.pad(jnp.concatenate([high, middle, low]), ((0, more_rows - carried_rows), (0, width - wide)))
    grads = jnp.concatenate([grads[: 2 * rows_here], carried])
    grads_all = lax.all_gather(grads, "dev", axis=0, axis_index_groups=groups).reshape(half * pair_rows, -1)
    normed_back = lax.ppermute(
        grad_normed[:rows_here], "dev", [(i, i ^ across) for i in range(half, count)]
    )
    own_grad_normed = jnp.where(student_side, grad_normed[rows_here : 2 * rows_here], normed_back)
    extras = student_parts[2].astype(single)
    grad_chosen, grad_gain, grad_bias = jax.vjp(layer_norm, chosen, extras[2], extras[3])[1](
        own_grad_normed
    )
    image_index = jnp.arange(images_here, dtype=jnp.int32)[:, None]
    grad_stream = (
        jnp.zeros(stream.shape, single)
        .at[image_index, row_index]
        .add(grad_chosen.reshape(images_here, 17, D))
    )

    grad_stream = grad_stream.reshape(images_here * PAD_SEQ, D)
    middle_row = block_rows // 2
    vector_grads = [None] * LAYERS

    def halves(array):
        middle = array.shape[-2] // 2
        return [array[..., :middle, :], array[..., middle:, :]]

    def cuts(parts, names, order):
        return [cut(part, name, axis, 1) for part, name, axis in zip(parts, names, order)]

    def moves(pieces, order):
        return [move(sent, kept, axis) for (sent, kept, left), axis in zip(pieces, order)]

    def over_core(weight_grad, rows):
        pairs_of = weight_grad.reshape(D // 128, -1, 2, rows, 128)
        return move(*cut(pairs_of, "pc", "c", 1)[:2], "c")

    def core_cut(weight_grad, rows):
        return cut(weight_grad.reshape(D // 128, -1, 2, rows, 128), "pc", "c", 1)[:2]

    def start(late, early, *others):
        shared_pair = 4 * D // (2 * block_rows)
        whole = jnp.concatenate(
            [
                early[:, :shared_pair],
                early[:, shared_pair:] + late[:, : early.shape[1] - shared_pair],
                late[:, early.shape[1] - shared_pair :],
            ],
            axis=1,
        )
        parts = [jnp.concatenate(pieces, axis=2) for pieces in zip(*[halves(array) for array in (whole, *others)])]
        by_bits = [part.reshape((D // 128, 2, 2, 2, 2) + part.shape[2:]) for part in parts]
        return (cuts(by_bits, ["bayx"] * 2, rounds[0]), 0)

    rounds = (("x", "b"), ("y", "a"), ("b", "x"), ("a", "y"))

    def advance(state):
        pieces, stage = state
        parts = moves(pieces, rounds[stage])
        names = [left for sent, kept, left in pieces]
        return cuts(parts, names, rounds[stage + 1]), stage + 1

    def finish(state):
        while state[1] < len(rounds) - 1:
            state = advance(state)
        return moves(state[0], rounds[-1])

    def sends(states):
        return tuple(sent for pieces, stage in states for sent, kept, left in pieces)

    def block_place(i):
        column = max(bounds[i], 0) // 128 * 128
        grad_column = 0 if i < first_w2 else HID
        return [column, bounds[i] - column if i else 0, sizes[i] if i else 0, grad_column]

    def third_place(i):
        return [0, 0, sizes[i], 0]

    place = per_device(
        [
            (third_place(i) if i >= first_w3 else block_place(i))
            + block_place(i ^ across)
            + [int(i >= first_w3), D + HID + max(bounds[i] - D - HID, 0) * (ROW // BOT)]
            for i in range(count)
        ]
    )
    started = []
    held_block = None
    waits = ()
    for layer_index in reversed(range(LAYERS)):
        saved, vectors = saved_layers[layer_index], vectors_all[1, layer_index]
        part = LAYERS + layer_index
        grad_stream, late_grad, late_vectors, *held_block = mlp_back(
            side,
            grad_stream,
            saved,
            vectors,
            gathered,
            part,
            waits + sends(started),
            [partner_block_grad] if started else [],
        )
        late = over_core(late_grad, block_rows)
        started = [advance(state) for state in started]
        if started:
            block_got = lax.ppermute(held_block[0], "dev", [(i, i ^ across) for i in range(half, count)])
        grad_stream, early_grad, early_vectors, *held_block = attention_back(
            side,
            grad_stream,
            saved,
            vectors,
            gathered,
            part,
            sends(started),
            [own_block_grad] if started else [],
        )
        vector_grads[layer_index] = (late_vectors + early_vectors)[:6]
        if layer_index == LAYERS - 1:
            sent, stay = core_cut(early_grad, block_rows)
            own_block_grad, partner_block_grad, stay = head_grads(
                place, inputs_all, grads_all, slot, -min(bounds[1], 0), (early_vectors,), [stay]
            )
            waits = (own_block_grad,)
        started = [advance(state) for state in started]
        if layer_index > 0:
            started.append(start(late, move(sent, stay, "c")))
    own_block_grad = held_block[0]
    rows = grads_all.reshape(half, pair_rows, width)[:, 2 * rows_here : 2 * rows_here + carried_rows, :wide]
    rows = rows.reshape(half, 3, carried_rows // 3, wide).astype(single)
    rows = rows[:, 0] + rows[:, 1] + rows[:, 2]
    half_centre = rows[:, 0, :protos_here]
    half_sums = jnp.sum(rows[:, 1:, :all_rows], axis=0)
    other_centre = lax.ppermute(half_centre, "dev", pairs(count, across))
    sums = half_sums + lax.ppermute(half_sums, "dev", pairs(count, across))
    new_centre = jnp.where(
        student_side,
        jnp.concatenate([other_centre, half_centre]),
        jnp.concatenate([half_centre, other_centre]),
    ).reshape(-1)
    cross = jnp.log(sums[1]) - sums[2] / (sums[0] * tau_student)
    loss_total = jnp.sum(row_weight * cross)
    student_scale, teacher_scale = scale / sums[1], scale / sums[0]
    head_block_grad = jnp.where(student_side, own_block_grad, block_got.astype(single))
    early = over_core(early_grad, block_rows)
    small_rows = -(-(EMBED_ROWS + 6 * LAYERS) // (16 * count)) * 16
    small = embed_back(
        grad_stream,
        patches.reshape(images_here * PATCHES, PIX),
        jnp.where(masked_here, 0.0, 1.0).reshape(images_here * PATCHES, 1),
        jnp.stack([grad_gain, grad_bias]),
        jnp.concatenate(vector_grads),
        small_rows * count,
        (),
    )
    started.append(start(late, early, over_core(small, small_rows)))
    last_rows = lax.dynamic_slice(
        head_block_grad, (jnp.array(sizes, jnp.int32)[me] - GROUP, 0), (GROUP, ROW)
    )
    previous = lax.ppermute(last_rows, "dev", step_pairs(count, 1))
    proto_grad, proto_square, *held = proto_grad_pass(
        teacher_z_all,
        student_z_all,
        proto_teacher,
        protos,
        centre_column,
        lines(student_scale, teacher_scale),
        [stay for pieces, stage in started for sent, stay, left in pieces],
    )
    held = iter(held)
    started = [([(sent, next(held), left) for sent, _, left in pieces], stage) for pieces, stage in started]
    blocks = [finish(state) for state in started][::-1]
    middle_row = block_rows // 2
    layer_block = jnp.stack([jnp.concatenate([part[:, :middle_row] for part in parts], axis=1) for parts in blocks])
    small_block = jnp.concatenate([part[:, middle_row:] for part in blocks[0]], axis=1)

    square_local = (
        jnp.sum(head_block_grad * head_block_grad)
        + jnp.sum(layer_block * layer_block)
        + jnp.sum(small_block * small_block)
        + proto_square[0, 0]
    )
    high = square_local.astype(narrow)
    middle = (square_local - high.astype(single)).astype(narrow)
    low = (square_local - high.astype(single) - middle.astype(single)).astype(narrow)
    tile = jnp.pad(jnp.stack([high, middle, low]).reshape(1, 1, 3), ((0, 0), (0, 15), (0, 125)))
    first_rows = small_block[:2].astype(narrow)
    other_rows = jnp.concatenate([small_block[2:].astype(narrow), tile], axis=1)
    first_rows = cube_gather(first_rows, "xya")
    other_rows = cube_gather(other_rows, "abx")
    behind = lax.ppermute(layer_block[:, :, :6], "dev", step_pairs(count, -1))
    place = per_device([spots(head_span - starts[i], drift * i) for i in range(count)])
    stem_lines, layer_lines, first_rows, other_rows = own_shards(
        place, head_block_grad, previous, layer_block, behind, lane_rows(stem_piece), lane_rows(layer_piece),
        [first_rows, other_rows],
    )
    first_rows = jnp.moveaxis(cube_gather(first_rows, "bc").reshape((2, 2, 8) + first_rows.shape[1:]), 0, 2)
    other_rows = cube_gather(other_rows, "yc")
    other_rows = other_rows.reshape((2,) * 5 + other_rows.shape[2:])
    other_rows = jnp.transpose(other_rows, (3, 4, 1, 2, 0, 5, 6, 7))
    first_rows = first_rows.reshape((count,) + first_rows.shape[3:])
    other_rows = other_rows.reshape((count,) + other_rows.shape[5:])
    square_total = jnp.sum(other_rows[:, 0, small_rows, :3].astype(single))
    small_all = jnp.concatenate([first_rows, other_rows[:, :, :small_rows]], axis=1).astype(single)
    small_all = jnp.transpose(small_all, (0, 2, 1, 3)).reshape(small_rows * count, D)
    embed_grad = small_all[:EMBED_ROWS].reshape(-1)
    vector_grad = small_all[EMBED_ROWS : EMBED_ROWS + 6 * LAYERS].reshape(LAYERS, 6 * D)
    layer_grad = layer_lines.reshape(LAYERS, -1)[:, :layer_piece]
    layer_grad = jnp.concatenate(
        [
            layer_grad[:, : layer_piece - tail],
            jnp.where(me == count - 1, vector_grad, layer_grad[:, layer_piece - tail :]),
        ],
        axis=1,
    )
    stem_grad = stem_lines.reshape(-1)[:stem_piece]
    rest = EMBED_FLAT - stem_piece
    second_part = jnp.concatenate([embed_grad[stem_piece:], stem_grad[rest:]])
    stem_grad = jnp.where(
        me == 0, embed_grad[:stem_piece], jnp.where(me == 1, second_part, stem_grad)
    )

    grad_norm = jnp.sqrt(square_total) / count_total
    factor = jnp.minimum(1.0, clip_limit / (grad_norm + 1e-06)) / count_total
    stem_set = adam_update(stem, stem_moment, stem_second, stem_grad * factor, stem_teacher)
    layer_set = adam_update(layers, layer_moment, layer_second, layer_grad * factor, layer_teacher)
    proto_set = proto_update(factor, protos, proto_moment, proto_second, proto_teacher, proto_grad)
    return (loss_total, count_total, grad_norm, new_centre) + stem_set + layer_set + tuple(proto_set)


def solution(mesh):
    count = mesh.shape["dev"]
    stem_length = -(-(EMBED_FLAT + HEAD_ROWS * ROW) // count) * count
    close = fits(count, stem_length // count, (MATRIX_ROWS + 6) * D // count)
    placed = (
        P("dev", None, None),
        P("dev", None),
        P("dev"),
        P("dev"),
        P("dev"),
        P("dev"),
        P("dev"),
        P(None, "dev"),
        P(None, "dev"),
        P(None, "dev"),
        P(None, "dev"),
        P("dev", None),
        P("dev", None),
        P("dev", None),
        P("dev", None),
        P(),
    )
    return jax.shard_map(
        close_local if close else spread_local,
        mesh=mesh,
        in_specs=placed,
        out_specs=(
            P(),
            P(),
            P(),
            P(),
            P("dev"),
            P("dev"),
            P("dev"),
            P("dev"),
            P("dev"),
            P(None, "dev"),
            P(None, "dev"),
            P(None, "dev"),
            P(None, "dev"),
            P(None, "dev"),
            P("dev", None),
            P("dev", None),
            P("dev", None),
            P("dev", None),
            P("dev", None),
        ),
        check_vma=False,
    )
```

```python
import jax
import jax.numpy as jnp
from jax import lax
from jax.experimental import pallas as pl
from jax.experimental.pallas import tpu as pltpu
from jax.sharding import PartitionSpec as P

D = 384
HEADS = 6
HEAD_DIM = 64
FF = 1536
HID = 2048
BOT = 256
PIX = 588
PATCHES = 256
LAYERS = 2
STEP = 10
SEQ = 257


tau_student = 0.1
tau_teacher = 0.04
clip_limit = 0.003
learn_rate = 0.03
beta_one = 0.9
beta_two = 0.999
adam_eps = 1e-08
decay_rate = 0.04
teacher_keep = 0.8
centre_keep = 0.9
narrow = jnp.bfloat16
single = jnp.float32


def layer_shapes():
    return ((D, 3 * D), (D, D), (D, FF), (FF, D), (6, D))


def stem_shapes():
    return ((PIX, D), (SEQ, D), (4, D), (D, HID), (HID, HID), (HID, BOT))


def cut_flat(flat_row, shape_list):
    pieces = []
    offset = 0
    for shape_pair in shape_list:
        length = shape_pair[0] * shape_pair[1]
        pieces.append(flat_row[offset : offset + length].reshape(shape_pair))
        offset = offset + length
    return pieces


def pack_flat(grad_list, total_length):
    joined = jnp.concatenate([grad_item.reshape(-1) for grad_item in grad_list])
    return jnp.concatenate([joined, jnp.zeros((total_length - joined.shape[0],), single)])


def contract(form, left_arg, right_arg):
    return jnp.einsum(form, left_arg, right_arg, preferred_element_type=single)


def layer_norm(values, gain_row, bias_row):
    centred = values - jnp.mean(values, axis=-1, keepdims=True)
    spread = jnp.mean(centred * centred, axis=-1, keepdims=True)
    return centred * lax.rsqrt(spread + 1e-06) * gain_row + bias_row


def unit_rows(values):
    return values * lax.rsqrt(jnp.sum(values * values, axis=-1, keepdims=True) + 1e-06)


def gelu_back(pre_act, grad_act):
    return jax.vjp(jax.nn.gelu, pre_act)[1](grad_act)[0]


def block_forward(stream, weights):
    w_qkv, w_proj, w_up, w_down, vectors = weights
    vectors = vectors.astype(single)
    batch_size = stream.shape[0]
    normed = layer_norm(stream, vectors[0], vectors[1]).astype(narrow)
    packed = (
        contract("bsd,de->bse", normed, w_qkv)
        .astype(narrow)
        .reshape(batch_size, SEQ, 3, HEADS, HEAD_DIM)
    )
    scores = contract("bqhe,bkhe->bhqk", packed[:, :, 0], packed[:, :, 1]) * HEAD_DIM ** (-0.5)
    top_score = jnp.max(scores, axis=-1, keepdims=True)
    exp_terms = jnp.exp(scores - top_score)
    totals = jnp.sum(exp_terms, axis=-1, keepdims=True)
    log_total = top_score + jnp.log(totals)
    mixed = contract("bhqk,bkhe->bqhe", (exp_terms / totals).astype(narrow), packed[:, :, 2])
    mixed = mixed.astype(narrow).reshape(batch_size, SEQ, D)
    attn_out = contract("bsd,de->bse", mixed, w_proj)
    middle = stream + vectors[2] * attn_out
    normed_two = layer_norm(middle, vectors[3], vectors[4]).astype(narrow)
    pre_act = contract("bsd,df->bsf", normed_two, w_up)
    hidden = jax.nn.gelu(pre_act).astype(narrow)
    mlp_out = contract("bsf,fd->bsd", hidden, w_down)
    saved = (
        stream,
        normed,
        packed,
        log_total,
        mixed,
        attn_out,
        middle,
        normed_two,
        pre_act,
        hidden,
        mlp_out,
    )
    return (middle + vectors[5] * mlp_out, saved)


def block_backward(grad_out, weights, saved):
    w_qkv, w_proj, w_up, w_down, vectors = weights
    vectors = vectors.astype(single)
    (
        stream,
        normed,
        packed,
        log_total,
        mixed,
        attn_out,
        middle,
        normed_two,
        pre_act,
        hidden,
        mlp_out,
    ) = saved
    batch_size = stream.shape[0]
    score_scale = HEAD_DIM ** (-0.5)
    grad_ls_two = jnp.sum(grad_out * mlp_out, axis=(0, 1))
    grad_mlp = (grad_out * vectors[5]).astype(narrow)
    grad_down = contract("bsf,bsd->fd", hidden, grad_mlp)
    grad_pre = gelu_back(pre_act, contract("bsd,fd->bsf", grad_mlp, w_down)).astype(narrow)
    grad_up = contract("bsd,bsf->df", normed_two, grad_pre)
    grad_normed_two = contract("bsf,df->bsd", grad_pre, w_up)
    grad_mid, grad_gain_two, grad_bias_two = jax.vjp(layer_norm, middle, vectors[3], vectors[4])[1](
        grad_normed_two
    )
    grad_mid = grad_mid + grad_out
    grad_ls_one = jnp.sum(grad_mid * attn_out, axis=(0, 1))
    grad_attn = (grad_mid * vectors[2]).astype(narrow)
    grad_proj = contract("bsd,bse->de", mixed, grad_attn)
    grad_mixed = (
        contract("bse,de->bsd", grad_attn, w_proj)
        .astype(narrow)
        .reshape(batch_size, SEQ, HEADS, HEAD_DIM)
    )
    query_rows = packed[:, :, 0]
    key_rows = packed[:, :, 1]
    value_rows = packed[:, :, 2]
    probs = jnp.exp(contract("bqhe,bkhe->bhqk", query_rows, key_rows) * score_scale - log_total)
    grad_probs = contract("bqhe,bkhe->bhqk", grad_mixed, value_rows)
    grad_values = contract("bhqk,bqhe->bkhe", probs.astype(narrow), grad_mixed)
    grad_scores = probs * (grad_probs - jnp.sum(probs * grad_probs, axis=-1, keepdims=True))
    grad_raw = (grad_scores * score_scale).astype(narrow)
    grad_queries = contract("bhqk,bkhe->bqhe", grad_raw, key_rows)
    grad_keys = contract("bhqk,bqhe->bkhe", grad_raw, query_rows)
    grad_packed = (
        jnp.stack([grad_queries, grad_keys, grad_values], axis=2)
        .astype(narrow)
        .reshape(batch_size, SEQ, 3 * D)
    )
    grad_qkv = contract("bsd,bse->de", normed, grad_packed)
    grad_normed = contract("bse,de->bsd", grad_packed, w_qkv)
    grad_in, grad_gain_one, grad_bias_one = jax.vjp(layer_norm, stream, vectors[0], vectors[1])[1](
        grad_normed
    )
    grad_vectors = jnp.stack(
        [grad_gain_one, grad_bias_one, grad_ls_one, grad_gain_two, grad_bias_two, grad_ls_two]
    )
    return (grad_in + grad_mid, (grad_qkv, grad_proj, grad_up, grad_down, grad_vectors))


def embed(stem_parts, image_rows, masked_here, student):
    patch_w, position, extras, w_first, w_second, w_third = stem_parts
    extras = extras.astype(single)
    embedded = contract("gpc,cd->gpd", image_rows, patch_w)
    if student:
        embedded = jnp.where(masked_here[:, :, None], extras[1], embedded)
    cls_rows = jnp.broadcast_to(extras[0], (image_rows.shape[0], 1, D))
    return jnp.concatenate([cls_rows, embedded], axis=1) + position.astype(single)


def embed_backward(grad_stream, image_rows, masked_here):
    grad_cls = jnp.sum(grad_stream[:, 0], axis=0)
    grad_position = jnp.sum(grad_stream, axis=0)
    grad_patch_rows = grad_stream[:, 1:]
    grad_mask_token = jnp.sum(jnp.where(masked_here[:, :, None], grad_patch_rows, 0.0), axis=(0, 1))
    grad_embedded = jnp.where(masked_here[:, :, None], 0.0, grad_patch_rows).astype(narrow)
    grad_patch_w = contract("gpc,gpd->cd", image_rows, grad_embedded)
    return (grad_patch_w, grad_position, grad_cls, grad_mask_token)


def head_forward(stem_parts, proto_rows, stream, row_index):
    patch_w, position, extras, w_first, w_second, w_third = stem_parts
    extras = extras.astype(single)
    chosen = jnp.take_along_axis(stream, row_index[:, :, None], axis=1)
    normed = layer_norm(chosen, extras[2], extras[3]).astype(narrow)
    pre_one = contract("grd,dh->grh", normed, w_first)
    hidden_one = jax.nn.gelu(pre_one).astype(narrow)
    pre_two = contract("grh,hk->grk", hidden_one, w_second)
    hidden_two = jax.nn.gelu(pre_two).astype(narrow)
    bottleneck = contract("grh,hb->grb", hidden_two, w_third)
    unit_z = unit_rows(bottleneck).astype(narrow)
    unit_protos = unit_rows(proto_rows.astype(single)).astype(narrow)
    logits = contract("grb,kb->grk", unit_z, unit_protos)
    return (
        logits,
        (chosen, normed, pre_one, hidden_one, pre_two, hidden_two, bottleneck, unit_z, unit_protos),
    )


def head_backward(grad_logits, stem_parts, saved, row_index, stream_shape):
    patch_w, position, extras, w_first, w_second, w_third = stem_parts
    extras = extras.astype(single)
    chosen, normed, pre_one, hidden_one, pre_two, hidden_two, bottleneck, unit_z, unit_protos = (
        saved
    )
    grad_rounded = grad_logits.astype(narrow)
    grad_unit_z = contract("grk,kb->grb", grad_rounded, unit_protos)
    grad_unit_protos = contract("grk,grb->kb", grad_rounded, unit_z)
    grad_bottle = jax.vjp(unit_rows, bottleneck)[1](grad_unit_z)[0].astype(narrow)
    grad_third = contract("grh,grb->hb", hidden_two, grad_bottle)
    grad_pre_two = gelu_back(pre_two, contract("grb,hb->grh", grad_bottle, w_third)).astype(narrow)
    grad_second = contract("grh,grk->hk", hidden_one, grad_pre_two)
    grad_pre_one = gelu_back(pre_one, contract("grk,hk->grh", grad_pre_two, w_second)).astype(
        narrow
    )
    grad_first = contract("grd,grh->dh", normed, grad_pre_one)
    grad_normed = contract("grh,dh->grd", grad_pre_one, w_first)
    grad_chosen, grad_gain, grad_bias = jax.vjp(layer_norm, chosen, extras[2], extras[3])[1](
        grad_normed
    )
    image_index = jnp.arange(row_index.shape[0], dtype=jnp.int32)[:, None]
    grad_stream = jnp.zeros(stream_shape, single).at[image_index, row_index].add(grad_chosen)
    return (
        grad_stream,
        (grad_first, grad_second, grad_third),
        grad_gain,
        grad_bias,
        grad_unit_protos,
    )


def adam_update(weight, moment, second, grad, teacher):
    new_moment = beta_one * moment + (1.0 - beta_one) * grad
    new_second = beta_two * second + (1.0 - beta_two) * grad * grad
    direction = (
        new_moment
        / (1.0 - beta_one**STEP)
        / (jnp.sqrt(new_second / (1.0 - beta_two**STEP)) + adam_eps)
    )
    new_weight = weight - learn_rate * (direction + decay_rate * weight)
    return (
        new_moment,
        new_second,
        new_weight,
        new_weight.astype(narrow),
        teacher_keep * teacher + (1.0 - teacher_keep) * new_weight,
    )


def spread_local(
    patches,
    masked,
    slot_used,
    stem,
    stem_moment,
    stem_second,
    stem_teacher,
    layers,
    layer_moment,
    layer_second,
    layer_teacher,
    protos,
    proto_moment,
    proto_second,
    proto_teacher,
    centre,
):
    images_here = patches.shape[0]
    row_index = jnp.concatenate([jnp.zeros((images_here, 1), jnp.int32), masked + 1], axis=1)
    masked_here = jnp.any(
        masked[:, :, None] == jnp.arange(PATCHES, dtype=jnp.int32)[None, None, :], axis=1
    )
    kept = slot_used.astype(single)
    teacher_flat, teacher_protos = (
        lax.all_gather(stem_teacher.astype(narrow), "dev", axis=0, tiled=True),
        lax.all_gather(proto_teacher.astype(narrow), "dev", axis=0, tiled=True),
    )
    teacher_parts = cut_flat(teacher_flat, stem_shapes())
    stream = embed(teacher_parts, patches, masked_here, False)
    for layer_index in range(LAYERS):
        teacher_layer = lax.all_gather(
            layer_teacher[layer_index].astype(narrow), "dev", axis=0, tiled=True
        )
        stream = block_forward(stream, cut_flat(teacher_layer, layer_shapes()))[0]
    teacher_logits = head_forward(teacher_parts, teacher_protos, stream, row_index)[0]
    teacher_probs = jax.nn.softmax((teacher_logits - centre) / tau_teacher, axis=-1)
    centre_terms = jnp.sum(kept[:, None] * teacher_logits[:, 0], axis=0)
    student_flat, student_protos = (
        lax.all_gather(stem.astype(narrow), "dev", axis=0, tiled=True),
        lax.all_gather(protos.astype(narrow), "dev", axis=0, tiled=True),
    )
    student_parts = cut_flat(student_flat, stem_shapes())
    stream = embed(student_parts, patches, masked_here, True)
    saved_layers = []
    gathered_layers = []
    for layer_index in range(LAYERS):
        layer_flat = lax.all_gather(layers[layer_index].astype(narrow), "dev", axis=0, tiled=True)
        gathered_layers.append(layer_flat)
        stream, saved = block_forward(stream, cut_flat(layer_flat, layer_shapes()))
        saved_layers.append(saved)
    logits, head_saved = head_forward(student_parts, student_protos, stream, row_index)

    def loss_piece(logit_rows):
        log_probs = jax.nn.log_softmax(logit_rows / tau_student, axis=-1)
        cross = -jnp.sum(teacher_probs * log_probs, axis=-1)
        return jnp.sum(kept * (cross[:, 0] + jnp.mean(cross[:, 1:], axis=1)))

    loss_local, loss_puller = jax.vjp(loss_piece, logits)
    grad_logits = loss_puller(jnp.float32(1.0))[0]
    count_local = jnp.sum(kept)
    loss_total, count_total, centre_total = lax.psum((loss_local, count_local, centre_terms), "dev")
    back_flat, back_protos = (
        lax.all_gather(stem.astype(narrow), "dev", axis=0, tiled=True),
        lax.all_gather(protos.astype(narrow), "dev", axis=0, tiled=True),
    )
    back_parts = cut_flat(back_flat, stem_shapes())
    grad_stream, head_grads, grad_gain, grad_bias, grad_unit_protos = head_backward(
        grad_logits, back_parts, head_saved, row_index, stream.shape
    )
    layer_grads = []
    for layer_index in reversed(range(LAYERS)):
        weight_flat = lax.all_gather(layers[layer_index].astype(narrow), "dev", axis=0, tiled=True)
        grad_stream, block_grads = block_backward(
            grad_stream, cut_flat(weight_flat, layer_shapes()), saved_layers[layer_index]
        )
        layer_grads.insert(
            0,
            lax.psum_scatter(
                pack_flat(block_grads, weight_flat.shape[0]), "dev", scatter_dimension=0, tiled=True
            ),
        )
    grad_patch_w, grad_position, grad_cls, grad_mask_token = embed_backward(
        grad_stream, patches, masked_here
    )
    grad_extras = jnp.stack([grad_cls, grad_mask_token, grad_gain, grad_bias])
    stem_flat_grad = pack_flat(
        (grad_patch_w, grad_position, grad_extras) + head_grads, back_flat.shape[0]
    )
    stem_grad, proto_row_grad = (
        lax.psum_scatter(stem_flat_grad, "dev", scatter_dimension=0, tiled=True),
        lax.psum_scatter(grad_unit_protos, "dev", scatter_dimension=0, tiled=True),
    )
    own_protos = lax.optimization_barrier(protos.astype(narrow)).astype(single)
    proto_grad = jax.vjp(unit_rows, own_protos)[1](proto_row_grad)[0]
    layer_grad = jnp.stack(layer_grads)
    square_local = (
        jnp.sum(stem_grad * stem_grad)
        + jnp.sum(layer_grad * layer_grad)
        + jnp.sum(proto_grad * proto_grad)
    )
    square_total = lax.psum(square_local, "dev")
    grad_norm = jnp.sqrt(square_total) / count_total
    factor = jnp.minimum(1.0, clip_limit / (grad_norm + 1e-06)) / count_total
    new_centre = centre_keep * centre + (1.0 - centre_keep) * centre_total / count_total
    stem_set = adam_update(stem, stem_moment, stem_second, stem_grad * factor, stem_teacher)
    layer_set = adam_update(layers, layer_moment, layer_second, layer_grad * factor, layer_teacher)
    proto_set = adam_update(protos, proto_moment, proto_second, proto_grad * factor, proto_teacher)
    return (
        loss_total,
        count_total,
        grad_norm,
        new_centre,
        stem_set[0],
        stem_set[1],
        stem_set[2],
        stem_set[3],
        stem_set[4],
        layer_set[0],
        layer_set[1],
        layer_set[2],
        layer_set[3],
        layer_set[4],
        proto_set[0],
        proto_set[1],
        proto_set[2],
        proto_set[3],
        proto_set[4],
    )


GROUP = 16
ROW = HID
MATRIX_ROWS = D * 3 + D + FF + FF
EMBED_ROWS = PIX + SEQ + 4
EMBED_FLAT = EMBED_ROWS * D
HEAD_ROWS = D + HID + BOT
BITS = ("b", "a", "y", "x", "c")
MASKS = {"c": 1, "x": 2, "y": 4, "a": 8, "b": 24, "g": 8}


def head_bounds(count, stem_piece):
    bounds = [-(-(stem_piece * device - EMBED_FLAT) // (ROW * GROUP)) * GROUP for device in range(count + 1)]
    bounds[0] = -(-EMBED_FLAT // (ROW * GROUP)) * -GROUP
    bounds[-1] = HEAD_ROWS
    return bounds


def fits(count, stem_piece, layer_piece):
    if count != 1 << len(BITS) or MATRIX_ROWS % (3 * count):
        return False
    bounds = head_bounds(count, stem_piece)
    sizes = [bounds[i + 1] - bounds[i] for i in range(count)]
    return (
        min(sizes) > GROUP
        and bounds[1] <= 0
        and stem_piece < EMBED_FLAT <= 2 * stem_piece
        and D in bounds
        and D + HID in bounds
        and stem_piece * count == EMBED_FLAT + HEAD_ROWS * ROW
    )


def pairs(count, mask):
    return [(i, i ^ mask) for i in range(count)]


def bit_flags(me):
    flags = {name: (me >> (len(BITS) - 1 - place)) & 1 for place, name in enumerate(BITS)}
    flags["g"] = flags["a"] ^ flags["b"]
    return flags


def cube_gather(part, order):
    count = 1 << len(BITS)
    flags = bit_flags(lax.axis_index("dev"))
    held = part[None]
    for name in order:
        got = lax.ppermute(held, "dev", pairs(count, MASKS[name]))
        held = jnp.where(
            flags[name] == 1,
            jnp.concatenate([got, held], axis=0),
            jnp.concatenate([held, got], axis=0),
        )
    return held


def cut(array, names, name, lead):
    mine = bit_flags(lax.axis_index("dev"))[name]
    place = names.index(name) + lead
    sent = lax.dynamic_index_in_dim(array, 1 - mine, place, keepdims=False)
    kept = lax.dynamic_index_in_dim(array, mine, place, keepdims=False)
    return (sent if name == "c" else sent.astype(narrow)), kept, names.replace(name, "")


def move(sent, kept, name):
    return kept + lax.ppermute(sent, "dev", pairs(1 << len(BITS), MASKS[name])).astype(single)


def cube_scatter(array, names, order, lead=0):
    for name in order:
        sent, kept, names = cut(array, names, name, lead)
        array = move(sent, kept, name)
    return array


def cube_sum(values):
    for name in "cxyab":
        values = values + lax.ppermute(values, "dev", pairs(1 << len(BITS), MASKS[name]))
    return values


def split_bits(array, lead=0):
    return array.reshape(array.shape[:lead] + (2,) * len(BITS) + array.shape[lead + 1 :])


def step_pairs(count, step):
    return [(i, i + step) for i in range(count) if 0 <= i + step < count]


def lane_rows(length):
    return -(-length // 1024) * 8


def as_lanes(flat):
    rows = lane_rows(flat.shape[-1])
    gap = rows * 128 - flat.shape[-1]
    padded = jnp.pad(flat, [(0, 0)] * (flat.ndim - 1) + [(0, gap)])
    return padded.reshape(flat.shape[:-1] + (rows, 128))


def shifted(line_ref, row, lane, first, rows, stride):
    spots = lax.broadcasted_iota(jnp.int32, (rows, 128), 1)
    turn = lax.rem(128 - lane, 128)
    here = pltpu.roll(line_ref[pl.ds(row + first, rows, stride=stride), :], turn, 1)
    there = pltpu.roll(line_ref[pl.ds(row + first + 1, rows, stride=stride), :], turn, 1)
    return jnp.where(spots < 128 - lane, here, there)


def blocks_kernel(
    shape,
    place_ref,
    stem_ref,
    after_ref,
    layer_ref,
    before_ref,
    last_ref,
    head_ref,
    block_ref,
    embed_ref,
    vector_ref,
    line_ref,
    flat_ref,
):
    front, stem_piece, layer_piece, tail = shape
    stem_lines = stem_ref.shape[1]
    end_row, end_lane = stem_piece // 128, stem_piece % 128
    after_lines = after_ref.shape[1]
    slot = head_ref.shape[1]
    for model in range(2):
        line_ref[pl.ds(0, front), :] = jnp.zeros((front, 128), single)
        line_ref[pl.ds(front, end_row), :] = stem_ref[model, pl.ds(0, end_row), :]
        turned = pltpu.roll(after_ref[model], end_lane, 1)
        spots = lax.broadcasted_iota(jnp.int32, (after_lines, 128), 1)
        line_ref[pl.ds(front + end_row, after_lines), :] = turned
        line_ref[pl.ds(front + end_row + after_lines, 128), :] = jnp.zeros((128, 128), single)
        lower = pltpu.roll(turned, 1, 0)
        first_line = jnp.broadcast_to(stem_ref[model, pl.ds(end_row, 1), :], (after_lines, 128))
        number = lax.broadcasted_iota(jnp.int32, (after_lines, 128), 0)
        lower = jnp.where(number == 0, first_line, lower)
        line_ref[pl.ds(front + end_row, after_lines), :] = jnp.where(spots < end_lane, lower, turned)
        per_row = ROW // 128
        for chunk in range(per_row):
            head_ref[model, :, pl.ds(chunk * 128, 128)] = shifted(
                line_ref, place_ref[0], place_ref[1], chunk, slot, per_row
            ).astype(narrow)
        for chunk in range(D // 128):
            embed_ref[model, :, pl.ds(chunk * 128, 128)] = shifted(
                line_ref, place_ref[2], place_ref[3], chunk, embed_ref.shape[1], D // 128
            ).astype(narrow)
    tail_lines = tail // 128
    layer_lines = layer_ref.shape[1]
    for part in range(layer_ref.shape[0]):
        flat_ref[pl.ds(0, tail_lines), :] = before_ref[part]
        flat_ref[pl.ds(tail_lines, layer_lines), :] = layer_ref[part]
        for chunk in range(D // 128):
            block_ref[part, :, pl.ds(chunk * 128, 128)] = shifted(
                flat_ref, place_ref[4], place_ref[5], chunk, block_ref.shape[1], D // 128
            ).astype(narrow)
            vector_ref[part, :, pl.ds(chunk * 128, 128)] = last_ref[
                part, pl.ds(chunk, 8, stride=D // 128), :
            ].astype(narrow)


def own_blocks(place, stems, after, layer_rows, before, last_lines, shape, slot, block_rows, embed_rows):
    front, stem_piece, layer_piece, tail = shape
    lines = front + stem_piece // 128 + after.shape[1] + slot * ROW // 128
    flats = tail // 128 + layer_rows.shape[1] + 48
    return pl.pallas_call(
        lambda *refs: blocks_kernel(shape, *refs),
        out_shape=[
            jax.ShapeDtypeStruct((2, slot, ROW), narrow),
            jax.ShapeDtypeStruct((2 * LAYERS, block_rows, D), narrow),
            jax.ShapeDtypeStruct((2, embed_rows, D), narrow),
            jax.ShapeDtypeStruct((2 * LAYERS, 8, D), narrow),
        ],
        in_specs=[pl.BlockSpec(memory_space=pltpu.SMEM)] + [pl.BlockSpec(memory_space=pltpu.VMEM)] * 5,
        out_specs=[pl.BlockSpec(memory_space=pltpu.VMEM)] * 4,
        scratch_shapes=[pltpu.VMEM((lines, 128), single), pltpu.VMEM((flats, 128), single)],
        compiler_params=pltpu.CompilerParams(vmem_limit_bytes=40 << 20),
    )(place, stems, after, layer_rows, before, last_lines)


def shards_kernel(held, place_ref, head_ref, previous_ref, block_ref, behind_ref, *refs):
    stem_ref, layer_ref = refs[held : held + 2]
    line_ref, flat_ref = refs[-2:]
    per_row = ROW // 128
    extra = previous_ref.shape[0]
    slot = head_ref.shape[0]
    for chunk in range(per_row):
        spot = pl.ds(chunk * 128, 128)
        line_ref[pl.ds(chunk, extra, stride=per_row), :] = previous_ref[:, spot]
        line_ref[pl.ds(extra * per_row + chunk, slot, stride=per_row), :] = head_ref[:, spot]
    stem_ref[...] = shifted(line_ref, place_ref[0], place_ref[1], 0, stem_ref.shape[0], 1)
    per_row = D // 128
    rows = block_ref.shape[2]
    for part in range(block_ref.shape[0]):
        for chunk in range(per_row):
            flat_ref[pl.ds(chunk, rows, stride=per_row), :] = block_ref[part, chunk]
            flat_ref[pl.ds(rows * per_row + chunk, 6, stride=per_row), :] = behind_ref[part, chunk]
        layer_ref[part] = shifted(flat_ref, place_ref[2], place_ref[3], 0, layer_ref.shape[1], 1)


def own_shards(place, head_grad, previous, block_grad, behind, stem_lines, layer_lines, held):
    per_row = ROW // 128
    lines = (head_grad.shape[0] + previous.shape[0]) * per_row + 256
    flats = max(block_grad.shape[2] * 3 + 18, layer_lines + 18) + 16
    return pl.pallas_call(
        lambda *refs: shards_kernel(len(held), *refs),
        out_shape=[
            jax.ShapeDtypeStruct((stem_lines, 128), single),
            jax.ShapeDtypeStruct((block_grad.shape[0], layer_lines, 128), single),
        ]
        + [jax.ShapeDtypeStruct(array.shape, array.dtype) for array in held],
        in_specs=[pl.BlockSpec(memory_space=pltpu.SMEM)]
        + [pl.BlockSpec(memory_space=pltpu.VMEM)] * 4
        + [pl.BlockSpec(memory_space=pl.ANY)] * len(held),
        out_specs=[pl.BlockSpec(memory_space=pltpu.VMEM)] * 2 + [pl.BlockSpec(memory_space=pl.ANY)] * len(held),
        input_output_aliases={5 + number: 2 + number for number in range(len(held))},
        scratch_shapes=[pltpu.VMEM((lines, 128), single), pltpu.VMEM((flats, 128), single)],
        compiler_params=pltpu.CompilerParams(vmem_limit_bytes=40 << 20),
    )(place, head_grad, previous, block_grad, behind, *held)


PAD_SEQ = 272
GELU_SCALE = 0.7978845608028654
GELU_CUBE = 0.044715


def product_plain(left, right):
    return lax.dot_general(left, right, (((1,), (0,)), ((), ())), preferred_element_type=single)


def product_right(left, right):
    return lax.dot_general(left, right, (((1,), (1,)), ((), ())), preferred_element_type=single)


def product_left(left, right):
    return lax.dot_general(left, right, (((0,), (0,)), ((), ())), preferred_element_type=single)


def norm_parts(values):
    centred = values - jnp.mean(values, axis=-1, keepdims=True)
    spread = lax.rsqrt(jnp.mean(centred * centred, axis=-1, keepdims=True) + 1e-06)
    return centred * spread, spread


def norm_back(grad, unit, spread, gain):
    grad_unit = grad * gain
    mean_one = jnp.mean(grad_unit, axis=-1, keepdims=True)
    mean_two = jnp.mean(grad_unit * unit, axis=-1, keepdims=True)
    return spread * (grad_unit - mean_one - unit * mean_two)


def gelu_tanh(values):
    return jnp.tanh(GELU_SCALE * (values + GELU_CUBE * values * values * values))


def gelu_value(values):
    return 0.5 * values * (1.0 + gelu_tanh(values))


def gelu_slope(values):
    bent = gelu_tanh(values)
    return 0.5 * (1.0 + bent) + 0.5 * values * (1.0 - bent * bent) * GELU_SCALE * (
        1.0 + 3.0 * GELU_CUBE * values * values
    )


def head_copies(plan, side_ref, gathered_ref, one_ref, two_ref, lines_ref, sems):
    quarter = gathered_ref.shape[0] // 2
    shift = side_ref[0] * quarter
    targets = (one_ref, two_ref, lines_ref)
    copies = []
    for number, (at, owner, first, rows, target, row) in enumerate(plan):
        spot = at + shift if at < quarter else at - shift
        copies.append(
            pltpu.make_async_copy(
                gathered_ref.at[spot, owner, pl.ds(first, rows)],
                targets[target].at[pl.ds(row, rows)],
                sems.at[number],
            )
        )
    for copy in copies:
        copy.start()
    return [[copy for copy, item in zip(copies, plan) if item[4] == target] for target in range(3)]


def wait_all(copies):
    for copy in copies:
        copy.wait()


def spread_third(lines_ref, wide_ref, third_ref):
    groups = ROW // BOT
    for lane in range(BOT // 128):
        for group in range(groups):
            at = group * BOT + lane * 128
            wide_ref[lane, pl.ds(group, lines_ref.shape[0], stride=groups), :] = lines_ref[
                :, at : at + 128
            ].astype(single)
        third_ref[:, pl.ds(lane * 128, 128)] = wide_ref[lane].astype(narrow)


def head_up_kernel(
    plan, side_ref, normed_ref, gathered_ref, unit_ref, acts_ref, bottle_ref, pre_one_ref, pre_two_ref,
    one_ref, two_ref, lines_ref, wide_ref, third_ref, sems,
):
    copies = head_copies(plan, side_ref, gathered_ref, one_ref, two_ref, lines_ref, sems)
    acts_ref[...] = jnp.zeros_like(acts_ref)
    normed = normed_ref[...]
    acts_ref[:, pl.ds(0, D)] = normed
    piece = HID // 4
    wait_all(copies[0])
    for number in range(4):
        spot = pl.ds(number * piece, piece)
        pre = product_plain(normed, one_ref[:, spot])
        pre_one_ref[:, spot] = pre
        acts_ref[:, pl.ds(D + number * piece, piece)] = gelu_value(pre).astype(narrow)
    wait_all(copies[2])
    spread_third(lines_ref, wide_ref, third_ref)
    wait_all(copies[1])
    hidden = acts_ref[:, pl.ds(D, HID)]
    for number in range(4):
        spot = pl.ds(number * piece, piece)
        pre = product_plain(hidden, two_ref[:, spot])
        pre_two_ref[:, spot] = pre
        acts_ref[:, pl.ds(D + HID + number * piece, piece)] = gelu_value(pre).astype(narrow)
    bottle = product_plain(acts_ref[:, pl.ds(D + HID, HID)], third_ref[...])
    bottle_ref[...] = bottle
    unit_ref[...] = (
        bottle * lax.rsqrt(jnp.sum(bottle * bottle, axis=-1, keepdims=True) + 1e-06)
    ).astype(narrow)


def head_down_kernel(
    plan, side_ref, grad_ref, bottle_ref, pre_one_ref, pre_two_ref, gathered_ref, grads_ref, normed_grad_ref,
    one_ref, two_ref, lines_ref, wide_ref, third_ref, sems,
):
    copies = head_copies(plan, side_ref, gathered_ref, one_ref, two_ref, lines_ref, sems)
    grad, bottle = grad_ref[...], bottle_ref[...]
    scale = lax.rsqrt(jnp.sum(bottle * bottle, axis=-1, keepdims=True) + 1e-06)
    along = jnp.sum(grad * bottle, axis=-1, keepdims=True)
    grad_bottle = (scale * (grad - bottle * (along * scale * scale))).astype(narrow)
    grads_ref[:, pl.ds(2 * HID, BOT)] = grad_bottle
    wait_all(copies[2])
    spread_third(lines_ref, wide_ref, third_ref)
    piece = HID // 4
    for number in range(4):
        spot = pl.ds(number * piece, piece)
        back = product_right(grad_bottle, third_ref[spot, :])
        grads_ref[:, pl.ds(HID + number * piece, piece)] = (back * gelu_slope(pre_two_ref[:, spot])).astype(narrow)
    wait_all(copies[1])
    grad_two = grads_ref[:, pl.ds(HID, HID)]
    for number in range(4):
        spot = pl.ds(number * piece, piece)
        back = product_right(grad_two, two_ref[spot, :])
        grads_ref[:, spot] = (back * gelu_slope(pre_one_ref[:, spot])).astype(narrow)
    wait_all(copies[0])
    normed_grad_ref[...] = product_right(grads_ref[:, pl.ds(0, HID)], one_ref[...])


def head_pass(kernel, plan, side, inputs, gathered, shapes, waits=()):
    read = len(inputs) + 2
    return pl.pallas_call(
        lambda *refs: kernel(plan, *refs[:read], *refs[read + len(waits) :]),
        out_shape=shapes,
        in_specs=[pl.BlockSpec(memory_space=pltpu.SMEM)]
        + [pl.BlockSpec(memory_space=pltpu.VMEM)] * len(inputs)
        + [pl.BlockSpec(memory_space=pl.ANY)] * (1 + len(waits)),
        out_specs=[pl.BlockSpec(memory_space=pltpu.VMEM)] * len(shapes),
        scratch_shapes=[
            pltpu.VMEM((D, HID), narrow),
            pltpu.VMEM((HID, HID), narrow),
            pltpu.VMEM((BOT, ROW), narrow),
            pltpu.VMEM((BOT // 128, HID, 128), single),
            pltpu.VMEM((HID, BOT), narrow),
            pltpu.SemaphoreType.DMA((len(plan),)),
        ],
        compiler_params=pltpu.CompilerParams(vmem_limit_bytes=56 << 20),
        cost_estimate=pl.CostEstimate(flops=100 * 10**6, bytes_accessed=370 * 10**5, transcendentals=0),
    )(side, *inputs, gathered, *waits)


def fetch_rows(side_ref, part, gathered_ref, flat_ref, sems, first_row, last_row):
    quarter = flat_ref.shape[0] // 4
    side = side_ref[0]
    first, second = side * quarter, (1 - side) * quarter
    copies = [
        pltpu.make_async_copy(
            gathered_ref.at[pl.ds(at, quarter), owner, part],
            flat_ref.at[pl.ds(spot * quarter, quarter)],
            sems.at[spot],
        )
        for spot, (at, owner) in enumerate(((first, 0), (second, 0), (second, 1), (first, 1)))
        if spot * quarter * flat_ref.shape[1] < last_row and first_row < (spot + 1) * quarter * flat_ref.shape[1]
    ]
    for copy in copies:
        copy.start()
    return copies


def matrix_rows(flat_ref, first_row, length):
    rows = flat_ref.shape[1]
    low, high = first_row // rows, -(-(first_row + length) // rows)
    lines = flat_ref[pl.ds(low, high - low)].reshape((high - low) * rows, D)
    at = first_row - low * rows
    return lines[at : at + length]


def spread_columns(flat_ref, first_row, width, wide_ref, out_ref):
    length = width * D
    lines = matrix_rows(flat_ref, first_row, length)
    for column in range(D // 128):
        lane = slice(column * 128, (column + 1) * 128)
        wide_ref[column, pl.ds(0, length), :] = lines[:, lane].astype(single)
    for group in range(width):
        for column in range(D // 128):
            out_ref[group, :, pl.ds(column * 128, 128)] = wide_ref[
                column, pl.ds(group, D, stride=width), :
            ].astype(narrow)


def head_lanes(values, odd):
    lanes = lax.broadcasted_iota(jnp.int32, values.shape, 1)
    return jnp.where((lanes >= HEAD_DIM) == odd, values, jnp.zeros_like(values))


def join_lanes(even, odd):
    lanes = lax.broadcasted_iota(jnp.int32, even.shape, 1)
    return jnp.where(lanes >= HEAD_DIM, odd, even)


def soft_rows(query, key):
    scores = product_right(query, key) * HEAD_DIM ** (-0.5)
    spots = lax.broadcasted_iota(jnp.int32, scores.shape, 1)
    scores = jnp.where(spots < SEQ, scores, -1e30)
    terms = jnp.exp(scores - jnp.max(scores, axis=-1, keepdims=True))
    return terms / jnp.sum(terms, axis=-1, keepdims=True)


def forward_kernel(part, keep, side_ref, stream_ref, vector_ref, gathered_ref, *refs):
    out_ref = refs[0]
    if keep:
        packed_ref, mixed_ref, attn_ref, pre_ref, mlp_ref = refs[1:6]
        flat_ref, wide_ref, qkv_ref, up_ref, hidden_ref, sems = refs[6:]
    else:
        flat_ref, wide_ref, qkv_ref, up_ref, hidden_ref, packed_ref, mixed_ref, sems = refs[1:]
    copies = fetch_rows(side_ref, part, gathered_ref, flat_ref, sems, 0, MATRIX_ROWS)
    vectors = vector_ref[...].astype(single)
    stream = stream_ref[...]
    normed = (norm_parts(stream)[0] * vectors[0:1] + vectors[1:2]).astype(narrow)
    wait_all(copies)
    spread_columns(flat_ref, 0, 3, wide_ref, qkv_ref)
    spread_columns(flat_ref, 4 * D, FF // D, wide_ref, up_ref)
    w_proj = matrix_rows(flat_ref, 3 * D, D)
    w_down = matrix_rows(flat_ref, 4 * D + FF, FF)
    for group in range(3):
        packed_ref[:, pl.ds(group * D, D)] = product_plain(normed, qkv_ref[group]).astype(narrow)
    for image in range(stream.shape[0] // PAD_SEQ):
        rows = pl.ds(image * PAD_SEQ, PAD_SEQ)
        for pair in range(HEADS // 2):
            query, key, value = [
                packed_ref[rows, pl.ds(group * D + pair * 128, 128)] for group in range(3)
            ]
            done = [
                product_plain(soft_rows(head_lanes(query, odd), key).astype(narrow), value)
                for odd in (False, True)
            ]
            mixed_ref[rows, pl.ds(pair * 128, 128)] = join_lanes(*done).astype(narrow)
    attn = product_plain(mixed_ref[...], w_proj)
    middle = stream + vectors[2:3] * attn
    normed_two = (norm_parts(middle)[0] * vectors[3:4] + vectors[4:5]).astype(narrow)
    for group in range(FF // D):
        spot = pl.ds(group * D, D)
        pre = product_plain(normed_two, up_ref[group])
        if keep:
            pre_ref[:, spot] = pre
        hidden_ref[:, spot] = (0.5 * pre * (1.0 + gelu_tanh(pre))).astype(narrow)
    mlp = product_plain(hidden_ref[...], w_down)
    out_ref[...] = middle + vectors[5:6] * mlp
    if keep:
        attn_ref[...] = attn
        mlp_ref[...] = mlp


def layer_scratch(gathered):
    rows, blocks = gathered.shape[3], 2 * gathered.shape[0]
    return [
        pltpu.VMEM((blocks, rows, D), narrow),
        pltpu.VMEM((D // 128, FF, 128), single),
        pltpu.VMEM((3, D, D), narrow),
        pltpu.VMEM((FF // D, D, D), narrow),
    ]


def layer_specs_in(count):
    return (
        [pl.BlockSpec(memory_space=pltpu.SMEM)]
        + [pl.BlockSpec(memory_space=pltpu.VMEM)] * (count - 2)
        + [pl.BlockSpec(memory_space=pl.ANY)]
    )


def layer_forward(side, stream, vectors, gathered, part, keep):
    tokens = stream.shape[0]
    shapes = [jax.ShapeDtypeStruct((tokens, D), single)]
    extra = [
        jax.ShapeDtypeStruct((tokens, 3 * D), narrow),
        jax.ShapeDtypeStruct((tokens, D), narrow),
        jax.ShapeDtypeStruct((tokens, D), single),
        jax.ShapeDtypeStruct((tokens, FF), single),
        jax.ShapeDtypeStruct((tokens, D), single),
    ]
    scratch = layer_scratch(gathered) + [pltpu.VMEM((tokens, FF), narrow)]
    if keep:
        shapes = shapes + extra
    else:
        scratch = scratch + [pltpu.VMEM((tokens, 3 * D), narrow), pltpu.VMEM((tokens, D), narrow)]
    scratch.append(pltpu.SemaphoreType.DMA((4,)))
    return pl.pallas_call(
        lambda *refs: forward_kernel(part, keep, *refs),
        out_shape=shapes,
        in_specs=layer_specs_in(4),
        out_specs=[pl.BlockSpec(memory_space=pltpu.VMEM)] * len(shapes),
        scratch_shapes=scratch,
        compiler_params=pltpu.CompilerParams(vmem_limit_bytes=56 << 20),
        cost_estimate=pl.CostEstimate(flops=100 * 10**6, bytes_accessed=430 * 10**5, transcendentals=0),
    )(side, stream, vectors, gathered)


def mlp_back_kernel(
    part,
    side_ref,
    grad_ref,
    stream_ref,
    attn_ref,
    pre_ref,
    mlp_ref,
    vector_ref,
    gathered_ref,
    *refs,
):
    grad_mid_ref, weight_grad_ref, vector_grad_ref = refs[-9:-6]
    flat_ref, wide_ref, up_ref, hidden_ref, grad_pre_ref, sems = refs[-6:]
    lead = weight_grad_ref.shape[1] - 2 * FF
    weight_grad_ref[:, pl.ds(0, lead), :] = jnp.zeros((D // 128, lead, 128), single)
    copies = fetch_rows(side_ref, part, gathered_ref, flat_ref, sems, 4 * D, MATRIX_ROWS)
    vectors = vector_ref[...].astype(single)
    grad_out = grad_ref[...]
    vector_grad_ref[...] = jnp.zeros_like(vector_grad_ref)
    attn = attn_ref[...]
    middle = stream_ref[...] + vectors[2:3] * attn
    unit_two, spread_two = norm_parts(middle)
    normed_two = (unit_two * vectors[3:4] + vectors[4:5]).astype(narrow)
    vector_grad_ref[pl.ds(5, 1), :] = jnp.sum(grad_out * mlp_ref[...], axis=0, keepdims=True)
    grad_mlp = (grad_out * vectors[5:6]).astype(narrow)
    wait_all(copies)
    spread_columns(flat_ref, 4 * D, FF // D, wide_ref, up_ref)
    w_down = matrix_rows(flat_ref, 4 * D + FF, FF)
    grad_normed_two = jnp.zeros_like(grad_out)
    for group in range(FF // D):
        spot = pl.ds(group * D, D)
        pre = pre_ref[:, spot]
        bent = gelu_tanh(pre)
        hidden_ref[:, spot] = (0.5 * pre * (1.0 + bent)).astype(narrow)
        slope = 0.5 * (1.0 + bent) + 0.5 * pre * (1.0 - bent * bent) * GELU_SCALE * (
            1.0 + 3.0 * GELU_CUBE * pre * pre
        )
        grad_hidden = product_right(grad_mlp, w_down[group * D : (group + 1) * D])
        grad_pre = (grad_hidden * slope).astype(narrow)
        grad_pre_ref[:, spot] = grad_pre
        grad_normed_two = grad_normed_two + product_right(grad_pre, up_ref[group])
    for group in range(FF // D):
        spot = pl.ds(group * D, D)
        up_grad = product_left(normed_two, grad_pre_ref[:, spot])
        down_grad = product_left(hidden_ref[:, spot], grad_mlp)
        for column in range(D // 128):
            lane = slice(column * 128, (column + 1) * 128)
            weight_grad_ref[column, pl.ds(lead + group, D, stride=FF // D), :] = up_grad[:, lane]
            weight_grad_ref[column, pl.ds(lead + FF + group * D, D), :] = down_grad[:, lane]
    vector_grad_ref[pl.ds(3, 1), :] = jnp.sum(grad_normed_two * unit_two, axis=0, keepdims=True)
    vector_grad_ref[pl.ds(4, 1), :] = jnp.sum(grad_normed_two, axis=0, keepdims=True)
    grad_mid = grad_out + norm_back(grad_normed_two, unit_two, spread_two, vectors[3:4])
    vector_grad_ref[pl.ds(2, 1), :] = jnp.sum(grad_mid * attn, axis=0, keepdims=True)
    grad_mid_ref[...] = grad_mid


def attention_back_kernel(
    part,
    side_ref,
    grad_ref,
    stream_ref,
    packed_ref,
    mixed_ref,
    vector_ref,
    gathered_ref,
    *refs,
):
    grad_in_ref, weight_grad_ref, vector_grad_ref = refs[-9:-6]
    flat_ref, wide_ref, qkv_ref, grad_mixed_ref, grad_packed_ref, sems = refs[-6:]
    rest = weight_grad_ref.shape[1] - 4 * D
    weight_grad_ref[:, pl.ds(4 * D, rest), :] = jnp.zeros((D // 128, rest, 128), single)
    copies = fetch_rows(side_ref, part, gathered_ref, flat_ref, sems, 0, 4 * D)
    vectors = vector_ref[...].astype(single)
    vector_grad_ref[...] = jnp.zeros_like(vector_grad_ref)
    grad_mid = grad_ref[...]
    stream = stream_ref[...]
    grad_attn = (grad_mid * vectors[2:3]).astype(narrow)
    proj_grad = product_left(mixed_ref[...], grad_attn)
    for column in range(D // 128):
        weight_grad_ref[column, pl.ds(3 * D, D), :] = proj_grad[:, column * 128 : (column + 1) * 128]
    wait_all(copies)
    spread_columns(flat_ref, 0, 3, wide_ref, qkv_ref)
    w_proj = matrix_rows(flat_ref, 3 * D, D)
    grad_mixed_ref[...] = product_right(grad_attn, w_proj).astype(narrow)
    for image in range(stream.shape[0] // PAD_SEQ):
        rows = pl.ds(image * PAD_SEQ, PAD_SEQ)
        for pair in range(HEADS // 2):
            query, key, value = [
                packed_ref[rows, pl.ds(group * D + pair * 128, 128)] for group in range(3)
            ]
            grad_mixed = grad_mixed_ref[rows, pl.ds(pair * 128, 128)]
            parts = []
            for odd in (False, True):
                probs = soft_rows(head_lanes(query, odd), key)
                grad_probs = product_right(head_lanes(grad_mixed, odd), value)
                grad_value = product_left(probs.astype(narrow), grad_mixed)
                grad_scores = probs * (grad_probs - jnp.sum(probs * grad_probs, axis=-1, keepdims=True))
                grad_raw = (grad_scores * HEAD_DIM ** (-0.5)).astype(narrow)
                parts.append((product_plain(grad_raw, key), product_left(grad_raw, query), grad_value))
            for group in range(3):
                grad_packed_ref[rows, pl.ds(group * D + pair * 128, 128)] = join_lanes(
                    parts[0][group], parts[1][group]
                ).astype(narrow)
    unit_one, spread_one = norm_parts(stream)
    normed = (unit_one * vectors[0:1] + vectors[1:2]).astype(narrow)
    grad_normed = jnp.zeros_like(grad_mid)
    for group in range(3):
        grad_part = grad_packed_ref[:, pl.ds(group * D, D)]
        grad_normed = grad_normed + product_right(grad_part, qkv_ref[group])
        qkv_grad = product_left(normed, grad_part)
        for column in range(D // 128):
            lane = slice(column * 128, (column + 1) * 128)
            weight_grad_ref[column, pl.ds(group, D, stride=3), :] = qkv_grad[:, lane]
    vector_grad_ref[pl.ds(0, 1), :] = jnp.sum(grad_normed * unit_one, axis=0, keepdims=True)
    vector_grad_ref[pl.ds(1, 1), :] = jnp.sum(grad_normed, axis=0, keepdims=True)
    grad_in_ref[...] = grad_mid + norm_back(grad_normed, unit_one, spread_one, vectors[0:1])


def layer_back(kernel, part, weight_rows, side, inputs, vectors, gathered, waits, held, columns, buffers):
    tokens = inputs[0].shape[0]
    rows, blocks = gathered.shape[3], 2 * gathered.shape[0]
    return pl.pallas_call(
        lambda *refs: kernel(part, *refs[: len(refs) - 6 - len(held)], *refs[len(refs) - 6 :]),
        out_shape=[
            jax.ShapeDtypeStruct((tokens, D), single),
            jax.ShapeDtypeStruct((D // 128, weight_rows, 128), single),
            jax.ShapeDtypeStruct((8, D), single),
        ]
        + [jax.ShapeDtypeStruct(array.shape, array.dtype) for array in held],
        in_specs=layer_specs_in(len(inputs) + 3) + [pl.BlockSpec(memory_space=pl.ANY)] * (len(waits) + len(held)),
        out_specs=[pl.BlockSpec(memory_space=pltpu.VMEM)] * 3 + [pl.BlockSpec(memory_space=pl.ANY)] * len(held),
        input_output_aliases={len(inputs) + 3 + len(waits) + number: 3 + number for number in range(len(held))},
        scratch_shapes=[
            pltpu.VMEM((blocks, rows, D), narrow),
            pltpu.VMEM((D // 128, columns * D, 128), single),
            pltpu.VMEM((columns, D, D), narrow),
        ]
        + [pltpu.VMEM((tokens, width), narrow) for width in buffers]
        + [pltpu.SemaphoreType.DMA((4,))],
        compiler_params=pltpu.CompilerParams(vmem_limit_bytes=56 << 20),
        cost_estimate=pl.CostEstimate(flops=100 * 10**6, bytes_accessed=600 * 10**5, transcendentals=0),
    )(side, *inputs, vectors, gathered, *waits, *held)


def pair_rows_of(block_rows):
    pair = 2 * block_rows
    return 4 * D // pair * pair, -(-4 * D // pair) * pair


def mlp_back(side, grad_out, saved, vectors, gathered, part, waits, held):
    stream, packed, mixed, attn, pre, mlp = saved
    return layer_back(
        mlp_back_kernel, part, MATRIX_ROWS - pair_rows_of(gathered.shape[3])[0], side,
        (grad_out, stream, attn, pre, mlp), vectors, gathered, waits, held,
        FF // D, (FF, FF),
    )


def attention_back(side, grad_mid, saved, vectors, gathered, part, waits, held):
    stream, packed, mixed, attn, pre, mlp = saved
    return layer_back(
        attention_back_kernel, part, pair_rows_of(gathered.shape[3])[1], side,
        (grad_mid, stream, packed, mixed), vectors, gathered, waits, held,
        3, (D, 3 * D),
    )


def after(value, *tokens):
    def kernel(*refs):
        refs[-1][...] = refs[0][...]

    return pl.pallas_call(
        kernel,
        out_shape=jax.ShapeDtypeStruct(value.shape, value.dtype),
        in_specs=[pl.BlockSpec(memory_space=pltpu.VMEM)] + [pl.BlockSpec(memory_space=pl.ANY)] * len(tokens),
        out_specs=pl.BlockSpec(memory_space=pltpu.VMEM),
    )(value, *tokens)


def embed_back_kernel(grad_ref, patch_ref, shown_ref, gain_ref, vector_ref, *refs):
    out_ref = refs[-1]
    grad = grad_ref[...]
    images = grad.shape[0] // PAD_SEQ
    shown = shown_ref[...]
    position = jnp.zeros((PAD_SEQ, D), single)
    token = jnp.zeros((1, D), single)
    patch_grads = []
    for image in range(images):
        here = grad[image * PAD_SEQ : (image + 1) * PAD_SEQ]
        position = position + here
        rows = here[1:SEQ]
        seen = shown[image * PATCHES : (image + 1) * PATCHES]
        token = token + jnp.sum(rows * (1.0 - seen), axis=0, keepdims=True)
        patch_grads.append((rows * seen).astype(narrow))
    patch_grad = product_left(patch_ref[...], jnp.concatenate(patch_grads))
    out_ref[...] = jnp.zeros_like(out_ref)
    for column in range(D // 128):
        lane = slice(column * 128, (column + 1) * 128)
        out_ref[column, pl.ds(0, PIX), :] = patch_grad[:, lane]
        out_ref[column, pl.ds(PIX, SEQ), :] = position[:SEQ, lane]
        out_ref[column, pl.ds(PIX + SEQ, 1), :] = position[0:1, lane]
        out_ref[column, pl.ds(PIX + SEQ + 1, 1), :] = token[:, lane]
        out_ref[column, pl.ds(PIX + SEQ + 2, 2), :] = gain_ref[:, lane]
        out_ref[column, pl.ds(EMBED_ROWS, vector_ref.shape[0]), :] = vector_ref[:, lane]


def embed_back(grad, patch_rows, shown, gains, vector_grads, rows, waits):
    return pl.pallas_call(
        embed_back_kernel,
        out_shape=jax.ShapeDtypeStruct((D // 128, rows, 128), single),
        in_specs=[pl.BlockSpec(memory_space=pltpu.VMEM)] * 5 + [pl.BlockSpec(memory_space=pl.ANY)] * len(waits),
        out_specs=pl.BlockSpec(memory_space=pltpu.VMEM),
        compiler_params=pltpu.CompilerParams(vmem_limit_bytes=40 << 20),
        cost_estimate=pl.CostEstimate(flops=100 * 10**6, bytes_accessed=37 * 10**5, transcendentals=0),
    )(grad, patch_rows, shown, gains, vector_grads, *waits)


def proto_units(values):
    rounded = values.astype(narrow).astype(single)
    scale = lax.rsqrt(jnp.sum(rounded * rounded, axis=-1, keepdims=True) + 1e-06)
    return rounded, scale, (rounded * scale).astype(narrow)


def proto_terms(teacher_z, student_z, teacher_unit, student_unit, centre_column):
    teacher_logits = product_right(teacher_unit, teacher_z)
    logits = product_right(student_unit, student_z)
    teacher_exp = jnp.exp((teacher_logits - centre_column) * (1.0 / tau_teacher))
    student_exp = jnp.exp(logits * (1.0 / tau_student))
    return teacher_logits, logits, teacher_exp, student_exp


def logits_kernel(
    teacher_z_ref,
    student_z_ref,
    teacher_ref,
    student_ref,
    centre_ref,
    class_ref,
    mixed_ref,
    mixed_teacher_ref,
    sums_ref,
    centre_sum_ref,
    student_mix_ref,
    teacher_mix_ref,
    totals_ref,
):
    step = pl.program_id(0)

    @pl.when(step == 0)
    def _():
        student_mix_ref[...] = jnp.zeros_like(student_mix_ref)
        teacher_mix_ref[...] = jnp.zeros_like(teacher_mix_ref)
        totals_ref[...] = jnp.zeros_like(totals_ref)

    teacher_unit = proto_units(teacher_ref[...])[2]
    student_unit = proto_units(student_ref[...])[2]
    teacher_logits, logits, teacher_exp, student_exp = proto_terms(
        teacher_z_ref[...], student_z_ref[...], teacher_unit, student_unit, centre_ref[...]
    )
    totals_ref[pl.ds(0, 1), :] += jnp.sum(teacher_exp, axis=0, keepdims=True)
    totals_ref[pl.ds(1, 1), :] += jnp.sum(student_exp, axis=0, keepdims=True)
    totals_ref[pl.ds(2, 1), :] += jnp.sum(teacher_exp * logits, axis=0, keepdims=True)
    centre_sum_ref[...] = jnp.sum(teacher_logits * class_ref[0:1], axis=1, keepdims=True)
    student_mix_ref[...] += product_left(student_unit, student_exp.astype(narrow))
    teacher_mix_ref[...] += product_left(student_unit, teacher_exp.astype(narrow))

    @pl.when(step == pl.num_programs(0) - 1)
    def _():
        mixed_ref[...] = student_mix_ref[...].T
        mixed_teacher_ref[:, pl.ds(0, BOT)] = teacher_mix_ref[...].T
        lower = jnp.zeros((128 - totals_ref.shape[0], totals_ref.shape[1]), single)
        mixed_teacher_ref[:, pl.ds(BOT, 128)] = jnp.concatenate([totals_ref[...], lower]).T
        sums_ref[...] = totals_ref[...]


def proto_specs(rows, block):
    whole = pl.BlockSpec((rows, BOT), lambda i: (0, 0))
    table = pl.BlockSpec((block, BOT), lambda i: (i, 0))
    column = pl.BlockSpec((block, 1), lambda i: (i, 0))
    lines = pl.BlockSpec((8, rows), lambda i: (0, 0))
    return whole, table, column, lines


def logits_pass(teacher_z, student_z, teacher, student, centre_column, class_lines):
    rows, protos_here = teacher_z.shape[0], student.shape[0]
    block = protos_here // 4
    whole, table, column, lines = proto_specs(rows, block)
    return pl.pallas_call(
        logits_kernel,
        grid=(4,),
        out_shape=[
            jax.ShapeDtypeStruct((rows, BOT), single),
            jax.ShapeDtypeStruct((rows, BOT + 128), single),
            jax.ShapeDtypeStruct((8, rows), single),
            jax.ShapeDtypeStruct((protos_here, 1), single),
        ],
        in_specs=[whole, whole, table, table, column, lines],
        out_specs=[whole, pl.BlockSpec((rows, BOT + 128), lambda i: (0, 0)), lines, column],
        scratch_shapes=[
            pltpu.VMEM((BOT, rows), single),
            pltpu.VMEM((BOT, rows), single),
            pltpu.VMEM((8, rows), single),
        ],
        compiler_params=pltpu.CompilerParams(vmem_limit_bytes=56 << 20),
        cost_estimate=pl.CostEstimate(flops=100 * 10**6, bytes_accessed=520 * 10**5, transcendentals=0),
    )(teacher_z, student_z, teacher, student, centre_column, class_lines)


def proto_grad_kernel(
    held, teacher_z_ref, student_z_ref, teacher_ref, student_ref, centre_ref, scale_ref, *refs
):
    grad_ref, square_ref = refs[held : held + 2]
    step = pl.program_id(0)

    @pl.when(step == 0)
    def _():
        square_ref[...] = jnp.zeros_like(square_ref)

    teacher_unit = proto_units(teacher_ref[...])[2]
    rounded, scale, student_unit = proto_units(student_ref[...])
    student_z = student_z_ref[...]
    _, _, teacher_exp, student_exp = proto_terms(
        teacher_z_ref[...], student_z, teacher_unit, student_unit, centre_ref[...]
    )
    grad_logits = (student_exp * scale_ref[0:1] - teacher_exp * scale_ref[1:2]).astype(narrow)
    unit_grad = product_plain(grad_logits, student_z)
    along = jnp.sum(unit_grad * rounded, axis=-1, keepdims=True)
    grad = scale * (unit_grad - rounded * (along * scale * scale))
    grad_ref[...] = grad
    square_ref[...] += jnp.broadcast_to(jnp.sum(grad * grad), square_ref.shape)


def proto_grad_pass(teacher_z, student_z, teacher, student, centre_column, scale_lines, held):
    rows, protos_here = teacher_z.shape[0], student.shape[0]
    block = protos_here // 4
    whole, table, column, lines = proto_specs(rows, block)
    return pl.pallas_call(
        lambda *refs: proto_grad_kernel(len(held), *refs),
        grid=(4,),
        out_shape=[
            jax.ShapeDtypeStruct((protos_here, BOT), single),
            jax.ShapeDtypeStruct((8, 128), single),
        ]
        + [jax.ShapeDtypeStruct(array.shape, array.dtype) for array in held],
        in_specs=[whole, whole, table, table, column, lines]
        + [pl.BlockSpec(memory_space=pl.ANY)] * len(held),
        out_specs=[table, pl.BlockSpec((8, 128), lambda i: (0, 0))]
        + [pl.BlockSpec(memory_space=pl.ANY)] * len(held),
        input_output_aliases={6 + number: 2 + number for number in range(len(held))},
        compiler_params=pltpu.CompilerParams(vmem_limit_bytes=56 << 20),
        cost_estimate=pl.CostEstimate(flops=100 * 10**6, bytes_accessed=400 * 10**5, transcendentals=0),
    )(teacher_z, student_z, teacher, student, centre_column, scale_lines, *held)


def proto_update(factor, student, moment, second, teacher, grad):
    def kernel(factor_ref, *refs):
        weight, moment, second, teacher, grad = [ref[...] for ref in refs[:5]]
        done = adam_update(weight, moment, second, grad * factor_ref[0], teacher)
        for ref, value in zip(refs[5:], done):
            ref[...] = value

    block = student.shape[0] // 4
    table = pl.BlockSpec((block, BOT), lambda i: (i, 0))
    return pl.pallas_call(
        kernel,
        grid=(4,),
        out_shape=[
            jax.ShapeDtypeStruct(student.shape, narrow if number == 3 else single) for number in range(5)
        ],
        in_specs=[pl.BlockSpec(memory_space=pltpu.SMEM)] + [table] * 5,
        out_specs=[table] * 5,
        compiler_params=pltpu.CompilerParams(vmem_limit_bytes=60 << 20),
        cost_estimate=pl.CostEstimate(flops=10**7, bytes_accessed=2 * 10**7, transcendentals=0),
    )(factor.reshape(1), student, moment, second, teacher, grad)


def head_grads_kernel(
    held, place_ref, inputs_ref, grads_ref, *refs,
):
    own_ref, partner_ref = refs[len(refs) - 9 - held :][:2] if held else refs[-9:-7]
    window_ref, rows_ref, product_ref, third_ref, bottle_ref, line_ref, sems = refs[-7:]
    slot = own_ref.shape[0]
    lead = product_ref.shape[0] - window_ref.shape[1]
    number = lax.broadcasted_iota(jnp.int32, (slot, 1), 0)
    product_ref[pl.ds(0, lead), :] = jnp.zeros((lead, ROW), single)

    def block(at, out_ref):
        column = pl.multiple_of(place_ref[at], 128)
        grad_column = pl.multiple_of(place_ref[at + 3], 128)
        copies = [
            pltpu.make_async_copy(
                inputs_ref.at[:, pl.ds(column, window_ref.shape[1])], window_ref, sems.at[0]
            ),
            pltpu.make_async_copy(grads_ref.at[:, pl.ds(grad_column, ROW)], rows_ref, sems.at[1]),
        ]
        for copy in copies:
            copy.start()
        for copy in copies:
            copy.wait()
        window = window_ref[...]
        for piece in range(4):
            spot = pl.ds(piece * (ROW // 4), ROW // 4)
            product_ref[pl.ds(lead, window.shape[1]), spot] = product_left(window, rows_ref[:, spot])
        from_row = pl.multiple_of(lead + place_ref[at + 1], 8)
        kept = jnp.where(number < place_ref[at + 2], product_ref[pl.ds(from_row, slot), :], 0.0)
        out_ref[...] = kept.astype(out_ref.dtype)

    @pl.when(place_ref[8] == 0)
    def _():
        block(0, own_ref)

    @pl.when(place_ref[8] == 1)
    def _():
        column = pl.multiple_of(place_ref[9], 128)
        copies = [
            pltpu.make_async_copy(
                inputs_ref.at[:, pl.ds(column, third_ref.shape[1])], third_ref, sems.at[0]
            ),
            pltpu.make_async_copy(grads_ref.at[:, pl.ds(2 * HID, BOT)], bottle_ref, sems.at[1]),
        ]
        for copy in copies:
            copy.start()
        for copy in copies:
            copy.wait()
        third = product_left(third_ref[...], bottle_ref[...])
        for lane in range(BOT // 128):
            line_ref[lane] = third[:, lane * 128 : (lane + 1) * 128]
        for group in range(ROW // BOT):
            for lane in range(BOT // 128):
                value = line_ref[lane, pl.ds(group, slot, stride=ROW // BOT), :]
                own_ref[:, pl.ds(group * BOT + lane * 128, 128)] = jnp.where(
                    number < place_ref[2], value, 0.0
                )

    block(4, partner_ref)


def head_grads(place, inputs_all, grads_all, slot, lead, waits, held):
    rows = inputs_all.shape[0]
    wide = slot * ROW // BOT
    return pl.pallas_call(
        lambda *refs: head_grads_kernel(len(held), *refs),
        out_shape=[jax.ShapeDtypeStruct((slot, ROW), kind) for kind in (single, narrow)]
        + [jax.ShapeDtypeStruct(array.shape, array.dtype) for array in held],
        in_specs=[pl.BlockSpec(memory_space=pltpu.SMEM)]
        + [pl.BlockSpec(memory_space=pl.ANY)] * (2 + len(waits) + len(held)),
        out_specs=[pl.BlockSpec(memory_space=pltpu.VMEM)] * 2
        + [pl.BlockSpec(memory_space=pl.ANY)] * len(held),
        input_output_aliases={3 + len(waits) + number: 2 + number for number in range(len(held))},
        scratch_shapes=[
            pltpu.VMEM((rows, 256), narrow),
            pltpu.VMEM((rows, ROW), narrow),
            pltpu.VMEM((lead + 256, ROW), single),
            pltpu.VMEM((rows, wide), narrow),
            pltpu.VMEM((rows, BOT), narrow),
            pltpu.VMEM((BOT // 128, wide, 128), single),
            pltpu.SemaphoreType.DMA((2,)),
        ],
        compiler_params=pltpu.CompilerParams(vmem_limit_bytes=56 << 20),
        cost_estimate=pl.CostEstimate(flops=100 * 10**6, bytes_accessed=370 * 10**5, transcendentals=0),
    )(place, inputs_all, grads_all, *waits, *held)


def close_local(
    patches,
    masked,
    slot_used,
    stem,
    stem_moment,
    stem_second,
    stem_teacher,
    layers,
    layer_moment,
    layer_second,
    layer_teacher,
    protos,
    proto_moment,
    proto_second,
    proto_teacher,
    centre,
):
    count = 1 << len(BITS)
    half = count // 2
    me = lax.axis_index("dev")
    across = MASKS["b"]
    student_side = me >= half
    groups = [list(range(half)), list(range(half, count))]
    quarter = half // 2
    swap = jnp.where(student_side, quarter, 0)
    side = student_side.astype(jnp.int32).reshape(1)
    images_here = patches.shape[0]
    rows_here = images_here * 17
    pair_rows = -(-2 * rows_here // 16) * 16
    more_rows = pair_rows - 2 * rows_here
    stem_piece = stem.shape[0]
    layer_piece = layers.shape[1]
    block_rows = MATRIX_ROWS // count
    block = block_rows * D
    tail = layer_piece * count - MATRIX_ROWS * D
    drift = layer_piece - block
    bounds = head_bounds(count, stem_piece)
    sizes = [bounds[i + 1] - bounds[i] for i in range(count)]
    slot = max(sizes)
    starts = [b * ROW + EMBED_FLAT - stem_piece * i for i, b in enumerate(bounds[:-1])]
    first_w2 = bounds.index(D)
    first_w3 = bounds.index(D + HID)
    row_index = jnp.concatenate([jnp.zeros((images_here, 1), jnp.int32), masked + 1], axis=1)
    masked_here = jnp.any(
        masked[:, :, None] == jnp.arange(PATCHES, dtype=jnp.int32)[None, None, :], axis=1
    )
    kept = slot_used.astype(single)

    front = 16
    early_rows = -(-stem_piece // D)
    late_start = early_rows * D - stem_piece
    embed_rows = -(-early_rows // 16) * 16
    own_layers = jnp.concatenate([layer_teacher, layers])
    own_tail = own_layers[:, layer_piece - tail :].reshape(2 * LAYERS, tail // 128, 128)
    before = lax.ppermute(own_tail, "dev", step_pairs(count, 1))
    last_lines = lax.ppermute(
        jnp.pad(own_tail, ((0, 0), (0, 24 - tail // 128), (0, 0))), "dev", [(count - 1, 0)]
    )
    head_span = GROUP * ROW
    stems = jnp.stack([as_lanes(stem_teacher), as_lanes(stem)])
    stems_next = lax.ppermute(stems[:, : head_span // 128], "dev", step_pairs(count, -1))
    def per_device(rows):
        return lax.dynamic_slice(jnp.array(rows, jnp.int32), (me, 0), (1, len(rows[0]))).reshape(-1)

    def spots(*values):
        return [part for value in values for part in (value // 128, value % 128)]

    place = per_device(
        [
            spots(starts[i] + front * 128, front * 128 + (0 if i == 0 else late_start), tail - drift * i)
            for i in range(count)
        ]
    )
    head_blocks, layer_blocks, embed_blocks, vector_blocks = own_blocks(
        place,
        stems,
        stems_next,
        as_lanes(own_layers),
        before,
        last_lines,
        (front, stem_piece, layer_piece, tail),
        slot,
        block_rows,
        embed_rows,
    )

    other_layers = lax.ppermute(layer_blocks, "dev", pairs(count, across))
    both_layers = jnp.where(
        student_side,
        jnp.stack([other_layers, layer_blocks]),
        jnp.stack([layer_blocks, other_layers]),
    )
    gathered = lax.all_gather(both_layers, "dev", axis=0, axis_index_groups=groups)
    head_out = jnp.where(student_side, head_blocks[0], head_blocks[1])
    head_keep = jnp.where(student_side, head_blocks[1], head_blocks[0])
    head_got = lax.ppermute(head_out, "dev", pairs(count, across))
    both_head = jnp.where(
        student_side, jnp.stack([head_got, head_keep]), jnp.stack([head_keep, head_got])
    )

    seed = jnp.concatenate([embed_blocks.reshape(2 * embed_rows, D), vector_blocks.reshape(8 * 2 * LAYERS, D)])
    third = -(-seed.shape[0] // 48) * 16
    spread_parts = []
    for number, order in enumerate(("xyba", "baxy", "ybax")):
        spread = seed[number * third : (number + 1) * third]
        reached = [0, 1]
        for name in order:
            moves = [(i, i ^ MASKS[name]) for i in reached]
            got = lax.ppermute(spread, "dev", moves)
            targets = [t for s, t in moves]
            is_target = jnp.array([i in targets for i in range(count)])[me]
            spread = jnp.where(is_target, got, spread)
            reached = reached + targets
        spread_parts.append(spread)
    spread = jnp.concatenate(spread_parts)
    other = lax.ppermute(spread, "dev", pairs(count, 1))
    is_even = me % 2 == 0
    even = jnp.where(is_even, spread, other)
    odd = jnp.where(is_even, other, spread)
    embed_all = [
        jnp.concatenate(
            [
                even[m * embed_rows : m * embed_rows + early_rows],
                odd[m * embed_rows : m * embed_rows + EMBED_ROWS - early_rows],
            ]
        )
        for m in range(2)
    ]
    gathered_head = lax.all_gather(after(both_head, gathered, even, odd), "dev", axis=0, axis_index_groups=groups)
    vectors_all = even[2 * embed_rows :].reshape(2, LAYERS, 8, D)

    plan = []
    for i in range(1, count):
        target = 0 if i < first_w2 else 1 if i < first_w3 else 2
        row = bounds[i] - (0, D, D + HID)[target]
        skip = max(-row, 0)
        owner = 1 if i >= half else 0
        plan.append((i ^ across if owner else i, owner, skip, sizes[i] - skip, target, row + skip))

    def embed_parts(model):
        rows = embed_all[model]
        return (rows[:PIX], rows[PIX : PIX + SEQ], rows[PIX + SEQ :], None, None, None)

    def head_rows(stream, extras):
        chosen = jnp.take_along_axis(stream, row_index[:, :, None], axis=1).reshape(rows_here, D)
        normed = layer_norm(chosen, extras[2].astype(single), extras[3].astype(single)).astype(narrow)
        return chosen, normed

    def start_rows(parts, student):
        stream = embed(parts, patches, masked_here, student)
        return jnp.pad(stream, ((0, 0), (0, PAD_SEQ - SEQ), (0, 0))).reshape(images_here * PAD_SEQ, D)

    student_parts = embed_parts(1)
    stream = start_rows(student_parts, True)
    saved_layers = []
    for layer_index in range(LAYERS):
        before_layer = stream
        stream, *saved = layer_forward(
            side, stream, vectors_all[1, layer_index], gathered, LAYERS + layer_index, True
        )
        saved_layers.append((before_layer, *saved))
    teacher_parts = embed_parts(0)
    teacher_stream = start_rows(teacher_parts, False)
    for layer_index in range(LAYERS):
        teacher_stream = layer_forward(
            side, teacher_stream, vectors_all[0, layer_index], gathered, layer_index, False
        )[0]
    stream = stream.reshape(images_here, PAD_SEQ, D)
    teacher_stream = teacher_stream.reshape(images_here, PAD_SEQ, D)
    chosen, student_normed = head_rows(stream, student_parts[2])
    teacher_normed = head_rows(teacher_stream, teacher_parts[2])[1]

    normed_got = lax.ppermute(
        jnp.where(student_side, teacher_normed, student_normed), "dev", pairs(count, across)
    )
    normed = jnp.where(
        student_side,
        jnp.concatenate([normed_got, student_normed]),
        jnp.concatenate([teacher_normed, normed_got]),
    )
    normed = jnp.pad(normed, ((0, more_rows), (0, 0)))
    third_end = (bounds[-2] - D - HID + slot) * (ROW // BOT)
    acts_width = D + HID + max(third_end, HID)
    unit_z, acts, bottleneck, pre_one, pre_two = head_pass(
        head_up_kernel,
        plan,
        side,
        (normed,),
        gathered_head,
        [
            jax.ShapeDtypeStruct((pair_rows, BOT), narrow),
            jax.ShapeDtypeStruct((pair_rows, acts_width), narrow),
            jax.ShapeDtypeStruct((pair_rows, BOT), single),
            jax.ShapeDtypeStruct((pair_rows, HID), single),
            jax.ShapeDtypeStruct((pair_rows, HID), single),
        ],
    )
    inputs_all = lax.all_gather(acts, "dev", axis=0, axis_index_groups=groups).reshape(half * pair_rows, -1)

    all_rows = half * pair_rows
    flag_row = 2 * rows_here
    kept_row = jnp.broadcast_to(kept[:, None] * (1.0 / 128.0), (images_here, 17)).reshape(1, rows_here)
    kept_row = jnp.pad(kept_row.astype(narrow), ((0, 0), (0, BOT - rows_here)))
    z_pair = cube_gather(jnp.concatenate([unit_z[:flag_row], kept_row, unit_z[flag_row + 1 :]]), "b")
    teacher_z_all = cube_gather(z_pair[0], "xygc")
    student_z_all = cube_gather(z_pair[1], "gxyc").reshape((2,) * 4 + (pair_rows, BOT))
    student_z_all = jnp.transpose(student_z_all, (0, 3, 1, 2, 4, 5)).reshape(half, pair_rows, BOT)
    all_kept = jnp.concatenate(
        [
            teacher_z_all[:, flag_row, :rows_here],
            student_z_all[:, flag_row, :rows_here],
            jnp.zeros((half, more_rows), narrow),
        ],
        axis=1,
    )
    all_kept = all_kept.astype(single).reshape(all_rows) * 128.0
    teacher_z_all = teacher_z_all.reshape(all_rows, BOT)
    student_z_all = student_z_all.reshape(all_rows, BOT)
    protos_here = protos.shape[0]
    own_centre = lax.dynamic_slice(centre, (me * protos_here,), (protos_here,))
    centre_column = own_centre.reshape(protos_here, 1)
    spot_in_pair = jnp.arange(all_rows) % pair_rows
    is_class = (spot_in_pair % 17) == 0
    class_kept = jnp.where(is_class, all_kept, 0.0)
    row_weight = jnp.where(is_class, all_kept, all_kept * (1.0 / 16.0))
    count_total = jnp.sum(class_kept)

    def lines(*values):
        return jnp.pad(jnp.stack(values), ((0, 8 - len(values)), (0, 0)))

    mixed_student, mixed_teacher, sums, centre_sum = logits_pass(
        teacher_z_all, student_z_all, proto_teacher, protos, centre_column, lines(class_kept)
    )
    by_pair = (2,) * 4 + (pair_rows, -1)
    mixed_own = jnp.concatenate(
        [
            cube_scatter(mixed_student.reshape(by_pair), "cgyx", "cgyx"),
            cube_scatter(mixed_teacher.reshape(by_pair), "cgyx", "cxyg"),
        ],
        axis=1,
    )
    mixed_own = mixed_own + lax.ppermute(
        mixed_own.astype(narrow), "dev", [(i, i ^ across) for i in range(half)]
    ).astype(single)
    scale = row_weight / tau_student
    flags = bit_flags(me)
    pair_at = flags["c"] * 8 + flags["g"] * 4 + flags["y"] * 2 + flags["x"]
    own_scale = lax.dynamic_slice(scale, (pair_at * pair_rows,), (pair_rows,))[:, None]
    grad_unit_z = own_scale * (
        mixed_own[:, :BOT] / mixed_own[:, 2 * BOT + 1 : 2 * BOT + 2]
        - mixed_own[:, BOT : 2 * BOT] / mixed_own[:, 2 * BOT : 2 * BOT + 1]
    )
    own_new_centre = (
        centre_keep * own_centre + (1.0 - centre_keep) * centre_sum.reshape(protos_here) / count_total
    )

    grads, grad_normed = head_pass(
        head_down_kernel,
        plan,
        side,
        (grad_unit_z, bottleneck, pre_one, pre_two),
        gathered_head,
        [
            jax.ShapeDtypeStruct((pair_rows, 2 * HID + BOT), narrow),
            jax.ShapeDtypeStruct((pair_rows, D), single),
        ],
    )
    width = grads.shape[1]
    wide = max(protos_here, all_rows)
    carried = jnp.stack(
        [jnp.pad(row, (0, wide - row.shape[0])) for row in (own_new_centre, sums[0], sums[1], sums[2])]
    )
    carried_rows = 3 * carried.shape[0]
    assert carried_rows <= more_rows and wide <= width
    high = carried.astype(narrow)
    middle = (carried - high.astype(single)).astype(narrow)
    low = (carried - high.astype(single) - middle.astype(single)).astype(narrow)
    carried = jnp.pad(jnp.concatenate([high, middle, low]), ((0, more_rows - carried_rows), (0, width - wide)))
    grads = jnp.concatenate([grads[: 2 * rows_here], carried])
    grads_all = lax.all_gather(grads, "dev", axis=0, axis_index_groups=groups).reshape(half * pair_rows, -1)
    normed_back = lax.ppermute(
        grad_normed[:rows_here], "dev", [(i, i ^ across) for i in range(half, count)]
    )
    own_grad_normed = jnp.where(student_side, grad_normed[rows_here : 2 * rows_here], normed_back)
    extras = student_parts[2].astype(single)
    grad_chosen, grad_gain, grad_bias = jax.vjp(layer_norm, chosen, extras[2], extras[3])[1](
        own_grad_normed
    )
    image_index = jnp.arange(images_here, dtype=jnp.int32)[:, None]
    grad_stream = (
        jnp.zeros(stream.shape, single)
        .at[image_index, row_index]
        .add(grad_chosen.reshape(images_here, 17, D))
    )

    grad_stream = grad_stream.reshape(images_here * PAD_SEQ, D)
    middle_row = block_rows // 2
    vector_grads = [None] * LAYERS

    def halves(array):
        middle = array.shape[-2] // 2
        return [array[..., :middle, :], array[..., middle:, :]]

    def cuts(parts, names, order):
        return [cut(part, name, axis, 1) for part, name, axis in zip(parts, names, order)]

    def moves(pieces, order):
        return [move(sent, kept, axis) for (sent, kept, left), axis in zip(pieces, order)]

    def over_core(weight_grad, rows):
        pairs_of = weight_grad.reshape(D // 128, -1, 2, rows, 128)
        return move(*cut(pairs_of, "pc", "c", 1)[:2], "c")

    def core_cut(weight_grad, rows):
        return cut(weight_grad.reshape(D // 128, -1, 2, rows, 128), "pc", "c", 1)[:2]

    def start(late, early, *others):
        shared_pair = 4 * D // (2 * block_rows)
        whole = jnp.concatenate(
            [
                early[:, :shared_pair],
                early[:, shared_pair:] + late[:, : early.shape[1] - shared_pair],
                late[:, early.shape[1] - shared_pair :],
            ],
            axis=1,
        )
        parts = [jnp.concatenate(pieces, axis=2) for pieces in zip(*[halves(array) for array in (whole, *others)])]
        by_bits = [part.reshape((D // 128, 2, 2, 2, 2) + part.shape[2:]) for part in parts]
        return (cuts(by_bits, ["bayx"] * 2, rounds[0]), 0)

    rounds = (("x", "b"), ("y", "a"), ("b", "x"), ("a", "y"))

    def advance(state):
        pieces, stage = state
        parts = moves(pieces, rounds[stage])
        names = [left for sent, kept, left in pieces]
        return cuts(parts, names, rounds[stage + 1]), stage + 1

    def finish(state):
        while state[1] < len(rounds) - 1:
            state = advance(state)
        return moves(state[0], rounds[-1])

    def sends(states):
        return tuple(sent for pieces, stage in states for sent, kept, left in pieces)

    def block_place(i):
        column = max(bounds[i], 0) // 128 * 128
        grad_column = 0 if i < first_w2 else HID
        return [column, bounds[i] - column if i else 0, sizes[i] if i else 0, grad_column]

    def third_place(i):
        return [0, 0, sizes[i], 0]

    place = per_device(
        [
            (third_place(i) if i >= first_w3 else block_place(i))
            + block_place(i ^ across)
            + [int(i >= first_w3), D + HID + max(bounds[i] - D - HID, 0) * (ROW // BOT)]
            for i in range(count)
        ]
    )
    started = []
    for layer_index in reversed(range(LAYERS)):
        saved, vectors = saved_layers[layer_index], vectors_all[1, layer_index]
        part = LAYERS + layer_index
        grad_stream, late_grad, late_vectors = mlp_back(
            side, grad_stream, saved, vectors, gathered, part, sends(started), []
        )
        late = over_core(late_grad, block_rows)
        started = [advance(state) for state in started]
        if layer_index == 0:
            own_block_grad, partner_block_grad, *held = head_grads(
                place,
                inputs_all,
                grads_all,
                slot,
                -min(bounds[1], 0),
                (late_vectors,),
                [stay for pieces, stage in started for sent, stay, left in pieces],
            )
            held = iter(held)
            started = [
                ([(sent, next(held), left) for sent, _, left in pieces], stage) for pieces, stage in started
            ]
            started = [advance(state) for state in started]
            block_got = lax.ppermute(partner_block_grad, "dev", [(i, i ^ across) for i in range(half, count)])
        grad_stream, early_grad, early_vectors, *held_block = attention_back(
            side,
            grad_stream,
            saved,
            vectors,
            gathered,
            part,
            sends(started),
            [own_block_grad] if layer_index == 0 else [],
        )
        vector_grads[layer_index] = (late_vectors + early_vectors)[:6]
        started = [advance(state) for state in started]
        if layer_index > 0:
            started.append(start(late, over_core(early_grad, block_rows)))
    own_block_grad = held_block[0]
    rows = grads_all.reshape(half, pair_rows, width)[:, 2 * rows_here : 2 * rows_here + carried_rows, :wide]
    rows = rows.reshape(half, 3, carried_rows // 3, wide).astype(single)
    rows = rows[:, 0] + rows[:, 1] + rows[:, 2]
    half_centre = rows[:, 0, :protos_here]
    half_sums = jnp.sum(rows[:, 1:, :all_rows], axis=0)
    other_centre = lax.ppermute(half_centre, "dev", pairs(count, across))
    sums = half_sums + lax.ppermute(half_sums, "dev", pairs(count, across))
    new_centre = jnp.where(
        student_side,
        jnp.concatenate([other_centre, half_centre]),
        jnp.concatenate([half_centre, other_centre]),
    ).reshape(-1)
    cross = jnp.log(sums[1]) - sums[2] / (sums[0] * tau_student)
    loss_total = jnp.sum(row_weight * cross)
    student_scale, teacher_scale = scale / sums[1], scale / sums[0]
    head_block_grad = jnp.where(student_side, own_block_grad, block_got.astype(single))
    early = over_core(early_grad, block_rows)
    small_rows = -(-(EMBED_ROWS + 6 * LAYERS) // (16 * count)) * 16
    small = embed_back(
        grad_stream,
        patches.reshape(images_here * PATCHES, PIX),
        jnp.where(masked_here, 0.0, 1.0).reshape(images_here * PATCHES, 1),
        jnp.stack([grad_gain, grad_bias]),
        jnp.concatenate(vector_grads),
        small_rows * count,
        (),
    )
    started.append(start(late, early, over_core(small, small_rows)))
    last_rows = lax.dynamic_slice(
        head_block_grad, (jnp.array(sizes, jnp.int32)[me] - GROUP, 0), (GROUP, ROW)
    )
    previous = lax.ppermute(last_rows, "dev", step_pairs(count, 1))
    proto_grad, proto_square, *held = proto_grad_pass(
        teacher_z_all,
        student_z_all,
        proto_teacher,
        protos,
        centre_column,
        lines(student_scale, teacher_scale),
        [stay for pieces, stage in started for sent, stay, left in pieces],
    )
    held = iter(held)
    started = [([(sent, next(held), left) for sent, _, left in pieces], stage) for pieces, stage in started]
    blocks = [finish(state) for state in started][::-1]
    middle_row = block_rows // 2
    layer_block = jnp.stack([jnp.concatenate([part[:, :middle_row] for part in parts], axis=1) for parts in blocks])
    small_block = jnp.concatenate([part[:, middle_row:] for part in blocks[0]], axis=1)

    square_local = (
        jnp.sum(head_block_grad * head_block_grad)
        + jnp.sum(layer_block * layer_block)
        + jnp.sum(small_block * small_block)
        + proto_square[0, 0]
    )
    high = square_local.astype(narrow)
    middle = (square_local - high.astype(single)).astype(narrow)
    low = (square_local - high.astype(single) - middle.astype(single)).astype(narrow)
    tile = jnp.pad(jnp.stack([high, middle, low]).reshape(1, 1, 3), ((0, 0), (0, 15), (0, 125)))
    first_rows = small_block[:2].astype(narrow)
    other_rows = jnp.concatenate([small_block[2:].astype(narrow), tile], axis=1)
    first_rows = cube_gather(first_rows, "xya")
    other_rows = cube_gather(other_rows, "abx")
    behind = lax.ppermute(layer_block[:, :, :6], "dev", step_pairs(count, -1))
    place = per_device([spots(head_span - starts[i], drift * i) for i in range(count)])
    stem_lines, layer_lines, first_rows, other_rows = own_shards(
        place, head_block_grad, previous, layer_block, behind, lane_rows(stem_piece), lane_rows(layer_piece),
        [first_rows, other_rows],
    )
    first_rows = jnp.moveaxis(cube_gather(first_rows, "bc").reshape((2, 2, 8) + first_rows.shape[1:]), 0, 2)
    other_rows = cube_gather(other_rows, "yc")
    other_rows = other_rows.reshape((2,) * 5 + other_rows.shape[2:])
    other_rows = jnp.transpose(other_rows, (3, 4, 1, 2, 0, 5, 6, 7))
    first_rows = first_rows.reshape((count,) + first_rows.shape[3:])
    other_rows = other_rows.reshape((count,) + other_rows.shape[5:])
    square_total = jnp.sum(other_rows[:, 0, small_rows, :3].astype(single))
    small_all = jnp.concatenate([first_rows, other_rows[:, :, :small_rows]], axis=1).astype(single)
    small_all = jnp.transpose(small_all, (0, 2, 1, 3)).reshape(small_rows * count, D)
    embed_grad = small_all[:EMBED_ROWS].reshape(-1)
    vector_grad = small_all[EMBED_ROWS : EMBED_ROWS + 6 * LAYERS].reshape(LAYERS, 6 * D)
    layer_grad = layer_lines.reshape(LAYERS, -1)[:, :layer_piece]
    layer_grad = jnp.concatenate(
        [
            layer_grad[:, : layer_piece - tail],
            jnp.where(me == count - 1, vector_grad, layer_grad[:, layer_piece - tail :]),
        ],
        axis=1,
    )
    stem_grad = stem_lines.reshape(-1)[:stem_piece]
    rest = EMBED_FLAT - stem_piece
    second_part = jnp.concatenate([embed_grad[stem_piece:], stem_grad[rest:]])
    stem_grad = jnp.where(
        me == 0, embed_grad[:stem_piece], jnp.where(me == 1, second_part, stem_grad)
    )

    grad_norm = jnp.sqrt(square_total) / count_total
    factor = jnp.minimum(1.0, clip_limit / (grad_norm + 1e-06)) / count_total
    stem_set = adam_update(stem, stem_moment, stem_second, stem_grad * factor, stem_teacher)
    layer_set = adam_update(layers, layer_moment, layer_second, layer_grad * factor, layer_teacher)
    proto_set = proto_update(factor, protos, proto_moment, proto_second, proto_teacher, proto_grad)
    return (loss_total, count_total, grad_norm, new_centre) + stem_set + layer_set + tuple(proto_set)


def solution(mesh):
    count = mesh.shape["dev"]
    stem_length = -(-(EMBED_FLAT + HEAD_ROWS * ROW) // count) * count
    close = fits(count, stem_length // count, (MATRIX_ROWS + 6) * D // count)
    placed = (
        P("dev", None, None),
        P("dev", None),
        P("dev"),
        P("dev"),
        P("dev"),
        P("dev"),
        P("dev"),
        P(None, "dev"),
        P(None, "dev"),
        P(None, "dev"),
        P(None, "dev"),
        P("dev", None),
        P("dev", None),
        P("dev", None),
        P("dev", None),
        P(),
    )
    return jax.shard_map(
        close_local if close else spread_local,
        mesh=mesh,
        in_specs=placed,
        out_specs=(
            P(),
            P(),
            P(),
            P(),
            P("dev"),
            P("dev"),
            P("dev"),
            P("dev"),
            P("dev"),
            P(None, "dev"),
            P(None, "dev"),
            P(None, "dev"),
            P(None, "dev"),
            P(None, "dev"),
            P("dev", None),
            P("dev", None),
            P("dev", None),
            P("dev", None),
            P("dev", None),
        ),
        check_vma=False,
    )
```

```python
import jax
import jax.numpy as jnp
from jax import lax
from jax.experimental import pallas as pl
from jax.experimental.pallas import tpu as pltpu
from jax.sharding import PartitionSpec as P

D = 384
HEADS = 6
HEAD_DIM = 64
FF = 1536
HID = 2048
BOT = 256
PIX = 588
PATCHES = 256
LAYERS = 2
STEP = 10
SEQ = 257


tau_student = 0.1
tau_teacher = 0.04
clip_limit = 0.003
learn_rate = 0.03
beta_one = 0.9
beta_two = 0.999
adam_eps = 1e-08
decay_rate = 0.04
teacher_keep = 0.8
centre_keep = 0.9
narrow = jnp.bfloat16
single = jnp.float32


def layer_shapes():
    return ((D, 3 * D), (D, D), (D, FF), (FF, D), (6, D))


def stem_shapes():
    return ((PIX, D), (SEQ, D), (4, D), (D, HID), (HID, HID), (HID, BOT))


def cut_flat(flat_row, shape_list):
    pieces = []
    offset = 0
    for shape_pair in shape_list:
        length = shape_pair[0] * shape_pair[1]
        pieces.append(flat_row[offset : offset + length].reshape(shape_pair))
        offset = offset + length
    return pieces


def pack_flat(grad_list, total_length):
    joined = jnp.concatenate([grad_item.reshape(-1) for grad_item in grad_list])
    return jnp.concatenate([joined, jnp.zeros((total_length - joined.shape[0],), single)])


def contract(form, left_arg, right_arg):
    return jnp.einsum(form, left_arg, right_arg, preferred_element_type=single)


def layer_norm(values, gain_row, bias_row):
    centred = values - jnp.mean(values, axis=-1, keepdims=True)
    spread = jnp.mean(centred * centred, axis=-1, keepdims=True)
    return centred * lax.rsqrt(spread + 1e-06) * gain_row + bias_row


def unit_rows(values):
    return values * lax.rsqrt(jnp.sum(values * values, axis=-1, keepdims=True) + 1e-06)


def gelu_back(pre_act, grad_act):
    return jax.vjp(jax.nn.gelu, pre_act)[1](grad_act)[0]


def block_forward(stream, weights):
    w_qkv, w_proj, w_up, w_down, vectors = weights
    vectors = vectors.astype(single)
    batch_size = stream.shape[0]
    normed = layer_norm(stream, vectors[0], vectors[1]).astype(narrow)
    packed = (
        contract("bsd,de->bse", normed, w_qkv)
        .astype(narrow)
        .reshape(batch_size, SEQ, 3, HEADS, HEAD_DIM)
    )
    scores = contract("bqhe,bkhe->bhqk", packed[:, :, 0], packed[:, :, 1]) * HEAD_DIM ** (-0.5)
    top_score = jnp.max(scores, axis=-1, keepdims=True)
    exp_terms = jnp.exp(scores - top_score)
    totals = jnp.sum(exp_terms, axis=-1, keepdims=True)
    log_total = top_score + jnp.log(totals)
    mixed = contract("bhqk,bkhe->bqhe", (exp_terms / totals).astype(narrow), packed[:, :, 2])
    mixed = mixed.astype(narrow).reshape(batch_size, SEQ, D)
    attn_out = contract("bsd,de->bse", mixed, w_proj)
    middle = stream + vectors[2] * attn_out
    normed_two = layer_norm(middle, vectors[3], vectors[4]).astype(narrow)
    pre_act = contract("bsd,df->bsf", normed_two, w_up)
    hidden = jax.nn.gelu(pre_act).astype(narrow)
    mlp_out = contract("bsf,fd->bsd", hidden, w_down)
    saved = (
        stream,
        normed,
        packed,
        log_total,
        mixed,
        attn_out,
        middle,
        normed_two,
        pre_act,
        hidden,
        mlp_out,
    )
    return (middle + vectors[5] * mlp_out, saved)


def block_backward(grad_out, weights, saved):
    w_qkv, w_proj, w_up, w_down, vectors = weights
    vectors = vectors.astype(single)
    (
        stream,
        normed,
        packed,
        log_total,
        mixed,
        attn_out,
        middle,
        normed_two,
        pre_act,
        hidden,
        mlp_out,
    ) = saved
    batch_size = stream.shape[0]
    score_scale = HEAD_DIM ** (-0.5)
    grad_ls_two = jnp.sum(grad_out * mlp_out, axis=(0, 1))
    grad_mlp = (grad_out * vectors[5]).astype(narrow)
    grad_down = contract("bsf,bsd->fd", hidden, grad_mlp)
    grad_pre = gelu_back(pre_act, contract("bsd,fd->bsf", grad_mlp, w_down)).astype(narrow)
    grad_up = contract("bsd,bsf->df", normed_two, grad_pre)
    grad_normed_two = contract("bsf,df->bsd", grad_pre, w_up)
    grad_mid, grad_gain_two, grad_bias_two = jax.vjp(layer_norm, middle, vectors[3], vectors[4])[1](
        grad_normed_two
    )
    grad_mid = grad_mid + grad_out
    grad_ls_one = jnp.sum(grad_mid * attn_out, axis=(0, 1))
    grad_attn = (grad_mid * vectors[2]).astype(narrow)
    grad_proj = contract("bsd,bse->de", mixed, grad_attn)
    grad_mixed = (
        contract("bse,de->bsd", grad_attn, w_proj)
        .astype(narrow)
        .reshape(batch_size, SEQ, HEADS, HEAD_DIM)
    )
    query_rows = packed[:, :, 0]
    key_rows = packed[:, :, 1]
    value_rows = packed[:, :, 2]
    probs = jnp.exp(contract("bqhe,bkhe->bhqk", query_rows, key_rows) * score_scale - log_total)
    grad_probs = contract("bqhe,bkhe->bhqk", grad_mixed, value_rows)
    grad_values = contract("bhqk,bqhe->bkhe", probs.astype(narrow), grad_mixed)
    grad_scores = probs * (grad_probs - jnp.sum(probs * grad_probs, axis=-1, keepdims=True))
    grad_raw = (grad_scores * score_scale).astype(narrow)
    grad_queries = contract("bhqk,bkhe->bqhe", grad_raw, key_rows)
    grad_keys = contract("bhqk,bqhe->bkhe", grad_raw, query_rows)
    grad_packed = (
        jnp.stack([grad_queries, grad_keys, grad_values], axis=2)
        .astype(narrow)
        .reshape(batch_size, SEQ, 3 * D)
    )
    grad_qkv = contract("bsd,bse->de", normed, grad_packed)
    grad_normed = contract("bse,de->bsd", grad_packed, w_qkv)
    grad_in, grad_gain_one, grad_bias_one = jax.vjp(layer_norm, stream, vectors[0], vectors[1])[1](
        grad_normed
    )
    grad_vectors = jnp.stack(
        [grad_gain_one, grad_bias_one, grad_ls_one, grad_gain_two, grad_bias_two, grad_ls_two]
    )
    return (grad_in + grad_mid, (grad_qkv, grad_proj, grad_up, grad_down, grad_vectors))


def embed(stem_parts, image_rows, masked_here, student):
    patch_w, position, extras, w_first, w_second, w_third = stem_parts
    extras = extras.astype(single)
    embedded = contract("gpc,cd->gpd", image_rows, patch_w)
    if student:
        embedded = jnp.where(masked_here[:, :, None], extras[1], embedded)
    cls_rows = jnp.broadcast_to(extras[0], (image_rows.shape[0], 1, D))
    return jnp.concatenate([cls_rows, embedded], axis=1) + position.astype(single)


def embed_backward(grad_stream, image_rows, masked_here):
    grad_cls = jnp.sum(grad_stream[:, 0], axis=0)
    grad_position = jnp.sum(grad_stream, axis=0)
    grad_patch_rows = grad_stream[:, 1:]
    grad_mask_token = jnp.sum(jnp.where(masked_here[:, :, None], grad_patch_rows, 0.0), axis=(0, 1))
    grad_embedded = jnp.where(masked_here[:, :, None], 0.0, grad_patch_rows).astype(narrow)
    grad_patch_w = contract("gpc,gpd->cd", image_rows, grad_embedded)
    return (grad_patch_w, grad_position, grad_cls, grad_mask_token)


def head_forward(stem_parts, proto_rows, stream, row_index):
    patch_w, position, extras, w_first, w_second, w_third = stem_parts
    extras = extras.astype(single)
    chosen = jnp.take_along_axis(stream, row_index[:, :, None], axis=1)
    normed = layer_norm(chosen, extras[2], extras[3]).astype(narrow)
    pre_one = contract("grd,dh->grh", normed, w_first)
    hidden_one = jax.nn.gelu(pre_one).astype(narrow)
    pre_two = contract("grh,hk->grk", hidden_one, w_second)
    hidden_two = jax.nn.gelu(pre_two).astype(narrow)
    bottleneck = contract("grh,hb->grb", hidden_two, w_third)
    unit_z = unit_rows(bottleneck).astype(narrow)
    unit_protos = unit_rows(proto_rows.astype(single)).astype(narrow)
    logits = contract("grb,kb->grk", unit_z, unit_protos)
    return (
        logits,
        (chosen, normed, pre_one, hidden_one, pre_two, hidden_two, bottleneck, unit_z, unit_protos),
    )


def head_backward(grad_logits, stem_parts, saved, row_index, stream_shape):
    patch_w, position, extras, w_first, w_second, w_third = stem_parts
    extras = extras.astype(single)
    chosen, normed, pre_one, hidden_one, pre_two, hidden_two, bottleneck, unit_z, unit_protos = (
        saved
    )
    grad_rounded = grad_logits.astype(narrow)
    grad_unit_z = contract("grk,kb->grb", grad_rounded, unit_protos)
    grad_unit_protos = contract("grk,grb->kb", grad_rounded, unit_z)
    grad_bottle = jax.vjp(unit_rows, bottleneck)[1](grad_unit_z)[0].astype(narrow)
    grad_third = contract("grh,grb->hb", hidden_two, grad_bottle)
    grad_pre_two = gelu_back(pre_two, contract("grb,hb->grh", grad_bottle, w_third)).astype(narrow)
    grad_second = contract("grh,grk->hk", hidden_one, grad_pre_two)
    grad_pre_one = gelu_back(pre_one, contract("grk,hk->grh", grad_pre_two, w_second)).astype(
        narrow
    )
    grad_first = contract("grd,grh->dh", normed, grad_pre_one)
    grad_normed = contract("grh,dh->grd", grad_pre_one, w_first)
    grad_chosen, grad_gain, grad_bias = jax.vjp(layer_norm, chosen, extras[2], extras[3])[1](
        grad_normed
    )
    image_index = jnp.arange(row_index.shape[0], dtype=jnp.int32)[:, None]
    grad_stream = jnp.zeros(stream_shape, single).at[image_index, row_index].add(grad_chosen)
    return (
        grad_stream,
        (grad_first, grad_second, grad_third),
        grad_gain,
        grad_bias,
        grad_unit_protos,
    )


def adam_update(weight, moment, second, grad, teacher):
    new_moment = beta_one * moment + (1.0 - beta_one) * grad
    new_second = beta_two * second + (1.0 - beta_two) * grad * grad
    direction = (
        new_moment
        / (1.0 - beta_one**STEP)
        / (jnp.sqrt(new_second / (1.0 - beta_two**STEP)) + adam_eps)
    )
    new_weight = weight - learn_rate * (direction + decay_rate * weight)
    return (
        new_moment,
        new_second,
        new_weight,
        new_weight.astype(narrow),
        teacher_keep * teacher + (1.0 - teacher_keep) * new_weight,
    )


def spread_local(
    patches,
    masked,
    slot_used,
    stem,
    stem_moment,
    stem_second,
    stem_teacher,
    layers,
    layer_moment,
    layer_second,
    layer_teacher,
    protos,
    proto_moment,
    proto_second,
    proto_teacher,
    centre,
):
    images_here = patches.shape[0]
    row_index = jnp.concatenate([jnp.zeros((images_here, 1), jnp.int32), masked + 1], axis=1)
    masked_here = jnp.any(
        masked[:, :, None] == jnp.arange(PATCHES, dtype=jnp.int32)[None, None, :], axis=1
    )
    kept = slot_used.astype(single)
    teacher_flat, teacher_protos = (
        lax.all_gather(stem_teacher.astype(narrow), "dev", axis=0, tiled=True),
        lax.all_gather(proto_teacher.astype(narrow), "dev", axis=0, tiled=True),
    )
    teacher_parts = cut_flat(teacher_flat, stem_shapes())
    stream = embed(teacher_parts, patches, masked_here, False)
    for layer_index in range(LAYERS):
        teacher_layer = lax.all_gather(
            layer_teacher[layer_index].astype(narrow), "dev", axis=0, tiled=True
        )
        stream = block_forward(stream, cut_flat(teacher_layer, layer_shapes()))[0]
    teacher_logits = head_forward(teacher_parts, teacher_protos, stream, row_index)[0]
    teacher_probs = jax.nn.softmax((teacher_logits - centre) / tau_teacher, axis=-1)
    centre_terms = jnp.sum(kept[:, None] * teacher_logits[:, 0], axis=0)
    student_flat, student_protos = (
        lax.all_gather(stem.astype(narrow), "dev", axis=0, tiled=True),
        lax.all_gather(protos.astype(narrow), "dev", axis=0, tiled=True),
    )
    student_parts = cut_flat(student_flat, stem_shapes())
    stream = embed(student_parts, patches, masked_here, True)
    saved_layers = []
    gathered_layers = []
    for layer_index in range(LAYERS):
        layer_flat = lax.all_gather(layers[layer_index].astype(narrow), "dev", axis=0, tiled=True)
        gathered_layers.append(layer_flat)
        stream, saved = block_forward(stream, cut_flat(layer_flat, layer_shapes()))
        saved_layers.append(saved)
    logits, head_saved = head_forward(student_parts, student_protos, stream, row_index)

    def loss_piece(logit_rows):
        log_probs = jax.nn.log_softmax(logit_rows / tau_student, axis=-1)
        cross = -jnp.sum(teacher_probs * log_probs, axis=-1)
        return jnp.sum(kept * (cross[:, 0] + jnp.mean(cross[:, 1:], axis=1)))

    loss_local, loss_puller = jax.vjp(loss_piece, logits)
    grad_logits = loss_puller(jnp.float32(1.0))[0]
    count_local = jnp.sum(kept)
    loss_total, count_total, centre_total = lax.psum((loss_local, count_local, centre_terms), "dev")
    back_flat, back_protos = (
        lax.all_gather(stem.astype(narrow), "dev", axis=0, tiled=True),
        lax.all_gather(protos.astype(narrow), "dev", axis=0, tiled=True),
    )
    back_parts = cut_flat(back_flat, stem_shapes())
    grad_stream, head_grads, grad_gain, grad_bias, grad_unit_protos = head_backward(
        grad_logits, back_parts, head_saved, row_index, stream.shape
    )
    layer_grads = []
    for layer_index in reversed(range(LAYERS)):
        weight_flat = lax.all_gather(layers[layer_index].astype(narrow), "dev", axis=0, tiled=True)
        grad_stream, block_grads = block_backward(
            grad_stream, cut_flat(weight_flat, layer_shapes()), saved_layers[layer_index]
        )
        layer_grads.insert(
            0,
            lax.psum_scatter(
                pack_flat(block_grads, weight_flat.shape[0]), "dev", scatter_dimension=0, tiled=True
            ),
        )
    grad_patch_w, grad_position, grad_cls, grad_mask_token = embed_backward(
        grad_stream, patches, masked_here
    )
    grad_extras = jnp.stack([grad_cls, grad_mask_token, grad_gain, grad_bias])
    stem_flat_grad = pack_flat(
        (grad_patch_w, grad_position, grad_extras) + head_grads, back_flat.shape[0]
    )
    stem_grad, proto_row_grad = (
        lax.psum_scatter(stem_flat_grad, "dev", scatter_dimension=0, tiled=True),
        lax.psum_scatter(grad_unit_protos, "dev", scatter_dimension=0, tiled=True),
    )
    own_protos = lax.optimization_barrier(protos.astype(narrow)).astype(single)
    proto_grad = jax.vjp(unit_rows, own_protos)[1](proto_row_grad)[0]
    layer_grad = jnp.stack(layer_grads)
    square_local = (
        jnp.sum(stem_grad * stem_grad)
        + jnp.sum(layer_grad * layer_grad)
        + jnp.sum(proto_grad * proto_grad)
    )
    square_total = lax.psum(square_local, "dev")
    grad_norm = jnp.sqrt(square_total) / count_total
    factor = jnp.minimum(1.0, clip_limit / (grad_norm + 1e-06)) / count_total
    new_centre = centre_keep * centre + (1.0 - centre_keep) * centre_total / count_total
    stem_set = adam_update(stem, stem_moment, stem_second, stem_grad * factor, stem_teacher)
    layer_set = adam_update(layers, layer_moment, layer_second, layer_grad * factor, layer_teacher)
    proto_set = adam_update(protos, proto_moment, proto_second, proto_grad * factor, proto_teacher)
    return (
        loss_total,
        count_total,
        grad_norm,
        new_centre,
        stem_set[0],
        stem_set[1],
        stem_set[2],
        stem_set[3],
        stem_set[4],
        layer_set[0],
        layer_set[1],
        layer_set[2],
        layer_set[3],
        layer_set[4],
        proto_set[0],
        proto_set[1],
        proto_set[2],
        proto_set[3],
        proto_set[4],
    )


GROUP = 16
ROW = HID
MATRIX_ROWS = D * 3 + D + FF + FF
EMBED_ROWS = PIX + SEQ + 4
EMBED_FLAT = EMBED_ROWS * D
HEAD_ROWS = D + HID + BOT
BITS = ("b", "a", "y", "x", "c")
MASKS = {"c": 1, "x": 2, "y": 4, "a": 8, "b": 24, "g": 8}


def head_bounds(count, stem_piece):
    bounds = [-(-(stem_piece * device - EMBED_FLAT) // (ROW * GROUP)) * GROUP for device in range(count + 1)]
    bounds[0] = -(-EMBED_FLAT // (ROW * GROUP)) * -GROUP
    bounds[-1] = HEAD_ROWS
    return bounds


def fits(count, stem_piece, layer_piece):
    if count != 1 << len(BITS) or MATRIX_ROWS % (3 * count):
        return False
    bounds = head_bounds(count, stem_piece)
    sizes = [bounds[i + 1] - bounds[i] for i in range(count)]
    return (
        min(sizes) > GROUP
        and bounds[1] <= 0
        and stem_piece < EMBED_FLAT <= 2 * stem_piece
        and D in bounds
        and D + HID in bounds
        and stem_piece * count == EMBED_FLAT + HEAD_ROWS * ROW
    )


def pairs(count, mask):
    return [(i, i ^ mask) for i in range(count)]


def bit_flags(me):
    flags = {name: (me >> (len(BITS) - 1 - place)) & 1 for place, name in enumerate(BITS)}
    flags["g"] = flags["a"] ^ flags["b"]
    return flags


def cube_gather(part, order):
    count = 1 << len(BITS)
    flags = bit_flags(lax.axis_index("dev"))
    held = part[None]
    for name in order:
        got = lax.ppermute(held, "dev", pairs(count, MASKS[name]))
        held = jnp.where(
            flags[name] == 1,
            jnp.concatenate([got, held], axis=0),
            jnp.concatenate([held, got], axis=0),
        )
    return held


def cut(array, names, name, lead):
    mine = bit_flags(lax.axis_index("dev"))[name]
    place = names.index(name) + lead
    sent = lax.dynamic_index_in_dim(array, 1 - mine, place, keepdims=False)
    kept = lax.dynamic_index_in_dim(array, mine, place, keepdims=False)
    return sent.astype(narrow), kept, names.replace(name, "")


def move(sent, kept, name):
    return kept + lax.ppermute(sent, "dev", pairs(1 << len(BITS), MASKS[name])).astype(single)


def cube_scatter(array, names, order, lead=0):
    for name in order:
        sent, kept, names = cut(array, names, name, lead)
        array = move(sent, kept, name)
    return array


def cube_sum(values):
    for name in "cxyab":
        values = values + lax.ppermute(values, "dev", pairs(1 << len(BITS), MASKS[name]))
    return values


def split_bits(array, lead=0):
    return array.reshape(array.shape[:lead] + (2,) * len(BITS) + array.shape[lead + 1 :])


def step_pairs(count, step):
    return [(i, i + step) for i in range(count) if 0 <= i + step < count]


def lane_rows(length):
    return -(-length // 1024) * 8


def as_lanes(flat):
    rows = lane_rows(flat.shape[-1])
    gap = rows * 128 - flat.shape[-1]
    padded = jnp.pad(flat, [(0, 0)] * (flat.ndim - 1) + [(0, gap)])
    return padded.reshape(flat.shape[:-1] + (rows, 128))


def shifted(line_ref, row, lane, first, rows, stride):
    spots = lax.broadcasted_iota(jnp.int32, (rows, 128), 1)
    turn = lax.rem(128 - lane, 128)
    here = pltpu.roll(line_ref[pl.ds(row + first, rows, stride=stride), :], turn, 1)
    there = pltpu.roll(line_ref[pl.ds(row + first + 1, rows, stride=stride), :], turn, 1)
    return jnp.where(spots < 128 - lane, here, there)


def blocks_kernel(
    shape,
    place_ref,
    stem_ref,
    after_ref,
    layer_ref,
    before_ref,
    last_ref,
    head_ref,
    block_ref,
    embed_ref,
    vector_ref,
    line_ref,
    flat_ref,
):
    front, stem_piece, layer_piece, tail = shape
    stem_lines = stem_ref.shape[1]
    end_row, end_lane = stem_piece // 128, stem_piece % 128
    after_lines = after_ref.shape[1]
    slot = head_ref.shape[1]
    for model in range(2):
        line_ref[pl.ds(0, front), :] = jnp.zeros((front, 128), single)
        line_ref[pl.ds(front, end_row), :] = stem_ref[model, pl.ds(0, end_row), :]
        turned = pltpu.roll(after_ref[model], end_lane, 1)
        spots = lax.broadcasted_iota(jnp.int32, (after_lines, 128), 1)
        line_ref[pl.ds(front + end_row, after_lines), :] = turned
        line_ref[pl.ds(front + end_row + after_lines, 128), :] = jnp.zeros((128, 128), single)
        lower = pltpu.roll(turned, 1, 0)
        first_line = jnp.broadcast_to(stem_ref[model, pl.ds(end_row, 1), :], (after_lines, 128))
        number = lax.broadcasted_iota(jnp.int32, (after_lines, 128), 0)
        lower = jnp.where(number == 0, first_line, lower)
        line_ref[pl.ds(front + end_row, after_lines), :] = jnp.where(spots < end_lane, lower, turned)
        per_row = ROW // 128
        for chunk in range(per_row):
            head_ref[model, :, pl.ds(chunk * 128, 128)] = shifted(
                line_ref, place_ref[0], place_ref[1], chunk, slot, per_row
            ).astype(narrow)
        for chunk in range(D // 128):
            embed_ref[model, :, pl.ds(chunk * 128, 128)] = shifted(
                line_ref, place_ref[2], place_ref[3], chunk, embed_ref.shape[1], D // 128
            ).astype(narrow)
    tail_lines = tail // 128
    layer_lines = layer_ref.shape[1]
    for part in range(layer_ref.shape[0]):
        flat_ref[pl.ds(0, tail_lines), :] = before_ref[part]
        flat_ref[pl.ds(tail_lines, layer_lines), :] = layer_ref[part]
        for chunk in range(D // 128):
            block_ref[part, :, pl.ds(chunk * 128, 128)] = shifted(
                flat_ref, place_ref[4], place_ref[5], chunk, block_ref.shape[1], D // 128
            ).astype(narrow)
            vector_ref[part, :, pl.ds(chunk * 128, 128)] = last_ref[
                part, pl.ds(chunk, 8, stride=D // 128), :
            ].astype(narrow)


def own_blocks(place, stems, after, layer_rows, before, last_lines, shape, slot, block_rows, embed_rows):
    front, stem_piece, layer_piece, tail = shape
    lines = front + stem_piece // 128 + after.shape[1] + slot * ROW // 128
    flats = tail // 128 + layer_rows.shape[1] + 48
    return pl.pallas_call(
        lambda *refs: blocks_kernel(shape, *refs),
        out_shape=[
            jax.ShapeDtypeStruct((2, slot, ROW), narrow),
            jax.ShapeDtypeStruct((2 * LAYERS, block_rows, D), narrow),
            jax.ShapeDtypeStruct((2, embed_rows, D), narrow),
            jax.ShapeDtypeStruct((2 * LAYERS, 8, D), narrow),
        ],
        in_specs=[pl.BlockSpec(memory_space=pltpu.SMEM)] + [pl.BlockSpec(memory_space=pltpu.VMEM)] * 5,
        out_specs=[pl.BlockSpec(memory_space=pltpu.VMEM)] * 4,
        scratch_shapes=[pltpu.VMEM((lines, 128), single), pltpu.VMEM((flats, 128), single)],
        compiler_params=pltpu.CompilerParams(vmem_limit_bytes=40 << 20),
    )(place, stems, after, layer_rows, before, last_lines)


def shards_kernel(held, place_ref, head_ref, previous_ref, block_ref, behind_ref, *refs):
    stem_ref, layer_ref = refs[held : held + 2]
    line_ref, flat_ref = refs[-2:]
    per_row = ROW // 128
    extra = previous_ref.shape[0]
    slot = head_ref.shape[0]
    for chunk in range(per_row):
        spot = pl.ds(chunk * 128, 128)
        line_ref[pl.ds(chunk, extra, stride=per_row), :] = previous_ref[:, spot]
        line_ref[pl.ds(extra * per_row + chunk, slot, stride=per_row), :] = head_ref[:, spot]
    stem_ref[...] = shifted(line_ref, place_ref[0], place_ref[1], 0, stem_ref.shape[0], 1)
    per_row = D // 128
    rows = block_ref.shape[2]
    for part in range(block_ref.shape[0]):
        for chunk in range(per_row):
            flat_ref[pl.ds(chunk, rows, stride=per_row), :] = block_ref[part, chunk]
            flat_ref[pl.ds(rows * per_row + chunk, 6, stride=per_row), :] = behind_ref[part, chunk]
        layer_ref[part] = shifted(flat_ref, place_ref[2], place_ref[3], 0, layer_ref.shape[1], 1)


def own_shards(place, head_grad, previous, block_grad, behind, stem_lines, layer_lines, held):
    per_row = ROW // 128
    lines = (head_grad.shape[0] + previous.shape[0]) * per_row + 256
    flats = max(block_grad.shape[2] * 3 + 18, layer_lines + 18) + 16
    return pl.pallas_call(
        lambda *refs: shards_kernel(len(held), *refs),
        out_shape=[
            jax.ShapeDtypeStruct((stem_lines, 128), single),
            jax.ShapeDtypeStruct((block_grad.shape[0], layer_lines, 128), single),
        ]
        + [jax.ShapeDtypeStruct(array.shape, array.dtype) for array in held],
        in_specs=[pl.BlockSpec(memory_space=pltpu.SMEM)]
        + [pl.BlockSpec(memory_space=pltpu.VMEM)] * 4
        + [pl.BlockSpec(memory_space=pl.ANY)] * len(held),
        out_specs=[pl.BlockSpec(memory_space=pltpu.VMEM)] * 2 + [pl.BlockSpec(memory_space=pl.ANY)] * len(held),
        input_output_aliases={5 + number: 2 + number for number in range(len(held))},
        scratch_shapes=[pltpu.VMEM((lines, 128), single), pltpu.VMEM((flats, 128), single)],
        compiler_params=pltpu.CompilerParams(vmem_limit_bytes=40 << 20),
    )(place, head_grad, previous, block_grad, behind, *held)


PAD_SEQ = 272
GELU_SCALE = 0.7978845608028654
GELU_CUBE = 0.044715


def product_plain(left, right):
    return lax.dot_general(left, right, (((1,), (0,)), ((), ())), preferred_element_type=single)


def product_right(left, right):
    return lax.dot_general(left, right, (((1,), (1,)), ((), ())), preferred_element_type=single)


def product_left(left, right):
    return lax.dot_general(left, right, (((0,), (0,)), ((), ())), preferred_element_type=single)


def norm_parts(values):
    centred = values - jnp.mean(values, axis=-1, keepdims=True)
    spread = lax.rsqrt(jnp.mean(centred * centred, axis=-1, keepdims=True) + 1e-06)
    return centred * spread, spread


def norm_back(grad, unit, spread, gain):
    grad_unit = grad * gain
    mean_one = jnp.mean(grad_unit, axis=-1, keepdims=True)
    mean_two = jnp.mean(grad_unit * unit, axis=-1, keepdims=True)
    return spread * (grad_unit - mean_one - unit * mean_two)


def gelu_tanh(values):
    return jnp.tanh(GELU_SCALE * (values + GELU_CUBE * values * values * values))


def gelu_value(values):
    return 0.5 * values * (1.0 + gelu_tanh(values))


def gelu_slope(values):
    bent = gelu_tanh(values)
    return 0.5 * (1.0 + bent) + 0.5 * values * (1.0 - bent * bent) * GELU_SCALE * (
        1.0 + 3.0 * GELU_CUBE * values * values
    )


def head_copies(plan, side_ref, gathered_ref, one_ref, two_ref, lines_ref, sems):
    quarter = gathered_ref.shape[0] // 2
    shift = side_ref[0] * quarter
    targets = (one_ref, two_ref, lines_ref)
    copies = []
    for number, (at, owner, first, rows, target, row) in enumerate(plan):
        spot = at + shift if at < quarter else at - shift
        copies.append(
            pltpu.make_async_copy(
                gathered_ref.at[spot, owner, pl.ds(first, rows)],
                targets[target].at[pl.ds(row, rows)],
                sems.at[number],
            )
        )
    for copy in copies:
        copy.start()
    return [[copy for copy, item in zip(copies, plan) if item[4] == target] for target in range(3)]


def wait_all(copies):
    for copy in copies:
        copy.wait()


def spread_third(lines_ref, wide_ref, third_ref):
    groups = ROW // BOT
    for lane in range(BOT // 128):
        for group in range(groups):
            at = group * BOT + lane * 128
            wide_ref[lane, pl.ds(group, lines_ref.shape[0], stride=groups), :] = lines_ref[
                :, at : at + 128
            ].astype(single)
        third_ref[:, pl.ds(lane * 128, 128)] = wide_ref[lane].astype(narrow)


def head_up_kernel(
    plan, side_ref, normed_ref, gathered_ref, unit_ref, acts_ref, bottle_ref, pre_one_ref, pre_two_ref,
    one_ref, two_ref, lines_ref, wide_ref, third_ref, sems,
):
    copies = head_copies(plan, side_ref, gathered_ref, one_ref, two_ref, lines_ref, sems)
    acts_ref[...] = jnp.zeros_like(acts_ref)
    normed = normed_ref[...]
    acts_ref[:, pl.ds(0, D)] = normed
    piece = HID // 4
    wait_all(copies[0])
    for number in range(4):
        spot = pl.ds(number * piece, piece)
        pre = product_plain(normed, one_ref[:, spot])
        pre_one_ref[:, spot] = pre
        acts_ref[:, pl.ds(D + number * piece, piece)] = gelu_value(pre).astype(narrow)
    wait_all(copies[2])
    spread_third(lines_ref, wide_ref, third_ref)
    wait_all(copies[1])
    hidden = acts_ref[:, pl.ds(D, HID)]
    for number in range(4):
        spot = pl.ds(number * piece, piece)
        pre = product_plain(hidden, two_ref[:, spot])
        pre_two_ref[:, spot] = pre
        acts_ref[:, pl.ds(D + HID + number * piece, piece)] = gelu_value(pre).astype(narrow)
    bottle = product_plain(acts_ref[:, pl.ds(D + HID, HID)], third_ref[...])
    bottle_ref[...] = bottle
    unit_ref[...] = (
        bottle * lax.rsqrt(jnp.sum(bottle * bottle, axis=-1, keepdims=True) + 1e-06)
    ).astype(narrow)


def head_down_kernel(
    plan, side_ref, grad_ref, bottle_ref, pre_one_ref, pre_two_ref, gathered_ref, grads_ref, normed_grad_ref,
    one_ref, two_ref, lines_ref, wide_ref, third_ref, sems,
):
    copies = head_copies(plan, side_ref, gathered_ref, one_ref, two_ref, lines_ref, sems)
    grad, bottle = grad_ref[...], bottle_ref[...]
    scale = lax.rsqrt(jnp.sum(bottle * bottle, axis=-1, keepdims=True) + 1e-06)
    along = jnp.sum(grad * bottle, axis=-1, keepdims=True)
    grad_bottle = (scale * (grad - bottle * (along * scale * scale))).astype(narrow)
    grads_ref[:, pl.ds(2 * HID, BOT)] = grad_bottle
    wait_all(copies[2])
    spread_third(lines_ref, wide_ref, third_ref)
    piece = HID // 4
    for number in range(4):
        spot = pl.ds(number * piece, piece)
        back = product_right(grad_bottle, third_ref[spot, :])
        grads_ref[:, pl.ds(HID + number * piece, piece)] = (back * gelu_slope(pre_two_ref[:, spot])).astype(narrow)
    wait_all(copies[1])
    grad_two = grads_ref[:, pl.ds(HID, HID)]
    for number in range(4):
        spot = pl.ds(number * piece, piece)
        back = product_right(grad_two, two_ref[spot, :])
        grads_ref[:, spot] = (back * gelu_slope(pre_one_ref[:, spot])).astype(narrow)
    wait_all(copies[0])
    normed_grad_ref[...] = product_right(grads_ref[:, pl.ds(0, HID)], one_ref[...])


def head_pass(kernel, plan, side, inputs, gathered, shapes, waits=()):
    read = len(inputs) + 2
    return pl.pallas_call(
        lambda *refs: kernel(plan, *refs[:read], *refs[read + len(waits) :]),
        out_shape=shapes,
        in_specs=[pl.BlockSpec(memory_space=pltpu.SMEM)]
        + [pl.BlockSpec(memory_space=pltpu.VMEM)] * len(inputs)
        + [pl.BlockSpec(memory_space=pl.ANY)] * (1 + len(waits)),
        out_specs=[pl.BlockSpec(memory_space=pltpu.VMEM)] * len(shapes),
        scratch_shapes=[
            pltpu.VMEM((D, HID), narrow),
            pltpu.VMEM((HID, HID), narrow),
            pltpu.VMEM((BOT, ROW), narrow),
            pltpu.VMEM((BOT // 128, HID, 128), single),
            pltpu.VMEM((HID, BOT), narrow),
            pltpu.SemaphoreType.DMA((len(plan),)),
        ],
        compiler_params=pltpu.CompilerParams(vmem_limit_bytes=56 << 20),
        cost_estimate=pl.CostEstimate(flops=100 * 10**6, bytes_accessed=370 * 10**5, transcendentals=0),
    )(side, *inputs, gathered, *waits)


def fetch_rows(side_ref, part, gathered_ref, flat_ref, sems, first_row, last_row):
    quarter = flat_ref.shape[0] // 4
    side = side_ref[0]
    first, second = side * quarter, (1 - side) * quarter
    copies = [
        pltpu.make_async_copy(
            gathered_ref.at[pl.ds(at, quarter), owner, part],
            flat_ref.at[pl.ds(spot * quarter, quarter)],
            sems.at[spot],
        )
        for spot, (at, owner) in enumerate(((first, 0), (second, 0), (second, 1), (first, 1)))
        if spot * quarter * flat_ref.shape[1] < last_row and first_row < (spot + 1) * quarter * flat_ref.shape[1]
    ]
    for copy in copies:
        copy.start()
    return copies


def matrix_rows(flat_ref, first_row, length):
    rows = flat_ref.shape[1]
    low, high = first_row // rows, -(-(first_row + length) // rows)
    lines = flat_ref[pl.ds(low, high - low)].reshape((high - low) * rows, D)
    at = first_row - low * rows
    return lines[at : at + length]


def spread_columns(flat_ref, first_row, width, wide_ref, out_ref):
    length = width * D
    lines = matrix_rows(flat_ref, first_row, length)
    for column in range(D // 128):
        lane = slice(column * 128, (column + 1) * 128)
        wide_ref[column, pl.ds(0, length), :] = lines[:, lane].astype(single)
    for group in range(width):
        for column in range(D // 128):
            out_ref[group, :, pl.ds(column * 128, 128)] = wide_ref[
                column, pl.ds(group, D, stride=width), :
            ].astype(narrow)


def head_lanes(values, odd):
    lanes = lax.broadcasted_iota(jnp.int32, values.shape, 1)
    return jnp.where((lanes >= HEAD_DIM) == odd, values, jnp.zeros_like(values))


def join_lanes(even, odd):
    lanes = lax.broadcasted_iota(jnp.int32, even.shape, 1)
    return jnp.where(lanes >= HEAD_DIM, odd, even)


def soft_rows(query, key):
    scores = product_right(query, key) * HEAD_DIM ** (-0.5)
    spots = lax.broadcasted_iota(jnp.int32, scores.shape, 1)
    scores = jnp.where(spots < SEQ, scores, -1e30)
    terms = jnp.exp(scores - jnp.max(scores, axis=-1, keepdims=True))
    return terms / jnp.sum(terms, axis=-1, keepdims=True)


def forward_kernel(part, keep, side_ref, stream_ref, vector_ref, gathered_ref, *refs):
    out_ref = refs[0]
    if keep:
        packed_ref, mixed_ref, attn_ref, pre_ref, mlp_ref = refs[1:6]
        flat_ref, wide_ref, qkv_ref, up_ref, hidden_ref, sems = refs[6:]
    else:
        flat_ref, wide_ref, qkv_ref, up_ref, hidden_ref, packed_ref, mixed_ref, sems = refs[1:]
    copies = fetch_rows(side_ref, part, gathered_ref, flat_ref, sems, 0, MATRIX_ROWS)
    vectors = vector_ref[...].astype(single)
    stream = stream_ref[...]
    normed = (norm_parts(stream)[0] * vectors[0:1] + vectors[1:2]).astype(narrow)
    wait_all(copies)
    spread_columns(flat_ref, 0, 3, wide_ref, qkv_ref)
    spread_columns(flat_ref, 4 * D, FF // D, wide_ref, up_ref)
    w_proj = matrix_rows(flat_ref, 3 * D, D)
    w_down = matrix_rows(flat_ref, 4 * D + FF, FF)
    for group in range(3):
        packed_ref[:, pl.ds(group * D, D)] = product_plain(normed, qkv_ref[group]).astype(narrow)
    for image in range(stream.shape[0] // PAD_SEQ):
        rows = pl.ds(image * PAD_SEQ, PAD_SEQ)
        for pair in range(HEADS // 2):
            query, key, value = [
                packed_ref[rows, pl.ds(group * D + pair * 128, 128)] for group in range(3)
            ]
            done = [
                product_plain(soft_rows(head_lanes(query, odd), key).astype(narrow), value)
                for odd in (False, True)
            ]
            mixed_ref[rows, pl.ds(pair * 128, 128)] = join_lanes(*done).astype(narrow)
    attn = product_plain(mixed_ref[...], w_proj)
    middle = stream + vectors[2:3] * attn
    normed_two = (norm_parts(middle)[0] * vectors[3:4] + vectors[4:5]).astype(narrow)
    for group in range(FF // D):
        spot = pl.ds(group * D, D)
        pre = product_plain(normed_two, up_ref[group])
        if keep:
            pre_ref[:, spot] = pre
        hidden_ref[:, spot] = (0.5 * pre * (1.0 + gelu_tanh(pre))).astype(narrow)
    mlp = product_plain(hidden_ref[...], w_down)
    out_ref[...] = middle + vectors[5:6] * mlp
    if keep:
        attn_ref[...] = attn
        mlp_ref[...] = mlp


def layer_scratch(gathered):
    rows, blocks = gathered.shape[3], 2 * gathered.shape[0]
    return [
        pltpu.VMEM((blocks, rows, D), narrow),
        pltpu.VMEM((D // 128, FF, 128), single),
        pltpu.VMEM((3, D, D), narrow),
        pltpu.VMEM((FF // D, D, D), narrow),
    ]


def layer_specs_in(count):
    return (
        [pl.BlockSpec(memory_space=pltpu.SMEM)]
        + [pl.BlockSpec(memory_space=pltpu.VMEM)] * (count - 2)
        + [pl.BlockSpec(memory_space=pl.ANY)]
    )


def layer_forward(side, stream, vectors, gathered, part, keep):
    tokens = stream.shape[0]
    shapes = [jax.ShapeDtypeStruct((tokens, D), single)]
    extra = [
        jax.ShapeDtypeStruct((tokens, 3 * D), narrow),
        jax.ShapeDtypeStruct((tokens, D), narrow),
        jax.ShapeDtypeStruct((tokens, D), single),
        jax.ShapeDtypeStruct((tokens, FF), single),
        jax.ShapeDtypeStruct((tokens, D), single),
    ]
    scratch = layer_scratch(gathered) + [pltpu.VMEM((tokens, FF), narrow)]
    if keep:
        shapes = shapes + extra
    else:
        scratch = scratch + [pltpu.VMEM((tokens, 3 * D), narrow), pltpu.VMEM((tokens, D), narrow)]
    scratch.append(pltpu.SemaphoreType.DMA((4,)))
    return pl.pallas_call(
        lambda *refs: forward_kernel(part, keep, *refs),
        out_shape=shapes,
        in_specs=layer_specs_in(4),
        out_specs=[pl.BlockSpec(memory_space=pltpu.VMEM)] * len(shapes),
        scratch_shapes=scratch,
        compiler_params=pltpu.CompilerParams(vmem_limit_bytes=56 << 20),
        cost_estimate=pl.CostEstimate(flops=100 * 10**6, bytes_accessed=430 * 10**5, transcendentals=0),
    )(side, stream, vectors, gathered)


def mlp_back_kernel(
    part,
    side_ref,
    grad_ref,
    stream_ref,
    attn_ref,
    pre_ref,
    mlp_ref,
    vector_ref,
    gathered_ref,
    *refs,
):
    grad_mid_ref, weight_grad_ref, vector_grad_ref = refs[-9:-6]
    flat_ref, wide_ref, up_ref, hidden_ref, grad_pre_ref, sems = refs[-6:]
    lead = weight_grad_ref.shape[1] - 2 * FF
    weight_grad_ref[:, pl.ds(0, lead), :] = jnp.zeros((D // 128, lead, 128), single)
    copies = fetch_rows(side_ref, part, gathered_ref, flat_ref, sems, 4 * D, MATRIX_ROWS)
    vectors = vector_ref[...].astype(single)
    grad_out = grad_ref[...]
    vector_grad_ref[...] = jnp.zeros_like(vector_grad_ref)
    attn = attn_ref[...]
    middle = stream_ref[...] + vectors[2:3] * attn
    unit_two, spread_two = norm_parts(middle)
    normed_two = (unit_two * vectors[3:4] + vectors[4:5]).astype(narrow)
    vector_grad_ref[pl.ds(5, 1), :] = jnp.sum(grad_out * mlp_ref[...], axis=0, keepdims=True)
    grad_mlp = (grad_out * vectors[5:6]).astype(narrow)
    wait_all(copies)
    spread_columns(flat_ref, 4 * D, FF // D, wide_ref, up_ref)
    w_down = matrix_rows(flat_ref, 4 * D + FF, FF)
    grad_normed_two = jnp.zeros_like(grad_out)
    for group in range(FF // D):
        spot = pl.ds(group * D, D)
        pre = pre_ref[:, spot]
        bent = gelu_tanh(pre)
        hidden_ref[:, spot] = (0.5 * pre * (1.0 + bent)).astype(narrow)
        slope = 0.5 * (1.0 + bent) + 0.5 * pre * (1.0 - bent * bent) * GELU_SCALE * (
            1.0 + 3.0 * GELU_CUBE * pre * pre
        )
        grad_hidden = product_right(grad_mlp, w_down[group * D : (group + 1) * D])
        grad_pre = (grad_hidden * slope).astype(narrow)
        grad_pre_ref[:, spot] = grad_pre
        grad_normed_two = grad_normed_two + product_right(grad_pre, up_ref[group])
    for group in range(FF // D):
        spot = pl.ds(group * D, D)
        up_grad = product_left(normed_two, grad_pre_ref[:, spot])
        down_grad = product_left(hidden_ref[:, spot], grad_mlp)
        for column in range(D // 128):
            lane = slice(column * 128, (column + 1) * 128)
            weight_grad_ref[column, pl.ds(lead + group, D, stride=FF // D), :] = up_grad[:, lane]
            weight_grad_ref[column, pl.ds(lead + FF + group * D, D), :] = down_grad[:, lane]
    vector_grad_ref[pl.ds(3, 1), :] = jnp.sum(grad_normed_two * unit_two, axis=0, keepdims=True)
    vector_grad_ref[pl.ds(4, 1), :] = jnp.sum(grad_normed_two, axis=0, keepdims=True)
    grad_mid = grad_out + norm_back(grad_normed_two, unit_two, spread_two, vectors[3:4])
    vector_grad_ref[pl.ds(2, 1), :] = jnp.sum(grad_mid * attn, axis=0, keepdims=True)
    grad_mid_ref[...] = grad_mid


def attention_back_kernel(
    part,
    side_ref,
    grad_ref,
    stream_ref,
    packed_ref,
    mixed_ref,
    vector_ref,
    gathered_ref,
    *refs,
):
    grad_in_ref, weight_grad_ref, vector_grad_ref = refs[-9:-6]
    flat_ref, wide_ref, qkv_ref, grad_mixed_ref, grad_packed_ref, sems = refs[-6:]
    rest = weight_grad_ref.shape[1] - 4 * D
    weight_grad_ref[:, pl.ds(4 * D, rest), :] = jnp.zeros((D // 128, rest, 128), single)
    copies = fetch_rows(side_ref, part, gathered_ref, flat_ref, sems, 0, 4 * D)
    vectors = vector_ref[...].astype(single)
    vector_grad_ref[...] = jnp.zeros_like(vector_grad_ref)
    grad_mid = grad_ref[...]
    stream = stream_ref[...]
    grad_attn = (grad_mid * vectors[2:3]).astype(narrow)
    proj_grad = product_left(mixed_ref[...], grad_attn)
    for column in range(D // 128):
        weight_grad_ref[column, pl.ds(3 * D, D), :] = proj_grad[:, column * 128 : (column + 1) * 128]
    wait_all(copies)
    spread_columns(flat_ref, 0, 3, wide_ref, qkv_ref)
    w_proj = matrix_rows(flat_ref, 3 * D, D)
    grad_mixed_ref[...] = product_right(grad_attn, w_proj).astype(narrow)
    for image in range(stream.shape[0] // PAD_SEQ):
        rows = pl.ds(image * PAD_SEQ, PAD_SEQ)
        for pair in range(HEADS // 2):
            query, key, value = [
                packed_ref[rows, pl.ds(group * D + pair * 128, 128)] for group in range(3)
            ]
            grad_mixed = grad_mixed_ref[rows, pl.ds(pair * 128, 128)]
            parts = []
            for odd in (False, True):
                probs = soft_rows(head_lanes(query, odd), key)
                grad_probs = product_right(head_lanes(grad_mixed, odd), value)
                grad_value = product_left(probs.astype(narrow), grad_mixed)
                grad_scores = probs * (grad_probs - jnp.sum(probs * grad_probs, axis=-1, keepdims=True))
                grad_raw = (grad_scores * HEAD_DIM ** (-0.5)).astype(narrow)
                parts.append((product_plain(grad_raw, key), product_left(grad_raw, query), grad_value))
            for group in range(3):
                grad_packed_ref[rows, pl.ds(group * D + pair * 128, 128)] = join_lanes(
                    parts[0][group], parts[1][group]
                ).astype(narrow)
    unit_one, spread_one = norm_parts(stream)
    normed = (unit_one * vectors[0:1] + vectors[1:2]).astype(narrow)
    grad_normed = jnp.zeros_like(grad_mid)
    for group in range(3):
        grad_part = grad_packed_ref[:, pl.ds(group * D, D)]
        grad_normed = grad_normed + product_right(grad_part, qkv_ref[group])
        qkv_grad = product_left(normed, grad_part)
        for column in range(D // 128):
            lane = slice(column * 128, (column + 1) * 128)
            weight_grad_ref[column, pl.ds(group, D, stride=3), :] = qkv_grad[:, lane]
    vector_grad_ref[pl.ds(0, 1), :] = jnp.sum(grad_normed * unit_one, axis=0, keepdims=True)
    vector_grad_ref[pl.ds(1, 1), :] = jnp.sum(grad_normed, axis=0, keepdims=True)
    grad_in_ref[...] = grad_mid + norm_back(grad_normed, unit_one, spread_one, vectors[0:1])


def layer_back(kernel, part, weight_rows, side, inputs, vectors, gathered, waits, held, columns, buffers):
    tokens = inputs[0].shape[0]
    rows, blocks = gathered.shape[3], 2 * gathered.shape[0]
    return pl.pallas_call(
        lambda *refs: kernel(part, *refs[: len(refs) - 6 - len(held)], *refs[len(refs) - 6 :]),
        out_shape=[
            jax.ShapeDtypeStruct((tokens, D), single),
            jax.ShapeDtypeStruct((D // 128, weight_rows, 128), single),
            jax.ShapeDtypeStruct((8, D), single),
        ]
        + [jax.ShapeDtypeStruct(array.shape, array.dtype) for array in held],
        in_specs=layer_specs_in(len(inputs) + 3) + [pl.BlockSpec(memory_space=pl.ANY)] * (len(waits) + len(held)),
        out_specs=[pl.BlockSpec(memory_space=pltpu.VMEM)] * 3 + [pl.BlockSpec(memory_space=pl.ANY)] * len(held),
        input_output_aliases={len(inputs) + 3 + len(waits) + number: 3 + number for number in range(len(held))},
        scratch_shapes=[
            pltpu.VMEM((blocks, rows, D), narrow),
            pltpu.VMEM((D // 128, columns * D, 128), single),
            pltpu.VMEM((columns, D, D), narrow),
        ]
        + [pltpu.VMEM((tokens, width), narrow) for width in buffers]
        + [pltpu.SemaphoreType.DMA((4,))],
        compiler_params=pltpu.CompilerParams(vmem_limit_bytes=56 << 20),
        cost_estimate=pl.CostEstimate(flops=100 * 10**6, bytes_accessed=600 * 10**5, transcendentals=0),
    )(side, *inputs, vectors, gathered, *waits, *held)


def pair_rows_of(block_rows):
    pair = 2 * block_rows
    return 4 * D // pair * pair, -(-4 * D // pair) * pair


def mlp_back(side, grad_out, saved, vectors, gathered, part, waits, held):
    stream, packed, mixed, attn, pre, mlp = saved
    return layer_back(
        mlp_back_kernel, part, MATRIX_ROWS - pair_rows_of(gathered.shape[3])[0], side,
        (grad_out, stream, attn, pre, mlp), vectors, gathered, waits, held,
        FF // D, (FF, FF),
    )


def attention_back(side, grad_mid, saved, vectors, gathered, part, waits, held):
    stream, packed, mixed, attn, pre, mlp = saved
    return layer_back(
        attention_back_kernel, part, pair_rows_of(gathered.shape[3])[1], side,
        (grad_mid, stream, packed, mixed), vectors, gathered, waits, held,
        3, (D, 3 * D),
    )


def after(value, *tokens):
    def kernel(*refs):
        refs[-1][...] = refs[0][...]

    return pl.pallas_call(
        kernel,
        out_shape=jax.ShapeDtypeStruct(value.shape, value.dtype),
        in_specs=[pl.BlockSpec(memory_space=pltpu.VMEM)] + [pl.BlockSpec(memory_space=pl.ANY)] * len(tokens),
        out_specs=pl.BlockSpec(memory_space=pltpu.VMEM),
    )(value, *tokens)


def embed_back_kernel(grad_ref, patch_ref, shown_ref, gain_ref, vector_ref, *refs):
    out_ref = refs[-1]
    grad = grad_ref[...]
    images = grad.shape[0] // PAD_SEQ
    shown = shown_ref[...]
    position = jnp.zeros((PAD_SEQ, D), single)
    token = jnp.zeros((1, D), single)
    patch_grads = []
    for image in range(images):
        here = grad[image * PAD_SEQ : (image + 1) * PAD_SEQ]
        position = position + here
        rows = here[1:SEQ]
        seen = shown[image * PATCHES : (image + 1) * PATCHES]
        token = token + jnp.sum(rows * (1.0 - seen), axis=0, keepdims=True)
        patch_grads.append((rows * seen).astype(narrow))
    patch_grad = product_left(patch_ref[...], jnp.concatenate(patch_grads))
    out_ref[...] = jnp.zeros_like(out_ref)
    for column in range(D // 128):
        lane = slice(column * 128, (column + 1) * 128)
        out_ref[column, pl.ds(0, PIX), :] = patch_grad[:, lane]
        out_ref[column, pl.ds(PIX, SEQ), :] = position[:SEQ, lane]
        out_ref[column, pl.ds(PIX + SEQ, 1), :] = position[0:1, lane]
        out_ref[column, pl.ds(PIX + SEQ + 1, 1), :] = token[:, lane]
        out_ref[column, pl.ds(PIX + SEQ + 2, 2), :] = gain_ref[:, lane]
        out_ref[column, pl.ds(EMBED_ROWS, vector_ref.shape[0]), :] = vector_ref[:, lane]


def embed_back(grad, patch_rows, shown, gains, vector_grads, rows, waits):
    return pl.pallas_call(
        embed_back_kernel,
        out_shape=jax.ShapeDtypeStruct((D // 128, rows, 128), single),
        in_specs=[pl.BlockSpec(memory_space=pltpu.VMEM)] * 5 + [pl.BlockSpec(memory_space=pl.ANY)] * len(waits),
        out_specs=pl.BlockSpec(memory_space=pltpu.VMEM),
        compiler_params=pltpu.CompilerParams(vmem_limit_bytes=40 << 20),
        cost_estimate=pl.CostEstimate(flops=100 * 10**6, bytes_accessed=37 * 10**5, transcendentals=0),
    )(grad, patch_rows, shown, gains, vector_grads, *waits)


def proto_units(values):
    rounded = values.astype(narrow).astype(single)
    scale = lax.rsqrt(jnp.sum(rounded * rounded, axis=-1, keepdims=True) + 1e-06)
    return rounded, scale, (rounded * scale).astype(narrow)


def proto_terms(teacher_z, student_z, teacher_unit, student_unit, centre_column):
    teacher_logits = product_right(teacher_unit, teacher_z)
    logits = product_right(student_unit, student_z)
    teacher_exp = jnp.exp((teacher_logits - centre_column) * (1.0 / tau_teacher))
    student_exp = jnp.exp(logits * (1.0 / tau_student))
    return teacher_logits, logits, teacher_exp, student_exp


def logits_kernel(
    teacher_z_ref,
    student_z_ref,
    teacher_ref,
    student_ref,
    centre_ref,
    class_ref,
    mixed_ref,
    mixed_teacher_ref,
    sums_ref,
    centre_sum_ref,
    student_mix_ref,
    teacher_mix_ref,
    totals_ref,
):
    step = pl.program_id(0)

    @pl.when(step == 0)
    def _():
        student_mix_ref[...] = jnp.zeros_like(student_mix_ref)
        teacher_mix_ref[...] = jnp.zeros_like(teacher_mix_ref)
        totals_ref[...] = jnp.zeros_like(totals_ref)

    teacher_unit = proto_units(teacher_ref[...])[2]
    student_unit = proto_units(student_ref[...])[2]
    teacher_logits, logits, teacher_exp, student_exp = proto_terms(
        teacher_z_ref[...], student_z_ref[...], teacher_unit, student_unit, centre_ref[...]
    )
    totals_ref[pl.ds(0, 1), :] += jnp.sum(teacher_exp, axis=0, keepdims=True)
    totals_ref[pl.ds(1, 1), :] += jnp.sum(student_exp, axis=0, keepdims=True)
    totals_ref[pl.ds(2, 1), :] += jnp.sum(teacher_exp * logits, axis=0, keepdims=True)
    centre_sum_ref[...] = jnp.sum(teacher_logits * class_ref[0:1], axis=1, keepdims=True)
    student_mix_ref[...] += product_left(student_unit, student_exp.astype(narrow))
    teacher_mix_ref[...] += product_left(student_unit, teacher_exp.astype(narrow))

    @pl.when(step == pl.num_programs(0) - 1)
    def _():
        mixed_ref[...] = student_mix_ref[...].T
        mixed_teacher_ref[:, pl.ds(0, BOT)] = teacher_mix_ref[...].T
        lower = jnp.zeros((128 - totals_ref.shape[0], totals_ref.shape[1]), single)
        mixed_teacher_ref[:, pl.ds(BOT, 128)] = jnp.concatenate([totals_ref[...], lower]).T
        sums_ref[...] = totals_ref[...]


def proto_specs(rows, block):
    whole = pl.BlockSpec((rows, BOT), lambda i: (0, 0))
    table = pl.BlockSpec((block, BOT), lambda i: (i, 0))
    column = pl.BlockSpec((block, 1), lambda i: (i, 0))
    lines = pl.BlockSpec((8, rows), lambda i: (0, 0))
    return whole, table, column, lines


def logits_pass(teacher_z, student_z, teacher, student, centre_column, class_lines):
    rows, protos_here = teacher_z.shape[0], student.shape[0]
    block = protos_here // 4
    whole, table, column, lines = proto_specs(rows, block)
    return pl.pallas_call(
        logits_kernel,
        grid=(4,),
        out_shape=[
            jax.ShapeDtypeStruct((rows, BOT), single),
            jax.ShapeDtypeStruct((rows, BOT + 128), single),
            jax.ShapeDtypeStruct((8, rows), single),
            jax.ShapeDtypeStruct((protos_here, 1), single),
        ],
        in_specs=[whole, whole, table, table, column, lines],
        out_specs=[whole, pl.BlockSpec((rows, BOT + 128), lambda i: (0, 0)), lines, column],
        scratch_shapes=[
            pltpu.VMEM((BOT, rows), single),
            pltpu.VMEM((BOT, rows), single),
            pltpu.VMEM((8, rows), single),
        ],
        compiler_params=pltpu.CompilerParams(vmem_limit_bytes=56 << 20),
        cost_estimate=pl.CostEstimate(flops=100 * 10**6, bytes_accessed=520 * 10**5, transcendentals=0),
    )(teacher_z, student_z, teacher, student, centre_column, class_lines)


def proto_grad_kernel(
    held, teacher_z_ref, student_z_ref, teacher_ref, student_ref, centre_ref, scale_ref, *refs
):
    grad_ref, square_ref = refs[held : held + 2]
    step = pl.program_id(0)

    @pl.when(step == 0)
    def _():
        square_ref[...] = jnp.zeros_like(square_ref)

    teacher_unit = proto_units(teacher_ref[...])[2]
    rounded, scale, student_unit = proto_units(student_ref[...])
    student_z = student_z_ref[...]
    _, _, teacher_exp, student_exp = proto_terms(
        teacher_z_ref[...], student_z, teacher_unit, student_unit, centre_ref[...]
    )
    grad_logits = (student_exp * scale_ref[0:1] - teacher_exp * scale_ref[1:2]).astype(narrow)
    unit_grad = product_plain(grad_logits, student_z)
    along = jnp.sum(unit_grad * rounded, axis=-1, keepdims=True)
    grad = scale * (unit_grad - rounded * (along * scale * scale))
    grad_ref[...] = grad
    square_ref[...] += jnp.broadcast_to(jnp.sum(grad * grad), square_ref.shape)


def proto_grad_pass(teacher_z, student_z, teacher, student, centre_column, scale_lines, held):
    rows, protos_here = teacher_z.shape[0], student.shape[0]
    block = protos_here // 4
    whole, table, column, lines = proto_specs(rows, block)
    return pl.pallas_call(
        lambda *refs: proto_grad_kernel(len(held), *refs),
        grid=(4,),
        out_shape=[
            jax.ShapeDtypeStruct((protos_here, BOT), single),
            jax.ShapeDtypeStruct((8, 128), single),
        ]
        + [jax.ShapeDtypeStruct(array.shape, array.dtype) for array in held],
        in_specs=[whole, whole, table, table, column, lines]
        + [pl.BlockSpec(memory_space=pl.ANY)] * len(held),
        out_specs=[table, pl.BlockSpec((8, 128), lambda i: (0, 0))]
        + [pl.BlockSpec(memory_space=pl.ANY)] * len(held),
        input_output_aliases={6 + number: 2 + number for number in range(len(held))},
        compiler_params=pltpu.CompilerParams(vmem_limit_bytes=56 << 20),
        cost_estimate=pl.CostEstimate(flops=100 * 10**6, bytes_accessed=400 * 10**5, transcendentals=0),
    )(teacher_z, student_z, teacher, student, centre_column, scale_lines, *held)


def proto_update(factor, student, moment, second, teacher, grad):
    def kernel(factor_ref, *refs):
        weight, moment, second, teacher, grad = [ref[...] for ref in refs[:5]]
        done = adam_update(weight, moment, second, grad * factor_ref[0], teacher)
        for ref, value in zip(refs[5:], done):
            ref[...] = value

    block = student.shape[0] // 4
    table = pl.BlockSpec((block, BOT), lambda i: (i, 0))
    return pl.pallas_call(
        kernel,
        grid=(4,),
        out_shape=[
            jax.ShapeDtypeStruct(student.shape, narrow if number == 3 else single) for number in range(5)
        ],
        in_specs=[pl.BlockSpec(memory_space=pltpu.SMEM)] + [table] * 5,
        out_specs=[table] * 5,
        compiler_params=pltpu.CompilerParams(vmem_limit_bytes=60 << 20),
        cost_estimate=pl.CostEstimate(flops=10**7, bytes_accessed=2 * 10**7, transcendentals=0),
    )(factor.reshape(1), student, moment, second, teacher, grad)


def head_grads_kernel(
    held, place_ref, inputs_ref, grads_ref, *refs,
):
    own_ref, partner_ref = refs[len(refs) - 9 - held :][:2] if held else refs[-9:-7]
    window_ref, rows_ref, product_ref, third_ref, bottle_ref, line_ref, sems = refs[-7:]
    slot = own_ref.shape[0]
    lead = product_ref.shape[0] - window_ref.shape[1]
    number = lax.broadcasted_iota(jnp.int32, (slot, 1), 0)
    product_ref[pl.ds(0, lead), :] = jnp.zeros((lead, ROW), single)

    def block(at, out_ref):
        column = pl.multiple_of(place_ref[at], 128)
        grad_column = pl.multiple_of(place_ref[at + 3], 128)
        copies = [
            pltpu.make_async_copy(
                inputs_ref.at[:, pl.ds(column, window_ref.shape[1])], window_ref, sems.at[0]
            ),
            pltpu.make_async_copy(grads_ref.at[:, pl.ds(grad_column, ROW)], rows_ref, sems.at[1]),
        ]
        for copy in copies:
            copy.start()
        for copy in copies:
            copy.wait()
        window = window_ref[...]
        for piece in range(4):
            spot = pl.ds(piece * (ROW // 4), ROW // 4)
            product_ref[pl.ds(lead, window.shape[1]), spot] = product_left(window, rows_ref[:, spot])
        from_row = pl.multiple_of(lead + place_ref[at + 1], 8)
        kept = jnp.where(number < place_ref[at + 2], product_ref[pl.ds(from_row, slot), :], 0.0)
        out_ref[...] = kept.astype(out_ref.dtype)

    @pl.when(place_ref[8] == 0)
    def _():
        block(0, own_ref)

    @pl.when(place_ref[8] == 1)
    def _():
        column = pl.multiple_of(place_ref[9], 128)
        copies = [
            pltpu.make_async_copy(
                inputs_ref.at[:, pl.ds(column, third_ref.shape[1])], third_ref, sems.at[0]
            ),
            pltpu.make_async_copy(grads_ref.at[:, pl.ds(2 * HID, BOT)], bottle_ref, sems.at[1]),
        ]
        for copy in copies:
            copy.start()
        for copy in copies:
            copy.wait()
        third = product_left(third_ref[...], bottle_ref[...])
        for lane in range(BOT // 128):
            line_ref[lane] = third[:, lane * 128 : (lane + 1) * 128]
        for group in range(ROW // BOT):
            for lane in range(BOT // 128):
                value = line_ref[lane, pl.ds(group, slot, stride=ROW // BOT), :]
                own_ref[:, pl.ds(group * BOT + lane * 128, 128)] = jnp.where(
                    number < place_ref[2], value, 0.0
                )

    block(4, partner_ref)


def head_grads(place, inputs_all, grads_all, slot, lead, waits, held):
    rows = inputs_all.shape[0]
    wide = slot * ROW // BOT
    return pl.pallas_call(
        lambda *refs: head_grads_kernel(len(held), *refs),
        out_shape=[jax.ShapeDtypeStruct((slot, ROW), kind) for kind in (single, narrow)]
        + [jax.ShapeDtypeStruct(array.shape, array.dtype) for array in held],
        in_specs=[pl.BlockSpec(memory_space=pltpu.SMEM)]
        + [pl.BlockSpec(memory_space=pl.ANY)] * (2 + len(waits) + len(held)),
        out_specs=[pl.BlockSpec(memory_space=pltpu.VMEM)] * 2
        + [pl.BlockSpec(memory_space=pl.ANY)] * len(held),
        input_output_aliases={3 + len(waits) + number: 2 + number for number in range(len(held))},
        scratch_shapes=[
            pltpu.VMEM((rows, 256), narrow),
            pltpu.VMEM((rows, ROW), narrow),
            pltpu.VMEM((lead + 256, ROW), single),
            pltpu.VMEM((rows, wide), narrow),
            pltpu.VMEM((rows, BOT), narrow),
            pltpu.VMEM((BOT // 128, wide, 128), single),
            pltpu.SemaphoreType.DMA((2,)),
        ],
        compiler_params=pltpu.CompilerParams(vmem_limit_bytes=56 << 20),
        cost_estimate=pl.CostEstimate(flops=100 * 10**6, bytes_accessed=370 * 10**5, transcendentals=0),
    )(place, inputs_all, grads_all, *waits, *held)


def close_local(
    patches,
    masked,
    slot_used,
    stem,
    stem_moment,
    stem_second,
    stem_teacher,
    layers,
    layer_moment,
    layer_second,
    layer_teacher,
    protos,
    proto_moment,
    proto_second,
    proto_teacher,
    centre,
):
    count = 1 << len(BITS)
    half = count // 2
    me = lax.axis_index("dev")
    across = MASKS["b"]
    student_side = me >= half
    groups = [list(range(half)), list(range(half, count))]
    quarter = half // 2
    swap = jnp.where(student_side, quarter, 0)
    side = student_side.astype(jnp.int32).reshape(1)
    images_here = patches.shape[0]
    rows_here = images_here * 17
    pair_rows = -(-2 * rows_here // 16) * 16
    more_rows = pair_rows - 2 * rows_here
    stem_piece = stem.shape[0]
    layer_piece = layers.shape[1]
    block_rows = MATRIX_ROWS // count
    block = block_rows * D
    tail = layer_piece * count - MATRIX_ROWS * D
    drift = layer_piece - block
    bounds = head_bounds(count, stem_piece)
    sizes = [bounds[i + 1] - bounds[i] for i in range(count)]
    slot = max(sizes)
    starts = [b * ROW + EMBED_FLAT - stem_piece * i for i, b in enumerate(bounds[:-1])]
    first_w2 = bounds.index(D)
    first_w3 = bounds.index(D + HID)
    row_index = jnp.concatenate([jnp.zeros((images_here, 1), jnp.int32), masked + 1], axis=1)
    masked_here = jnp.any(
        masked[:, :, None] == jnp.arange(PATCHES, dtype=jnp.int32)[None, None, :], axis=1
    )
    kept = slot_used.astype(single)

    front = 16
    early_rows = -(-stem_piece // D)
    late_start = early_rows * D - stem_piece
    embed_rows = -(-early_rows // 16) * 16
    own_layers = jnp.concatenate([layer_teacher, layers])
    own_tail = own_layers[:, layer_piece - tail :].reshape(2 * LAYERS, tail // 128, 128)
    before = lax.ppermute(own_tail, "dev", step_pairs(count, 1))
    last_lines = lax.ppermute(
        jnp.pad(own_tail, ((0, 0), (0, 24 - tail // 128), (0, 0))), "dev", [(count - 1, 0)]
    )
    head_span = GROUP * ROW
    stems = jnp.stack([as_lanes(stem_teacher), as_lanes(stem)])
    stems_next = lax.ppermute(stems[:, : head_span // 128], "dev", step_pairs(count, -1))
    def per_device(rows):
        return lax.dynamic_slice(jnp.array(rows, jnp.int32), (me, 0), (1, len(rows[0]))).reshape(-1)

    def spots(*values):
        return [part for value in values for part in (value // 128, value % 128)]

    place = per_device(
        [
            spots(starts[i] + front * 128, front * 128 + (0 if i == 0 else late_start), tail - drift * i)
            for i in range(count)
        ]
    )
    head_blocks, layer_blocks, embed_blocks, vector_blocks = own_blocks(
        place,
        stems,
        stems_next,
        as_lanes(own_layers),
        before,
        last_lines,
        (front, stem_piece, layer_piece, tail),
        slot,
        block_rows,
        embed_rows,
    )

    other_layers = lax.ppermute(layer_blocks, "dev", pairs(count, across))
    both_layers = jnp.where(
        student_side,
        jnp.stack([other_layers, layer_blocks]),
        jnp.stack([layer_blocks, other_layers]),
    )
    gathered = lax.all_gather(both_layers, "dev", axis=0, axis_index_groups=groups)
    head_out = jnp.where(student_side, head_blocks[0], head_blocks[1])
    head_keep = jnp.where(student_side, head_blocks[1], head_blocks[0])
    head_got = lax.ppermute(head_out, "dev", pairs(count, across))
    both_head = jnp.where(
        student_side, jnp.stack([head_got, head_keep]), jnp.stack([head_keep, head_got])
    )

    seed = jnp.concatenate([embed_blocks.reshape(2 * embed_rows, D), vector_blocks.reshape(8 * 2 * LAYERS, D)])
    third = -(-seed.shape[0] // 48) * 16
    spread_parts = []
    for number, order in enumerate(("xyba", "baxy", "ybax")):
        spread = seed[number * third : (number + 1) * third]
        reached = [0, 1]
        for name in order:
            moves = [(i, i ^ MASKS[name]) for i in reached]
            got = lax.ppermute(spread, "dev", moves)
            targets = [t for s, t in moves]
            is_target = jnp.array([i in targets for i in range(count)])[me]
            spread = jnp.where(is_target, got, spread)
            reached = reached + targets
        spread_parts.append(spread)
    spread = jnp.concatenate(spread_parts)
    other = lax.ppermute(spread, "dev", pairs(count, 1))
    is_even = me % 2 == 0
    even = jnp.where(is_even, spread, other)
    odd = jnp.where(is_even, other, spread)
    embed_all = [
        jnp.concatenate(
            [
                even[m * embed_rows : m * embed_rows + early_rows],
                odd[m * embed_rows : m * embed_rows + EMBED_ROWS - early_rows],
            ]
        )
        for m in range(2)
    ]
    gathered_head = lax.all_gather(after(both_head, gathered, even, odd), "dev", axis=0, axis_index_groups=groups)
    vectors_all = even[2 * embed_rows :].reshape(2, LAYERS, 8, D)

    plan = []
    for i in range(1, count):
        target = 0 if i < first_w2 else 1 if i < first_w3 else 2
        row = bounds[i] - (0, D, D + HID)[target]
        skip = max(-row, 0)
        owner = 1 if i >= half else 0
        plan.append((i ^ across if owner else i, owner, skip, sizes[i] - skip, target, row + skip))

    def embed_parts(model):
        rows = embed_all[model]
        return (rows[:PIX], rows[PIX : PIX + SEQ], rows[PIX + SEQ :], None, None, None)

    def head_rows(stream, extras):
        chosen = jnp.take_along_axis(stream, row_index[:, :, None], axis=1).reshape(rows_here, D)
        normed = layer_norm(chosen, extras[2].astype(single), extras[3].astype(single)).astype(narrow)
        return chosen, normed

    def start_rows(parts, student):
        stream = embed(parts, patches, masked_here, student)
        return jnp.pad(stream, ((0, 0), (0, PAD_SEQ - SEQ), (0, 0))).reshape(images_here * PAD_SEQ, D)

    student_parts = embed_parts(1)
    stream = start_rows(student_parts, True)
    saved_layers = []
    for layer_index in range(LAYERS):
        before_layer = stream
        stream, *saved = layer_forward(
            side, stream, vectors_all[1, layer_index], gathered, LAYERS + layer_index, True
        )
        saved_layers.append((before_layer, *saved))
    teacher_parts = embed_parts(0)
    teacher_stream = start_rows(teacher_parts, False)
    for layer_index in range(LAYERS):
        teacher_stream = layer_forward(
            side, teacher_stream, vectors_all[0, layer_index], gathered, layer_index, False
        )[0]
    stream = stream.reshape(images_here, PAD_SEQ, D)
    teacher_stream = teacher_stream.reshape(images_here, PAD_SEQ, D)
    chosen, student_normed = head_rows(stream, student_parts[2])
    teacher_normed = head_rows(teacher_stream, teacher_parts[2])[1]

    normed_got = lax.ppermute(
        jnp.where(student_side, teacher_normed, student_normed), "dev", pairs(count, across)
    )
    normed = jnp.where(
        student_side,
        jnp.concatenate([normed_got, student_normed]),
        jnp.concatenate([teacher_normed, normed_got]),
    )
    normed = jnp.pad(normed, ((0, more_rows), (0, 0)))
    third_end = (bounds[-2] - D - HID + slot) * (ROW // BOT)
    acts_width = D + HID + max(third_end, HID)
    unit_z, acts, bottleneck, pre_one, pre_two = head_pass(
        head_up_kernel,
        plan,
        side,
        (normed,),
        gathered_head,
        [
            jax.ShapeDtypeStruct((pair_rows, BOT), narrow),
            jax.ShapeDtypeStruct((pair_rows, acts_width), narrow),
            jax.ShapeDtypeStruct((pair_rows, BOT), single),
            jax.ShapeDtypeStruct((pair_rows, HID), single),
            jax.ShapeDtypeStruct((pair_rows, HID), single),
        ],
    )
    inputs_all = lax.all_gather(acts, "dev", axis=0, axis_index_groups=groups).reshape(half * pair_rows, -1)

    all_rows = half * pair_rows
    flag_row = 2 * rows_here
    kept_row = jnp.broadcast_to(kept[:, None] * (1.0 / 128.0), (images_here, 17)).reshape(1, rows_here)
    kept_row = jnp.pad(kept_row.astype(narrow), ((0, 0), (0, BOT - rows_here)))
    z_pair = cube_gather(jnp.concatenate([unit_z[:flag_row], kept_row, unit_z[flag_row + 1 :]]), "b")
    teacher_z_all = cube_gather(z_pair[0], "xygc")
    student_z_all = cube_gather(z_pair[1], "gxyc").reshape((2,) * 4 + (pair_rows, BOT))
    student_z_all = jnp.transpose(student_z_all, (0, 3, 1, 2, 4, 5)).reshape(half, pair_rows, BOT)
    all_kept = jnp.concatenate(
        [
            teacher_z_all[:, flag_row, :rows_here],
            student_z_all[:, flag_row, :rows_here],
            jnp.zeros((half, more_rows), narrow),
        ],
        axis=1,
    )
    all_kept = all_kept.astype(single).reshape(all_rows) * 128.0
    teacher_z_all = teacher_z_all.reshape(all_rows, BOT)
    student_z_all = student_z_all.reshape(all_rows, BOT)
    protos_here = protos.shape[0]
    own_centre = lax.dynamic_slice(centre, (me * protos_here,), (protos_here,))
    centre_column = own_centre.reshape(protos_here, 1)
    spot_in_pair = jnp.arange(all_rows) % pair_rows
    is_class = (spot_in_pair % 17) == 0
    class_kept = jnp.where(is_class, all_kept, 0.0)
    row_weight = jnp.where(is_class, all_kept, all_kept * (1.0 / 16.0))
    count_total = jnp.sum(class_kept)

    def lines(*values):
        return jnp.pad(jnp.stack(values), ((0, 8 - len(values)), (0, 0)))

    mixed_student, mixed_teacher, sums, centre_sum = logits_pass(
        teacher_z_all, student_z_all, proto_teacher, protos, centre_column, lines(class_kept)
    )
    by_pair = (2,) * 4 + (pair_rows, -1)
    mixed_own = jnp.concatenate(
        [
            cube_scatter(mixed_student.reshape(by_pair), "cgyx", "cgyx"),
            cube_scatter(mixed_teacher.reshape(by_pair), "cgyx", "cxyg"),
        ],
        axis=1,
    )
    mixed_own = mixed_own + lax.ppermute(
        mixed_own.astype(narrow), "dev", [(i, i ^ across) for i in range(half)]
    ).astype(single)
    scale = row_weight / tau_student
    flags = bit_flags(me)
    pair_at = flags["c"] * 8 + flags["g"] * 4 + flags["y"] * 2 + flags["x"]
    own_scale = lax.dynamic_slice(scale, (pair_at * pair_rows,), (pair_rows,))[:, None]
    grad_unit_z = own_scale * (
        mixed_own[:, :BOT] / mixed_own[:, 2 * BOT + 1 : 2 * BOT + 2]
        - mixed_own[:, BOT : 2 * BOT] / mixed_own[:, 2 * BOT : 2 * BOT + 1]
    )
    own_new_centre = (
        centre_keep * own_centre + (1.0 - centre_keep) * centre_sum.reshape(protos_here) / count_total
    )

    grads, grad_normed = head_pass(
        head_down_kernel,
        plan,
        side,
        (grad_unit_z, bottleneck, pre_one, pre_two),
        gathered_head,
        [
            jax.ShapeDtypeStruct((pair_rows, 2 * HID + BOT), narrow),
            jax.ShapeDtypeStruct((pair_rows, D), single),
        ],
    )
    width = grads.shape[1]
    wide = max(protos_here, all_rows)
    carried = jnp.stack(
        [jnp.pad(row, (0, wide - row.shape[0])) for row in (own_new_centre, sums[0], sums[1], sums[2])]
    )
    carried_rows = 3 * carried.shape[0]
    assert carried_rows <= more_rows and wide <= width
    high = carried.astype(narrow)
    middle = (carried - high.astype(single)).astype(narrow)
    low = (carried - high.astype(single) - middle.astype(single)).astype(narrow)
    carried = jnp.pad(jnp.concatenate([high, middle, low]), ((0, more_rows - carried_rows), (0, width - wide)))
    grads = jnp.concatenate([grads[: 2 * rows_here], carried])
    grads_all = lax.all_gather(grads, "dev", axis=0, axis_index_groups=groups).reshape(half * pair_rows, -1)
    normed_back = lax.ppermute(
        grad_normed[:rows_here], "dev", [(i, i ^ across) for i in range(half, count)]
    )
    own_grad_normed = jnp.where(student_side, grad_normed[rows_here : 2 * rows_here], normed_back)
    extras = student_parts[2].astype(single)
    grad_chosen, grad_gain, grad_bias = jax.vjp(layer_norm, chosen, extras[2], extras[3])[1](
        own_grad_normed
    )
    image_index = jnp.arange(images_here, dtype=jnp.int32)[:, None]
    grad_stream = (
        jnp.zeros(stream.shape, single)
        .at[image_index, row_index]
        .add(grad_chosen.reshape(images_here, 17, D))
    )

    grad_stream = grad_stream.reshape(images_here * PAD_SEQ, D)
    middle_row = block_rows // 2
    vector_grads = [None] * LAYERS

    def halves(array):
        middle = array.shape[-2] // 2
        return [array[..., :middle, :], array[..., middle:, :]]

    def cuts(parts, names, order):
        return [cut(part, name, axis, 1) for part, name, axis in zip(parts, names, order)]

    def moves(pieces, order):
        return [move(sent, kept, axis) for (sent, kept, left), axis in zip(pieces, order)]

    def over_core(weight_grad, rows):
        pairs_of = weight_grad.reshape(D // 128, -1, 2, rows, 128)
        return move(*cut(pairs_of, "pc", "c", 1)[:2], "c")

    def core_cut(weight_grad, rows):
        return cut(weight_grad.reshape(D // 128, -1, 2, rows, 128), "pc", "c", 1)[:2]

    def start(late, early, *others):
        shared_pair = 4 * D // (2 * block_rows)
        whole = jnp.concatenate(
            [
                early[:, :shared_pair],
                early[:, shared_pair:] + late[:, : early.shape[1] - shared_pair],
                late[:, early.shape[1] - shared_pair :],
            ],
            axis=1,
        )
        parts = [jnp.concatenate(pieces, axis=2) for pieces in zip(*[halves(array) for array in (whole, *others)])]
        by_bits = [part.reshape((D // 128, 2, 2, 2, 2) + part.shape[2:]) for part in parts]
        return (cuts(by_bits, ["bayx"] * 2, rounds[0]), 0)

    rounds = (("x", "b"), ("y", "a"), ("b", "x"), ("a", "y"))

    def advance(state):
        pieces, stage = state
        parts = moves(pieces, rounds[stage])
        names = [left for sent, kept, left in pieces]
        return cuts(parts, names, rounds[stage + 1]), stage + 1

    def finish(state):
        while state[1] < len(rounds) - 1:
            state = advance(state)
        return moves(state[0], rounds[-1])

    def sends(states):
        return tuple(sent for pieces, stage in states for sent, kept, left in pieces)

    def block_place(i):
        column = max(bounds[i], 0) // 128 * 128
        grad_column = 0 if i < first_w2 else HID
        return [column, bounds[i] - column if i else 0, sizes[i] if i else 0, grad_column]

    def third_place(i):
        return [0, 0, sizes[i], 0]

    place = per_device(
        [
            (third_place(i) if i >= first_w3 else block_place(i))
            + block_place(i ^ across)
            + [int(i >= first_w3), D + HID + max(bounds[i] - D - HID, 0) * (ROW // BOT)]
            for i in range(count)
        ]
    )
    started = []
    held_block = None
    waits = ()
    for layer_index in reversed(range(LAYERS)):
        saved, vectors = saved_layers[layer_index], vectors_all[1, layer_index]
        part = LAYERS + layer_index
        grad_stream, late_grad, late_vectors, *held_block = mlp_back(
            side,
            grad_stream,
            saved,
            vectors,
            gathered,
            part,
            waits + sends(started),
            [partner_block_grad] if started else [],
        )
        late = over_core(late_grad, block_rows)
        started = [advance(state) for state in started]
        if started:
            block_got = lax.ppermute(held_block[0], "dev", [(i, i ^ across) for i in range(half, count)])
        grad_stream, early_grad, early_vectors, *held_block = attention_back(
            side,
            grad_stream,
            saved,
            vectors,
            gathered,
            part,
            sends(started),
            [own_block_grad] if started else [],
        )
        vector_grads[layer_index] = (late_vectors + early_vectors)[:6]
        if layer_index == LAYERS - 1:
            sent, stay = core_cut(early_grad, block_rows)
            own_block_grad, partner_block_grad, stay = head_grads(
                place, inputs_all, grads_all, slot, -min(bounds[1], 0), (early_vectors,), [stay]
            )
            waits = (own_block_grad,)
        started = [advance(state) for state in started]
        if layer_index > 0:
            started.append(start(late, move(sent, stay, "c")))
    own_block_grad = held_block[0]
    rows = grads_all.reshape(half, pair_rows, width)[:, 2 * rows_here : 2 * rows_here + carried_rows, :wide]
    rows = rows.reshape(half, 3, carried_rows // 3, wide).astype(single)
    rows = rows[:, 0] + rows[:, 1] + rows[:, 2]
    half_centre = rows[:, 0, :protos_here]
    half_sums = jnp.sum(rows[:, 1:, :all_rows], axis=0)
    other_centre = lax.ppermute(half_centre, "dev", pairs(count, across))
    sums = half_sums + lax.ppermute(half_sums, "dev", pairs(count, across))
    new_centre = jnp.where(
        student_side,
        jnp.concatenate([other_centre, half_centre]),
        jnp.concatenate([half_centre, other_centre]),
    ).reshape(-1)
    cross = jnp.log(sums[1]) - sums[2] / (sums[0] * tau_student)
    loss_total = jnp.sum(row_weight * cross)
    student_scale, teacher_scale = scale / sums[1], scale / sums[0]
    head_block_grad = jnp.where(student_side, own_block_grad, block_got.astype(single))
    early = over_core(early_grad, block_rows)
    small_rows = -(-(EMBED_ROWS + 6 * LAYERS) // (16 * count)) * 16
    small = embed_back(
        grad_stream,
        patches.reshape(images_here * PATCHES, PIX),
        jnp.where(masked_here, 0.0, 1.0).reshape(images_here * PATCHES, 1),
        jnp.stack([grad_gain, grad_bias]),
        jnp.concatenate(vector_grads),
        small_rows * count,
        (),
    )
    started.append(start(late, early, over_core(small, small_rows)))
    last_rows = lax.dynamic_slice(
        head_block_grad, (jnp.array(sizes, jnp.int32)[me] - GROUP, 0), (GROUP, ROW)
    )
    previous = lax.ppermute(last_rows, "dev", step_pairs(count, 1))
    proto_grad, proto_square, *held = proto_grad_pass(
        teacher_z_all,
        student_z_all,
        proto_teacher,
        protos,
        centre_column,
        lines(student_scale, teacher_scale),
        [stay for pieces, stage in started for sent, stay, left in pieces],
    )
    held = iter(held)
    started = [([(sent, next(held), left) for sent, _, left in pieces], stage) for pieces, stage in started]
    blocks = [finish(state) for state in started][::-1]
    middle_row = block_rows // 2
    layer_block = jnp.stack([jnp.concatenate([part[:, :middle_row] for part in parts], axis=1) for parts in blocks])
    small_block = jnp.concatenate([part[:, middle_row:] for part in blocks[0]], axis=1)

    square_local = (
        jnp.sum(head_block_grad * head_block_grad)
        + jnp.sum(layer_block * layer_block)
        + jnp.sum(small_block * small_block)
        + proto_square[0, 0]
    )
    high = square_local.astype(narrow)
    middle = (square_local - high.astype(single)).astype(narrow)
    low = (square_local - high.astype(single) - middle.astype(single)).astype(narrow)
    tile = jnp.pad(jnp.stack([high, middle, low]).reshape(1, 1, 3), ((0, 0), (0, 15), (0, 125)))
    first_rows = small_block[:2].astype(narrow)
    other_rows = jnp.concatenate([small_block[2:].astype(narrow), tile], axis=1)
    first_rows = cube_gather(first_rows, "xya")
    other_rows = cube_gather(other_rows, "abx")
    behind = lax.ppermute(layer_block[:, :, :6], "dev", step_pairs(count, -1))
    place = per_device([spots(head_span - starts[i], drift * i) for i in range(count)])
    stem_lines, layer_lines, first_rows, other_rows = own_shards(
        place, head_block_grad, previous, layer_block, behind, lane_rows(stem_piece), lane_rows(layer_piece),
        [first_rows, other_rows],
    )
    first_rows = jnp.moveaxis(cube_gather(first_rows, "bc").reshape((2, 2, 8) + first_rows.shape[1:]), 0, 2)
    other_rows = cube_gather(other_rows, "yc")
    other_rows = other_rows.reshape((2,) * 5 + other_rows.shape[2:])
    other_rows = jnp.transpose(other_rows, (3, 4, 1, 2, 0, 5, 6, 7))
    first_rows = first_rows.reshape((count,) + first_rows.shape[3:])
    other_rows = other_rows.reshape((count,) + other_rows.shape[5:])
    square_total = jnp.sum(other_rows[:, 0, small_rows, :3].astype(single))
    small_all = jnp.concatenate([first_rows, other_rows[:, :, :small_rows]], axis=1).astype(single)
    small_all = jnp.transpose(small_all, (0, 2, 1, 3)).reshape(small_rows * count, D)
    embed_grad = small_all[:EMBED_ROWS].reshape(-1)
    vector_grad = small_all[EMBED_ROWS : EMBED_ROWS + 6 * LAYERS].reshape(LAYERS, 6 * D)
    layer_grad = layer_lines.reshape(LAYERS, -1)[:, :layer_piece]
    layer_grad = jnp.concatenate(
        [
            layer_grad[:, : layer_piece - tail],
            jnp.where(me == count - 1, vector_grad, layer_grad[:, layer_piece - tail :]),
        ],
        axis=1,
    )
    stem_grad = stem_lines.reshape(-1)[:stem_piece]
    rest = EMBED_FLAT - stem_piece
    second_part = jnp.concatenate([embed_grad[stem_piece:], stem_grad[rest:]])
    stem_grad = jnp.where(
        me == 0, embed_grad[:stem_piece], jnp.where(me == 1, second_part, stem_grad)
    )

    grad_norm = jnp.sqrt(square_total) / count_total
    factor = jnp.minimum(1.0, clip_limit / (grad_norm + 1e-06)) / count_total
    stem_set = adam_update(stem, stem_moment, stem_second, stem_grad * factor, stem_teacher)
    layer_set = adam_update(layers, layer_moment, layer_second, layer_grad * factor, layer_teacher)
    proto_set = proto_update(factor, protos, proto_moment, proto_second, proto_teacher, proto_grad)
    return (loss_total, count_total, grad_norm, new_centre) + stem_set + layer_set + tuple(proto_set)


def solution(mesh):
    count = mesh.shape["dev"]
    stem_length = -(-(EMBED_FLAT + HEAD_ROWS * ROW) // count) * count
    close = fits(count, stem_length // count, (MATRIX_ROWS + 6) * D // count)
    placed = (
        P("dev", None, None),
        P("dev", None),
        P("dev"),
        P("dev"),
        P("dev"),
        P("dev"),
        P("dev"),
        P(None, "dev"),
        P(None, "dev"),
        P(None, "dev"),
        P(None, "dev"),
        P("dev", None),
        P("dev", None),
        P("dev", None),
        P("dev", None),
        P(),
    )
    return jax.shard_map(
        close_local if close else spread_local,
        mesh=mesh,
        in_specs=placed,
        out_specs=(
            P(),
            P(),
            P(),
            P(),
            P("dev"),
            P("dev"),
            P("dev"),
            P("dev"),
            P("dev"),
            P(None, "dev"),
            P(None, "dev"),
            P(None, "dev"),
            P(None, "dev"),
            P(None, "dev"),
            P("dev", None),
            P("dev", None),
            P("dev", None),
            P("dev", None),
            P("dev", None),
        ),
        check_vma=False,
    )
```
